32 devices in a mesh: dp: 4 (over y, x), row: 4 (over z), col: 2 (over core).
Axes of the slice: x: 2, y: 2, z: 4, core: 2. Of those that a mesh axis runs over, the one named last changes fastest.
Arguments:
- activations: bfloat16 [4096, 2048], P(('dp', 'col'), 'row'), may hold values from -6 to 6
- per_layer: bfloat16 [4096, 256], P(('dp', 'row'), 'col'), may hold values from -6 to 6
- cotangent: bfloat16 [4096, 2048], P(('dp', 'col'), 'row'), may hold values from -6 to 6
- lengths: int32 [4], replicated, may hold values from 1 to 1024, 2560 in all
- starts: int32 [4, 2], replicated, may hold values from 0 to 768, as said below
- w_query: float32 [2048, 2048], P('row', ('col', 'dp')), may hold values from -0.125 to 0.125
- m_query: float32 [2048, 2048], P('row', ('col', 'dp')), may hold values from -0.0007324219 to 0.0007324219
- v_query: float32 [2048, 2048], P('row', ('col', 'dp')), may hold values from 1.609199e-08 to 6.436796e-08
- key_value_weight: float32 [2048, 1024], P('row', 'dp'), may hold values from -0.125 to 0.125
- key_value_first_moment: float32 [2048, 1024], P('row', 'dp'), may hold values from -0.0007324219 to 0.0007324219
- key_value_second_moment: float32 [2048, 1024], P('row', 'dp'), may hold values from 1.609199e-08 to 6.436796e-08
- w_attend: float32 [2048, 2048], P('col', ('row', 'dp')), may hold values from -0.125 to 0.125
- m_attend: float32 [2048, 2048], P('col', ('row', 'dp')), may hold values from -0.0007324219 to 0.0007324219
- v_attend: float32 [2048, 2048], P('col', ('row', 'dp')), may hold values from 1.609199e-08 to 6.436796e-08
- w_gateup: float32 [2, 2048, 8192], P(None, 'row', ('col', 'dp')), may hold values from -0.125 to 0.125
- m_gateup: float32 [2, 2048, 8192], P(None, 'row', ('col', 'dp')), may hold values from -0.0007324219 to 0.0007324219
- v_gateup: float32 [2, 2048, 8192], P(None, 'row', ('col', 'dp')), may hold values from 1.609199e-08 to 6.436796e-08
- w_down: float32 [8192, 2048], P('col', ('row', 'dp')), may hold values from -0.0625 to 0.0625
- m_down: float32 [8192, 2048], P('col', ('row', 'dp')), may hold values from -0.0007324219 to 0.0007324219
- v_down: float32 [8192, 2048], P('col', ('row', 'dp')), may hold values from 1.609199e-08 to 6.436796e-08
- w_left: float32 [2048, 64], P('row', ('col', 'dp')), may hold values from -0.125 to 0.125
- m_left: float32 [2048, 64], P('row', ('col', 'dp')), may hold values from -0.0007324219 to 0.0007324219
- v_left: float32 [2048, 64], P('row', ('col', 'dp')), may hold values from 1.609199e-08 to 6.436796e-08
- w_right: float32 [64, 2048], P('col', ('row', 'dp')), may hold values from -0.75 to 0.75
- m_right: float32 [64, 2048], P('col', ('row', 'dp')), may hold values from -0.0007324219 to 0.0007324219
- v_right: float32 [64, 2048], P('col', ('row', 'dp')), may hold values from 1.609199e-08 to 6.436796e-08
- w_pergate: float32 [2048, 256], P('row', ('col', 'dp')), may hold values from -0.125 to 0.125
- m_pergate: float32 [2048, 256], P('row', ('col', 'dp')), may hold values from -0.0007324219 to 0.0007324219
- v_pergate: float32 [2048, 256], P('row', ('col', 'dp')), may hold values from 1.609199e-08 to 6.436796e-08
- w_perproj: float32 [256, 2048], P('col', ('row', 'dp')), may hold values from -0.375 to 0.375
- m_perproj: float32 [256, 2048], P('col', ('row', 'dp')), may hold values from -0.0007324219 to 0.0007324219
- v_perproj: float32 [256, 2048], P('col', ('row', 'dp')), may hold values from 1.609199e-08 to 6.436796e-08
- w_gains: float32 [6, 2048], P(None, 'row')
- m_gains: float32 [6, 2048], P(None, 'row'), may hold values from -0.0007324219 to 0.0007324219
- v_gains: float32 [6, 2048], P(None, 'row'), may hold values from 3.218398e-08 to 1.2873592e-07
- w_heads: float32 [9, 256], replicated
- m_heads: float32 [9, 256], replicated, may hold values from -0.0029296875 to 0.0029296875
- v_heads: float32 [9, 256], replicated, may hold values from 2.5747184e-07 to 1.0298874e-06
Outputs:
- result: bfloat16 [4096, 2048], P(('dp', 'col'), 'row')
- grad_input: bfloat16 [4096, 2048], P(('dp', 'col'), 'row')
- grad_norm: float32 [], replicated
- clip_factors: float32 [8], replicated
- mom_query: float32 [2048, 2048], P('row', ('col', 'dp'))
- sec_query: float32 [2048, 2048], P('row', ('col', 'dp'))
- new_query: float32 [2048, 2048], P('row', ('col', 'dp'))
- mom_keyval: float32 [2048, 1024], P('row', 'dp')
- sec_keyval: float32 [2048, 1024], P('row', 'dp')
- new_keyval: float32 [2048, 1024], P('row', 'dp')
- mom_attend: float32 [2048, 2048], P('col', ('row', 'dp'))
- sec_attend: float32 [2048, 2048], P('col', ('row', 'dp'))
- new_attend: float32 [2048, 2048], P('col', ('row', 'dp'))
- mom_gateup: float32 [2, 2048, 8192], P(None, 'row', ('col', 'dp'))
- sec_gateup: float32 [2, 2048, 8192], P(None, 'row', ('col', 'dp'))
- new_gateup: float32 [2, 2048, 8192], P(None, 'row', ('col', 'dp'))
- mom_down: float32 [8192, 2048], P('col', ('row', 'dp'))
- sec_down: float32 [8192, 2048], P('col', ('row', 'dp'))
- new_down: float32 [8192, 2048], P('col', ('row', 'dp'))
- mom_left: float32 [2048, 64], P('row', ('col', 'dp'))
- sec_left: float32 [2048, 64], P('row', ('col', 'dp'))
- new_left: float32 [2048, 64], P('row', ('col', 'dp'))
- mom_right: float32 [64, 2048], P('col', ('row', 'dp'))
- sec_right: float32 [64, 2048], P('col', ('row', 'dp'))
- new_right: float32 [64, 2048], P('col', ('row', 'dp'))
- mom_pergate: float32 [2048, 256], P('row', ('col', 'dp'))
- sec_pergate: float32 [2048, 256], P('row', ('col', 'dp'))
- new_pergate: float32 [2048, 256], P('row', ('col', 'dp'))
- mom_perproj: float32 [256, 2048], P('col', ('row', 'dp'))
- sec_perproj: float32 [256, 2048], P('col', ('row', 'dp'))
- new_perproj: float32 [256, 2048], P('col', ('row', 'dp'))
- mom_gains: float32 [6, 2048], P(None, 'row')
- sec_gains: float32 [6, 2048], P(None, 'row')
- new_gains: float32 [6, 2048], P(None, 'row')
- mom_heads: float32 [9, 256], replicated
- sec_heads: float32 [9, 256], replicated
- new_heads: float32 [9, 256], replicated
The draws below stay inside these ranges and needn't reach their ends.
Inputs may be any that keep to these rules, and one draw needn't show every extreme that they name: Tokens of sequence s from lengths[s] on are padding; one sequence uses all 1024 tokens. Piece k of sequence s covers starts[s, k] to starts[s, k] + 255 and starts between k * 512 and (k + 1) * 512 - 256.
All inputs are finite; a program needn't handle non-finite values.
Results may differ from the reference program's by a relative error of at most 0.02.
The reference program's roundings to bfloat16 on the way count: a program that leaves them out, or rounds other values in their place, can miss the bound.
Values may be sent and summed in bfloat16 or wider, within the bound.
A program may use at most 384 MiB of HBM per device.

```python
import math
import jax
import jax.numpy as jnp
import numpy as np
from jax import lax

MODEL_WIDTH = 2048
QUERY_HEADS = 8
KEY_VALUE_HEADS = 2
HEAD_WIDTH = 256
FF = 8192
RANK = 64
PLD = 256
IMG = 256
NIMG = 2
STEP = 10
GROUP = 1024
TOKENS = 4096
BLOCK_WEIGHTS = 62142720
N_DP = 4


def draw_starts(key, part):
    key = jax.random.fold_in(key, 11)
    slot_size = GROUP // NIMG
    offsets = jax.random.randint(key, (N_DP, NIMG), 0, slot_size - IMG + 1)
    offsets = offsets.at[0, NIMG - 1].set(slot_size - IMG)
    offsets = offsets.at[N_DP - 1, 0].set(0)
    return (offsets + jnp.arange(NIMG, dtype=jnp.int32)[None, :] * slot_size).astype(jnp.int32)


def draw_w_gains(key, part):
    key = jax.random.fold_in(key, 12)
    ramp_line = 0.5 + 1.5 * jnp.arange(MODEL_WIDTH, dtype=jnp.float32) / (MODEL_WIDTH - 1)
    factor = jax.random.uniform(key, (6, MODEL_WIDTH), jnp.float32, 0.8, 1.2)
    return ramp_line[None, :] * factor


def draw_w_heads(key, part):
    key = jax.random.fold_in(key, 13)
    key_one, key_two, key_three, key_four = jax.random.split(key, 4)
    levels = jnp.exp(jax.random.uniform(key_one, (QUERY_HEADS,), jnp.float32, jnp.log(0.2), jnp.log(0.6)))
    order = jax.random.permutation(key_four, QUERY_HEADS)
    levels = levels.at[order[0]].set(0.6)
    levels = levels.at[order[1]].set(0.2)
    bottom, summit = (0.8, 1.2)
    query_rows = jax.random.uniform(key_two, (QUERY_HEADS, HEAD_WIDTH), jnp.float32, bottom, summit) * levels[:, None]
    key_row = jax.random.uniform(key_three, (1, HEAD_WIDTH), jnp.float32, bottom, summit) * (5.0 / HEAD_WIDTH ** 0.5)
    return jnp.concatenate([query_rows, key_row], axis=0)


def level_of(own_key, extent, cuts, low, high):
    gain, own = 1.0, jax.random.fold_in(own_key, 6)
    for dim, parts in cuts:
        draws = jnp.exp(jax.random.uniform(jax.random.fold_in(own, dim), (parts,), jnp.float32, low / len(cuts), high / len(cuts)))
        gain = gain * jnp.repeat(draws, extent[dim] // parts).reshape([-1 if axis == dim else 1 for axis in range(len(extent))])
    return gain


def split_up(amount, total, most, slope):
    loads = [(1 << 20) // math.isqrt(standing ** slope) + 1 for standing in range(2, amount + 1)]
    surplus, holding = total - most - (amount - 1), [1] * (amount - 1)
    while surplus > 0:
        movable = [i for i in range(amount - 1) if holding[i] < most]
        whole, budget = sum([loads[i] for i in movable]), surplus
        for i in movable:
            extra = min(most - holding[i], max(1, budget * loads[i] // whole), surplus)
            holding[i] = holding[i] + extra
            surplus = surplus - extra
    return np.array([most] + holding)


def ragged(own_key, number_of, total, reach, slope):
    if number_of == 2:
        one = jax.random.randint(own_key, (), max(1, total - reach), min(reach, total - 1) + 1)
        return jnp.stack([one, total - one])
    sizes = jnp.asarray(split_up(number_of, total, reach, slope), jnp.int32)
    pairs = (number_of - 1) // 2
    donor, sink = sizes[1:1 + 2 * pairs:2], sizes[2:2 + 2 * pairs:2]
    slack = jnp.minimum(donor - 1, reach - sink)
    moved = jax.random.randint(jax.random.fold_in(own_key, 1), (pairs,), 0, 1 << 20) % (slack + 1)
    sizes = sizes.at[1:1 + 2 * pairs:2].set(donor - moved).at[2:2 + 2 * pairs:2].set(sink + moved)
    return sizes[jax.random.permutation(jax.random.fold_in(own_key, 2), number_of)]


def gaussian(stream_key, dims, deviation, bound, cuts=(), kind=jnp.bfloat16):
    drawn = deviation * jax.random.normal(stream_key, dims, jnp.float32)
    if cuts:
        drawn = drawn * level_of(stream_key, dims, cuts, -0.22, 0.18)
    return jnp.clip(drawn, -bound, bound).astype(kind)


def setup_inputs(seed: int = 0) -> dict:
    keys = jax.random.split(jax.random.key(seed), 39)
    return {
        "activations": gaussian(keys[0], (TOKENS, MODEL_WIDTH), 1.0, 6.0, ((0, 8), (1, 4))),
        "per_layer": gaussian(keys[1], (TOKENS, PLD), 1.0, 6.0, ((0, 16), (1, 2))),
        "cotangent": gaussian(keys[2], (TOKENS, MODEL_WIDTH), 1.0, 6.0, ((0, 8), (1, 4))),
        "lengths": ragged(keys[3], N_DP, GROUP * (N_DP + 1) // 2, GROUP, 0).astype(jnp.int32),
        "starts": draw_starts(jax.random.fold_in(keys[38], 71), 0),
        "w_query": gaussian(keys[5], (MODEL_WIDTH, QUERY_HEADS * HEAD_WIDTH), MODEL_WIDTH ** -0.5, 0.125, ((0, 4), (1, 8)), jnp.float32),
        "m_query": gaussian(keys[6], (MODEL_WIDTH, QUERY_HEADS * HEAD_WIDTH), (1.0 / BLOCK_WEIGHTS ** 0.5), 0.0007324219, ((0, 4), (1, 8)), jnp.float32),
        "v_query": jnp.clip(jnp.exp(math.log(6.436795985109711e-08) - 1.3862944 * jax.random.uniform(keys[7], (MODEL_WIDTH, QUERY_HEADS * HEAD_WIDTH), jnp.float32) ** level_of(keys[7], (MODEL_WIDTH, QUERY_HEADS * HEAD_WIDTH), ((0, 4), (1, 8)), -0.2, 0.2)), 1.6091989962774278e-08, 6.436795985109711e-08),
        "key_value_weight": gaussian(keys[8], (MODEL_WIDTH, 2 * KEY_VALUE_HEADS * HEAD_WIDTH), MODEL_WIDTH ** -0.5, 0.125, ((0, 4), (1, 4)), jnp.float32),
        "key_value_first_moment": gaussian(keys[9], (MODEL_WIDTH, 2 * KEY_VALUE_HEADS * HEAD_WIDTH), (1.0 / BLOCK_WEIGHTS ** 0.5), 0.0007324219, ((0, 4), (1, 4)), jnp.float32),
        "key_value_second_moment": jnp.clip(jnp.exp(math.log(6.436795985109711e-08) - 1.3862944 * jax.random.uniform(keys[10], (MODEL_WIDTH, 2 * KEY_VALUE_HEADS * HEAD_WIDTH), jnp.float32) ** level_of(keys[10], (MODEL_WIDTH, 2 * KEY_VALUE_HEADS * HEAD_WIDTH), ((0, 4), (1, 4)), -0.2, 0.2)), 1.6091989962774278e-08, 6.436795985109711e-08),
        "w_attend": gaussian(keys[11], (QUERY_HEADS * HEAD_WIDTH, MODEL_WIDTH), (QUERY_HEADS * HEAD_WIDTH) ** -0.5, 0.125, ((0, 2), (1, 16)), jnp.float32),
        "m_attend": gaussian(keys[12], (QUERY_HEADS * HEAD_WIDTH, MODEL_WIDTH), (1.0 / BLOCK_WEIGHTS ** 0.5), 0.0007324219, ((0, 2), (1, 16)), jnp.float32),
        "v_attend": jnp.clip(jnp.exp(math.log(6.436795985109711e-08) - 1.3862944 * jax.random.uniform(keys[13], (QUERY_HEADS * HEAD_WIDTH, MODEL_WIDTH), jnp.float32) ** level_of(keys[13], (QUERY_HEADS * HEAD_WIDTH, MODEL_WIDTH), ((0, 2), (1, 16)), -0.2, 0.2)), 1.6091989962774278e-08, 6.436795985109711e-08),
        "w_gateup": gaussian(keys[14], (2, MODEL_WIDTH, FF), MODEL_WIDTH ** -0.5, 0.125, ((1, 4), (2, 8)), jnp.float32),
        "m_gateup": gaussian(keys[15], (2, MODEL_WIDTH, FF), (1.0 / BLOCK_WEIGHTS ** 0.5), 0.0007324219, ((1, 4), (2, 8)), jnp.float32),
        "v_gateup": jnp.clip(jnp.exp(math.log(6.436795985109711e-08) - 1.3862944 * jax.random.uniform(keys[16], (2, MODEL_WIDTH, FF), jnp.float32) ** level_of(keys[16], (2, MODEL_WIDTH, FF), ((1, 4), (2, 8)), -0.2, 0.2)), 1.6091989962774278e-08, 6.436795985109711e-08),
        "w_down": gaussian(keys[17], (FF, MODEL_WIDTH), FF ** -0.5, 0.0625, ((0, 2), (1, 16)), jnp.float32),
        "m_down": gaussian(keys[18], (FF, MODEL_WIDTH), (1.0 / BLOCK_WEIGHTS ** 0.5), 0.0007324219, ((0, 2), (1, 16)), jnp.float32),
        "v_down": jnp.clip(jnp.exp(math.log(6.436795985109711e-08) - 1.3862944 * jax.random.uniform(keys[19], (FF, MODEL_WIDTH), jnp.float32) ** level_of(keys[19], (FF, MODEL_WIDTH), ((0, 2), (1, 16)), -0.2, 0.2)), 1.6091989962774278e-08, 6.436795985109711e-08),
        "w_left": gaussian(keys[20], (MODEL_WIDTH, RANK), MODEL_WIDTH ** -0.5, 0.125, ((0, 4), (1, 8)), jnp.float32),
        "m_left": gaussian(keys[21], (MODEL_WIDTH, RANK), (1.0 / BLOCK_WEIGHTS ** 0.5), 0.0007324219, ((0, 4), (1, 8)), jnp.float32),
        "v_left": jnp.clip(jnp.exp(math.log(6.436795985109711e-08) - 1.3862944 * jax.random.uniform(keys[22], (MODEL_WIDTH, RANK), jnp.float32) ** level_of(keys[22], (MODEL_WIDTH, RANK), ((0, 4), (1, 8)), -0.2, 0.2)), 1.6091989962774278e-08, 6.436795985109711e-08),
        "w_right": gaussian(keys[23], (RANK, MODEL_WIDTH), RANK ** -0.5, 0.75, ((0, 2), (1, 16)), jnp.float32),
        "m_right": gaussian(keys[24], (RANK, MODEL_WIDTH), (1.0 / BLOCK_WEIGHTS ** 0.5), 0.0007324219, ((0, 2), (1, 16)), jnp.float32),
        "v_right": jnp.clip(jnp.exp(math.log(6.436795985109711e-08) - 1.3862944 * jax.random.uniform(keys[25], (RANK, MODEL_WIDTH), jnp.float32) ** level_of(keys[25], (RANK, MODEL_WIDTH), ((0, 2), (1, 16)), -0.2, 0.2)), 1.6091989962774278e-08, 6.436795985109711e-08),
        "w_pergate": gaussian(keys[26], (MODEL_WIDTH, PLD), MODEL_WIDTH ** -0.5, 0.125, ((0, 4), (1, 8)), jnp.float32),
        "m_pergate": gaussian(keys[27], (MODEL_WIDTH, PLD), (1.0 / BLOCK_WEIGHTS ** 0.5), 0.0007324219, ((0, 4), (1, 8)), jnp.float32),
        "v_pergate": jnp.clip(jnp.exp(math.log(6.436795985109711e-08) - 1.3862944 * jax.random.uniform(keys[28], (MODEL_WIDTH, PLD), jnp.float32) ** level_of(keys[28], (MODEL_WIDTH, PLD), ((0, 4), (1, 8)), -0.2, 0.2)), 1.6091989962774278e-08, 6.436795985109711e-08),
        "w_perproj": gaussian(keys[29], (PLD, MODEL_WIDTH), PLD ** -0.5, 0.375, ((0, 2), (1, 16)), jnp.float32),
        "m_perproj": gaussian(keys[30], (PLD, MODEL_WIDTH), (1.0 / BLOCK_WEIGHTS ** 0.5), 0.0007324219, ((0, 2), (1, 16)), jnp.float32),
        "v_perproj": jnp.clip(jnp.exp(math.log(6.436795985109711e-08) - 1.3862944 * jax.random.uniform(keys[31], (PLD, MODEL_WIDTH), jnp.float32) ** level_of(keys[31], (PLD, MODEL_WIDTH), ((0, 2), (1, 16)), -0.2, 0.2)), 1.6091989962774278e-08, 6.436795985109711e-08),
        "w_gains": draw_w_gains(jax.random.fold_in(keys[38], 71), 0),
        "m_gains": gaussian(keys[33], (6, MODEL_WIDTH), (1.0 / BLOCK_WEIGHTS ** 0.5), 0.0007324219, ((1, 4),), jnp.float32),
        "v_gains": jnp.clip(jnp.exp(math.log(1.2873591970219422e-07) - 1.3862944 * jax.random.uniform(keys[34], (6, MODEL_WIDTH), jnp.float32) ** level_of(keys[34], (6, MODEL_WIDTH), ((1, 4),), -0.2, 0.2)), 3.2183979925548556e-08, 1.2873591970219422e-07),
        "w_heads": draw_w_heads(jax.random.fold_in(keys[38], 71), 0),
        "m_heads": gaussian(keys[36], (QUERY_HEADS + 1, HEAD_WIDTH), (4.0 / BLOCK_WEIGHTS ** 0.5), 0.0029296875, (), jnp.float32),
        "v_heads": jnp.clip(jnp.exp(jax.random.uniform(keys[37], (QUERY_HEADS + 1, HEAD_WIDTH), jnp.float32, math.log(2.5747183940438845e-07), math.log(1.0298873576175538e-06))), 2.5747183940438845e-07, 1.0298873576175538e-06),
    }


EPS = 1e-06
ROPE_BASE = 1000000.0
BETA_ONE = 0.5
BETA_TWO = 0.5
ADAM_EPS = 1e-08
DECAY = 0.01
CLIP = 1.0
LOGIT_CAP = 4.0
GAIN_RATE = 0.6
HEAD_RATE = 0.1
HALF_ROOT = 0.7071067811865476
NEGATIVE = -1e+30
HIGH = lax.Precision.HIGHEST

@jax.custom_vjp
def low(v):
    return lax.optimization_barrier(v.astype(jnp.bfloat16)).astype(jnp.float32)

@jax.custom_vjp
def low_back(v):
    return v

def low_keep(v):
    return (low(v), None)

def low_pass(kept, grad):
    return (grad,)

def back_keep(v):
    return (v, None)

def back_low(kept, grad):
    return (low(grad),)
low.defvjp(low_keep, low_pass)
low_back.defvjp(back_keep, back_low)

def product(left_mat, right_mat):
    return jnp.dot(left_mat, right_mat, precision=HIGH, preferred_element_type=jnp.float32)

def norm_rows(values_in, gain_vec):
    return values_in * lax.rsqrt(lax.optimization_barrier(jnp.mean(values_in * values_in, axis=-1, keepdims=True)) + EPS) * gain_vec

def rope_tables(count_of_rows, feat_width):
    half_width = feat_width // 2
    places = jnp.arange(count_of_rows, dtype=jnp.int32).astype(jnp.float32)
    powers = jnp.arange(half_width, dtype=jnp.int32).astype(jnp.float32) * (2.0 / feat_width)
    frequency = jnp.power(jnp.float32(ROPE_BASE), -powers)
    angles = places[:, None] * frequency[None, :]
    return (jnp.cos(angles), jnp.sin(angles))

def rotate(values_in, cos_tab, sin_tab):
    half_width = values_in.shape[-1] // 2
    part_one = values_in[..., :half_width]
    part_two = values_in[..., half_width:]
    return jnp.concatenate([part_one * cos_tab - part_two * sin_tab, part_two * cos_tab + part_one * sin_tab], axis=-1)

def piece_of(places, starts):
    inside = (places[:, None] >= starts[None, :]) & (places[:, None] < starts[None, :] + IMG)
    labels = jnp.arange(1, starts.shape[0] + 1, dtype=jnp.int32)
    return lax.optimization_barrier(jnp.sum(jnp.where(inside, labels[None, :], 0), axis=1)).astype(jnp.int32) - 1

def visible(query_places, key_places, query_pieces, key_pieces, length):
    causal = key_places[None, :] <= query_places[:, None]
    same_piece = (query_pieces[:, None] == key_pieces[None, :]) & (query_pieces[:, None] >= 0)
    return (key_places[None, :] < length) & (causal | same_piece)

def attend(queries, key_rows, value_rows, length, starts):
    head_count, count_of_rows, feat_width = queries.shape
    group_size = head_count // key_rows.shape[0]
    keys_all = jnp.repeat(key_rows, group_size, axis=0)
    values_all = jnp.repeat(value_rows, group_size, axis=0)
    key_places = jnp.arange(count_of_rows, dtype=jnp.int32)
    key_pieces = piece_of(key_places, starts)
    block_size = min(512, count_of_rows)
    stacked = queries.reshape(head_count, count_of_rows // block_size, block_size, feat_width).transpose(1, 0, 2, 3)

    @jax.checkpoint
    def one_block(element):
        block_rows, block_at = element
        query_places = block_at * block_size + jnp.arange(block_size, dtype=jnp.int32)
        allowed = visible(query_places, key_places, piece_of(query_places, starts), key_pieces, length)
        scores = low_back(jnp.einsum('hqd,hkd->hqk', block_rows, keys_all, precision=HIGH))
        masked = jnp.where(allowed[None], scores, NEGATIVE)
        peak_row = lax.optimization_barrier(jnp.max(masked, axis=-1, keepdims=True))
        raw_weights = jnp.where(allowed[None], jnp.exp(masked - peak_row), 0.0)
        attn_probs = low(raw_weights / lax.optimization_barrier(jnp.sum(raw_weights, axis=-1, keepdims=True)))
        outputs = jnp.einsum('hqk,hkd->hqd', attn_probs, values_all, precision=HIGH)
        return (outputs, lax.optimization_barrier(jnp.max(peak_row[..., 0], axis=1)))
    outputs, block_peaks = lax.map(one_block, (stacked, jnp.arange(count_of_rows // block_size, dtype=jnp.int32)))
    return (outputs.transpose(1, 0, 2, 3).reshape(head_count, count_of_rows, feat_width), lax.optimization_barrier(jnp.max(block_peaks, axis=0)))

def forward(params, seq_rows, seq_extra, length, starts):
    w_query, key_value_weight, w_attend, w_gateup, w_down, w_left, w_right, w_pergate, w_perproj, w_gains, w_heads = params
    count_of_rows = seq_rows.shape[0]
    hidden = norm_rows(seq_rows, w_gains[0])
    hidden_low = low(hidden)
    middle = low(low_back(product(hidden_low, low(w_left))))
    query_raw = low_back(product(hidden_low, low(w_query)))
    key_value_unscaled = low_back(product(hidden_low, low(key_value_weight)))
    cos_tab, sin_tab = rope_tables(count_of_rows, HEAD_WIDTH)
    queries = query_raw.reshape(count_of_rows, QUERY_HEADS, HEAD_WIDTH).transpose(1, 0, 2)
    queries = low(rotate(norm_rows(queries, w_heads[:QUERY_HEADS][:, None, :]), cos_tab, sin_tab))
    key_rows = key_value_unscaled[:, :KEY_VALUE_HEADS * HEAD_WIDTH].reshape(count_of_rows, KEY_VALUE_HEADS, HEAD_WIDTH).transpose(1, 0, 2)
    key_rows = low(rotate(norm_rows(key_rows, w_heads[QUERY_HEADS]), cos_tab, sin_tab))
    value_rows = key_value_unscaled[:, KEY_VALUE_HEADS * HEAD_WIDTH:].reshape(count_of_rows, KEY_VALUE_HEADS, HEAD_WIDTH).transpose(1, 0, 2)
    value_rows = low(norm_rows(value_rows, 1.0))
    attended, peaks = attend(queries, key_rows, value_rows, length, starts)
    merged = low(low_back(attended.transpose(1, 0, 2).reshape(count_of_rows, QUERY_HEADS * HEAD_WIDTH)))
    projected = low_back(product(merged, low(w_attend)))
    right_raw = low_back(product(middle, low(w_right)))
    laurel = hidden + norm_rows(right_raw, w_gains[1])
    gated_sum = seq_rows + norm_rows(projected, w_gains[2])
    mixture = (gated_sum + laurel) * HALF_ROOT
    ffn_in = low(norm_rows(mixture, w_gains[3]))
    gate_raw = low_back(product(ffn_in, low(w_gateup[0])))
    up_raw = low_back(product(ffn_in, low(w_gateup[1])))
    act_low = low(jax.nn.gelu(gate_raw, approximate=True) * up_raw)
    down_raw = low_back(product(act_low, low(w_down)))
    block_out = mixture + norm_rows(down_raw, w_gains[4])
    pgate = low_back(product(low(block_out), low(w_pergate)))
    pact = low(jax.nn.gelu(pgate, approximate=True) * seq_extra)
    perproj = low_back(product(pact, low(w_perproj)))
    return (block_out + norm_rows(perproj, w_gains[5]), peaks)

def adamw_step(weight, moment_one, moment_two, gradient, rate, decay):
    moment_one = BETA_ONE * moment_one + (1.0 - BETA_ONE) * gradient
    moment_two = BETA_TWO * moment_two + (1.0 - BETA_TWO) * gradient * gradient
    mean_step = moment_one / (1.0 - BETA_ONE ** STEP)
    spread = moment_two / (1.0 - BETA_TWO ** STEP)
    return (moment_one, moment_two, weight - rate * (mean_step / (jnp.sqrt(spread) + ADAM_EPS) + decay * weight))

def reference(activations, per_layer, cotangent, lengths, starts, w_query, m_query, v_query, key_value_weight, key_value_first_moment, key_value_second_moment, w_attend, m_attend, v_attend, w_gateup, m_gateup, v_gateup, w_down, m_down, v_down, w_left, m_left, v_left, w_right, m_right, v_right, w_pergate, m_pergate, v_pergate, w_perproj, m_perproj, v_perproj, w_gains, m_gains, v_gains, w_heads, m_heads, v_heads):
    weights = (w_query, key_value_weight, w_attend, w_gateup, w_down, w_left, w_right, w_pergate, w_perproj, w_gains, w_heads)
    moments = (m_query, key_value_first_moment, m_attend, m_gateup, m_down, m_left, m_right, m_pergate, m_perproj, m_gains, m_heads)
    seconds = (v_query, key_value_second_moment, v_attend, v_gateup, v_down, v_left, v_right, v_pergate, v_perproj, v_gains, v_heads)
    seq_inputs = activations.astype(jnp.float32).reshape(N_DP, GROUP, MODEL_WIDTH)
    seq_extras = per_layer.astype(jnp.float32).reshape(N_DP, GROUP, PLD)
    seq_backs = cotangent.astype(jnp.float32).reshape(N_DP, GROUP, MODEL_WIDTH)

    def one_sequence(totals, element):
        seq_rows, seq_extra, seq_back, length, piece_starts = element

        def apply_block(*values_in):
            return forward(values_in[:-1], values_in[-1], seq_extra, length, piece_starts)
        block_result, pullback, peaks = jax.vjp(apply_block, *weights, seq_rows, has_aux=True)
        gradients = pullback(seq_back)
        totals = tuple((a + b for a, b in zip(totals, gradients[:-1])))
        return (totals, (block_result.astype(jnp.bfloat16), gradients[-1].astype(jnp.bfloat16), peaks))
    zero_sums = tuple((jnp.zeros_like(w) for w in weights))
    totals, (results, grad_rows, peaks) = lax.scan(one_sequence, zero_sums, (seq_inputs, seq_extras, seq_backs, lengths, starts))
    logit_top = lax.optimization_barrier(jnp.max(peaks, axis=0))
    squares = jnp.float32(0.0)
    for gradient in totals:
        squares = squares + jnp.sum(gradient * gradient)
    grad_norm = jnp.sqrt(squares)
    clip_scale = CLIP / jnp.maximum(grad_norm, CLIP)
    scale_factors = LOGIT_CAP / jnp.maximum(logit_top, LOGIT_CAP)
    step_rates = (MODEL_WIDTH ** (-0.5), MODEL_WIDTH ** (-0.5), (QUERY_HEADS * HEAD_WIDTH) ** (-0.5), MODEL_WIDTH ** (-0.5), FF ** (-0.5), MODEL_WIDTH ** (-0.5), RANK ** (-0.5), MODEL_WIDTH ** (-0.5), PLD ** (-0.5), GAIN_RATE, HEAD_RATE)
    decays = (DECAY, DECAY, DECAY, DECAY, DECAY, DECAY, DECAY, DECAY, DECAY, 0.0, 0.0)
    updated = [adamw_step(weights[k], moments[k], seconds[k], totals[k] * clip_scale, step_rates[k], decays[k]) for k in range(11)]
    head_scale = jnp.sqrt(scale_factors)
    key_value_scale = jnp.sqrt(lax.optimization_barrier(jnp.min(scale_factors.reshape(KEY_VALUE_HEADS, QUERY_HEADS // KEY_VALUE_HEADS), axis=1)))
    query_cols = jnp.repeat(head_scale, HEAD_WIDTH)
    key_value_columns = jnp.concatenate([jnp.repeat(key_value_scale, HEAD_WIDTH), jnp.ones((KEY_VALUE_HEADS * HEAD_WIDTH,), jnp.float32)])
    new_query = updated[0][2] * query_cols[None, :]
    new_keyval = updated[1][2] * key_value_columns[None, :]
    return (results.reshape(TOKENS, MODEL_WIDTH), grad_rows.reshape(TOKENS, MODEL_WIDTH), grad_norm, scale_factors, updated[0][0], updated[0][1], new_query, updated[1][0], updated[1][1], new_keyval, updated[2][0], updated[2][1], updated[2][2], updated[3][0], updated[3][1], updated[3][2], updated[4][0], updated[4][1], updated[4][2], updated[5][0], updated[5][1], updated[5][2], updated[6][0], updated[6][1], updated[6][2], updated[7][0], updated[7][1], updated[7][2], updated[8][0], updated[8][1], updated[8][2], updated[9][0], updated[9][1], updated[9][2], updated[10][0], updated[10][1], updated[10][2])
```

```python
import jax
import jax.numpy as jnp
from jax import lax
from jax.experimental import pallas as pl
from jax.experimental.pallas import tpu as pltpu
from jax.sharding import PartitionSpec as P

MODEL_WIDTH = 2048
QUERY_HEADS = 8
KEY_VALUE_HEADS = 2
HEAD_WIDTH = 256
FF = 8192
RANK = 64
PLD = 256
IMG = 256
STEP = 10


EPS = 1e-06
ROPE_BASE = 1000000.0
BETA_ONE = 0.5
BETA_TWO = 0.5
ADAM_EPS = 1e-08
DECAY = 0.01
CLIP = 1.0
LOGIT_CAP = 4.0
GAIN_RATE = 0.6
HEAD_RATE = 0.1
HALF_ROOT = 0.7071067811865476
NEGATIVE = -1e30


def joined(part, axis, combine):
    gathered = jax.tree.map(lambda a: lax.all_gather(a, axis), part)

    def take(source):
        return jax.tree.map(lambda a: lax.dynamic_index_in_dim(a, source, 0, False), gathered)

    return lax.fori_loop(
        1, lax.axis_size(axis), lambda source, state: combine(state, take(source)), take(0)
    )


def row_total(values_in):
    return lax.psum(values_in, "row")


def spread_col(values_in):
    return lax.all_gather(values_in, "col", axis=0, tiled=True)


def reduce_row(values_in):
    return lax.psum_scatter(values_in, "row", scatter_dimension=0, tiled=True)


def spread_row(values_in):
    return lax.all_gather(values_in, "row", axis=0, tiled=True)


def reduce_col(values_in):
    return lax.psum_scatter(values_in, "col", scatter_dimension=0, tiled=True)


def grads_col(values_in):
    return lax.all_gather(values_in, "col", axis=0, tiled=True)


def grads_row(values_in):
    return lax.all_gather(values_in, "row", axis=0, tiled=True)


def inner_rows(left_mat, right_mat):
    return lax.dot_general(
        left_mat, right_mat, (((0,), (0,)), ((), ())), preferred_element_type=jnp.float32
    )


def against(grad_mat, weight_mat):
    return lax.dot_general(
        grad_mat, weight_mat, (((1,), (1,)), ((), ())), preferred_element_type=jnp.float32
    )


def flat_dot(left_mat, right_mat):
    return jnp.dot(left_mat, right_mat, preferred_element_type=jnp.float32)


def norm_forward(values_in, gain_vec):
    total_sq = row_total(jnp.sum(values_in * values_in, axis=-1, keepdims=True))
    norm_scale = lax.rsqrt(total_sq / MODEL_WIDTH + EPS)
    return (values_in * norm_scale * gain_vec, norm_scale)


def norm_backward(values_in, norm_scale, gain_vec, grad_out):
    weighted = grad_out * gain_vec
    inner_sum = row_total(jnp.sum(weighted * values_in, axis=-1, keepdims=True))
    grad_in = norm_scale * weighted - values_in * (norm_scale * norm_scale * norm_scale) * (
        inner_sum / MODEL_WIDTH
    )
    return (grad_in, jnp.sum(grad_out * values_in * norm_scale, axis=0))


def norm_rows(values_in, gain_vec):
    return (
        values_in
        * lax.rsqrt(jnp.mean(values_in * values_in, axis=-1, keepdims=True) + EPS)
        * gain_vec
    )


def rope_tables(places, feat_width):
    half_width = feat_width // 2
    powers = jnp.arange(half_width, dtype=jnp.int32).astype(jnp.float32) * (2.0 / feat_width)
    frequency = jnp.power(jnp.float32(ROPE_BASE), -powers)
    angles = places.astype(jnp.float32)[:, None] * frequency[None, :]
    return (jnp.cos(angles), jnp.sin(angles))


def rotate(values_in, cos_tab, sin_tab):
    half_width = values_in.shape[-1] // 2
    part_one = values_in[..., :half_width]
    part_two = values_in[..., half_width:]
    cos_row = cos_tab[:, None, :]
    sin_row = sin_tab[:, None, :]
    return jnp.concatenate(
        [part_one * cos_row - part_two * sin_row, part_two * cos_row + part_one * sin_row], axis=-1
    )


def query_form(unscaled_rows, gain_rows, cos_tab, sin_tab):
    shaped = unscaled_rows.reshape(unscaled_rows.shape[0], gain_rows.shape[0], HEAD_WIDTH)
    return rotate(norm_rows(shaped, gain_rows[None]), cos_tab, sin_tab)


def key_form(unscaled_rows, gain_vec, cos_tab, sin_tab):
    count_of_rows = unscaled_rows.shape[0]
    key_rows = unscaled_rows[:, : KEY_VALUE_HEADS * HEAD_WIDTH].reshape(
        count_of_rows, KEY_VALUE_HEADS, HEAD_WIDTH
    )
    value_rows = unscaled_rows[:, KEY_VALUE_HEADS * HEAD_WIDTH :].reshape(
        count_of_rows, KEY_VALUE_HEADS, HEAD_WIDTH
    )
    key_rows = rotate(norm_rows(key_rows, gain_vec), cos_tab, sin_tab)
    value_rows = norm_rows(value_rows, 1.0)
    return jnp.concatenate(
        [
            key_rows.reshape(count_of_rows, KEY_VALUE_HEADS * HEAD_WIDTH),
            value_rows.reshape(count_of_rows, KEY_VALUE_HEADS * HEAD_WIDTH),
        ],
        axis=1,
    )


def piece_of(places, starts):
    inside = (places[:, None] >= starts[None, :]) & (places[:, None] < starts[None, :] + IMG)
    labels = jnp.arange(1, starts.shape[0] + 1, dtype=jnp.int32)
    return jnp.sum(jnp.where(inside, labels[None, :], 0), axis=1) - 1


def visible(query_places, key_places, query_pieces, key_pieces, length):
    causal = key_places[None, :] <= query_places[:, None]
    same_piece = (query_pieces[:, None] == key_pieces[None, :]) & (query_pieces[:, None] >= 0)
    return (key_places[None, :] < length) & (causal | same_piece)


def block_mask(own_places, key_places, key_pieces, length, starts):
    return visible(own_places, key_places, piece_of(own_places, starts), key_pieces, length)


def attention_forward(queries, key_sel, value_sel, own_places, key_places, length, starts):
    count_of_rows, head_count = (queries.shape[0], queries.shape[1])
    block_size = min(512, count_of_rows)
    key_pieces = piece_of(key_places, starts)
    stacked = queries.reshape(count_of_rows // block_size, block_size, head_count, HEAD_WIDTH)

    def one_block(element):
        block_rows, block_at = element
        allowed = block_mask(own_places, key_places, key_pieces, length, starts)
        scores = jnp.einsum("qhd,khd->hqk", block_rows, key_sel, preferred_element_type=jnp.float32)
        masked = jnp.where(allowed[None], scores, NEGATIVE)
        peak_row = jnp.max(masked, axis=-1, keepdims=True)
        raw_weights = jnp.where(allowed[None], jnp.exp(masked - peak_row), 0.0)
        total_row = jnp.sum(raw_weights, axis=-1, keepdims=True)
        attn_probs = (raw_weights / total_row).astype(jnp.bfloat16)
        outputs = jnp.einsum(
            "hqk,khd->qhd", attn_probs, value_sel, preferred_element_type=jnp.float32
        )
        return (outputs, peak_row[..., 0], total_row[..., 0])

    return lax.map(one_block, (stacked, jnp.arange(count_of_rows // block_size, dtype=jnp.int32)))


def attention_backward(
    queries,
    key_sel,
    value_sel,
    grad_attended,
    block_peaks,
    block_totals,
    own_places,
    key_places,
    length,
    starts,
):
    count_of_rows, head_count = (queries.shape[0], queries.shape[1])
    block_size = min(512, count_of_rows)
    block_count = count_of_rows // block_size
    key_pieces = piece_of(key_places, starts)
    stacked = queries.reshape(block_count, block_size, head_count, HEAD_WIDTH)
    grad_stacked = grad_attended.reshape(block_count, block_size, head_count, HEAD_WIDTH)

    def one_block(carry, element):
        dk_sum, dv_sum = carry
        block_rows, grad_rows, peak_row, total_row, block_at = element
        allowed = block_mask(own_places, key_places, key_pieces, length, starts)
        scores = jnp.einsum("qhd,khd->hqk", block_rows, key_sel, preferred_element_type=jnp.float32)
        masked = jnp.where(allowed[None], scores, NEGATIVE)
        raw_weights = jnp.where(allowed[None], jnp.exp(masked - peak_row[..., None]), 0.0)
        attn_probs = raw_weights / total_row[..., None]
        probs_low = attn_probs.astype(jnp.bfloat16)
        grad_probs = jnp.einsum(
            "qhd,khd->hqk", grad_rows, value_sel, preferred_element_type=jnp.float32
        )
        delta_row = jnp.sum(attn_probs * grad_probs, axis=-1, keepdims=True)
        grad_scores = (attn_probs * (grad_probs - delta_row)).astype(jnp.bfloat16)
        grad_query = jnp.einsum(
            "hqk,khd->qhd", grad_scores, key_sel, preferred_element_type=jnp.float32
        )
        dk_sum = dk_sum + jnp.einsum(
            "hqk,qhd->khd", grad_scores, block_rows, preferred_element_type=jnp.float32
        )
        dv_sum = dv_sum + jnp.einsum(
            "hqk,qhd->khd", probs_low, grad_rows, preferred_element_type=jnp.float32
        )
        return ((dk_sum, dv_sum), grad_query)

    zero_keys = jnp.zeros(key_sel.shape, jnp.float32)
    (dk_sum, dv_sum), grad_query = lax.scan(
        one_block,
        (zero_keys, zero_keys),
        (
            stacked,
            grad_stacked,
            block_peaks,
            block_totals,
            jnp.arange(block_count, dtype=jnp.int32),
        ),
    )
    return (grad_query.reshape(count_of_rows, head_count, HEAD_WIDTH), dk_sum, dv_sum)


def adamw_step(weight, moment_one, moment_two, gradient, rate, decay):
    moment_one = BETA_ONE * moment_one + (1.0 - BETA_ONE) * gradient
    moment_two = BETA_TWO * moment_two + (1.0 - BETA_TWO) * gradient * gradient
    mean_step = moment_one / (1.0 - BETA_ONE**STEP)
    spread = moment_two / (1.0 - BETA_TWO**STEP)
    return (
        moment_one,
        moment_two,
        weight - rate * (mean_step / (jnp.sqrt(spread) + ADAM_EPS) + decay * weight),
    )


MESH = pl.DeviceIdType.MESH
LOW = jnp.bfloat16
FULL = jnp.float32


def cost(micros, flops=0):
    return pl.CostEstimate(
        flops=flops, bytes_accessed=int(micros * 3.0e6), transcendentals=0
    )


def params(ident, mebibytes=48):
    return pltpu.CompilerParams(
        collective_id=ident, has_side_effects=True, vmem_limit_bytes=mebibytes * 2**20
    )


def push(source, target, send, recv, device):
    return pltpu.make_async_remote_copy(
        source, target, send, recv, device_id=device, device_id_type=MESH
    )


def greet_line(me, count, column, core):
    barrier = pltpu.get_barrier_semaphore()

    @pl.when(me > 0)
    def _():
        pl.semaphore_signal(barrier, inc=1, device_id={"row": me - 1}, device_id_type=MESH)

    @pl.when(me < count - 1)
    def _():
        pl.semaphore_signal(barrier, inc=1, device_id={"row": me + 1}, device_id_type=MESH)

    if core:
        pl.semaphore_signal(barrier, inc=1, device_id={"col": 1 - column}, device_id_type=MESH)

    ends = (me == 0) | (me == count - 1)

    @pl.when(ends)
    def _():
        pl.semaphore_wait(barrier, 1 + int(core))

    @pl.when(jnp.logical_not(ends))
    def _():
        pl.semaphore_wait(barrier, 2 + int(core))


def line_gather(block, ident, core, micros):
    count = lax.axis_size("row")

    def kernel(x_ref, o_ref, send_l, send_r, send_c, recv_l, recv_r, recv_c, local):
        me = lax.axis_index("row")
        column = lax.axis_index("col")

        def slot(source):
            return o_ref.at[column, source] if core else o_ref.at[source]

        def other(source):
            return o_ref.at[1 - column, source]

        def to_left(source, k):
            origin = x_ref if k == 0 else slot(source)
            return push(origin, slot(source), send_l.at[k], recv_r.at[k], {"row": me - 1})

        def to_right(source, k):
            origin = x_ref if k == 0 else slot(source)
            return push(origin, slot(source), send_r.at[k], recv_l.at[k], {"row": me + 1})

        def to_core(source, k):
            origin = x_ref if k == 0 else slot(source)
            return push(origin, slot(source), send_c.at[k], recv_c.at[k], {"col": 1 - column})

        def from_core(source, k):
            return push(other(source), other(source), send_c.at[k], recv_c.at[k], {"col": 1 - column})

        greet_line(me, count, column, core)

        @pl.when(me > 0)
        def _():
            to_left(me, 0).start()

        @pl.when(me < count - 1)
        def _():
            to_right(me, 0).start()

        if core:
            to_core(me, 0).start()
        own = pltpu.make_async_copy(x_ref, slot(me), local)
        own.start()
        for k in range(1, count):

            @pl.when(me - k >= 0)
            def _():
                push(slot(me - k), slot(me - k), send_r.at[k], recv_l.at[k - 1], {"row": me - 1}).wait_recv()

                @pl.when(me < count - 1)
                def _():
                    to_right(me - k, k).start()

                if core:
                    to_core(me - k, k).start()

            @pl.when(me + k < count)
            def _():
                push(slot(me + k), slot(me + k), send_l.at[k], recv_r.at[k - 1], {"row": me + 1}).wait_recv()

                @pl.when(me > 0)
                def _():
                    to_left(me + k, k).start()

                if core:
                    to_core(me + k, count - 1 + k).start()

        own.wait()

        @pl.when(me > 0)
        def _():
            to_left(me, 0).wait_send()

        @pl.when(me < count - 1)
        def _():
            to_right(me, 0).wait_send()

        if core:
            to_core(me, 0).wait_send()
            from_core(me, 0).wait_recv()
        for k in range(1, count):

            @pl.when(me - k >= 0)
            def _():
                @pl.when(me < count - 1)
                def _():
                    to_right(me - k, k).wait_send()

                if core:
                    to_core(me - k, k).wait_send()
                    from_core(me - k, k).wait_recv()

            @pl.when(me + k < count)
            def _():
                @pl.when(me > 0)
                def _():
                    to_left(me + k, k).wait_send()

                if core:
                    to_core(me + k, count - 1 + k).wait_send()
                    from_core(me + k, count - 1 + k).wait_recv()

    shape = ((2, count) if core else (count,)) + block.shape
    dma = pltpu.SemaphoreType.DMA
    return pl.pallas_call(
        kernel,
        out_shape=jax.ShapeDtypeStruct(shape, block.dtype),
        in_specs=[pl.BlockSpec(memory_space=pl.ANY)],
        out_specs=pl.BlockSpec(memory_space=pl.ANY),
        scratch_shapes=[
            dma((count,)),
            dma((count,)),
            dma((2 * count,)),
            dma((count,)),
            dma((count,)),
            dma((2 * count,)),
            dma,
        ],
        compiler_params=params(ident),
        cost_estimate=cost(micros),
    )(block)


def line_reduce(parts, ident, core, micros):
    count = lax.axis_size("row")
    high, wide = parts.shape[-2:]
    chunk = min(high, max(16, 65536 // wide))

    def kernel(x_ref, o_ref, c_buf, l_buf, r_buf, s_buf, send_l, send_r, send_c, recv_l, recv_r, recv_c):
        me = lax.axis_index("row")
        column = lax.axis_index("col")

        def mine(q):
            return x_ref.at[column, q] if core else x_ref.at[q]

        def core_copy(q):
            return push(x_ref.at[1 - column, q], c_buf.at[q], send_c.at[q], recv_c.at[q], {"col": 1 - column})

        def left_copy(q):
            return push(s_buf.at[q], l_buf.at[q], send_l.at[q], recv_l.at[q], {"row": me - 1})

        def right_copy(q):
            return push(s_buf.at[q], r_buf.at[q], send_r.at[q], recv_r.at[q], {"row": me + 1})

        def left_arrival(q):
            return push(s_buf.at[q], l_buf.at[q], send_l.at[q], recv_l.at[q], {"row": me + 1})

        def right_arrival(q):
            return push(s_buf.at[q], r_buf.at[q], send_r.at[q], recv_r.at[q], {"row": me - 1})

        def added(target, terms):
            @pl.loop(0, high // chunk)
            def _(at):
                rows = pl.ds(pl.multiple_of(at * chunk, chunk), chunk)
                total = terms[0][rows].astype(FULL)
                for term in terms[1:]:
                    total = total + term[rows].astype(FULL)
                target[rows] = total.astype(target.dtype)

        def base(q):
            return [mine(q)] + ([c_buf.at[q]] if core else [])

        greet_line(me, count, column, core)
        if core:
            for q in range(count):
                core_copy(q).start()

        def leftward(q):
            @pl.when(me > q)
            def _():
                if core:
                    core_copy(q).wait_recv()

                @pl.when(me < count - 1)
                def _():
                    left_arrival(q).wait_recv()
                    added(s_buf.at[q], base(q) + [l_buf.at[q]])

                @pl.when(me == count - 1)
                def _():
                    added(s_buf.at[q], base(q))

                left_copy(q).start()

        def rightward(q):
            @pl.when(me < q)
            def _():
                if core:
                    core_copy(q).wait_recv()

                @pl.when(me > 0)
                def _():
                    right_arrival(q).wait_recv()
                    added(s_buf.at[q], base(q) + [r_buf.at[q]])

                @pl.when(me == 0)
                def _():
                    added(s_buf.at[q], base(q))

                right_copy(q).start()

        for j in range(count - 1):

            @pl.when(me < count // 2)
            def _():
                rightward(count - 1 - j)

            leftward(j)

            @pl.when(me >= count // 2)
            def _():
                rightward(count - 1 - j)

        if core:
            core_copy(me).wait_recv()

        @pl.when(me < count - 1)
        def _():
            left_arrival(me).wait_recv()

        @pl.when(me > 0)
        def _():
            right_arrival(me).wait_recv()

        @pl.when(me == 0)
        def _():
            added(o_ref, base(me) + [l_buf.at[me]])

        @pl.when(me == count - 1)
        def _():
            added(o_ref, base(me) + [r_buf.at[me]])

        @pl.when((me > 0) & (me < count - 1))
        def _():
            added(o_ref, base(me) + [l_buf.at[me], r_buf.at[me]])

        for q in range(count):
            if core:
                core_copy(q).wait_send()

            @pl.when(me > q)
            def _():
                left_copy(q).wait_send()

            @pl.when(me < q)
            def _():
                right_copy(q).wait_send()

    dma = pltpu.SemaphoreType.DMA
    slots = (count, high, wide)
    vmem = pl.BlockSpec(memory_space=pltpu.VMEM)
    return pl.pallas_call(
        kernel,
        out_shape=jax.ShapeDtypeStruct((high, wide), FULL),
        in_specs=[vmem],
        out_specs=vmem,
        scratch_shapes=[
            pltpu.VMEM(slots if core else (1, 16, 128), parts.dtype),
            pltpu.VMEM(slots, parts.dtype),
            pltpu.VMEM(slots, parts.dtype),
            pltpu.VMEM(slots, parts.dtype),
        ]
        + [dma((count,))] * 6,
        compiler_params=params(ident),
        cost_estimate=cost(micros),
    )(parts)


def core_gather(block, ident):
    def kernel(x_ref, o_ref, send, recv, local):
        column = lax.axis_index("col")
        barrier = pltpu.get_barrier_semaphore()
        pl.semaphore_signal(barrier, inc=1, device_id={"col": 1 - column}, device_id_type=MESH)
        pl.semaphore_wait(barrier, 1)
        copy = push(x_ref, o_ref.at[column], send, recv, {"col": 1 - column})
        copy.start()
        own = pltpu.make_async_copy(x_ref, o_ref.at[column], local)
        own.start()
        own.wait()
        copy.wait_send()
        push(x_ref, o_ref.at[1 - column], send, recv, {"col": 1 - column}).wait_recv()

    dma = pltpu.SemaphoreType.DMA
    return pl.pallas_call(
        kernel,
        out_shape=jax.ShapeDtypeStruct((2,) + block.shape, block.dtype),
        in_specs=[pl.BlockSpec(memory_space=pl.ANY)],
        out_specs=pl.BlockSpec(memory_space=pl.ANY),
        scratch_shapes=[dma, dma, dma],
        compiler_params=params(ident),
        cost_estimate=cost(6),
    )(block)


def core_reduce(parts, ident):
    def kernel(x_ref, o_ref, buf, send, recv):
        column = lax.axis_index("col")
        barrier = pltpu.get_barrier_semaphore()
        pl.semaphore_signal(barrier, inc=1, device_id={"col": 1 - column}, device_id_type=MESH)
        pl.semaphore_wait(barrier, 1)
        copy = push(x_ref.at[1 - column], buf, send, recv, {"col": 1 - column})
        copy.start()
        copy.wait()

        @pl.loop(0, o_ref.shape[0] // 64)
        def _(at):
            rows = pl.ds(pl.multiple_of(at * 64, 64), 64)
            o_ref[rows] = x_ref[column, rows].astype(FULL) + buf[rows].astype(FULL)

    dma = pltpu.SemaphoreType.DMA
    vmem = pl.BlockSpec(memory_space=pltpu.VMEM)
    return pl.pallas_call(
        kernel,
        out_shape=jax.ShapeDtypeStruct(parts.shape[1:], FULL),
        in_specs=[vmem],
        out_specs=vmem,
        scratch_shapes=[pltpu.VMEM(parts.shape[1:], parts.dtype), dma, dma],
        compiler_params=params(ident),
        cost_estimate=cost(6),
    )(parts)


def small_total(values_in, axes, max_rows, ident):
    sizes = [lax.axis_size(axis) for axis in axes]
    high = values_in.shape[0]

    def kernel(x_ref, o_ref, *scratch):
        slots, sends, recvs = (scratch[k :: 3] for k in range(3))
        barrier = pltpu.get_barrier_semaphore()
        spots = [lax.axis_index(axis) for axis in axes]
        for axis, size, me in zip(axes, sizes, spots):
            for k in range(1, size):
                pl.semaphore_signal(
                    barrier, inc=1, device_id={axis: lax.rem(me + k, size)}, device_id_type=MESH
                )
        pl.semaphore_wait(barrier, sum(sizes) - len(sizes))
        for at, (axis, size, me) in enumerate(zip(axes, sizes, spots)):
            buf, send, recv = slots[at], sends[at], recvs[at]
            buf[me] = x_ref[...] if at == 0 else o_ref[...]
            for k in range(1, size):
                push(buf.at[me], buf.at[me], send.at[k], recv.at[k], {axis: lax.rem(me + k, size)}).start()
            for k in range(1, size):
                origin = lax.rem(me + size - k, size)
                push(buf.at[origin], buf.at[origin], send.at[k], recv.at[k], {axis: origin}).wait()
            total = buf[0]
            for k in range(1, size):
                total = total + buf[k]
            o_ref[...] = total
            if max_rows:
                top = buf[0, high - max_rows :]
                for k in range(1, size):
                    top = jnp.maximum(top, buf[k, high - max_rows :])
                o_ref[high - max_rows :] = top

    dma = pltpu.SemaphoreType.DMA
    vmem = pl.BlockSpec(memory_space=pltpu.VMEM)
    scratch = []
    for size in sizes:
        scratch += [pltpu.VMEM((size,) + values_in.shape, FULL), dma((size,)), dma((size,))]
    return pl.pallas_call(
        kernel,
        out_shape=jax.ShapeDtypeStruct(values_in.shape, FULL),
        in_specs=[vmem],
        out_specs=vmem,
        scratch_shapes=scratch,
        compiler_params=params(ident, 16),
        cost_estimate=cost(4 * len(sizes)),
    )(values_in)


def allowed_block(at, high, width, spans):
    key_places = lax.broadcasted_iota(jnp.int32, (high, width), 1)
    query_places = at * high + lax.broadcasted_iota(jnp.int32, (high, width), 0)
    seen = key_places <= query_places
    for piece in range(spans.shape[0] - 1):
        start = spans[piece + 1]
        both = (
            (key_places >= start)
            & (key_places < start + IMG)
            & (query_places >= start)
            & (query_places < start + IMG)
        )
        seen = seen | both
    return seen & (key_places < spans[0])


def softmax_block(block_rows, keys, allowed):
    scores = against(block_rows, keys)
    masked = jnp.where(allowed, scores, NEGATIVE)
    peak_row = jnp.max(masked, axis=-1, keepdims=True)
    raw_weights = jnp.where(allowed, jnp.exp(masked - peak_row), 0.0)
    return raw_weights / jnp.sum(raw_weights, axis=-1, keepdims=True), peak_row


def head_forward(queries, keys, values, spans):
    rows = queries.shape[0]
    step = min(256, rows)

    def kernel(spans_ref, q_ref, k_ref, v_ref, o_ref, top_ref):
        top_ref[...] = jnp.full(top_ref.shape, NEGATIVE, FULL)

        @pl.loop(0, rows // step)
        def _(at):
            here = pl.ds(pl.multiple_of(at * step, step), step)
            allowed = allowed_block(at, step, keys.shape[0], spans_ref)
            probs, peak_row = softmax_block(q_ref[here], k_ref[...], allowed)
            o_ref[here] = flat_dot(probs.astype(LOW), v_ref[...]).astype(LOW)
            top_ref[...] = jnp.maximum(top_ref[...], jnp.max(peak_row))

    vmem = pl.BlockSpec(memory_space=pltpu.VMEM)
    return pl.pallas_call(
        kernel,
        out_shape=(
            jax.ShapeDtypeStruct(queries.shape, LOW),
            jax.ShapeDtypeStruct((8, 128), FULL),
        ),
        in_specs=[pl.BlockSpec(memory_space=pltpu.SMEM), vmem, vmem, vmem],
        out_specs=(vmem, vmem),
        compiler_params=pltpu.CompilerParams(vmem_limit_bytes=48 * 2**20),
        cost_estimate=cost(10),
    )(spans, queries, keys, values)


def head_backward(queries, keys, values, grads, spans):
    rows = queries.shape[0]
    step = min(256, rows)

    def kernel(spans_ref, q_ref, k_ref, v_ref, g_ref, dq_ref, dk_ref, dv_ref):
        dk_ref[...] = jnp.zeros(dk_ref.shape, FULL)
        dv_ref[...] = jnp.zeros(dv_ref.shape, FULL)

        @pl.loop(0, rows // step)
        def _(at):
            here = pl.ds(pl.multiple_of(at * step, step), step)
            allowed = allowed_block(at, step, keys.shape[0], spans_ref)
            block_rows, grad_rows = q_ref[here], g_ref[here]
            probs, _ = softmax_block(block_rows, k_ref[...], allowed)
            grad_probs = against(grad_rows, v_ref[...])
            delta_row = jnp.sum(probs * grad_probs, axis=-1, keepdims=True)
            grad_scores = (probs * (grad_probs - delta_row)).astype(LOW)
            dq_ref[here] = flat_dot(grad_scores, k_ref[...])
            dk_ref[...] += inner_rows(grad_scores, block_rows)
            dv_ref[...] += inner_rows(probs.astype(LOW), grad_rows)

    vmem = pl.BlockSpec(memory_space=pltpu.VMEM)
    return pl.pallas_call(
        kernel,
        out_shape=(jax.ShapeDtypeStruct(queries.shape, FULL),)
        + (jax.ShapeDtypeStruct(keys.shape, FULL),) * 2,
        in_specs=[pl.BlockSpec(memory_space=pltpu.SMEM)] + [vmem] * 4,
        out_specs=(vmem, vmem, vmem),
        compiler_params=pltpu.CompilerParams(vmem_limit_bytes=48 * 2**20),
        cost_estimate=cost(20),
    )(spans, queries, keys, values, grads)


def whole_norm(values_in, gain_vec):
    scale = lax.rsqrt(jnp.mean(values_in * values_in, axis=-1, keepdims=True) + EPS)
    return values_in * scale * gain_vec, scale


def whole_norm_backward(values_in, scale, gain_vec, grad_out):
    weighted = grad_out * gain_vec
    inner = jnp.mean(weighted * values_in, axis=-1, keepdims=True)
    return (
        scale * weighted - values_in * (scale * scale * scale) * inner,
        jnp.sum(grad_out * values_in * scale, axis=0),
    )


def turn(values_in, cos_tab, sin_tab):
    half_width = values_in.shape[-1] // 2
    one, two = values_in[:, :half_width], values_in[:, half_width:]
    return jnp.concatenate(
        [one * cos_tab - two * sin_tab, two * cos_tab + one * sin_tab], axis=1
    )


def turn_back(values_in, cos_tab, sin_tab):
    return turn(values_in, cos_tab, -sin_tab)


def swap_row(values_in, split, concat, tiled=True):
    return lax.all_to_all(values_in, "row", split, concat, tiled=tiled)


def line_device(
    activations,
    per_layer,
    cotangent,
    lengths,
    starts,
    w_query,
    m_query,
    v_query,
    key_value_weight,
    key_value_first_moment,
    key_value_second_moment,
    w_attend,
    m_attend,
    v_attend,
    w_gateup,
    m_gateup,
    v_gateup,
    w_down,
    m_down,
    v_down,
    w_left,
    m_left,
    v_left,
    w_right,
    m_right,
    v_right,
    w_pergate,
    m_pergate,
    v_pergate,
    w_perproj,
    m_perproj,
    v_perproj,
    w_gains,
    m_gains,
    v_gains,
    w_heads,
    m_heads,
    v_heads,
):
    rows_n = lax.axis_size("row")
    cols_n = lax.axis_size("col")
    data_n = lax.axis_size("dp")
    me = lax.axis_index("row")
    column = lax.axis_index("col")
    data_at = lax.axis_index("dp")
    half_tok, width_a = activations.shape
    tokens = half_tok * cols_n
    share = half_tok // rows_n
    quarter = tokens // rows_n
    width = width_a * rows_n

    heads_here = data_n
    qkv = lax.all_gather(
        jnp.concatenate([w_query, key_value_weight], axis=1).astype(LOW), "dp", axis=0
    )
    query_w = qkv[:, :, : w_query.shape[1]]
    kv_w = qkv[:, :, w_query.shape[1] :]
    key_w = lax.dynamic_index_in_dim(kv_w, column, 0, False)
    value_w = lax.dynamic_index_in_dim(kv_w, KEY_VALUE_HEADS + column, 0, False)
    attend_cols = w_attend.shape[1]
    attend_w = swap_row(
        w_attend.astype(LOW).reshape(rows_n, -1, attend_cols), 0, 1, False
    )
    attend_w = lax.all_gather(attend_w, "dp", axis=2).reshape(-1, width)
    gateup_w = swap_row(w_gateup.astype(LOW), 2, 1)
    ff_part = gateup_w.shape[2]
    gateup_w = lax.all_gather(gateup_w, "dp", axis=2, tiled=True)
    down_w = swap_row(
        w_down.astype(LOW).reshape(data_n, rows_n, ff_part, w_down.shape[1]), 1, 2, False
    )
    down_w = lax.all_gather(
        down_w.reshape(data_n * ff_part, rows_n, w_down.shape[1]), "dp", axis=2
    ).reshape(data_n * ff_part, width)
    smalls = (w_left, w_right, w_pergate, w_perproj)
    flat = jnp.concatenate([w.astype(LOW).reshape(-1) for w in smalls]).reshape(-1, 128)
    flat = lax.all_gather(lax.all_gather(lax.all_gather(flat, "dp"), "row"), "col")
    flat = flat.reshape(cols_n, rows_n, data_n, -1)
    cuts = []
    start = 0
    for w in smalls:
        cuts.append(flat[..., start : start + w.size].reshape((cols_n, rows_n, data_n) + w.shape))
        start += w.size
    left_w = cuts[0].transpose(1, 3, 0, 2, 4).reshape(width, -1)
    right_w = cuts[1].transpose(0, 3, 1, 2, 4).reshape(-1, width)
    pergate_w = cuts[2].transpose(1, 3, 0, 2, 4).reshape(width, -1)
    perproj_w = cuts[3].transpose(0, 3, 1, 2, 4).reshape(-1, width)

    inputs = swap_row(activations, 0, 1).astype(FULL)
    upstream = swap_row(cotangent, 0, 1).astype(FULL)
    extras = lax.all_gather(lax.all_gather(per_layer, "row"), "col", axis=2)
    extras = extras.reshape(tokens, -1)
    token_at = column * half_tok + me * share
    extras = lax.dynamic_slice_in_dim(extras, token_at, share, 0).astype(FULL)
    length = lax.dynamic_index_in_dim(lengths, data_at, 0, keepdims=True)
    piece_starts = lax.dynamic_index_in_dim(starts, data_at, 0, keepdims=False)
    spans = jnp.concatenate([length, piece_starts])
    gains_here = lax.dynamic_slice_in_dim(w_gains, 0, 1, 0)[0]
    gains = lax.all_gather(w_gains, "row", axis=1, tiled=True)

    acts = activations.astype(FULL)
    sums = jnp.sum(acts * acts, axis=1)
    sums = small_total(sums.reshape(-1, 128), ("row",), 0, 1).reshape(-1, 1)
    scale_here = lax.rsqrt(sums / MODEL_WIDTH + EPS)
    hidden_here = (acts * scale_here * gains_here).astype(LOW)
    spread_h = core_gather(hidden_here, 2).reshape(tokens, width_a)

    raw_q = [flat_dot(spread_h, query_w[k]).astype(LOW) for k in range(heads_here)]
    raw_k = flat_dot(spread_h, key_w).astype(LOW).reshape(rows_n, quarter, HEAD_WIDTH)
    raw_v = flat_dot(spread_h, value_w).astype(LOW).reshape(rows_n, quarter, HEAD_WIDTH)
    qkv_parts = jnp.concatenate([jnp.stack(raw_q), raw_k, raw_v], axis=1)
    qkv_raw = line_reduce(qkv_parts, 3, False, 55)
    query_raw = qkv_raw[:tokens]
    key_raw = qkv_raw[tokens : tokens + quarter]
    value_raw = qkv_raw[tokens + quarter :]
    query_gain = lax.dynamic_index_in_dim(w_heads, column * rows_n + me, 0, True)
    key_gain = w_heads[QUERY_HEADS :]
    all_cos, all_sin = rope_tables(jnp.arange(tokens, dtype=jnp.int32), HEAD_WIDTH)
    own_cos = lax.dynamic_slice_in_dim(all_cos, me * quarter, quarter, 0)
    own_sin = lax.dynamic_slice_in_dim(all_sin, me * quarter, quarter, 0)
    query_n, query_scale = whole_norm(query_raw, query_gain)
    queries = turn(query_n, all_cos, all_sin).astype(LOW)
    key_n, key_scale = whole_norm(key_raw, key_gain)
    value_n, value_scale = whole_norm(value_raw, 1.0)
    kv_here = jnp.concatenate([turn(key_n, own_cos, own_sin), value_n], axis=0).astype(LOW)
    kv_all = line_gather(kv_here, 4, False, 20)
    keys = kv_all[:, :quarter].reshape(tokens, HEAD_WIDTH)
    values = kv_all[:, quarter:].reshape(tokens, HEAD_WIDTH)
    attended, top = head_forward(queries, keys, values, spans)

    def shares(parts):
        return parts.astype(LOW).reshape(cols_n, rows_n, share, width)

    hidden, _ = whole_norm(inputs, gains[0])
    hidden_low = hidden.astype(LOW)
    middle = flat_dot(hidden_low, left_w).astype(LOW)
    right_raw = flat_dot(middle, right_w)
    right_n, scale_r = whole_norm(right_raw, gains[1])
    projected = line_reduce(shares(flat_dot(attended, attend_w)), 5, True, 45)
    proj_n, scale_p = whole_norm(projected, gains[2])
    mixture = ((inputs + proj_n) + (hidden + right_n)) * HALF_ROOT
    ffn_n, scale_f = whole_norm(mixture, gains[3])
    spread_f = line_gather(ffn_n.astype(LOW), 6, True, 40).reshape(tokens, width)
    gate_raw = flat_dot(spread_f, gateup_w[0])
    up_raw = flat_dot(spread_f, gateup_w[1])
    act = (jax.nn.gelu(gate_raw, approximate=True) * up_raw).astype(LOW)
    down_raw = line_reduce(shares(flat_dot(act, down_w)), 7, True, 45)
    down_n, scale_d = whole_norm(down_raw, gains[4])
    block_out = mixture + down_n
    out_low = block_out.astype(LOW)
    pgate = flat_dot(out_low, pergate_w)
    pact = (jax.nn.gelu(pgate, approximate=True) * extras).astype(LOW)
    perproj = flat_dot(pact, perproj_w)
    perproj_n, scale_pp = whole_norm(perproj, gains[5])
    result = swap_row((block_out + perproj_n).astype(LOW), 1, 0)

    gain_grads = [None] * 6
    d_perproj, gain_grads[5] = whole_norm_backward(perproj, scale_pp, gains[5], upstream)
    d_perproj = d_perproj.astype(LOW)
    dw_perproj = inner_rows(pact, d_perproj)
    d_pact = against(d_perproj, perproj_w)
    _, pullback = jax.vjp(lambda v: jax.nn.gelu(v, approximate=True), pgate)
    (d_pgate,) = pullback(d_pact * extras)
    d_pgate = d_pgate.astype(LOW)
    dw_pergate = inner_rows(out_low, d_pgate)
    d_out = upstream + against(d_pgate, pergate_w)
    d_down, gain_grads[4] = whole_norm_backward(down_raw, scale_d, gains[4], d_out)
    spread_d = line_gather(d_down.astype(LOW), 8, True, 40).reshape(tokens, width)
    d_act = against(spread_d, down_w)
    _, pullback = jax.vjp(
        lambda a, b: jax.nn.gelu(a, approximate=True) * b, gate_raw, up_raw
    )
    d_gate, d_up = pullback(d_act)
    d_gate, d_up = d_gate.astype(LOW), d_up.astype(LOW)
    d_ffn = against(d_gate, gateup_w[0]) + against(d_up, gateup_w[1])
    d_ffn = line_reduce(shares(d_ffn), 9, True, 45)
    dw_down = inner_rows(act, spread_d).astype(LOW)
    dw_gateup = jnp.stack(
        [inner_rows(spread_f, d_gate).astype(LOW), inner_rows(spread_f, d_up).astype(LOW)]
    )
    d_mix, gain_grads[3] = whole_norm_backward(mixture, scale_f, gains[3], d_ffn)
    d_half = (d_out + d_mix) * HALF_ROOT
    d_proj, gain_grads[2] = whole_norm_backward(projected, scale_p, gains[2], d_half)
    spread_p = line_gather(d_proj.astype(LOW), 10, True, 40).reshape(tokens, width)
    d_right, gain_grads[1] = whole_norm_backward(right_raw, scale_r, gains[1], d_half)
    d_right = d_right.astype(LOW)
    dw_right = inner_rows(middle, d_right)
    d_middle = against(d_right, right_w).astype(LOW)
    dw_left = inner_rows(hidden_low, d_middle)
    d_hidden_share = d_half + against(d_middle, left_w)
    both = jnp.stack([d_half, d_hidden_share]).astype(LOW)
    both = swap_row(both, 2, 1)
    d_attended = against(spread_p, attend_w).astype(LOW)
    dw_attend = inner_rows(attended, spread_p).astype(LOW)
    d_queries, d_keys, d_values = head_backward(queries, keys, values, d_attended, spans)
    kv_parts = jnp.concatenate(
        [
            d_keys.astype(LOW).reshape(rows_n, quarter, HEAD_WIDTH),
            d_values.astype(LOW).reshape(rows_n, quarter, HEAD_WIDTH),
        ],
        axis=1,
    )
    d_kv = line_reduce(kv_parts, 11, False, 20)
    d_q_raw, dg_query = whole_norm_backward(
        query_raw, query_scale, query_gain, turn_back(d_queries, all_cos, all_sin)
    )
    d_k_raw, dg_key = whole_norm_backward(
        key_raw, key_scale, key_gain, turn_back(d_kv[:quarter], own_cos, own_sin)
    )
    d_v_raw, _ = whole_norm_backward(value_raw, value_scale, 1.0, d_kv[quarter:])
    d_raw = jnp.concatenate([d_q_raw, d_k_raw, d_v_raw], axis=0).astype(LOW)
    spread_q = line_gather(d_raw, 12, False, 55)
    d_q_all = spread_q[:, :tokens]
    d_k_all = spread_q[:, tokens : tokens + quarter].reshape(tokens, HEAD_WIDTH)
    d_v_all = spread_q[:, tokens + quarter :].reshape(tokens, HEAD_WIDTH)
    d_hidden = against(d_k_all, key_w) + against(d_v_all, value_w)
    for k in range(heads_here):
        d_hidden = d_hidden + against(d_q_all[k], query_w[k])
    d_hidden = core_reduce(d_hidden.astype(LOW).reshape(cols_n, half_tok, width_a), 13)
    d_hidden = d_hidden + both[1].astype(FULL)
    weighted = d_hidden * gains_here
    inner = jnp.sum(weighted * acts, axis=1)
    inner = small_total(inner.reshape(-1, 128), ("row",), 0, 14).reshape(-1, 1) / MODEL_WIDTH
    grad_input = (
        both[0].astype(FULL)
        + scale_here * weighted
        - acts * (scale_here * scale_here * scale_here) * inner
    ).astype(LOW)
    gain_zero = jnp.sum(d_hidden * acts * scale_here, axis=0)

    dw_query = jnp.stack([inner_rows(spread_h, d_q_all[k]) for k in range(heads_here)])
    dw_key = inner_rows(spread_h, d_k_all)
    dw_value = inner_rows(spread_h, d_v_all)
    zero = jnp.zeros_like(dw_key)
    first = column == 0
    dw_kv = jnp.stack(
        [
            jnp.where(first, dw_key, zero),
            jnp.where(first, zero, dw_key),
            jnp.where(first, dw_value, zero),
            jnp.where(first, zero, dw_value),
        ]
    )
    g_qkv = lax.psum_scatter(
        jnp.concatenate([dw_query, dw_kv], axis=2).astype(LOW), "dp", scatter_dimension=0
    ).astype(FULL)
    g_query = g_qkv[:, : w_query.shape[1]]
    g_keyval = g_qkv[:, w_query.shape[1] :]
    g_keyval = g_keyval + lax.ppermute(g_keyval, "col", [(0, 1), (1, 0)])
    g_attend = lax.psum_scatter(
        dw_attend.reshape(HEAD_WIDTH, rows_n, data_n, attend_cols), "dp", scatter_dimension=2
    )
    g_attend = swap_row(g_attend, 1, 0, False).reshape(w_attend.shape).astype(FULL)
    g_gateup = lax.psum_scatter(dw_gateup, "dp", scatter_dimension=2, tiled=True)
    g_gateup = swap_row(g_gateup, 1, 2).astype(FULL)
    g_down = lax.psum_scatter(
        dw_down.reshape(data_n * ff_part, rows_n, data_n, w_down.shape[1]),
        "dp",
        scatter_dimension=2,
    )
    g_down = swap_row(g_down.reshape(data_n, ff_part, rows_n, w_down.shape[1]), 2, 1, False)
    g_down = g_down.reshape(w_down.shape).astype(FULL)

    def to_shards(grad, rows_first):
        if rows_first:
            cut = grad.reshape(rows_n, width_a, cols_n, data_n, -1).transpose(2, 0, 3, 1, 4)
        else:
            cut = grad.reshape(cols_n, -1, rows_n, data_n, width_a // data_n).transpose(0, 2, 3, 1, 4)
        return cut.astype(LOW).reshape(cols_n, rows_n, data_n, -1)

    flat_grads = jnp.concatenate(
        [
            to_shards(dw_left, True),
            to_shards(dw_right, False),
            to_shards(dw_pergate, True),
            to_shards(dw_perproj, False),
        ],
        axis=3,
    ).reshape(cols_n, rows_n, data_n, -1, 128)
    flat_grads = lax.psum_scatter(flat_grads, "col", scatter_dimension=0)
    flat_grads = lax.psum_scatter(flat_grads, "row", scatter_dimension=0)
    flat_grads = lax.psum_scatter(flat_grads, "dp", scatter_dimension=0).astype(FULL).reshape(-1)
    small_grads = []
    start = 0
    for w in smalls:
        small_grads.append(flat_grads[start : start + w.size].reshape(w.shape))
        start += w.size
    g_left, g_right, g_pergate, g_perproj = small_grads

    gain_full = jnp.stack(
        [
            lax.dynamic_update_slice_in_dim(
                jnp.zeros((width,), FULL), gain_zero, me * width_a, 0
            )
        ]
        + gain_grads[1:]
    )
    head_full = lax.dynamic_update_slice_in_dim(
        jnp.zeros((QUERY_HEADS + 1, HEAD_WIDTH), FULL), dg_query[None], column * rows_n + me, 0
    )
    head_full = head_full.at[QUERY_HEADS].add(dg_key)
    logit_row = lax.dynamic_update_slice_in_dim(
        jnp.full((128,), NEGATIVE, FULL), top[0, :1], column * rows_n + me, 0
    )
    gain_rows = gain_full.size // 128
    head_rows = head_full.size // 128
    pad_rows = -(gain_rows + head_rows) % 8
    small = jnp.concatenate(
        [
            gain_full.reshape(-1, 128),
            head_full.reshape(-1, 128),
            jnp.zeros((pad_rows, 128), FULL),
            jnp.broadcast_to(logit_row[None], (8, 128)),
        ]
    )
    small = small_total(small, ("col", "row", "dp"), 8, 15)
    gain_sum = small[:gain_rows].reshape(6, width)
    head_sum = small[gain_rows : gain_rows + head_rows].reshape(QUERY_HEADS + 1, HEAD_WIDTH)
    logit_top = small[-1, :QUERY_HEADS]
    g_gains = lax.dynamic_slice_in_dim(gain_sum, me * width_a, width_a, 1)
    squares = jnp.where(first, jnp.sum(g_keyval * g_keyval), 0.0)
    for gradient in (g_query, g_attend, g_gateup, g_down, g_left, g_right, g_pergate, g_perproj):
        squares = squares + jnp.sum(gradient * gradient)
    squares = small_total(jnp.broadcast_to(squares, (8, 128)), ("col", "row", "dp"), 0, 16)[0, 0]
    squares = squares + jnp.sum(gain_sum * gain_sum) + jnp.sum(head_sum * head_sum)
    grad_norm = jnp.sqrt(squares)
    clip_scale = CLIP / jnp.maximum(grad_norm, CLIP)
    scale_factors = LOGIT_CAP / jnp.maximum(logit_top, LOGIT_CAP)
    weights = (
        w_query,
        key_value_weight,
        w_attend,
        w_gateup,
        w_down,
        w_left,
        w_right,
        w_pergate,
        w_perproj,
        w_gains,
        w_heads,
    )
    moments = (
        m_query,
        key_value_first_moment,
        m_attend,
        m_gateup,
        m_down,
        m_left,
        m_right,
        m_pergate,
        m_perproj,
        m_gains,
        m_heads,
    )
    seconds = (
        v_query,
        key_value_second_moment,
        v_attend,
        v_gateup,
        v_down,
        v_left,
        v_right,
        v_pergate,
        v_perproj,
        v_gains,
        v_heads,
    )
    gradients = (
        g_query,
        g_keyval,
        g_attend,
        g_gateup,
        g_down,
        g_left,
        g_right,
        g_pergate,
        g_perproj,
        g_gains,
        head_sum,
    )
    step_rates = (
        MODEL_WIDTH ** (-0.5),
        MODEL_WIDTH ** (-0.5),
        (QUERY_HEADS * HEAD_WIDTH) ** (-0.5),
        MODEL_WIDTH ** (-0.5),
        FF ** (-0.5),
        MODEL_WIDTH ** (-0.5),
        RANK ** (-0.5),
        MODEL_WIDTH ** (-0.5),
        PLD ** (-0.5),
        GAIN_RATE,
        HEAD_RATE,
    )
    decays = (DECAY, DECAY, DECAY, DECAY, DECAY, DECAY, DECAY, DECAY, DECAY, 0.0, 0.0)
    updated = [
        adamw_step(
            weights[k], moments[k], seconds[k], gradients[k] * clip_scale, step_rates[k], decays[k]
        )
        for k in range(11)
    ]
    head_scale = jnp.sqrt(scale_factors)
    q_width = w_query.shape[1]
    q_head = (
        (column * data_n + data_at) * q_width + jnp.arange(q_width, dtype=jnp.int32)
    ) // HEAD_WIDTH
    q_factor = jnp.sum(
        jnp.where(
            q_head[:, None] == jnp.arange(QUERY_HEADS, dtype=jnp.int32)[None, :],
            head_scale[None, :],
            0.0,
        ),
        axis=1,
    )
    new_query = updated[0][2] * q_factor[None, :]
    kv_width = key_value_weight.shape[1]
    key_value_index = data_at * kv_width + jnp.arange(kv_width, dtype=jnp.int32)
    key_value_scale = jnp.sqrt(
        jnp.min(scale_factors.reshape(KEY_VALUE_HEADS, QUERY_HEADS // KEY_VALUE_HEADS), axis=1)
    )
    key_value_choice = jnp.sum(
        jnp.where(
            (key_value_index // HEAD_WIDTH)[:, None]
            == jnp.arange(KEY_VALUE_HEADS, dtype=jnp.int32)[None, :],
            key_value_scale[None, :],
            0.0,
        ),
        axis=1,
    )
    key_value_factor = jnp.where(
        key_value_index < KEY_VALUE_HEADS * HEAD_WIDTH, key_value_choice, 1.0
    )
    new_keyval = updated[1][2] * key_value_factor[None, :]
    return (
        result,
        grad_input,
        grad_norm,
        scale_factors,
        updated[0][0],
        updated[0][1],
        new_query,
        updated[1][0],
        updated[1][1],
        new_keyval,
        updated[2][0],
        updated[2][1],
        updated[2][2],
        updated[3][0],
        updated[3][1],
        updated[3][2],
        updated[4][0],
        updated[4][1],
        updated[4][2],
        updated[5][0],
        updated[5][1],
        updated[5][2],
        updated[6][0],
        updated[6][1],
        updated[6][2],
        updated[7][0],
        updated[7][1],
        updated[7][2],
        updated[8][0],
        updated[8][1],
        updated[8][2],
        updated[9][0],
        updated[9][1],
        updated[9][2],
        updated[10][0],
        updated[10][1],
        updated[10][2],
    )


def per_device(
    activations,
    per_layer,
    cotangent,
    lengths,
    starts,
    w_query,
    m_query,
    v_query,
    key_value_weight,
    key_value_first_moment,
    key_value_second_moment,
    w_attend,
    m_attend,
    v_attend,
    w_gateup,
    m_gateup,
    v_gateup,
    w_down,
    m_down,
    v_down,
    w_left,
    m_left,
    v_left,
    w_right,
    m_right,
    v_right,
    w_pergate,
    m_pergate,
    v_pergate,
    w_perproj,
    m_perproj,
    v_perproj,
    w_gains,
    m_gains,
    v_gains,
    w_heads,
    m_heads,
    v_heads,
):
    row_devs = lax.axis_size("row")
    col_devs = lax.axis_size("col")
    data_devs = lax.axis_size("dp")
    row_place = lax.axis_index("row")
    column_place = lax.axis_index("col")
    data_at = lax.axis_index("dp")
    bf16 = jnp.bfloat16
    single_float = jnp.float32
    query_b, keyval_b, attend_b, gateup_b, down_b, left_b, right_b, pergate_b, perproj_b = (
        lax.all_gather(w_query.astype(bf16), "dp", axis=1, tiled=True),
        lax.all_gather(key_value_weight.astype(bf16), "dp", axis=1, tiled=True),
        lax.all_gather(w_attend.astype(bf16), "dp", axis=1, tiled=True),
        lax.all_gather(w_gateup.astype(bf16), "dp", axis=2, tiled=True),
        lax.all_gather(w_down.astype(bf16), "dp", axis=1, tiled=True),
        lax.all_gather(w_left.astype(bf16), "dp", axis=1, tiled=True),
        lax.all_gather(w_right.astype(bf16), "dp", axis=1, tiled=True),
        lax.all_gather(w_pergate.astype(bf16), "dp", axis=1, tiled=True),
        lax.all_gather(w_perproj.astype(bf16), "dp", axis=1, tiled=True),
    )
    inputs = activations.astype(single_float)
    tok_a, width_a = inputs.shape
    grouped_rows = tok_a * col_devs
    token_batch = grouped_rows // row_devs
    q_cols = query_b.shape[1]
    l_cols = left_b.shape[1]
    kv_cols = keyval_b.shape[1]
    ff_here = gateup_b.shape[2]
    local_heads = q_cols // HEAD_WIDTH
    length = lax.dynamic_index_in_dim(lengths, data_at, 0, keepdims=False)
    piece_starts = lax.dynamic_index_in_dim(starts, data_at, 0, keepdims=False)
    own_places = row_place * token_batch + jnp.arange(token_batch, dtype=jnp.int32)
    all_places = jnp.arange(grouped_rows, dtype=jnp.int32)
    own_cos, own_sin = rope_tables(own_places, HEAD_WIDTH)
    query_gains = lax.dynamic_slice_in_dim(w_heads, column_place * local_heads, local_heads, 0)
    key_gain = w_heads[QUERY_HEADS]
    hidden, scale_in = norm_forward(inputs, w_gains[0])
    hidden_b = hidden.astype(bf16)
    spread_h = spread_col(hidden_b)
    type_one = reduce_row(flat_dot(spread_h, jnp.concatenate([query_b, left_b], axis=1)))
    key_raw_all = lax.psum(flat_dot(spread_h, keyval_b), "row")
    all_cos, all_sin = rope_tables(all_places, HEAD_WIDTH)
    key_value_whole = key_form(key_raw_all, key_gain, all_cos, all_sin).astype(bf16)
    key_raw = lax.dynamic_slice_in_dim(key_raw_all, row_place * token_batch, token_batch, 0)
    query_raw = type_one[:, :q_cols]
    middle_b = type_one[:, q_cols : q_cols + l_cols].astype(bf16)
    queries = query_form(query_raw, query_gains, own_cos, own_sin).astype(bf16)
    key_value_heads = (column_place * local_heads + jnp.arange(local_heads, dtype=jnp.int32)) // (
        QUERY_HEADS // KEY_VALUE_HEADS
    )
    every_key = key_value_whole[:, : KEY_VALUE_HEADS * HEAD_WIDTH].reshape(
        grouped_rows, KEY_VALUE_HEADS, HEAD_WIDTH
    )
    every_value = key_value_whole[:, KEY_VALUE_HEADS * HEAD_WIDTH :].reshape(
        grouped_rows, KEY_VALUE_HEADS, HEAD_WIDTH
    )
    key_sel = jnp.take(every_key, key_value_heads, axis=1)
    value_sel = jnp.take(every_value, key_value_heads, axis=1)
    attended, block_peaks, block_totals = attention_forward(
        queries, key_sel, value_sel, own_places, all_places, length, piece_starts
    )
    attended_b = attended.reshape(token_batch, q_cols).astype(bf16)
    joined_b = jnp.concatenate([attended_b, middle_b], axis=1)
    spread_j = spread_row(joined_b)
    type_two = reduce_col(
        jnp.concatenate(
            [flat_dot(spread_j[:, :q_cols], attend_b), flat_dot(spread_j[:, q_cols:], right_b)],
            axis=1,
        )
    )
    projected = type_two[:, :width_a]
    right_raw = type_two[:, width_a:]
    right_n, scale_r = norm_forward(right_raw, w_gains[1])
    laurel = hidden + right_n
    proj_n, scale_p = norm_forward(projected, w_gains[2])
    gated_sum = inputs + proj_n
    mixture = (gated_sum + laurel) * HALF_ROOT
    ffn_n, scale_f = norm_forward(mixture, w_gains[3])
    ffn_b = ffn_n.astype(bf16)
    spread_f = spread_col(ffn_b)
    gateup_pair = jnp.concatenate([gateup_b[0], gateup_b[1]], axis=1)
    gate_up = reduce_row(flat_dot(spread_f, gateup_pair))
    gate_raw = gate_up[:, :ff_here]
    up_raw = gate_up[:, ff_here:]
    act_b = (jax.nn.gelu(gate_raw, approximate=True) * up_raw).astype(bf16)
    spread_a = spread_row(act_b)
    down_raw = reduce_col(flat_dot(spread_a, down_b))
    down_n, scale_d = norm_forward(down_raw, w_gains[4])
    block_out = mixture + down_n
    out_b = block_out.astype(bf16)
    spread_o = spread_col(out_b)
    pgate = reduce_row(flat_dot(spread_o, pergate_b))
    extras = per_layer.astype(single_float)
    pact_b = (jax.nn.gelu(pgate, approximate=True) * extras).astype(bf16)
    spread_p = spread_row(pact_b)
    perproj = reduce_col(flat_dot(spread_p, perproj_b))
    perproj_n, scale_pp = norm_forward(perproj, w_gains[5])
    result = (block_out + perproj_n).astype(bf16)
    upstream = cotangent.astype(single_float)
    gain_grads = [None, None, None, None, None, None]
    d_perproj, gain_grads[5] = norm_backward(perproj, scale_pp, w_gains[5], upstream)
    grads_five = grads_col(d_perproj.astype(bf16))
    dw_perproj = inner_rows(spread_p, grads_five)
    d_pact = reduce_row(against(grads_five, perproj_b))
    gelu_out, pullback = jax.vjp(lambda v: jax.nn.gelu(v, approximate=True), pgate)
    (d_pgate,) = pullback(d_pact * extras)
    grads_four = grads_row(d_pgate.astype(bf16))
    dw_pergate = inner_rows(spread_o, grads_four)
    d_out = upstream + reduce_col(against(grads_four, pergate_b))
    d_down, gain_grads[4] = norm_backward(down_raw, scale_d, w_gains[4], d_out)
    grads_three = grads_col(d_down.astype(bf16))
    dw_down = inner_rows(spread_a, grads_three)
    d_act = reduce_row(against(grads_three, down_b))
    act_out, pullback = jax.vjp(lambda a, b: jax.nn.gelu(a, approximate=True) * b, gate_raw, up_raw)
    d_gate, d_up = pullback(d_act)
    local_two = jnp.concatenate([d_gate, d_up], axis=1).astype(bf16)
    grads_two = grads_row(local_two)
    dw_gateup = jnp.stack(
        [inner_rows(spread_f, grads_two[:, :ff_here]), inner_rows(spread_f, grads_two[:, ff_here:])]
    )
    d_ffn = reduce_col(
        against(grads_two[:, :ff_here], gateup_b[0]) + against(grads_two[:, ff_here:], gateup_b[1])
    )
    d_mix_norm, gain_grads[3] = norm_backward(mixture, scale_f, w_gains[3], d_ffn)
    d_half = (d_out + d_mix_norm) * HALF_ROOT
    d_proj, gain_grads[2] = norm_backward(projected, scale_p, w_gains[2], d_half)
    d_right, gain_grads[1] = norm_backward(right_raw, scale_r, w_gains[1], d_half)
    grads_one = grads_col(jnp.concatenate([d_proj, d_right], axis=1).astype(bf16))
    dw_attend = inner_rows(spread_j[:, :q_cols], grads_one[:, :width_a])
    dw_right = inner_rows(spread_j[:, q_cols:], grads_one[:, width_a:])
    d_joined = reduce_row(
        jnp.concatenate(
            [against(grads_one[:, :width_a], attend_b), against(grads_one[:, width_a:], right_b)],
            axis=1,
        )
    )
    d_attended = d_joined[:, :q_cols].astype(bf16).reshape(token_batch, local_heads, HEAD_WIDTH)
    d_middle = d_joined[:, q_cols:]
    d_queries, d_key_sel, d_value_sel = attention_backward(
        queries,
        key_sel,
        value_sel,
        d_attended,
        block_peaks,
        block_totals,
        own_places,
        all_places,
        length,
        piece_starts,
    )
    single_hot_mask = (
        key_value_heads[:, None] == jnp.arange(KEY_VALUE_HEADS, dtype=jnp.int32)[None, :]
    ).astype(single_float)
    key_gradient = jnp.sum(d_key_sel[:, :, None, :] * single_hot_mask[None, :, :, None], axis=1)
    value_gradient = jnp.sum(d_value_sel[:, :, None, :] * single_hot_mask[None, :, :, None], axis=1)
    key_gradient, value_gradient = lax.psum((key_gradient, value_gradient), ("row", "col"))
    local_key_gradient = lax.dynamic_slice_in_dim(
        key_gradient, row_place * token_batch, token_batch, 0
    ).reshape(token_batch, KEY_VALUE_HEADS * HEAD_WIDTH)
    local_value_gradient = lax.dynamic_slice_in_dim(
        value_gradient, row_place * token_batch, token_batch, 0
    ).reshape(token_batch, KEY_VALUE_HEADS * HEAD_WIDTH)
    query_out, pullback = jax.vjp(
        lambda r, g: query_form(r, g, own_cos, own_sin), query_raw, query_gains
    )
    d_query_raw, dg_query = pullback(d_queries)
    key_tile = jnp.broadcast_to(key_gain, (token_batch, 1, HEAD_WIDTH))
    key_out, pullback = jax.vjp(lambda r, g: key_form(r, g, own_cos, own_sin), key_raw, key_tile)
    d_key_raw, dg_key_rows = pullback(
        jnp.concatenate([local_key_gradient, local_value_gradient], axis=1)
    )
    slice_rows = token_batch // col_devs
    dg_key = jnp.sum(
        lax.dynamic_slice_in_dim(dg_key_rows, column_place * slice_rows, slice_rows, 0), axis=(0, 1)
    )
    grads_zero = grads_row(jnp.concatenate([d_query_raw, d_middle, d_key_raw], axis=1).astype(bf16))
    dw_query = inner_rows(spread_h, grads_zero[:, :q_cols])
    dw_left = inner_rows(spread_h, grads_zero[:, q_cols : q_cols + l_cols])
    key_grad_rows = grads_zero[:, q_cols + l_cols :]
    dw_keyval = inner_rows(spread_h, key_grad_rows)
    slab_width = kv_cols // col_devs
    d_hidden = reduce_col(
        against(grads_zero[:, :q_cols], query_b)
        + against(grads_zero[:, q_cols : q_cols + l_cols], left_b)
        + against(
            lax.dynamic_slice_in_dim(key_grad_rows, column_place * slab_width, slab_width, 1),
            lax.dynamic_slice_in_dim(keyval_b, column_place * slab_width, slab_width, 1),
        )
    )
    d_in, gain_grads[0] = norm_backward(inputs, scale_in, w_gains[0], d_hidden + d_half)
    grad_input = (d_half + d_in).astype(bf16)
    g_query, g_keyval, g_attend, g_gateup, g_down, g_left, g_right, g_pergate, g_perproj = (
        lax.psum_scatter(dw_query, "dp", scatter_dimension=1, tiled=True),
        lax.psum_scatter(dw_keyval, "dp", scatter_dimension=1, tiled=True),
        lax.psum_scatter(dw_attend, "dp", scatter_dimension=1, tiled=True),
        lax.psum_scatter(dw_gateup, "dp", scatter_dimension=2, tiled=True),
        lax.psum_scatter(dw_down, "dp", scatter_dimension=1, tiled=True),
        lax.psum_scatter(dw_left, "dp", scatter_dimension=1, tiled=True),
        lax.psum_scatter(dw_right, "dp", scatter_dimension=1, tiled=True),
        lax.psum_scatter(dw_pergate, "dp", scatter_dimension=1, tiled=True),
        lax.psum_scatter(dw_perproj, "dp", scatter_dimension=1, tiled=True),
    )
    gain_full = lax.dynamic_update_slice_in_dim(
        jnp.zeros((6, MODEL_WIDTH), single_float), jnp.stack(gain_grads), row_place * width_a, 1
    )
    head_full = lax.dynamic_update_slice_in_dim(
        jnp.zeros((QUERY_HEADS + 1, HEAD_WIDTH), single_float),
        dg_query,
        column_place * local_heads,
        0,
    )
    head_full = head_full.at[QUERY_HEADS].add(dg_key)
    logit_here = lax.dynamic_update_slice_in_dim(
        jnp.full((QUERY_HEADS,), NEGATIVE, single_float),
        jnp.max(block_peaks, axis=(0, 2)),
        column_place * local_heads,
        0,
    )

    def combine(left_part, right_part):
        return (
            left_part[0] + right_part[0],
            left_part[1] + right_part[1],
            jnp.maximum(left_part[2], right_part[2]),
        )

    gain_sum, head_sum, logit_top = joined(
        (gain_full, head_full, logit_here), ("dp", "row", "col"), combine
    )
    g_gains = lax.dynamic_slice_in_dim(gain_sum, row_place * width_a, width_a, 1)
    lead_device = (column_place == 0) & (data_at == 0)
    solo_device = lead_device & (row_place == 0)
    squares = jnp.float32(0.0)
    for gradient in (g_query, g_attend, g_gateup, g_down, g_left, g_right, g_pergate, g_perproj):
        squares = squares + jnp.sum(gradient * gradient)
    squares = squares + jnp.where(column_place == 0, jnp.sum(g_keyval * g_keyval), 0.0)
    squares = squares + jnp.where(lead_device, jnp.sum(g_gains * g_gains), 0.0)
    squares = squares + jnp.where(solo_device, jnp.sum(head_sum * head_sum), 0.0)
    grad_norm = jnp.sqrt(lax.psum(squares, ("dp", "row", "col")))
    clip_scale = CLIP / jnp.maximum(grad_norm, CLIP)
    scale_factors = LOGIT_CAP / jnp.maximum(logit_top, LOGIT_CAP)
    weights = (
        w_query,
        key_value_weight,
        w_attend,
        w_gateup,
        w_down,
        w_left,
        w_right,
        w_pergate,
        w_perproj,
        w_gains,
        w_heads,
    )
    moments = (
        m_query,
        key_value_first_moment,
        m_attend,
        m_gateup,
        m_down,
        m_left,
        m_right,
        m_pergate,
        m_perproj,
        m_gains,
        m_heads,
    )
    seconds = (
        v_query,
        key_value_second_moment,
        v_attend,
        v_gateup,
        v_down,
        v_left,
        v_right,
        v_pergate,
        v_perproj,
        v_gains,
        v_heads,
    )
    gradients = (
        g_query,
        g_keyval,
        g_attend,
        g_gateup,
        g_down,
        g_left,
        g_right,
        g_pergate,
        g_perproj,
        g_gains,
        head_sum,
    )
    step_rates = (
        MODEL_WIDTH ** (-0.5),
        MODEL_WIDTH ** (-0.5),
        (QUERY_HEADS * HEAD_WIDTH) ** (-0.5),
        MODEL_WIDTH ** (-0.5),
        FF ** (-0.5),
        MODEL_WIDTH ** (-0.5),
        RANK ** (-0.5),
        MODEL_WIDTH ** (-0.5),
        PLD ** (-0.5),
        GAIN_RATE,
        HEAD_RATE,
    )
    decays = (DECAY, DECAY, DECAY, DECAY, DECAY, DECAY, DECAY, DECAY, DECAY, 0.0, 0.0)
    updated = [
        adamw_step(
            weights[k], moments[k], seconds[k], gradients[k] * clip_scale, step_rates[k], decays[k]
        )
        for k in range(11)
    ]
    head_scale = jnp.sqrt(scale_factors)
    q_width = w_query.shape[1]
    q_head = (
        (column_place * data_devs + data_at) * q_width + jnp.arange(q_width, dtype=jnp.int32)
    ) // HEAD_WIDTH
    q_factor = jnp.sum(
        jnp.where(
            q_head[:, None] == jnp.arange(QUERY_HEADS, dtype=jnp.int32)[None, :],
            head_scale[None, :],
            0.0,
        ),
        axis=1,
    )
    new_query = updated[0][2] * q_factor[None, :]
    kv_width = key_value_weight.shape[1]
    key_value_index = data_at * kv_width + jnp.arange(kv_width, dtype=jnp.int32)
    key_value_scale = jnp.sqrt(
        jnp.min(scale_factors.reshape(KEY_VALUE_HEADS, QUERY_HEADS // KEY_VALUE_HEADS), axis=1)
    )
    key_value_choice = jnp.sum(
        jnp.where(
            (key_value_index // HEAD_WIDTH)[:, None]
            == jnp.arange(KEY_VALUE_HEADS, dtype=jnp.int32)[None, :],
            key_value_scale[None, :],
            0.0,
        ),
        axis=1,
    )
    key_value_factor = jnp.where(
        key_value_index < KEY_VALUE_HEADS * HEAD_WIDTH, key_value_choice, 1.0
    )
    new_keyval = updated[1][2] * key_value_factor[None, :]
    return (
        result,
        grad_input,
        grad_norm,
        scale_factors,
        updated[0][0],
        updated[0][1],
        new_query,
        updated[1][0],
        updated[1][1],
        new_keyval,
        updated[2][0],
        updated[2][1],
        updated[2][2],
        updated[3][0],
        updated[3][1],
        updated[3][2],
        updated[4][0],
        updated[4][1],
        updated[4][2],
        updated[5][0],
        updated[5][1],
        updated[5][2],
        updated[6][0],
        updated[6][1],
        updated[6][2],
        updated[7][0],
        updated[7][1],
        updated[7][2],
        updated[8][0],
        updated[8][1],
        updated[8][2],
        updated[9][0],
        updated[9][1],
        updated[9][2],
        updated[10][0],
        updated[10][1],
        updated[10][2],
    )


def solution(mesh):
    placed = (
        P(("dp", "col"), "row"),
        P(("dp", "row"), "col"),
        P(("dp", "col"), "row"),
        P(),
        P(),
        P("row", ("col", "dp")),
        P("row", ("col", "dp")),
        P("row", ("col", "dp")),
        P("row", "dp"),
        P("row", "dp"),
        P("row", "dp"),
        P("col", ("row", "dp")),
        P("col", ("row", "dp")),
        P("col", ("row", "dp")),
        P(None, "row", ("col", "dp")),
        P(None, "row", ("col", "dp")),
        P(None, "row", ("col", "dp")),
        P("col", ("row", "dp")),
        P("col", ("row", "dp")),
        P("col", ("row", "dp")),
        P("row", ("col", "dp")),
        P("row", ("col", "dp")),
        P("row", ("col", "dp")),
        P("col", ("row", "dp")),
        P("col", ("row", "dp")),
        P("col", ("row", "dp")),
        P("row", ("col", "dp")),
        P("row", ("col", "dp")),
        P("row", ("col", "dp")),
        P("col", ("row", "dp")),
        P("col", ("row", "dp")),
        P("col", ("row", "dp")),
        P(None, "row"),
        P(None, "row"),
        P(None, "row"),
        P(),
        P(),
        P(),
    )
    fits = (
        mesh.shape["col"] == KEY_VALUE_HEADS
        and mesh.shape["row"] * KEY_VALUE_HEADS == QUERY_HEADS
        and mesh.shape["dp"] == mesh.shape["row"]
    )
    return jax.shard_map(
        line_device if fits else per_device,
        mesh=mesh,
        in_specs=placed,
        out_specs=(
            P(("dp", "col"), "row"),
            P(("dp", "col"), "row"),
            P(),
            P(),
            P("row", ("col", "dp")),
            P("row", ("col", "dp")),
            P("row", ("col", "dp")),
            P("row", "dp"),
            P("row", "dp"),
            P("row", "dp"),
            P("col", ("row", "dp")),
            P("col", ("row", "dp")),
            P("col", ("row", "dp")),
            P(None, "row", ("col", "dp")),
            P(None, "row", ("col", "dp")),
            P(None, "row", ("col", "dp")),
            P("col", ("row", "dp")),
            P("col", ("row", "dp")),
            P("col", ("row", "dp")),
            P("row", ("col", "dp")),
            P("row", ("col", "dp")),
            P("row", ("col", "dp")),
            P("col", ("row", "dp")),
            P("col", ("row", "dp")),
            P("col", ("row", "dp")),
            P("row", ("col", "dp")),
            P("row", ("col", "dp")),
            P("row", ("col", "dp")),
            P("col", ("row", "dp")),
            P("col", ("row", "dp")),
            P("col", ("row", "dp")),
            P(None, "row"),
            P(None, "row"),
            P(None, "row"),
            P(),
            P(),
            P(),
        ),
        check_vma=False,
    )
```

```python
import jax
import jax.numpy as jnp
from jax import lax
from jax.experimental import pallas as pl
from jax.experimental.pallas import tpu as pltpu
from jax.sharding import PartitionSpec as P

MODEL_WIDTH = 2048
QUERY_HEADS = 8
KEY_VALUE_HEADS = 2
HEAD_WIDTH = 256
FF = 8192
RANK = 64
PLD = 256
IMG = 256
STEP = 10


EPS = 1e-06
ROPE_BASE = 1000000.0
BETA_ONE = 0.5
BETA_TWO = 0.5
ADAM_EPS = 1e-08
DECAY = 0.01
CLIP = 1.0
LOGIT_CAP = 4.0
GAIN_RATE = 0.6
HEAD_RATE = 0.1
HALF_ROOT = 0.7071067811865476
NEGATIVE = -1e30


def joined(part, axis, combine):
    gathered = jax.tree.map(lambda a: lax.all_gather(a, axis), part)

    def take(source):
        return jax.tree.map(lambda a: lax.dynamic_index_in_dim(a, source, 0, False), gathered)

    return lax.fori_loop(
        1, lax.axis_size(axis), lambda source, state: combine(state, take(source)), take(0)
    )


def row_total(values_in):
    return lax.psum(values_in, "row")


def spread_col(values_in):
    return lax.all_gather(values_in, "col", axis=0, tiled=True)


def reduce_row(values_in):
    return lax.psum_scatter(values_in, "row", scatter_dimension=0, tiled=True)


def spread_row(values_in):
    return lax.all_gather(values_in, "row", axis=0, tiled=True)


def reduce_col(values_in):
    return lax.psum_scatter(values_in, "col", scatter_dimension=0, tiled=True)


def grads_col(values_in):
    return lax.all_gather(values_in, "col", axis=0, tiled=True)


def grads_row(values_in):
    return lax.all_gather(values_in, "row", axis=0, tiled=True)


def inner_rows(left_mat, right_mat):
    return lax.dot_general(
        left_mat, right_mat, (((0,), (0,)), ((), ())), preferred_element_type=jnp.float32
    )


def against(grad_mat, weight_mat):
    return lax.dot_general(
        grad_mat, weight_mat, (((1,), (1,)), ((), ())), preferred_element_type=jnp.float32
    )


def flat_dot(left_mat, right_mat):
    return jnp.dot(left_mat, right_mat, preferred_element_type=jnp.float32)


def norm_forward(values_in, gain_vec):
    total_sq = row_total(jnp.sum(values_in * values_in, axis=-1, keepdims=True))
    norm_scale = lax.rsqrt(total_sq / MODEL_WIDTH + EPS)
    return (values_in * norm_scale * gain_vec, norm_scale)


def norm_backward(values_in, norm_scale, gain_vec, grad_out):
    weighted = grad_out * gain_vec
    inner_sum = row_total(jnp.sum(weighted * values_in, axis=-1, keepdims=True))
    grad_in = norm_scale * weighted - values_in * (norm_scale * norm_scale * norm_scale) * (
        inner_sum / MODEL_WIDTH
    )
    return (grad_in, jnp.sum(grad_out * values_in * norm_scale, axis=0))


def norm_rows(values_in, gain_vec):
    return (
        values_in
        * lax.rsqrt(jnp.mean(values_in * values_in, axis=-1, keepdims=True) + EPS)
        * gain_vec
    )


def rope_tables(places, feat_width):
    half_width = feat_width // 2
    powers = jnp.arange(half_width, dtype=jnp.int32).astype(jnp.float32) * (2.0 / feat_width)
    frequency = jnp.power(jnp.float32(ROPE_BASE), -powers)
    angles = places.astype(jnp.float32)[:, None] * frequency[None, :]
    return (jnp.cos(angles), jnp.sin(angles))


def rotate(values_in, cos_tab, sin_tab):
    half_width = values_in.shape[-1] // 2
    part_one = values_in[..., :half_width]
    part_two = values_in[..., half_width:]
    cos_row = cos_tab[:, None, :]
    sin_row = sin_tab[:, None, :]
    return jnp.concatenate(
        [part_one * cos_row - part_two * sin_row, part_two * cos_row + part_one * sin_row], axis=-1
    )


def query_form(unscaled_rows, gain_rows, cos_tab, sin_tab):
    shaped = unscaled_rows.reshape(unscaled_rows.shape[0], gain_rows.shape[0], HEAD_WIDTH)
    return rotate(norm_rows(shaped, gain_rows[None]), cos_tab, sin_tab)


def key_form(unscaled_rows, gain_vec, cos_tab, sin_tab):
    count_of_rows = unscaled_rows.shape[0]
    key_rows = unscaled_rows[:, : KEY_VALUE_HEADS * HEAD_WIDTH].reshape(
        count_of_rows, KEY_VALUE_HEADS, HEAD_WIDTH
    )
    value_rows = unscaled_rows[:, KEY_VALUE_HEADS * HEAD_WIDTH :].reshape(
        count_of_rows, KEY_VALUE_HEADS, HEAD_WIDTH
    )
    key_rows = rotate(norm_rows(key_rows, gain_vec), cos_tab, sin_tab)
    value_rows = norm_rows(value_rows, 1.0)
    return jnp.concatenate(
        [
            key_rows.reshape(count_of_rows, KEY_VALUE_HEADS * HEAD_WIDTH),
            value_rows.reshape(count_of_rows, KEY_VALUE_HEADS * HEAD_WIDTH),
        ],
        axis=1,
    )


def piece_of(places, starts):
    inside = (places[:, None] >= starts[None, :]) & (places[:, None] < starts[None, :] + IMG)
    labels = jnp.arange(1, starts.shape[0] + 1, dtype=jnp.int32)
    return jnp.sum(jnp.where(inside, labels[None, :], 0), axis=1) - 1


def visible(query_places, key_places, query_pieces, key_pieces, length):
    causal = key_places[None, :] <= query_places[:, None]
    same_piece = (query_pieces[:, None] == key_pieces[None, :]) & (query_pieces[:, None] >= 0)
    return (key_places[None, :] < length) & (causal | same_piece)


def block_mask(own_places, key_places, key_pieces, length, starts):
    return visible(own_places, key_places, piece_of(own_places, starts), key_pieces, length)


def attention_forward(queries, key_sel, value_sel, own_places, key_places, length, starts):
    count_of_rows, head_count = (queries.shape[0], queries.shape[1])
    block_size = min(512, count_of_rows)
    key_pieces = piece_of(key_places, starts)
    stacked = queries.reshape(count_of_rows // block_size, block_size, head_count, HEAD_WIDTH)

    def one_block(element):
        block_rows, block_at = element
        allowed = block_mask(own_places, key_places, key_pieces, length, starts)
        scores = jnp.einsum("qhd,khd->hqk", block_rows, key_sel, preferred_element_type=jnp.float32)
        masked = jnp.where(allowed[None], scores, NEGATIVE)
        peak_row = jnp.max(masked, axis=-1, keepdims=True)
        raw_weights = jnp.where(allowed[None], jnp.exp(masked - peak_row), 0.0)
        total_row = jnp.sum(raw_weights, axis=-1, keepdims=True)
        attn_probs = (raw_weights / total_row).astype(jnp.bfloat16)
        outputs = jnp.einsum(
            "hqk,khd->qhd", attn_probs, value_sel, preferred_element_type=jnp.float32
        )
        return (outputs, peak_row[..., 0], total_row[..., 0])

    return lax.map(one_block, (stacked, jnp.arange(count_of_rows // block_size, dtype=jnp.int32)))


def attention_backward(
    queries,
    key_sel,
    value_sel,
    grad_attended,
    block_peaks,
    block_totals,
    own_places,
    key_places,
    length,
    starts,
):
    count_of_rows, head_count = (queries.shape[0], queries.shape[1])
    block_size = min(512, count_of_rows)
    block_count = count_of_rows // block_size
    key_pieces = piece_of(key_places, starts)
    stacked = queries.reshape(block_count, block_size, head_count, HEAD_WIDTH)
    grad_stacked = grad_attended.reshape(block_count, block_size, head_count, HEAD_WIDTH)

    def one_block(carry, element):
        dk_sum, dv_sum = carry
        block_rows, grad_rows, peak_row, total_row, block_at = element
        allowed = block_mask(own_places, key_places, key_pieces, length, starts)
        scores = jnp.einsum("qhd,khd->hqk", block_rows, key_sel, preferred_element_type=jnp.float32)
        masked = jnp.where(allowed[None], scores, NEGATIVE)
        raw_weights = jnp.where(allowed[None], jnp.exp(masked - peak_row[..., None]), 0.0)
        attn_probs = raw_weights / total_row[..., None]
        probs_low = attn_probs.astype(jnp.bfloat16)
        grad_probs = jnp.einsum(
            "qhd,khd->hqk", grad_rows, value_sel, preferred_element_type=jnp.float32
        )
        delta_row = jnp.sum(attn_probs * grad_probs, axis=-1, keepdims=True)
        grad_scores = (attn_probs * (grad_probs - delta_row)).astype(jnp.bfloat16)
        grad_query = jnp.einsum(
            "hqk,khd->qhd", grad_scores, key_sel, preferred_element_type=jnp.float32
        )
        dk_sum = dk_sum + jnp.einsum(
            "hqk,qhd->khd", grad_scores, block_rows, preferred_element_type=jnp.float32
        )
        dv_sum = dv_sum + jnp.einsum(
            "hqk,qhd->khd", probs_low, grad_rows, preferred_element_type=jnp.float32
        )
        return ((dk_sum, dv_sum), grad_query)

    zero_keys = jnp.zeros(key_sel.shape, jnp.float32)
    (dk_sum, dv_sum), grad_query = lax.scan(
        one_block,
        (zero_keys, zero_keys),
        (
            stacked,
            grad_stacked,
            block_peaks,
            block_totals,
            jnp.arange(block_count, dtype=jnp.int32),
        ),
    )
    return (grad_query.reshape(count_of_rows, head_count, HEAD_WIDTH), dk_sum, dv_sum)


def adamw_step(weight, moment_one, moment_two, gradient, rate, decay):
    moment_one = BETA_ONE * moment_one + (1.0 - BETA_ONE) * gradient
    moment_two = BETA_TWO * moment_two + (1.0 - BETA_TWO) * gradient * gradient
    mean_step = moment_one / (1.0 - BETA_ONE**STEP)
    spread = moment_two / (1.0 - BETA_TWO**STEP)
    return (
        moment_one,
        moment_two,
        weight - rate * (mean_step / (jnp.sqrt(spread) + ADAM_EPS) + decay * weight),
    )


MESH = pl.DeviceIdType.MESH
LOW = jnp.bfloat16
FULL = jnp.float32


def cost(micros, flops=0):
    return pl.CostEstimate(
        flops=flops, bytes_accessed=int(micros * 3.0e6), transcendentals=0
    )


def params(ident, mebibytes=48):
    return pltpu.CompilerParams(
        collective_id=ident, has_side_effects=True, vmem_limit_bytes=mebibytes * 2**20
    )


def push(source, target, send, recv, device):
    return pltpu.make_async_remote_copy(
        source, target, send, recv, device_id=device, device_id_type=MESH
    )


def greet_line(me, count, column, core):
    barrier = pltpu.get_barrier_semaphore()

    @pl.when(me > 0)
    def _():
        pl.semaphore_signal(barrier, inc=1, device_id={"row": me - 1}, device_id_type=MESH)

    @pl.when(me < count - 1)
    def _():
        pl.semaphore_signal(barrier, inc=1, device_id={"row": me + 1}, device_id_type=MESH)

    if core:
        pl.semaphore_signal(barrier, inc=1, device_id={"col": 1 - column}, device_id_type=MESH)

    ends = (me == 0) | (me == count - 1)

    @pl.when(ends)
    def _():
        pl.semaphore_wait(barrier, 1 + int(core))

    @pl.when(jnp.logical_not(ends))
    def _():
        pl.semaphore_wait(barrier, 2 + int(core))


def line_gather(block, ident, core, micros):
    count = lax.axis_size("row")

    def kernel(x_ref, o_ref, send_l, send_r, send_c, recv_l, recv_r, recv_c, local):
        me = lax.axis_index("row")
        column = lax.axis_index("col")

        def slot(source):
            return o_ref.at[column, source] if core else o_ref.at[source]

        def other(source):
            return o_ref.at[1 - column, source]

        def to_left(source, k):
            origin = x_ref if k == 0 else slot(source)
            return push(origin, slot(source), send_l.at[k], recv_r.at[k], {"row": me - 1})

        def to_right(source, k):
            origin = x_ref if k == 0 else slot(source)
            return push(origin, slot(source), send_r.at[k], recv_l.at[k], {"row": me + 1})

        def to_core(source, k):
            origin = x_ref if k == 0 else slot(source)
            return push(origin, slot(source), send_c.at[k], recv_c.at[k], {"col": 1 - column})

        def from_core(source, k):
            return push(other(source), other(source), send_c.at[k], recv_c.at[k], {"col": 1 - column})

        greet_line(me, count, column, core)

        @pl.when(me > 0)
        def _():
            to_left(me, 0).start()

        @pl.when(me < count - 1)
        def _():
            to_right(me, 0).start()

        if core:
            to_core(me, 0).start()
        own = pltpu.make_async_copy(x_ref, slot(me), local)
        own.start()
        for k in range(1, count):

            @pl.when(me - k >= 0)
            def _():
                push(slot(me - k), slot(me - k), send_r.at[k], recv_l.at[k - 1], {"row": me - 1}).wait_recv()

                @pl.when(me < count - 1)
                def _():
                    to_right(me - k, k).start()

                if core:
                    to_core(me - k, k).start()

            @pl.when(me + k < count)
            def _():
                push(slot(me + k), slot(me + k), send_l.at[k], recv_r.at[k - 1], {"row": me + 1}).wait_recv()

                @pl.when(me > 0)
                def _():
                    to_left(me + k, k).start()

                if core:
                    to_core(me + k, count - 1 + k).start()

        own.wait()

        @pl.when(me > 0)
        def _():
            to_left(me, 0).wait_send()

        @pl.when(me < count - 1)
        def _():
            to_right(me, 0).wait_send()

        if core:
            to_core(me, 0).wait_send()
            from_core(me, 0).wait_recv()
        for k in range(1, count):

            @pl.when(me - k >= 0)
            def _():
                @pl.when(me < count - 1)
                def _():
                    to_right(me - k, k).wait_send()

                if core:
                    to_core(me - k, k).wait_send()
                    from_core(me - k, k).wait_recv()

            @pl.when(me + k < count)
            def _():
                @pl.when(me > 0)
                def _():
                    to_left(me + k, k).wait_send()

                if core:
                    to_core(me + k, count - 1 + k).wait_send()
                    from_core(me + k, count - 1 + k).wait_recv()

    shape = ((2, count) if core else (count,)) + block.shape
    dma = pltpu.SemaphoreType.DMA
    return pl.pallas_call(
        kernel,
        out_shape=jax.ShapeDtypeStruct(shape, block.dtype),
        in_specs=[pl.BlockSpec(memory_space=pl.ANY)],
        out_specs=pl.BlockSpec(memory_space=pl.ANY),
        scratch_shapes=[
            dma((count,)),
            dma((count,)),
            dma((2 * count,)),
            dma((count,)),
            dma((count,)),
            dma((2 * count,)),
            dma,
        ],
        compiler_params=params(ident),
        cost_estimate=cost(micros),
    )(block)


def line_reduce(parts, ident, core, micros):
    count = lax.axis_size("row")
    high, wide = parts.shape[-2:]
    chunk = min(high, max(16, 65536 // wide))
    while high % chunk:
        chunk //= 2

    def kernel(x_ref, o_ref, c_buf, l_buf, r_buf, s_buf, send_l, send_r, send_c, recv_l, recv_r, recv_c):
        me = lax.axis_index("row")
        column = lax.axis_index("col")

        def mine(q):
            return x_ref.at[column, q] if core else x_ref.at[q]

        def core_copy(q):
            return push(x_ref.at[1 - column, q], c_buf.at[q], send_c.at[q], recv_c.at[q], {"col": 1 - column})

        def left_copy(q):
            return push(s_buf.at[q], l_buf.at[q], send_l.at[q], recv_l.at[q], {"row": me - 1})

        def right_copy(q):
            return push(s_buf.at[q], r_buf.at[q], send_r.at[q], recv_r.at[q], {"row": me + 1})

        def left_arrival(q):
            return push(s_buf.at[q], l_buf.at[q], send_l.at[q], recv_l.at[q], {"row": me + 1})

        def right_arrival(q):
            return push(s_buf.at[q], r_buf.at[q], send_r.at[q], recv_r.at[q], {"row": me - 1})

        def added(target, terms):
            @pl.loop(0, high // chunk)
            def _(at):
                rows = pl.ds(pl.multiple_of(at * chunk, chunk), chunk)
                total = terms[0][rows].astype(FULL)
                for term in terms[1:]:
                    total = total + term[rows].astype(FULL)
                target[rows] = total.astype(target.dtype)

        def base(q):
            return [mine(q)] + ([c_buf.at[q]] if core else [])

        greet_line(me, count, column, core)
        if core:
            for q in range(count):
                core_copy(q).start()

        def leftward(q):
            @pl.when(me > q)
            def _():
                if core:
                    core_copy(q).wait_recv()

                @pl.when(me < count - 1)
                def _():
                    left_arrival(q).wait_recv()
                    added(s_buf.at[q], base(q) + [l_buf.at[q]])

                @pl.when(me == count - 1)
                def _():
                    added(s_buf.at[q], base(q))

                left_copy(q).start()

        def rightward(q):
            @pl.when(me < q)
            def _():
                if core:
                    core_copy(q).wait_recv()

                @pl.when(me > 0)
                def _():
                    right_arrival(q).wait_recv()
                    added(s_buf.at[q], base(q) + [r_buf.at[q]])

                @pl.when(me == 0)
                def _():
                    added(s_buf.at[q], base(q))

                right_copy(q).start()

        for j in range(count - 1):

            @pl.when(me < count // 2)
            def _():
                rightward(count - 1 - j)

            leftward(j)

            @pl.when(me >= count // 2)
            def _():
                rightward(count - 1 - j)

        if core:
            core_copy(me).wait_recv()

        @pl.when(me < count - 1)
        def _():
            left_arrival(me).wait_recv()

        @pl.when(me > 0)
        def _():
            right_arrival(me).wait_recv()

        @pl.when(me == 0)
        def _():
            added(o_ref, base(me) + [l_buf.at[me]])

        @pl.when(me == count - 1)
        def _():
            added(o_ref, base(me) + [r_buf.at[me]])

        @pl.when((me > 0) & (me < count - 1))
        def _():
            added(o_ref, base(me) + [l_buf.at[me], r_buf.at[me]])

        for q in range(count):
            if core:
                core_copy(q).wait_send()

            @pl.when(me > q)
            def _():
                left_copy(q).wait_send()

            @pl.when(me < q)
            def _():
                right_copy(q).wait_send()

    dma = pltpu.SemaphoreType.DMA
    slots = (count, high, wide)
    vmem = pl.BlockSpec(memory_space=pltpu.VMEM)
    return pl.pallas_call(
        kernel,
        out_shape=jax.ShapeDtypeStruct((high, wide), FULL),
        in_specs=[vmem],
        out_specs=vmem,
        scratch_shapes=[
            pltpu.VMEM(slots if core else (1, 16, 128), parts.dtype),
            pltpu.VMEM(slots, parts.dtype),
            pltpu.VMEM(slots, parts.dtype),
            pltpu.VMEM(slots, parts.dtype),
        ]
        + [dma((count,))] * 6,
        compiler_params=params(ident),
        cost_estimate=cost(micros),
    )(parts)


class Line:
    def __init__(self, source, shape, place, core=False):
        self.source, self.shape, self.place, self.core = source, shape, place, core

    def semaphores(self, count, data):
        dma = pltpu.SemaphoreType.DMA
        return [dma((count,)), dma((count,)), dma((2 * count,))] * 2 + [dma]

    def bind(self, x_ref, o_ref, sems, spots, sizes):
        self.x_ref, self.o_ref, self.sems = x_ref, o_ref, sems
        self.me, self.column, self.at = spots
        self.count = sizes[0]

    def slot(self, source):
        return self.place(self.o_ref, self.column, source)

    def other(self, source):
        return self.place(self.o_ref, 1 - self.column, source)

    def to_left(self, source, k):
        origin = self.x_ref if k == 0 else self.slot(source)
        return push(origin, self.slot(source), self.sems[0].at[k], self.sems[4].at[k], {"row": self.me - 1})

    def to_right(self, source, k):
        origin = self.x_ref if k == 0 else self.slot(source)
        return push(origin, self.slot(source), self.sems[1].at[k], self.sems[3].at[k], {"row": self.me + 1})

    def to_core(self, source, k):
        origin = self.x_ref if k == 0 else self.slot(source)
        return push(origin, self.slot(source), self.sems[2].at[k], self.sems[5].at[k], {"col": 1 - self.column})

    def from_core(self, source, k):
        there = self.other(source)
        return push(there, there, self.sems[2].at[k], self.sems[5].at[k], {"col": 1 - self.column})

    def from_left(self, source, k):
        there = self.slot(source)
        return push(there, there, self.sems[1].at[k], self.sems[3].at[k - 1], {"row": self.me - 1})

    def from_right(self, source, k):
        there = self.slot(source)
        return push(there, there, self.sems[0].at[k], self.sems[4].at[k - 1], {"row": self.me + 1})

    def own(self):
        return pltpu.make_async_copy(self.x_ref, self.slot(self.me), self.sems[6])

    def start(self):
        me, count = self.me, self.count

        @pl.when(me > 0)
        def _():
            self.to_left(me, 0).start()

        @pl.when(me < count - 1)
        def _():
            self.to_right(me, 0).start()

        if self.core:
            self.to_core(me, 0).start()
        self.own().start()

    def step(self, k):
        me, count = self.me, self.count

        @pl.when(me - k >= 0)
        def _():
            self.from_left(me - k, k).wait_recv()

            @pl.when(me < count - 1)
            def _():
                self.to_right(me - k, k).start()

            if self.core:
                self.to_core(me - k, k).start()

        @pl.when(me + k < count)
        def _():
            self.from_right(me + k, k).wait_recv()

            @pl.when(me > 0)
            def _():
                self.to_left(me + k, k).start()

            if self.core:
                self.to_core(me + k, count - 1 + k).start()

    def finish(self):
        me, count = self.me, self.count
        self.own().wait()

        @pl.when(me > 0)
        def _():
            self.to_left(me, 0).wait_send()

        @pl.when(me < count - 1)
        def _():
            self.to_right(me, 0).wait_send()

        if self.core:
            self.to_core(me, 0).wait_send()
            self.from_core(me, 0).wait_recv()
        for k in range(1, count):

            @pl.when(me - k >= 0)
            def _():
                @pl.when(me < count - 1)
                def _():
                    self.to_right(me - k, k).wait_send()

                if self.core:
                    self.to_core(me - k, k).wait_send()
                    self.from_core(me - k, k).wait_recv()

            @pl.when(me + k < count)
            def _():
                @pl.when(me > 0)
                def _():
                    self.to_left(me + k, k).wait_send()

                if self.core:
                    self.to_core(me + k, count - 1 + k).wait_send()
                    self.from_core(me + k, count - 1 + k).wait_recv()


class Swap:
    def __init__(self, source, shape, take, place, axis="row"):
        self.source, self.shape, self.take, self.place = source, shape, take, place
        self.axis = axis

    def semaphores(self, count, data):
        size = count if self.axis == "row" else data
        return [pltpu.SemaphoreType.DMA((size,)), pltpu.SemaphoreType.DMA((size,))]

    def bind(self, x_ref, o_ref, sems, spots, sizes):
        self.x_ref, self.o_ref, self.sems = x_ref, o_ref, sems
        self.me = spots[0] if self.axis == "row" else spots[2]
        self.count = sizes[0] if self.axis == "row" else sizes[1]

    def copy(self, k):
        target = lax.rem(self.me + k, self.count)
        return push(
            self.take(self.x_ref, target),
            self.place(self.o_ref, self.me),
            self.sems[0].at[k],
            self.sems[1].at[k],
            {self.axis: target},
        )

    def own(self):
        return pltpu.make_async_copy(
            self.take(self.x_ref, self.me), self.place(self.o_ref, self.me), self.sems[0].at[0]
        )

    def start(self):
        for k in range(1, self.count):
            self.copy(k).start()
        self.own().start()

    def step(self, k):
        pass

    def finish(self):
        self.own().wait()
        for k in range(1, self.count):
            self.copy(k).wait_send()
            origin = lax.rem(self.me + self.count - k, self.count)
            there = self.place(self.o_ref, origin)
            push(there, there, self.sems[0].at[k], self.sems[1].at[k], {self.axis: origin}).wait_recv()


class Pair:
    core = True

    def __init__(self, source):
        self.source, self.shape = source, source.shape

    def semaphores(self, count, data):
        dma = pltpu.SemaphoreType.DMA
        return [dma, dma, dma]

    def bind(self, x_ref, o_ref, sems, spots, sizes):
        self.x_ref, self.o_ref, self.sems = x_ref, o_ref, sems
        self.column = spots[1]

    def copy(self):
        other = 1 - self.column
        return push(self.x_ref.at[other], self.o_ref.at[1], self.sems[0], self.sems[1], {"col": other})

    def own(self):
        return pltpu.make_async_copy(self.x_ref.at[self.column], self.o_ref.at[0], self.sems[2])

    def start(self):
        self.copy().start()
        self.own().start()

    def step(self, k):
        pass

    def finish(self):
        self.own().wait()
        self.copy().wait()


def transfers(items, ident, micros):
    count, data = lax.axis_size("row"), lax.axis_size("dp")
    kinds = [item.semaphores(count, data) for item in items]
    number = len(items)
    across = any(getattr(item, "axis", None) == "dp" for item in items)
    cores = any(getattr(item, "core", False) for item in items)

    def kernel(*refs):
        x_refs, o_refs, sems = refs[:number], refs[number : 2 * number], refs[2 * number :]
        me, column, at = lax.axis_index("row"), lax.axis_index("col"), lax.axis_index("dp")
        for item, x_ref, o_ref, kind in zip(items, x_refs, o_refs, kinds):
            item.bind(x_ref, o_ref, sems[: len(kind)], (me, column, at), (count, data))
            sems = sems[len(kind) :]
        barrier = pltpu.get_barrier_semaphore()
        for k in range(1, count):
            pl.semaphore_signal(
                barrier, inc=1, device_id={"row": lax.rem(me + k, count)}, device_id_type=MESH
            )
        if across:
            for k in range(1, data):
                pl.semaphore_signal(
                    barrier, inc=1, device_id={"dp": lax.rem(at + k, data)}, device_id_type=MESH
                )
        if cores:
            pl.semaphore_signal(barrier, inc=1, device_id={"col": 1 - column}, device_id_type=MESH)
        pl.semaphore_wait(barrier, count - 1 + (data - 1) * int(across) + int(cores))
        for item in items:
            item.start()
        for k in range(1, count):
            for item in items:
                item.step(k)
        for item in items:
            item.finish()

    anywhere = pl.BlockSpec(memory_space=pl.ANY)
    return pl.pallas_call(
        kernel,
        out_shape=[jax.ShapeDtypeStruct(item.shape, item.source.dtype) for item in items],
        in_specs=[anywhere] * number,
        out_specs=[anywhere] * number,
        scratch_shapes=sum(kinds, []),
        compiler_params=params(ident, 16),
        cost_estimate=cost(micros),
    )(*[item.source for item in items])


def shard_total(query_parts, kv_parts, flat_parts, ident):
    data = lax.axis_size("dp")
    half = data // 2

    def kernel(q_ref, kv_ref, f_ref, oq_ref, okv_ref, of_ref, q_buf, kv_buf, f_buf, *sems):
        column, at = lax.axis_index("col"), lax.axis_index("dp")
        barrier = pltpu.get_barrier_semaphore()
        for k in range(1, data):
            pl.semaphore_signal(barrier, inc=1, device_id={"dp": lax.rem(at + k, data)}, device_id_type=MESH)
        pl.semaphore_signal(barrier, inc=1, device_id={"col": 1 - column}, device_id_type=MESH)
        pl.semaphore_wait(barrier, data)
        mine = lax.rem(at, 2) == column

        def copies(k):
            target = lax.rem(at + k, data)
            device = {"dp": target}
            return (
                push(q_ref.at[target], q_buf.at[k], sems[0].at[k], sems[1].at[k], device),
                push(kv_ref.at[target // 2], kv_buf.at[k], sems[2].at[k], sems[3].at[k], device),
                push(f_ref.at[target], f_buf.at[k], sems[4].at[k], sems[5].at[k], device),
                lax.rem(target, 2) == column,
            )

        for k in range(1, data):
            query_copy, kv_copy, flat_copy, there = copies(k)
            query_copy.start()
            flat_copy.start()

            @pl.when(there)
            def _():
                kv_copy.start()

        for k in range(1, data):
            query_copy, kv_copy, flat_copy, there = copies(k)
            query_copy.wait()
            flat_copy.wait()

            @pl.when(there)
            def _():
                kv_copy.wait_send()

            @pl.when(mine)
            def _():
                kv_copy.wait_recv()

        def added(target, own, buf, chunk):
            @pl.loop(0, target.shape[0] // chunk)
            def _(step):
                rows = pl.ds(pl.multiple_of(step * chunk, chunk), chunk)
                total = own[rows].astype(FULL)
                for k in range(1, data):
                    total = total + buf[k, rows].astype(FULL)
                target[rows] = total

        share = push(okv_ref, okv_ref, sems[6], sems[7], {"col": 1 - column})

        @pl.when(mine)
        def _():
            added(okv_ref, kv_ref.at[at // 2], kv_buf, 128)
            share.start()

        added(oq_ref, q_ref.at[at], q_buf, 128)
        added(of_ref, f_ref.at[at], f_buf, 64)

        @pl.when(mine)
        def _():
            share.wait_send()

        @pl.when(jnp.logical_not(mine))
        def _():
            share.wait_recv()

    vmem = pl.BlockSpec(memory_space=pltpu.VMEM)
    dma = pltpu.SemaphoreType.DMA
    shapes = [query_parts.shape[1:], kv_parts.shape[1:], flat_parts.shape[1:]]
    return pl.pallas_call(
        kernel,
        out_shape=[jax.ShapeDtypeStruct(shape, FULL) for shape in shapes],
        in_specs=[vmem] * 3,
        out_specs=[vmem] * 3,
        scratch_shapes=[pltpu.VMEM((data,) + shape, LOW) for shape in shapes]
        + [dma((data,))] * 6
        + [dma, dma],
        compiler_params=params(ident),
        cost_estimate=cost(20),
    )(query_parts, kv_parts, flat_parts)


def small_total(values_in, axes, max_rows, ident):
    sizes = [lax.axis_size(axis) for axis in axes]
    high = values_in.shape[0]

    def kernel(x_ref, o_ref, *scratch):
        slots, sends, recvs = (scratch[k :: 3] for k in range(3))
        barrier = pltpu.get_barrier_semaphore()
        spots = [lax.axis_index(axis) for axis in axes]
        for axis, size, me in zip(axes, sizes, spots):
            for k in range(1, size):
                pl.semaphore_signal(
                    barrier, inc=1, device_id={axis: lax.rem(me + k, size)}, device_id_type=MESH
                )
        pl.semaphore_wait(barrier, sum(sizes) - len(sizes))
        for at, (axis, size, me) in enumerate(zip(axes, sizes, spots)):
            buf, send, recv = slots[at], sends[at], recvs[at]
            buf[me] = x_ref[...] if at == 0 else o_ref[...]
            for k in range(1, size):
                push(buf.at[me], buf.at[me], send.at[k], recv.at[k], {axis: lax.rem(me + k, size)}).start()
            for k in range(1, size):
                origin = lax.rem(me + size - k, size)
                push(buf.at[origin], buf.at[origin], send.at[k], recv.at[k], {axis: origin}).wait()
            total = buf[0]
            for k in range(1, size):
                total = total + buf[k]
            o_ref[...] = total
            if max_rows:
                top = buf[0, high - max_rows :]
                for k in range(1, size):
                    top = jnp.maximum(top, buf[k, high - max_rows :])
                o_ref[high - max_rows :] = top

    dma = pltpu.SemaphoreType.DMA
    vmem = pl.BlockSpec(memory_space=pltpu.VMEM)
    scratch = []
    for size in sizes:
        scratch += [pltpu.VMEM((size,) + values_in.shape, FULL), dma((size,)), dma((size,))]
    return pl.pallas_call(
        kernel,
        out_shape=jax.ShapeDtypeStruct(values_in.shape, FULL),
        in_specs=[vmem],
        out_specs=vmem,
        scratch_shapes=scratch,
        compiler_params=params(ident, 16),
        cost_estimate=cost(4 * len(sizes)),
    )(values_in)


def allowed_block(at, high, width, spans):
    key_places = lax.broadcasted_iota(jnp.int32, (high, width), 1)
    query_places = at * high + lax.broadcasted_iota(jnp.int32, (high, width), 0)
    seen = key_places <= query_places
    for piece in range(spans.shape[0] - 1):
        start = spans[piece + 1]
        both = (
            (key_places >= start)
            & (key_places < start + IMG)
            & (query_places >= start)
            & (query_places < start + IMG)
        )
        seen = seen | both
    return seen & (key_places < spans[0])


def softmax_block(block_rows, keys, allowed):
    scores = against(block_rows, keys)
    masked = jnp.where(allowed, scores, NEGATIVE)
    peak_row = jnp.max(masked, axis=-1, keepdims=True)
    raw_weights = jnp.where(allowed, jnp.exp(masked - peak_row), 0.0)
    return raw_weights / jnp.sum(raw_weights, axis=-1, keepdims=True), peak_row


def head_forward(queries, keys, values, spans):
    rows = queries.shape[0]
    step = min(256, rows)

    def kernel(spans_ref, q_ref, k_ref, v_ref, o_ref, top_ref):
        top_ref[...] = jnp.full(top_ref.shape, NEGATIVE, FULL)

        @pl.loop(0, rows // step)
        def _(at):
            here = pl.ds(pl.multiple_of(at * step, step), step)
            allowed = allowed_block(at, step, keys.shape[0], spans_ref)
            probs, peak_row = softmax_block(q_ref[here], k_ref[...], allowed)
            o_ref[here] = flat_dot(probs.astype(LOW), v_ref[...]).astype(LOW)
            top_ref[...] = jnp.maximum(top_ref[...], jnp.max(peak_row))

    vmem = pl.BlockSpec(memory_space=pltpu.VMEM)
    return pl.pallas_call(
        kernel,
        out_shape=(
            jax.ShapeDtypeStruct(queries.shape, LOW),
            jax.ShapeDtypeStruct((8, 128), FULL),
        ),
        in_specs=[pl.BlockSpec(memory_space=pltpu.SMEM), vmem, vmem, vmem],
        out_specs=(vmem, vmem),
        compiler_params=pltpu.CompilerParams(vmem_limit_bytes=48 * 2**20),
        cost_estimate=cost(10),
    )(spans, queries, keys, values)


def head_backward(queries, keys, values, grads, spans):
    rows = queries.shape[0]
    step = min(256, rows)

    def kernel(spans_ref, q_ref, k_ref, v_ref, g_ref, dq_ref, dk_ref, dv_ref):
        dk_ref[...] = jnp.zeros(dk_ref.shape, FULL)
        dv_ref[...] = jnp.zeros(dv_ref.shape, FULL)

        @pl.loop(0, rows // step)
        def _(at):
            here = pl.ds(pl.multiple_of(at * step, step), step)
            allowed = allowed_block(at, step, keys.shape[0], spans_ref)
            block_rows, grad_rows = q_ref[here], g_ref[here]
            probs, _ = softmax_block(block_rows, k_ref[...], allowed)
            grad_probs = against(grad_rows, v_ref[...])
            delta_row = jnp.sum(probs * grad_probs, axis=-1, keepdims=True)
            grad_scores = (probs * (grad_probs - delta_row)).astype(LOW)
            dq_ref[here] = flat_dot(grad_scores, k_ref[...])
            dk_ref[...] += inner_rows(grad_scores, block_rows)
            dv_ref[...] += inner_rows(probs.astype(LOW), grad_rows)

    vmem = pl.BlockSpec(memory_space=pltpu.VMEM)
    return pl.pallas_call(
        kernel,
        out_shape=(jax.ShapeDtypeStruct(queries.shape, FULL),)
        + (jax.ShapeDtypeStruct(keys.shape, FULL),) * 2,
        in_specs=[pl.BlockSpec(memory_space=pltpu.SMEM)] + [vmem] * 4,
        out_specs=(vmem, vmem, vmem),
        compiler_params=pltpu.CompilerParams(vmem_limit_bytes=48 * 2**20),
        cost_estimate=cost(20),
    )(spans, queries, keys, values, grads)


def whole_norm(values_in, gain_vec):
    scale = lax.rsqrt(jnp.mean(values_in * values_in, axis=-1, keepdims=True) + EPS)
    return values_in * scale * gain_vec, scale


def whole_norm_backward(values_in, scale, gain_vec, grad_out):
    weighted = grad_out * gain_vec
    inner = jnp.mean(weighted * values_in, axis=-1, keepdims=True)
    return (
        scale * weighted - values_in * (scale * scale * scale) * inner,
        jnp.sum(grad_out * values_in * scale, axis=0),
    )


def turn(values_in, cos_tab, sin_tab):
    half_width = values_in.shape[-1] // 2
    one, two = values_in[:, :half_width], values_in[:, half_width:]
    return jnp.concatenate(
        [one * cos_tab - two * sin_tab, two * cos_tab + one * sin_tab], axis=1
    )


def turn_back(values_in, cos_tab, sin_tab):
    return turn(values_in, cos_tab, -sin_tab)


def swap_row(values_in, split, concat, tiled=True):
    return lax.all_to_all(values_in, "row", split, concat, tiled=tiled)


def line_device(
    activations,
    per_layer,
    cotangent,
    lengths,
    starts,
    w_query,
    m_query,
    v_query,
    key_value_weight,
    key_value_first_moment,
    key_value_second_moment,
    w_attend,
    m_attend,
    v_attend,
    w_gateup,
    m_gateup,
    v_gateup,
    w_down,
    m_down,
    v_down,
    w_left,
    m_left,
    v_left,
    w_right,
    m_right,
    v_right,
    w_pergate,
    m_pergate,
    v_pergate,
    w_perproj,
    m_perproj,
    v_perproj,
    w_gains,
    m_gains,
    v_gains,
    w_heads,
    m_heads,
    v_heads,
):
    rows_n = lax.axis_size("row")
    cols_n = lax.axis_size("col")
    data_n = lax.axis_size("dp")
    me = lax.axis_index("row")
    column = lax.axis_index("col")
    data_at = lax.axis_index("dp")
    half_tok, width_a = activations.shape
    tokens = half_tok * cols_n
    share = half_tok // rows_n
    quarter = tokens // rows_n
    width = width_a * rows_n

    ff_part = w_gateup.shape[2] // rows_n
    out_cols = w_down.shape[1]
    heads_here = data_n
    smalls = (w_left, w_right, w_pergate, w_perproj)
    flat = jnp.concatenate([w.astype(LOW).reshape(-1) for w in smalls]).reshape(-1, 128)
    flat_rows = flat.shape[0]

    def columns_of(at, size):
        return pl.ds(pl.multiple_of(at * size, size), size)

    gateup_own, down_own, attend_own, upstream, qkv_w, flat = transfers(
        [
            Swap(
                w_gateup.astype(LOW),
                (2, width, ff_part),
                lambda ref, q: ref.at[:, :, columns_of(q, ff_part)],
                lambda ref, at: ref.at[:, columns_of(at, width_a), :],
            ),
            Swap(
                w_down.astype(LOW).reshape(data_n, rows_n, ff_part, out_cols),
                (data_n, ff_part, rows_n * out_cols),
                lambda ref, q: ref.at[:, q],
                lambda ref, at: ref.at[:, :, columns_of(at, out_cols)],
            ),
            Swap(
                w_attend.astype(LOW).reshape(rows_n, HEAD_WIDTH, out_cols),
                (HEAD_WIDTH, rows_n * out_cols),
                lambda ref, q: ref.at[q],
                lambda ref, at: ref.at[:, columns_of(at, out_cols)],
            ),
            Swap(
                cotangent,
                (share, width),
                lambda ref, q: ref.at[columns_of(q, share)],
                lambda ref, at: ref.at[:, columns_of(at, width_a)],
            ),
            Swap(
                jnp.concatenate([w_query, key_value_weight], axis=1).astype(LOW),
                (data_n, width_a, 2 * HEAD_WIDTH),
                lambda ref, q: ref,
                lambda ref, at: ref.at[at],
                "dp",
            ),
            Swap(
                flat,
                (data_n * flat_rows, 128),
                lambda ref, q: ref,
                lambda ref, at: ref.at[columns_of(at, flat_rows)],
                "dp",
            ),
        ],
        1,
        90,
    )
    gateup_all = lax.all_gather(gateup_own, "dp")
    down_all = lax.all_gather(down_own, "dp")
    query_w = qkv_w[:, :, :HEAD_WIDTH]
    kv_w = qkv_w[:, :, HEAD_WIDTH:]
    key_w = lax.dynamic_index_in_dim(kv_w, column, 0, False)
    value_w = lax.dynamic_index_in_dim(kv_w, KEY_VALUE_HEADS + column, 0, False)
    whole_acts, whole_kv, head_w, flat, gains, extras, attend_all = transfers(
        [
            Line(
                activations,
                (tokens, width),
                lambda ref, c, r: ref.at[columns_of(c, half_tok), columns_of(r, width_a)],
                True,
            ),
            Line(
                jnp.stack([key_w, value_w]),
                (2, width, HEAD_WIDTH),
                lambda ref, c, r: ref.at[:, columns_of(r, width_a)],
            ),
            Swap(
                query_w,
                (width, HEAD_WIDTH),
                lambda ref, q: ref.at[q],
                lambda ref, at: ref.at[columns_of(at, width_a)],
            ),
            Line(
                flat, (cols_n, rows_n) + flat.shape, lambda ref, c, r: ref.at[c, r], True
            ),
            Line(w_gains, (6, width), lambda ref, c, r: ref.at[:, columns_of(r, width_a)]),
            Line(
                per_layer,
                (tokens, PLD),
                lambda ref, c, r: ref.at[columns_of(r, quarter), columns_of(c, PLD // cols_n)],
                True,
            ),
            Swap(
                attend_own,
                (data_n, HEAD_WIDTH, rows_n * out_cols),
                lambda ref, q: ref,
                lambda ref, at: ref.at[at],
                "dp",
            ),
        ],
        2,
        115,
    )
    attend_w = (
        attend_all.reshape(data_n, HEAD_WIDTH, rows_n, out_cols)
        .transpose(1, 2, 0, 3)
        .reshape(HEAD_WIDTH, width)
    )
    flat = flat.reshape(cols_n, rows_n, data_n, -1)
    cuts = []
    start = 0
    for w in smalls:
        cuts.append(flat[..., start : start + w.size].reshape((cols_n, rows_n, data_n) + w.shape))
        start += w.size
    left_w = cuts[0].transpose(1, 3, 0, 2, 4).reshape(width, -1)
    right_w = cuts[1].transpose(0, 3, 1, 2, 4).reshape(-1, width)
    pergate_w = cuts[2].transpose(1, 3, 0, 2, 4).reshape(width, -1)
    perproj_w = cuts[3].transpose(0, 3, 1, 2, 4).reshape(-1, width)
    upstream = upstream.astype(FULL)
    token_at = column * half_tok + me * share
    extras = lax.dynamic_slice_in_dim(extras, token_at, share, 0).astype(FULL)
    length = lax.dynamic_index_in_dim(lengths, data_at, 0, keepdims=True)
    piece_starts = lax.dynamic_index_in_dim(starts, data_at, 0, keepdims=False)
    spans = jnp.concatenate([length, piece_starts])

    whole_hidden, whole_scale = whole_norm(whole_acts.astype(FULL), gains[0])
    whole_hidden = whole_hidden.astype(LOW)
    inputs = lax.dynamic_slice_in_dim(whole_acts, token_at, share, 0).astype(FULL)
    query_raw = flat_dot(whole_hidden, head_w)
    all_key_raw = flat_dot(whole_hidden, whole_kv[0])
    all_value_raw = flat_dot(whole_hidden, whole_kv[1])
    query_gain = lax.dynamic_index_in_dim(w_heads, column * rows_n + me, 0, True)
    key_gain = w_heads[QUERY_HEADS:]
    all_cos, all_sin = rope_tables(jnp.arange(tokens, dtype=jnp.int32), HEAD_WIDTH)
    own_cos = lax.dynamic_slice_in_dim(all_cos, me * quarter, quarter, 0)
    own_sin = lax.dynamic_slice_in_dim(all_sin, me * quarter, quarter, 0)
    query_n, query_scale = whole_norm(query_raw, query_gain)
    queries = turn(query_n, all_cos, all_sin).astype(LOW)
    keys = turn(whole_norm(all_key_raw, key_gain)[0], all_cos, all_sin).astype(LOW)
    values = whole_norm(all_value_raw, 1.0)[0].astype(LOW)
    attended, top = head_forward(queries, keys, values, spans)
    key_raw = lax.dynamic_slice_in_dim(all_key_raw, me * quarter, quarter, 0)
    value_raw = lax.dynamic_slice_in_dim(all_value_raw, me * quarter, quarter, 0)
    _, key_scale = whole_norm(key_raw, key_gain)
    _, value_scale = whole_norm(value_raw, 1.0)
    gateup_w = gateup_all.transpose(1, 2, 0, 3).reshape(2, width, -1)
    down_w = (
        down_all.reshape(data_n, data_n, ff_part, rows_n, out_cols)
        .transpose(1, 2, 3, 0, 4)
        .reshape(-1, width)
    )

    def shares(parts):
        return parts.astype(LOW).reshape(cols_n, rows_n, share, width)

    hidden, _ = whole_norm(inputs, gains[0])
    hidden_low = hidden.astype(LOW)
    middle = flat_dot(hidden_low, left_w).astype(LOW)
    right_raw = flat_dot(middle, right_w)
    right_n, scale_r = whole_norm(right_raw, gains[1])
    projected = line_reduce(shares(flat_dot(attended, attend_w)), 5, True, 45)
    proj_n, scale_p = whole_norm(projected, gains[2])
    mixture = ((inputs + proj_n) + (hidden + right_n)) * HALF_ROOT
    ffn_n, scale_f = whole_norm(mixture, gains[3])
    spread_f = line_gather(ffn_n.astype(LOW), 6, True, 40).reshape(tokens, width)
    gate_raw = flat_dot(spread_f, gateup_w[0])
    up_raw = flat_dot(spread_f, gateup_w[1])
    act = (jax.nn.gelu(gate_raw, approximate=True) * up_raw).astype(LOW)
    down_raw = line_reduce(shares(flat_dot(act, down_w)), 7, True, 45)
    down_n, scale_d = whole_norm(down_raw, gains[4])
    block_out = mixture + down_n
    out_low = block_out.astype(LOW)
    pgate = flat_dot(out_low, pergate_w)
    pact = (jax.nn.gelu(pgate, approximate=True) * extras).astype(LOW)
    perproj = flat_dot(pact, perproj_w)
    perproj_n, scale_pp = whole_norm(perproj, gains[5])
    result = (block_out + perproj_n).astype(LOW)

    gain_grads = [None] * 6
    d_perproj, gain_grads[5] = whole_norm_backward(perproj, scale_pp, gains[5], upstream)
    d_perproj = d_perproj.astype(LOW)
    dw_perproj = inner_rows(pact, d_perproj)
    d_pact = against(d_perproj, perproj_w)
    _, pullback = jax.vjp(lambda v: jax.nn.gelu(v, approximate=True), pgate)
    (d_pgate,) = pullback(d_pact * extras)
    d_pgate = d_pgate.astype(LOW)
    dw_pergate = inner_rows(out_low, d_pgate)
    d_out = upstream + against(d_pgate, pergate_w)
    d_down, gain_grads[4] = whole_norm_backward(down_raw, scale_d, gains[4], d_out)
    spread_d, result = transfers(
        [
            Line(
                d_down.astype(LOW),
                (cols_n, rows_n, share, width),
                lambda ref, c, r: ref.at[c, r],
                True,
            ),
            Swap(
                result,
                (half_tok, width_a),
                lambda ref, q: ref.at[:, columns_of(q, width_a)],
                lambda ref, at: ref.at[columns_of(at, share)],
            ),
        ],
        8,
        50,
    )
    spread_d = spread_d.reshape(tokens, width)
    d_act = against(spread_d, down_w)
    _, pullback = jax.vjp(
        lambda a, b: jax.nn.gelu(a, approximate=True) * b, gate_raw, up_raw
    )
    d_gate, d_up = pullback(d_act)
    d_gate, d_up = d_gate.astype(LOW), d_up.astype(LOW)
    d_ffn = against(d_gate, gateup_w[0]) + against(d_up, gateup_w[1])
    dw_down = inner_rows(act, spread_d).astype(LOW)
    dw_down = dw_down.reshape(data_n, ff_part, rows_n, data_n, out_cols).transpose(3, 0, 1, 2, 4)
    dw_gateup = jnp.stack(
        [
            inner_rows(spread_f, grad[:, k * ff_part : (k + 1) * ff_part]).astype(LOW)
            for k in range(data_n)
            for grad in (d_gate, d_up)
        ]
    ).reshape(data_n, 2, width, ff_part)
    d_ffn, dw_down, dw_gateup = lax.optimization_barrier((shares(d_ffn), dw_down, dw_gateup))
    g_gateup = lax.psum_scatter(dw_gateup, "dp", scatter_dimension=0)
    g_down = lax.psum_scatter(
        dw_down.reshape(data_n, data_n, ff_part, -1), "dp", scatter_dimension=0
    )
    d_ffn = line_reduce(d_ffn, 9, True, 45)
    d_mix, gain_grads[3] = whole_norm_backward(mixture, scale_f, gains[3], d_ffn)
    d_half = (d_out + d_mix) * HALF_ROOT
    d_proj, gain_grads[2] = whole_norm_backward(projected, scale_p, gains[2], d_half)
    spread_p = line_gather(d_proj.astype(LOW), 10, True, 40).reshape(tokens, width)
    d_right, gain_grads[1] = whole_norm_backward(right_raw, scale_r, gains[1], d_half)
    d_right = d_right.astype(LOW)
    dw_right = inner_rows(middle, d_right)
    d_middle = against(d_right, right_w).astype(LOW)
    dw_left = inner_rows(hidden_low, d_middle)
    d_hidden_share = d_half + against(d_middle, left_w)
    inner_share = jnp.sum(d_hidden_share * gains[0] * inputs, axis=1)
    half_low, share_low = d_half.astype(LOW), d_hidden_share.astype(LOW)
    d_attended = against(spread_p, attend_w).astype(LOW)
    dw_attend = inner_rows(attended, spread_p).astype(LOW)
    d_queries, d_keys, d_values = head_backward(queries, keys, values, d_attended, spans)
    kv_parts = jnp.concatenate(
        [
            d_keys.astype(LOW).reshape(rows_n, quarter, HEAD_WIDTH),
            d_values.astype(LOW).reshape(rows_n, quarter, HEAD_WIDTH),
        ],
        axis=1,
    )
    d_kv = line_reduce(kv_parts, 11, False, 20)
    d_q_raw, dg_query = whole_norm_backward(
        query_raw, query_scale, query_gain, turn_back(d_queries, all_cos, all_sin)
    )
    d_k_raw, dg_key = whole_norm_backward(
        key_raw, key_scale, key_gain, turn_back(d_kv[:quarter], own_cos, own_sin)
    )
    d_v_raw, _ = whole_norm_backward(value_raw, value_scale, 1.0, d_kv[quarter:])
    d_raw = jnp.concatenate([d_q_raw, d_k_raw, d_v_raw], axis=0).astype(LOW)
    spread_q = line_gather(d_raw, 12, False, 55)
    d_q_all = spread_q[:, :tokens]
    d_k_all = spread_q[:, tokens : tokens + quarter].reshape(tokens, HEAD_WIDTH)
    d_v_all = spread_q[:, tokens + quarter :].reshape(tokens, HEAD_WIDTH)
    d_hidden = against(d_k_all, key_w) + against(d_v_all, value_w)
    for k in range(heads_here):
        d_hidden = d_hidden + against(d_q_all[k], query_w[k])
    acts = activations.astype(FULL)
    gains_here = lax.dynamic_slice_in_dim(w_gains, 0, 1, 0)[0]
    scale_here = lax.dynamic_slice_in_dim(whole_scale, column * half_tok, half_tok, 0)
    own_acts = lax.dynamic_slice_in_dim(whole_acts, me * width_a, width_a, 1).astype(FULL)
    inner = jnp.sum(d_hidden * gains_here * own_acts, axis=1)
    inner = lax.dynamic_update_slice_in_dim(
        inner, lax.dynamic_slice_in_dim(inner, token_at, share, 0) + inner_share, token_at, 0
    ).reshape(-1, 128)

    spread_h = lax.dynamic_slice_in_dim(whole_hidden, me * width_a, width_a, 1)
    dw_query = jnp.stack([inner_rows(spread_h, d_q_all[k]).astype(LOW) for k in range(heads_here)])
    dw_kv = jnp.stack(
        [inner_rows(spread_h, d_k_all).astype(LOW), inner_rows(spread_h, d_v_all).astype(LOW)]
    )
    g_attend = lax.psum_scatter(
        dw_attend.reshape(HEAD_WIDTH, rows_n, data_n, out_cols).transpose(2, 0, 1, 3).reshape(data_n, HEAD_WIDTH, -1),
        "dp",
        scatter_dimension=0,
    )

    def to_shards(grad, rows_first):
        if rows_first:
            cut = grad.reshape(rows_n, width_a, cols_n, data_n, -1).transpose(2, 0, 3, 1, 4)
        else:
            cut = grad.reshape(cols_n, -1, rows_n, data_n, out_cols).transpose(0, 2, 3, 1, 4)
        return cut.astype(LOW).reshape(cols_n, rows_n, data_n, -1)

    flat_grads = jnp.concatenate(
        [
            to_shards(dw_left, True),
            to_shards(dw_right, False),
            to_shards(dw_pergate, True),
            to_shards(dw_perproj, False),
        ],
        axis=3,
    ).reshape(cols_n, rows_n, data_n * flat_rows, 128)
    flat_grads = line_reduce(flat_grads, 17, True, 28).astype(LOW).reshape(data_n, flat_rows, 128)
    g_query, g_keyval, flat_grads = shard_total(dw_query, dw_kv, flat_grads, 13)
    squares = jnp.where(column == 0, jnp.sum(g_keyval * g_keyval), 0.0)
    for gradient in (g_query, g_attend, g_gateup, g_down, flat_grads):
        gradient = gradient.astype(FULL)
        squares = squares + jnp.sum(gradient * gradient)
    g_gateup, g_down, g_attend, half_here, share_here, d_hidden, inner = transfers(
        [
            Swap(
                g_gateup,
                w_gateup.shape,
                lambda ref, q: ref.at[:, columns_of(q, width_a), :],
                lambda ref, at: ref.at[:, :, columns_of(at, ff_part)],
            ),
            Swap(
                g_down,
                (data_n, rows_n, ff_part, out_cols),
                lambda ref, q: ref.at[:, :, columns_of(q, out_cols)],
                lambda ref, at: ref.at[:, at],
            ),
            Swap(
                g_attend,
                (rows_n, HEAD_WIDTH, out_cols),
                lambda ref, q: ref.at[:, columns_of(q, out_cols)],
                lambda ref, at: ref.at[at],
            ),
            Swap(
                half_low,
                (half_tok, width_a),
                lambda ref, q: ref.at[:, columns_of(q, width_a)],
                lambda ref, at: ref.at[columns_of(at, share)],
            ),
            Swap(
                share_low,
                (half_tok, width_a),
                lambda ref, q: ref.at[:, columns_of(q, width_a)],
                lambda ref, at: ref.at[columns_of(at, share)],
            ),
            Pair(d_hidden.astype(LOW).reshape(cols_n, half_tok, width_a)),
            Line(inner, (cols_n, rows_n) + inner.shape, lambda ref, c, r: ref.at[c, r], True),
        ],
        14,
        100,
    )
    g_gateup = g_gateup.astype(FULL)
    g_down = g_down.reshape(w_down.shape).astype(FULL)
    g_attend = g_attend.reshape(w_attend.shape).astype(FULL)
    flat_grads = flat_grads.reshape(-1)
    small_grads = []
    start = 0
    for w in smalls:
        small_grads.append(flat_grads[start : start + w.size].reshape(w.shape))
        start += w.size
    g_left, g_right, g_pergate, g_perproj = small_grads

    inner = jnp.sum(inner, axis=(0, 1)).reshape(cols_n, half_tok) / MODEL_WIDTH
    inner = lax.dynamic_index_in_dim(inner, column, 0, False)[:, None]
    d_hidden = d_hidden[0].astype(FULL) + d_hidden[1].astype(FULL) + share_here.astype(FULL)
    grad_input = (
        half_here.astype(FULL)
        + scale_here * d_hidden * gains_here
        - acts * (scale_here * scale_here * scale_here) * inner
    ).astype(LOW)
    gain_zero = jnp.sum(d_hidden * acts * scale_here, axis=0)

    gain_full = jnp.stack(
        [
            lax.dynamic_update_slice_in_dim(
                jnp.zeros((width,), FULL), gain_zero, me * width_a, 0
            )
        ]
        + gain_grads[1:]
    )
    head_full = lax.dynamic_update_slice_in_dim(
        jnp.zeros((QUERY_HEADS + 1, HEAD_WIDTH), FULL), dg_query[None], column * rows_n + me, 0
    )
    head_full = head_full.at[QUERY_HEADS].add(dg_key)
    logit_row = lax.dynamic_update_slice_in_dim(
        jnp.full((128,), NEGATIVE, FULL), top[0, :1], column * rows_n + me, 0
    )
    gain_rows = gain_full.size // 128
    head_rows = head_full.size // 128
    pad_rows = -(gain_rows + head_rows) % 8
    small = jnp.concatenate(
        [
            gain_full.reshape(-1, 128),
            head_full.reshape(-1, 128),
            jnp.broadcast_to(squares, (pad_rows, 128)),
            jnp.broadcast_to(logit_row[None], (8, 128)),
        ]
    )
    small = small_total(small, ("col", "row", "dp"), 8, 15)
    gain_sum = small[:gain_rows].reshape(6, width)
    head_sum = small[gain_rows : gain_rows + head_rows].reshape(QUERY_HEADS + 1, HEAD_WIDTH)
    logit_top = small[-1, :QUERY_HEADS]
    g_gains = lax.dynamic_slice_in_dim(gain_sum, me * width_a, width_a, 1)
    squares = small[gain_rows + head_rows, 0]
    squares = squares + jnp.sum(gain_sum * gain_sum) + jnp.sum(head_sum * head_sum)
    grad_norm = jnp.sqrt(squares)
    clip_scale = CLIP / jnp.maximum(grad_norm, CLIP)
    scale_factors = LOGIT_CAP / jnp.maximum(logit_top, LOGIT_CAP)
    weights = (
        w_query,
        key_value_weight,
        w_attend,
        w_gateup,
        w_down,
        w_left,
        w_right,
        w_pergate,
        w_perproj,
        w_gains,
        w_heads,
    )
    moments = (
        m_query,
        key_value_first_moment,
        m_attend,
        m_gateup,
        m_down,
        m_left,
        m_right,
        m_pergate,
        m_perproj,
        m_gains,
        m_heads,
    )
    seconds = (
        v_query,
        key_value_second_moment,
        v_attend,
        v_gateup,
        v_down,
        v_left,
        v_right,
        v_pergate,
        v_perproj,
        v_gains,
        v_heads,
    )
    gradients = (
        g_query,
        g_keyval,
        g_attend,
        g_gateup,
        g_down,
        g_left,
        g_right,
        g_pergate,
        g_perproj,
        g_gains,
        head_sum,
    )
    step_rates = (
        MODEL_WIDTH ** (-0.5),
        MODEL_WIDTH ** (-0.5),
        (QUERY_HEADS * HEAD_WIDTH) ** (-0.5),
        MODEL_WIDTH ** (-0.5),
        FF ** (-0.5),
        MODEL_WIDTH ** (-0.5),
        RANK ** (-0.5),
        MODEL_WIDTH ** (-0.5),
        PLD ** (-0.5),
        GAIN_RATE,
        HEAD_RATE,
    )
    decays = (DECAY, DECAY, DECAY, DECAY, DECAY, DECAY, DECAY, DECAY, DECAY, 0.0, 0.0)
    updated = [
        adamw_step(
            weights[k], moments[k], seconds[k], gradients[k] * clip_scale, step_rates[k], decays[k]
        )
        for k in range(11)
    ]
    head_scale = jnp.sqrt(scale_factors)
    q_width = w_query.shape[1]
    q_head = (
        (column * data_n + data_at) * q_width + jnp.arange(q_width, dtype=jnp.int32)
    ) // HEAD_WIDTH
    q_factor = jnp.sum(
        jnp.where(
            q_head[:, None] == jnp.arange(QUERY_HEADS, dtype=jnp.int32)[None, :],
            head_scale[None, :],
            0.0,
        ),
        axis=1,
    )
    new_query = updated[0][2] * q_factor[None, :]
    kv_width = key_value_weight.shape[1]
    key_value_index = data_at * kv_width + jnp.arange(kv_width, dtype=jnp.int32)
    key_value_scale = jnp.sqrt(
        jnp.min(scale_factors.reshape(KEY_VALUE_HEADS, QUERY_HEADS // KEY_VALUE_HEADS), axis=1)
    )
    key_value_choice = jnp.sum(
        jnp.where(
            (key_value_index // HEAD_WIDTH)[:, None]
            == jnp.arange(KEY_VALUE_HEADS, dtype=jnp.int32)[None, :],
            key_value_scale[None, :],
            0.0,
        ),
        axis=1,
    )
    key_value_factor = jnp.where(
        key_value_index < KEY_VALUE_HEADS * HEAD_WIDTH, key_value_choice, 1.0
    )
    new_keyval = updated[1][2] * key_value_factor[None, :]
    return (
        result,
        grad_input,
        grad_norm,
        scale_factors,
        updated[0][0],
        updated[0][1],
        new_query,
        updated[1][0],
        updated[1][1],
        new_keyval,
        updated[2][0],
        updated[2][1],
        updated[2][2],
        updated[3][0],
        updated[3][1],
        updated[3][2],
        updated[4][0],
        updated[4][1],
        updated[4][2],
        updated[5][0],
        updated[5][1],
        updated[5][2],
        updated[6][0],
        updated[6][1],
        updated[6][2],
        updated[7][0],
        updated[7][1],
        updated[7][2],
        updated[8][0],
        updated[8][1],
        updated[8][2],
        updated[9][0],
        updated[9][1],
        updated[9][2],
        updated[10][0],
        updated[10][1],
        updated[10][2],
    )


def per_device(
    activations,
    per_layer,
    cotangent,
    lengths,
    starts,
    w_query,
    m_query,
    v_query,
    key_value_weight,
    key_value_first_moment,
    key_value_second_moment,
    w_attend,
    m_attend,
    v_attend,
    w_gateup,
    m_gateup,
    v_gateup,
    w_down,
    m_down,
    v_down,
    w_left,
    m_left,
    v_left,
    w_right,
    m_right,
    v_right,
    w_pergate,
    m_pergate,
    v_pergate,
    w_perproj,
    m_perproj,
    v_perproj,
    w_gains,
    m_gains,
    v_gains,
    w_heads,
    m_heads,
    v_heads,
):
    row_devs = lax.axis_size("row")
    col_devs = lax.axis_size("col")
    data_devs = lax.axis_size("dp")
    row_place = lax.axis_index("row")
    column_place = lax.axis_index("col")
    data_at = lax.axis_index("dp")
    bf16 = jnp.bfloat16
    single_float = jnp.float32
    query_b, keyval_b, attend_b, gateup_b, down_b, left_b, right_b, pergate_b, perproj_b = (
        lax.all_gather(w_query.astype(bf16), "dp", axis=1, tiled=True),
        lax.all_gather(key_value_weight.astype(bf16), "dp", axis=1, tiled=True),
        lax.all_gather(w_attend.astype(bf16), "dp", axis=1, tiled=True),
        lax.all_gather(w_gateup.astype(bf16), "dp", axis=2, tiled=True),
        lax.all_gather(w_down.astype(bf16), "dp", axis=1, tiled=True),
        lax.all_gather(w_left.astype(bf16), "dp", axis=1, tiled=True),
        lax.all_gather(w_right.astype(bf16), "dp", axis=1, tiled=True),
        lax.all_gather(w_pergate.astype(bf16), "dp", axis=1, tiled=True),
        lax.all_gather(w_perproj.astype(bf16), "dp", axis=1, tiled=True),
    )
    inputs = activations.astype(single_float)
    tok_a, width_a = inputs.shape
    grouped_rows = tok_a * col_devs
    token_batch = grouped_rows // row_devs
    q_cols = query_b.shape[1]
    l_cols = left_b.shape[1]
    kv_cols = keyval_b.shape[1]
    ff_here = gateup_b.shape[2]
    local_heads = q_cols // HEAD_WIDTH
    length = lax.dynamic_index_in_dim(lengths, data_at, 0, keepdims=False)
    piece_starts = lax.dynamic_index_in_dim(starts, data_at, 0, keepdims=False)
    own_places = row_place * token_batch + jnp.arange(token_batch, dtype=jnp.int32)
    all_places = jnp.arange(grouped_rows, dtype=jnp.int32)
    own_cos, own_sin = rope_tables(own_places, HEAD_WIDTH)
    query_gains = lax.dynamic_slice_in_dim(w_heads, column_place * local_heads, local_heads, 0)
    key_gain = w_heads[QUERY_HEADS]
    hidden, scale_in = norm_forward(inputs, w_gains[0])
    hidden_b = hidden.astype(bf16)
    spread_h = spread_col(hidden_b)
    type_one = reduce_row(flat_dot(spread_h, jnp.concatenate([query_b, left_b], axis=1)))
    key_raw_all = lax.psum(flat_dot(spread_h, keyval_b), "row")
    all_cos, all_sin = rope_tables(all_places, HEAD_WIDTH)
    key_value_whole = key_form(key_raw_all, key_gain, all_cos, all_sin).astype(bf16)
    key_raw = lax.dynamic_slice_in_dim(key_raw_all, row_place * token_batch, token_batch, 0)
    query_raw = type_one[:, :q_cols]
    middle_b = type_one[:, q_cols : q_cols + l_cols].astype(bf16)
    queries = query_form(query_raw, query_gains, own_cos, own_sin).astype(bf16)
    key_value_heads = (column_place * local_heads + jnp.arange(local_heads, dtype=jnp.int32)) // (
        QUERY_HEADS // KEY_VALUE_HEADS
    )
    every_key = key_value_whole[:, : KEY_VALUE_HEADS * HEAD_WIDTH].reshape(
        grouped_rows, KEY_VALUE_HEADS, HEAD_WIDTH
    )
    every_value = key_value_whole[:, KEY_VALUE_HEADS * HEAD_WIDTH :].reshape(
        grouped_rows, KEY_VALUE_HEADS, HEAD_WIDTH
    )
    key_sel = jnp.take(every_key, key_value_heads, axis=1)
    value_sel = jnp.take(every_value, key_value_heads, axis=1)
    attended, block_peaks, block_totals = attention_forward(
        queries, key_sel, value_sel, own_places, all_places, length, piece_starts
    )
    attended_b = attended.reshape(token_batch, q_cols).astype(bf16)
    joined_b = jnp.concatenate([attended_b, middle_b], axis=1)
    spread_j = spread_row(joined_b)
    type_two = reduce_col(
        jnp.concatenate(
            [flat_dot(spread_j[:, :q_cols], attend_b), flat_dot(spread_j[:, q_cols:], right_b)],
            axis=1,
        )
    )
    projected = type_two[:, :width_a]
    right_raw = type_two[:, width_a:]
    right_n, scale_r = norm_forward(right_raw, w_gains[1])
    laurel = hidden + right_n
    proj_n, scale_p = norm_forward(projected, w_gains[2])
    gated_sum = inputs + proj_n
    mixture = (gated_sum + laurel) * HALF_ROOT
    ffn_n, scale_f = norm_forward(mixture, w_gains[3])
    ffn_b = ffn_n.astype(bf16)
    spread_f = spread_col(ffn_b)
    gateup_pair = jnp.concatenate([gateup_b[0], gateup_b[1]], axis=1)
    gate_up = reduce_row(flat_dot(spread_f, gateup_pair))
    gate_raw = gate_up[:, :ff_here]
    up_raw = gate_up[:, ff_here:]
    act_b = (jax.nn.gelu(gate_raw, approximate=True) * up_raw).astype(bf16)
    spread_a = spread_row(act_b)
    down_raw = reduce_col(flat_dot(spread_a, down_b))
    down_n, scale_d = norm_forward(down_raw, w_gains[4])
    block_out = mixture + down_n
    out_b = block_out.astype(bf16)
    spread_o = spread_col(out_b)
    pgate = reduce_row(flat_dot(spread_o, pergate_b))
    extras = per_layer.astype(single_float)
    pact_b = (jax.nn.gelu(pgate, approximate=True) * extras).astype(bf16)
    spread_p = spread_row(pact_b)
    perproj = reduce_col(flat_dot(spread_p, perproj_b))
    perproj_n, scale_pp = norm_forward(perproj, w_gains[5])
    result = (block_out + perproj_n).astype(bf16)
    upstream = cotangent.astype(single_float)
    gain_grads = [None, None, None, None, None, None]
    d_perproj, gain_grads[5] = norm_backward(perproj, scale_pp, w_gains[5], upstream)
    grads_five = grads_col(d_perproj.astype(bf16))
    dw_perproj = inner_rows(spread_p, grads_five)
    d_pact = reduce_row(against(grads_five, perproj_b))
    gelu_out, pullback = jax.vjp(lambda v: jax.nn.gelu(v, approximate=True), pgate)
    (d_pgate,) = pullback(d_pact * extras)
    grads_four = grads_row(d_pgate.astype(bf16))
    dw_pergate = inner_rows(spread_o, grads_four)
    d_out = upstream + reduce_col(against(grads_four, pergate_b))
    d_down, gain_grads[4] = norm_backward(down_raw, scale_d, w_gains[4], d_out)
    grads_three = grads_col(d_down.astype(bf16))
    dw_down = inner_rows(spread_a, grads_three)
    d_act = reduce_row(against(grads_three, down_b))
    act_out, pullback = jax.vjp(lambda a, b: jax.nn.gelu(a, approximate=True) * b, gate_raw, up_raw)
    d_gate, d_up = pullback(d_act)
    local_two = jnp.concatenate([d_gate, d_up], axis=1).astype(bf16)
    grads_two = grads_row(local_two)
    dw_gateup = jnp.stack(
        [inner_rows(spread_f, grads_two[:, :ff_here]), inner_rows(spread_f, grads_two[:, ff_here:])]
    )
    d_ffn = reduce_col(
        against(grads_two[:, :ff_here], gateup_b[0]) + against(grads_two[:, ff_here:], gateup_b[1])
    )
    d_mix_norm, gain_grads[3] = norm_backward(mixture, scale_f, w_gains[3], d_ffn)
    d_half = (d_out + d_mix_norm) * HALF_ROOT
    d_proj, gain_grads[2] = norm_backward(projected, scale_p, w_gains[2], d_half)
    d_right, gain_grads[1] = norm_backward(right_raw, scale_r, w_gains[1], d_half)
    grads_one = grads_col(jnp.concatenate([d_proj, d_right], axis=1).astype(bf16))
    dw_attend = inner_rows(spread_j[:, :q_cols], grads_one[:, :width_a])
    dw_right = inner_rows(spread_j[:, q_cols:], grads_one[:, width_a:])
    d_joined = reduce_row(
        jnp.concatenate(
            [against(grads_one[:, :width_a], attend_b), against(grads_one[:, width_a:], right_b)],
            axis=1,
        )
    )
    d_attended = d_joined[:, :q_cols].astype(bf16).reshape(token_batch, local_heads, HEAD_WIDTH)
    d_middle = d_joined[:, q_cols:]
    d_queries, d_key_sel, d_value_sel = attention_backward(
        queries,
        key_sel,
        value_sel,
        d_attended,
        block_peaks,
        block_totals,
        own_places,
        all_places,
        length,
        piece_starts,
    )
    single_hot_mask = (
        key_value_heads[:, None] == jnp.arange(KEY_VALUE_HEADS, dtype=jnp.int32)[None, :]
    ).astype(single_float)
    key_gradient = jnp.sum(d_key_sel[:, :, None, :] * single_hot_mask[None, :, :, None], axis=1)
    value_gradient = jnp.sum(d_value_sel[:, :, None, :] * single_hot_mask[None, :, :, None], axis=1)
    key_gradient, value_gradient = lax.psum((key_gradient, value_gradient), ("row", "col"))
    local_key_gradient = lax.dynamic_slice_in_dim(
        key_gradient, row_place * token_batch, token_batch, 0
    ).reshape(token_batch, KEY_VALUE_HEADS * HEAD_WIDTH)
    local_value_gradient = lax.dynamic_slice_in_dim(
        value_gradient, row_place * token_batch, token_batch, 0
    ).reshape(token_batch, KEY_VALUE_HEADS * HEAD_WIDTH)
    query_out, pullback = jax.vjp(
        lambda r, g: query_form(r, g, own_cos, own_sin), query_raw, query_gains
    )
    d_query_raw, dg_query = pullback(d_queries)
    key_tile = jnp.broadcast_to(key_gain, (token_batch, 1, HEAD_WIDTH))
    key_out, pullback = jax.vjp(lambda r, g: key_form(r, g, own_cos, own_sin), key_raw, key_tile)
    d_key_raw, dg_key_rows = pullback(
        jnp.concatenate([local_key_gradient, local_value_gradient], axis=1)
    )
    slice_rows = token_batch // col_devs
    dg_key = jnp.sum(
        lax.dynamic_slice_in_dim(dg_key_rows, column_place * slice_rows, slice_rows, 0), axis=(0, 1)
    )
    grads_zero = grads_row(jnp.concatenate([d_query_raw, d_middle, d_key_raw], axis=1).astype(bf16))
    dw_query = inner_rows(spread_h, grads_zero[:, :q_cols])
    dw_left = inner_rows(spread_h, grads_zero[:, q_cols : q_cols + l_cols])
    key_grad_rows = grads_zero[:, q_cols + l_cols :]
    dw_keyval = inner_rows(spread_h, key_grad_rows)
    slab_width = kv_cols // col_devs
    d_hidden = reduce_col(
        against(grads_zero[:, :q_cols], query_b)
        + against(grads_zero[:, q_cols : q_cols + l_cols], left_b)
        + against(
            lax.dynamic_slice_in_dim(key_grad_rows, column_place * slab_width, slab_width, 1),
            lax.dynamic_slice_in_dim(keyval_b, column_place * slab_width, slab_width, 1),
        )
    )
    d_in, gain_grads[0] = norm_backward(inputs, scale_in, w_gains[0], d_hidden + d_half)
    grad_input = (d_half + d_in).astype(bf16)
    g_query, g_keyval, g_attend, g_gateup, g_down, g_left, g_right, g_pergate, g_perproj = (
        lax.psum_scatter(dw_query, "dp", scatter_dimension=1, tiled=True),
        lax.psum_scatter(dw_keyval, "dp", scatter_dimension=1, tiled=True),
        lax.psum_scatter(dw_attend, "dp", scatter_dimension=1, tiled=True),
        lax.psum_scatter(dw_gateup, "dp", scatter_dimension=2, tiled=True),
        lax.psum_scatter(dw_down, "dp", scatter_dimension=1, tiled=True),
        lax.psum_scatter(dw_left, "dp", scatter_dimension=1, tiled=True),
        lax.psum_scatter(dw_right, "dp", scatter_dimension=1, tiled=True),
        lax.psum_scatter(dw_pergate, "dp", scatter_dimension=1, tiled=True),
        lax.psum_scatter(dw_perproj, "dp", scatter_dimension=1, tiled=True),
    )
    gain_full = lax.dynamic_update_slice_in_dim(
        jnp.zeros((6, MODEL_WIDTH), single_float), jnp.stack(gain_grads), row_place * width_a, 1
    )
    head_full = lax.dynamic_update_slice_in_dim(
        jnp.zeros((QUERY_HEADS + 1, HEAD_WIDTH), single_float),
        dg_query,
        column_place * local_heads,
        0,
    )
    head_full = head_full.at[QUERY_HEADS].add(dg_key)
    logit_here = lax.dynamic_update_slice_in_dim(
        jnp.full((QUERY_HEADS,), NEGATIVE, single_float),
        jnp.max(block_peaks, axis=(0, 2)),
        column_place * local_heads,
        0,
    )

    def combine(left_part, right_part):
        return (
            left_part[0] + right_part[0],
            left_part[1] + right_part[1],
            jnp.maximum(left_part[2], right_part[2]),
        )

    gain_sum, head_sum, logit_top = joined(
        (gain_full, head_full, logit_here), ("dp", "row", "col"), combine
    )
    g_gains = lax.dynamic_slice_in_dim(gain_sum, row_place * width_a, width_a, 1)
    lead_device = (column_place == 0) & (data_at == 0)
    solo_device = lead_device & (row_place == 0)
    squares = jnp.float32(0.0)
    for gradient in (g_query, g_attend, g_gateup, g_down, g_left, g_right, g_pergate, g_perproj):
        squares = squares + jnp.sum(gradient * gradient)
    squares = squares + jnp.where(column_place == 0, jnp.sum(g_keyval * g_keyval), 0.0)
    squares = squares + jnp.where(lead_device, jnp.sum(g_gains * g_gains), 0.0)
    squares = squares + jnp.where(solo_device, jnp.sum(head_sum * head_sum), 0.0)
    grad_norm = jnp.sqrt(lax.psum(squares, ("dp", "row", "col")))
    clip_scale = CLIP / jnp.maximum(grad_norm, CLIP)
    scale_factors = LOGIT_CAP / jnp.maximum(logit_top, LOGIT_CAP)
    weights = (
        w_query,
        key_value_weight,
        w_attend,
        w_gateup,
        w_down,
        w_left,
        w_right,
        w_pergate,
        w_perproj,
        w_gains,
        w_heads,
    )
    moments = (
        m_query,
        key_value_first_moment,
        m_attend,
        m_gateup,
        m_down,
        m_left,
        m_right,
        m_pergate,
        m_perproj,
        m_gains,
        m_heads,
    )
    seconds = (
        v_query,
        key_value_second_moment,
        v_attend,
        v_gateup,
        v_down,
        v_left,
        v_right,
        v_pergate,
        v_perproj,
        v_gains,
        v_heads,
    )
    gradients = (
        g_query,
        g_keyval,
        g_attend,
        g_gateup,
        g_down,
        g_left,
        g_right,
        g_pergate,
        g_perproj,
        g_gains,
        head_sum,
    )
    step_rates = (
        MODEL_WIDTH ** (-0.5),
        MODEL_WIDTH ** (-0.5),
        (QUERY_HEADS * HEAD_WIDTH) ** (-0.5),
        MODEL_WIDTH ** (-0.5),
        FF ** (-0.5),
        MODEL_WIDTH ** (-0.5),
        RANK ** (-0.5),
        MODEL_WIDTH ** (-0.5),
        PLD ** (-0.5),
        GAIN_RATE,
        HEAD_RATE,
    )
    decays = (DECAY, DECAY, DECAY, DECAY, DECAY, DECAY, DECAY, DECAY, DECAY, 0.0, 0.0)
    updated = [
        adamw_step(
            weights[k], moments[k], seconds[k], gradients[k] * clip_scale, step_rates[k], decays[k]
        )
        for k in range(11)
    ]
    head_scale = jnp.sqrt(scale_factors)
    q_width = w_query.shape[1]
    q_head = (
        (column_place * data_devs + data_at) * q_width + jnp.arange(q_width, dtype=jnp.int32)
    ) // HEAD_WIDTH
    q_factor = jnp.sum(
        jnp.where(
            q_head[:, None] == jnp.arange(QUERY_HEADS, dtype=jnp.int32)[None, :],
            head_scale[None, :],
            0.0,
        ),
        axis=1,
    )
    new_query = updated[0][2] * q_factor[None, :]
    kv_width = key_value_weight.shape[1]
    key_value_index = data_at * kv_width + jnp.arange(kv_width, dtype=jnp.int32)
    key_value_scale = jnp.sqrt(
        jnp.min(scale_factors.reshape(KEY_VALUE_HEADS, QUERY_HEADS // KEY_VALUE_HEADS), axis=1)
    )
    key_value_choice = jnp.sum(
        jnp.where(
            (key_value_index // HEAD_WIDTH)[:, None]
            == jnp.arange(KEY_VALUE_HEADS, dtype=jnp.int32)[None, :],
            key_value_scale[None, :],
            0.0,
        ),
        axis=1,
    )
    key_value_factor = jnp.where(
        key_value_index < KEY_VALUE_HEADS * HEAD_WIDTH, key_value_choice, 1.0
    )
    new_keyval = updated[1][2] * key_value_factor[None, :]
    return (
        result,
        grad_input,
        grad_norm,
        scale_factors,
        updated[0][0],
        updated[0][1],
        new_query,
        updated[1][0],
        updated[1][1],
        new_keyval,
        updated[2][0],
        updated[2][1],
        updated[2][2],
        updated[3][0],
        updated[3][1],
        updated[3][2],
        updated[4][0],
        updated[4][1],
        updated[4][2],
        updated[5][0],
        updated[5][1],
        updated[5][2],
        updated[6][0],
        updated[6][1],
        updated[6][2],
        updated[7][0],
        updated[7][1],
        updated[7][2],
        updated[8][0],
        updated[8][1],
        updated[8][2],
        updated[9][0],
        updated[9][1],
        updated[9][2],
        updated[10][0],
        updated[10][1],
        updated[10][2],
    )


def solution(mesh):
    placed = (
        P(("dp", "col"), "row"),
        P(("dp", "row"), "col"),
        P(("dp", "col"), "row"),
        P(),
        P(),
        P("row", ("col", "dp")),
        P("row", ("col", "dp")),
        P("row", ("col", "dp")),
        P("row", "dp"),
        P("row", "dp"),
        P("row", "dp"),
        P("col", ("row", "dp")),
        P("col", ("row", "dp")),
        P("col", ("row", "dp")),
        P(None, "row", ("col", "dp")),
        P(None, "row", ("col", "dp")),
        P(None, "row", ("col", "dp")),
        P("col", ("row", "dp")),
        P("col", ("row", "dp")),
        P("col", ("row", "dp")),
        P("row", ("col", "dp")),
        P("row", ("col", "dp")),
        P("row", ("col", "dp")),
        P("col", ("row", "dp")),
        P("col", ("row", "dp")),
        P("col", ("row", "dp")),
        P("row", ("col", "dp")),
        P("row", ("col", "dp")),
        P("row", ("col", "dp")),
        P("col", ("row", "dp")),
        P("col", ("row", "dp")),
        P("col", ("row", "dp")),
        P(None, "row"),
        P(None, "row"),
        P(None, "row"),
        P(),
        P(),
        P(),
    )
    fits = (
        mesh.shape["col"] == KEY_VALUE_HEADS
        and mesh.shape["row"] * KEY_VALUE_HEADS == QUERY_HEADS
        and mesh.shape["dp"] == mesh.shape["row"]
    )
    return jax.shard_map(
        line_device if fits else per_device,
        mesh=mesh,
        in_specs=placed,
        out_specs=(
            P(("dp", "col"), "row"),
            P(("dp", "col"), "row"),
            P(),
            P(),
            P("row", ("col", "dp")),
            P("row", ("col", "dp")),
            P("row", ("col", "dp")),
            P("row", "dp"),
            P("row", "dp"),
            P("row", "dp"),
            P("col", ("row", "dp")),
            P("col", ("row", "dp")),
            P("col", ("row", "dp")),
            P(None, "row", ("col", "dp")),
            P(None, "row", ("col", "dp")),
            P(None, "row", ("col", "dp")),
            P("col", ("row", "dp")),
            P("col", ("row", "dp")),
            P("col", ("row", "dp")),
            P("row", ("col", "dp")),
            P("row", ("col", "dp")),
            P("row", ("col", "dp")),
            P("col", ("row", "dp")),
            P("col", ("row", "dp")),
            P("col", ("row", "dp")),
            P("row", ("col", "dp")),
            P("row", ("col", "dp")),
            P("row", ("col", "dp")),
            P("col", ("row", "dp")),
            P("col", ("row", "dp")),
            P("col", ("row", "dp")),
            P(None, "row"),
            P(None, "row"),
            P(None, "row"),
            P(),
            P(),
            P(),
        ),
        check_vma=False,
    )
```

```python
import jax
import jax.numpy as jnp
from jax import lax
from jax.experimental import pallas as pl
from jax.experimental.pallas import tpu as pltpu
from jax.sharding import PartitionSpec as P

MODEL_WIDTH = 2048
QUERY_HEADS = 8
KEY_VALUE_HEADS = 2
HEAD_WIDTH = 256
FF = 8192
RANK = 64
PLD = 256
IMG = 256
STEP = 10


EPS = 1e-06
ROPE_BASE = 1000000.0
BETA_ONE = 0.5
BETA_TWO = 0.5
ADAM_EPS = 1e-08
DECAY = 0.01
CLIP = 1.0
LOGIT_CAP = 4.0
GAIN_RATE = 0.6
HEAD_RATE = 0.1
HALF_ROOT = 0.7071067811865476
NEGATIVE = -1e30


def joined(part, axis, combine):
    gathered = jax.tree.map(lambda a: lax.all_gather(a, axis), part)

    def take(source):
        return jax.tree.map(lambda a: lax.dynamic_index_in_dim(a, source, 0, False), gathered)

    return lax.fori_loop(
        1, lax.axis_size(axis), lambda source, state: combine(state, take(source)), take(0)
    )


def row_total(values_in):
    return lax.psum(values_in, "row")


def spread_col(values_in):
    return lax.all_gather(values_in, "col", axis=0, tiled=True)


def reduce_row(values_in):
    return lax.psum_scatter(values_in, "row", scatter_dimension=0, tiled=True)


def spread_row(values_in):
    return lax.all_gather(values_in, "row", axis=0, tiled=True)


def reduce_col(values_in):
    return lax.psum_scatter(values_in, "col", scatter_dimension=0, tiled=True)


def grads_col(values_in):
    return lax.all_gather(values_in, "col", axis=0, tiled=True)


def grads_row(values_in):
    return lax.all_gather(values_in, "row", axis=0, tiled=True)


def inner_rows(left_mat, right_mat):
    return lax.dot_general(
        left_mat, right_mat, (((0,), (0,)), ((), ())), preferred_element_type=jnp.float32
    )


def against(grad_mat, weight_mat):
    return lax.dot_general(
        grad_mat, weight_mat, (((1,), (1,)), ((), ())), preferred_element_type=jnp.float32
    )


def flat_dot(left_mat, right_mat):
    return jnp.dot(left_mat, right_mat, preferred_element_type=jnp.float32)


def norm_forward(values_in, gain_vec):
    total_sq = row_total(jnp.sum(values_in * values_in, axis=-1, keepdims=True))
    norm_scale = lax.rsqrt(total_sq / MODEL_WIDTH + EPS)
    return (values_in * norm_scale * gain_vec, norm_scale)


def norm_backward(values_in, norm_scale, gain_vec, grad_out):
    weighted = grad_out * gain_vec
    inner_sum = row_total(jnp.sum(weighted * values_in, axis=-1, keepdims=True))
    grad_in = norm_scale * weighted - values_in * (norm_scale * norm_scale * norm_scale) * (
        inner_sum / MODEL_WIDTH
    )
    return (grad_in, jnp.sum(grad_out * values_in * norm_scale, axis=0))


def norm_rows(values_in, gain_vec):
    return (
        values_in
        * lax.rsqrt(jnp.mean(values_in * values_in, axis=-1, keepdims=True) + EPS)
        * gain_vec
    )


def rope_tables(places, feat_width):
    half_width = feat_width // 2
    powers = jnp.arange(half_width, dtype=jnp.int32).astype(jnp.float32) * (2.0 / feat_width)
    frequency = jnp.power(jnp.float32(ROPE_BASE), -powers)
    angles = places.astype(jnp.float32)[:, None] * frequency[None, :]
    return (jnp.cos(angles), jnp.sin(angles))


def rotate(values_in, cos_tab, sin_tab):
    half_width = values_in.shape[-1] // 2
    part_one = values_in[..., :half_width]
    part_two = values_in[..., half_width:]
    cos_row = cos_tab[:, None, :]
    sin_row = sin_tab[:, None, :]
    return jnp.concatenate(
        [part_one * cos_row - part_two * sin_row, part_two * cos_row + part_one * sin_row], axis=-1
    )


def query_form(unscaled_rows, gain_rows, cos_tab, sin_tab):
    shaped = unscaled_rows.reshape(unscaled_rows.shape[0], gain_rows.shape[0], HEAD_WIDTH)
    return rotate(norm_rows(shaped, gain_rows[None]), cos_tab, sin_tab)


def key_form(unscaled_rows, gain_vec, cos_tab, sin_tab):
    count_of_rows = unscaled_rows.shape[0]
    key_rows = unscaled_rows[:, : KEY_VALUE_HEADS * HEAD_WIDTH].reshape(
        count_of_rows, KEY_VALUE_HEADS, HEAD_WIDTH
    )
    value_rows = unscaled_rows[:, KEY_VALUE_HEADS * HEAD_WIDTH :].reshape(
        count_of_rows, KEY_VALUE_HEADS, HEAD_WIDTH
    )
    key_rows = rotate(norm_rows(key_rows, gain_vec), cos_tab, sin_tab)
    value_rows = norm_rows(value_rows, 1.0)
    return jnp.concatenate(
        [
            key_rows.reshape(count_of_rows, KEY_VALUE_HEADS * HEAD_WIDTH),
            value_rows.reshape(count_of_rows, KEY_VALUE_HEADS * HEAD_WIDTH),
        ],
        axis=1,
    )


def piece_of(places, starts):
    inside = (places[:, None] >= starts[None, :]) & (places[:, None] < starts[None, :] + IMG)
    labels = jnp.arange(1, starts.shape[0] + 1, dtype=jnp.int32)
    return jnp.sum(jnp.where(inside, labels[None, :], 0), axis=1) - 1


def visible(query_places, key_places, query_pieces, key_pieces, length):
    causal = key_places[None, :] <= query_places[:, None]
    same_piece = (query_pieces[:, None] == key_pieces[None, :]) & (query_pieces[:, None] >= 0)
    return (key_places[None, :] < length) & (causal | same_piece)


def block_mask(own_places, key_places, key_pieces, length, starts):
    return visible(own_places, key_places, piece_of(own_places, starts), key_pieces, length)


def attention_forward(queries, key_sel, value_sel, own_places, key_places, length, starts):
    count_of_rows, head_count = (queries.shape[0], queries.shape[1])
    block_size = min(512, count_of_rows)
    key_pieces = piece_of(key_places, starts)
    stacked = queries.reshape(count_of_rows // block_size, block_size, head_count, HEAD_WIDTH)

    def one_block(element):
        block_rows, block_at = element
        allowed = block_mask(own_places, key_places, key_pieces, length, starts)
        scores = jnp.einsum("qhd,khd->hqk", block_rows, key_sel, preferred_element_type=jnp.float32)
        masked = jnp.where(allowed[None], scores, NEGATIVE)
        peak_row = jnp.max(masked, axis=-1, keepdims=True)
        raw_weights = jnp.where(allowed[None], jnp.exp(masked - peak_row), 0.0)
        total_row = jnp.sum(raw_weights, axis=-1, keepdims=True)
        attn_probs = (raw_weights / total_row).astype(jnp.bfloat16)
        outputs = jnp.einsum(
            "hqk,khd->qhd", attn_probs, value_sel, preferred_element_type=jnp.float32
        )
        return (outputs, peak_row[..., 0], total_row[..., 0])

    return lax.map(one_block, (stacked, jnp.arange(count_of_rows // block_size, dtype=jnp.int32)))


def attention_backward(
    queries,
    key_sel,
    value_sel,
    grad_attended,
    block_peaks,
    block_totals,
    own_places,
    key_places,
    length,
    starts,
):
    count_of_rows, head_count = (queries.shape[0], queries.shape[1])
    block_size = min(512, count_of_rows)
    block_count = count_of_rows // block_size
    key_pieces = piece_of(key_places, starts)
    stacked = queries.reshape(block_count, block_size, head_count, HEAD_WIDTH)
    grad_stacked = grad_attended.reshape(block_count, block_size, head_count, HEAD_WIDTH)

    def one_block(carry, element):
        dk_sum, dv_sum = carry
        block_rows, grad_rows, peak_row, total_row, block_at = element
        allowed = block_mask(own_places, key_places, key_pieces, length, starts)
        scores = jnp.einsum("qhd,khd->hqk", block_rows, key_sel, preferred_element_type=jnp.float32)
        masked = jnp.where(allowed[None], scores, NEGATIVE)
        raw_weights = jnp.where(allowed[None], jnp.exp(masked - peak_row[..., None]), 0.0)
        attn_probs = raw_weights / total_row[..., None]
        probs_low = attn_probs.astype(jnp.bfloat16)
        grad_probs = jnp.einsum(
            "qhd,khd->hqk", grad_rows, value_sel, preferred_element_type=jnp.float32
        )
        delta_row = jnp.sum(attn_probs * grad_probs, axis=-1, keepdims=True)
        grad_scores = (attn_probs * (grad_probs - delta_row)).astype(jnp.bfloat16)
        grad_query = jnp.einsum(
            "hqk,khd->qhd", grad_scores, key_sel, preferred_element_type=jnp.float32
        )
        dk_sum = dk_sum + jnp.einsum(
            "hqk,qhd->khd", grad_scores, block_rows, preferred_element_type=jnp.float32
        )
        dv_sum = dv_sum + jnp.einsum(
            "hqk,qhd->khd", probs_low, grad_rows, preferred_element_type=jnp.float32
        )
        return ((dk_sum, dv_sum), grad_query)

    zero_keys = jnp.zeros(key_sel.shape, jnp.float32)
    (dk_sum, dv_sum), grad_query = lax.scan(
        one_block,
        (zero_keys, zero_keys),
        (
            stacked,
            grad_stacked,
            block_peaks,
            block_totals,
            jnp.arange(block_count, dtype=jnp.int32),
        ),
    )
    return (grad_query.reshape(count_of_rows, head_count, HEAD_WIDTH), dk_sum, dv_sum)


def adamw_step(weight, moment_one, moment_two, gradient, rate, decay):
    moment_one = BETA_ONE * moment_one + (1.0 - BETA_ONE) * gradient
    moment_two = BETA_TWO * moment_two + (1.0 - BETA_TWO) * gradient * gradient
    mean_step = moment_one / (1.0 - BETA_ONE**STEP)
    spread = moment_two / (1.0 - BETA_TWO**STEP)
    return (
        moment_one,
        moment_two,
        weight - rate * (mean_step / (jnp.sqrt(spread) + ADAM_EPS) + decay * weight),
    )


MESH = pl.DeviceIdType.MESH
LOW = jnp.bfloat16
FULL = jnp.float32


def cost(micros, flops=0):
    return pl.CostEstimate(
        flops=flops, bytes_accessed=int(micros * 3.0e6), transcendentals=0
    )


def params(ident, mebibytes=48):
    return pltpu.CompilerParams(
        collective_id=ident, has_side_effects=True, vmem_limit_bytes=mebibytes * 2**20
    )


def push(source, target, send, recv, device):
    return pltpu.make_async_remote_copy(
        source, target, send, recv, device_id=device, device_id_type=MESH
    )


def greet_line(me, count, column, core):
    barrier = pltpu.get_barrier_semaphore()

    @pl.when(me > 0)
    def _():
        pl.semaphore_signal(barrier, inc=1, device_id={"row": me - 1}, device_id_type=MESH)

    @pl.when(me < count - 1)
    def _():
        pl.semaphore_signal(barrier, inc=1, device_id={"row": me + 1}, device_id_type=MESH)

    if core:
        pl.semaphore_signal(barrier, inc=1, device_id={"col": 1 - column}, device_id_type=MESH)

    ends = (me == 0) | (me == count - 1)

    @pl.when(ends)
    def _():
        pl.semaphore_wait(barrier, 1 + int(core))

    @pl.when(jnp.logical_not(ends))
    def _():
        pl.semaphore_wait(barrier, 2 + int(core))


def line_gather(block, ident, core, micros):
    count = lax.axis_size("row")

    def kernel(x_ref, o_ref, send_l, send_r, send_c, recv_l, recv_r, recv_c, local):
        me = lax.axis_index("row")
        column = lax.axis_index("col")

        def slot(source):
            return o_ref.at[column, source] if core else o_ref.at[source]

        def other(source):
            return o_ref.at[1 - column, source]

        def to_left(source, k):
            origin = x_ref if k == 0 else slot(source)
            return push(origin, slot(source), send_l.at[k], recv_r.at[k], {"row": me - 1})

        def to_right(source, k):
            origin = x_ref if k == 0 else slot(source)
            return push(origin, slot(source), send_r.at[k], recv_l.at[k], {"row": me + 1})

        def to_core(source, k):
            origin = x_ref if k == 0 else slot(source)
            return push(origin, slot(source), send_c.at[k], recv_c.at[k], {"col": 1 - column})

        def from_core(source, k):
            return push(other(source), other(source), send_c.at[k], recv_c.at[k], {"col": 1 - column})

        greet_line(me, count, column, core)

        @pl.when(me > 0)
        def _():
            to_left(me, 0).start()

        @pl.when(me < count - 1)
        def _():
            to_right(me, 0).start()

        if core:
            to_core(me, 0).start()
        own = pltpu.make_async_copy(x_ref, slot(me), local)
        own.start()
        for k in range(1, count):

            @pl.when(me - k >= 0)
            def _():
                push(slot(me - k), slot(me - k), send_r.at[k], recv_l.at[k - 1], {"row": me - 1}).wait_recv()

                @pl.when(me < count - 1)
                def _():
                    to_right(me - k, k).start()

                if core:
                    to_core(me - k, k).start()

            @pl.when(me + k < count)
            def _():
                push(slot(me + k), slot(me + k), send_l.at[k], recv_r.at[k - 1], {"row": me + 1}).wait_recv()

                @pl.when(me > 0)
                def _():
                    to_left(me + k, k).start()

                if core:
                    to_core(me + k, count - 1 + k).start()

        own.wait()

        @pl.when(me > 0)
        def _():
            to_left(me, 0).wait_send()

        @pl.when(me < count - 1)
        def _():
            to_right(me, 0).wait_send()

        if core:
            to_core(me, 0).wait_send()
            from_core(me, 0).wait_recv()
        for k in range(1, count):

            @pl.when(me - k >= 0)
            def _():
                @pl.when(me < count - 1)
                def _():
                    to_right(me - k, k).wait_send()

                if core:
                    to_core(me - k, k).wait_send()
                    from_core(me - k, k).wait_recv()

            @pl.when(me + k < count)
            def _():
                @pl.when(me > 0)
                def _():
                    to_left(me + k, k).wait_send()

                if core:
                    to_core(me + k, count - 1 + k).wait_send()
                    from_core(me + k, count - 1 + k).wait_recv()

    shape = ((2, count) if core else (count,)) + block.shape
    dma = pltpu.SemaphoreType.DMA
    return pl.pallas_call(
        kernel,
        out_shape=jax.ShapeDtypeStruct(shape, block.dtype),
        in_specs=[pl.BlockSpec(memory_space=pl.ANY)],
        out_specs=pl.BlockSpec(memory_space=pl.ANY),
        scratch_shapes=[
            dma((count,)),
            dma((count,)),
            dma((2 * count,)),
            dma((count,)),
            dma((count,)),
            dma((2 * count,)),
            dma,
        ],
        compiler_params=params(ident),
        cost_estimate=cost(micros),
    )(block)


def line_reduce(parts, ident, core, micros):
    count = lax.axis_size("row")
    high, wide = parts.shape[-2:]
    chunk = min(high, max(16, 65536 // wide))
    while high % chunk:
        chunk //= 2

    def kernel(x_ref, o_ref, c_buf, l_buf, r_buf, s_buf, send_l, send_r, send_c, recv_l, recv_r, recv_c):
        me = lax.axis_index("row")
        column = lax.axis_index("col")

        def mine(q):
            return x_ref.at[column, q] if core else x_ref.at[q]

        def core_copy(q):
            return push(x_ref.at[1 - column, q], c_buf.at[q], send_c.at[q], recv_c.at[q], {"col": 1 - column})

        def left_copy(q):
            return push(s_buf.at[q], l_buf.at[q], send_l.at[q], recv_l.at[q], {"row": me - 1})

        def right_copy(q):
            return push(s_buf.at[q], r_buf.at[q], send_r.at[q], recv_r.at[q], {"row": me + 1})

        def left_arrival(q):
            return push(s_buf.at[q], l_buf.at[q], send_l.at[q], recv_l.at[q], {"row": me + 1})

        def right_arrival(q):
            return push(s_buf.at[q], r_buf.at[q], send_r.at[q], recv_r.at[q], {"row": me - 1})

        def added(target, terms):
            @pl.loop(0, high // chunk)
            def _(at):
                rows = pl.ds(pl.multiple_of(at * chunk, chunk), chunk)
                total = terms[0][rows].astype(FULL)
                for term in terms[1:]:
                    total = total + term[rows].astype(FULL)
                target[rows] = total.astype(target.dtype)

        def base(q):
            return [mine(q)] + ([c_buf.at[q]] if core else [])

        greet_line(me, count, column, core)
        if core:
            for q in range(count):
                core_copy(q).start()

        def leftward(q):
            @pl.when(me > q)
            def _():
                if core:
                    core_copy(q).wait_recv()

                @pl.when(me < count - 1)
                def _():
                    left_arrival(q).wait_recv()
                    added(s_buf.at[q], base(q) + [l_buf.at[q]])

                @pl.when(me == count - 1)
                def _():
                    added(s_buf.at[q], base(q))

                left_copy(q).start()

        def rightward(q):
            @pl.when(me < q)
            def _():
                if core:
                    core_copy(q).wait_recv()

                @pl.when(me > 0)
                def _():
                    right_arrival(q).wait_recv()
                    added(s_buf.at[q], base(q) + [r_buf.at[q]])

                @pl.when(me == 0)
                def _():
                    added(s_buf.at[q], base(q))

                right_copy(q).start()

        for j in range(count - 1):

            @pl.when(me < count // 2)
            def _():
                rightward(count - 1 - j)

            leftward(j)

            @pl.when(me >= count // 2)
            def _():
                rightward(count - 1 - j)

        if core:
            core_copy(me).wait_recv()

        @pl.when(me < count - 1)
        def _():
            left_arrival(me).wait_recv()

        @pl.when(me > 0)
        def _():
            right_arrival(me).wait_recv()

        @pl.when(me == 0)
        def _():
            added(o_ref, base(me) + [l_buf.at[me]])

        @pl.when(me == count - 1)
        def _():
            added(o_ref, base(me) + [r_buf.at[me]])

        @pl.when((me > 0) & (me < count - 1))
        def _():
            added(o_ref, base(me) + [l_buf.at[me], r_buf.at[me]])

        for q in range(count):
            if core:
                core_copy(q).wait_send()

            @pl.when(me > q)
            def _():
                left_copy(q).wait_send()

            @pl.when(me < q)
            def _():
                right_copy(q).wait_send()

    dma = pltpu.SemaphoreType.DMA
    slots = (count, high, wide)
    vmem = pl.BlockSpec(memory_space=pltpu.VMEM)
    return pl.pallas_call(
        kernel,
        out_shape=jax.ShapeDtypeStruct((high, wide), FULL),
        in_specs=[vmem],
        out_specs=vmem,
        scratch_shapes=[
            pltpu.VMEM(slots if core else (1, 16, 128), parts.dtype),
            pltpu.VMEM(slots, parts.dtype),
            pltpu.VMEM(slots, parts.dtype),
            pltpu.VMEM(slots, parts.dtype),
        ]
        + [dma((count,))] * 6,
        compiler_params=params(ident),
        cost_estimate=cost(micros),
    )(parts)


class Line:
    def __init__(self, source, shape, place, core=False):
        self.source, self.shape, self.place, self.core = source, shape, place, core

    def semaphores(self, count, data):
        dma = pltpu.SemaphoreType.DMA
        return [dma((count,)), dma((count,)), dma((2 * count,))] * 2 + [dma]

    def bind(self, x_ref, o_ref, sems, spots, sizes):
        self.x_ref, self.o_ref, self.sems = x_ref, o_ref, sems
        self.me, self.column, self.at = spots
        self.count = sizes[0]

    def slot(self, source):
        return self.place(self.o_ref, self.column, source)

    def other(self, source):
        return self.place(self.o_ref, 1 - self.column, source)

    def to_left(self, source, k):
        origin = self.x_ref if k == 0 else self.slot(source)
        return push(origin, self.slot(source), self.sems[0].at[k], self.sems[4].at[k], {"row": self.me - 1})

    def to_right(self, source, k):
        origin = self.x_ref if k == 0 else self.slot(source)
        return push(origin, self.slot(source), self.sems[1].at[k], self.sems[3].at[k], {"row": self.me + 1})

    def to_core(self, source, k):
        origin = self.x_ref if k == 0 else self.slot(source)
        return push(origin, self.slot(source), self.sems[2].at[k], self.sems[5].at[k], {"col": 1 - self.column})

    def from_core(self, source, k):
        there = self.other(source)
        return push(there, there, self.sems[2].at[k], self.sems[5].at[k], {"col": 1 - self.column})

    def from_left(self, source, k):
        there = self.slot(source)
        return push(there, there, self.sems[1].at[k], self.sems[3].at[k - 1], {"row": self.me - 1})

    def from_right(self, source, k):
        there = self.slot(source)
        return push(there, there, self.sems[0].at[k], self.sems[4].at[k - 1], {"row": self.me + 1})

    def own(self):
        return pltpu.make_async_copy(self.x_ref, self.slot(self.me), self.sems[6])

    def start(self):
        me, count = self.me, self.count

        @pl.when(me > 0)
        def _():
            self.to_left(me, 0).start()

        @pl.when(me < count - 1)
        def _():
            self.to_right(me, 0).start()

        if self.core:
            self.to_core(me, 0).start()
        self.own().start()

    def step(self, k):
        me, count = self.me, self.count

        @pl.when(me - k >= 0)
        def _():
            self.from_left(me - k, k).wait_recv()

            @pl.when(me < count - 1)
            def _():
                self.to_right(me - k, k).start()

            if self.core:
                self.to_core(me - k, k).start()

        @pl.when(me + k < count)
        def _():
            self.from_right(me + k, k).wait_recv()

            @pl.when(me > 0)
            def _():
                self.to_left(me + k, k).start()

            if self.core:
                self.to_core(me + k, count - 1 + k).start()

    def finish(self):
        me, count = self.me, self.count
        self.own().wait()

        @pl.when(me > 0)
        def _():
            self.to_left(me, 0).wait_send()

        @pl.when(me < count - 1)
        def _():
            self.to_right(me, 0).wait_send()

        if self.core:
            self.to_core(me, 0).wait_send()
            self.from_core(me, 0).wait_recv()
        for k in range(1, count):

            @pl.when(me - k >= 0)
            def _():
                @pl.when(me < count - 1)
                def _():
                    self.to_right(me - k, k).wait_send()

                if self.core:
                    self.to_core(me - k, k).wait_send()
                    self.from_core(me - k, k).wait_recv()

            @pl.when(me + k < count)
            def _():
                @pl.when(me > 0)
                def _():
                    self.to_left(me + k, k).wait_send()

                if self.core:
                    self.to_core(me + k, count - 1 + k).wait_send()
                    self.from_core(me + k, count - 1 + k).wait_recv()


class Swap:
    def __init__(self, source, shape, take, place, axis="row"):
        self.source, self.shape, self.take, self.place = source, shape, take, place
        self.axis = axis

    def semaphores(self, count, data):
        size = count if self.axis == "row" else data
        return [pltpu.SemaphoreType.DMA((size,)), pltpu.SemaphoreType.DMA((size,))]

    def bind(self, x_ref, o_ref, sems, spots, sizes):
        self.x_ref, self.o_ref, self.sems = x_ref, o_ref, sems
        self.me = spots[0] if self.axis == "row" else spots[2]
        self.count = sizes[0] if self.axis == "row" else sizes[1]

    def copy(self, k):
        target = lax.rem(self.me + k, self.count)
        return push(
            self.take(self.x_ref, target),
            self.place(self.o_ref, self.me),
            self.sems[0].at[k],
            self.sems[1].at[k],
            {self.axis: target},
        )

    def own(self):
        return pltpu.make_async_copy(
            self.take(self.x_ref, self.me), self.place(self.o_ref, self.me), self.sems[0].at[0]
        )

    def start(self):
        for k in range(1, self.count):
            self.copy(k).start()
        self.own().start()

    def step(self, k):
        pass

    def finish(self):
        self.own().wait()
        for k in range(1, self.count):
            self.copy(k).wait_send()
            origin = lax.rem(self.me + self.count - k, self.count)
            there = self.place(self.o_ref, origin)
            push(there, there, self.sems[0].at[k], self.sems[1].at[k], {self.axis: origin}).wait_recv()


class Pair:
    core = True

    def __init__(self, source):
        self.source, self.shape = source, source.shape

    def semaphores(self, count, data):
        dma = pltpu.SemaphoreType.DMA
        return [dma, dma, dma]

    def bind(self, x_ref, o_ref, sems, spots, sizes):
        self.x_ref, self.o_ref, self.sems = x_ref, o_ref, sems
        self.column = spots[1]

    def copy(self):
        other = 1 - self.column
        return push(self.x_ref.at[other], self.o_ref.at[1], self.sems[0], self.sems[1], {"col": other})

    def own(self):
        return pltpu.make_async_copy(self.x_ref.at[self.column], self.o_ref.at[0], self.sems[2])

    def start(self):
        self.copy().start()
        self.own().start()

    def step(self, k):
        pass

    def finish(self):
        self.own().wait()
        self.copy().wait()


def transfers(items, ident, micros):
    count, data = lax.axis_size("row"), lax.axis_size("dp")
    kinds = [item.semaphores(count, data) for item in items]
    number = len(items)
    across = any(getattr(item, "axis", None) == "dp" for item in items)
    cores = any(getattr(item, "core", False) for item in items)

    def kernel(*refs):
        x_refs, o_refs, sems = refs[:number], refs[number : 2 * number], refs[2 * number :]
        me, column, at = lax.axis_index("row"), lax.axis_index("col"), lax.axis_index("dp")
        for item, x_ref, o_ref, kind in zip(items, x_refs, o_refs, kinds):
            item.bind(x_ref, o_ref, sems[: len(kind)], (me, column, at), (count, data))
            sems = sems[len(kind) :]
        barrier = pltpu.get_barrier_semaphore()
        for k in range(1, count):
            pl.semaphore_signal(
                barrier, inc=1, device_id={"row": lax.rem(me + k, count)}, device_id_type=MESH
            )
        if across:
            for k in range(1, data):
                pl.semaphore_signal(
                    barrier, inc=1, device_id={"dp": lax.rem(at + k, data)}, device_id_type=MESH
                )
        if cores:
            pl.semaphore_signal(barrier, inc=1, device_id={"col": 1 - column}, device_id_type=MESH)
        pl.semaphore_wait(barrier, count - 1 + (data - 1) * int(across) + int(cores))
        for item in items:
            item.start()
        for k in range(1, count):
            for item in items:
                item.step(k)
        for item in items:
            item.finish()

    anywhere = pl.BlockSpec(memory_space=pl.ANY)
    return pl.pallas_call(
        kernel,
        out_shape=[jax.ShapeDtypeStruct(item.shape, item.source.dtype) for item in items],
        in_specs=[anywhere] * number,
        out_specs=[anywhere] * number,
        scratch_shapes=sum(kinds, []),
        compiler_params=params(ident, 16),
        cost_estimate=cost(micros),
    )(*[item.source for item in items])


def shard_total(query_parts, kv_parts, flat_parts, ident):
    data = lax.axis_size("dp")
    half = data // 2

    def kernel(q_ref, kv_ref, f_ref, oq_ref, okv_ref, of_ref, q_buf, kv_buf, f_buf, *sems):
        column, at = lax.axis_index("col"), lax.axis_index("dp")
        barrier = pltpu.get_barrier_semaphore()
        for k in range(1, data):
            pl.semaphore_signal(barrier, inc=1, device_id={"dp": lax.rem(at + k, data)}, device_id_type=MESH)
        pl.semaphore_signal(barrier, inc=1, device_id={"col": 1 - column}, device_id_type=MESH)
        pl.semaphore_wait(barrier, data)
        mine = lax.rem(at, 2) == column

        def copies(k):
            target = lax.rem(at + k, data)
            device = {"dp": target}
            return (
                push(q_ref.at[target], q_buf.at[k], sems[0].at[k], sems[1].at[k], device),
                push(kv_ref.at[target // 2], kv_buf.at[k], sems[2].at[k], sems[3].at[k], device),
                push(f_ref.at[target], f_buf.at[k], sems[4].at[k], sems[5].at[k], device),
                lax.rem(target, 2) == column,
            )

        for k in range(1, data):
            query_copy, kv_copy, flat_copy, there = copies(k)
            query_copy.start()
            flat_copy.start()

            @pl.when(there)
            def _():
                kv_copy.start()

        for k in range(1, data):
            query_copy, kv_copy, flat_copy, there = copies(k)
            query_copy.wait()
            flat_copy.wait()

            @pl.when(there)
            def _():
                kv_copy.wait_send()

            @pl.when(mine)
            def _():
                kv_copy.wait_recv()

        def added(target, own, buf, chunk):
            @pl.loop(0, target.shape[0] // chunk)
            def _(step):
                rows = pl.ds(pl.multiple_of(step * chunk, chunk), chunk)
                total = own[rows].astype(FULL)
                for k in range(1, data):
                    total = total + buf[k, rows].astype(FULL)
                target[rows] = total

        share = push(okv_ref, okv_ref, sems[6], sems[7], {"col": 1 - column})

        @pl.when(mine)
        def _():
            added(okv_ref, kv_ref.at[at // 2], kv_buf, 128)
            share.start()

        added(oq_ref, q_ref.at[at], q_buf, 128)
        added(of_ref, f_ref.at[at], f_buf, 64)

        @pl.when(mine)
        def _():
            share.wait_send()

        @pl.when(jnp.logical_not(mine))
        def _():
            share.wait_recv()

    vmem = pl.BlockSpec(memory_space=pltpu.VMEM)
    dma = pltpu.SemaphoreType.DMA
    shapes = [query_parts.shape[1:], kv_parts.shape[1:], flat_parts.shape[1:]]
    return pl.pallas_call(
        kernel,
        out_shape=[jax.ShapeDtypeStruct(shape, FULL) for shape in shapes],
        in_specs=[vmem] * 3,
        out_specs=[vmem] * 3,
        scratch_shapes=[pltpu.VMEM((data,) + shape, LOW) for shape in shapes]
        + [dma((data,))] * 6
        + [dma, dma],
        compiler_params=params(ident),
        cost_estimate=cost(20),
    )(query_parts, kv_parts, flat_parts)


class Flow:
    def __init__(self, x_ref, blocks, own, core_out, core_in, left_in, right_in, sems):
        self.x_ref, self.blocks, self.own = x_ref, blocks, own
        self.core_out, self.core_in = core_out, core_in
        self.left_in, self.right_in = left_in, right_in
        self.sems = sems
        self.me, self.column = lax.axis_index("row"), lax.axis_index("col")
        self.count = blocks.shape[0]

    @staticmethod
    def scratch(count, share, width):
        dma = pltpu.SemaphoreType.DMA
        slots = (count, share, width)
        return [
            pltpu.VMEM((count, 2, share, width), LOW),
            pltpu.VMEM(slots, FULL),
            pltpu.VMEM(slots, LOW),
            pltpu.VMEM(slots, LOW),
            pltpu.VMEM(slots, LOW),
            pltpu.VMEM(slots, LOW),
        ], [dma((count,))] * 12 + [dma]

    def left(self):
        return {"row": self.me - 1}

    def right(self):
        return {"row": self.me + 1}

    def beside(self):
        return {"col": 1 - self.column}

    def to_left(self, source, k, origin):
        return push(origin, self.blocks.at[source, 0], self.sems[0].at[k], self.sems[4].at[k], self.left())

    def to_right(self, source, k, origin):
        return push(origin, self.blocks.at[source, 0], self.sems[1].at[k], self.sems[3].at[k], self.right())

    def to_core(self, source, origin):
        return push(origin, self.blocks.at[source, 1], self.sems[2].at[source], self.sems[5].at[source], self.beside())

    def back_core(self, q):
        return push(self.core_out.at[q], self.core_in.at[q], self.sems[6].at[q], self.sems[9].at[q], self.beside())

    def back_left(self, q):
        return push(self.core_out.at[q], self.left_in.at[q], self.sems[7].at[q], self.sems[10].at[q], self.left())

    def back_right(self, q):
        return push(self.core_out.at[q], self.right_in.at[q], self.sems[8].at[q], self.sems[11].at[q], self.right())

    def mine(self):
        return pltpu.make_async_copy(self.x_ref, self.blocks.at[self.me, 0], self.sems[12])

    def start(self):
        me, count = self.me, self.count
        greet_line(me, count, self.column, True)

        @pl.when(me > 0)
        def _():
            self.to_left(me, 0, self.x_ref).start()

        @pl.when(me < count - 1)
        def _():
            self.to_right(me, 0, self.x_ref).start()

        self.to_core(me, self.x_ref).start()
        self.mine().start()

    def arrive(self, k):
        me, count = self.me, self.count

        @pl.when(k == 0)
        def _():
            self.mine().wait()
            self.to_core(me, self.x_ref).wait()

        @pl.when((k > 0) & (me - k >= 0))
        def _():
            source = me - k
            block = self.blocks.at[source, 0]
            push(block, block, self.sems[1].at[k], self.sems[3].at[k - 1], self.left()).wait_recv()

            @pl.when(me < count - 1)
            def _():
                self.to_right(source, k, block).start()

            self.to_core(source, block).start()

        @pl.when((k > 0) & (me + k < count))
        def _():
            source = me + k
            block = self.blocks.at[source, 0]
            push(block, block, self.sems[0].at[k], self.sems[4].at[k - 1], self.right()).wait_recv()

            @pl.when(me > 0)
            def _():
                self.to_left(source, k, block).start()

            self.to_core(source, block).start()

        @pl.when((k > 0) & (me - k >= 0))
        def _():
            self.to_core(me - k, self.x_ref).wait()

        @pl.when((k > 0) & (me + k < count))
        def _():
            self.to_core(me + k, self.x_ref).wait()

    def visit(self, body):
        me, count = self.me, self.count

        @pl.loop(0, count)
        def _(k):
            self.arrive(k)

            @pl.loop(0, 2)
            def _(side):
                source = jnp.where(side == 0, me - k, me + k)

                @pl.when((source >= 0) & (source < count) & ((side == 0) | (k > 0)))
                def _():
                    body(source)
                    self.back_core(source).start()

    def added(self, target, terms):
        high, wide = target.shape
        step = min(high, max(16, 65536 // wide))

        @pl.loop(0, high // step)
        def _(at):
            rows = pl.ds(pl.multiple_of(at * step, step), step)
            total = terms[0][rows]
            for term in terms[1:]:
                total = total + term[rows].astype(FULL)
            target[rows] = total.astype(target.dtype)

    def give_back(self, t):
        me, count = self.me, self.count
        q_left = t - (count - 1 - me)
        q_right = count - 1 - (t - me)

        def leftward():
            q = q_left
            self.back_core(q).wait()

            @pl.when(me < count - 1)
            def _():
                push(self.left_in.at[q], self.left_in.at[q], self.sems[7].at[q], self.sems[10].at[q], self.right()).wait_recv()
                self.added(self.core_out.at[q], [self.own.at[q], self.core_in.at[q], self.left_in.at[q]])

            @pl.when(me == count - 1)
            def _():
                self.added(self.core_out.at[q], [self.own.at[q], self.core_in.at[q]])

            self.back_left(q).start()

        def rightward():
            q = q_right
            self.back_core(q).wait()

            @pl.when(me > 0)
            def _():
                push(self.right_in.at[q], self.right_in.at[q], self.sems[8].at[q], self.sems[11].at[q], self.left()).wait_recv()
                self.added(self.core_out.at[q], [self.own.at[q], self.core_in.at[q], self.right_in.at[q]])

            @pl.when(me == 0)
            def _():
                self.added(self.core_out.at[q], [self.own.at[q], self.core_in.at[q]])

            self.back_right(q).start()

        pl.when((q_left >= 0) & (q_left < me))(leftward)
        pl.when((t >= me) & (q_right > me))(rightward)

    def finish(self, o_ref):
        me, count = self.me, self.count
        self.back_core(me).wait()

        @pl.when(me < count - 1)
        def _():
            push(self.left_in.at[me], self.left_in.at[me], self.sems[7].at[me], self.sems[10].at[me], self.right()).wait_recv()

        @pl.when(me > 0)
        def _():
            push(self.right_in.at[me], self.right_in.at[me], self.sems[8].at[me], self.sems[11].at[me], self.left()).wait_recv()

        base = [self.own.at[me], self.core_in.at[me]]

        @pl.when(me == 0)
        def _():
            self.added(o_ref, base + [self.left_in.at[me]])

        @pl.when(me == count - 1)
        def _():
            self.added(o_ref, base + [self.right_in.at[me]])

        @pl.when((me > 0) & (me < count - 1))
        def _():
            self.added(o_ref, base + [self.left_in.at[me], self.right_in.at[me]])

        @pl.when(me > 0)
        def _():
            self.to_left(me, 0, self.x_ref).wait_send()

        @pl.when(me < count - 1)
        def _():
            self.to_right(me, 0, self.x_ref).wait_send()

        @pl.loop(1, count)
        def _(k):
            @pl.when((me - k >= 0) & (me < count - 1))
            def _():
                self.to_right(me - k, k, self.x_ref).wait_send()

            @pl.when((me + k < count) & (me > 0))
            def _():
                self.to_left(me + k, k, self.x_ref).wait_send()

        @pl.loop(0, count)
        def _(q):
            @pl.when(q < me)
            def _():
                self.back_left(q).wait_send()

            @pl.when(q > me)
            def _():
                self.back_right(q).wait_send()


GELU_ONE = 0.7978845608028654
GELU_TWO = 0.044715


def gelu_of(values_in):
    inner = GELU_ONE * (values_in + GELU_TWO * values_in * values_in * values_in)
    bend = jnp.tanh(inner)
    half = 0.5 * (1.0 + bend)
    slope = half + 0.5 * values_in * (1.0 - bend * bend) * GELU_ONE * (
        1.0 + 3.0 * GELU_TWO * values_in * values_in
    )
    return values_in * half, slope


def ffn_forward(block, gateup, down, ident):
    count = lax.axis_size("row")
    share, width = block.shape
    groups, _, _, part = gateup.shape
    hidden = groups * part
    out_cols = down.shape[2] // count
    rows = 2 * share

    def kernel(x_ref, gw_hbm, dw_hbm, o_ref, xt_hbm, at_hbm, g_hbm, u_hbm, *scratch):
        flow = Flow(x_ref, *scratch[:6], scratch[6:19])
        gw, dw, xt, at, act, gate, up = scratch[19:26]
        gw_sem, dw_sem, xt_sem, at_sem, g_sem, u_sem = scratch[26:]
        gw_load = pltpu.make_async_copy(gw_hbm, gw, gw_sem)
        dw_load = pltpu.make_async_copy(dw_hbm, dw, dw_sem)
        gw_load.start()
        dw_load.start()
        flow.start()
        gw_load.wait()
        dw_load.wait()

        def stores(source):
            return (
                pltpu.make_async_copy(gate.at[source], g_hbm.at[source], g_sem.at[source]),
                pltpu.make_async_copy(up.at[source], u_hbm.at[source], u_sem.at[source]),
            )

        def body(source):
            here = pl.ds(pl.multiple_of(source * rows, rows), rows)
            x = flow.blocks[source].reshape(rows, width)
            xt[:, here] = x.T

            @pl.loop(0, groups)
            def _(d):
                columns = pl.ds(pl.multiple_of(d * part, part), part)
                g = flat_dot(x, gw[d, 0])
                u = flat_dot(x, gw[d, 1])
                gate[source, :, columns] = g
                up[source, :, columns] = u
                act[:, columns] = (gelu_of(g)[0] * u).astype(LOW)

            for copy in stores(source):
                copy.start()
            at[:, here] = act[...].T
            for d in range(groups):
                out = flat_dot(act[...], dw[d])
                for s in range(count):
                    columns = slice((s * groups + d) * out_cols, (s * groups + d + 1) * out_cols)
                    piece = out[:, s * out_cols : (s + 1) * out_cols]
                    flow.own[source, :, columns] = piece[:share]
                    flow.core_out[source, :, columns] = piece[share:].astype(LOW)

        flow.visit(body)
        xt_store = pltpu.make_async_copy(xt, xt_hbm, xt_sem)
        at_store = pltpu.make_async_copy(at, at_hbm, at_sem)
        xt_store.start()
        at_store.start()

        @pl.loop(0, count - 1)
        def _(t):
            flow.give_back(t)

        flow.finish(o_ref)
        xt_store.wait()
        at_store.wait()

        @pl.loop(0, count)
        def _(source):
            for copy in stores(source):
                copy.wait()

    dma = pltpu.SemaphoreType.DMA
    buffers, sems = Flow.scratch(count, share, width)
    vmem, anywhere = pl.BlockSpec(memory_space=pltpu.VMEM), pl.BlockSpec(memory_space=pl.ANY)
    tokens = count * rows
    return pl.pallas_call(
        kernel,
        out_shape=[
            jax.ShapeDtypeStruct((share, width), FULL),
            jax.ShapeDtypeStruct((width, tokens), LOW),
            jax.ShapeDtypeStruct((hidden, tokens), LOW),
            jax.ShapeDtypeStruct((count, rows, hidden), FULL),
            jax.ShapeDtypeStruct((count, rows, hidden), FULL),
        ],
        in_specs=[vmem, anywhere, anywhere],
        out_specs=[vmem] + [anywhere] * 4,
        scratch_shapes=buffers
        + sems
        + [
            pltpu.VMEM(gateup.shape, LOW),
            pltpu.VMEM(down.shape, LOW),
            pltpu.VMEM((width, tokens), LOW),
            pltpu.VMEM((hidden, tokens), LOW),
            pltpu.VMEM((rows, hidden), LOW),
            pltpu.VMEM((count, rows, hidden), FULL),
            pltpu.VMEM((count, rows, hidden), FULL),
        ]
        + [dma, dma, dma, dma, dma((count,)), dma((count,))],
        compiler_params=params(ident, 60),
        cost_estimate=cost(80),
    )(block, gateup, down)


def ffn_backward(block, gateup, down, xt, at, gate, up, ident):
    count = lax.axis_size("row")
    share, width = block.shape
    groups, _, _, part = gateup.shape
    hidden = groups * part
    out_cols = down.shape[2] // count
    rows = 2 * share
    tokens = count * rows
    pieces = 3 * groups

    def kernel(x_ref, gw_hbm, dw_hbm, xt_hbm, at_hbm, g_hbm, u_hbm, o_ref, dgu_hbm, ddn_hbm, *scratch):
        flow = Flow(x_ref, *scratch[:6], scratch[6:19])
        gw, dw, xt_own, at_own, gate_own, up_own, d_gate, d_up, total, stage, stage_down = scratch[19:30]
        load_sems, g_sem, u_sem, out_sem, down_sem = scratch[30:]
        loads = [
            pltpu.make_async_copy(source, target, load_sems.at[k])
            for k, (source, target) in enumerate(
                [(dw_hbm, dw), (gw_hbm, gw), (xt_hbm, xt_own), (at_hbm, at_own)]
            )
        ]

        def fetches(source):
            return (
                pltpu.make_async_copy(g_hbm.at[source], gate_own.at[source], g_sem.at[source]),
                pltpu.make_async_copy(u_hbm.at[source], up_own.at[source], u_sem.at[source]),
            )

        for load in loads[:2]:
            load.start()

        @pl.loop(0, count)
        def _(source):
            for copy in fetches(source):
                copy.start()

        for load in loads[2:]:
            load.start()
        flow.start()
        loads[0].wait()
        loads[1].wait()

        def columns_of(s, d):
            return pl.ds(pl.multiple_of((s * groups + d) * out_cols, out_cols), out_cols)

        def body(source):
            for copy in fetches(source):
                copy.wait()
            grad = flow.blocks[source].reshape(rows, width)
            d_act = None
            for d in range(groups):
                cut = jnp.concatenate(
                    [
                        grad[:, (s * groups + d) * out_cols : (s * groups + d + 1) * out_cols]
                        for s in range(count)
                    ],
                    axis=1,
                )
                term = against(cut, dw[d])
                d_act = term if d_act is None else d_act + term
            total[:, :hidden] = d_act

            @pl.loop(0, groups)
            def _(d):
                columns = pl.ds(pl.multiple_of(d * part, part), part)
                grad_act = total[:, columns]
                curve, slope = gelu_of(gate_own[source, :, columns])
                d_gate[source, :, columns] = (grad_act * up_own[source, :, columns] * slope).astype(LOW)
                d_up[source, :, columns] = (grad_act * curve).astype(LOW)

            total[...] = jnp.zeros(total.shape, FULL)

            @pl.loop(0, groups)
            def _(d):
                columns = pl.ds(pl.multiple_of(d * part, part), part)
                total[...] += against(d_gate[source, :, columns], gw[d, 0]) + against(
                    d_up[source, :, columns], gw[d, 1]
                )

            flow.own[source] = total[:share]
            flow.core_out[source] = total[share:].astype(LOW)

        flow.visit(body)
        loads[2].wait()
        loads[3].wait()

        def gateup_store(d, which):
            return pltpu.make_async_copy(stage.at[which], dgu_hbm.at[d, which], out_sem.at[which])

        def down_store(d):
            return pltpu.make_async_copy(stage_down, ddn_hbm.at[d], down_sem)

        def weights(d):
            columns = pl.ds(pl.multiple_of(d * part, part), part)
            for which, grads in ((0, d_gate), (1, d_up)):

                @pl.when(d > 0)
                def _():
                    gateup_store(d - 1, which).wait()

                right = grads[:, :, columns].reshape(tokens, part)

                @pl.loop(0, width // 512)
                def _(k):
                    high = pl.ds(pl.multiple_of(k * 512, 512), 512)
                    stage[which, high] = flat_dot(xt_own[high], right).astype(LOW)

                gateup_store(d, which).start()

            @pl.when(d > 0)
            def _():
                down_store(d - 1).wait()

            right = jnp.concatenate(
                [flow.blocks[:, :, :, columns_of(s, d)].reshape(tokens, out_cols) for s in range(count)],
                axis=1,
            )

            @pl.loop(0, hidden // 256)
            def _(k):
                high = pl.ds(pl.multiple_of(k * 256, 256), 256)
                stage_down[high] = flat_dot(at_own[high], right).astype(LOW)

            down_store(d).start()

        @pl.loop(0, count - 1)
        def _(t):
            flow.give_back(t)
            weights(t)

        weights(groups - 1)
        for which in range(2):
            gateup_store(groups - 1, which).wait()
        down_store(groups - 1).wait()
        flow.finish(o_ref)

    dma = pltpu.SemaphoreType.DMA
    buffers, sems = Flow.scratch(count, share, width)
    vmem, anywhere = pl.BlockSpec(memory_space=pltpu.VMEM), pl.BlockSpec(memory_space=pl.ANY)
    return pl.pallas_call(
        kernel,
        out_shape=[
            jax.ShapeDtypeStruct((share, width), FULL),
            jax.ShapeDtypeStruct(gateup.shape, LOW),
            jax.ShapeDtypeStruct(down.shape, LOW),
        ],
        in_specs=[vmem] + [anywhere] * 6,
        out_specs=[vmem, anywhere, anywhere],
        scratch_shapes=buffers
        + sems
        + [
            pltpu.VMEM(gateup.shape, LOW),
            pltpu.VMEM(down.shape, LOW),
            pltpu.VMEM((width, tokens), LOW),
            pltpu.VMEM((hidden, tokens), LOW),
            pltpu.VMEM((count, rows, hidden), FULL),
            pltpu.VMEM((count, rows, hidden), FULL),
            pltpu.VMEM((count, rows, hidden), LOW),
            pltpu.VMEM((count, rows, hidden), LOW),
            pltpu.VMEM((rows, width), FULL),
            pltpu.VMEM((2, width, part), LOW),
            pltpu.VMEM((hidden, count * out_cols), LOW),
        ]
        + [dma((4,)), dma((count,)), dma((count,)), dma((2,)), dma],
        compiler_params=params(ident, 62),
        cost_estimate=cost(90),
    )(block, gateup, down, xt, at, gate, up)


def small_total(values_in, axes, max_rows, ident):
    sizes = [lax.axis_size(axis) for axis in axes]
    high = values_in.shape[0]

    def kernel(x_ref, o_ref, *scratch):
        slots, sends, recvs = (scratch[k :: 3] for k in range(3))
        barrier = pltpu.get_barrier_semaphore()
        spots = [lax.axis_index(axis) for axis in axes]
        for axis, size, me in zip(axes, sizes, spots):
            for k in range(1, size):
                pl.semaphore_signal(
                    barrier, inc=1, device_id={axis: lax.rem(me + k, size)}, device_id_type=MESH
                )
        pl.semaphore_wait(barrier, sum(sizes) - len(sizes))
        for at, (axis, size, me) in enumerate(zip(axes, sizes, spots)):
            buf, send, recv = slots[at], sends[at], recvs[at]
            buf[me] = x_ref[...] if at == 0 else o_ref[...]
            for k in range(1, size):
                push(buf.at[me], buf.at[me], send.at[k], recv.at[k], {axis: lax.rem(me + k, size)}).start()
            for k in range(1, size):
                origin = lax.rem(me + size - k, size)
                push(buf.at[origin], buf.at[origin], send.at[k], recv.at[k], {axis: origin}).wait()
            total = buf[0]
            for k in range(1, size):
                total = total + buf[k]
            o_ref[...] = total
            if max_rows:
                top = buf[0, high - max_rows :]
                for k in range(1, size):
                    top = jnp.maximum(top, buf[k, high - max_rows :])
                o_ref[high - max_rows :] = top

    dma = pltpu.SemaphoreType.DMA
    vmem = pl.BlockSpec(memory_space=pltpu.VMEM)
    scratch = []
    for size in sizes:
        scratch += [pltpu.VMEM((size,) + values_in.shape, FULL), dma((size,)), dma((size,))]
    return pl.pallas_call(
        kernel,
        out_shape=jax.ShapeDtypeStruct(values_in.shape, FULL),
        in_specs=[vmem],
        out_specs=vmem,
        scratch_shapes=scratch,
        compiler_params=params(ident, 16),
        cost_estimate=cost(4 * len(sizes)),
    )(values_in)


def allowed_block(at, high, width, spans):
    key_places = lax.broadcasted_iota(jnp.int32, (high, width), 1)
    query_places = at * high + lax.broadcasted_iota(jnp.int32, (high, width), 0)
    seen = key_places <= query_places
    for piece in range(spans.shape[0] - 1):
        start = spans[piece + 1]
        both = (
            (key_places >= start)
            & (key_places < start + IMG)
            & (query_places >= start)
            & (query_places < start + IMG)
        )
        seen = seen | both
    return seen & (key_places < spans[0])


def softmax_block(block_rows, keys, allowed):
    scores = against(block_rows, keys)
    masked = jnp.where(allowed, scores, NEGATIVE)
    peak_row = jnp.max(masked, axis=-1, keepdims=True)
    raw_weights = jnp.where(allowed, jnp.exp(masked - peak_row), 0.0)
    return raw_weights / jnp.sum(raw_weights, axis=-1, keepdims=True), peak_row


def head_forward(queries, keys, values, spans):
    rows = queries.shape[0]
    step = min(256, rows)

    def kernel(spans_ref, q_ref, k_ref, v_ref, o_ref, top_ref):
        top_ref[...] = jnp.full(top_ref.shape, NEGATIVE, FULL)

        @pl.loop(0, rows // step)
        def _(at):
            here = pl.ds(pl.multiple_of(at * step, step), step)
            allowed = allowed_block(at, step, keys.shape[0], spans_ref)
            probs, peak_row = softmax_block(q_ref[here], k_ref[...], allowed)
            o_ref[here] = flat_dot(probs.astype(LOW), v_ref[...]).astype(LOW)
            top_ref[...] = jnp.maximum(top_ref[...], jnp.max(peak_row))

    vmem = pl.BlockSpec(memory_space=pltpu.VMEM)
    return pl.pallas_call(
        kernel,
        out_shape=(
            jax.ShapeDtypeStruct(queries.shape, LOW),
            jax.ShapeDtypeStruct((8, 128), FULL),
        ),
        in_specs=[pl.BlockSpec(memory_space=pltpu.SMEM), vmem, vmem, vmem],
        out_specs=(vmem, vmem),
        compiler_params=pltpu.CompilerParams(vmem_limit_bytes=48 * 2**20),
        cost_estimate=cost(10),
    )(spans, queries, keys, values)


def head_backward(queries, keys, values, grads, spans):
    rows = queries.shape[0]
    step = min(256, rows)

    def kernel(spans_ref, q_ref, k_ref, v_ref, g_ref, dq_ref, dk_ref, dv_ref):
        dk_ref[...] = jnp.zeros(dk_ref.shape, FULL)
        dv_ref[...] = jnp.zeros(dv_ref.shape, FULL)

        @pl.loop(0, rows // step)
        def _(at):
            here = pl.ds(pl.multiple_of(at * step, step), step)
            allowed = allowed_block(at, step, keys.shape[0], spans_ref)
            block_rows, grad_rows = q_ref[here], g_ref[here]
            probs, _ = softmax_block(block_rows, k_ref[...], allowed)
            grad_probs = against(grad_rows, v_ref[...])
            delta_row = jnp.sum(probs * grad_probs, axis=-1, keepdims=True)
            grad_scores = (probs * (grad_probs - delta_row)).astype(LOW)
            dq_ref[here] = flat_dot(grad_scores, k_ref[...])
            dk_ref[...] += inner_rows(grad_scores, block_rows)
            dv_ref[...] += inner_rows(probs.astype(LOW), grad_rows)

    vmem = pl.BlockSpec(memory_space=pltpu.VMEM)
    return pl.pallas_call(
        kernel,
        out_shape=(jax.ShapeDtypeStruct(queries.shape, FULL),)
        + (jax.ShapeDtypeStruct(keys.shape, FULL),) * 2,
        in_specs=[pl.BlockSpec(memory_space=pltpu.SMEM)] + [vmem] * 4,
        out_specs=(vmem, vmem, vmem),
        compiler_params=pltpu.CompilerParams(vmem_limit_bytes=48 * 2**20),
        cost_estimate=cost(20),
    )(spans, queries, keys, values, grads)


def whole_norm(values_in, gain_vec):
    scale = lax.rsqrt(jnp.mean(values_in * values_in, axis=-1, keepdims=True) + EPS)
    return values_in * scale * gain_vec, scale


def whole_norm_backward(values_in, scale, gain_vec, grad_out):
    weighted = grad_out * gain_vec
    inner = jnp.mean(weighted * values_in, axis=-1, keepdims=True)
    return (
        scale * weighted - values_in * (scale * scale * scale) * inner,
        jnp.sum(grad_out * values_in * scale, axis=0),
    )


def turn(values_in, cos_tab, sin_tab):
    half_width = values_in.shape[-1] // 2
    one, two = values_in[:, :half_width], values_in[:, half_width:]
    return jnp.concatenate(
        [one * cos_tab - two * sin_tab, two * cos_tab + one * sin_tab], axis=1
    )


def turn_back(values_in, cos_tab, sin_tab):
    return turn(values_in, cos_tab, -sin_tab)


def swap_row(values_in, split, concat, tiled=True):
    return lax.all_to_all(values_in, "row", split, concat, tiled=tiled)


def line_device(
    activations,
    per_layer,
    cotangent,
    lengths,
    starts,
    w_query,
    m_query,
    v_query,
    key_value_weight,
    key_value_first_moment,
    key_value_second_moment,
    w_attend,
    m_attend,
    v_attend,
    w_gateup,
    m_gateup,
    v_gateup,
    w_down,
    m_down,
    v_down,
    w_left,
    m_left,
    v_left,
    w_right,
    m_right,
    v_right,
    w_pergate,
    m_pergate,
    v_pergate,
    w_perproj,
    m_perproj,
    v_perproj,
    w_gains,
    m_gains,
    v_gains,
    w_heads,
    m_heads,
    v_heads,
):
    rows_n = lax.axis_size("row")
    cols_n = lax.axis_size("col")
    data_n = lax.axis_size("dp")
    me = lax.axis_index("row")
    column = lax.axis_index("col")
    data_at = lax.axis_index("dp")
    half_tok, width_a = activations.shape
    tokens = half_tok * cols_n
    share = half_tok // rows_n
    quarter = tokens // rows_n
    width = width_a * rows_n

    ff_part = w_gateup.shape[2] // rows_n
    out_cols = w_down.shape[1]
    heads_here = data_n
    smalls = (w_left, w_right, w_pergate, w_perproj)
    flat = jnp.concatenate([w.astype(LOW).reshape(-1) for w in smalls]).reshape(-1, 128)
    flat_rows = flat.shape[0]

    def columns_of(at, size):
        return pl.ds(pl.multiple_of(at * size, size), size)

    gateup_own, down_own, attend_own, upstream, qkv_w, flat = transfers(
        [
            Swap(
                w_gateup.astype(LOW),
                (2, width, ff_part),
                lambda ref, q: ref.at[:, :, columns_of(q, ff_part)],
                lambda ref, at: ref.at[:, columns_of(at, width_a), :],
            ),
            Swap(
                w_down.astype(LOW).reshape(data_n, rows_n, ff_part, out_cols),
                (data_n, ff_part, rows_n * out_cols),
                lambda ref, q: ref.at[:, q],
                lambda ref, at: ref.at[:, :, columns_of(at, out_cols)],
            ),
            Swap(
                w_attend.astype(LOW).reshape(rows_n, HEAD_WIDTH, out_cols),
                (HEAD_WIDTH, rows_n * out_cols),
                lambda ref, q: ref.at[q],
                lambda ref, at: ref.at[:, columns_of(at, out_cols)],
            ),
            Swap(
                cotangent,
                (share, width),
                lambda ref, q: ref.at[columns_of(q, share)],
                lambda ref, at: ref.at[:, columns_of(at, width_a)],
            ),
            Swap(
                jnp.concatenate([w_query, key_value_weight], axis=1).astype(LOW),
                (data_n, width_a, 2 * HEAD_WIDTH),
                lambda ref, q: ref,
                lambda ref, at: ref.at[at],
                "dp",
            ),
            Swap(
                flat,
                (data_n * flat_rows, 128),
                lambda ref, q: ref,
                lambda ref, at: ref.at[columns_of(at, flat_rows)],
                "dp",
            ),
        ],
        1,
        90,
    )
    gateup_all = lax.all_gather(gateup_own, "dp")
    down_all = lax.all_gather(down_own, "dp")
    query_w = qkv_w[:, :, :HEAD_WIDTH]
    kv_w = qkv_w[:, :, HEAD_WIDTH:]
    key_w = lax.dynamic_index_in_dim(kv_w, column, 0, False)
    value_w = lax.dynamic_index_in_dim(kv_w, KEY_VALUE_HEADS + column, 0, False)
    whole_acts, whole_kv, head_w, flat, gains, extras, attend_all = transfers(
        [
            Line(
                activations,
                (tokens, width),
                lambda ref, c, r: ref.at[columns_of(c, half_tok), columns_of(r, width_a)],
                True,
            ),
            Line(
                jnp.stack([key_w, value_w]),
                (2, width, HEAD_WIDTH),
                lambda ref, c, r: ref.at[:, columns_of(r, width_a)],
            ),
            Swap(
                query_w,
                (width, HEAD_WIDTH),
                lambda ref, q: ref.at[q],
                lambda ref, at: ref.at[columns_of(at, width_a)],
            ),
            Line(
                flat, (cols_n, rows_n) + flat.shape, lambda ref, c, r: ref.at[c, r], True
            ),
            Line(w_gains, (6, width), lambda ref, c, r: ref.at[:, columns_of(r, width_a)]),
            Line(
                per_layer,
                (tokens, PLD),
                lambda ref, c, r: ref.at[columns_of(r, quarter), columns_of(c, PLD // cols_n)],
                True,
            ),
            Swap(
                attend_own,
                (data_n, HEAD_WIDTH, rows_n * out_cols),
                lambda ref, q: ref,
                lambda ref, at: ref.at[at],
                "dp",
            ),
        ],
        2,
        115,
    )
    attend_w = (
        attend_all.reshape(data_n, HEAD_WIDTH, rows_n, out_cols)
        .transpose(1, 2, 0, 3)
        .reshape(HEAD_WIDTH, width)
    )
    flat = flat.reshape(cols_n, rows_n, data_n, -1)
    cuts = []
    start = 0
    for w in smalls:
        cuts.append(flat[..., start : start + w.size].reshape((cols_n, rows_n, data_n) + w.shape))
        start += w.size
    left_w = cuts[0].transpose(1, 3, 0, 2, 4).reshape(width, -1)
    right_w = cuts[1].transpose(0, 3, 1, 2, 4).reshape(-1, width)
    pergate_w = cuts[2].transpose(1, 3, 0, 2, 4).reshape(width, -1)
    perproj_w = cuts[3].transpose(0, 3, 1, 2, 4).reshape(-1, width)
    upstream = upstream.astype(FULL)
    token_at = column * half_tok + me * share
    extras = lax.dynamic_slice_in_dim(extras, token_at, share, 0).astype(FULL)
    length = lax.dynamic_index_in_dim(lengths, data_at, 0, keepdims=True)
    piece_starts = lax.dynamic_index_in_dim(starts, data_at, 0, keepdims=False)
    spans = jnp.concatenate([length, piece_starts])

    whole_hidden, whole_scale = whole_norm(whole_acts.astype(FULL), gains[0])
    whole_hidden = whole_hidden.astype(LOW)
    inputs = lax.dynamic_slice_in_dim(whole_acts, token_at, share, 0).astype(FULL)
    query_raw = flat_dot(whole_hidden, head_w)
    all_key_raw = flat_dot(whole_hidden, whole_kv[0])
    all_value_raw = flat_dot(whole_hidden, whole_kv[1])
    query_gain = lax.dynamic_index_in_dim(w_heads, column * rows_n + me, 0, True)
    key_gain = w_heads[QUERY_HEADS:]
    all_cos, all_sin = rope_tables(jnp.arange(tokens, dtype=jnp.int32), HEAD_WIDTH)
    own_cos = lax.dynamic_slice_in_dim(all_cos, me * quarter, quarter, 0)
    own_sin = lax.dynamic_slice_in_dim(all_sin, me * quarter, quarter, 0)
    query_n, query_scale = whole_norm(query_raw, query_gain)
    queries = turn(query_n, all_cos, all_sin).astype(LOW)
    keys = turn(whole_norm(all_key_raw, key_gain)[0], all_cos, all_sin).astype(LOW)
    values = whole_norm(all_value_raw, 1.0)[0].astype(LOW)
    attended, top = head_forward(queries, keys, values, spans)
    key_raw = lax.dynamic_slice_in_dim(all_key_raw, me * quarter, quarter, 0)
    value_raw = lax.dynamic_slice_in_dim(all_value_raw, me * quarter, quarter, 0)
    _, key_scale = whole_norm(key_raw, key_gain)
    _, value_scale = whole_norm(value_raw, 1.0)
    down_all = down_all.reshape(data_n, data_n * ff_part, -1)

    def shares(parts):
        return parts.astype(LOW).reshape(cols_n, rows_n, share, width)

    hidden, _ = whole_norm(inputs, gains[0])
    hidden_low = hidden.astype(LOW)
    middle = flat_dot(hidden_low, left_w).astype(LOW)
    right_raw = flat_dot(middle, right_w)
    right_n, scale_r = whole_norm(right_raw, gains[1])
    projected = line_reduce(shares(flat_dot(attended, attend_w)), 5, True, 45)
    proj_n, scale_p = whole_norm(projected, gains[2])
    mixture = ((inputs + proj_n) + (hidden + right_n)) * HALF_ROOT
    ffn_n, scale_f = whole_norm(mixture, gains[3])
    down_raw, spread_ft, act_t, gate_raw, up_raw = ffn_forward(
        ffn_n.astype(LOW), gateup_all, down_all, 6
    )
    down_n, scale_d = whole_norm(down_raw, gains[4])
    block_out = mixture + down_n
    out_low = block_out.astype(LOW)
    pgate = flat_dot(out_low, pergate_w)
    pact = (jax.nn.gelu(pgate, approximate=True) * extras).astype(LOW)
    perproj = flat_dot(pact, perproj_w)
    perproj_n, scale_pp = whole_norm(perproj, gains[5])
    result = (block_out + perproj_n).astype(LOW)

    gain_grads = [None] * 6
    d_perproj, gain_grads[5] = whole_norm_backward(perproj, scale_pp, gains[5], upstream)
    d_perproj = d_perproj.astype(LOW)
    dw_perproj = inner_rows(pact, d_perproj)
    d_pact = against(d_perproj, perproj_w)
    _, pullback = jax.vjp(lambda v: jax.nn.gelu(v, approximate=True), pgate)
    (d_pgate,) = pullback(d_pact * extras)
    d_pgate = d_pgate.astype(LOW)
    dw_pergate = inner_rows(out_low, d_pgate)
    d_out = upstream + against(d_pgate, pergate_w)
    d_down, gain_grads[4] = whole_norm_backward(down_raw, scale_d, gains[4], d_out)
    d_ffn, dw_gateup, dw_down = ffn_backward(
        d_down.astype(LOW), gateup_all, down_all, spread_ft, act_t, gate_raw, up_raw, 8
    )
    g_gateup = lax.psum_scatter(dw_gateup, "dp", scatter_dimension=0)
    g_down = lax.psum_scatter(
        dw_down.reshape(data_n, data_n, ff_part, -1), "dp", scatter_dimension=0
    )
    d_mix, gain_grads[3] = whole_norm_backward(mixture, scale_f, gains[3], d_ffn)
    d_half = (d_out + d_mix) * HALF_ROOT
    d_proj, gain_grads[2] = whole_norm_backward(projected, scale_p, gains[2], d_half)
    spread_p, result = transfers(
        [
            Line(
                d_proj.astype(LOW),
                (cols_n, rows_n, share, width),
                lambda ref, c, r: ref.at[c, r],
                True,
            ),
            Swap(
                result,
                (half_tok, width_a),
                lambda ref, q: ref.at[:, columns_of(q, width_a)],
                lambda ref, at: ref.at[columns_of(at, share)],
            ),
        ],
        10,
        50,
    )
    spread_p = spread_p.reshape(tokens, width)
    d_right, gain_grads[1] = whole_norm_backward(right_raw, scale_r, gains[1], d_half)
    d_right = d_right.astype(LOW)
    dw_right = inner_rows(middle, d_right)
    d_middle = against(d_right, right_w).astype(LOW)
    dw_left = inner_rows(hidden_low, d_middle)
    d_hidden_share = d_half + against(d_middle, left_w)
    inner_share = jnp.sum(d_hidden_share * gains[0] * inputs, axis=1)
    half_low, share_low = d_half.astype(LOW), d_hidden_share.astype(LOW)
    d_attended = against(spread_p, attend_w).astype(LOW)
    dw_attend = inner_rows(attended, spread_p).astype(LOW)
    d_queries, d_keys, d_values = head_backward(queries, keys, values, d_attended, spans)
    kv_parts = jnp.concatenate(
        [
            d_keys.astype(LOW).reshape(rows_n, quarter, HEAD_WIDTH),
            d_values.astype(LOW).reshape(rows_n, quarter, HEAD_WIDTH),
        ],
        axis=1,
    )
    d_kv = line_reduce(kv_parts, 11, False, 20)
    d_q_raw, dg_query = whole_norm_backward(
        query_raw, query_scale, query_gain, turn_back(d_queries, all_cos, all_sin)
    )
    d_k_raw, dg_key = whole_norm_backward(
        key_raw, key_scale, key_gain, turn_back(d_kv[:quarter], own_cos, own_sin)
    )
    d_v_raw, _ = whole_norm_backward(value_raw, value_scale, 1.0, d_kv[quarter:])
    d_raw = jnp.concatenate([d_q_raw, d_k_raw, d_v_raw], axis=0).astype(LOW)
    spread_q = line_gather(d_raw, 12, False, 55)
    d_q_all = spread_q[:, :tokens]
    d_k_all = spread_q[:, tokens : tokens + quarter].reshape(tokens, HEAD_WIDTH)
    d_v_all = spread_q[:, tokens + quarter :].reshape(tokens, HEAD_WIDTH)
    d_hidden = against(d_k_all, key_w) + against(d_v_all, value_w)
    for k in range(heads_here):
        d_hidden = d_hidden + against(d_q_all[k], query_w[k])
    acts = activations.astype(FULL)
    gains_here = lax.dynamic_slice_in_dim(w_gains, 0, 1, 0)[0]
    scale_here = lax.dynamic_slice_in_dim(whole_scale, column * half_tok, half_tok, 0)
    own_acts = lax.dynamic_slice_in_dim(whole_acts, me * width_a, width_a, 1).astype(FULL)
    inner = jnp.sum(d_hidden * gains_here * own_acts, axis=1)
    inner = lax.dynamic_update_slice_in_dim(
        inner, lax.dynamic_slice_in_dim(inner, token_at, share, 0) + inner_share, token_at, 0
    ).reshape(-1, 128)

    spread_h = lax.dynamic_slice_in_dim(whole_hidden, me * width_a, width_a, 1)
    dw_query = jnp.stack([inner_rows(spread_h, d_q_all[k]).astype(LOW) for k in range(heads_here)])
    dw_kv = jnp.stack(
        [inner_rows(spread_h, d_k_all).astype(LOW), inner_rows(spread_h, d_v_all).astype(LOW)]
    )
    g_attend = lax.psum_scatter(
        dw_attend.reshape(HEAD_WIDTH, rows_n, data_n, out_cols).transpose(2, 0, 1, 3).reshape(data_n, HEAD_WIDTH, -1),
        "dp",
        scatter_dimension=0,
    )

    def to_shards(grad, rows_first):
        if rows_first:
            cut = grad.reshape(rows_n, width_a, cols_n, data_n, -1).transpose(2, 0, 3, 1, 4)
        else:
            cut = grad.reshape(cols_n, -1, rows_n, data_n, out_cols).transpose(0, 2, 3, 1, 4)
        return cut.astype(LOW).reshape(cols_n, rows_n, data_n, -1)

    flat_grads = jnp.concatenate(
        [
            to_shards(dw_left, True),
            to_shards(dw_right, False),
            to_shards(dw_pergate, True),
            to_shards(dw_perproj, False),
        ],
        axis=3,
    ).reshape(cols_n, rows_n, data_n * flat_rows, 128)
    flat_grads = line_reduce(flat_grads, 17, True, 28).astype(LOW).reshape(data_n, flat_rows, 128)
    g_query, g_keyval, flat_grads = shard_total(dw_query, dw_kv, flat_grads, 13)
    squares = jnp.where(column == 0, jnp.sum(g_keyval * g_keyval), 0.0)
    for gradient in (g_query, g_attend, g_gateup, g_down, flat_grads):
        gradient = gradient.astype(FULL)
        squares = squares + jnp.sum(gradient * gradient)
    g_gateup, g_down, g_attend, half_here, share_here, d_hidden, inner = transfers(
        [
            Swap(
                g_gateup,
                w_gateup.shape,
                lambda ref, q: ref.at[:, columns_of(q, width_a), :],
                lambda ref, at: ref.at[:, :, columns_of(at, ff_part)],
            ),
            Swap(
                g_down,
                (data_n, rows_n, ff_part, out_cols),
                lambda ref, q: ref.at[:, :, columns_of(q, out_cols)],
                lambda ref, at: ref.at[:, at],
            ),
            Swap(
                g_attend,
                (rows_n, HEAD_WIDTH, out_cols),
                lambda ref, q: ref.at[:, columns_of(q, out_cols)],
                lambda ref, at: ref.at[at],
            ),
            Swap(
                half_low,
                (half_tok, width_a),
                lambda ref, q: ref.at[:, columns_of(q, width_a)],
                lambda ref, at: ref.at[columns_of(at, share)],
            ),
            Swap(
                share_low,
                (half_tok, width_a),
                lambda ref, q: ref.at[:, columns_of(q, width_a)],
                lambda ref, at: ref.at[columns_of(at, share)],
            ),
            Pair(d_hidden.astype(LOW).reshape(cols_n, half_tok, width_a)),
            Line(inner, (cols_n, rows_n) + inner.shape, lambda ref, c, r: ref.at[c, r], True),
        ],
        14,
        100,
    )
    g_gateup = g_gateup.astype(FULL)
    g_down = g_down.reshape(w_down.shape).astype(FULL)
    g_attend = g_attend.reshape(w_attend.shape).astype(FULL)
    flat_grads = flat_grads.reshape(-1)
    small_grads = []
    start = 0
    for w in smalls:
        small_grads.append(flat_grads[start : start + w.size].reshape(w.shape))
        start += w.size
    g_left, g_right, g_pergate, g_perproj = small_grads

    inner = jnp.sum(inner, axis=(0, 1)).reshape(cols_n, half_tok) / MODEL_WIDTH
    inner = lax.dynamic_index_in_dim(inner, column, 0, False)[:, None]
    d_hidden = d_hidden[0].astype(FULL) + d_hidden[1].astype(FULL) + share_here.astype(FULL)
    grad_input = (
        half_here.astype(FULL)
        + scale_here * d_hidden * gains_here
        - acts * (scale_here * scale_here * scale_here) * inner
    ).astype(LOW)
    gain_zero = jnp.sum(d_hidden * acts * scale_here, axis=0)

    gain_full = jnp.stack(
        [
            lax.dynamic_update_slice_in_dim(
                jnp.zeros((width,), FULL), gain_zero, me * width_a, 0
            )
        ]
        + gain_grads[1:]
    )
    head_full = lax.dynamic_update_slice_in_dim(
        jnp.zeros((QUERY_HEADS + 1, HEAD_WIDTH), FULL), dg_query[None], column * rows_n + me, 0
    )
    head_full = head_full.at[QUERY_HEADS].add(dg_key)
    logit_row = lax.dynamic_update_slice_in_dim(
        jnp.full((128,), NEGATIVE, FULL), top[0, :1], column * rows_n + me, 0
    )
    gain_rows = gain_full.size // 128
    head_rows = head_full.size // 128
    pad_rows = -(gain_rows + head_rows) % 8
    small = jnp.concatenate(
        [
            gain_full.reshape(-1, 128),
            head_full.reshape(-1, 128),
            jnp.broadcast_to(squares, (pad_rows, 128)),
            jnp.broadcast_to(logit_row[None], (8, 128)),
        ]
    )
    small = small_total(small, ("col", "row", "dp"), 8, 15)
    gain_sum = small[:gain_rows].reshape(6, width)
    head_sum = small[gain_rows : gain_rows + head_rows].reshape(QUERY_HEADS + 1, HEAD_WIDTH)
    logit_top = small[-1, :QUERY_HEADS]
    g_gains = lax.dynamic_slice_in_dim(gain_sum, me * width_a, width_a, 1)
    squares = small[gain_rows + head_rows, 0]
    squares = squares + jnp.sum(gain_sum * gain_sum) + jnp.sum(head_sum * head_sum)
    grad_norm = jnp.sqrt(squares)
    clip_scale = CLIP / jnp.maximum(grad_norm, CLIP)
    scale_factors = LOGIT_CAP / jnp.maximum(logit_top, LOGIT_CAP)
    weights = (
        w_query,
        key_value_weight,
        w_attend,
        w_gateup,
        w_down,
        w_left,
        w_right,
        w_pergate,
        w_perproj,
        w_gains,
        w_heads,
    )
    moments = (
        m_query,
        key_value_first_moment,
        m_attend,
        m_gateup,
        m_down,
        m_left,
        m_right,
        m_pergate,
        m_perproj,
        m_gains,
        m_heads,
    )
    seconds = (
        v_query,
        key_value_second_moment,
        v_attend,
        v_gateup,
        v_down,
        v_left,
        v_right,
        v_pergate,
        v_perproj,
        v_gains,
        v_heads,
    )
    gradients = (
        g_query,
        g_keyval,
        g_attend,
        g_gateup,
        g_down,
        g_left,
        g_right,
        g_pergate,
        g_perproj,
        g_gains,
        head_sum,
    )
    step_rates = (
        MODEL_WIDTH ** (-0.5),
        MODEL_WIDTH ** (-0.5),
        (QUERY_HEADS * HEAD_WIDTH) ** (-0.5),
        MODEL_WIDTH ** (-0.5),
        FF ** (-0.5),
        MODEL_WIDTH ** (-0.5),
        RANK ** (-0.5),
        MODEL_WIDTH ** (-0.5),
        PLD ** (-0.5),
        GAIN_RATE,
        HEAD_RATE,
    )
    decays = (DECAY, DECAY, DECAY, DECAY, DECAY, DECAY, DECAY, DECAY, DECAY, 0.0, 0.0)
    updated = [
        adamw_step(
            weights[k], moments[k], seconds[k], gradients[k] * clip_scale, step_rates[k], decays[k]
        )
        for k in range(11)
    ]
    head_scale = jnp.sqrt(scale_factors)
    q_width = w_query.shape[1]
    q_head = (
        (column * data_n + data_at) * q_width + jnp.arange(q_width, dtype=jnp.int32)
    ) // HEAD_WIDTH
    q_factor = jnp.sum(
        jnp.where(
            q_head[:, None] == jnp.arange(QUERY_HEADS, dtype=jnp.int32)[None, :],
            head_scale[None, :],
            0.0,
        ),
        axis=1,
    )
    new_query = updated[0][2] * q_factor[None, :]
    kv_width = key_value_weight.shape[1]
    key_value_index = data_at * kv_width + jnp.arange(kv_width, dtype=jnp.int32)
    key_value_scale = jnp.sqrt(
        jnp.min(scale_factors.reshape(KEY_VALUE_HEADS, QUERY_HEADS // KEY_VALUE_HEADS), axis=1)
    )
    key_value_choice = jnp.sum(
        jnp.where(
            (key_value_index // HEAD_WIDTH)[:, None]
            == jnp.arange(KEY_VALUE_HEADS, dtype=jnp.int32)[None, :],
            key_value_scale[None, :],
            0.0,
        ),
        axis=1,
    )
    key_value_factor = jnp.where(
        key_value_index < KEY_VALUE_HEADS * HEAD_WIDTH, key_value_choice, 1.0
    )
    new_keyval = updated[1][2] * key_value_factor[None, :]
    return (
        result,
        grad_input,
        grad_norm,
        scale_factors,
        updated[0][0],
        updated[0][1],
        new_query,
        updated[1][0],
        updated[1][1],
        new_keyval,
        updated[2][0],
        updated[2][1],
        updated[2][2],
        updated[3][0],
        updated[3][1],
        updated[3][2],
        updated[4][0],
        updated[4][1],
        updated[4][2],
        updated[5][0],
        updated[5][1],
        updated[5][2],
        updated[6][0],
        updated[6][1],
        updated[6][2],
        updated[7][0],
        updated[7][1],
        updated[7][2],
        updated[8][0],
        updated[8][1],
        updated[8][2],
        updated[9][0],
        updated[9][1],
        updated[9][2],
        updated[10][0],
        updated[10][1],
        updated[10][2],
    )


def per_device(
    activations,
    per_layer,
    cotangent,
    lengths,
    starts,
    w_query,
    m_query,
    v_query,
    key_value_weight,
    key_value_first_moment,
    key_value_second_moment,
    w_attend,
    m_attend,
    v_attend,
    w_gateup,
    m_gateup,
    v_gateup,
    w_down,
    m_down,
    v_down,
    w_left,
    m_left,
    v_left,
    w_right,
    m_right,
    v_right,
    w_pergate,
    m_pergate,
    v_pergate,
    w_perproj,
    m_perproj,
    v_perproj,
    w_gains,
    m_gains,
    v_gains,
    w_heads,
    m_heads,
    v_heads,
):
    row_devs = lax.axis_size("row")
    col_devs = lax.axis_size("col")
    data_devs = lax.axis_size("dp")
    row_place = lax.axis_index("row")
    column_place = lax.axis_index("col")
    data_at = lax.axis_index("dp")
    bf16 = jnp.bfloat16
    single_float = jnp.float32
    query_b, keyval_b, attend_b, gateup_b, down_b, left_b, right_b, pergate_b, perproj_b = (
        lax.all_gather(w_query.astype(bf16), "dp", axis=1, tiled=True),
        lax.all_gather(key_value_weight.astype(bf16), "dp", axis=1, tiled=True),
        lax.all_gather(w_attend.astype(bf16), "dp", axis=1, tiled=True),
        lax.all_gather(w_gateup.astype(bf16), "dp", axis=2, tiled=True),
        lax.all_gather(w_down.astype(bf16), "dp", axis=1, tiled=True),
        lax.all_gather(w_left.astype(bf16), "dp", axis=1, tiled=True),
        lax.all_gather(w_right.astype(bf16), "dp", axis=1, tiled=True),
        lax.all_gather(w_pergate.astype(bf16), "dp", axis=1, tiled=True),
        lax.all_gather(w_perproj.astype(bf16), "dp", axis=1, tiled=True),
    )
    inputs = activations.astype(single_float)
    tok_a, width_a = inputs.shape
    grouped_rows = tok_a * col_devs
    token_batch = grouped_rows // row_devs
    q_cols = query_b.shape[1]
    l_cols = left_b.shape[1]
    kv_cols = keyval_b.shape[1]
    ff_here = gateup_b.shape[2]
    local_heads = q_cols // HEAD_WIDTH
    length = lax.dynamic_index_in_dim(lengths, data_at, 0, keepdims=False)
    piece_starts = lax.dynamic_index_in_dim(starts, data_at, 0, keepdims=False)
    own_places = row_place * token_batch + jnp.arange(token_batch, dtype=jnp.int32)
    all_places = jnp.arange(grouped_rows, dtype=jnp.int32)
    own_cos, own_sin = rope_tables(own_places, HEAD_WIDTH)
    query_gains = lax.dynamic_slice_in_dim(w_heads, column_place * local_heads, local_heads, 0)
    key_gain = w_heads[QUERY_HEADS]
    hidden, scale_in = norm_forward(inputs, w_gains[0])
    hidden_b = hidden.astype(bf16)
    spread_h = spread_col(hidden_b)
    type_one = reduce_row(flat_dot(spread_h, jnp.concatenate([query_b, left_b], axis=1)))
    key_raw_all = lax.psum(flat_dot(spread_h, keyval_b), "row")
    all_cos, all_sin = rope_tables(all_places, HEAD_WIDTH)
    key_value_whole = key_form(key_raw_all, key_gain, all_cos, all_sin).astype(bf16)
    key_raw = lax.dynamic_slice_in_dim(key_raw_all, row_place * token_batch, token_batch, 0)
    query_raw = type_one[:, :q_cols]
    middle_b = type_one[:, q_cols : q_cols + l_cols].astype(bf16)
    queries = query_form(query_raw, query_gains, own_cos, own_sin).astype(bf16)
    key_value_heads = (column_place * local_heads + jnp.arange(local_heads, dtype=jnp.int32)) // (
        QUERY_HEADS // KEY_VALUE_HEADS
    )
    every_key = key_value_whole[:, : KEY_VALUE_HEADS * HEAD_WIDTH].reshape(
        grouped_rows, KEY_VALUE_HEADS, HEAD_WIDTH
    )
    every_value = key_value_whole[:, KEY_VALUE_HEADS * HEAD_WIDTH :].reshape(
        grouped_rows, KEY_VALUE_HEADS, HEAD_WIDTH
    )
    key_sel = jnp.take(every_key, key_value_heads, axis=1)
    value_sel = jnp.take(every_value, key_value_heads, axis=1)
    attended, block_peaks, block_totals = attention_forward(
        queries, key_sel, value_sel, own_places, all_places, length, piece_starts
    )
    attended_b = attended.reshape(token_batch, q_cols).astype(bf16)
    joined_b = jnp.concatenate([attended_b, middle_b], axis=1)
    spread_j = spread_row(joined_b)
    type_two = reduce_col(
        jnp.concatenate(
            [flat_dot(spread_j[:, :q_cols], attend_b), flat_dot(spread_j[:, q_cols:], right_b)],
            axis=1,
        )
    )
    projected = type_two[:, :width_a]
    right_raw = type_two[:, width_a:]
    right_n, scale_r = norm_forward(right_raw, w_gains[1])
    laurel = hidden + right_n
    proj_n, scale_p = norm_forward(projected, w_gains[2])
    gated_sum = inputs + proj_n
    mixture = (gated_sum + laurel) * HALF_ROOT
    ffn_n, scale_f = norm_forward(mixture, w_gains[3])
    ffn_b = ffn_n.astype(bf16)
    spread_f = spread_col(ffn_b)
    gateup_pair = jnp.concatenate([gateup_b[0], gateup_b[1]], axis=1)
    gate_up = reduce_row(flat_dot(spread_f, gateup_pair))
    gate_raw = gate_up[:, :ff_here]
    up_raw = gate_up[:, ff_here:]
    act_b = (jax.nn.gelu(gate_raw, approximate=True) * up_raw).astype(bf16)
    spread_a = spread_row(act_b)
    down_raw = reduce_col(flat_dot(spread_a, down_b))
    down_n, scale_d = norm_forward(down_raw, w_gains[4])
    block_out = mixture + down_n
    out_b = block_out.astype(bf16)
    spread_o = spread_col(out_b)
    pgate = reduce_row(flat_dot(spread_o, pergate_b))
    extras = per_layer.astype(single_float)
    pact_b = (jax.nn.gelu(pgate, approximate=True) * extras).astype(bf16)
    spread_p = spread_row(pact_b)
    perproj = reduce_col(flat_dot(spread_p, perproj_b))
    perproj_n, scale_pp = norm_forward(perproj, w_gains[5])
    result = (block_out + perproj_n).astype(bf16)
    upstream = cotangent.astype(single_float)
    gain_grads = [None, None, None, None, None, None]
    d_perproj, gain_grads[5] = norm_backward(perproj, scale_pp, w_gains[5], upstream)
    grads_five = grads_col(d_perproj.astype(bf16))
    dw_perproj = inner_rows(spread_p, grads_five)
    d_pact = reduce_row(against(grads_five, perproj_b))
    gelu_out, pullback = jax.vjp(lambda v: jax.nn.gelu(v, approximate=True), pgate)
    (d_pgate,) = pullback(d_pact * extras)
    grads_four = grads_row(d_pgate.astype(bf16))
    dw_pergate = inner_rows(spread_o, grads_four)
    d_out = upstream + reduce_col(against(grads_four, pergate_b))
    d_down, gain_grads[4] = norm_backward(down_raw, scale_d, w_gains[4], d_out)
    grads_three = grads_col(d_down.astype(bf16))
    dw_down = inner_rows(spread_a, grads_three)
    d_act = reduce_row(against(grads_three, down_b))
    act_out, pullback = jax.vjp(lambda a, b: jax.nn.gelu(a, approximate=True) * b, gate_raw, up_raw)
    d_gate, d_up = pullback(d_act)
    local_two = jnp.concatenate([d_gate, d_up], axis=1).astype(bf16)
    grads_two = grads_row(local_two)
    dw_gateup = jnp.stack(
        [inner_rows(spread_f, grads_two[:, :ff_here]), inner_rows(spread_f, grads_two[:, ff_here:])]
    )
    d_ffn = reduce_col(
        against(grads_two[:, :ff_here], gateup_b[0]) + against(grads_two[:, ff_here:], gateup_b[1])
    )
    d_mix_norm, gain_grads[3] = norm_backward(mixture, scale_f, w_gains[3], d_ffn)
    d_half = (d_out + d_mix_norm) * HALF_ROOT
    d_proj, gain_grads[2] = norm_backward(projected, scale_p, w_gains[2], d_half)
    d_right, gain_grads[1] = norm_backward(right_raw, scale_r, w_gains[1], d_half)
    grads_one = grads_col(jnp.concatenate([d_proj, d_right], axis=1).astype(bf16))
    dw_attend = inner_rows(spread_j[:, :q_cols], grads_one[:, :width_a])
    dw_right = inner_rows(spread_j[:, q_cols:], grads_one[:, width_a:])
    d_joined = reduce_row(
        jnp.concatenate(
            [against(grads_one[:, :width_a], attend_b), against(grads_one[:, width_a:], right_b)],
            axis=1,
        )
    )
    d_attended = d_joined[:, :q_cols].astype(bf16).reshape(token_batch, local_heads, HEAD_WIDTH)
    d_middle = d_joined[:, q_cols:]
    d_queries, d_key_sel, d_value_sel = attention_backward(
        queries,
        key_sel,
        value_sel,
        d_attended,
        block_peaks,
        block_totals,
        own_places,
        all_places,
        length,
        piece_starts,
    )
    single_hot_mask = (
        key_value_heads[:, None] == jnp.arange(KEY_VALUE_HEADS, dtype=jnp.int32)[None, :]
    ).astype(single_float)
    key_gradient = jnp.sum(d_key_sel[:, :, None, :] * single_hot_mask[None, :, :, None], axis=1)
    value_gradient = jnp.sum(d_value_sel[:, :, None, :] * single_hot_mask[None, :, :, None], axis=1)
    key_gradient, value_gradient = lax.psum((key_gradient, value_gradient), ("row", "col"))
    local_key_gradient = lax.dynamic_slice_in_dim(
        key_gradient, row_place * token_batch, token_batch, 0
    ).reshape(token_batch, KEY_VALUE_HEADS * HEAD_WIDTH)
    local_value_gradient = lax.dynamic_slice_in_dim(
        value_gradient, row_place * token_batch, token_batch, 0
    ).reshape(token_batch, KEY_VALUE_HEADS * HEAD_WIDTH)
    query_out, pullback = jax.vjp(
        lambda r, g: query_form(r, g, own_cos, own_sin), query_raw, query_gains
    )
    d_query_raw, dg_query = pullback(d_queries)
    key_tile = jnp.broadcast_to(key_gain, (token_batch, 1, HEAD_WIDTH))
    key_out, pullback = jax.vjp(lambda r, g: key_form(r, g, own_cos, own_sin), key_raw, key_tile)
    d_key_raw, dg_key_rows = pullback(
        jnp.concatenate([local_key_gradient, local_value_gradient], axis=1)
    )
    slice_rows = token_batch // col_devs
    dg_key = jnp.sum(
        lax.dynamic_slice_in_dim(dg_key_rows, column_place * slice_rows, slice_rows, 0), axis=(0, 1)
    )
    grads_zero = grads_row(jnp.concatenate([d_query_raw, d_middle, d_key_raw], axis=1).astype(bf16))
    dw_query = inner_rows(spread_h, grads_zero[:, :q_cols])
    dw_left = inner_rows(spread_h, grads_zero[:, q_cols : q_cols + l_cols])
    key_grad_rows = grads_zero[:, q_cols + l_cols :]
    dw_keyval = inner_rows(spread_h, key_grad_rows)
    slab_width = kv_cols // col_devs
    d_hidden = reduce_col(
        against(grads_zero[:, :q_cols], query_b)
        + against(grads_zero[:, q_cols : q_cols + l_cols], left_b)
        + against(
            lax.dynamic_slice_in_dim(key_grad_rows, column_place * slab_width, slab_width, 1),
            lax.dynamic_slice_in_dim(keyval_b, column_place * slab_width, slab_width, 1),
        )
    )
    d_in, gain_grads[0] = norm_backward(inputs, scale_in, w_gains[0], d_hidden + d_half)
    grad_input = (d_half + d_in).astype(bf16)
    g_query, g_keyval, g_attend, g_gateup, g_down, g_left, g_right, g_pergate, g_perproj = (
        lax.psum_scatter(dw_query, "dp", scatter_dimension=1, tiled=True),
        lax.psum_scatter(dw_keyval, "dp", scatter_dimension=1, tiled=True),
        lax.psum_scatter(dw_attend, "dp", scatter_dimension=1, tiled=True),
        lax.psum_scatter(dw_gateup, "dp", scatter_dimension=2, tiled=True),
        lax.psum_scatter(dw_down, "dp", scatter_dimension=1, tiled=True),
        lax.psum_scatter(dw_left, "dp", scatter_dimension=1, tiled=True),
        lax.psum_scatter(dw_right, "dp", scatter_dimension=1, tiled=True),
        lax.psum_scatter(dw_pergate, "dp", scatter_dimension=1, tiled=True),
        lax.psum_scatter(dw_perproj, "dp", scatter_dimension=1, tiled=True),
    )
    gain_full = lax.dynamic_update_slice_in_dim(
        jnp.zeros((6, MODEL_WIDTH), single_float), jnp.stack(gain_grads), row_place * width_a, 1
    )
    head_full = lax.dynamic_update_slice_in_dim(
        jnp.zeros((QUERY_HEADS + 1, HEAD_WIDTH), single_float),
        dg_query,
        column_place * local_heads,
        0,
    )
    head_full = head_full.at[QUERY_HEADS].add(dg_key)
    logit_here = lax.dynamic_update_slice_in_dim(
        jnp.full((QUERY_HEADS,), NEGATIVE, single_float),
        jnp.max(block_peaks, axis=(0, 2)),
        column_place * local_heads,
        0,
    )

    def combine(left_part, right_part):
        return (
            left_part[0] + right_part[0],
            left_part[1] + right_part[1],
            jnp.maximum(left_part[2], right_part[2]),
        )

    gain_sum, head_sum, logit_top = joined(
        (gain_full, head_full, logit_here), ("dp", "row", "col"), combine
    )
    g_gains = lax.dynamic_slice_in_dim(gain_sum, row_place * width_a, width_a, 1)
    lead_device = (column_place == 0) & (data_at == 0)
    solo_device = lead_device & (row_place == 0)
    squares = jnp.float32(0.0)
    for gradient in (g_query, g_attend, g_gateup, g_down, g_left, g_right, g_pergate, g_perproj):
        squares = squares + jnp.sum(gradient * gradient)
    squares = squares + jnp.where(column_place == 0, jnp.sum(g_keyval * g_keyval), 0.0)
    squares = squares + jnp.where(lead_device, jnp.sum(g_gains * g_gains), 0.0)
    squares = squares + jnp.where(solo_device, jnp.sum(head_sum * head_sum), 0.0)
    grad_norm = jnp.sqrt(lax.psum(squares, ("dp", "row", "col")))
    clip_scale = CLIP / jnp.maximum(grad_norm, CLIP)
    scale_factors = LOGIT_CAP / jnp.maximum(logit_top, LOGIT_CAP)
    weights = (
        w_query,
        key_value_weight,
        w_attend,
        w_gateup,
        w_down,
        w_left,
        w_right,
        w_pergate,
        w_perproj,
        w_gains,
        w_heads,
    )
    moments = (
        m_query,
        key_value_first_moment,
        m_attend,
        m_gateup,
        m_down,
        m_left,
        m_right,
        m_pergate,
        m_perproj,
        m_gains,
        m_heads,
    )
    seconds = (
        v_query,
        key_value_second_moment,
        v_attend,
        v_gateup,
        v_down,
        v_left,
        v_right,
        v_pergate,
        v_perproj,
        v_gains,
        v_heads,
    )
    gradients = (
        g_query,
        g_keyval,
        g_attend,
        g_gateup,
        g_down,
        g_left,
        g_right,
        g_pergate,
        g_perproj,
        g_gains,
        head_sum,
    )
    step_rates = (
        MODEL_WIDTH ** (-0.5),
        MODEL_WIDTH ** (-0.5),
        (QUERY_HEADS * HEAD_WIDTH) ** (-0.5),
        MODEL_WIDTH ** (-0.5),
        FF ** (-0.5),
        MODEL_WIDTH ** (-0.5),
        RANK ** (-0.5),
        MODEL_WIDTH ** (-0.5),
        PLD ** (-0.5),
        GAIN_RATE,
        HEAD_RATE,
    )
    decays = (DECAY, DECAY, DECAY, DECAY, DECAY, DECAY, DECAY, DECAY, DECAY, 0.0, 0.0)
    updated = [
        adamw_step(
            weights[k], moments[k], seconds[k], gradients[k] * clip_scale, step_rates[k], decays[k]
        )
        for k in range(11)
    ]
    head_scale = jnp.sqrt(scale_factors)
    q_width = w_query.shape[1]
    q_head = (
        (column_place * data_devs + data_at) * q_width + jnp.arange(q_width, dtype=jnp.int32)
    ) // HEAD_WIDTH
    q_factor = jnp.sum(
        jnp.where(
            q_head[:, None] == jnp.arange(QUERY_HEADS, dtype=jnp.int32)[None, :],
            head_scale[None, :],
            0.0,
        ),
        axis=1,
    )
    new_query = updated[0][2] * q_factor[None, :]
    kv_width = key_value_weight.shape[1]
    key_value_index = data_at * kv_width + jnp.arange(kv_width, dtype=jnp.int32)
    key_value_scale = jnp.sqrt(
        jnp.min(scale_factors.reshape(KEY_VALUE_HEADS, QUERY_HEADS // KEY_VALUE_HEADS), axis=1)
    )
    key_value_choice = jnp.sum(
        jnp.where(
            (key_value_index // HEAD_WIDTH)[:, None]
            == jnp.arange(KEY_VALUE_HEADS, dtype=jnp.int32)[None, :],
            key_value_scale[None, :],
            0.0,
        ),
        axis=1,
    )
    key_value_factor = jnp.where(
        key_value_index < KEY_VALUE_HEADS * HEAD_WIDTH, key_value_choice, 1.0
    )
    new_keyval = updated[1][2] * key_value_factor[None, :]
    return (
        result,
        grad_input,
        grad_norm,
        scale_factors,
        updated[0][0],
        updated[0][1],
        new_query,
        updated[1][0],
        updated[1][1],
        new_keyval,
        updated[2][0],
        updated[2][1],
        updated[2][2],
        updated[3][0],
        updated[3][1],
        updated[3][2],
        updated[4][0],
        updated[4][1],
        updated[4][2],
        updated[5][0],
        updated[5][1],
        updated[5][2],
        updated[6][0],
        updated[6][1],
        updated[6][2],
        updated[7][0],
        updated[7][1],
        updated[7][2],
        updated[8][0],
        updated[8][1],
        updated[8][2],
        updated[9][0],
        updated[9][1],
        updated[9][2],
        updated[10][0],
        updated[10][1],
        updated[10][2],
    )


def solution(mesh):
    placed = (
        P(("dp", "col"), "row"),
        P(("dp", "row"), "col"),
        P(("dp", "col"), "row"),
        P(),
        P(),
        P("row", ("col", "dp")),
        P("row", ("col", "dp")),
        P("row", ("col", "dp")),
        P("row", "dp"),
        P("row", "dp"),
        P("row", "dp"),
        P("col", ("row", "dp")),
        P("col", ("row", "dp")),
        P("col", ("row", "dp")),
        P(None, "row", ("col", "dp")),
        P(None, "row", ("col", "dp")),
        P(None, "row", ("col", "dp")),
        P("col", ("row", "dp")),
        P("col", ("row", "dp")),
        P("col", ("row", "dp")),
        P("row", ("col", "dp")),
        P("row", ("col", "dp")),
        P("row", ("col", "dp")),
        P("col", ("row", "dp")),
        P("col", ("row", "dp")),
        P("col", ("row", "dp")),
        P("row", ("col", "dp")),
        P("row", ("col", "dp")),
        P("row", ("col", "dp")),
        P("col", ("row", "dp")),
        P("col", ("row", "dp")),
        P("col", ("row", "dp")),
        P(None, "row"),
        P(None, "row"),
        P(None, "row"),
        P(),
        P(),
        P(),
    )
    fits = (
        mesh.shape["col"] == KEY_VALUE_HEADS
        and mesh.shape["row"] * KEY_VALUE_HEADS == QUERY_HEADS
        and mesh.shape["dp"] == mesh.shape["row"]
    )
    return jax.shard_map(
        line_device if fits else per_device,
        mesh=mesh,
        in_specs=placed,
        out_specs=(
            P(("dp", "col"), "row"),
            P(("dp", "col"), "row"),
            P(),
            P(),
            P("row", ("col", "dp")),
            P("row", ("col", "dp")),
            P("row", ("col", "dp")),
            P("row", "dp"),
            P("row", "dp"),
            P("row", "dp"),
            P("col", ("row", "dp")),
            P("col", ("row", "dp")),
            P("col", ("row", "dp")),
            P(None, "row", ("col", "dp")),
            P(None, "row", ("col", "dp")),
            P(None, "row", ("col", "dp")),
            P("col", ("row", "dp")),
            P("col", ("row", "dp")),
            P("col", ("row", "dp")),
            P("row", ("col", "dp")),
            P("row", ("col", "dp")),
            P("row", ("col", "dp")),
            P("col", ("row", "dp")),
            P("col", ("row", "dp")),
            P("col", ("row", "dp")),
            P("row", ("col", "dp")),
            P("row", ("col", "dp")),
            P("row", ("col", "dp")),
            P("col", ("row", "dp")),
            P("col", ("row", "dp")),
            P("col", ("row", "dp")),
            P(None, "row"),
            P(None, "row"),
            P(None, "row"),
            P(),
            P(),
            P(),
        ),
        check_vma=False,
    )
```

```python
import jax
import jax.numpy as jnp
from jax import lax
from jax.experimental import pallas as pl
from jax.experimental.pallas import tpu as pltpu
from jax.sharding import PartitionSpec as P

MODEL_WIDTH = 2048
QUERY_HEADS = 8
KEY_VALUE_HEADS = 2
HEAD_WIDTH = 256
FF = 8192
RANK = 64
PLD = 256
IMG = 256
STEP = 10


EPS = 1e-06
ROPE_BASE = 1000000.0
BETA_ONE = 0.5
BETA_TWO = 0.5
ADAM_EPS = 1e-08
DECAY = 0.01
CLIP = 1.0
LOGIT_CAP = 4.0
GAIN_RATE = 0.6
HEAD_RATE = 0.1
HALF_ROOT = 0.7071067811865476
NEGATIVE = -1e30


def joined(part, axis, combine):
    gathered = jax.tree.map(lambda a: lax.all_gather(a, axis), part)

    def take(source):
        return jax.tree.map(lambda a: lax.dynamic_index_in_dim(a, source, 0, False), gathered)

    return lax.fori_loop(
        1, lax.axis_size(axis), lambda source, state: combine(state, take(source)), take(0)
    )


def row_total(values_in):
    return lax.psum(values_in, "row")


def spread_col(values_in):
    return lax.all_gather(values_in, "col", axis=0, tiled=True)


def reduce_row(values_in):
    return lax.psum_scatter(values_in, "row", scatter_dimension=0, tiled=True)


def spread_row(values_in):
    return lax.all_gather(values_in, "row", axis=0, tiled=True)


def reduce_col(values_in):
    return lax.psum_scatter(values_in, "col", scatter_dimension=0, tiled=True)


def grads_col(values_in):
    return lax.all_gather(values_in, "col", axis=0, tiled=True)


def grads_row(values_in):
    return lax.all_gather(values_in, "row", axis=0, tiled=True)


def inner_rows(left_mat, right_mat):
    return lax.dot_general(
        left_mat, right_mat, (((0,), (0,)), ((), ())), preferred_element_type=jnp.float32
    )


def against(grad_mat, weight_mat):
    return lax.dot_general(
        grad_mat, weight_mat, (((1,), (1,)), ((), ())), preferred_element_type=jnp.float32
    )


def flat_dot(left_mat, right_mat):
    return jnp.dot(left_mat, right_mat, preferred_element_type=jnp.float32)


def norm_forward(values_in, gain_vec):
    total_sq = row_total(jnp.sum(values_in * values_in, axis=-1, keepdims=True))
    norm_scale = lax.rsqrt(total_sq / MODEL_WIDTH + EPS)
    return (values_in * norm_scale * gain_vec, norm_scale)


def norm_backward(values_in, norm_scale, gain_vec, grad_out):
    weighted = grad_out * gain_vec
    inner_sum = row_total(jnp.sum(weighted * values_in, axis=-1, keepdims=True))
    grad_in = norm_scale * weighted - values_in * (norm_scale * norm_scale * norm_scale) * (
        inner_sum / MODEL_WIDTH
    )
    return (grad_in, jnp.sum(grad_out * values_in * norm_scale, axis=0))


def norm_rows(values_in, gain_vec):
    return (
        values_in
        * lax.rsqrt(jnp.mean(values_in * values_in, axis=-1, keepdims=True) + EPS)
        * gain_vec
    )


def rope_tables(places, feat_width):
    half_width = feat_width // 2
    powers = jnp.arange(half_width, dtype=jnp.int32).astype(jnp.float32) * (2.0 / feat_width)
    frequency = jnp.power(jnp.float32(ROPE_BASE), -powers)
    angles = places.astype(jnp.float32)[:, None] * frequency[None, :]
    return (jnp.cos(angles), jnp.sin(angles))


def rotate(values_in, cos_tab, sin_tab):
    half_width = values_in.shape[-1] // 2
    part_one = values_in[..., :half_width]
    part_two = values_in[..., half_width:]
    cos_row = cos_tab[:, None, :]
    sin_row = sin_tab[:, None, :]
    return jnp.concatenate(
        [part_one * cos_row - part_two * sin_row, part_two * cos_row + part_one * sin_row], axis=-1
    )


def query_form(unscaled_rows, gain_rows, cos_tab, sin_tab):
    shaped = unscaled_rows.reshape(unscaled_rows.shape[0], gain_rows.shape[0], HEAD_WIDTH)
    return rotate(norm_rows(shaped, gain_rows[None]), cos_tab, sin_tab)


def key_form(unscaled_rows, gain_vec, cos_tab, sin_tab):
    count_of_rows = unscaled_rows.shape[0]
    key_rows = unscaled_rows[:, : KEY_VALUE_HEADS * HEAD_WIDTH].reshape(
        count_of_rows, KEY_VALUE_HEADS, HEAD_WIDTH
    )
    value_rows = unscaled_rows[:, KEY_VALUE_HEADS * HEAD_WIDTH :].reshape(
        count_of_rows, KEY_VALUE_HEADS, HEAD_WIDTH
    )
    key_rows = rotate(norm_rows(key_rows, gain_vec), cos_tab, sin_tab)
    value_rows = norm_rows(value_rows, 1.0)
    return jnp.concatenate(
        [
            key_rows.reshape(count_of_rows, KEY_VALUE_HEADS * HEAD_WIDTH),
            value_rows.reshape(count_of_rows, KEY_VALUE_HEADS * HEAD_WIDTH),
        ],
        axis=1,
    )


def piece_of(places, starts):
    inside = (places[:, None] >= starts[None, :]) & (places[:, None] < starts[None, :] + IMG)
    labels = jnp.arange(1, starts.shape[0] + 1, dtype=jnp.int32)
    return jnp.sum(jnp.where(inside, labels[None, :], 0), axis=1) - 1


def visible(query_places, key_places, query_pieces, key_pieces, length):
    causal = key_places[None, :] <= query_places[:, None]
    same_piece = (query_pieces[:, None] == key_pieces[None, :]) & (query_pieces[:, None] >= 0)
    return (key_places[None, :] < length) & (causal | same_piece)


def block_mask(own_places, key_places, key_pieces, length, starts):
    return visible(own_places, key_places, piece_of(own_places, starts), key_pieces, length)


def attention_forward(queries, key_sel, value_sel, own_places, key_places, length, starts):
    count_of_rows, head_count = (queries.shape[0], queries.shape[1])
    block_size = min(512, count_of_rows)
    key_pieces = piece_of(key_places, starts)
    stacked = queries.reshape(count_of_rows // block_size, block_size, head_count, HEAD_WIDTH)

    def one_block(element):
        block_rows, block_at = element
        allowed = block_mask(own_places, key_places, key_pieces, length, starts)
        scores = jnp.einsum("qhd,khd->hqk", block_rows, key_sel, preferred_element_type=jnp.float32)
        masked = jnp.where(allowed[None], scores, NEGATIVE)
        peak_row = jnp.max(masked, axis=-1, keepdims=True)
        raw_weights = jnp.where(allowed[None], jnp.exp(masked - peak_row), 0.0)
        total_row = jnp.sum(raw_weights, axis=-1, keepdims=True)
        attn_probs = (raw_weights / total_row).astype(jnp.bfloat16)
        outputs = jnp.einsum(
            "hqk,khd->qhd", attn_probs, value_sel, preferred_element_type=jnp.float32
        )
        return (outputs, peak_row[..., 0], total_row[..., 0])

    return lax.map(one_block, (stacked, jnp.arange(count_of_rows // block_size, dtype=jnp.int32)))


def attention_backward(
    queries,
    key_sel,
    value_sel,
    grad_attended,
    block_peaks,
    block_totals,
    own_places,
    key_places,
    length,
    starts,
):
    count_of_rows, head_count = (queries.shape[0], queries.shape[1])
    block_size = min(512, count_of_rows)
    block_count = count_of_rows // block_size
    key_pieces = piece_of(key_places, starts)
    stacked = queries.reshape(block_count, block_size, head_count, HEAD_WIDTH)
    grad_stacked = grad_attended.reshape(block_count, block_size, head_count, HEAD_WIDTH)

    def one_block(carry, element):
        dk_sum, dv_sum = carry
        block_rows, grad_rows, peak_row, total_row, block_at = element
        allowed = block_mask(own_places, key_places, key_pieces, length, starts)
        scores = jnp.einsum("qhd,khd->hqk", block_rows, key_sel, preferred_element_type=jnp.float32)
        masked = jnp.where(allowed[None], scores, NEGATIVE)
        raw_weights = jnp.where(allowed[None], jnp.exp(masked - peak_row[..., None]), 0.0)
        attn_probs = raw_weights / total_row[..., None]
        probs_low = attn_probs.astype(jnp.bfloat16)
        grad_probs = jnp.einsum(
            "qhd,khd->hqk", grad_rows, value_sel, preferred_element_type=jnp.float32
        )
        delta_row = jnp.sum(attn_probs * grad_probs, axis=-1, keepdims=True)
        grad_scores = (attn_probs * (grad_probs - delta_row)).astype(jnp.bfloat16)
        grad_query = jnp.einsum(
            "hqk,khd->qhd", grad_scores, key_sel, preferred_element_type=jnp.float32
        )
        dk_sum = dk_sum + jnp.einsum(
            "hqk,qhd->khd", grad_scores, block_rows, preferred_element_type=jnp.float32
        )
        dv_sum = dv_sum + jnp.einsum(
            "hqk,qhd->khd", probs_low, grad_rows, preferred_element_type=jnp.float32
        )
        return ((dk_sum, dv_sum), grad_query)

    zero_keys = jnp.zeros(key_sel.shape, jnp.float32)
    (dk_sum, dv_sum), grad_query = lax.scan(
        one_block,
        (zero_keys, zero_keys),
        (
            stacked,
            grad_stacked,
            block_peaks,
            block_totals,
            jnp.arange(block_count, dtype=jnp.int32),
        ),
    )
    return (grad_query.reshape(count_of_rows, head_count, HEAD_WIDTH), dk_sum, dv_sum)


def adamw_step(weight, moment_one, moment_two, gradient, rate, decay):
    moment_one = BETA_ONE * moment_one + (1.0 - BETA_ONE) * gradient
    moment_two = BETA_TWO * moment_two + (1.0 - BETA_TWO) * gradient * gradient
    mean_step = moment_one / (1.0 - BETA_ONE**STEP)
    spread = moment_two / (1.0 - BETA_TWO**STEP)
    return (
        moment_one,
        moment_two,
        weight - rate * (mean_step / (jnp.sqrt(spread) + ADAM_EPS) + decay * weight),
    )


MESH = pl.DeviceIdType.MESH
LOW = jnp.bfloat16
FULL = jnp.float32


def cost(micros, flops=0):
    return pl.CostEstimate(
        flops=flops, bytes_accessed=int(micros * 3.0e6), transcendentals=0
    )


def params(ident, mebibytes=48):
    return pltpu.CompilerParams(
        collective_id=ident, has_side_effects=True, vmem_limit_bytes=mebibytes * 2**20
    )


def push(source, target, send, recv, device):
    return pltpu.make_async_remote_copy(
        source, target, send, recv, device_id=device, device_id_type=MESH
    )


def greet_line(me, count, column, core):
    barrier = pltpu.get_barrier_semaphore()

    @pl.when(me > 0)
    def _():
        pl.semaphore_signal(barrier, inc=1, device_id={"row": me - 1}, device_id_type=MESH)

    @pl.when(me < count - 1)
    def _():
        pl.semaphore_signal(barrier, inc=1, device_id={"row": me + 1}, device_id_type=MESH)

    if core:
        pl.semaphore_signal(barrier, inc=1, device_id={"col": 1 - column}, device_id_type=MESH)

    ends = (me == 0) | (me == count - 1)

    @pl.when(ends)
    def _():
        pl.semaphore_wait(barrier, 1 + int(core))

    @pl.when(jnp.logical_not(ends))
    def _():
        pl.semaphore_wait(barrier, 2 + int(core))


def line_reduce(parts, ident, core, micros):
    count = lax.axis_size("row")
    high, wide = parts.shape[-2:]
    chunk = min(high, max(16, 65536 // wide))
    while high % chunk:
        chunk //= 2

    def kernel(x_ref, o_ref, c_buf, l_buf, r_buf, s_buf, send_l, send_r, send_c, recv_l, recv_r, recv_c):
        me = lax.axis_index("row")
        column = lax.axis_index("col")

        def mine(q):
            return x_ref.at[column, q] if core else x_ref.at[q]

        def core_copy(q):
            return push(x_ref.at[1 - column, q], c_buf.at[q], send_c.at[q], recv_c.at[q], {"col": 1 - column})

        def left_copy(q):
            return push(s_buf.at[q], l_buf.at[q], send_l.at[q], recv_l.at[q], {"row": me - 1})

        def right_copy(q):
            return push(s_buf.at[q], r_buf.at[q], send_r.at[q], recv_r.at[q], {"row": me + 1})

        def left_arrival(q):
            return push(s_buf.at[q], l_buf.at[q], send_l.at[q], recv_l.at[q], {"row": me + 1})

        def right_arrival(q):
            return push(s_buf.at[q], r_buf.at[q], send_r.at[q], recv_r.at[q], {"row": me - 1})

        def added(target, terms):
            @pl.loop(0, high // chunk)
            def _(at):
                rows = pl.ds(pl.multiple_of(at * chunk, chunk), chunk)
                total = terms[0][rows].astype(FULL)
                for term in terms[1:]:
                    total = total + term[rows].astype(FULL)
                target[rows] = total.astype(target.dtype)

        def base(q):
            return [mine(q)] + ([c_buf.at[q]] if core else [])

        greet_line(me, count, column, core)
        if core:
            for q in range(count):
                core_copy(q).start()

        def leftward(q):
            @pl.when(me > q)
            def _():
                if core:
                    core_copy(q).wait_recv()

                @pl.when(me < count - 1)
                def _():
                    left_arrival(q).wait_recv()
                    added(s_buf.at[q], base(q) + [l_buf.at[q]])

                @pl.when(me == count - 1)
                def _():
                    added(s_buf.at[q], base(q))

                left_copy(q).start()

        def rightward(q):
            @pl.when(me < q)
            def _():
                if core:
                    core_copy(q).wait_recv()

                @pl.when(me > 0)
                def _():
                    right_arrival(q).wait_recv()
                    added(s_buf.at[q], base(q) + [r_buf.at[q]])

                @pl.when(me == 0)
                def _():
                    added(s_buf.at[q], base(q))

                right_copy(q).start()

        for j in range(count - 1):

            @pl.when(me < count // 2)
            def _():
                rightward(count - 1 - j)

            leftward(j)

            @pl.when(me >= count // 2)
            def _():
                rightward(count - 1 - j)

        if core:
            core_copy(me).wait_recv()

        @pl.when(me < count - 1)
        def _():
            left_arrival(me).wait_recv()

        @pl.when(me > 0)
        def _():
            right_arrival(me).wait_recv()

        @pl.when(me == 0)
        def _():
            added(o_ref, base(me) + [l_buf.at[me]])

        @pl.when(me == count - 1)
        def _():
            added(o_ref, base(me) + [r_buf.at[me]])

        @pl.when((me > 0) & (me < count - 1))
        def _():
            added(o_ref, base(me) + [l_buf.at[me], r_buf.at[me]])

        for q in range(count):
            if core:
                core_copy(q).wait_send()

            @pl.when(me > q)
            def _():
                left_copy(q).wait_send()

            @pl.when(me < q)
            def _():
                right_copy(q).wait_send()

    dma = pltpu.SemaphoreType.DMA
    slots = (count, high, wide)
    vmem = pl.BlockSpec(memory_space=pltpu.VMEM)
    return pl.pallas_call(
        kernel,
        out_shape=jax.ShapeDtypeStruct((high, wide), FULL),
        in_specs=[vmem],
        out_specs=vmem,
        scratch_shapes=[
            pltpu.VMEM(slots if core else (1, 16, 128), parts.dtype),
            pltpu.VMEM(slots, parts.dtype),
            pltpu.VMEM(slots, parts.dtype),
            pltpu.VMEM(slots, parts.dtype),
        ]
        + [dma((count,))] * 6,
        compiler_params=params(ident),
        cost_estimate=cost(micros),
    )(parts)


class Line:
    def __init__(self, source, shape, place, core=False):
        self.source, self.shape, self.place, self.core = source, shape, place, core

    def semaphores(self, count, data):
        dma = pltpu.SemaphoreType.DMA
        return [dma((count,)), dma((count,)), dma((2 * count,))] * 2 + [dma]

    def bind(self, x_ref, o_ref, sems, spots, sizes):
        self.x_ref, self.o_ref, self.sems = x_ref, o_ref, sems
        self.me, self.column, self.at = spots
        self.count = sizes[0]

    def slot(self, source):
        return self.place(self.o_ref, self.column, source)

    def other(self, source):
        return self.place(self.o_ref, 1 - self.column, source)

    def to_left(self, source, k, origin):
        return push(origin, self.slot(source), self.sems[0].at[k], self.sems[4].at[k], {"row": self.me - 1})

    def to_right(self, source, k, origin):
        return push(origin, self.slot(source), self.sems[1].at[k], self.sems[3].at[k], {"row": self.me + 1})

    def to_core(self, source, k, origin):
        return push(origin, self.slot(source), self.sems[2].at[k], self.sems[5].at[k], {"col": 1 - self.column})

    def from_core(self, source, k):
        there = self.other(source)
        return push(there, there, self.sems[2].at[k], self.sems[5].at[k], {"col": 1 - self.column})

    def from_left(self, source, k):
        there = self.slot(source)
        return push(there, there, self.sems[1].at[k], self.sems[3].at[k - 1], {"row": self.me - 1})

    def from_right(self, source, k):
        there = self.slot(source)
        return push(there, there, self.sems[0].at[k], self.sems[4].at[k - 1], {"row": self.me + 1})

    def own(self):
        return pltpu.make_async_copy(self.x_ref, self.slot(self.me), self.sems[6])

    def start(self):
        me, count = self.me, self.count

        @pl.when(me > 0)
        def _():
            self.to_left(me, 0, self.x_ref).start()

        @pl.when(me < count - 1)
        def _():
            self.to_right(me, 0, self.x_ref).start()

        if self.core:
            self.to_core(me, 0, self.x_ref).start()
        self.own().start()

    def step(self, k):
        me, count = self.me, self.count

        @pl.when(me - k >= 0)
        def _():
            self.from_left(me - k, k).wait_recv()
            block = self.slot(me - k)

            @pl.when(me < count - 1)
            def _():
                self.to_right(me - k, k, block).start()

            if self.core:
                self.to_core(me - k, k, block).start()

        @pl.when(me + k < count)
        def _():
            self.from_right(me + k, k).wait_recv()
            block = self.slot(me + k)

            @pl.when(me > 0)
            def _():
                self.to_left(me + k, k, block).start()

            if self.core:
                self.to_core(me + k, count - 1 + k, block).start()

    def finish(self):
        me, count = self.me, self.count
        self.own().wait()

        @pl.when(me > 0)
        def _():
            self.to_left(me, 0, self.x_ref).wait_send()

        @pl.when(me < count - 1)
        def _():
            self.to_right(me, 0, self.x_ref).wait_send()

        if self.core:
            self.to_core(me, 0, self.x_ref).wait_send()
            self.from_core(me, 0).wait_recv()

        @pl.loop(1, count)
        def _(k):
            @pl.when(me - k >= 0)
            def _():
                @pl.when(me < count - 1)
                def _():
                    self.to_right(me - k, k, self.x_ref).wait_send()

                if self.core:
                    self.to_core(me - k, k, self.x_ref).wait_send()
                    self.from_core(me - k, k).wait_recv()

            @pl.when(me + k < count)
            def _():
                @pl.when(me > 0)
                def _():
                    self.to_left(me + k, k, self.x_ref).wait_send()

                if self.core:
                    self.to_core(me + k, count - 1 + k, self.x_ref).wait_send()
                    self.from_core(me + k, count - 1 + k).wait_recv()


class Swap:
    def __init__(self, source, shape, take, place, axis="row"):
        self.source, self.shape, self.take, self.place = source, shape, take, place
        self.axis = axis

    def semaphores(self, count, data):
        size = count if self.axis == "row" else data
        return [pltpu.SemaphoreType.DMA((size,)), pltpu.SemaphoreType.DMA((size,))]

    def bind(self, x_ref, o_ref, sems, spots, sizes):
        self.x_ref, self.o_ref, self.sems = x_ref, o_ref, sems
        self.me = spots[0] if self.axis == "row" else spots[2]
        self.count = sizes[0] if self.axis == "row" else sizes[1]

    def copy(self, k):
        target = lax.rem(self.me + k, self.count)
        return push(
            self.take(self.x_ref, target),
            self.place(self.o_ref, self.me),
            self.sems[0].at[k],
            self.sems[1].at[k],
            {self.axis: target},
        )

    def own(self):
        return pltpu.make_async_copy(
            self.take(self.x_ref, self.me), self.place(self.o_ref, self.me), self.sems[0].at[0]
        )

    def start(self):
        for k in range(1, self.count):
            self.copy(k).start()
        self.own().start()

    def step(self, k):
        pass

    def finish(self):
        self.own().wait()
        for k in range(1, self.count):
            self.copy(k).wait_send()
            origin = lax.rem(self.me + self.count - k, self.count)
            there = self.place(self.o_ref, origin)
            push(there, there, self.sems[0].at[k], self.sems[1].at[k], {self.axis: origin}).wait_recv()


class Pair:
    core = True

    def __init__(self, source):
        self.source, self.shape = source, source.shape

    def semaphores(self, count, data):
        dma = pltpu.SemaphoreType.DMA
        return [dma, dma, dma]

    def bind(self, x_ref, o_ref, sems, spots, sizes):
        self.x_ref, self.o_ref, self.sems = x_ref, o_ref, sems
        self.column = spots[1]

    def copy(self):
        other = 1 - self.column
        return push(self.x_ref.at[other], self.o_ref.at[1], self.sems[0], self.sems[1], {"col": other})

    def own(self):
        return pltpu.make_async_copy(self.x_ref.at[self.column], self.o_ref.at[0], self.sems[2])

    def start(self):
        self.copy().start()
        self.own().start()

    def step(self, k):
        pass

    def finish(self):
        self.own().wait()
        self.copy().wait()


class Bundle:
    def __init__(self, items):
        self.items = items
        self.number = len(items)
        self.sizes = lax.axis_size("row"), lax.axis_size("dp")
        self.kinds = [item.semaphores(*self.sizes) for item in items]
        self.across = any(getattr(item, "axis", None) == "dp" for item in items)
        self.cores = any(getattr(item, "core", False) for item in items)
        self.sources = [item.source for item in items]
        self.shapes = [jax.ShapeDtypeStruct(item.shape, item.source.dtype) for item in items]
        self.specs = [pl.BlockSpec(memory_space=pl.ANY)] * self.number
        self.scratch = sum(self.kinds, [])

    def bind(self, x_refs, o_refs, sems):
        self.spots = lax.axis_index("row"), lax.axis_index("col"), lax.axis_index("dp")
        for item, x_ref, o_ref, kind in zip(self.items, x_refs, o_refs, self.kinds):
            item.bind(x_ref, o_ref, sems[: len(kind)], self.spots, self.sizes)
            sems = sems[len(kind) :]

    def greet(self, across=False, cores=False):
        me, column, at = self.spots
        count, data = self.sizes
        across, cores = across or self.across, cores or self.cores
        barrier = pltpu.get_barrier_semaphore()
        for k in range(1, count):
            pl.semaphore_signal(
                barrier, inc=1, device_id={"row": lax.rem(me + k, count)}, device_id_type=MESH
            )
        if across:
            for k in range(1, data):
                pl.semaphore_signal(
                    barrier, inc=1, device_id={"dp": lax.rem(at + k, data)}, device_id_type=MESH
                )
        if cores:
            pl.semaphore_signal(barrier, inc=1, device_id={"col": 1 - column}, device_id_type=MESH)
        pl.semaphore_wait(barrier, count - 1 + (data - 1) * int(across) + int(cores))

    def start(self):
        for item in self.items:
            item.start()

    def step(self, k):
        for item in self.items:
            item.step(k)

    def finish(self):
        for item in self.items:
            item.finish()


def transfers(items, ident, micros):
    bundle = Bundle(items)
    number = bundle.number

    def kernel(*refs):
        bundle.bind(refs[:number], refs[number : 2 * number], refs[2 * number :])
        bundle.greet()
        bundle.start()
        for k in range(1, bundle.sizes[0]):
            bundle.step(k)
        bundle.finish()

    return pl.pallas_call(
        kernel,
        out_shape=bundle.shapes,
        in_specs=bundle.specs,
        out_specs=bundle.specs,
        scratch_shapes=bundle.scratch,
        compiler_params=params(ident, 16),
        cost_estimate=cost(micros),
    )(*bundle.sources)


def shard_total(query_parts, kv_parts, flat_parts, items, ident):
    data = lax.axis_size("dp")
    bundle = Bundle(items)
    number = bundle.number

    def kernel(q_ref, kv_ref, f_ref, *refs):
        x_refs, refs = refs[:number], refs[number:]
        oq_ref, okv_ref, of_ref = refs[:3]
        o_refs, refs = refs[3 : 3 + number], refs[3 + number :]
        q_buf, kv_buf, f_buf = refs[:3]
        sems = refs[3:11]
        bundle.bind(x_refs, o_refs, refs[11:])
        column, at = lax.axis_index("col"), lax.axis_index("dp")
        bundle.greet(True, True)
        bundle.start()
        mine = lax.rem(at, 2) == column

        def copies(k):
            target = lax.rem(at + k, data)
            device = {"dp": target}
            return (
                push(q_ref.at[target], q_buf.at[k], sems[0].at[k], sems[1].at[k], device),
                push(kv_ref.at[target // 2], kv_buf.at[k], sems[2].at[k], sems[3].at[k], device),
                push(f_ref.at[target], f_buf.at[k], sems[4].at[k], sems[5].at[k], device),
                lax.rem(target, 2) == column,
            )

        for k in range(1, data):
            query_copy, kv_copy, flat_copy, there = copies(k)
            query_copy.start()
            flat_copy.start()

            @pl.when(there)
            def _():
                kv_copy.start()

        for k in range(1, data):
            query_copy, kv_copy, flat_copy, there = copies(k)
            query_copy.wait()
            flat_copy.wait()

            @pl.when(there)
            def _():
                kv_copy.wait_send()

            @pl.when(mine)
            def _():
                kv_copy.wait_recv()

        def added(target, own, buf, chunk):
            @pl.loop(0, target.shape[0] // chunk)
            def _(step):
                rows = pl.ds(pl.multiple_of(step * chunk, chunk), chunk)
                total = own[rows].astype(FULL)
                for k in range(1, data):
                    total = total + buf[k, rows].astype(FULL)
                target[rows] = total

        share = push(okv_ref, okv_ref, sems[6], sems[7], {"col": 1 - column})

        @pl.when(mine)
        def _():
            added(okv_ref, kv_ref.at[at // 2], kv_buf, 128)
            share.start()

        added(oq_ref, q_ref.at[at], q_buf, 128)
        added(of_ref, f_ref.at[at], f_buf, 64)

        @pl.when(mine)
        def _():
            share.wait_send()

        @pl.when(jnp.logical_not(mine))
        def _():
            share.wait_recv()

        for k in range(1, bundle.sizes[0]):
            bundle.step(k)
        bundle.finish()

    vmem = pl.BlockSpec(memory_space=pltpu.VMEM)
    dma = pltpu.SemaphoreType.DMA
    shapes = [query_parts.shape[1:], kv_parts.shape[1:], flat_parts.shape[1:]]
    return pl.pallas_call(
        kernel,
        out_shape=[jax.ShapeDtypeStruct(shape, FULL) for shape in shapes] + bundle.shapes,
        in_specs=[vmem] * 3 + bundle.specs,
        out_specs=[vmem] * 3 + bundle.specs,
        scratch_shapes=[pltpu.VMEM((data,) + shape, LOW) for shape in shapes]
        + [dma((data,))] * 6
        + [dma, dma]
        + bundle.scratch,
        compiler_params=params(ident),
        cost_estimate=cost(40),
    )(query_parts, kv_parts, flat_parts, *bundle.sources)


class Flow:
    def __init__(self, x_ref, blocks, own, core_out, core_in, left_in, right_in, sems):
        self.x_ref, self.blocks, self.own = x_ref, blocks, own
        self.core_out, self.core_in = core_out, core_in
        self.left_in, self.right_in = left_in, right_in
        self.sems = sems
        self.me, self.column = lax.axis_index("row"), lax.axis_index("col")
        self.count = blocks.shape[0]

    @staticmethod
    def scratch(count, share, width):
        dma = pltpu.SemaphoreType.DMA
        slots = (count, share, width)
        return [
            pltpu.VMEM((count, 2, share, width), LOW),
            pltpu.VMEM(slots, FULL),
            pltpu.VMEM(slots, LOW),
            pltpu.VMEM(slots, LOW),
            pltpu.VMEM(slots, LOW),
            pltpu.VMEM(slots, LOW),
        ], [dma((count,))] * 12 + [dma]

    def left(self):
        return {"row": self.me - 1}

    def right(self):
        return {"row": self.me + 1}

    def beside(self):
        return {"col": 1 - self.column}

    def to_left(self, source, k, origin):
        return push(origin, self.blocks.at[source, 0], self.sems[0].at[k], self.sems[4].at[k], self.left())

    def to_right(self, source, k, origin):
        return push(origin, self.blocks.at[source, 0], self.sems[1].at[k], self.sems[3].at[k], self.right())

    def to_core(self, source, origin):
        return push(origin, self.blocks.at[source, 1], self.sems[2].at[source], self.sems[5].at[source], self.beside())

    def back_core(self, q):
        return push(self.core_out.at[q], self.core_in.at[q], self.sems[6].at[q], self.sems[9].at[q], self.beside())

    def back_left(self, q):
        return push(self.core_out.at[q], self.left_in.at[q], self.sems[7].at[q], self.sems[10].at[q], self.left())

    def back_right(self, q):
        return push(self.core_out.at[q], self.right_in.at[q], self.sems[8].at[q], self.sems[11].at[q], self.right())

    def mine(self):
        return pltpu.make_async_copy(self.x_ref, self.blocks.at[self.me, 0], self.sems[12])

    def start(self):
        me, count = self.me, self.count

        @pl.when(me > 0)
        def _():
            self.to_left(me, 0, self.x_ref).start()

        @pl.when(me < count - 1)
        def _():
            self.to_right(me, 0, self.x_ref).start()

        self.to_core(me, self.x_ref).start()
        self.mine().start()

    def arrive(self, k):
        me, count = self.me, self.count

        @pl.when(k == 0)
        def _():
            self.mine().wait()
            self.to_core(me, self.x_ref).wait()

        @pl.when((k > 0) & (me - k >= 0))
        def _():
            source = me - k
            block = self.blocks.at[source, 0]
            push(block, block, self.sems[1].at[k], self.sems[3].at[k - 1], self.left()).wait_recv()

            @pl.when(me < count - 1)
            def _():
                self.to_right(source, k, block).start()

            self.to_core(source, block).start()

        @pl.when((k > 0) & (me + k < count))
        def _():
            source = me + k
            block = self.blocks.at[source, 0]
            push(block, block, self.sems[0].at[k], self.sems[4].at[k - 1], self.right()).wait_recv()

            @pl.when(me > 0)
            def _():
                self.to_left(source, k, block).start()

            self.to_core(source, block).start()

        @pl.when((k > 0) & (me - k >= 0))
        def _():
            self.to_core(me - k, self.x_ref).wait()

        @pl.when((k > 0) & (me + k < count))
        def _():
            self.to_core(me + k, self.x_ref).wait()

    def visit(self, body, bundle):
        me, count = self.me, self.count

        @pl.loop(0, count)
        def _(k):
            self.arrive(k)

            @pl.when(k > 0)
            def _():
                bundle.step(k)

            @pl.loop(0, 2)
            def _(side):
                source = jnp.where(side == 0, me - k, me + k)

                @pl.when((source >= 0) & (source < count) & ((side == 0) | (k > 0)))
                def _():
                    body(source)
                    self.back_core(source).start()

    def added(self, target, terms):
        high, wide = target.shape
        step = min(high, max(16, 65536 // wide))

        @pl.loop(0, high // step)
        def _(at):
            rows = pl.ds(pl.multiple_of(at * step, step), step)
            total = terms[0][rows]
            for term in terms[1:]:
                total = total + term[rows].astype(FULL)
            target[rows] = total.astype(target.dtype)

    def give_back(self, t):
        me, count = self.me, self.count
        q_left = t - (count - 1 - me)
        q_right = count - 1 - (t - me)

        def leftward():
            q = q_left
            self.back_core(q).wait()

            @pl.when(me < count - 1)
            def _():
                push(self.left_in.at[q], self.left_in.at[q], self.sems[7].at[q], self.sems[10].at[q], self.right()).wait_recv()
                self.added(self.core_out.at[q], [self.own.at[q], self.core_in.at[q], self.left_in.at[q]])

            @pl.when(me == count - 1)
            def _():
                self.added(self.core_out.at[q], [self.own.at[q], self.core_in.at[q]])

            self.back_left(q).start()

        def rightward():
            q = q_right
            self.back_core(q).wait()

            @pl.when(me > 0)
            def _():
                push(self.right_in.at[q], self.right_in.at[q], self.sems[8].at[q], self.sems[11].at[q], self.left()).wait_recv()
                self.added(self.core_out.at[q], [self.own.at[q], self.core_in.at[q], self.right_in.at[q]])

            @pl.when(me == 0)
            def _():
                self.added(self.core_out.at[q], [self.own.at[q], self.core_in.at[q]])

            self.back_right(q).start()

        pl.when((q_left >= 0) & (q_left < me))(leftward)
        pl.when((t >= me) & (q_right > me))(rightward)

    def finish(self, o_ref):
        me, count = self.me, self.count
        self.back_core(me).wait()

        @pl.when(me < count - 1)
        def _():
            push(self.left_in.at[me], self.left_in.at[me], self.sems[7].at[me], self.sems[10].at[me], self.right()).wait_recv()

        @pl.when(me > 0)
        def _():
            push(self.right_in.at[me], self.right_in.at[me], self.sems[8].at[me], self.sems[11].at[me], self.left()).wait_recv()

        base = [self.own.at[me], self.core_in.at[me]]

        @pl.when(me == 0)
        def _():
            self.added(o_ref, base + [self.left_in.at[me]])

        @pl.when(me == count - 1)
        def _():
            self.added(o_ref, base + [self.right_in.at[me]])

        @pl.when((me > 0) & (me < count - 1))
        def _():
            self.added(o_ref, base + [self.left_in.at[me], self.right_in.at[me]])

        @pl.when(me > 0)
        def _():
            self.to_left(me, 0, self.x_ref).wait_send()

        @pl.when(me < count - 1)
        def _():
            self.to_right(me, 0, self.x_ref).wait_send()

        @pl.loop(1, count)
        def _(k):
            @pl.when((me - k >= 0) & (me < count - 1))
            def _():
                self.to_right(me - k, k, self.x_ref).wait_send()

            @pl.when((me + k < count) & (me > 0))
            def _():
                self.to_left(me + k, k, self.x_ref).wait_send()

        @pl.loop(0, count)
        def _(q):
            @pl.when(q < me)
            def _():
                self.back_left(q).wait_send()

            @pl.when(q > me)
            def _():
                self.back_right(q).wait_send()


GELU_ONE = 0.7978845608028654
GELU_TWO = 0.044715


def gelu_of(values_in):
    inner = GELU_ONE * (values_in + GELU_TWO * values_in * values_in * values_in)
    bend = jnp.tanh(inner)
    half = 0.5 * (1.0 + bend)
    slope = half + 0.5 * values_in * (1.0 - bend * bend) * GELU_ONE * (
        1.0 + 3.0 * GELU_TWO * values_in * values_in
    )
    return values_in * half, slope


def ffn_forward(block, gateup, down, items, ident):
    count = lax.axis_size("row")
    share, width = block.shape
    groups, _, _, part = gateup.shape
    hidden = groups * part
    out_cols = down.shape[2] // count
    rows = 2 * share
    bundle = Bundle(items)
    number = bundle.number

    def kernel(x_ref, gw_hbm, dw_hbm, *refs):
        x_refs, refs = refs[:number], refs[number:]
        o_ref, xt_hbm, at_hbm, g_hbm, u_hbm = refs[:5]
        o_refs, scratch = refs[5 : 5 + number], refs[5 + number :]
        flow = Flow(x_ref, *scratch[:6], scratch[6:19])
        gw, dw, xt, at, act, gate, up = scratch[19:26]
        gw_sem, dw_sem, xt_sem, at_sem, g_sem, u_sem = scratch[26:32]
        bundle.bind(x_refs, o_refs, scratch[32:])
        gw_load = pltpu.make_async_copy(gw_hbm, gw, gw_sem)
        dw_load = pltpu.make_async_copy(dw_hbm, dw, dw_sem)
        gw_load.start()
        dw_load.start()
        bundle.greet(False, True)
        flow.start()
        bundle.start()
        gw_load.wait()
        dw_load.wait()

        def stores(source):
            return (
                pltpu.make_async_copy(gate.at[source], g_hbm.at[source], g_sem.at[source]),
                pltpu.make_async_copy(up.at[source], u_hbm.at[source], u_sem.at[source]),
            )

        def body(source):
            here = pl.ds(pl.multiple_of(source * rows, rows), rows)
            x = flow.blocks[source].reshape(rows, width)
            xt[:, here] = x.T

            @pl.loop(0, groups)
            def _(d):
                columns = pl.ds(pl.multiple_of(d * part, part), part)
                g = flat_dot(x, gw[d, 0])
                u = flat_dot(x, gw[d, 1])
                gate[source, :, columns] = g
                up[source, :, columns] = u
                act[:, columns] = (gelu_of(g)[0] * u).astype(LOW)

            for copy in stores(source):
                copy.start()
            at[:, here] = act[...].T
            for d in range(groups):
                out = flat_dot(act[...], dw[d])
                for s in range(count):
                    columns = slice((s * groups + d) * out_cols, (s * groups + d + 1) * out_cols)
                    piece = out[:, s * out_cols : (s + 1) * out_cols]
                    flow.own[source, :, columns] = piece[:share]
                    flow.core_out[source, :, columns] = piece[share:].astype(LOW)

        flow.visit(body, bundle)
        xt_store = pltpu.make_async_copy(xt, xt_hbm, xt_sem)
        at_store = pltpu.make_async_copy(at, at_hbm, at_sem)
        xt_store.start()
        at_store.start()

        @pl.loop(0, count - 1)
        def _(t):
            flow.give_back(t)

        flow.finish(o_ref)
        bundle.finish()
        xt_store.wait()
        at_store.wait()

        @pl.loop(0, count)
        def _(source):
            for copy in stores(source):
                copy.wait()

    dma = pltpu.SemaphoreType.DMA
    buffers, sems = Flow.scratch(count, share, width)
    vmem, anywhere = pl.BlockSpec(memory_space=pltpu.VMEM), pl.BlockSpec(memory_space=pl.ANY)
    tokens = count * rows
    return pl.pallas_call(
        kernel,
        out_shape=[
            jax.ShapeDtypeStruct((share, width), FULL),
            jax.ShapeDtypeStruct((width, tokens), LOW),
            jax.ShapeDtypeStruct((hidden, tokens), LOW),
            jax.ShapeDtypeStruct((count, rows, hidden), FULL),
            jax.ShapeDtypeStruct((count, rows, hidden), FULL),
        ]
        + bundle.shapes,
        in_specs=[vmem, anywhere, anywhere] + bundle.specs,
        out_specs=[vmem] + [anywhere] * 4 + bundle.specs,
        scratch_shapes=buffers
        + sems
        + [
            pltpu.VMEM(gateup.shape, LOW),
            pltpu.VMEM(down.shape, LOW),
            pltpu.VMEM((width, tokens), LOW),
            pltpu.VMEM((hidden, tokens), LOW),
            pltpu.VMEM((rows, hidden), LOW),
            pltpu.VMEM((count, rows, hidden), FULL),
            pltpu.VMEM((count, rows, hidden), FULL),
        ]
        + [dma, dma, dma, dma, dma((count,)), dma((count,))]
        + bundle.scratch,
        compiler_params=params(ident, 60),
        cost_estimate=cost(80),
    )(block, gateup, down, *bundle.sources)


def ffn_backward(block, gateup, down, xt, at, gate, up, items, ident):
    count = lax.axis_size("row")
    share, width = block.shape
    groups, _, _, part = gateup.shape
    hidden = groups * part
    out_cols = down.shape[2] // count
    rows = 2 * share
    tokens = count * rows
    bundle = Bundle(items)
    number = bundle.number

    def kernel(x_ref, gw_hbm, dw_hbm, xt_hbm, at_hbm, g_hbm, u_hbm, *refs):
        x_refs, refs = refs[:number], refs[number:]
        o_ref, dgu_hbm, ddn_hbm = refs[:3]
        o_refs, scratch = refs[3 : 3 + number], refs[3 + number :]
        flow = Flow(x_ref, *scratch[:6], scratch[6:19])
        gw, dw, xt_own, at_own, gate_own, up_own, d_gate, d_up, total, stage, stage_down = scratch[19:30]
        load_sems, g_sem, u_sem, out_sem, down_sem = scratch[30:35]
        bundle.bind(x_refs, o_refs, scratch[35:])
        loads = [
            pltpu.make_async_copy(source, target, load_sems.at[k])
            for k, (source, target) in enumerate(
                [(dw_hbm, dw), (gw_hbm, gw), (xt_hbm, xt_own), (at_hbm, at_own)]
            )
        ]

        def fetches(source):
            return (
                pltpu.make_async_copy(g_hbm.at[source], gate_own.at[source], g_sem.at[source]),
                pltpu.make_async_copy(u_hbm.at[source], up_own.at[source], u_sem.at[source]),
            )

        for load in loads[:2]:
            load.start()

        @pl.loop(0, count)
        def _(source):
            for copy in fetches(source):
                copy.start()

        for load in loads[2:]:
            load.start()
        bundle.greet(False, True)
        flow.start()
        bundle.start()
        loads[0].wait()
        loads[1].wait()

        def columns_of(s, d):
            return pl.ds(pl.multiple_of((s * groups + d) * out_cols, out_cols), out_cols)

        def body(source):
            for copy in fetches(source):
                copy.wait()
            grad = flow.blocks[source].reshape(rows, width)
            d_act = None
            for d in range(groups):
                cut = jnp.concatenate(
                    [
                        grad[:, (s * groups + d) * out_cols : (s * groups + d + 1) * out_cols]
                        for s in range(count)
                    ],
                    axis=1,
                )
                term = against(cut, dw[d])
                d_act = term if d_act is None else d_act + term
            total[:, :hidden] = d_act

            @pl.loop(0, groups)
            def _(d):
                columns = pl.ds(pl.multiple_of(d * part, part), part)
                grad_act = total[:, columns]
                curve, slope = gelu_of(gate_own[source, :, columns])
                d_gate[source, :, columns] = (grad_act * up_own[source, :, columns] * slope).astype(LOW)
                d_up[source, :, columns] = (grad_act * curve).astype(LOW)

            total[...] = jnp.zeros(total.shape, FULL)

            @pl.loop(0, groups)
            def _(d):
                columns = pl.ds(pl.multiple_of(d * part, part), part)
                total[...] += against(d_gate[source, :, columns], gw[d, 0]) + against(
                    d_up[source, :, columns], gw[d, 1]
                )

            flow.own[source] = total[:share]
            flow.core_out[source] = total[share:].astype(LOW)

        flow.visit(body, bundle)
        loads[2].wait()
        loads[3].wait()

        def gateup_store(d, which):
            return pltpu.make_async_copy(stage.at[which], dgu_hbm.at[d, which], out_sem.at[which])

        def down_store(d):
            return pltpu.make_async_copy(stage_down, ddn_hbm.at[d], down_sem)

        def weights(d):
            columns = pl.ds(pl.multiple_of(d * part, part), part)
            for which, grads in ((0, d_gate), (1, d_up)):

                @pl.when(d > 0)
                def _():
                    gateup_store(d - 1, which).wait()

                right = grads[:, :, columns].reshape(tokens, part)

                @pl.loop(0, width // 512)
                def _(k):
                    high = pl.ds(pl.multiple_of(k * 512, 512), 512)
                    stage[which, high] = flat_dot(xt_own[high], right).astype(LOW)

                gateup_store(d, which).start()

            @pl.when(d > 0)
            def _():
                down_store(d - 1).wait()

            right = jnp.concatenate(
                [flow.blocks[:, :, :, columns_of(s, d)].reshape(tokens, out_cols) for s in range(count)],
                axis=1,
            )

            @pl.loop(0, hidden // 256)
            def _(k):
                high = pl.ds(pl.multiple_of(k * 256, 256), 256)
                stage_down[high] = flat_dot(at_own[high], right).astype(LOW)

            down_store(d).start()

        @pl.loop(0, count - 1)
        def _(t):
            flow.give_back(t)
            weights(t)

        weights(groups - 1)
        for which in range(2):
            gateup_store(groups - 1, which).wait()
        down_store(groups - 1).wait()
        flow.finish(o_ref)
        bundle.finish()

    dma = pltpu.SemaphoreType.DMA
    buffers, sems = Flow.scratch(count, share, width)
    vmem, anywhere = pl.BlockSpec(memory_space=pltpu.VMEM), pl.BlockSpec(memory_space=pl.ANY)
    return pl.pallas_call(
        kernel,
        out_shape=[
            jax.ShapeDtypeStruct((share, width), FULL),
            jax.ShapeDtypeStruct(gateup.shape, LOW),
            jax.ShapeDtypeStruct(down.shape, LOW),
        ]
        + bundle.shapes,
        in_specs=[vmem] + [anywhere] * 6 + bundle.specs,
        out_specs=[vmem, anywhere, anywhere] + bundle.specs,
        scratch_shapes=buffers
        + sems
        + [
            pltpu.VMEM(gateup.shape, LOW),
            pltpu.VMEM(down.shape, LOW),
            pltpu.VMEM((width, tokens), LOW),
            pltpu.VMEM((hidden, tokens), LOW),
            pltpu.VMEM((count, rows, hidden), FULL),
            pltpu.VMEM((count, rows, hidden), FULL),
            pltpu.VMEM((count, rows, hidden), LOW),
            pltpu.VMEM((count, rows, hidden), LOW),
            pltpu.VMEM((rows, width), FULL),
            pltpu.VMEM((2, width, part), LOW),
            pltpu.VMEM((hidden, count * out_cols), LOW),
        ]
        + [dma((4,)), dma((count,)), dma((count,)), dma((2,)), dma]
        + bundle.scratch,
        compiler_params=params(ident, 62),
        cost_estimate=cost(90),
    )(block, gateup, down, xt, at, gate, up, *bundle.sources)


def finish_step(small, sum_rows, groups, ident):
    axes = ("col", "row", "dp")
    sizes = [lax.axis_size(axis) for axis in axes]
    high = small.shape[0]
    number = len(groups)
    arrays = [array for group in groups for array in group[:4]]

    def kernel(x_ref, *refs):
        sources, refs = refs[: 4 * number], refs[4 * number :]
        o_ref, outs, refs = refs[0], refs[1 : 1 + 3 * number], refs[1 + 3 * number :]
        held, refs = refs[: 4 * number], refs[4 * number :]
        load_sem, store_sem, refs = refs[0], refs[1], refs[2:]
        slots, sends, recvs = (refs[k::3] for k in range(3))

        def load(k):
            return pltpu.make_async_copy(sources[k], held[k], load_sem.at[k])

        def store(group, k):
            return pltpu.make_async_copy(held[4 * group + (1, 2, 0)[k]], outs[3 * group + k], store_sem.at[3 * group + k])

        spots = [lax.axis_index(axis) for axis in axes]
        barrier = pltpu.get_barrier_semaphore()
        for axis, size, me in zip(axes, sizes, spots):
            for k in range(1, size):
                pl.semaphore_signal(
                    barrier, inc=1, device_id={axis: lax.rem(me + k, size)}, device_id_type=MESH
                )
        for k in range(4 * number):
            load(k).start()
        pl.semaphore_wait(barrier, sum(sizes) - len(sizes))
        for at, (axis, size, me) in enumerate(zip(axes, sizes, spots)):
            buf, send, recv = slots[at], sends[at], recvs[at]
            buf[me] = x_ref[...] if at == 0 else o_ref[...]
            for k in range(1, size):
                push(buf.at[me], buf.at[me], send.at[k], recv.at[k], {axis: lax.rem(me + k, size)}).start()
            for k in range(1, size):
                origin = lax.rem(me + size - k, size)
                push(buf.at[origin], buf.at[origin], send.at[k], recv.at[k], {axis: origin}).wait()
            total = buf[0]
            top = buf[0, high - 8 :]
            for k in range(1, size):
                total = total + buf[k]
                top = jnp.maximum(top, buf[k, high - 8 :])
            o_ref[...] = total
            o_ref[high - 8 :] = top
        sums = o_ref[:sum_rows]
        squares = jnp.sum(jnp.sum(sums * sums, axis=1, keepdims=True), axis=0, keepdims=True)
        squares = squares + o_ref[sum_rows : sum_rows + 1, :1]
        clip = CLIP / jnp.maximum(jnp.sqrt(squares), CLIP)
        tops = o_ref[high - 1 :]
        lanes = lax.broadcasted_iota(jnp.int32, (1, 128), 1)
        group_size = QUERY_HEADS // KEY_VALUE_HEADS

        def factor(first, count):
            chosen = (lanes >= first) & (lanes < first + count)
            top = jnp.max(jnp.where(chosen, tops, NEGATIVE), axis=1, keepdims=True)
            return jnp.sqrt(LOGIT_CAP / jnp.maximum(top, LOGIT_CAP))

        factors = {
            "query": factor(spots[0] * sizes[2] + spots[2], 1),
            "keyval": jnp.where(
                spots[2] < KEY_VALUE_HEADS, factor(spots[2] * group_size, group_size), 1.0
            ),
        }
        for group in range(number):
            rate, kind = groups[group][4:]
            for k in range(4):
                load(4 * group + k).wait()
            w_ref, m_ref, v_ref, g_ref = held[4 * group : 4 * group + 4]
            rows, cols = w_ref.shape
            step = min(rows, max(16, 32768 // max(cols, 128)))

            @pl.loop(0, rows // step)
            def _(at):
                here = pl.ds(pl.multiple_of(at * step, step), step)
                new = adamw_step(
                    w_ref[here], m_ref[here], v_ref[here], g_ref[here].astype(FULL) * clip, rate, DECAY
                )
                m_ref[here], v_ref[here] = new[0], new[1]
                w_ref[here] = new[2] * factors[kind] if kind else new[2]

            for k in range(3):
                store(group, k).start()
        for group in range(number):
            for k in range(3):
                store(group, k).wait()

    dma = pltpu.SemaphoreType.DMA
    vmem, anywhere = pl.BlockSpec(memory_space=pltpu.VMEM), pl.BlockSpec(memory_space=pl.ANY)
    scratch = [pltpu.VMEM(array.shape, array.dtype) for array in arrays]
    scratch += [dma((4 * number,)), dma((3 * number,))]
    for size in sizes:
        scratch += [pltpu.VMEM((size,) + small.shape, FULL), dma((size,)), dma((size,))]
    outs = [jax.ShapeDtypeStruct(group[0].shape, FULL) for group in groups for _ in range(3)]
    return pl.pallas_call(
        kernel,
        out_shape=[jax.ShapeDtypeStruct(small.shape, FULL)] + outs,
        in_specs=[vmem] + [anywhere] * (4 * number),
        out_specs=[vmem] + [anywhere] * (3 * number),
        scratch_shapes=scratch,
        compiler_params=params(ident, 56),
        cost_estimate=cost(25),
    )(small, *arrays)


def allowed_block(at, high, width, spans):
    key_places = lax.broadcasted_iota(jnp.int32, (high, width), 1)
    query_places = at * high + lax.broadcasted_iota(jnp.int32, (high, width), 0)
    seen = key_places <= query_places
    for piece in range(spans.shape[0] - 1):
        start = spans[piece + 1]
        both = (
            (key_places >= start)
            & (key_places < start + IMG)
            & (query_places >= start)
            & (query_places < start + IMG)
        )
        seen = seen | both
    return seen & (key_places < spans[0])


def softmax_block(block_rows, keys, allowed):
    scores = against(block_rows, keys)
    masked = jnp.where(allowed, scores, NEGATIVE)
    peak_row = jnp.max(masked, axis=-1, keepdims=True)
    raw_weights = jnp.where(allowed, jnp.exp(masked - peak_row), 0.0)
    return raw_weights / jnp.sum(raw_weights, axis=-1, keepdims=True), peak_row


def attention_forward_head(acts, gain, head_w, kv_w, query_gain, key_gain, cos_tab, sin_tab, spans, items, ident):
    tokens, width = acts.shape
    step = 256
    bundle = Bundle(items)
    number = bundle.number

    def kernel(spans_ref, x_ref, gain_ref, qw_ref, kvw_ref, qg_ref, kg_ref, cos_ref, sin_ref, *refs):
        x_refs, refs = refs[:number], refs[number:]
        h_ref, scale_ref, qr_ref, kr_ref, vr_ref, q_ref, k_ref, v_ref, o_ref, top_ref = refs[:10]
        o_refs, sems = refs[10 : 10 + number], refs[10 + number :]
        bundle.bind(x_refs, o_refs, sems)
        bundle.greet()
        bundle.start()

        def project(at):
            here = pl.ds(pl.multiple_of(at * step, step), step)
            rows = x_ref[here].astype(FULL)
            scale = lax.rsqrt(jnp.mean(rows * rows, axis=-1, keepdims=True) + EPS)
            scale_ref[here] = jnp.broadcast_to(scale, (step, 128))
            h_ref[here] = (rows * scale * gain_ref[...]).astype(LOW)
            hidden = h_ref[here]
            cos_rows, sin_rows = cos_ref[here], sin_ref[here]
            query = flat_dot(hidden, qw_ref[...])
            qr_ref[here] = query
            q_ref[here] = turn(whole_norm(query, qg_ref[...])[0], cos_rows, sin_rows).astype(LOW)
            key = flat_dot(hidden, kvw_ref[0])
            kr_ref[here] = key
            k_ref[here] = turn(whole_norm(key, kg_ref[...])[0], cos_rows, sin_rows).astype(LOW)
            value = flat_dot(hidden, kvw_ref[1])
            vr_ref[here] = value
            v_ref[here] = whole_norm(value, 1.0)[0].astype(LOW)

        def attend(at):
            here = pl.ds(pl.multiple_of(at * step, step), step)
            allowed = allowed_block(at, step, tokens, spans_ref)
            probs, peak_row = softmax_block(q_ref[here], k_ref[...], allowed)
            o_ref[here] = flat_dot(probs.astype(LOW), v_ref[...]).astype(LOW)
            top_ref[...] = jnp.maximum(top_ref[...], jnp.max(peak_row))

        top_ref[...] = jnp.full(top_ref.shape, NEGATIVE, FULL)
        pl.loop(0, tokens // step)(project)
        bundle.step(1)
        pl.loop(0, tokens // step)(attend)
        for k in range(2, bundle.sizes[0]):
            bundle.step(k)
        bundle.finish()

    vmem = pl.BlockSpec(memory_space=pltpu.VMEM)
    low = jax.ShapeDtypeStruct((tokens, HEAD_WIDTH), LOW)
    full = jax.ShapeDtypeStruct((tokens, HEAD_WIDTH), FULL)
    return pl.pallas_call(
        kernel,
        out_shape=[
            jax.ShapeDtypeStruct((tokens, width), LOW),
            jax.ShapeDtypeStruct((tokens, 128), FULL),
            full,
            full,
            full,
            low,
            low,
            low,
            low,
            jax.ShapeDtypeStruct((8, 128), FULL),
        ]
        + bundle.shapes,
        in_specs=[pl.BlockSpec(memory_space=pltpu.SMEM)] + [vmem] * 8 + bundle.specs,
        out_specs=[vmem] * 10 + bundle.specs,
        scratch_shapes=bundle.scratch,
        compiler_params=params(ident),
        cost_estimate=cost(40),
    )(spans, acts, gain, head_w, kv_w, query_gain, key_gain, cos_tab, sin_tab, *bundle.sources)


def head_backward(queries, keys, values, grads, spans, items, ident):
    rows = queries.shape[0]
    step = min(256, rows)

    bundle = Bundle(items)
    number = bundle.number

    def kernel(spans_ref, q_ref, k_ref, v_ref, g_ref, *refs):
        x_refs, refs = refs[:number], refs[number:]
        dq_ref, dk_ref, dv_ref = refs[:3]
        bundle.bind(x_refs, refs[3 : 3 + number], refs[3 + number :])
        bundle.greet()
        bundle.start()
        dk_ref[...] = jnp.zeros(dk_ref.shape, FULL)
        dv_ref[...] = jnp.zeros(dv_ref.shape, FULL)

        @pl.loop(0, rows // step)
        def _(at):
            here = pl.ds(pl.multiple_of(at * step, step), step)
            allowed = allowed_block(at, step, keys.shape[0], spans_ref)
            block_rows, grad_rows = q_ref[here], g_ref[here]
            probs, _ = softmax_block(block_rows, k_ref[...], allowed)
            grad_probs = against(grad_rows, v_ref[...])
            delta_row = jnp.sum(probs * grad_probs, axis=-1, keepdims=True)
            grad_scores = (probs * (grad_probs - delta_row)).astype(LOW)
            dq_ref[here] = flat_dot(grad_scores, k_ref[...])
            dk_ref[...] += inner_rows(grad_scores, block_rows)
            dv_ref[...] += inner_rows(probs.astype(LOW), grad_rows)

        for k in range(1, bundle.sizes[0]):
            bundle.step(k)
        bundle.finish()

    vmem = pl.BlockSpec(memory_space=pltpu.VMEM)
    return pl.pallas_call(
        kernel,
        out_shape=[jax.ShapeDtypeStruct(queries.shape, FULL)]
        + [jax.ShapeDtypeStruct(keys.shape, FULL)] * 2
        + bundle.shapes,
        in_specs=[pl.BlockSpec(memory_space=pltpu.SMEM)] + [vmem] * 4 + bundle.specs,
        out_specs=[vmem] * 3 + bundle.specs,
        scratch_shapes=bundle.scratch,
        compiler_params=params(ident),
        cost_estimate=cost(25),
    )(spans, queries, keys, values, grads, *bundle.sources)


def whole_norm(values_in, gain_vec):
    scale = lax.rsqrt(jnp.mean(values_in * values_in, axis=-1, keepdims=True) + EPS)
    return values_in * scale * gain_vec, scale


def whole_norm_backward(values_in, scale, gain_vec, grad_out):
    weighted = grad_out * gain_vec
    inner = jnp.mean(weighted * values_in, axis=-1, keepdims=True)
    return (
        scale * weighted - values_in * (scale * scale * scale) * inner,
        jnp.sum(grad_out * values_in * scale, axis=0),
    )


def turn(values_in, cos_tab, sin_tab):
    half_width = values_in.shape[-1] // 2
    one, two = values_in[:, :half_width], values_in[:, half_width:]
    return jnp.concatenate(
        [one * cos_tab - two * sin_tab, two * cos_tab + one * sin_tab], axis=1
    )


def turn_back(values_in, cos_tab, sin_tab):
    return turn(values_in, cos_tab, -sin_tab)


def line_device(
    activations,
    per_layer,
    cotangent,
    lengths,
    starts,
    w_query,
    m_query,
    v_query,
    key_value_weight,
    key_value_first_moment,
    key_value_second_moment,
    w_attend,
    m_attend,
    v_attend,
    w_gateup,
    m_gateup,
    v_gateup,
    w_down,
    m_down,
    v_down,
    w_left,
    m_left,
    v_left,
    w_right,
    m_right,
    v_right,
    w_pergate,
    m_pergate,
    v_pergate,
    w_perproj,
    m_perproj,
    v_perproj,
    w_gains,
    m_gains,
    v_gains,
    w_heads,
    m_heads,
    v_heads,
):
    rows_n = lax.axis_size("row")
    cols_n = lax.axis_size("col")
    data_n = lax.axis_size("dp")
    me = lax.axis_index("row")
    column = lax.axis_index("col")
    data_at = lax.axis_index("dp")
    half_tok, width_a = activations.shape
    tokens = half_tok * cols_n
    share = half_tok // rows_n
    quarter = tokens // rows_n
    width = width_a * rows_n

    ff_part = w_gateup.shape[2] // rows_n
    out_cols = w_down.shape[1]
    heads_here = data_n
    left_cols, right_rows = w_left.shape[1], w_right.shape[0]
    gate_cols, proj_rows = w_pergate.shape[1], w_perproj.shape[0]

    def columns_of(at, size):
        return pl.ds(pl.multiple_of(at * size, size), size)

    def across(source, by_rows):
        high, wide = source.shape
        if by_rows:
            return Swap(
                source,
                (data_n * high, wide),
                lambda ref, q: ref,
                lambda ref, at: ref.at[columns_of(at, high)],
                "dp",
            )
        return Swap(
            source,
            (high, data_n * wide),
            lambda ref, q: ref,
            lambda ref, at: ref.at[:, columns_of(at, wide)],
            "dp",
        )

    def along(source):
        high, wide = source.shape
        return Line(
            source,
            (cols_n * high, rows_n * wide),
            lambda ref, c, r: ref.at[columns_of(c, high), columns_of(r, wide)],
            True,
        )

    whole_acts, gateup_own, attend_own, qkv_w, left_t, right_w, pergate_t, perproj_w = transfers(
        [
            along(activations),
            Swap(
                w_gateup.astype(LOW),
                (2, width, ff_part),
                lambda ref, q: ref.at[:, :, columns_of(q, ff_part)],
                lambda ref, at: ref.at[:, columns_of(at, width_a), :],
            ),
            Swap(
                w_attend.astype(LOW).reshape(rows_n, HEAD_WIDTH, out_cols),
                (HEAD_WIDTH, rows_n * out_cols),
                lambda ref, q: ref.at[q],
                lambda ref, at: ref.at[:, columns_of(at, out_cols)],
            ),
            Swap(
                jnp.concatenate([w_query, key_value_weight], axis=1).astype(LOW),
                (data_n, width_a, 2 * HEAD_WIDTH),
                lambda ref, q: ref,
                lambda ref, at: ref.at[at],
                "dp",
            ),
            across(w_left.T, True),
            across(w_right.astype(LOW), False),
            across(w_pergate.T.astype(LOW), True),
            across(w_perproj.astype(LOW), False),
        ],
        1,
        90,
    )
    gateup_all = lax.all_gather(gateup_own, "dp")
    query_w = qkv_w[:, :, :HEAD_WIDTH]
    kv_w = qkv_w[:, :, HEAD_WIDTH:]
    key_w = lax.dynamic_index_in_dim(kv_w, column, 0, False)
    value_w = lax.dynamic_index_in_dim(kv_w, KEY_VALUE_HEADS + column, 0, False)
    whole_kv, head_w, gains, extras, attend_all = transfers(
        [
            Line(
                jnp.stack([key_w, value_w]),
                (2, width, HEAD_WIDTH),
                lambda ref, c, r: ref.at[:, columns_of(r, width_a)],
            ),
            Swap(
                query_w,
                (width, HEAD_WIDTH),
                lambda ref, q: ref.at[q],
                lambda ref, at: ref.at[columns_of(at, width_a)],
            ),
            Line(w_gains, (6, width), lambda ref, c, r: ref.at[:, columns_of(r, width_a)]),
            Line(
                per_layer,
                (tokens, PLD),
                lambda ref, c, r: ref.at[columns_of(r, quarter), columns_of(c, PLD // cols_n)],
                True,
            ),
            Swap(
                attend_own,
                (data_n, HEAD_WIDTH, rows_n * out_cols),
                lambda ref, q: ref,
                lambda ref, at: ref.at[at],
                "dp",
            ),
        ],
        2,
        60,
    )
    attend_w = (
        attend_all.reshape(data_n, HEAD_WIDTH, rows_n, out_cols)
        .transpose(1, 2, 0, 3)
        .reshape(HEAD_WIDTH, width)
    )
    token_at = column * half_tok + me * share
    extras = lax.dynamic_slice_in_dim(extras, token_at, share, 0).astype(FULL)
    length = lax.dynamic_index_in_dim(lengths, data_at, 0, keepdims=True)
    piece_starts = lax.dynamic_index_in_dim(starts, data_at, 0, keepdims=False)
    spans = jnp.concatenate([length, piece_starts])

    query_gain = lax.dynamic_index_in_dim(w_heads, column * rows_n + me, 0, True)
    key_gain = w_heads[QUERY_HEADS:]
    all_cos, all_sin = rope_tables(jnp.arange(tokens, dtype=jnp.int32), HEAD_WIDTH)
    own_cos = lax.dynamic_slice_in_dim(all_cos, me * quarter, quarter, 0)
    own_sin = lax.dynamic_slice_in_dim(all_sin, me * quarter, quarter, 0)
    (
        whole_hidden,
        whole_scale,
        query_raw,
        all_key_raw,
        all_value_raw,
        queries,
        keys,
        values,
        attended,
        top,
        down_own,
        left_t,
        right_w,
    ) = attention_forward_head(
        whole_acts,
        gains[:1],
        head_w,
        whole_kv,
        query_gain,
        key_gain,
        all_cos,
        all_sin,
        spans,
        [
            Swap(
                w_down.astype(LOW).reshape(data_n, rows_n, ff_part, out_cols),
                (data_n, ff_part, rows_n * out_cols),
                lambda ref, q: ref.at[:, q],
                lambda ref, at: ref.at[:, :, columns_of(at, out_cols)],
            ),
            along(left_t.astype(LOW)),
            along(right_w),
        ],
        3,
    )
    down_own, gateup_all = lax.optimization_barrier((down_own, gateup_all))
    down_all = lax.all_gather(down_own, "dp").reshape(data_n, data_n * ff_part, -1)
    inputs = lax.dynamic_slice_in_dim(whole_acts, token_at, share, 0).astype(FULL)
    key_raw = lax.dynamic_slice_in_dim(all_key_raw, me * quarter, quarter, 0)
    value_raw = lax.dynamic_slice_in_dim(all_value_raw, me * quarter, quarter, 0)
    _, query_scale = whole_norm(query_raw, query_gain)
    _, key_scale = whole_norm(key_raw, key_gain)
    _, value_scale = whole_norm(value_raw, 1.0)

    def shares(parts):
        return parts.astype(LOW).reshape(cols_n, rows_n, share, width)

    hidden, _ = whole_norm(inputs, gains[0])
    hidden_low = hidden.astype(LOW)
    middle = against(hidden_low, left_t).astype(LOW)
    right_raw = flat_dot(middle, right_w)
    right_n, scale_r = whole_norm(right_raw, gains[1])
    projected = line_reduce(shares(flat_dot(attended, attend_w)), 5, True, 45)
    proj_n, scale_p = whole_norm(projected, gains[2])
    mixture = ((inputs + proj_n) + (hidden + right_n)) * HALF_ROOT
    ffn_n, scale_f = whole_norm(mixture, gains[3])
    down_raw, spread_ft, act_t, gate_raw, up_raw, upstream, pergate_t, perproj_w = ffn_forward(
        ffn_n.astype(LOW),
        gateup_all,
        down_all,
        [
            Swap(
                cotangent,
                (share, width),
                lambda ref, q: ref.at[columns_of(q, share)],
                lambda ref, at: ref.at[:, columns_of(at, width_a)],
            ),
            along(pergate_t),
            along(perproj_w),
        ],
        6,
    )
    upstream = upstream.astype(FULL)
    down_n, scale_d = whole_norm(down_raw, gains[4])
    block_out = mixture + down_n
    out_low = block_out.astype(LOW)
    pgate = against(out_low, pergate_t)
    pact = (jax.nn.gelu(pgate, approximate=True) * extras).astype(LOW)
    perproj = flat_dot(pact, perproj_w)
    perproj_n, scale_pp = whole_norm(perproj, gains[5])
    result = (block_out + perproj_n).astype(LOW)

    gain_grads = [None] * 6
    d_perproj, gain_grads[5] = whole_norm_backward(perproj, scale_pp, gains[5], upstream)
    d_perproj = d_perproj.astype(LOW)
    dw_perproj = inner_rows(pact, d_perproj)
    d_pact = against(d_perproj, perproj_w)
    _, pullback = jax.vjp(lambda v: jax.nn.gelu(v, approximate=True), pgate)
    (d_pgate,) = pullback(d_pact * extras)
    d_pgate = d_pgate.astype(LOW)
    dw_pergate = inner_rows(d_pgate, out_low)
    d_out = upstream + flat_dot(d_pgate, pergate_t)
    d_down, gain_grads[4] = whole_norm_backward(down_raw, scale_d, gains[4], d_out)
    d_ffn, dw_gateup, dw_down, result = ffn_backward(
        d_down.astype(LOW),
        gateup_all,
        down_all,
        spread_ft,
        act_t,
        gate_raw,
        up_raw,
        [
            Swap(
                result,
                (half_tok, width_a),
                lambda ref, q: ref.at[:, columns_of(q, width_a)],
                lambda ref, at: ref.at[columns_of(at, share)],
            )
        ],
        8,
    )
    g_gateup = lax.psum_scatter(dw_gateup, "dp", scatter_dimension=0)
    d_mix, gain_grads[3] = whole_norm_backward(mixture, scale_f, gains[3], d_ffn)
    d_half = (d_out + d_mix) * HALF_ROOT
    d_proj, gain_grads[2] = whole_norm_backward(projected, scale_p, gains[2], d_half)
    (spread_p,) = transfers(
        [
            Line(
                d_proj.astype(LOW),
                (cols_n, rows_n, share, width),
                lambda ref, c, r: ref.at[c, r],
                True,
            )
        ],
        10,
        40,
    )
    spread_p = spread_p.reshape(tokens, width)
    d_right, gain_grads[1] = whole_norm_backward(right_raw, scale_r, gains[1], d_half)
    d_right = d_right.astype(LOW)
    dw_right = inner_rows(middle, d_right)
    d_middle = against(d_right, right_w).astype(LOW)
    dw_left = inner_rows(d_middle, hidden_low)
    d_hidden_share = d_half + flat_dot(d_middle, left_t)
    inner_share = jnp.sum(d_hidden_share * gains[0] * inputs, axis=1)
    d_attended = against(spread_p, attend_w).astype(LOW)
    dw_attend = inner_rows(attended, spread_p).astype(LOW)
    d_queries, d_keys, d_values, half_here, middle_here = head_backward(
        queries,
        keys,
        values,
        d_attended,
        spans,
        [
            Swap(
                d_half.astype(LOW),
                (half_tok, width_a),
                lambda ref, q: ref.at[:, columns_of(q, width_a)],
                lambda ref, at: ref.at[columns_of(at, share)],
            ),
            Line(
                d_middle, (half_tok, d_middle.shape[1]), lambda ref, c, r: ref.at[columns_of(r, share)]
            ),
        ],
        4,
    )

    d_queries, dw_down, dw_attend, g_gateup = lax.optimization_barrier(
        (d_queries, dw_down, dw_attend, g_gateup)
    )
    g_down = lax.psum_scatter(
        dw_down.reshape(data_n, data_n, ff_part, -1), "dp", scatter_dimension=0
    )
    g_attend = lax.psum_scatter(
        dw_attend.reshape(HEAD_WIDTH, rows_n, data_n, out_cols)
        .transpose(2, 0, 1, 3)
        .reshape(data_n, HEAD_WIDTH, -1),
        "dp",
        scatter_dimension=0,
    )

    def to_shards(grad):
        return grad.astype(LOW).reshape(cols_n, -1, rows_n, width_a).transpose(0, 2, 1, 3)

    small_parts = jnp.concatenate(
        [to_shards(grad) for grad in (dw_left, dw_right, dw_pergate, dw_perproj)], axis=2
    )
    small_parts = line_reduce(small_parts, 17, True, 28).astype(LOW)
    kv_parts = jnp.concatenate(
        [
            d_keys.astype(LOW).reshape(rows_n, quarter, HEAD_WIDTH),
            d_values.astype(LOW).reshape(rows_n, quarter, HEAD_WIDTH),
        ],
        axis=1,
    )
    d_kv = line_reduce(kv_parts, 11, False, 20)
    d_q_raw, dg_query = whole_norm_backward(
        query_raw, query_scale, query_gain, turn_back(d_queries, all_cos, all_sin)
    )
    d_k_raw, dg_key = whole_norm_backward(
        key_raw, key_scale, key_gain, turn_back(d_kv[:quarter], own_cos, own_sin)
    )
    d_v_raw, _ = whole_norm_backward(value_raw, value_scale, 1.0, d_kv[quarter:])
    d_raw = jnp.concatenate([d_q_raw, d_k_raw, d_v_raw], axis=0).astype(LOW)
    gateup_squares = jnp.sum(jnp.square(g_gateup.astype(FULL)))
    spread_q, g_gateup = transfers(
        [
            Line(d_raw, (rows_n,) + d_raw.shape, lambda ref, c, r: ref.at[r]),
            Swap(
                g_gateup,
                w_gateup.shape,
                lambda ref, q: ref.at[:, columns_of(q, width_a), :],
                lambda ref, at: ref.at[:, :, columns_of(at, ff_part)],
            ),
        ],
        12,
        100,
    )
    d_q_all = spread_q[:, :tokens]
    d_k_all = spread_q[:, tokens : tokens + quarter].reshape(tokens, HEAD_WIDTH)
    d_v_all = spread_q[:, tokens + quarter :].reshape(tokens, HEAD_WIDTH)
    d_hidden = against(d_k_all, key_w) + against(d_v_all, value_w)
    for k in range(heads_here):
        d_hidden = d_hidden + against(d_q_all[k], query_w[k])
    acts = activations.astype(FULL)
    gains_here = lax.dynamic_slice_in_dim(w_gains, 0, 1, 0)[0]
    scale_here = lax.dynamic_slice_in_dim(whole_scale[:, :1], column * half_tok, half_tok, 0)
    own_acts = lax.dynamic_slice_in_dim(whole_acts, me * width_a, width_a, 1).astype(FULL)
    inner = jnp.sum(d_hidden * gains_here * own_acts, axis=1)
    inner = lax.dynamic_update_slice_in_dim(
        inner, lax.dynamic_slice_in_dim(inner, token_at, share, 0) + inner_share, token_at, 0
    ).reshape(-1, 128)

    spread_h = lax.dynamic_slice_in_dim(whole_hidden, me * width_a, width_a, 1)
    dw_query = jnp.stack([inner_rows(spread_h, d_q_all[k]).astype(LOW) for k in range(heads_here)])
    dw_kv = jnp.stack(
        [inner_rows(spread_h, d_k_all).astype(LOW), inner_rows(spread_h, d_v_all).astype(LOW)]
    )
    cuts = []
    start = 0
    for rows, by_rows in (
        (data_n * left_cols, True),
        (right_rows, False),
        (data_n * gate_cols, True),
        (proj_rows, False),
    ):
        cut = small_parts[start : start + rows]
        start += rows
        if by_rows:
            cut = cut.reshape(data_n, -1, width_a)
            cut = [cut[:, :, k * out_cols : (k + 1) * out_cols] for k in range(data_n)]
            cuts.append(jnp.concatenate(cut, axis=1))
        else:
            cuts.append(jnp.stack([cut[:, k * out_cols : (k + 1) * out_cols] for k in range(data_n)]))
    squares = gateup_squares
    for gradient in (g_attend, g_down):
        squares = squares + jnp.sum(jnp.square(gradient.astype(FULL)))
    g_query, g_keyval, flat_grads, g_down, g_attend, d_hidden, inner = shard_total(
        dw_query,
        dw_kv,
        jnp.concatenate(cuts, axis=1),
        [
            Swap(
                g_down,
                (data_n, rows_n, ff_part, out_cols),
                lambda ref, q: ref.at[:, :, columns_of(q, out_cols)],
                lambda ref, at: ref.at[:, at],
            ),
            Swap(
                g_attend,
                (rows_n, HEAD_WIDTH, out_cols),
                lambda ref, q: ref.at[:, columns_of(q, out_cols)],
                lambda ref, at: ref.at[at],
            ),
            Pair(d_hidden.astype(LOW).reshape(cols_n, half_tok, width_a)),
            Line(inner, (cols_n, rows_n) + inner.shape, lambda ref, c, r: ref.at[c, r], True),
        ],
        13,
    )
    squares = squares + jnp.where(column == 0, jnp.sum(g_keyval * g_keyval), 0.0)
    squares = squares + jnp.sum(g_query * g_query) + jnp.sum(flat_grads * flat_grads)
    g_down = g_down.reshape(w_down.shape)
    g_attend = g_attend.reshape(w_attend.shape)
    small_grads = []
    start = 0
    for w, by_rows in ((w_left, True), (w_right, False), (w_pergate, True), (w_perproj, False)):
        rows = w.size // out_cols
        cut = flat_grads[start : start + rows]
        start += rows
        if by_rows:
            high = rows // data_n
            cut = [cut[k * high : (k + 1) * high] for k in range(data_n)]
            cut = jnp.concatenate(cut, axis=1).T
        small_grads.append(cut)
    g_left, g_right, g_pergate, g_perproj = small_grads

    inner = jnp.sum(inner, axis=(0, 1)).reshape(cols_n, half_tok) / MODEL_WIDTH
    inner = lax.dynamic_index_in_dim(inner, column, 0, False)[:, None]
    half_here = half_here.astype(FULL)
    own_left = lax.dynamic_slice_in_dim(left_t, me * width_a, width_a, 1)
    d_hidden = d_hidden[0].astype(FULL) + d_hidden[1].astype(FULL) + half_here
    d_hidden = d_hidden + flat_dot(middle_here, own_left)
    grad_input = (
        half_here
        + scale_here * d_hidden * gains_here
        - acts * (scale_here * scale_here * scale_here) * inner
    ).astype(LOW)
    gain_zero = jnp.sum(d_hidden * acts * scale_here, axis=0)

    gain_full = jnp.stack(
        [
            lax.dynamic_update_slice_in_dim(
                jnp.zeros((width,), FULL), gain_zero, me * width_a, 0
            )
        ]
        + gain_grads[1:]
    )
    head_full = lax.dynamic_update_slice_in_dim(
        jnp.zeros((QUERY_HEADS + 1, HEAD_WIDTH), FULL), dg_query[None], column * rows_n + me, 0
    )
    head_full = head_full.at[QUERY_HEADS].add(dg_key)
    logit_row = lax.dynamic_update_slice_in_dim(
        jnp.full((128,), NEGATIVE, FULL), top[0, :1], column * rows_n + me, 0
    )
    gain_rows = gain_full.size // 128
    head_rows = head_full.size // 128
    pad_rows = -(gain_rows + head_rows) % 8
    small = jnp.concatenate(
        [
            gain_full.reshape(-1, 128),
            head_full.reshape(-1, 128),
            jnp.broadcast_to(squares, (pad_rows, 128)),
            jnp.broadcast_to(logit_row[None], (8, 128)),
        ]
    )
    weights = (
        w_query,
        key_value_weight,
        w_attend,
        w_gateup,
        w_down,
        w_left,
        w_right,
        w_pergate,
        w_perproj,
    )
    moments = (
        m_query,
        key_value_first_moment,
        m_attend,
        m_gateup,
        m_down,
        m_left,
        m_right,
        m_pergate,
        m_perproj,
    )
    seconds = (
        v_query,
        key_value_second_moment,
        v_attend,
        v_gateup,
        v_down,
        v_left,
        v_right,
        v_pergate,
        v_perproj,
    )
    gradients = (
        g_query,
        g_keyval,
        g_attend,
        g_gateup,
        g_down,
        g_left,
        g_right,
        g_pergate,
        g_perproj,
    )
    fan_ins = (
        MODEL_WIDTH,
        MODEL_WIDTH,
        QUERY_HEADS * HEAD_WIDTH,
        MODEL_WIDTH,
        FF,
        MODEL_WIDTH,
        RANK,
        MODEL_WIDTH,
        PLD,
    )
    kinds = ("query", "keyval") + (None,) * 7
    order = (3, 4, 0, 1, 2, 5, 6, 7, 8)
    groups = [
        tuple(
            array.reshape(-1, array.shape[-1])
            for array in (weights[k], moments[k], seconds[k], gradients[k])
        )
        + (fan_ins[k] ** (-0.5), kinds[k])
        for k in order
    ]
    small, *stepped = finish_step(small, gain_rows + head_rows, groups, 15)
    updated = [None] * 9
    for at, k in enumerate(order):
        updated[k] = [array.reshape(weights[k].shape) for array in stepped[3 * at : 3 * at + 3]]
    gain_sum = small[:gain_rows].reshape(6, width)
    head_sum = small[gain_rows : gain_rows + head_rows].reshape(QUERY_HEADS + 1, HEAD_WIDTH)
    logit_top = small[-1, :QUERY_HEADS]
    g_gains = lax.dynamic_slice_in_dim(gain_sum, me * width_a, width_a, 1)
    squares = small[gain_rows + head_rows, 0]
    squares = squares + jnp.sum(gain_sum * gain_sum) + jnp.sum(head_sum * head_sum)
    grad_norm = jnp.sqrt(squares)
    clip_scale = CLIP / jnp.maximum(grad_norm, CLIP)
    scale_factors = LOGIT_CAP / jnp.maximum(logit_top, LOGIT_CAP)
    updated.append(
        adamw_step(w_gains, m_gains, v_gains, g_gains * clip_scale, GAIN_RATE, 0.0)
    )
    updated.append(
        adamw_step(w_heads, m_heads, v_heads, head_sum * clip_scale, HEAD_RATE, 0.0)
    )
    new_query, new_keyval = updated[0][2], updated[1][2]
    return (
        result,
        grad_input,
        grad_norm,
        scale_factors,
        updated[0][0],
        updated[0][1],
        new_query,
        updated[1][0],
        updated[1][1],
        new_keyval,
        updated[2][0],
        updated[2][1],
        updated[2][2],
        updated[3][0],
        updated[3][1],
        updated[3][2],
        updated[4][0],
        updated[4][1],
        updated[4][2],
        updated[5][0],
        updated[5][1],
        updated[5][2],
        updated[6][0],
        updated[6][1],
        updated[6][2],
        updated[7][0],
        updated[7][1],
        updated[7][2],
        updated[8][0],
        updated[8][1],
        updated[8][2],
        updated[9][0],
        updated[9][1],
        updated[9][2],
        updated[10][0],
        updated[10][1],
        updated[10][2],
    )


def per_device(
    activations,
    per_layer,
    cotangent,
    lengths,
    starts,
    w_query,
    m_query,
    v_query,
    key_value_weight,
    key_value_first_moment,
    key_value_second_moment,
    w_attend,
    m_attend,
    v_attend,
    w_gateup,
    m_gateup,
    v_gateup,
    w_down,
    m_down,
    v_down,
    w_left,
    m_left,
    v_left,
    w_right,
    m_right,
    v_right,
    w_pergate,
    m_pergate,
    v_pergate,
    w_perproj,
    m_perproj,
    v_perproj,
    w_gains,
    m_gains,
    v_gains,
    w_heads,
    m_heads,
    v_heads,
):
    row_devs = lax.axis_size("row")
    col_devs = lax.axis_size("col")
    data_devs = lax.axis_size("dp")
    row_place = lax.axis_index("row")
    column_place = lax.axis_index("col")
    data_at = lax.axis_index("dp")
    bf16 = jnp.bfloat16
    single_float = jnp.float32
    query_b, keyval_b, attend_b, gateup_b, down_b, left_b, right_b, pergate_b, perproj_b = (
        lax.all_gather(w_query.astype(bf16), "dp", axis=1, tiled=True),
        lax.all_gather(key_value_weight.astype(bf16), "dp", axis=1, tiled=True),
        lax.all_gather(w_attend.astype(bf16), "dp", axis=1, tiled=True),
        lax.all_gather(w_gateup.astype(bf16), "dp", axis=2, tiled=True),
        lax.all_gather(w_down.astype(bf16), "dp", axis=1, tiled=True),
        lax.all_gather(w_left.astype(bf16), "dp", axis=1, tiled=True),
        lax.all_gather(w_right.astype(bf16), "dp", axis=1, tiled=True),
        lax.all_gather(w_pergate.astype(bf16), "dp", axis=1, tiled=True),
        lax.all_gather(w_perproj.astype(bf16), "dp", axis=1, tiled=True),
    )
    inputs = activations.astype(single_float)
    tok_a, width_a = inputs.shape
    grouped_rows = tok_a * col_devs
    token_batch = grouped_rows // row_devs
    q_cols = query_b.shape[1]
    l_cols = left_b.shape[1]
    kv_cols = keyval_b.shape[1]
    ff_here = gateup_b.shape[2]
    local_heads = q_cols // HEAD_WIDTH
    length = lax.dynamic_index_in_dim(lengths, data_at, 0, keepdims=False)
    piece_starts = lax.dynamic_index_in_dim(starts, data_at, 0, keepdims=False)
    own_places = row_place * token_batch + jnp.arange(token_batch, dtype=jnp.int32)
    all_places = jnp.arange(grouped_rows, dtype=jnp.int32)
    own_cos, own_sin = rope_tables(own_places, HEAD_WIDTH)
    query_gains = lax.dynamic_slice_in_dim(w_heads, column_place * local_heads, local_heads, 0)
    key_gain = w_heads[QUERY_HEADS]
    hidden, scale_in = norm_forward(inputs, w_gains[0])
    hidden_b = hidden.astype(bf16)
    spread_h = spread_col(hidden_b)
    type_one = reduce_row(flat_dot(spread_h, jnp.concatenate([query_b, left_b], axis=1)))
    key_raw_all = lax.psum(flat_dot(spread_h, keyval_b), "row")
    all_cos, all_sin = rope_tables(all_places, HEAD_WIDTH)
    key_value_whole = key_form(key_raw_all, key_gain, all_cos, all_sin).astype(bf16)
    key_raw = lax.dynamic_slice_in_dim(key_raw_all, row_place * token_batch, token_batch, 0)
    query_raw = type_one[:, :q_cols]
    middle_b = type_one[:, q_cols : q_cols + l_cols].astype(bf16)
    queries = query_form(query_raw, query_gains, own_cos, own_sin).astype(bf16)
    key_value_heads = (column_place * local_heads + jnp.arange(local_heads, dtype=jnp.int32)) // (
        QUERY_HEADS // KEY_VALUE_HEADS
    )
    every_key = key_value_whole[:, : KEY_VALUE_HEADS * HEAD_WIDTH].reshape(
        grouped_rows, KEY_VALUE_HEADS, HEAD_WIDTH
    )
    every_value = key_value_whole[:, KEY_VALUE_HEADS * HEAD_WIDTH :].reshape(
        grouped_rows, KEY_VALUE_HEADS, HEAD_WIDTH
    )
    key_sel = jnp.take(every_key, key_value_heads, axis=1)
    value_sel = jnp.take(every_value, key_value_heads, axis=1)
    attended, block_peaks, block_totals = attention_forward(
        queries, key_sel, value_sel, own_places, all_places, length, piece_starts
    )
    attended_b = attended.reshape(token_batch, q_cols).astype(bf16)
    joined_b = jnp.concatenate([attended_b, middle_b], axis=1)
    spread_j = spread_row(joined_b)
    type_two = reduce_col(
        jnp.concatenate(
            [flat_dot(spread_j[:, :q_cols], attend_b), flat_dot(spread_j[:, q_cols:], right_b)],
            axis=1,
        )
    )
    projected = type_two[:, :width_a]
    right_raw = type_two[:, width_a:]
    right_n, scale_r = norm_forward(right_raw, w_gains[1])
    laurel = hidden + right_n
    proj_n, scale_p = norm_forward(projected, w_gains[2])
    gated_sum = inputs + proj_n
    mixture = (gated_sum + laurel) * HALF_ROOT
    ffn_n, scale_f = norm_forward(mixture, w_gains[3])
    ffn_b = ffn_n.astype(bf16)
    spread_f = spread_col(ffn_b)
    gateup_pair = jnp.concatenate([gateup_b[0], gateup_b[1]], axis=1)
    gate_up = reduce_row(flat_dot(spread_f, gateup_pair))
    gate_raw = gate_up[:, :ff_here]
    up_raw = gate_up[:, ff_here:]
    act_b = (jax.nn.gelu(gate_raw, approximate=True) * up_raw).astype(bf16)
    spread_a = spread_row(act_b)
    down_raw = reduce_col(flat_dot(spread_a, down_b))
    down_n, scale_d = norm_forward(down_raw, w_gains[4])
    block_out = mixture + down_n
    out_b = block_out.astype(bf16)
    spread_o = spread_col(out_b)
    pgate = reduce_row(flat_dot(spread_o, pergate_b))
    extras = per_layer.astype(single_float)
    pact_b = (jax.nn.gelu(pgate, approximate=True) * extras).astype(bf16)
    spread_p = spread_row(pact_b)
    perproj = reduce_col(flat_dot(spread_p, perproj_b))
    perproj_n, scale_pp = norm_forward(perproj, w_gains[5])
    result = (block_out + perproj_n).astype(bf16)
    upstream = cotangent.astype(single_float)
    gain_grads = [None, None, None, None, None, None]
    d_perproj, gain_grads[5] = norm_backward(perproj, scale_pp, w_gains[5], upstream)
    grads_five = grads_col(d_perproj.astype(bf16))
    dw_perproj = inner_rows(spread_p, grads_five)
    d_pact = reduce_row(against(grads_five, perproj_b))
    gelu_out, pullback = jax.vjp(lambda v: jax.nn.gelu(v, approximate=True), pgate)
    (d_pgate,) = pullback(d_pact * extras)
    grads_four = grads_row(d_pgate.astype(bf16))
    dw_pergate = inner_rows(spread_o, grads_four)
    d_out = upstream + reduce_col(against(grads_four, pergate_b))
    d_down, gain_grads[4] = norm_backward(down_raw, scale_d, w_gains[4], d_out)
    grads_three = grads_col(d_down.astype(bf16))
    dw_down = inner_rows(spread_a, grads_three)
    d_act = reduce_row(against(grads_three, down_b))
    act_out, pullback = jax.vjp(lambda a, b: jax.nn.gelu(a, approximate=True) * b, gate_raw, up_raw)
    d_gate, d_up = pullback(d_act)
    local_two = jnp.concatenate([d_gate, d_up], axis=1).astype(bf16)
    grads_two = grads_row(local_two)
    dw_gateup = jnp.stack(
        [inner_rows(spread_f, grads_two[:, :ff_here]), inner_rows(spread_f, grads_two[:, ff_here:])]
    )
    d_ffn = reduce_col(
        against(grads_two[:, :ff_here], gateup_b[0]) + against(grads_two[:, ff_here:], gateup_b[1])
    )
    d_mix_norm, gain_grads[3] = norm_backward(mixture, scale_f, w_gains[3], d_ffn)
    d_half = (d_out + d_mix_norm) * HALF_ROOT
    d_proj, gain_grads[2] = norm_backward(projected, scale_p, w_gains[2], d_half)
    d_right, gain_grads[1] = norm_backward(right_raw, scale_r, w_gains[1], d_half)
    grads_one = grads_col(jnp.concatenate([d_proj, d_right], axis=1).astype(bf16))
    dw_attend = inner_rows(spread_j[:, :q_cols], grads_one[:, :width_a])
    dw_right = inner_rows(spread_j[:, q_cols:], grads_one[:, width_a:])
    d_joined = reduce_row(
        jnp.concatenate(
            [against(grads_one[:, :width_a], attend_b), against(grads_one[:, width_a:], right_b)],
            axis=1,
        )
    )
    d_attended = d_joined[:, :q_cols].astype(bf16).reshape(token_batch, local_heads, HEAD_WIDTH)
    d_middle = d_joined[:, q_cols:]
    d_queries, d_key_sel, d_value_sel = attention_backward(
        queries,
        key_sel,
        value_sel,
        d_attended,
        block_peaks,
        block_totals,
        own_places,
        all_places,
        length,
        piece_starts,
    )
    single_hot_mask = (
        key_value_heads[:, None] == jnp.arange(KEY_VALUE_HEADS, dtype=jnp.int32)[None, :]
    ).astype(single_float)
    key_gradient = jnp.sum(d_key_sel[:, :, None, :] * single_hot_mask[None, :, :, None], axis=1)
    value_gradient = jnp.sum(d_value_sel[:, :, None, :] * single_hot_mask[None, :, :, None], axis=1)
    key_gradient, value_gradient = lax.psum((key_gradient, value_gradient), ("row", "col"))
    local_key_gradient = lax.dynamic_slice_in_dim(
        key_gradient, row_place * token_batch, token_batch, 0
    ).reshape(token_batch, KEY_VALUE_HEADS * HEAD_WIDTH)
    local_value_gradient = lax.dynamic_slice_in_dim(
        value_gradient, row_place * token_batch, token_batch, 0
    ).reshape(token_batch, KEY_VALUE_HEADS * HEAD_WIDTH)
    query_out, pullback = jax.vjp(
        lambda r, g: query_form(r, g, own_cos, own_sin), query_raw, query_gains
    )
    d_query_raw, dg_query = pullback(d_queries)
    key_tile = jnp.broadcast_to(key_gain, (token_batch, 1, HEAD_WIDTH))
    key_out, pullback = jax.vjp(lambda r, g: key_form(r, g, own_cos, own_sin), key_raw, key_tile)
    d_key_raw, dg_key_rows = pullback(
        jnp.concatenate([local_key_gradient, local_value_gradient], axis=1)
    )
    slice_rows = token_batch // col_devs
    dg_key = jnp.sum(
        lax.dynamic_slice_in_dim(dg_key_rows, column_place * slice_rows, slice_rows, 0), axis=(0, 1)
    )
    grads_zero = grads_row(jnp.concatenate([d_query_raw, d_middle, d_key_raw], axis=1).astype(bf16))
    dw_query = inner_rows(spread_h, grads_zero[:, :q_cols])
    dw_left = inner_rows(spread_h, grads_zero[:, q_cols : q_cols + l_cols])
    key_grad_rows = grads_zero[:, q_cols + l_cols :]
    dw_keyval = inner_rows(spread_h, key_grad_rows)
    slab_width = kv_cols // col_devs
    d_hidden = reduce_col(
        against(grads_zero[:, :q_cols], query_b)
        + against(grads_zero[:, q_cols : q_cols + l_cols], left_b)
        + against(
            lax.dynamic_slice_in_dim(key_grad_rows, column_place * slab_width, slab_width, 1),
            lax.dynamic_slice_in_dim(keyval_b, column_place * slab_width, slab_width, 1),
        )
    )
    d_in, gain_grads[0] = norm_backward(inputs, scale_in, w_gains[0], d_hidden + d_half)
    grad_input = (d_half + d_in).astype(bf16)
    g_query, g_keyval, g_attend, g_gateup, g_down, g_left, g_right, g_pergate, g_perproj = (
        lax.psum_scatter(dw_query, "dp", scatter_dimension=1, tiled=True),
        lax.psum_scatter(dw_keyval, "dp", scatter_dimension=1, tiled=True),
        lax.psum_scatter(dw_attend, "dp", scatter_dimension=1, tiled=True),
        lax.psum_scatter(dw_gateup, "dp", scatter_dimension=2, tiled=True),
        lax.psum_scatter(dw_down, "dp", scatter_dimension=1, tiled=True),
        lax.psum_scatter(dw_left, "dp", scatter_dimension=1, tiled=True),
        lax.psum_scatter(dw_right, "dp", scatter_dimension=1, tiled=True),
        lax.psum_scatter(dw_pergate, "dp", scatter_dimension=1, tiled=True),
        lax.psum_scatter(dw_perproj, "dp", scatter_dimension=1, tiled=True),
    )
    gain_full = lax.dynamic_update_slice_in_dim(
        jnp.zeros((6, MODEL_WIDTH), single_float), jnp.stack(gain_grads), row_place * width_a, 1
    )
    head_full = lax.dynamic_update_slice_in_dim(
        jnp.zeros((QUERY_HEADS + 1, HEAD_WIDTH), single_float),
        dg_query,
        column_place * local_heads,
        0,
    )
    head_full = head_full.at[QUERY_HEADS].add(dg_key)
    logit_here = lax.dynamic_update_slice_in_dim(
        jnp.full((QUERY_HEADS,), NEGATIVE, single_float),
        jnp.max(block_peaks, axis=(0, 2)),
        column_place * local_heads,
        0,
    )

    def combine(left_part, right_part):
        return (
            left_part[0] + right_part[0],
            left_part[1] + right_part[1],
            jnp.maximum(left_part[2], right_part[2]),
        )

    gain_sum, head_sum, logit_top = joined(
        (gain_full, head_full, logit_here), ("dp", "row", "col"), combine
    )
    g_gains = lax.dynamic_slice_in_dim(gain_sum, row_place * width_a, width_a, 1)
    lead_device = (column_place == 0) & (data_at == 0)
    solo_device = lead_device & (row_place == 0)
    squares = jnp.float32(0.0)
    for gradient in (g_query, g_attend, g_gateup, g_down, g_left, g_right, g_pergate, g_perproj):
        squares = squares + jnp.sum(gradient * gradient)
    squares = squares + jnp.where(column_place == 0, jnp.sum(g_keyval * g_keyval), 0.0)
    squares = squares + jnp.where(lead_device, jnp.sum(g_gains * g_gains), 0.0)
    squares = squares + jnp.where(solo_device, jnp.sum(head_sum * head_sum), 0.0)
    grad_norm = jnp.sqrt(lax.psum(squares, ("dp", "row", "col")))
    clip_scale = CLIP / jnp.maximum(grad_norm, CLIP)
    scale_factors = LOGIT_CAP / jnp.maximum(logit_top, LOGIT_CAP)
    weights = (
        w_query,
        key_value_weight,
        w_attend,
        w_gateup,
        w_down,
        w_left,
        w_right,
        w_pergate,
        w_perproj,
        w_gains,
        w_heads,
    )
    moments = (
        m_query,
        key_value_first_moment,
        m_attend,
        m_gateup,
        m_down,
        m_left,
        m_right,
        m_pergate,
        m_perproj,
        m_gains,
        m_heads,
    )
    seconds = (
        v_query,
        key_value_second_moment,
        v_attend,
        v_gateup,
        v_down,
        v_left,
        v_right,
        v_pergate,
        v_perproj,
        v_gains,
        v_heads,
    )
    gradients = (
        g_query,
        g_keyval,
        g_attend,
        g_gateup,
        g_down,
        g_left,
        g_right,
        g_pergate,
        g_perproj,
        g_gains,
        head_sum,
    )
    step_rates = (
        MODEL_WIDTH ** (-0.5),
        MODEL_WIDTH ** (-0.5),
        (QUERY_HEADS * HEAD_WIDTH) ** (-0.5),
        MODEL_WIDTH ** (-0.5),
        FF ** (-0.5),
        MODEL_WIDTH ** (-0.5),
        RANK ** (-0.5),
        MODEL_WIDTH ** (-0.5),
        PLD ** (-0.5),
        GAIN_RATE,
        HEAD_RATE,
    )
    decays = (DECAY, DECAY, DECAY, DECAY, DECAY, DECAY, DECAY, DECAY, DECAY, 0.0, 0.0)
    updated = [
        adamw_step(
            weights[k], moments[k], seconds[k], gradients[k] * clip_scale, step_rates[k], decays[k]
        )
        for k in range(11)
    ]
    head_scale = jnp.sqrt(scale_factors)
    q_width = w_query.shape[1]
    q_head = (
        (column_place * data_devs + data_at) * q_width + jnp.arange(q_width, dtype=jnp.int32)
    ) // HEAD_WIDTH
    q_factor = jnp.sum(
        jnp.where(
            q_head[:, None] == jnp.arange(QUERY_HEADS, dtype=jnp.int32)[None, :],
            head_scale[None, :],
            0.0,
        ),
        axis=1,
    )
    new_query = updated[0][2] * q_factor[None, :]
    kv_width = key_value_weight.shape[1]
    key_value_index = data_at * kv_width + jnp.arange(kv_width, dtype=jnp.int32)
    key_value_scale = jnp.sqrt(
        jnp.min(scale_factors.reshape(KEY_VALUE_HEADS, QUERY_HEADS // KEY_VALUE_HEADS), axis=1)
    )
    key_value_choice = jnp.sum(
        jnp.where(
            (key_value_index // HEAD_WIDTH)[:, None]
            == jnp.arange(KEY_VALUE_HEADS, dtype=jnp.int32)[None, :],
            key_value_scale[None, :],
            0.0,
        ),
        axis=1,
    )
    key_value_factor = jnp.where(
        key_value_index < KEY_VALUE_HEADS * HEAD_WIDTH, key_value_choice, 1.0
    )
    new_keyval = updated[1][2] * key_value_factor[None, :]
    return (
        result,
        grad_input,
        grad_norm,
        scale_factors,
        updated[0][0],
        updated[0][1],
        new_query,
        updated[1][0],
        updated[1][1],
        new_keyval,
        updated[2][0],
        updated[2][1],
        updated[2][2],
        updated[3][0],
        updated[3][1],
        updated[3][2],
        updated[4][0],
        updated[4][1],
        updated[4][2],
        updated[5][0],
        updated[5][1],
        updated[5][2],
        updated[6][0],
        updated[6][1],
        updated[6][2],
        updated[7][0],
        updated[7][1],
        updated[7][2],
        updated[8][0],
        updated[8][1],
        updated[8][2],
        updated[9][0],
        updated[9][1],
        updated[9][2],
        updated[10][0],
        updated[10][1],
        updated[10][2],
    )


def solution(mesh):
    placed = (
        P(("dp", "col"), "row"),
        P(("dp", "row"), "col"),
        P(("dp", "col"), "row"),
        P(),
        P(),
        P("row", ("col", "dp")),
        P("row", ("col", "dp")),
        P("row", ("col", "dp")),
        P("row", "dp"),
        P("row", "dp"),
        P("row", "dp"),
        P("col", ("row", "dp")),
        P("col", ("row", "dp")),
        P("col", ("row", "dp")),
        P(None, "row", ("col", "dp")),
        P(None, "row", ("col", "dp")),
        P(None, "row", ("col", "dp")),
        P("col", ("row", "dp")),
        P("col", ("row", "dp")),
        P("col", ("row", "dp")),
        P("row", ("col", "dp")),
        P("row", ("col", "dp")),
        P("row", ("col", "dp")),
        P("col", ("row", "dp")),
        P("col", ("row", "dp")),
        P("col", ("row", "dp")),
        P("row", ("col", "dp")),
        P("row", ("col", "dp")),
        P("row", ("col", "dp")),
        P("col", ("row", "dp")),
        P("col", ("row", "dp")),
        P("col", ("row", "dp")),
        P(None, "row"),
        P(None, "row"),
        P(None, "row"),
        P(),
        P(),
        P(),
    )
    fits = (
        mesh.shape["col"] == KEY_VALUE_HEADS
        and mesh.shape["row"] * KEY_VALUE_HEADS == QUERY_HEADS
        and mesh.shape["dp"] == mesh.shape["row"]
    )
    return jax.shard_map(
        line_device if fits else per_device,
        mesh=mesh,
        in_specs=placed,
        out_specs=(
            P(("dp", "col"), "row"),
            P(("dp", "col"), "row"),
            P(),
            P(),
            P("row", ("col", "dp")),
            P("row", ("col", "dp")),
            P("row", ("col", "dp")),
            P("row", "dp"),
            P("row", "dp"),
            P("row", "dp"),
            P("col", ("row", "dp")),
            P("col", ("row", "dp")),
            P("col", ("row", "dp")),
            P(None, "row", ("col", "dp")),
            P(None, "row", ("col", "dp")),
            P(None, "row", ("col", "dp")),
            P("col", ("row", "dp")),
            P("col", ("row", "dp")),
            P("col", ("row", "dp")),
            P("row", ("col", "dp")),
            P("row", ("col", "dp")),
            P("row", ("col", "dp")),
            P("col", ("row", "dp")),
            P("col", ("row", "dp")),
            P("col", ("row", "dp")),
            P("row", ("col", "dp")),
            P("row", ("col", "dp")),
            P("row", ("col", "dp")),
            P("col", ("row", "dp")),
            P("col", ("row", "dp")),
            P("col", ("row", "dp")),
            P(None, "row"),
            P(None, "row"),
            P(None, "row"),
            P(),
            P(),
            P(),
        ),
        check_vma=False,
    )
```

```python
import jax
import jax.numpy as jnp
from jax import lax
from jax.experimental import pallas as pl
from jax.experimental.pallas import tpu as pltpu
from jax.sharding import PartitionSpec as P

MODEL_WIDTH = 2048
QUERY_HEADS = 8
KEY_VALUE_HEADS = 2
HEAD_WIDTH = 256
FF = 8192
RANK = 64
PLD = 256
IMG = 256
STEP = 10


EPS = 1e-06
ROPE_BASE = 1000000.0
BETA_ONE = 0.5
BETA_TWO = 0.5
ADAM_EPS = 1e-08
DECAY = 0.01
CLIP = 1.0
LOGIT_CAP = 4.0
GAIN_RATE = 0.6
HEAD_RATE = 0.1
HALF_ROOT = 0.7071067811865476
NEGATIVE = -1e30


def joined(part, axis, combine):
    gathered = jax.tree.map(lambda a: lax.all_gather(a, axis), part)

    def take(source):
        return jax.tree.map(lambda a: lax.dynamic_index_in_dim(a, source, 0, False), gathered)

    return lax.fori_loop(
        1, lax.axis_size(axis), lambda source, state: combine(state, take(source)), take(0)
    )


def row_total(values_in):
    return lax.psum(values_in, "row")


def spread_col(values_in):
    return lax.all_gather(values_in, "col", axis=0, tiled=True)


def reduce_row(values_in):
    return lax.psum_scatter(values_in, "row", scatter_dimension=0, tiled=True)


def spread_row(values_in):
    return lax.all_gather(values_in, "row", axis=0, tiled=True)


def reduce_col(values_in):
    return lax.psum_scatter(values_in, "col", scatter_dimension=0, tiled=True)


def grads_col(values_in):
    return lax.all_gather(values_in, "col", axis=0, tiled=True)


def grads_row(values_in):
    return lax.all_gather(values_in, "row", axis=0, tiled=True)


def inner_rows(left_mat, right_mat):
    return lax.dot_general(
        left_mat, right_mat, (((0,), (0,)), ((), ())), preferred_element_type=jnp.float32
    )


def against(grad_mat, weight_mat):
    return lax.dot_general(
        grad_mat, weight_mat, (((1,), (1,)), ((), ())), preferred_element_type=jnp.float32
    )


def flat_dot(left_mat, right_mat):
    return jnp.dot(left_mat, right_mat, preferred_element_type=jnp.float32)


def norm_forward(values_in, gain_vec):
    total_sq = row_total(jnp.sum(values_in * values_in, axis=-1, keepdims=True))
    norm_scale = lax.rsqrt(total_sq / MODEL_WIDTH + EPS)
    return (values_in * norm_scale * gain_vec, norm_scale)


def norm_backward(values_in, norm_scale, gain_vec, grad_out):
    weighted = grad_out * gain_vec
    inner_sum = row_total(jnp.sum(weighted * values_in, axis=-1, keepdims=True))
    grad_in = norm_scale * weighted - values_in * (norm_scale * norm_scale * norm_scale) * (
        inner_sum / MODEL_WIDTH
    )
    return (grad_in, jnp.sum(grad_out * values_in * norm_scale, axis=0))


def norm_rows(values_in, gain_vec):
    return (
        values_in
        * lax.rsqrt(jnp.mean(values_in * values_in, axis=-1, keepdims=True) + EPS)
        * gain_vec
    )


def rope_tables(places, feat_width):
    half_width = feat_width // 2
    powers = jnp.arange(half_width, dtype=jnp.int32).astype(jnp.float32) * (2.0 / feat_width)
    frequency = jnp.power(jnp.float32(ROPE_BASE), -powers)
    angles = places.astype(jnp.float32)[:, None] * frequency[None, :]
    return (jnp.cos(angles), jnp.sin(angles))


def rotate(values_in, cos_tab, sin_tab):
    half_width = values_in.shape[-1] // 2
    part_one = values_in[..., :half_width]
    part_two = values_in[..., half_width:]
    cos_row = cos_tab[:, None, :]
    sin_row = sin_tab[:, None, :]
    return jnp.concatenate(
        [part_one * cos_row - part_two * sin_row, part_two * cos_row + part_one * sin_row], axis=-1
    )


def query_form(unscaled_rows, gain_rows, cos_tab, sin_tab):
    shaped = unscaled_rows.reshape(unscaled_rows.shape[0], gain_rows.shape[0], HEAD_WIDTH)
    return rotate(norm_rows(shaped, gain_rows[None]), cos_tab, sin_tab)


def key_form(unscaled_rows, gain_vec, cos_tab, sin_tab):
    count_of_rows = unscaled_rows.shape[0]
    key_rows = unscaled_rows[:, : KEY_VALUE_HEADS * HEAD_WIDTH].reshape(
        count_of_rows, KEY_VALUE_HEADS, HEAD_WIDTH
    )
    value_rows = unscaled_rows[:, KEY_VALUE_HEADS * HEAD_WIDTH :].reshape(
        count_of_rows, KEY_VALUE_HEADS, HEAD_WIDTH
    )
    key_rows = rotate(norm_rows(key_rows, gain_vec), cos_tab, sin_tab)
    value_rows = norm_rows(value_rows, 1.0)
    return jnp.concatenate(
        [
            key_rows.reshape(count_of_rows, KEY_VALUE_HEADS * HEAD_WIDTH),
            value_rows.reshape(count_of_rows, KEY_VALUE_HEADS * HEAD_WIDTH),
        ],
        axis=1,
    )


def piece_of(places, starts):
    inside = (places[:, None] >= starts[None, :]) & (places[:, None] < starts[None, :] + IMG)
    labels = jnp.arange(1, starts.shape[0] + 1, dtype=jnp.int32)
    return jnp.sum(jnp.where(inside, labels[None, :], 0), axis=1) - 1


def visible(query_places, key_places, query_pieces, key_pieces, length):
    causal = key_places[None, :] <= query_places[:, None]
    same_piece = (query_pieces[:, None] == key_pieces[None, :]) & (query_pieces[:, None] >= 0)
    return (key_places[None, :] < length) & (causal | same_piece)


def block_mask(own_places, key_places, key_pieces, length, starts):
    return visible(own_places, key_places, piece_of(own_places, starts), key_pieces, length)


def attention_forward(queries, key_sel, value_sel, own_places, key_places, length, starts):
    count_of_rows, head_count = (queries.shape[0], queries.shape[1])
    block_size = min(512, count_of_rows)
    key_pieces = piece_of(key_places, starts)
    stacked = queries.reshape(count_of_rows // block_size, block_size, head_count, HEAD_WIDTH)

    def one_block(element):
        block_rows, block_at = element
        allowed = block_mask(own_places, key_places, key_pieces, length, starts)
        scores = jnp.einsum("qhd,khd->hqk", block_rows, key_sel, preferred_element_type=jnp.float32)
        masked = jnp.where(allowed[None], scores, NEGATIVE)
        peak_row = jnp.max(masked, axis=-1, keepdims=True)
        raw_weights = jnp.where(allowed[None], jnp.exp(masked - peak_row), 0.0)
        total_row = jnp.sum(raw_weights, axis=-1, keepdims=True)
        attn_probs = (raw_weights / total_row).astype(jnp.bfloat16)
        outputs = jnp.einsum(
            "hqk,khd->qhd", attn_probs, value_sel, preferred_element_type=jnp.float32
        )
        return (outputs, peak_row[..., 0], total_row[..., 0])

    return lax.map(one_block, (stacked, jnp.arange(count_of_rows // block_size, dtype=jnp.int32)))


def attention_backward(
    queries,
    key_sel,
    value_sel,
    grad_attended,
    block_peaks,
    block_totals,
    own_places,
    key_places,
    length,
    starts,
):
    count_of_rows, head_count = (queries.shape[0], queries.shape[1])
    block_size = min(512, count_of_rows)
    block_count = count_of_rows // block_size
    key_pieces = piece_of(key_places, starts)
    stacked = queries.reshape(block_count, block_size, head_count, HEAD_WIDTH)
    grad_stacked = grad_attended.reshape(block_count, block_size, head_count, HEAD_WIDTH)

    def one_block(carry, element):
        dk_sum, dv_sum = carry
        block_rows, grad_rows, peak_row, total_row, block_at = element
        allowed = block_mask(own_places, key_places, key_pieces, length, starts)
        scores = jnp.einsum("qhd,khd->hqk", block_rows, key_sel, preferred_element_type=jnp.float32)
        masked = jnp.where(allowed[None], scores, NEGATIVE)
        raw_weights = jnp.where(allowed[None], jnp.exp(masked - peak_row[..., None]), 0.0)
        attn_probs = raw_weights / total_row[..., None]
        probs_low = attn_probs.astype(jnp.bfloat16)
        grad_probs = jnp.einsum(
            "qhd,khd->hqk", grad_rows, value_sel, preferred_element_type=jnp.float32
        )
        delta_row = jnp.sum(attn_probs * grad_probs, axis=-1, keepdims=True)
        grad_scores = (attn_probs * (grad_probs - delta_row)).astype(jnp.bfloat16)
        grad_query = jnp.einsum(
            "hqk,khd->qhd", grad_scores, key_sel, preferred_element_type=jnp.float32
        )
        dk_sum = dk_sum + jnp.einsum(
            "hqk,qhd->khd", grad_scores, block_rows, preferred_element_type=jnp.float32
        )
        dv_sum = dv_sum + jnp.einsum(
            "hqk,qhd->khd", probs_low, grad_rows, preferred_element_type=jnp.float32
        )
        return ((dk_sum, dv_sum), grad_query)

    zero_keys = jnp.zeros(key_sel.shape, jnp.float32)
    (dk_sum, dv_sum), grad_query = lax.scan(
        one_block,
        (zero_keys, zero_keys),
        (
            stacked,
            grad_stacked,
            block_peaks,
            block_totals,
            jnp.arange(block_count, dtype=jnp.int32),
        ),
    )
    return (grad_query.reshape(count_of_rows, head_count, HEAD_WIDTH), dk_sum, dv_sum)


def adamw_step(weight, moment_one, moment_two, gradient, rate, decay):
    moment_one = BETA_ONE * moment_one + (1.0 - BETA_ONE) * gradient
    moment_two = BETA_TWO * moment_two + (1.0 - BETA_TWO) * gradient * gradient
    mean_step = moment_one / (1.0 - BETA_ONE**STEP)
    spread = moment_two / (1.0 - BETA_TWO**STEP)
    return (
        moment_one,
        moment_two,
        weight - rate * (mean_step / (jnp.sqrt(spread) + ADAM_EPS) + decay * weight),
    )


MESH = pl.DeviceIdType.MESH
LOW = jnp.bfloat16
FULL = jnp.float32


def cost(micros, flops=0):
    return pl.CostEstimate(
        flops=flops, bytes_accessed=int(micros * 3.0e6), transcendentals=0
    )


def params(ident, mebibytes=48):
    return pltpu.CompilerParams(
        collective_id=ident, has_side_effects=True, vmem_limit_bytes=mebibytes * 2**20
    )


def push(source, target, send, recv, device):
    return pltpu.make_async_remote_copy(
        source, target, send, recv, device_id=device, device_id_type=MESH
    )


def greet_line(me, count, column, core):
    barrier = pltpu.get_barrier_semaphore()

    @pl.when(me > 0)
    def _():
        pl.semaphore_signal(barrier, inc=1, device_id={"row": me - 1}, device_id_type=MESH)

    @pl.when(me < count - 1)
    def _():
        pl.semaphore_signal(barrier, inc=1, device_id={"row": me + 1}, device_id_type=MESH)

    if core:
        pl.semaphore_signal(barrier, inc=1, device_id={"col": 1 - column}, device_id_type=MESH)

    ends = (me == 0) | (me == count - 1)

    @pl.when(ends)
    def _():
        pl.semaphore_wait(barrier, 1 + int(core))

    @pl.when(jnp.logical_not(ends))
    def _():
        pl.semaphore_wait(barrier, 2 + int(core))


def line_reduce(parts, ident, core, micros):
    count = lax.axis_size("row")
    high, wide = parts.shape[-2:]
    chunk = min(high, max(16, 65536 // wide))
    while high % chunk:
        chunk //= 2

    def kernel(x_ref, o_ref, c_buf, l_buf, r_buf, s_buf, send_l, send_r, send_c, recv_l, recv_r, recv_c):
        me = lax.axis_index("row")
        column = lax.axis_index("col")

        def mine(q):
            return x_ref.at[column, q] if core else x_ref.at[q]

        def core_copy(q):
            return push(x_ref.at[1 - column, q], c_buf.at[q], send_c.at[q], recv_c.at[q], {"col": 1 - column})

        def left_copy(q):
            return push(s_buf.at[q], l_buf.at[q], send_l.at[q], recv_l.at[q], {"row": me - 1})

        def right_copy(q):
            return push(s_buf.at[q], r_buf.at[q], send_r.at[q], recv_r.at[q], {"row": me + 1})

        def left_arrival(q):
            return push(s_buf.at[q], l_buf.at[q], send_l.at[q], recv_l.at[q], {"row": me + 1})

        def right_arrival(q):
            return push(s_buf.at[q], r_buf.at[q], send_r.at[q], recv_r.at[q], {"row": me - 1})

        def added(target, terms):
            @pl.loop(0, high // chunk)
            def _(at):
                rows = pl.ds(pl.multiple_of(at * chunk, chunk), chunk)
                total = terms[0][rows].astype(FULL)
                for term in terms[1:]:
                    total = total + term[rows].astype(FULL)
                target[rows] = total.astype(target.dtype)

        def base(q):
            return [mine(q)] + ([c_buf.at[q]] if core else [])

        greet_line(me, count, column, core)
        if core:
            for q in range(count):
                core_copy(q).start()

        def leftward(q):
            @pl.when(me > q)
            def _():
                if core:
                    core_copy(q).wait_recv()

                @pl.when(me < count - 1)
                def _():
                    left_arrival(q).wait_recv()
                    added(s_buf.at[q], base(q) + [l_buf.at[q]])

                @pl.when(me == count - 1)
                def _():
                    added(s_buf.at[q], base(q))

                left_copy(q).start()

        def rightward(q):
            @pl.when(me < q)
            def _():
                if core:
                    core_copy(q).wait_recv()

                @pl.when(me > 0)
                def _():
                    right_arrival(q).wait_recv()
                    added(s_buf.at[q], base(q) + [r_buf.at[q]])

                @pl.when(me == 0)
                def _():
                    added(s_buf.at[q], base(q))

                right_copy(q).start()

        for j in range(count - 1):

            @pl.when(me < count // 2)
            def _():
                rightward(count - 1 - j)

            leftward(j)

            @pl.when(me >= count // 2)
            def _():
                rightward(count - 1 - j)

        if core:
            core_copy(me).wait_recv()

        @pl.when(me < count - 1)
        def _():
            left_arrival(me).wait_recv()

        @pl.when(me > 0)
        def _():
            right_arrival(me).wait_recv()

        @pl.when(me == 0)
        def _():
            added(o_ref, base(me) + [l_buf.at[me]])

        @pl.when(me == count - 1)
        def _():
            added(o_ref, base(me) + [r_buf.at[me]])

        @pl.when((me > 0) & (me < count - 1))
        def _():
            added(o_ref, base(me) + [l_buf.at[me], r_buf.at[me]])

        for q in range(count):
            if core:
                core_copy(q).wait_send()

            @pl.when(me > q)
            def _():
                left_copy(q).wait_send()

            @pl.when(me < q)
            def _():
                right_copy(q).wait_send()

    dma = pltpu.SemaphoreType.DMA
    slots = (count, high, wide)
    vmem = pl.BlockSpec(memory_space=pltpu.VMEM)
    return pl.pallas_call(
        kernel,
        out_shape=jax.ShapeDtypeStruct((high, wide), FULL),
        in_specs=[vmem],
        out_specs=vmem,
        scratch_shapes=[
            pltpu.VMEM(slots if core else (1, 16, 128), parts.dtype),
            pltpu.VMEM(slots, parts.dtype),
            pltpu.VMEM(slots, parts.dtype),
            pltpu.VMEM(slots, parts.dtype),
        ]
        + [dma((count,))] * 6,
        compiler_params=params(ident),
        cost_estimate=cost(micros),
    )(parts)


class Line:
    def __init__(self, source, shape, place, core=False, view=None):
        self.source, self.shape, self.place, self.core = source, shape, place, core
        self.view = view

    def semaphores(self, count, data):
        dma = pltpu.SemaphoreType.DMA
        return [dma((count,)), dma((count,)), dma((2 * count,))] * 2 + [dma]

    def bind(self, x_ref, o_ref, sems, spots, sizes):
        self.o_ref, self.sems = o_ref, sems
        self.me, self.column, self.at = spots
        self.count = sizes[0]
        self.x_ref = self.view(x_ref, self.column) if self.view else x_ref

    def slot(self, source):
        return self.place(self.o_ref, self.column, source)

    def other(self, source):
        return self.place(self.o_ref, 1 - self.column, source)

    def to_left(self, source, k, origin):
        return push(origin, self.slot(source), self.sems[0].at[k], self.sems[4].at[k], {"row": self.me - 1})

    def to_right(self, source, k, origin):
        return push(origin, self.slot(source), self.sems[1].at[k], self.sems[3].at[k], {"row": self.me + 1})

    def to_core(self, source, k, origin):
        return push(origin, self.slot(source), self.sems[2].at[k], self.sems[5].at[k], {"col": 1 - self.column})

    def from_core(self, source, k):
        there = self.other(source)
        return push(there, there, self.sems[2].at[k], self.sems[5].at[k], {"col": 1 - self.column})

    def from_left(self, source, k):
        there = self.slot(source)
        return push(there, there, self.sems[1].at[k], self.sems[3].at[k - 1], {"row": self.me - 1})

    def from_right(self, source, k):
        there = self.slot(source)
        return push(there, there, self.sems[0].at[k], self.sems[4].at[k - 1], {"row": self.me + 1})

    def own(self):
        return pltpu.make_async_copy(self.x_ref, self.slot(self.me), self.sems[6])

    def start(self):
        me, count = self.me, self.count

        @pl.when(me > 0)
        def _():
            self.to_left(me, 0, self.x_ref).start()

        @pl.when(me < count - 1)
        def _():
            self.to_right(me, 0, self.x_ref).start()

        if self.core:
            self.to_core(me, 0, self.x_ref).start()
        self.own().start()

    def step(self, k):
        me, count = self.me, self.count

        @pl.when(me - k >= 0)
        def _():
            self.from_left(me - k, k).wait_recv()
            block = self.slot(me - k)

            @pl.when(me < count - 1)
            def _():
                self.to_right(me - k, k, block).start()

            if self.core:
                self.to_core(me - k, k, block).start()

        @pl.when(me + k < count)
        def _():
            self.from_right(me + k, k).wait_recv()
            block = self.slot(me + k)

            @pl.when(me > 0)
            def _():
                self.to_left(me + k, k, block).start()

            if self.core:
                self.to_core(me + k, count - 1 + k, block).start()

    def finish(self):
        me, count = self.me, self.count
        self.own().wait()

        @pl.when(me > 0)
        def _():
            self.to_left(me, 0, self.x_ref).wait_send()

        @pl.when(me < count - 1)
        def _():
            self.to_right(me, 0, self.x_ref).wait_send()

        if self.core:
            self.to_core(me, 0, self.x_ref).wait_send()
            self.from_core(me, 0).wait_recv()

        @pl.loop(1, count)
        def _(k):
            @pl.when(me - k >= 0)
            def _():
                @pl.when(me < count - 1)
                def _():
                    self.to_right(me - k, k, self.x_ref).wait_send()

                if self.core:
                    self.to_core(me - k, k, self.x_ref).wait_send()
                    self.from_core(me - k, k).wait_recv()

            @pl.when(me + k < count)
            def _():
                @pl.when(me > 0)
                def _():
                    self.to_left(me + k, k, self.x_ref).wait_send()

                if self.core:
                    self.to_core(me + k, count - 1 + k, self.x_ref).wait_send()
                    self.from_core(me + k, count - 1 + k).wait_recv()


class Swap:
    def __init__(self, source, shape, take, place, axis="row"):
        self.source, self.shape, self.take, self.place = source, shape, take, place
        self.axis = axis

    def semaphores(self, count, data):
        size = count if self.axis == "row" else data
        return [pltpu.SemaphoreType.DMA((size,)), pltpu.SemaphoreType.DMA((size,))]

    def bind(self, x_ref, o_ref, sems, spots, sizes):
        self.x_ref, self.o_ref, self.sems = x_ref, o_ref, sems
        self.me = spots[0] if self.axis == "row" else spots[2]
        self.count = sizes[0] if self.axis == "row" else sizes[1]

    def copy(self, k):
        target = lax.rem(self.me + k, self.count)
        return push(
            self.take(self.x_ref, target),
            self.place(self.o_ref, self.me),
            self.sems[0].at[k],
            self.sems[1].at[k],
            {self.axis: target},
        )

    def own(self):
        return pltpu.make_async_copy(
            self.take(self.x_ref, self.me), self.place(self.o_ref, self.me), self.sems[0].at[0]
        )

    def start(self):
        for k in range(1, self.count):
            self.copy(k).start()
        self.own().start()

    def step(self, k):
        pass

    def finish(self):
        self.own().wait()
        for k in range(1, self.count):
            self.copy(k).wait_send()
            origin = lax.rem(self.me + self.count - k, self.count)
            there = self.place(self.o_ref, origin)
            push(there, there, self.sems[0].at[k], self.sems[1].at[k], {self.axis: origin}).wait_recv()


class Pair:
    core = True

    def __init__(self, source):
        self.source, self.shape = source, source.shape

    def semaphores(self, count, data):
        dma = pltpu.SemaphoreType.DMA
        return [dma, dma, dma]

    def bind(self, x_ref, o_ref, sems, spots, sizes):
        self.x_ref, self.o_ref, self.sems = x_ref, o_ref, sems
        self.column = spots[1]

    def copy(self):
        other = 1 - self.column
        return push(self.x_ref.at[other], self.o_ref.at[1], self.sems[0], self.sems[1], {"col": other})

    def own(self):
        return pltpu.make_async_copy(self.x_ref.at[self.column], self.o_ref.at[0], self.sems[2])

    def start(self):
        self.copy().start()
        self.own().start()

    def step(self, k):
        pass

    def finish(self):
        self.own().wait()
        self.copy().wait()


class Reduce:
    core = True

    def __init__(self, source):
        self.source = source
        self.high, self.wide = source.shape[1], source.shape[2] // lax.axis_size("row")
        self.shape, self.dtype = (self.high, self.wide), FULL

    def semaphores(self, count, data):
        dma = pltpu.SemaphoreType.DMA
        slots = pltpu.VMEM((count, self.high, self.wide), self.source.dtype)
        whole = pltpu.VMEM(self.source.shape[1:], self.source.dtype)
        stage = pltpu.VMEM(self.shape, FULL)
        return [whole, stage, slots, slots, slots, slots] + [dma((count,))] * 6 + [dma, dma]

    def bind(self, x_ref, o_ref, sems, spots, sizes):
        self.x_ref, self.o_ref = x_ref, o_ref
        self.mine, self.stage, self.core_in, self.left_in, self.right_in, self.out = sems[:6]
        self.sems = sems[6:]
        self.me, self.column = spots[0], spots[1]
        self.count = sizes[0]

    def cut(self, ref, q):
        return ref.at[:, pl.ds(pl.multiple_of(q * self.wide, self.wide), self.wide)]

    def beside(self, q):
        return push(
            self.cut(self.x_ref.at[1 - self.column], q),
            self.core_in.at[q],
            self.sems[0].at[q],
            self.sems[3].at[q],
            {"col": 1 - self.column},
        )

    def to_left(self, q):
        return push(self.out.at[q], self.left_in.at[q], self.sems[1].at[q], self.sems[4].at[q], {"row": self.me - 1})

    def to_right(self, q):
        return push(self.out.at[q], self.right_in.at[q], self.sems[2].at[q], self.sems[5].at[q], {"row": self.me + 1})

    def from_right(self, q):
        return push(self.left_in.at[q], self.left_in.at[q], self.sems[1].at[q], self.sems[4].at[q], {"row": self.me + 1})

    def from_left(self, q):
        return push(self.right_in.at[q], self.right_in.at[q], self.sems[2].at[q], self.sems[5].at[q], {"row": self.me - 1})

    def own(self):
        return pltpu.make_async_copy(self.x_ref.at[self.column], self.mine, self.sems[6])

    def start(self):
        self.own().start()
        for q in range(self.count):
            self.beside(q).start()

    def added(self, target, q, others):
        step = 64
        cut = self.cut(self.mine, q)

        @pl.loop(0, self.high // step)
        def _(at):
            rows = pl.ds(pl.multiple_of(at * step, step), step)
            total = cut[rows].astype(FULL) + self.core_in[q, rows].astype(FULL)
            for other in others:
                total = total + other[q, rows].astype(FULL)
            target[rows] = total.astype(target.dtype)

    def step(self, k):
        me, count = self.me, self.count
        t = k - 1
        q_left = t - (count - 1 - me)
        q_right = count - 1 - (t - me)

        @pl.when(t == 0)
        def _():
            self.own().wait()

        @pl.when((q_left >= 0) & (q_left < me))
        def _():
            self.beside(q_left).wait()

            @pl.when(me < count - 1)
            def _():
                self.from_right(q_left).wait_recv()
                self.added(self.out.at[q_left], q_left, [self.left_in])

            @pl.when(me == count - 1)
            def _():
                self.added(self.out.at[q_left], q_left, [])

            self.to_left(q_left).start()

        @pl.when((t >= me) & (q_right > me))
        def _():
            self.beside(q_right).wait()

            @pl.when(me > 0)
            def _():
                self.from_left(q_right).wait_recv()
                self.added(self.out.at[q_right], q_right, [self.right_in])

            @pl.when(me == 0)
            def _():
                self.added(self.out.at[q_right], q_right, [])

            self.to_right(q_right).start()

    def finish(self):
        me, count = self.me, self.count
        self.beside(me).wait()

        @pl.when(me < count - 1)
        def _():
            self.from_right(me).wait_recv()

        @pl.when(me > 0)
        def _():
            self.from_left(me).wait_recv()

        @pl.when(me == 0)
        def _():
            self.added(self.stage, me, [self.left_in])

        @pl.when(me == count - 1)
        def _():
            self.added(self.stage, me, [self.right_in])

        @pl.when((me > 0) & (me < count - 1))
        def _():
            self.added(self.stage, me, [self.left_in, self.right_in])

        out = pltpu.make_async_copy(self.stage, self.o_ref, self.sems[7])
        out.start()

        @pl.loop(0, count)
        def _(q):
            @pl.when(q < me)
            def _():
                self.to_left(q).wait_send()

            @pl.when(q > me)
            def _():
                self.to_right(q).wait_send()

        out.wait()


class ShardSum:
    axis = "dp"

    def __init__(self, source, out_cols):
        self.source, self.out_cols = source, out_cols
        self.parts = source.shape[1] // out_cols // lax.axis_size("dp")
        self.shape = (source.shape[0], self.parts * out_cols)

    def semaphores(self, count, data):
        dma = pltpu.SemaphoreType.DMA
        buf = pltpu.VMEM((data,) + self.shape, self.source.dtype)
        stage = pltpu.VMEM(self.shape, self.source.dtype)
        return [buf, stage, dma((data, self.parts)), dma((data, self.parts)), dma]

    def bind(self, x_ref, o_ref, sems, spots, sizes):
        self.x_ref, self.o_ref = x_ref, o_ref
        self.buf, self.stage, self.send, self.recv, self.local = sems
        self.at, self.data = spots[2], sizes[1]

    def copy(self, k, s):
        target = lax.rem(self.at + k, self.data)
        wide = self.out_cols
        source = self.x_ref.at[:, pl.ds(pl.multiple_of((s * self.data + target) * wide, wide), wide)]
        slot = self.buf.at[k, :, pl.ds(s * wide, wide)]
        if k == 0:
            return pltpu.make_async_copy(source, slot, self.send.at[k, s])
        return push(source, slot, self.send.at[k, s], self.recv.at[k, s], {"dp": target})

    def start(self):
        for k in range(self.data):
            for s in range(self.parts):
                self.copy(k, s).start()

    def step(self, k):
        pass

    def finish(self):
        for k in range(self.data):
            for s in range(self.parts):
                self.copy(k, s).wait()

        @pl.loop(0, self.shape[0] // 64)
        def _(at):
            rows = pl.ds(pl.multiple_of(at * 64, 64), 64)
            total = self.buf[0, rows].astype(FULL)
            for k in range(1, self.data):
                total = total + self.buf[k, rows].astype(FULL)
            self.stage[rows] = total.astype(self.stage.dtype)

        out = pltpu.make_async_copy(self.stage, self.o_ref, self.local)
        out.start()
        out.wait()


class Bundle:
    def __init__(self, items):
        self.items = items
        self.number = len(items)
        self.sizes = lax.axis_size("row"), lax.axis_size("dp")
        self.kinds = [item.semaphores(*self.sizes) for item in items]
        self.across = any(getattr(item, "axis", None) == "dp" for item in items)
        self.cores = any(getattr(item, "core", False) for item in items)
        self.sources = [item.source for item in items]
        self.shapes = [
            jax.ShapeDtypeStruct(item.shape, getattr(item, "dtype", item.source.dtype)) for item in items
        ]
        self.specs = [pl.BlockSpec(memory_space=pl.ANY)] * self.number
        self.scratch = sum(self.kinds, [])

    def bind(self, x_refs, o_refs, sems):
        self.spots = lax.axis_index("row"), lax.axis_index("col"), lax.axis_index("dp")
        for item, x_ref, o_ref, kind in zip(self.items, x_refs, o_refs, self.kinds):
            item.bind(x_ref, o_ref, sems[: len(kind)], self.spots, self.sizes)
            sems = sems[len(kind) :]

    def greet(self, across=False, cores=False):
        me, column, at = self.spots
        count, data = self.sizes
        across, cores = across or self.across, cores or self.cores
        barrier = pltpu.get_barrier_semaphore()
        for k in range(1, count):
            pl.semaphore_signal(
                barrier, inc=1, device_id={"row": lax.rem(me + k, count)}, device_id_type=MESH
            )
        if across:
            for k in range(1, data):
                pl.semaphore_signal(
                    barrier, inc=1, device_id={"dp": lax.rem(at + k, data)}, device_id_type=MESH
                )
        if cores:
            pl.semaphore_signal(barrier, inc=1, device_id={"col": 1 - column}, device_id_type=MESH)
        pl.semaphore_wait(barrier, count - 1 + (data - 1) * int(across) + int(cores))

    def start(self):
        for item in self.items:
            item.start()

    def step(self, k):
        for item in self.items:
            item.step(k)

    def finish(self):
        for item in self.items:
            item.finish()


def transfers(items, ident, micros):
    bundle = Bundle(items)
    number = bundle.number

    def kernel(*refs):
        bundle.bind(refs[:number], refs[number : 2 * number], refs[2 * number :])
        bundle.greet()
        bundle.start()
        for k in range(1, bundle.sizes[0]):
            bundle.step(k)
        bundle.finish()

    return pl.pallas_call(
        kernel,
        out_shape=bundle.shapes,
        in_specs=bundle.specs,
        out_specs=bundle.specs,
        scratch_shapes=bundle.scratch,
        compiler_params=params(ident, 16),
        cost_estimate=cost(micros),
    )(*bundle.sources)


def shard_total(query_parts, kv_parts, flat_parts, items, ident):
    data = lax.axis_size("dp")
    bundle = Bundle(items)
    number = bundle.number

    def kernel(q_ref, kv_ref, f_ref, *refs):
        x_refs, refs = refs[:number], refs[number:]
        oq_ref, okv_ref, of_ref = refs[:3]
        o_refs, refs = refs[3 : 3 + number], refs[3 + number :]
        q_buf, kv_buf, f_buf = refs[:3]
        sems = refs[3:11]
        bundle.bind(x_refs, o_refs, refs[11:])
        column, at = lax.axis_index("col"), lax.axis_index("dp")
        bundle.greet(True, True)
        bundle.start()
        mine = lax.rem(at, 2) == column

        def copies(k):
            target = lax.rem(at + k, data)
            device = {"dp": target}
            return (
                push(q_ref.at[target], q_buf.at[k], sems[0].at[k], sems[1].at[k], device),
                push(kv_ref.at[target // 2], kv_buf.at[k], sems[2].at[k], sems[3].at[k], device),
                push(f_ref.at[target], f_buf.at[k], sems[4].at[k], sems[5].at[k], device),
                lax.rem(target, 2) == column,
            )

        for k in range(1, data):
            query_copy, kv_copy, flat_copy, there = copies(k)
            query_copy.start()
            flat_copy.start()

            @pl.when(there)
            def _():
                kv_copy.start()

        for k in range(1, data):
            query_copy, kv_copy, flat_copy, there = copies(k)
            query_copy.wait()
            flat_copy.wait()

            @pl.when(there)
            def _():
                kv_copy.wait_send()

            @pl.when(mine)
            def _():
                kv_copy.wait_recv()

        def added(target, own, buf, chunk):
            @pl.loop(0, target.shape[0] // chunk)
            def _(step):
                rows = pl.ds(pl.multiple_of(step * chunk, chunk), chunk)
                total = own[rows].astype(FULL)
                for k in range(1, data):
                    total = total + buf[k, rows].astype(FULL)
                target[rows] = total

        share = push(okv_ref, okv_ref, sems[6], sems[7], {"col": 1 - column})

        @pl.when(mine)
        def _():
            added(okv_ref, kv_ref.at[at // 2], kv_buf, 128)
            share.start()

        added(oq_ref, q_ref.at[at], q_buf, 128)
        added(of_ref, f_ref.at[at], f_buf, 64)

        @pl.when(mine)
        def _():
            share.wait_send()

        @pl.when(jnp.logical_not(mine))
        def _():
            share.wait_recv()

        for k in range(1, bundle.sizes[0]):
            bundle.step(k)
        bundle.finish()

    vmem = pl.BlockSpec(memory_space=pltpu.VMEM)
    dma = pltpu.SemaphoreType.DMA
    shapes = [query_parts.shape[1:], kv_parts.shape[1:], flat_parts.shape[1:]]
    return pl.pallas_call(
        kernel,
        out_shape=[jax.ShapeDtypeStruct(shape, FULL) for shape in shapes] + bundle.shapes,
        in_specs=[vmem] * 3 + bundle.specs,
        out_specs=[vmem] * 3 + bundle.specs,
        scratch_shapes=[pltpu.VMEM((data,) + shape, LOW) for shape in shapes]
        + [dma((data,))] * 6
        + [dma, dma]
        + bundle.scratch,
        compiler_params=params(ident),
        cost_estimate=cost(40),
    )(query_parts, kv_parts, flat_parts, *bundle.sources)


class Flow:
    def __init__(self, x_ref, blocks, own, core_out, core_in, left_in, right_in, sems):
        self.x_ref, self.blocks, self.own = x_ref, blocks, own
        self.core_out, self.core_in = core_out, core_in
        self.left_in, self.right_in = left_in, right_in
        self.sems = sems
        self.me, self.column = lax.axis_index("row"), lax.axis_index("col")
        self.count = blocks.shape[0]

    @staticmethod
    def scratch(count, share, width):
        dma = pltpu.SemaphoreType.DMA
        slots = (count, share, width)
        return [
            pltpu.VMEM((count, 2, share, width), LOW),
            pltpu.VMEM(slots, FULL),
            pltpu.VMEM(slots, LOW),
            pltpu.VMEM(slots, LOW),
            pltpu.VMEM(slots, LOW),
            pltpu.VMEM(slots, LOW),
        ], [dma((count,))] * 12 + [dma]

    def left(self):
        return {"row": self.me - 1}

    def right(self):
        return {"row": self.me + 1}

    def beside(self):
        return {"col": 1 - self.column}

    def to_left(self, source, k, origin):
        return push(origin, self.blocks.at[source, 0], self.sems[0].at[k], self.sems[4].at[k], self.left())

    def to_right(self, source, k, origin):
        return push(origin, self.blocks.at[source, 0], self.sems[1].at[k], self.sems[3].at[k], self.right())

    def to_core(self, source, origin):
        return push(origin, self.blocks.at[source, 1], self.sems[2].at[source], self.sems[5].at[source], self.beside())

    def back_core(self, q):
        return push(self.core_out.at[q], self.core_in.at[q], self.sems[6].at[q], self.sems[9].at[q], self.beside())

    def back_left(self, q):
        return push(self.core_out.at[q], self.left_in.at[q], self.sems[7].at[q], self.sems[10].at[q], self.left())

    def back_right(self, q):
        return push(self.core_out.at[q], self.right_in.at[q], self.sems[8].at[q], self.sems[11].at[q], self.right())

    def mine(self):
        return pltpu.make_async_copy(self.x_ref, self.blocks.at[self.me, 0], self.sems[12])

    def start(self):
        me, count = self.me, self.count

        @pl.when(me > 0)
        def _():
            self.to_left(me, 0, self.x_ref).start()

        @pl.when(me < count - 1)
        def _():
            self.to_right(me, 0, self.x_ref).start()

        self.to_core(me, self.x_ref).start()
        self.mine().start()

    def arrive(self, k):
        me, count = self.me, self.count

        @pl.when(k == 0)
        def _():
            self.mine().wait()
            self.to_core(me, self.x_ref).wait()

        @pl.when((k > 0) & (me - k >= 0))
        def _():
            source = me - k
            block = self.blocks.at[source, 0]
            push(block, block, self.sems[1].at[k], self.sems[3].at[k - 1], self.left()).wait_recv()

            @pl.when(me < count - 1)
            def _():
                self.to_right(source, k, block).start()

            self.to_core(source, block).start()

        @pl.when((k > 0) & (me + k < count))
        def _():
            source = me + k
            block = self.blocks.at[source, 0]
            push(block, block, self.sems[0].at[k], self.sems[4].at[k - 1], self.right()).wait_recv()

            @pl.when(me > 0)
            def _():
                self.to_left(source, k, block).start()

            self.to_core(source, block).start()

        @pl.when((k > 0) & (me - k >= 0))
        def _():
            self.to_core(me - k, self.x_ref).wait()

        @pl.when((k > 0) & (me + k < count))
        def _():
            self.to_core(me + k, self.x_ref).wait()

    def visit(self, body, bundle):
        me, count = self.me, self.count

        @pl.loop(0, count)
        def _(k):
            self.arrive(k)

            @pl.when(k > 0)
            def _():
                bundle.step(k)

            @pl.loop(0, 2)
            def _(side):
                source = jnp.where(side == 0, me - k, me + k)

                @pl.when((source >= 0) & (source < count) & ((side == 0) | (k > 0)))
                def _():
                    body(source)
                    self.back_core(source).start()

    def added(self, target, terms):
        high, wide = target.shape
        step = min(high, max(16, 65536 // wide))

        @pl.loop(0, high // step)
        def _(at):
            rows = pl.ds(pl.multiple_of(at * step, step), step)
            total = terms[0][rows]
            for term in terms[1:]:
                total = total + term[rows].astype(FULL)
            target[rows] = total.astype(target.dtype)

    def give_back(self, t):
        me, count = self.me, self.count
        q_left = t - (count - 1 - me)
        q_right = count - 1 - (t - me)

        def leftward():
            q = q_left
            self.back_core(q).wait()

            @pl.when(me < count - 1)
            def _():
                push(self.left_in.at[q], self.left_in.at[q], self.sems[7].at[q], self.sems[10].at[q], self.right()).wait_recv()
                self.added(self.core_out.at[q], [self.own.at[q], self.core_in.at[q], self.left_in.at[q]])

            @pl.when(me == count - 1)
            def _():
                self.added(self.core_out.at[q], [self.own.at[q], self.core_in.at[q]])

            self.back_left(q).start()

        def rightward():
            q = q_right
            self.back_core(q).wait()

            @pl.when(me > 0)
            def _():
                push(self.right_in.at[q], self.right_in.at[q], self.sems[8].at[q], self.sems[11].at[q], self.left()).wait_recv()
                self.added(self.core_out.at[q], [self.own.at[q], self.core_in.at[q], self.right_in.at[q]])

            @pl.when(me == 0)
            def _():
                self.added(self.core_out.at[q], [self.own.at[q], self.core_in.at[q]])

            self.back_right(q).start()

        pl.when((q_left >= 0) & (q_left < me))(leftward)
        pl.when((t >= me) & (q_right > me))(rightward)

    def finish(self, o_ref):
        me, count = self.me, self.count
        self.back_core(me).wait()

        @pl.when(me < count - 1)
        def _():
            push(self.left_in.at[me], self.left_in.at[me], self.sems[7].at[me], self.sems[10].at[me], self.right()).wait_recv()

        @pl.when(me > 0)
        def _():
            push(self.right_in.at[me], self.right_in.at[me], self.sems[8].at[me], self.sems[11].at[me], self.left()).wait_recv()

        base = [self.own.at[me], self.core_in.at[me]]

        @pl.when(me == 0)
        def _():
            self.added(o_ref, base + [self.left_in.at[me]])

        @pl.when(me == count - 1)
        def _():
            self.added(o_ref, base + [self.right_in.at[me]])

        @pl.when((me > 0) & (me < count - 1))
        def _():
            self.added(o_ref, base + [self.left_in.at[me], self.right_in.at[me]])

        @pl.when(me > 0)
        def _():
            self.to_left(me, 0, self.x_ref).wait_send()

        @pl.when(me < count - 1)
        def _():
            self.to_right(me, 0, self.x_ref).wait_send()

        @pl.loop(1, count)
        def _(k):
            @pl.when((me - k >= 0) & (me < count - 1))
            def _():
                self.to_right(me - k, k, self.x_ref).wait_send()

            @pl.when((me + k < count) & (me > 0))
            def _():
                self.to_left(me + k, k, self.x_ref).wait_send()

        @pl.loop(0, count)
        def _(q):
            @pl.when(q < me)
            def _():
                self.back_left(q).wait_send()

            @pl.when(q > me)
            def _():
                self.back_right(q).wait_send()


GELU_ONE = 0.7978845608028654
GELU_TWO = 0.044715


def gelu_of(values_in):
    inner = GELU_ONE * (values_in + GELU_TWO * values_in * values_in * values_in)
    bend = jnp.tanh(inner)
    half = 0.5 * (1.0 + bend)
    slope = half + 0.5 * values_in * (1.0 - bend * bend) * GELU_ONE * (
        1.0 + 3.0 * GELU_TWO * values_in * values_in
    )
    return values_in * half, slope


def ffn_forward(block, gateup, down, items, ident):
    count = lax.axis_size("row")
    share, width = block.shape
    groups, _, _, part = gateup.shape
    hidden = groups * part
    out_cols = down.shape[2] // count
    rows = 2 * share
    bundle = Bundle(items)
    number = bundle.number

    def kernel(x_ref, gw_hbm, dw_hbm, *refs):
        x_refs, refs = refs[:number], refs[number:]
        o_ref, xt_hbm, at_hbm, g_hbm, u_hbm = refs[:5]
        o_refs, scratch = refs[5 : 5 + number], refs[5 + number :]
        flow = Flow(x_ref, *scratch[:6], scratch[6:19])
        gw, dw, xt, at, act, gate, up = scratch[19:26]
        gw_sem, dw_sem, xt_sem, at_sem, g_sem, u_sem = scratch[26:32]
        bundle.bind(x_refs, o_refs, scratch[32:])
        gw_load = pltpu.make_async_copy(gw_hbm, gw, gw_sem)
        dw_load = pltpu.make_async_copy(dw_hbm, dw, dw_sem)
        gw_load.start()
        dw_load.start()
        bundle.greet(False, True)
        flow.start()
        bundle.start()
        gw_load.wait()
        dw_load.wait()

        def stores(source):
            return (
                pltpu.make_async_copy(gate.at[source], g_hbm.at[source], g_sem.at[source]),
                pltpu.make_async_copy(up.at[source], u_hbm.at[source], u_sem.at[source]),
            )

        def body(source):
            here = pl.ds(pl.multiple_of(source * rows, rows), rows)
            x = flow.blocks[source].reshape(rows, width)
            xt[:, here] = x.T

            @pl.loop(0, groups)
            def _(d):
                columns = pl.ds(pl.multiple_of(d * part, part), part)
                g = flat_dot(x, gw[d, 0])
                u = flat_dot(x, gw[d, 1])
                gate[source, :, columns] = g
                up[source, :, columns] = u
                act[:, columns] = (gelu_of(g)[0] * u).astype(LOW)

            for copy in stores(source):
                copy.start()
            at[:, here] = act[...].T
            for d in range(groups):
                out = flat_dot(act[...], dw[d])
                for s in range(count):
                    columns = slice((s * groups + d) * out_cols, (s * groups + d + 1) * out_cols)
                    piece = out[:, s * out_cols : (s + 1) * out_cols]
                    flow.own[source, :, columns] = piece[:share]
                    flow.core_out[source, :, columns] = piece[share:].astype(LOW)

        flow.visit(body, bundle)
        xt_store = pltpu.make_async_copy(xt, xt_hbm, xt_sem)
        at_store = pltpu.make_async_copy(at, at_hbm, at_sem)
        xt_store.start()
        at_store.start()

        @pl.loop(0, count - 1)
        def _(t):
            flow.give_back(t)

        flow.finish(o_ref)
        bundle.finish()
        xt_store.wait()
        at_store.wait()

        @pl.loop(0, count)
        def _(source):
            for copy in stores(source):
                copy.wait()

    dma = pltpu.SemaphoreType.DMA
    buffers, sems = Flow.scratch(count, share, width)
    vmem, anywhere = pl.BlockSpec(memory_space=pltpu.VMEM), pl.BlockSpec(memory_space=pl.ANY)
    tokens = count * rows
    return pl.pallas_call(
        kernel,
        out_shape=[
            jax.ShapeDtypeStruct((share, width), FULL),
            jax.ShapeDtypeStruct((width, tokens), LOW),
            jax.ShapeDtypeStruct((hidden, tokens), LOW),
            jax.ShapeDtypeStruct((count, rows, hidden), FULL),
            jax.ShapeDtypeStruct((count, rows, hidden), FULL),
        ]
        + bundle.shapes,
        in_specs=[vmem, anywhere, anywhere] + bundle.specs,
        out_specs=[vmem] + [anywhere] * 4 + bundle.specs,
        scratch_shapes=buffers
        + sems
        + [
            pltpu.VMEM(gateup.shape, LOW),
            pltpu.VMEM(down.shape, LOW),
            pltpu.VMEM((width, tokens), LOW),
            pltpu.VMEM((hidden, tokens), LOW),
            pltpu.VMEM((rows, hidden), LOW),
            pltpu.VMEM((count, rows, hidden), FULL),
            pltpu.VMEM((count, rows, hidden), FULL),
        ]
        + [dma, dma, dma, dma, dma((count,)), dma((count,))]
        + bundle.scratch,
        compiler_params=params(ident, 60),
        cost_estimate=cost(80),
    )(block, gateup, down, *bundle.sources)


def ffn_backward(block, gateup, down, xt, at, gate, up, items, ident):
    count = lax.axis_size("row")
    share, width = block.shape
    groups, _, _, part = gateup.shape
    hidden = groups * part
    out_cols = down.shape[2] // count
    rows = 2 * share
    tokens = count * rows
    bundle = Bundle(items)
    number = bundle.number

    def kernel(x_ref, gw_hbm, dw_hbm, xt_hbm, at_hbm, g_hbm, u_hbm, *refs):
        x_refs, refs = refs[:number], refs[number:]
        o_ref, dgu_hbm, ddn_hbm = refs[:3]
        o_refs, scratch = refs[3 : 3 + number], refs[3 + number :]
        flow = Flow(x_ref, *scratch[:6], scratch[6:19])
        gw, dw, xt_own, at_own, gate_own, up_own, d_gate, d_up, total, stage, stage_down = scratch[19:30]
        load_sems, g_sem, u_sem, out_sem, down_sem = scratch[30:35]
        bundle.bind(x_refs, o_refs, scratch[35:])
        loads = [
            pltpu.make_async_copy(source, target, load_sems.at[k])
            for k, (source, target) in enumerate(
                [(dw_hbm, dw), (gw_hbm, gw), (xt_hbm, xt_own), (at_hbm, at_own)]
            )
        ]

        def fetches(source):
            return (
                pltpu.make_async_copy(g_hbm.at[source], gate_own.at[source], g_sem.at[source]),
                pltpu.make_async_copy(u_hbm.at[source], up_own.at[source], u_sem.at[source]),
            )

        for load in loads[:2]:
            load.start()

        @pl.loop(0, count)
        def _(source):
            for copy in fetches(source):
                copy.start()

        for load in loads[2:]:
            load.start()
        bundle.greet(False, True)
        flow.start()
        bundle.start()
        loads[0].wait()
        loads[1].wait()

        def columns_of(s, d):
            return pl.ds(pl.multiple_of((s * groups + d) * out_cols, out_cols), out_cols)

        def body(source):
            for copy in fetches(source):
                copy.wait()
            grad = flow.blocks[source].reshape(rows, width)
            d_act = None
            for d in range(groups):
                cut = jnp.concatenate(
                    [
                        grad[:, (s * groups + d) * out_cols : (s * groups + d + 1) * out_cols]
                        for s in range(count)
                    ],
                    axis=1,
                )
                term = against(cut, dw[d])
                d_act = term if d_act is None else d_act + term
            total[:, :hidden] = d_act

            @pl.loop(0, groups)
            def _(d):
                columns = pl.ds(pl.multiple_of(d * part, part), part)
                grad_act = total[:, columns]
                curve, slope = gelu_of(gate_own[source, :, columns])
                d_gate[source, :, columns] = (grad_act * up_own[source, :, columns] * slope).astype(LOW)
                d_up[source, :, columns] = (grad_act * curve).astype(LOW)

            total[...] = jnp.zeros(total.shape, FULL)

            @pl.loop(0, groups)
            def _(d):
                columns = pl.ds(pl.multiple_of(d * part, part), part)
                total[...] += against(d_gate[source, :, columns], gw[d, 0]) + against(
                    d_up[source, :, columns], gw[d, 1]
                )

            flow.own[source] = total[:share]
            flow.core_out[source] = total[share:].astype(LOW)

        flow.visit(body, bundle)
        loads[2].wait()
        loads[3].wait()

        def gateup_store(d, which):
            return pltpu.make_async_copy(stage.at[which], dgu_hbm.at[d, which], out_sem.at[which])

        def down_store(d):
            return pltpu.make_async_copy(stage_down, ddn_hbm.at[d], down_sem)

        def weights(d):
            columns = pl.ds(pl.multiple_of(d * part, part), part)
            for which, grads in ((0, d_gate), (1, d_up)):

                @pl.when(d > 0)
                def _():
                    gateup_store(d - 1, which).wait()

                right = grads[:, :, columns].reshape(tokens, part)

                @pl.loop(0, width // 512)
                def _(k):
                    high = pl.ds(pl.multiple_of(k * 512, 512), 512)
                    stage[which, high] = flat_dot(xt_own[high], right).astype(LOW)

                gateup_store(d, which).start()

            @pl.when(d > 0)
            def _():
                down_store(d - 1).wait()

            right = jnp.concatenate(
                [flow.blocks[:, :, :, columns_of(s, d)].reshape(tokens, out_cols) for s in range(count)],
                axis=1,
            )

            @pl.loop(0, hidden // 256)
            def _(k):
                high = pl.ds(pl.multiple_of(k * 256, 256), 256)
                stage_down[high] = flat_dot(at_own[high], right).astype(LOW)

            down_store(d).start()

        @pl.loop(0, count - 1)
        def _(t):
            flow.give_back(t)
            weights(t)

        weights(groups - 1)
        for which in range(2):
            gateup_store(groups - 1, which).wait()
        down_store(groups - 1).wait()
        flow.finish(o_ref)
        bundle.finish()

    dma = pltpu.SemaphoreType.DMA
    buffers, sems = Flow.scratch(count, share, width)
    vmem, anywhere = pl.BlockSpec(memory_space=pltpu.VMEM), pl.BlockSpec(memory_space=pl.ANY)
    return pl.pallas_call(
        kernel,
        out_shape=[
            jax.ShapeDtypeStruct((share, width), FULL),
            jax.ShapeDtypeStruct(gateup.shape, LOW),
            jax.ShapeDtypeStruct(down.shape, LOW),
        ]
        + bundle.shapes,
        in_specs=[vmem] + [anywhere] * 6 + bundle.specs,
        out_specs=[vmem, anywhere, anywhere] + bundle.specs,
        scratch_shapes=buffers
        + sems
        + [
            pltpu.VMEM(gateup.shape, LOW),
            pltpu.VMEM(down.shape, LOW),
            pltpu.VMEM((width, tokens), LOW),
            pltpu.VMEM((hidden, tokens), LOW),
            pltpu.VMEM((count, rows, hidden), FULL),
            pltpu.VMEM((count, rows, hidden), FULL),
            pltpu.VMEM((count, rows, hidden), LOW),
            pltpu.VMEM((count, rows, hidden), LOW),
            pltpu.VMEM((rows, width), FULL),
            pltpu.VMEM((2, width, part), LOW),
            pltpu.VMEM((hidden, count * out_cols), LOW),
        ]
        + [dma((4,)), dma((count,)), dma((count,)), dma((2,)), dma]
        + bundle.scratch,
        compiler_params=params(ident, 62),
        cost_estimate=cost(90),
    )(block, gateup, down, xt, at, gate, up, *bundle.sources)


def last_sums(small, ident):
    axes = ("col", "row", "dp")
    sizes = [lax.axis_size(axis) for axis in axes]
    high = small.shape[0]

    def kernel(x_ref, o_ref, *refs):
        slots, sends, recvs = (refs[k::3] for k in range(3))
        spots = [lax.axis_index(axis) for axis in axes]
        barrier = pltpu.get_barrier_semaphore()
        for axis, size, me in zip(axes, sizes, spots):
            for k in range(1, size):
                pl.semaphore_signal(
                    barrier, inc=1, device_id={axis: lax.rem(me + k, size)}, device_id_type=MESH
                )
        pl.semaphore_wait(barrier, sum(sizes) - len(sizes))
        for at, (axis, size, me) in enumerate(zip(axes, sizes, spots)):
            buf, send, recv = slots[at], sends[at], recvs[at]
            buf[me] = x_ref[...] if at == 0 else o_ref[...]
            for k in range(1, size):
                push(buf.at[me], buf.at[me], send.at[k], recv.at[k], {axis: lax.rem(me + k, size)}).start()
            for k in range(1, size):
                origin = lax.rem(me + size - k, size)
                push(buf.at[origin], buf.at[origin], send.at[k], recv.at[k], {axis: origin}).wait()
            total = buf[0]
            top = buf[0, high - 8 :]
            for k in range(1, size):
                total = total + buf[k]
                top = jnp.maximum(top, buf[k, high - 8 :])
            o_ref[...] = total
            o_ref[high - 8 :] = top

    dma = pltpu.SemaphoreType.DMA
    vmem = pl.BlockSpec(memory_space=pltpu.VMEM)
    scratch = []
    for size in sizes:
        scratch += [pltpu.VMEM((size,) + small.shape, FULL), dma((size,)), dma((size,))]
    return pl.pallas_call(
        kernel,
        out_shape=jax.ShapeDtypeStruct(small.shape, FULL),
        in_specs=[vmem],
        out_specs=vmem,
        scratch_shapes=scratch,
        compiler_params=params(ident, 16),
        cost_estimate=cost(14),
    )(small)


def adam_all(small, sum_rows, groups):
    high = small.shape[0]
    number = len(groups)
    arrays = [array for group in groups for array in group[:4]]
    cuts = []
    for group in range(number):
        rows, cols = arrays[4 * group].shape
        pieces = max(1, rows * cols // 262144)
        cuts += [(group, piece, rows // pieces) for piece in range(pieces)]

    def kernel(x_ref, *refs):
        sources, refs = refs[: 4 * number], refs[4 * number :]
        info_ref, outs, refs = refs[0], refs[1 : 1 + 3 * number], refs[1 + 3 * number :]
        held, load_sem, store_sem = refs[: 4 * number], refs[4 * number], refs[4 * number + 1]

        def rows_of(at):
            group, piece, rows = cuts[at]
            return pl.ds(piece * rows, rows) if rows < arrays[4 * group].shape[0] else slice(None)

        def load(at, k):
            here, array = rows_of(at), 4 * cuts[at][0] + k
            return pltpu.make_async_copy(
                sources[array].at[here], held[array].at[here], load_sem.at[at, k]
            )

        def store(at, k):
            here, group = rows_of(at), cuts[at][0]
            return pltpu.make_async_copy(
                held[4 * group + (1, 2, 0)[k]].at[here], outs[3 * group + k].at[here], store_sem.at[at, k]
            )

        for at in range(len(cuts)):
            for k in range(4):
                load(at, k).start()
        column, data_at = lax.axis_index("col"), lax.axis_index("dp")
        sums = x_ref[:sum_rows]
        squares = jnp.sum(jnp.sum(sums * sums, axis=1, keepdims=True), axis=0, keepdims=True)
        squares = squares + x_ref[sum_rows : sum_rows + 1, :1]
        norm = jnp.sqrt(squares)
        clip = CLIP / jnp.maximum(norm, CLIP)
        tops = x_ref[high - 1 :]
        lanes = lax.broadcasted_iota(jnp.int32, (1, 128), 1)
        group_size = QUERY_HEADS // KEY_VALUE_HEADS
        info_ref[0:1] = jnp.broadcast_to(norm, (1, 128))
        info_ref[1:2] = LOGIT_CAP / jnp.maximum(tops, LOGIT_CAP)

        def factor(first, count):
            chosen = (lanes >= first) & (lanes < first + count)
            top = jnp.max(jnp.where(chosen, tops, NEGATIVE), axis=1, keepdims=True)
            return jnp.sqrt(LOGIT_CAP / jnp.maximum(top, LOGIT_CAP))

        factors = {
            "query": factor(column * lax.axis_size("dp") + data_at, 1),
            "keyval": jnp.where(
                data_at < KEY_VALUE_HEADS, factor(data_at * group_size, group_size), 1.0
            ),
        }
        for at, (group, piece, rows) in enumerate(cuts):
            rate, decay, kind = groups[group][4:]
            for k in range(4):
                load(at, k).wait()
            w_ref, m_ref, v_ref, g_ref = held[4 * group : 4 * group + 4]
            cols = w_ref.shape[1]
            step = rows if rows % 8 else min(rows, max(16, 32768 // max(cols, 128)))

            def stepped(here):
                new = adamw_step(
                    w_ref[here], m_ref[here], v_ref[here], g_ref[here].astype(FULL) * clip, rate, decay
                )
                m_ref[here], v_ref[here] = new[0], new[1]
                w_ref[here] = new[2] * factors[kind] if kind else new[2]

            if step == rows:
                stepped(rows_of(at))
            else:

                @pl.loop(0, rows // step)
                def _(k):
                    stepped(pl.ds(pl.multiple_of(piece * rows + k * step, step), step))

            for k in range(3):
                store(at, k).start()
        for at in range(len(cuts)):
            for k in range(3):
                store(at, k).wait()

    dma = pltpu.SemaphoreType.DMA
    vmem, anywhere = pl.BlockSpec(memory_space=pltpu.VMEM), pl.BlockSpec(memory_space=pl.ANY)
    outs = [jax.ShapeDtypeStruct(group[0].shape, FULL) for group in groups for _ in range(3)]
    return pl.pallas_call(
        kernel,
        out_shape=[jax.ShapeDtypeStruct((8, 128), FULL)] + outs,
        in_specs=[vmem] + [anywhere] * (4 * number),
        out_specs=[vmem] + [anywhere] * (3 * number),
        scratch_shapes=[pltpu.VMEM(array.shape, array.dtype) for array in arrays]
        + [dma((len(cuts), 4)), dma((len(cuts), 3))],
        compiler_params=pltpu.CompilerParams(vmem_limit_bytes=56 * 2**20),
        cost_estimate=cost(25),
    )(small, *arrays)


def allowed_block(at, high, width, spans):
    key_places = lax.broadcasted_iota(jnp.int32, (high, width), 1)
    query_places = at * high + lax.broadcasted_iota(jnp.int32, (high, width), 0)
    seen = key_places <= query_places
    for piece in range(spans.shape[0] - 1):
        start = spans[piece + 1]
        both = (
            (key_places >= start)
            & (key_places < start + IMG)
            & (query_places >= start)
            & (query_places < start + IMG)
        )
        seen = seen | both
    return seen & (key_places < spans[0])


def softmax_block(block_rows, keys, allowed):
    scores = against(block_rows, keys)
    masked = jnp.where(allowed, scores, NEGATIVE)
    peak_row = jnp.max(masked, axis=-1, keepdims=True)
    raw_weights = jnp.where(allowed, jnp.exp(masked - peak_row), 0.0)
    return raw_weights / jnp.sum(raw_weights, axis=-1, keepdims=True), peak_row


def attention_forward_head(acts, gain, head_w, key_w, value_w, query_gain, key_gain, cos_tab, sin_tab, spans, items, ident):
    tokens, width = acts.shape
    step = 256
    bundle = Bundle(items)
    number = bundle.number

    def kernel(spans_ref, x_ref, gain_ref, qw_ref, kw_ref, vw_ref, qg_ref, kg_ref, cos_ref, sin_ref, *refs):
        x_refs, refs = refs[:number], refs[number:]
        h_ref, scale_ref, qr_ref, kr_ref, vr_ref, q_ref, k_ref, v_ref, o_ref, top_ref = refs[:10]
        o_refs, sems = refs[10 : 10 + number], refs[10 + number :]
        bundle.bind(x_refs, o_refs, sems)
        bundle.greet()
        bundle.start()

        def project(at):
            here = pl.ds(pl.multiple_of(at * step, step), step)
            rows = x_ref[here].astype(FULL)
            scale = lax.rsqrt(jnp.mean(rows * rows, axis=-1, keepdims=True) + EPS)
            scale_ref[here] = jnp.broadcast_to(scale, (step, 128))
            h_ref[here] = (rows * scale * gain_ref[...]).astype(LOW)
            hidden = h_ref[here]
            cos_rows, sin_rows = cos_ref[here], sin_ref[here]
            query = flat_dot(hidden, qw_ref[...])
            qr_ref[here] = query
            q_ref[here] = turn(whole_norm(query, qg_ref[...])[0], cos_rows, sin_rows).astype(LOW)
            key = flat_dot(hidden, kw_ref[...])
            kr_ref[here] = key
            k_ref[here] = turn(whole_norm(key, kg_ref[...])[0], cos_rows, sin_rows).astype(LOW)
            value = flat_dot(hidden, vw_ref[...])
            vr_ref[here] = value
            v_ref[here] = whole_norm(value, 1.0)[0].astype(LOW)

        def attend(at):
            here = pl.ds(pl.multiple_of(at * step, step), step)
            allowed = allowed_block(at, step, tokens, spans_ref)
            probs, peak_row = softmax_block(q_ref[here], k_ref[...], allowed)
            o_ref[here] = flat_dot(probs.astype(LOW), v_ref[...]).astype(LOW)
            top_ref[...] = jnp.maximum(top_ref[...], jnp.max(peak_row))

        top_ref[...] = jnp.full(top_ref.shape, NEGATIVE, FULL)
        pl.loop(0, tokens // step)(project)
        bundle.step(1)
        pl.loop(0, tokens // step)(attend)
        for k in range(2, bundle.sizes[0]):
            bundle.step(k)
        bundle.finish()

    vmem = pl.BlockSpec(memory_space=pltpu.VMEM)
    low = jax.ShapeDtypeStruct((tokens, HEAD_WIDTH), LOW)
    full = jax.ShapeDtypeStruct((tokens, HEAD_WIDTH), FULL)
    return pl.pallas_call(
        kernel,
        out_shape=[
            jax.ShapeDtypeStruct((tokens, width), LOW),
            jax.ShapeDtypeStruct((tokens, 128), FULL),
            full,
            full,
            full,
            low,
            low,
            low,
            low,
            jax.ShapeDtypeStruct((8, 128), FULL),
        ]
        + bundle.shapes,
        in_specs=[pl.BlockSpec(memory_space=pltpu.SMEM)] + [vmem] * 9 + bundle.specs,
        out_specs=[vmem] * 10 + bundle.specs,
        scratch_shapes=bundle.scratch,
        compiler_params=params(ident),
        cost_estimate=cost(40),
    )(spans, acts, gain, head_w, key_w, value_w, query_gain, key_gain, cos_tab, sin_tab, *bundle.sources)


def head_backward(queries, keys, values, grads, spans, items, ident):
    rows = queries.shape[0]
    step = min(256, rows)

    bundle = Bundle(items)
    number = bundle.number

    def kernel(spans_ref, q_ref, k_ref, v_ref, g_ref, *refs):
        x_refs, refs = refs[:number], refs[number:]
        dq_ref, dk_ref, dv_ref = refs[:3]
        bundle.bind(x_refs, refs[3 : 3 + number], refs[3 + number :])
        bundle.greet()
        bundle.start()
        dk_ref[...] = jnp.zeros(dk_ref.shape, FULL)
        dv_ref[...] = jnp.zeros(dv_ref.shape, FULL)

        blocks = rows // step
        ahead = min(blocks, bundle.sizes[0])

        @pl.loop(0, blocks)
        def _(at):
            @pl.when((at > 0) & (at < ahead))
            def _():
                bundle.step(at)

            here = pl.ds(pl.multiple_of(at * step, step), step)
            allowed = allowed_block(at, step, keys.shape[0], spans_ref)
            block_rows, grad_rows = q_ref[here], g_ref[here]
            probs, _ = softmax_block(block_rows, k_ref[...], allowed)
            grad_probs = against(grad_rows, v_ref[...])
            delta_row = jnp.sum(probs * grad_probs, axis=-1, keepdims=True)
            grad_scores = (probs * (grad_probs - delta_row)).astype(LOW)
            dq_ref[here] = flat_dot(grad_scores, k_ref[...])
            dk_ref[...] += inner_rows(grad_scores, block_rows)
            dv_ref[...] += inner_rows(probs.astype(LOW), grad_rows)

        for k in range(ahead, bundle.sizes[0]):
            bundle.step(k)
        bundle.finish()

    vmem = pl.BlockSpec(memory_space=pltpu.VMEM)
    return pl.pallas_call(
        kernel,
        out_shape=[jax.ShapeDtypeStruct(queries.shape, FULL)]
        + [jax.ShapeDtypeStruct(keys.shape, FULL)] * 2
        + bundle.shapes,
        in_specs=[pl.BlockSpec(memory_space=pltpu.SMEM)] + [vmem] * 4 + bundle.specs,
        out_specs=[vmem] * 3 + bundle.specs,
        scratch_shapes=bundle.scratch,
        compiler_params=params(ident),
        cost_estimate=cost(25),
    )(spans, queries, keys, values, grads, *bundle.sources)


def whole_norm(values_in, gain_vec):
    scale = lax.rsqrt(jnp.mean(values_in * values_in, axis=-1, keepdims=True) + EPS)
    return values_in * scale * gain_vec, scale


def whole_norm_backward(values_in, scale, gain_vec, grad_out):
    weighted = grad_out * gain_vec
    inner = jnp.mean(weighted * values_in, axis=-1, keepdims=True)
    return (
        scale * weighted - values_in * (scale * scale * scale) * inner,
        jnp.sum(grad_out * values_in * scale, axis=0),
    )


def turn(values_in, cos_tab, sin_tab):
    half_width = values_in.shape[-1] // 2
    one, two = values_in[:, :half_width], values_in[:, half_width:]
    return jnp.concatenate(
        [one * cos_tab - two * sin_tab, two * cos_tab + one * sin_tab], axis=1
    )


def turn_back(values_in, cos_tab, sin_tab):
    return turn(values_in, cos_tab, -sin_tab)


def line_device(
    activations,
    per_layer,
    cotangent,
    lengths,
    starts,
    w_query,
    m_query,
    v_query,
    key_value_weight,
    key_value_first_moment,
    key_value_second_moment,
    w_attend,
    m_attend,
    v_attend,
    w_gateup,
    m_gateup,
    v_gateup,
    w_down,
    m_down,
    v_down,
    w_left,
    m_left,
    v_left,
    w_right,
    m_right,
    v_right,
    w_pergate,
    m_pergate,
    v_pergate,
    w_perproj,
    m_perproj,
    v_perproj,
    w_gains,
    m_gains,
    v_gains,
    w_heads,
    m_heads,
    v_heads,
):
    rows_n = lax.axis_size("row")
    cols_n = lax.axis_size("col")
    data_n = lax.axis_size("dp")
    me = lax.axis_index("row")
    column = lax.axis_index("col")
    data_at = lax.axis_index("dp")
    half_tok, width_a = activations.shape
    tokens = half_tok * cols_n
    share = half_tok // rows_n
    quarter = tokens // rows_n
    width = width_a * rows_n

    ff_part = w_gateup.shape[2] // rows_n
    out_cols = w_down.shape[1]
    heads_here = data_n
    left_cols, right_rows = w_left.shape[1], w_right.shape[0]
    gate_cols, proj_rows = w_pergate.shape[1], w_perproj.shape[0]

    def columns_of(at, size):
        return pl.ds(pl.multiple_of(at * size, size), size)

    def across(source, by_rows):
        high, wide = source.shape
        if by_rows:
            return Swap(
                source,
                (data_n * high, wide),
                lambda ref, q: ref,
                lambda ref, at: ref.at[columns_of(at, high)],
                "dp",
            )
        return Swap(
            source,
            (high, data_n * wide),
            lambda ref, q: ref,
            lambda ref, at: ref.at[:, columns_of(at, wide)],
            "dp",
        )

    def along(source):
        high, wide = source.shape
        return Line(
            source,
            (cols_n * high, rows_n * wide),
            lambda ref, c, r: ref.at[columns_of(c, high), columns_of(r, wide)],
            True,
        )

    gateup_own, attend_own, qkv_w, left_t, right_w, pergate_t, perproj_w = transfers(
        [
            Swap(
                w_gateup.astype(LOW),
                (2, width, ff_part),
                lambda ref, q: ref.at[:, :, columns_of(q, ff_part)],
                lambda ref, at: ref.at[:, columns_of(at, width_a), :],
            ),
            Swap(
                w_attend.astype(LOW).reshape(rows_n, HEAD_WIDTH, out_cols),
                (HEAD_WIDTH, rows_n * out_cols),
                lambda ref, q: ref.at[q],
                lambda ref, at: ref.at[:, columns_of(at, out_cols)],
            ),
            Swap(
                jnp.concatenate([w_query, key_value_weight], axis=1).astype(LOW),
                (data_n, width_a, 2 * HEAD_WIDTH),
                lambda ref, q: ref,
                lambda ref, at: ref.at[at],
                "dp",
            ),
            across(w_left.T, True),
            across(w_right.astype(LOW), False),
            across(w_pergate.T.astype(LOW), True),
            across(w_perproj.astype(LOW), False),
        ],
        1,
        60,
    )
    gateup_all = lax.all_gather(gateup_own, "dp")
    query_w = qkv_w[:, :, :HEAD_WIDTH]
    kv_w = qkv_w[:, :, HEAD_WIDTH:]
    key_w = lax.dynamic_index_in_dim(kv_w, column, 0, False)
    value_w = lax.dynamic_index_in_dim(kv_w, KEY_VALUE_HEADS + column, 0, False)
    last = pl.ds(HEAD_WIDTH, HEAD_WIDTH)
    whole_acts, whole_key, whole_value, head_w, gains, extras, attend_all = transfers(
        [
            along(activations),
            Line(
                qkv_w,
                (width, HEAD_WIDTH),
                lambda ref, c, r: ref.at[columns_of(r, width_a)],
                False,
                lambda ref, c: ref.at[c, :, last],
            ),
            Line(
                qkv_w,
                (width, HEAD_WIDTH),
                lambda ref, c, r: ref.at[columns_of(r, width_a)],
                False,
                lambda ref, c: ref.at[KEY_VALUE_HEADS + c, :, last],
            ),
            Swap(
                qkv_w,
                (width, HEAD_WIDTH),
                lambda ref, q: ref.at[q, :, pl.ds(0, HEAD_WIDTH)],
                lambda ref, at: ref.at[columns_of(at, width_a)],
            ),
            Line(w_gains, (6, width), lambda ref, c, r: ref.at[:, columns_of(r, width_a)]),
            Line(
                per_layer,
                (tokens, PLD),
                lambda ref, c, r: ref.at[columns_of(r, quarter), columns_of(c, PLD // cols_n)],
                True,
            ),
            Swap(
                attend_own,
                (data_n, HEAD_WIDTH, rows_n * out_cols),
                lambda ref, q: ref,
                lambda ref, at: ref.at[at],
                "dp",
            ),
        ],
        2,
        95,
    )
    attend_w = (
        attend_all.reshape(data_n, HEAD_WIDTH, rows_n, out_cols)
        .transpose(1, 2, 0, 3)
        .reshape(HEAD_WIDTH, width)
    )
    token_at = column * half_tok + me * share
    extras = lax.dynamic_slice_in_dim(extras, token_at, share, 0).astype(FULL)
    length = lax.dynamic_index_in_dim(lengths, data_at, 0, keepdims=True)
    piece_starts = lax.dynamic_index_in_dim(starts, data_at, 0, keepdims=False)
    spans = jnp.concatenate([length, piece_starts])

    query_gain = lax.dynamic_index_in_dim(w_heads, column * rows_n + me, 0, True)
    key_gain = w_heads[QUERY_HEADS:]
    all_cos, all_sin = rope_tables(jnp.arange(tokens, dtype=jnp.int32), HEAD_WIDTH)
    own_cos = lax.dynamic_slice_in_dim(all_cos, me * quarter, quarter, 0)
    own_sin = lax.dynamic_slice_in_dim(all_sin, me * quarter, quarter, 0)
    (
        whole_hidden,
        whole_scale,
        query_raw,
        all_key_raw,
        all_value_raw,
        queries,
        keys,
        values,
        attended,
        top,
        down_own,
        left_t,
        right_w,
    ) = attention_forward_head(
        whole_acts,
        gains[:1],
        head_w,
        whole_key,
        whole_value,
        query_gain,
        key_gain,
        all_cos,
        all_sin,
        spans,
        [
            Swap(
                w_down.astype(LOW).reshape(data_n, rows_n, ff_part, out_cols),
                (data_n, ff_part, rows_n * out_cols),
                lambda ref, q: ref.at[:, q],
                lambda ref, at: ref.at[:, :, columns_of(at, out_cols)],
            ),
            along(left_t.astype(LOW)),
            along(right_w),
        ],
        3,
    )
    down_own, gateup_all = lax.optimization_barrier((down_own, gateup_all))
    down_all = lax.all_gather(down_own, "dp").reshape(data_n, data_n * ff_part, -1)
    inputs = lax.dynamic_slice_in_dim(whole_acts, token_at, share, 0).astype(FULL)
    key_raw = lax.dynamic_slice_in_dim(all_key_raw, me * quarter, quarter, 0)
    value_raw = lax.dynamic_slice_in_dim(all_value_raw, me * quarter, quarter, 0)
    _, query_scale = whole_norm(query_raw, query_gain)
    _, key_scale = whole_norm(key_raw, key_gain)
    _, value_scale = whole_norm(value_raw, 1.0)

    def shares(parts):
        return parts.astype(LOW).reshape(cols_n, rows_n, share, width)

    hidden, _ = whole_norm(inputs, gains[0])
    hidden_low = hidden.astype(LOW)
    middle = against(hidden_low, left_t).astype(LOW)
    right_raw = flat_dot(middle, right_w)
    right_n, scale_r = whole_norm(right_raw, gains[1])
    projected = line_reduce(shares(flat_dot(attended, attend_w)), 5, True, 45)
    proj_n, scale_p = whole_norm(projected, gains[2])
    mixture = ((inputs + proj_n) + (hidden + right_n)) * HALF_ROOT
    ffn_n, scale_f = whole_norm(mixture, gains[3])
    down_raw, spread_ft, act_t, gate_raw, up_raw, upstream, pergate_t, perproj_w = ffn_forward(
        ffn_n.astype(LOW),
        gateup_all,
        down_all,
        [
            Swap(
                cotangent,
                (share, width),
                lambda ref, q: ref.at[columns_of(q, share)],
                lambda ref, at: ref.at[:, columns_of(at, width_a)],
            ),
            along(pergate_t),
            along(perproj_w),
        ],
        6,
    )
    upstream = upstream.astype(FULL)
    down_n, scale_d = whole_norm(down_raw, gains[4])
    block_out = mixture + down_n
    out_low = block_out.astype(LOW)
    pgate = against(out_low, pergate_t)
    pact = (jax.nn.gelu(pgate, approximate=True) * extras).astype(LOW)
    perproj = flat_dot(pact, perproj_w)
    perproj_n, scale_pp = whole_norm(perproj, gains[5])
    result = (block_out + perproj_n).astype(LOW)

    gain_grads = [None] * 6
    d_perproj, gain_grads[5] = whole_norm_backward(perproj, scale_pp, gains[5], upstream)
    d_perproj = d_perproj.astype(LOW)
    dw_perproj = inner_rows(pact, d_perproj)
    d_pact = against(d_perproj, perproj_w)
    _, pullback = jax.vjp(lambda v: jax.nn.gelu(v, approximate=True), pgate)
    (d_pgate,) = pullback(d_pact * extras)
    d_pgate = d_pgate.astype(LOW)
    dw_pergate = inner_rows(d_pgate, out_low)
    d_out = upstream + flat_dot(d_pgate, pergate_t)
    d_down, gain_grads[4] = whole_norm_backward(down_raw, scale_d, gains[4], d_out)
    d_ffn, dw_gateup, dw_down, result = ffn_backward(
        d_down.astype(LOW),
        gateup_all,
        down_all,
        spread_ft,
        act_t,
        gate_raw,
        up_raw,
        [
            Swap(
                result,
                (half_tok, width_a),
                lambda ref, q: ref.at[:, columns_of(q, width_a)],
                lambda ref, at: ref.at[columns_of(at, share)],
            )
        ],
        8,
    )
    g_gateup = lax.psum_scatter(dw_gateup, "dp", scatter_dimension=0)
    d_mix, gain_grads[3] = whole_norm_backward(mixture, scale_f, gains[3], d_ffn)
    d_half = (d_out + d_mix) * HALF_ROOT
    d_proj, gain_grads[2] = whole_norm_backward(projected, scale_p, gains[2], d_half)
    (spread_p,) = transfers(
        [
            Line(
                d_proj.astype(LOW),
                (cols_n, rows_n, share, width),
                lambda ref, c, r: ref.at[c, r],
                True,
            )
        ],
        10,
        40,
    )
    spread_p = spread_p.reshape(tokens, width)
    d_right, gain_grads[1] = whole_norm_backward(right_raw, scale_r, gains[1], d_half)
    d_right = d_right.astype(LOW)
    dw_right = inner_rows(middle, d_right)
    d_middle = against(d_right, right_w).astype(LOW)
    dw_left = inner_rows(d_middle, hidden_low)
    d_hidden_share = d_half + flat_dot(d_middle, left_t)
    inner_share = jnp.sum(d_hidden_share * gains[0] * inputs, axis=1)
    d_attended = against(spread_p, attend_w).astype(LOW)
    dw_attend = inner_rows(attended, spread_p).astype(LOW)
    small_parts = jnp.concatenate(
        [
            grad.astype(LOW).reshape(cols_n, -1, width)
            for grad in (dw_left, dw_right, dw_pergate, dw_perproj)
        ],
        axis=1,
    )
    d_queries, d_keys, d_values, small_parts, half_here, middle_here = head_backward(
        queries,
        keys,
        values,
        d_attended,
        spans,
        [
            Reduce(small_parts),
            Swap(
                d_half.astype(LOW),
                (half_tok, width_a),
                lambda ref, q: ref.at[:, columns_of(q, width_a)],
                lambda ref, at: ref.at[columns_of(at, share)],
            ),
            Line(
                d_middle, (half_tok, d_middle.shape[1]), lambda ref, c, r: ref.at[columns_of(r, share)]
            ),
        ],
        4,
    )

    small_parts = small_parts.astype(LOW)
    d_queries, dw_down, g_gateup = lax.optimization_barrier((d_queries, dw_down, g_gateup))
    g_down = lax.psum_scatter(
        dw_down.reshape(data_n, data_n, ff_part, -1), "dp", scatter_dimension=0
    )
    kv_parts = jnp.concatenate(
        [
            d_keys.astype(LOW).reshape(rows_n, quarter, HEAD_WIDTH),
            d_values.astype(LOW).reshape(rows_n, quarter, HEAD_WIDTH),
        ],
        axis=1,
    )
    d_kv = line_reduce(kv_parts, 11, False, 20)
    d_q_raw, dg_query = whole_norm_backward(
        query_raw, query_scale, query_gain, turn_back(d_queries, all_cos, all_sin)
    )
    d_k_raw, dg_key = whole_norm_backward(
        key_raw, key_scale, key_gain, turn_back(d_kv[:quarter], own_cos, own_sin)
    )
    d_v_raw, _ = whole_norm_backward(value_raw, value_scale, 1.0, d_kv[quarter:])
    d_raw = jnp.concatenate([d_q_raw, d_k_raw, d_v_raw], axis=0).astype(LOW)
    gateup_squares = jnp.sum(jnp.square(g_gateup.astype(FULL)))
    spread_q, g_gateup, g_attend = transfers(
        [
            Line(d_raw, (rows_n,) + d_raw.shape, lambda ref, c, r: ref.at[r]),
            Swap(
                g_gateup,
                w_gateup.shape,
                lambda ref, q: ref.at[:, columns_of(q, width_a), :],
                lambda ref, at: ref.at[:, :, columns_of(at, ff_part)],
            ),
            ShardSum(dw_attend, out_cols),
        ],
        12,
        100,
    )
    d_q_all = spread_q[:, :tokens]
    d_k_all = spread_q[:, tokens : tokens + quarter].reshape(tokens, HEAD_WIDTH)
    d_v_all = spread_q[:, tokens + quarter :].reshape(tokens, HEAD_WIDTH)
    d_hidden = against(d_k_all, key_w) + against(d_v_all, value_w)
    for k in range(heads_here):
        d_hidden = d_hidden + against(d_q_all[k], query_w[k])
    acts = activations.astype(FULL)
    gains_here = lax.dynamic_slice_in_dim(w_gains, 0, 1, 0)[0]
    scale_here = lax.dynamic_slice_in_dim(whole_scale[:, :1], column * half_tok, half_tok, 0)
    own_acts = lax.dynamic_slice_in_dim(whole_acts, me * width_a, width_a, 1).astype(FULL)
    inner = jnp.sum(d_hidden * gains_here * own_acts, axis=1)
    inner = lax.dynamic_update_slice_in_dim(
        inner, lax.dynamic_slice_in_dim(inner, token_at, share, 0) + inner_share, token_at, 0
    ).reshape(-1, 128)

    spread_h = lax.dynamic_slice_in_dim(whole_hidden, me * width_a, width_a, 1)
    dw_query = jnp.stack([inner_rows(spread_h, d_q_all[k]).astype(LOW) for k in range(heads_here)])
    dw_kv = jnp.stack(
        [inner_rows(spread_h, d_k_all).astype(LOW), inner_rows(spread_h, d_v_all).astype(LOW)]
    )
    cuts = []
    start = 0
    for rows, by_rows in (
        (data_n * left_cols, True),
        (right_rows, False),
        (data_n * gate_cols, True),
        (proj_rows, False),
    ):
        cut = small_parts[start : start + rows]
        start += rows
        if by_rows:
            cut = cut.reshape(data_n, -1, width_a)
            cut = [cut[:, :, k * out_cols : (k + 1) * out_cols] for k in range(data_n)]
            cuts.append(jnp.concatenate(cut, axis=1))
        else:
            cuts.append(jnp.stack([cut[:, k * out_cols : (k + 1) * out_cols] for k in range(data_n)]))
    squares = gateup_squares
    for gradient in (g_attend, g_down):
        squares = squares + jnp.sum(jnp.square(gradient.astype(FULL)))
    g_query, g_keyval, flat_grads, g_down, g_attend, d_hidden, inner = shard_total(
        dw_query,
        dw_kv,
        jnp.concatenate(cuts, axis=1),
        [
            Swap(
                g_down,
                (data_n, rows_n, ff_part, out_cols),
                lambda ref, q: ref.at[:, :, columns_of(q, out_cols)],
                lambda ref, at: ref.at[:, at],
            ),
            Swap(
                g_attend,
                (rows_n, HEAD_WIDTH, out_cols),
                lambda ref, q: ref.at[:, columns_of(q, out_cols)],
                lambda ref, at: ref.at[at],
            ),
            Pair(d_hidden.astype(LOW).reshape(cols_n, half_tok, width_a)),
            Line(inner, (cols_n, rows_n) + inner.shape, lambda ref, c, r: ref.at[c, r], True),
        ],
        13,
    )
    squares = squares + jnp.where(column == 0, jnp.sum(g_keyval * g_keyval), 0.0)
    squares = squares + jnp.sum(g_query * g_query) + jnp.sum(flat_grads * flat_grads)
    g_down = g_down.reshape(w_down.shape)
    g_attend = g_attend.reshape(w_attend.shape)
    small_grads = []
    start = 0
    for w, by_rows in ((w_left, True), (w_right, False), (w_pergate, True), (w_perproj, False)):
        rows = w.size // out_cols
        cut = flat_grads[start : start + rows]
        start += rows
        if by_rows:
            high = rows // data_n
            cut = [cut[k * high : (k + 1) * high] for k in range(data_n)]
            cut = jnp.concatenate(cut, axis=1).T
        small_grads.append(cut)
    g_left, g_right, g_pergate, g_perproj = small_grads

    inner = jnp.sum(inner, axis=(0, 1)).reshape(cols_n, half_tok) / MODEL_WIDTH
    inner = lax.dynamic_index_in_dim(inner, column, 0, False)[:, None]
    half_here = half_here.astype(FULL)
    own_left = lax.dynamic_slice_in_dim(left_t, me * width_a, width_a, 1)
    d_hidden = d_hidden[0].astype(FULL) + d_hidden[1].astype(FULL) + half_here
    d_hidden = d_hidden + flat_dot(middle_here, own_left)
    grad_input = (
        half_here
        + scale_here * d_hidden * gains_here
        - acts * (scale_here * scale_here * scale_here) * inner
    ).astype(LOW)
    gain_zero = jnp.sum(d_hidden * acts * scale_here, axis=0)

    gain_full = jnp.stack(
        [
            lax.dynamic_update_slice_in_dim(
                jnp.zeros((width,), FULL), gain_zero, me * width_a, 0
            )
        ]
        + gain_grads[1:]
    )
    head_full = lax.dynamic_update_slice_in_dim(
        jnp.zeros((QUERY_HEADS + 1, HEAD_WIDTH), FULL), dg_query[None], column * rows_n + me, 0
    )
    head_full = head_full.at[QUERY_HEADS].add(dg_key)
    logit_row = lax.dynamic_update_slice_in_dim(
        jnp.full((128,), NEGATIVE, FULL), top[0, :1], column * rows_n + me, 0
    )
    gain_rows = gain_full.size // 128
    head_rows = head_full.size // 128
    pad_rows = -(gain_rows + head_rows) % 8
    small = jnp.concatenate(
        [
            gain_full.reshape(-1, 128),
            head_full.reshape(-1, 128),
            jnp.broadcast_to(squares, (pad_rows, 128)),
            jnp.broadcast_to(logit_row[None], (8, 128)),
        ]
    )
    small = last_sums(small, 15)
    gain_sum = small[:gain_rows].reshape(6, width)
    head_sum = small[gain_rows : gain_rows + head_rows].reshape(QUERY_HEADS + 1, HEAD_WIDTH)
    g_gains = lax.dynamic_slice_in_dim(gain_sum, me * width_a, width_a, 1)
    matrix_rate = MODEL_WIDTH ** (-0.5)

    def flat_rows_of(array):
        return array.reshape(-1, array.shape[-1])

    def kept(array):
        return array

    def turned(array):
        return array.T

    groups = [
        tuple(change(array) for array in arrays) + rest
        for arrays, change, rest in (
            ((w_gateup, m_gateup, v_gateup, g_gateup), flat_rows_of, (matrix_rate, DECAY, None)),
            ((w_down, m_down, v_down, g_down), kept, (FF ** (-0.5), DECAY, None)),
            ((w_query, m_query, v_query, g_query), kept, (matrix_rate, DECAY, "query")),
            (
                (key_value_weight, key_value_first_moment, key_value_second_moment, g_keyval),
                kept,
                (matrix_rate, DECAY, "keyval"),
            ),
            (
                (w_attend, m_attend, v_attend, g_attend),
                kept,
                ((QUERY_HEADS * HEAD_WIDTH) ** (-0.5), DECAY, None),
            ),
            ((w_left, m_left, v_left, g_left), turned, (matrix_rate, DECAY, None)),
            ((w_right, m_right, v_right, g_right), kept, (RANK ** (-0.5), DECAY, None)),
            ((w_pergate, m_pergate, v_pergate, g_pergate), turned, (matrix_rate, DECAY, None)),
            ((w_perproj, m_perproj, v_perproj, g_perproj), kept, (PLD ** (-0.5), DECAY, None)),
            ((w_gains, m_gains, v_gains, g_gains), kept, (GAIN_RATE, 0.0, None)),
            ((w_heads, m_heads, v_heads, head_sum), kept, (HEAD_RATE, 0.0, None)),
        )
    ]
    info, *stepped = adam_all(small, gain_rows + head_rows, groups)
    grad_norm = info[0, 0]
    scale_factors = info[1, :QUERY_HEADS]
    gateup, down, query, keyval, attend, left, right, pergate, perproj, gain, head = (
        stepped[3 * k : 3 * k + 3] for k in range(11)
    )
    gateup = [array.reshape(w_gateup.shape) for array in gateup]
    left = [array.T for array in left]
    pergate = [array.T for array in pergate]
    return (
        result,
        grad_input,
        grad_norm,
        scale_factors,
        *query,
        *keyval,
        *attend,
        *gateup,
        *down,
        *left,
        *right,
        *pergate,
        *perproj,
        *gain,
        *head,
    )


def per_device(
    activations,
    per_layer,
    cotangent,
    lengths,
    starts,
    w_query,
    m_query,
    v_query,
    key_value_weight,
    key_value_first_moment,
    key_value_second_moment,
    w_attend,
    m_attend,
    v_attend,
    w_gateup,
    m_gateup,
    v_gateup,
    w_down,
    m_down,
    v_down,
    w_left,
    m_left,
    v_left,
    w_right,
    m_right,
    v_right,
    w_pergate,
    m_pergate,
    v_pergate,
    w_perproj,
    m_perproj,
    v_perproj,
    w_gains,
    m_gains,
    v_gains,
    w_heads,
    m_heads,
    v_heads,
):
    row_devs = lax.axis_size("row")
    col_devs = lax.axis_size("col")
    data_devs = lax.axis_size("dp")
    row_place = lax.axis_index("row")
    column_place = lax.axis_index("col")
    data_at = lax.axis_index("dp")
    bf16 = jnp.bfloat16
    single_float = jnp.float32
    query_b, keyval_b, attend_b, gateup_b, down_b, left_b, right_b, pergate_b, perproj_b = (
        lax.all_gather(w_query.astype(bf16), "dp", axis=1, tiled=True),
        lax.all_gather(key_value_weight.astype(bf16), "dp", axis=1, tiled=True),
        lax.all_gather(w_attend.astype(bf16), "dp", axis=1, tiled=True),
        lax.all_gather(w_gateup.astype(bf16), "dp", axis=2, tiled=True),
        lax.all_gather(w_down.astype(bf16), "dp", axis=1, tiled=True),
        lax.all_gather(w_left.astype(bf16), "dp", axis=1, tiled=True),
        lax.all_gather(w_right.astype(bf16), "dp", axis=1, tiled=True),
        lax.all_gather(w_pergate.astype(bf16), "dp", axis=1, tiled=True),
        lax.all_gather(w_perproj.astype(bf16), "dp", axis=1, tiled=True),
    )
    inputs = activations.astype(single_float)
    tok_a, width_a = inputs.shape
    grouped_rows = tok_a * col_devs
    token_batch = grouped_rows // row_devs
    q_cols = query_b.shape[1]
    l_cols = left_b.shape[1]
    kv_cols = keyval_b.shape[1]
    ff_here = gateup_b.shape[2]
    local_heads = q_cols // HEAD_WIDTH
    length = lax.dynamic_index_in_dim(lengths, data_at, 0, keepdims=False)
    piece_starts = lax.dynamic_index_in_dim(starts, data_at, 0, keepdims=False)
    own_places = row_place * token_batch + jnp.arange(token_batch, dtype=jnp.int32)
    all_places = jnp.arange(grouped_rows, dtype=jnp.int32)
    own_cos, own_sin = rope_tables(own_places, HEAD_WIDTH)
    query_gains = lax.dynamic_slice_in_dim(w_heads, column_place * local_heads, local_heads, 0)
    key_gain = w_heads[QUERY_HEADS]
    hidden, scale_in = norm_forward(inputs, w_gains[0])
    hidden_b = hidden.astype(bf16)
    spread_h = spread_col(hidden_b)
    type_one = reduce_row(flat_dot(spread_h, jnp.concatenate([query_b, left_b], axis=1)))
    key_raw_all = lax.psum(flat_dot(spread_h, keyval_b), "row")
    all_cos, all_sin = rope_tables(all_places, HEAD_WIDTH)
    key_value_whole = key_form(key_raw_all, key_gain, all_cos, all_sin).astype(bf16)
    key_raw = lax.dynamic_slice_in_dim(key_raw_all, row_place * token_batch, token_batch, 0)
    query_raw = type_one[:, :q_cols]
    middle_b = type_one[:, q_cols : q_cols + l_cols].astype(bf16)
    queries = query_form(query_raw, query_gains, own_cos, own_sin).astype(bf16)
    key_value_heads = (column_place * local_heads + jnp.arange(local_heads, dtype=jnp.int32)) // (
        QUERY_HEADS // KEY_VALUE_HEADS
    )
    every_key = key_value_whole[:, : KEY_VALUE_HEADS * HEAD_WIDTH].reshape(
        grouped_rows, KEY_VALUE_HEADS, HEAD_WIDTH
    )
    every_value = key_value_whole[:, KEY_VALUE_HEADS * HEAD_WIDTH :].reshape(
        grouped_rows, KEY_VALUE_HEADS, HEAD_WIDTH
    )
    key_sel = jnp.take(every_key, key_value_heads, axis=1)
    value_sel = jnp.take(every_value, key_value_heads, axis=1)
    attended, block_peaks, block_totals = attention_forward(
        queries, key_sel, value_sel, own_places, all_places, length, piece_starts
    )
    attended_b = attended.reshape(token_batch, q_cols).astype(bf16)
    joined_b = jnp.concatenate([attended_b, middle_b], axis=1)
    spread_j = spread_row(joined_b)
    type_two = reduce_col(
        jnp.concatenate(
            [flat_dot(spread_j[:, :q_cols], attend_b), flat_dot(spread_j[:, q_cols:], right_b)],
            axis=1,
        )
    )
    projected = type_two[:, :width_a]
    right_raw = type_two[:, width_a:]
    right_n, scale_r = norm_forward(right_raw, w_gains[1])
    laurel = hidden + right_n
    proj_n, scale_p = norm_forward(projected, w_gains[2])
    gated_sum = inputs + proj_n
    mixture = (gated_sum + laurel) * HALF_ROOT
    ffn_n, scale_f = norm_forward(mixture, w_gains[3])
    ffn_b = ffn_n.astype(bf16)
    spread_f = spread_col(ffn_b)
    gateup_pair = jnp.concatenate([gateup_b[0], gateup_b[1]], axis=1)
    gate_up = reduce_row(flat_dot(spread_f, gateup_pair))
    gate_raw = gate_up[:, :ff_here]
    up_raw = gate_up[:, ff_here:]
    act_b = (jax.nn.gelu(gate_raw, approximate=True) * up_raw).astype(bf16)
    spread_a = spread_row(act_b)
    down_raw = reduce_col(flat_dot(spread_a, down_b))
    down_n, scale_d = norm_forward(down_raw, w_gains[4])
    block_out = mixture + down_n
    out_b = block_out.astype(bf16)
    spread_o = spread_col(out_b)
    pgate = reduce_row(flat_dot(spread_o, pergate_b))
    extras = per_layer.astype(single_float)
    pact_b = (jax.nn.gelu(pgate, approximate=True) * extras).astype(bf16)
    spread_p = spread_row(pact_b)
    perproj = reduce_col(flat_dot(spread_p, perproj_b))
    perproj_n, scale_pp = norm_forward(perproj, w_gains[5])
    result = (block_out + perproj_n).astype(bf16)
    upstream = cotangent.astype(single_float)
    gain_grads = [None, None, None, None, None, None]
    d_perproj, gain_grads[5] = norm_backward(perproj, scale_pp, w_gains[5], upstream)
    grads_five = grads_col(d_perproj.astype(bf16))
    dw_perproj = inner_rows(spread_p, grads_five)
    d_pact = reduce_row(against(grads_five, perproj_b))
    gelu_out, pullback = jax.vjp(lambda v: jax.nn.gelu(v, approximate=True), pgate)
    (d_pgate,) = pullback(d_pact * extras)
    grads_four = grads_row(d_pgate.astype(bf16))
    dw_pergate = inner_rows(spread_o, grads_four)
    d_out = upstream + reduce_col(against(grads_four, pergate_b))
    d_down, gain_grads[4] = norm_backward(down_raw, scale_d, w_gains[4], d_out)
    grads_three = grads_col(d_down.astype(bf16))
    dw_down = inner_rows(spread_a, grads_three)
    d_act = reduce_row(against(grads_three, down_b))
    act_out, pullback = jax.vjp(lambda a, b: jax.nn.gelu(a, approximate=True) * b, gate_raw, up_raw)
    d_gate, d_up = pullback(d_act)
    local_two = jnp.concatenate([d_gate, d_up], axis=1).astype(bf16)
    grads_two = grads_row(local_two)
    dw_gateup = jnp.stack(
        [inner_rows(spread_f, grads_two[:, :ff_here]), inner_rows(spread_f, grads_two[:, ff_here:])]
    )
    d_ffn = reduce_col(
        against(grads_two[:, :ff_here], gateup_b[0]) + against(grads_two[:, ff_here:], gateup_b[1])
    )
    d_mix_norm, gain_grads[3] = norm_backward(mixture, scale_f, w_gains[3], d_ffn)
    d_half = (d_out + d_mix_norm) * HALF_ROOT
    d_proj, gain_grads[2] = norm_backward(projected, scale_p, w_gains[2], d_half)
    d_right, gain_grads[1] = norm_backward(right_raw, scale_r, w_gains[1], d_half)
    grads_one = grads_col(jnp.concatenate([d_proj, d_right], axis=1).astype(bf16))
    dw_attend = inner_rows(spread_j[:, :q_cols], grads_one[:, :width_a])
    dw_right = inner_rows(spread_j[:, q_cols:], grads_one[:, width_a:])
    d_joined = reduce_row(
        jnp.concatenate(
            [against(grads_one[:, :width_a], attend_b), against(grads_one[:, width_a:], right_b)],
            axis=1,
        )
    )
    d_attended = d_joined[:, :q_cols].astype(bf16).reshape(token_batch, local_heads, HEAD_WIDTH)
    d_middle = d_joined[:, q_cols:]
    d_queries, d_key_sel, d_value_sel = attention_backward(
        queries,
        key_sel,
        value_sel,
        d_attended,
        block_peaks,
        block_totals,
        own_places,
        all_places,
        length,
        piece_starts,
    )
    single_hot_mask = (
        key_value_heads[:, None] == jnp.arange(KEY_VALUE_HEADS, dtype=jnp.int32)[None, :]
    ).astype(single_float)
    key_gradient = jnp.sum(d_key_sel[:, :, None, :] * single_hot_mask[None, :, :, None], axis=1)
    value_gradient = jnp.sum(d_value_sel[:, :, None, :] * single_hot_mask[None, :, :, None], axis=1)
    key_gradient, value_gradient = lax.psum((key_gradient, value_gradient), ("row", "col"))
    local_key_gradient = lax.dynamic_slice_in_dim(
        key_gradient, row_place * token_batch, token_batch, 0
    ).reshape(token_batch, KEY_VALUE_HEADS * HEAD_WIDTH)
    local_value_gradient = lax.dynamic_slice_in_dim(
        value_gradient, row_place * token_batch, token_batch, 0
    ).reshape(token_batch, KEY_VALUE_HEADS * HEAD_WIDTH)
    query_out, pullback = jax.vjp(
        lambda r, g: query_form(r, g, own_cos, own_sin), query_raw, query_gains
    )
    d_query_raw, dg_query = pullback(d_queries)
    key_tile = jnp.broadcast_to(key_gain, (token_batch, 1, HEAD_WIDTH))
    key_out, pullback = jax.vjp(lambda r, g: key_form(r, g, own_cos, own_sin), key_raw, key_tile)
    d_key_raw, dg_key_rows = pullback(
        jnp.concatenate([local_key_gradient, local_value_gradient], axis=1)
    )
    slice_rows = token_batch // col_devs
    dg_key = jnp.sum(
        lax.dynamic_slice_in_dim(dg_key_rows, column_place * slice_rows, slice_rows, 0), axis=(0, 1)
    )
    grads_zero = grads_row(jnp.concatenate([d_query_raw, d_middle, d_key_raw], axis=1).astype(bf16))
    dw_query = inner_rows(spread_h, grads_zero[:, :q_cols])
    dw_left = inner_rows(spread_h, grads_zero[:, q_cols : q_cols + l_cols])
    key_grad_rows = grads_zero[:, q_cols + l_cols :]
    dw_keyval = inner_rows(spread_h, key_grad_rows)
    slab_width = kv_cols // col_devs
    d_hidden = reduce_col(
        against(grads_zero[:, :q_cols], query_b)
        + against(grads_zero[:, q_cols : q_cols + l_cols], left_b)
        + against(
            lax.dynamic_slice_in_dim(key_grad_rows, column_place * slab_width, slab_width, 1),
            lax.dynamic_slice_in_dim(keyval_b, column_place * slab_width, slab_width, 1),
        )
    )
    d_in, gain_grads[0] = norm_backward(inputs, scale_in, w_gains[0], d_hidden + d_half)
    grad_input = (d_half + d_in).astype(bf16)
    g_query, g_keyval, g_attend, g_gateup, g_down, g_left, g_right, g_pergate, g_perproj = (
        lax.psum_scatter(dw_query, "dp", scatter_dimension=1, tiled=True),
        lax.psum_scatter(dw_keyval, "dp", scatter_dimension=1, tiled=True),
        lax.psum_scatter(dw_attend, "dp", scatter_dimension=1, tiled=True),
        lax.psum_scatter(dw_gateup, "dp", scatter_dimension=2, tiled=True),
        lax.psum_scatter(dw_down, "dp", scatter_dimension=1, tiled=True),
        lax.psum_scatter(dw_left, "dp", scatter_dimension=1, tiled=True),
        lax.psum_scatter(dw_right, "dp", scatter_dimension=1, tiled=True),
        lax.psum_scatter(dw_pergate, "dp", scatter_dimension=1, tiled=True),
        lax.psum_scatter(dw_perproj, "dp", scatter_dimension=1, tiled=True),
    )
    gain_full = lax.dynamic_update_slice_in_dim(
        jnp.zeros((6, MODEL_WIDTH), single_float), jnp.stack(gain_grads), row_place * width_a, 1
    )
    head_full = lax.dynamic_update_slice_in_dim(
        jnp.zeros((QUERY_HEADS + 1, HEAD_WIDTH), single_float),
        dg_query,
        column_place * local_heads,
        0,
    )
    head_full = head_full.at[QUERY_HEADS].add(dg_key)
    logit_here = lax.dynamic_update_slice_in_dim(
        jnp.full((QUERY_HEADS,), NEGATIVE, single_float),
        jnp.max(block_peaks, axis=(0, 2)),
        column_place * local_heads,
        0,
    )

    def combine(left_part, right_part):
        return (
            left_part[0] + right_part[0],
            left_part[1] + right_part[1],
            jnp.maximum(left_part[2], right_part[2]),
        )

    gain_sum, head_sum, logit_top = joined(
        (gain_full, head_full, logit_here), ("dp", "row", "col"), combine
    )
    g_gains = lax.dynamic_slice_in_dim(gain_sum, row_place * width_a, width_a, 1)
    lead_device = (column_place == 0) & (data_at == 0)
    solo_device = lead_device & (row_place == 0)
    squares = jnp.float32(0.0)
    for gradient in (g_query, g_attend, g_gateup, g_down, g_left, g_right, g_pergate, g_perproj):
        squares = squares + jnp.sum(gradient * gradient)
    squares = squares + jnp.where(column_place == 0, jnp.sum(g_keyval * g_keyval), 0.0)
    squares = squares + jnp.where(lead_device, jnp.sum(g_gains * g_gains), 0.0)
    squares = squares + jnp.where(solo_device, jnp.sum(head_sum * head_sum), 0.0)
    grad_norm = jnp.sqrt(lax.psum(squares, ("dp", "row", "col")))
    clip_scale = CLIP / jnp.maximum(grad_norm, CLIP)
    scale_factors = LOGIT_CAP / jnp.maximum(logit_top, LOGIT_CAP)
    weights = (
        w_query,
        key_value_weight,
        w_attend,
        w_gateup,
        w_down,
        w_left,
        w_right,
        w_pergate,
        w_perproj,
        w_gains,
        w_heads,
    )
    moments = (
        m_query,
        key_value_first_moment,
        m_attend,
        m_gateup,
        m_down,
        m_left,
        m_right,
        m_pergate,
        m_perproj,
        m_gains,
        m_heads,
    )
    seconds = (
        v_query,
        key_value_second_moment,
        v_attend,
        v_gateup,
        v_down,
        v_left,
        v_right,
        v_pergate,
        v_perproj,
        v_gains,
        v_heads,
    )
    gradients = (
        g_query,
        g_keyval,
        g_attend,
        g_gateup,
        g_down,
        g_left,
        g_right,
        g_pergate,
        g_perproj,
        g_gains,
        head_sum,
    )
    step_rates = (
        MODEL_WIDTH ** (-0.5),
        MODEL_WIDTH ** (-0.5),
        (QUERY_HEADS * HEAD_WIDTH) ** (-0.5),
        MODEL_WIDTH ** (-0.5),
        FF ** (-0.5),
        MODEL_WIDTH ** (-0.5),
        RANK ** (-0.5),
        MODEL_WIDTH ** (-0.5),
        PLD ** (-0.5),
        GAIN_RATE,
        HEAD_RATE,
    )
    decays = (DECAY, DECAY, DECAY, DECAY, DECAY, DECAY, DECAY, DECAY, DECAY, 0.0, 0.0)
    updated = [
        adamw_step(
            weights[k], moments[k], seconds[k], gradients[k] * clip_scale, step_rates[k], decays[k]
        )
        for k in range(11)
    ]
    head_scale = jnp.sqrt(scale_factors)
    q_width = w_query.shape[1]
    q_head = (
        (column_place * data_devs + data_at) * q_width + jnp.arange(q_width, dtype=jnp.int32)
    ) // HEAD_WIDTH
    q_factor = jnp.sum(
        jnp.where(
            q_head[:, None] == jnp.arange(QUERY_HEADS, dtype=jnp.int32)[None, :],
            head_scale[None, :],
            0.0,
        ),
        axis=1,
    )
    new_query = updated[0][2] * q_factor[None, :]
    kv_width = key_value_weight.shape[1]
    key_value_index = data_at * kv_width + jnp.arange(kv_width, dtype=jnp.int32)
    key_value_scale = jnp.sqrt(
        jnp.min(scale_factors.reshape(KEY_VALUE_HEADS, QUERY_HEADS // KEY_VALUE_HEADS), axis=1)
    )
    key_value_choice = jnp.sum(
        jnp.where(
            (key_value_index // HEAD_WIDTH)[:, None]
            == jnp.arange(KEY_VALUE_HEADS, dtype=jnp.int32)[None, :],
            key_value_scale[None, :],
            0.0,
        ),
        axis=1,
    )
    key_value_factor = jnp.where(
        key_value_index < KEY_VALUE_HEADS * HEAD_WIDTH, key_value_choice, 1.0
    )
    new_keyval = updated[1][2] * key_value_factor[None, :]
    return (
        result,
        grad_input,
        grad_norm,
        scale_factors,
        updated[0][0],
        updated[0][1],
        new_query,
        updated[1][0],
        updated[1][1],
        new_keyval,
        updated[2][0],
        updated[2][1],
        updated[2][2],
        updated[3][0],
        updated[3][1],
        updated[3][2],
        updated[4][0],
        updated[4][1],
        updated[4][2],
        updated[5][0],
        updated[5][1],
        updated[5][2],
        updated[6][0],
        updated[6][1],
        updated[6][2],
        updated[7][0],
        updated[7][1],
        updated[7][2],
        updated[8][0],
        updated[8][1],
        updated[8][2],
        updated[9][0],
        updated[9][1],
        updated[9][2],
        updated[10][0],
        updated[10][1],
        updated[10][2],
    )


def solution(mesh):
    placed = (
        P(("dp", "col"), "row"),
        P(("dp", "row"), "col"),
        P(("dp", "col"), "row"),
        P(),
        P(),
        P("row", ("col", "dp")),
        P("row", ("col", "dp")),
        P("row", ("col", "dp")),
        P("row", "dp"),
        P("row", "dp"),
        P("row", "dp"),
        P("col", ("row", "dp")),
        P("col", ("row", "dp")),
        P("col", ("row", "dp")),
        P(None, "row", ("col", "dp")),
        P(None, "row", ("col", "dp")),
        P(None, "row", ("col", "dp")),
        P("col", ("row", "dp")),
        P("col", ("row", "dp")),
        P("col", ("row", "dp")),
        P("row", ("col", "dp")),
        P("row", ("col", "dp")),
        P("row", ("col", "dp")),
        P("col", ("row", "dp")),
        P("col", ("row", "dp")),
        P("col", ("row", "dp")),
        P("row", ("col", "dp")),
        P("row", ("col", "dp")),
        P("row", ("col", "dp")),
        P("col", ("row", "dp")),
        P("col", ("row", "dp")),
        P("col", ("row", "dp")),
        P(None, "row"),
        P(None, "row"),
        P(None, "row"),
        P(),
        P(),
        P(),
    )
    fits = (
        mesh.shape["col"] == KEY_VALUE_HEADS
        and mesh.shape["row"] * KEY_VALUE_HEADS == QUERY_HEADS
        and mesh.shape["dp"] == mesh.shape["row"]
    )
    return jax.shard_map(
        line_device if fits else per_device,
        mesh=mesh,
        in_specs=placed,
        out_specs=(
            P(("dp", "col"), "row"),
            P(("dp", "col"), "row"),
            P(),
            P(),
            P("row", ("col", "dp")),
            P("row", ("col", "dp")),
            P("row", ("col", "dp")),
            P("row", "dp"),
            P("row", "dp"),
            P("row", "dp"),
            P("col", ("row", "dp")),
            P("col", ("row", "dp")),
            P("col", ("row", "dp")),
            P(None, "row", ("col", "dp")),
            P(None, "row", ("col", "dp")),
            P(None, "row", ("col", "dp")),
            P("col", ("row", "dp")),
            P("col", ("row", "dp")),
            P("col", ("row", "dp")),
            P("row", ("col", "dp")),
            P("row", ("col", "dp")),
            P("row", ("col", "dp")),
            P("col", ("row", "dp")),
            P("col", ("row", "dp")),
            P("col", ("row", "dp")),
            P("row", ("col", "dp")),
            P("row", ("col", "dp")),
            P("row", ("col", "dp")),
            P("col", ("row", "dp")),
            P("col", ("row", "dp")),
            P("col", ("row", "dp")),
            P(None, "row"),
            P(None, "row"),
            P(None, "row"),
            P(),
            P(),
            P(),
        ),
        check_vma=False,
    )
```

```python
import jax
import jax.numpy as jnp
from jax import lax
from jax.experimental import pallas as pl
from jax.experimental.pallas import tpu as pltpu
from jax.sharding import PartitionSpec as P

MODEL_WIDTH = 2048
QUERY_HEADS = 8
KEY_VALUE_HEADS = 2
HEAD_WIDTH = 256
FF = 8192
RANK = 64
PLD = 256
IMG = 256
STEP = 10


EPS = 1e-06
ROPE_BASE = 1000000.0
BETA_ONE = 0.5
BETA_TWO = 0.5
ADAM_EPS = 1e-08
DECAY = 0.01
CLIP = 1.0
LOGIT_CAP = 4.0
GAIN_RATE = 0.6
HEAD_RATE = 0.1
HALF_ROOT = 0.7071067811865476
NEGATIVE = -1e30


def joined(part, axis, combine):
    gathered = jax.tree.map(lambda a: lax.all_gather(a, axis), part)

    def take(source):
        return jax.tree.map(lambda a: lax.dynamic_index_in_dim(a, source, 0, False), gathered)

    return lax.fori_loop(
        1, lax.axis_size(axis), lambda source, state: combine(state, take(source)), take(0)
    )


def row_total(values_in):
    return lax.psum(values_in, "row")


def spread_col(values_in):
    return lax.all_gather(values_in, "col", axis=0, tiled=True)


def reduce_row(values_in):
    return lax.psum_scatter(values_in, "row", scatter_dimension=0, tiled=True)


def spread_row(values_in):
    return lax.all_gather(values_in, "row", axis=0, tiled=True)


def reduce_col(values_in):
    return lax.psum_scatter(values_in, "col", scatter_dimension=0, tiled=True)


def grads_col(values_in):
    return lax.all_gather(values_in, "col", axis=0, tiled=True)


def grads_row(values_in):
    return lax.all_gather(values_in, "row", axis=0, tiled=True)


def inner_rows(left_mat, right_mat):
    return lax.dot_general(
        left_mat, right_mat, (((0,), (0,)), ((), ())), preferred_element_type=jnp.float32
    )


def against(grad_mat, weight_mat):
    return lax.dot_general(
        grad_mat, weight_mat, (((1,), (1,)), ((), ())), preferred_element_type=jnp.float32
    )


def flat_dot(left_mat, right_mat):
    return jnp.dot(left_mat, right_mat, preferred_element_type=jnp.float32)


def norm_forward(values_in, gain_vec):
    total_sq = row_total(jnp.sum(values_in * values_in, axis=-1, keepdims=True))
    norm_scale = lax.rsqrt(total_sq / MODEL_WIDTH + EPS)
    return (values_in * norm_scale * gain_vec, norm_scale)


def norm_backward(values_in, norm_scale, gain_vec, grad_out):
    weighted = grad_out * gain_vec
    inner_sum = row_total(jnp.sum(weighted * values_in, axis=-1, keepdims=True))
    grad_in = norm_scale * weighted - values_in * (norm_scale * norm_scale * norm_scale) * (
        inner_sum / MODEL_WIDTH
    )
    return (grad_in, jnp.sum(grad_out * values_in * norm_scale, axis=0))


def norm_rows(values_in, gain_vec):
    return (
        values_in
        * lax.rsqrt(jnp.mean(values_in * values_in, axis=-1, keepdims=True) + EPS)
        * gain_vec
    )


def rope_tables(places, feat_width):
    half_width = feat_width // 2
    powers = jnp.arange(half_width, dtype=jnp.int32).astype(jnp.float32) * (2.0 / feat_width)
    frequency = jnp.power(jnp.float32(ROPE_BASE), -powers)
    angles = places.astype(jnp.float32)[:, None] * frequency[None, :]
    return (jnp.cos(angles), jnp.sin(angles))


def rotate(values_in, cos_tab, sin_tab):
    half_width = values_in.shape[-1] // 2
    part_one = values_in[..., :half_width]
    part_two = values_in[..., half_width:]
    cos_row = cos_tab[:, None, :]
    sin_row = sin_tab[:, None, :]
    return jnp.concatenate(
        [part_one * cos_row - part_two * sin_row, part_two * cos_row + part_one * sin_row], axis=-1
    )


def query_form(unscaled_rows, gain_rows, cos_tab, sin_tab):
    shaped = unscaled_rows.reshape(unscaled_rows.shape[0], gain_rows.shape[0], HEAD_WIDTH)
    return rotate(norm_rows(shaped, gain_rows[None]), cos_tab, sin_tab)


def key_form(unscaled_rows, gain_vec, cos_tab, sin_tab):
    count_of_rows = unscaled_rows.shape[0]
    key_rows = unscaled_rows[:, : KEY_VALUE_HEADS * HEAD_WIDTH].reshape(
        count_of_rows, KEY_VALUE_HEADS, HEAD_WIDTH
    )
    value_rows = unscaled_rows[:, KEY_VALUE_HEADS * HEAD_WIDTH :].reshape(
        count_of_rows, KEY_VALUE_HEADS, HEAD_WIDTH
    )
    key_rows = rotate(norm_rows(key_rows, gain_vec), cos_tab, sin_tab)
    value_rows = norm_rows(value_rows, 1.0)
    return jnp.concatenate(
        [
            key_rows.reshape(count_of_rows, KEY_VALUE_HEADS * HEAD_WIDTH),
            value_rows.reshape(count_of_rows, KEY_VALUE_HEADS * HEAD_WIDTH),
        ],
        axis=1,
    )


def piece_of(places, starts):
    inside = (places[:, None] >= starts[None, :]) & (places[:, None] < starts[None, :] + IMG)
    labels = jnp.arange(1, starts.shape[0] + 1, dtype=jnp.int32)
    return jnp.sum(jnp.where(inside, labels[None, :], 0), axis=1) - 1


def visible(query_places, key_places, query_pieces, key_pieces, length):
    causal = key_places[None, :] <= query_places[:, None]
    same_piece = (query_pieces[:, None] == key_pieces[None, :]) & (query_pieces[:, None] >= 0)
    return (key_places[None, :] < length) & (causal | same_piece)


def block_mask(own_places, key_places, key_pieces, length, starts):
    return visible(own_places, key_places, piece_of(own_places, starts), key_pieces, length)


def attention_forward(queries, key_sel, value_sel, own_places, key_places, length, starts):
    count_of_rows, head_count = (queries.shape[0], queries.shape[1])
    block_size = min(512, count_of_rows)
    key_pieces = piece_of(key_places, starts)
    stacked = queries.reshape(count_of_rows // block_size, block_size, head_count, HEAD_WIDTH)

    def one_block(element):
        block_rows, block_at = element
        allowed = block_mask(own_places, key_places, key_pieces, length, starts)
        scores = jnp.einsum("qhd,khd->hqk", block_rows, key_sel, preferred_element_type=jnp.float32)
        masked = jnp.where(allowed[None], scores, NEGATIVE)
        peak_row = jnp.max(masked, axis=-1, keepdims=True)
        raw_weights = jnp.where(allowed[None], jnp.exp(masked - peak_row), 0.0)
        total_row = jnp.sum(raw_weights, axis=-1, keepdims=True)
        attn_probs = (raw_weights / total_row).astype(jnp.bfloat16)
        outputs = jnp.einsum(
            "hqk,khd->qhd", attn_probs, value_sel, preferred_element_type=jnp.float32
        )
        return (outputs, peak_row[..., 0], total_row[..., 0])

    return lax.map(one_block, (stacked, jnp.arange(count_of_rows // block_size, dtype=jnp.int32)))


def attention_backward(
    queries,
    key_sel,
    value_sel,
    grad_attended,
    block_peaks,
    block_totals,
    own_places,
    key_places,
    length,
    starts,
):
    count_of_rows, head_count = (queries.shape[0], queries.shape[1])
    block_size = min(512, count_of_rows)
    block_count = count_of_rows // block_size
    key_pieces = piece_of(key_places, starts)
    stacked = queries.reshape(block_count, block_size, head_count, HEAD_WIDTH)
    grad_stacked = grad_attended.reshape(block_count, block_size, head_count, HEAD_WIDTH)

    def one_block(carry, element):
        dk_sum, dv_sum = carry
        block_rows, grad_rows, peak_row, total_row, block_at = element
        allowed = block_mask(own_places, key_places, key_pieces, length, starts)
        scores = jnp.einsum("qhd,khd->hqk", block_rows, key_sel, preferred_element_type=jnp.float32)
        masked = jnp.where(allowed[None], scores, NEGATIVE)
        raw_weights = jnp.where(allowed[None], jnp.exp(masked - peak_row[..., None]), 0.0)
        attn_probs = raw_weights / total_row[..., None]
        probs_low = attn_probs.astype(jnp.bfloat16)
        grad_probs = jnp.einsum(
            "qhd,khd->hqk", grad_rows, value_sel, preferred_element_type=jnp.float32
        )
        delta_row = jnp.sum(attn_probs * grad_probs, axis=-1, keepdims=True)
        grad_scores = (attn_probs * (grad_probs - delta_row)).astype(jnp.bfloat16)
        grad_query = jnp.einsum(
            "hqk,khd->qhd", grad_scores, key_sel, preferred_element_type=jnp.float32
        )
        dk_sum = dk_sum + jnp.einsum(
            "hqk,qhd->khd", grad_scores, block_rows, preferred_element_type=jnp.float32
        )
        dv_sum = dv_sum + jnp.einsum(
            "hqk,qhd->khd", probs_low, grad_rows, preferred_element_type=jnp.float32
        )
        return ((dk_sum, dv_sum), grad_query)

    zero_keys = jnp.zeros(key_sel.shape, jnp.float32)
    (dk_sum, dv_sum), grad_query = lax.scan(
        one_block,
        (zero_keys, zero_keys),
        (
            stacked,
            grad_stacked,
            block_peaks,
            block_totals,
            jnp.arange(block_count, dtype=jnp.int32),
        ),
    )
    return (grad_query.reshape(count_of_rows, head_count, HEAD_WIDTH), dk_sum, dv_sum)


def adamw_step(weight, moment_one, moment_two, gradient, rate, decay):
    moment_one = BETA_ONE * moment_one + (1.0 - BETA_ONE) * gradient
    moment_two = BETA_TWO * moment_two + (1.0 - BETA_TWO) * gradient * gradient
    mean_step = moment_one / (1.0 - BETA_ONE**STEP)
    spread = moment_two / (1.0 - BETA_TWO**STEP)
    return (
        moment_one,
        moment_two,
        weight - rate * (mean_step / (jnp.sqrt(spread) + ADAM_EPS) + decay * weight),
    )


MESH = pl.DeviceIdType.MESH
LOW = jnp.bfloat16
FULL = jnp.float32


def cost(micros, flops=0):
    return pl.CostEstimate(
        flops=flops, bytes_accessed=int(micros * 3.0e6), transcendentals=0
    )


def params(ident, mebibytes=48):
    return pltpu.CompilerParams(
        collective_id=ident, has_side_effects=True, vmem_limit_bytes=mebibytes * 2**20
    )


def push(source, target, send, recv, device):
    return pltpu.make_async_remote_copy(
        source, target, send, recv, device_id=device, device_id_type=MESH
    )


class Line:
    def __init__(self, source, shape, place, core=False, view=None):
        self.source, self.shape, self.place, self.core = source, shape, place, core
        self.view = view

    def semaphores(self, count, data):
        dma = pltpu.SemaphoreType.DMA
        return [dma((count,)), dma((count,)), dma((2 * count,))] * 2 + [dma]

    def bind(self, x_ref, o_ref, sems, spots, sizes):
        self.o_ref, self.sems = o_ref, sems
        self.me, self.column, self.at = spots
        self.count = sizes[0]
        self.x_ref = self.view(x_ref, self.column) if self.view else x_ref

    def slot(self, source):
        return self.place(self.o_ref, self.column, source)

    def other(self, source):
        return self.place(self.o_ref, 1 - self.column, source)

    def to_left(self, source, k, origin):
        return push(origin, self.slot(source), self.sems[0].at[k], self.sems[4].at[k], {"row": self.me - 1})

    def to_right(self, source, k, origin):
        return push(origin, self.slot(source), self.sems[1].at[k], self.sems[3].at[k], {"row": self.me + 1})

    def to_core(self, source, k, origin):
        return push(origin, self.slot(source), self.sems[2].at[k], self.sems[5].at[k], {"col": 1 - self.column})

    def from_core(self, source, k):
        there = self.other(source)
        return push(there, there, self.sems[2].at[k], self.sems[5].at[k], {"col": 1 - self.column})

    def from_left(self, source, k):
        there = self.slot(source)
        return push(there, there, self.sems[1].at[k], self.sems[3].at[k - 1], {"row": self.me - 1})

    def from_right(self, source, k):
        there = self.slot(source)
        return push(there, there, self.sems[0].at[k], self.sems[4].at[k - 1], {"row": self.me + 1})

    def own(self):
        return pltpu.make_async_copy(self.x_ref, self.slot(self.me), self.sems[6])

    def start(self):
        me, count = self.me, self.count

        @pl.when(me > 0)
        def _():
            self.to_left(me, 0, self.x_ref).start()

        @pl.when(me < count - 1)
        def _():
            self.to_right(me, 0, self.x_ref).start()

        if self.core:
            self.to_core(me, 0, self.x_ref).start()
        self.own().start()

    def step(self, k):
        me, count = self.me, self.count

        @pl.when(me - k >= 0)
        def _():
            self.from_left(me - k, k).wait_recv()
            block = self.slot(me - k)

            @pl.when(me < count - 1)
            def _():
                self.to_right(me - k, k, block).start()

            if self.core:
                self.to_core(me - k, k, block).start()

        @pl.when(me + k < count)
        def _():
            self.from_right(me + k, k).wait_recv()
            block = self.slot(me + k)

            @pl.when(me > 0)
            def _():
                self.to_left(me + k, k, block).start()

            if self.core:
                self.to_core(me + k, count - 1 + k, block).start()

    def finish(self):
        me, count = self.me, self.count
        self.own().wait()

        @pl.when(me > 0)
        def _():
            self.to_left(me, 0, self.x_ref).wait_send()

        @pl.when(me < count - 1)
        def _():
            self.to_right(me, 0, self.x_ref).wait_send()

        if self.core:
            self.to_core(me, 0, self.x_ref).wait_send()
            self.from_core(me, 0).wait_recv()

        @pl.loop(1, count)
        def _(k):
            @pl.when(me - k >= 0)
            def _():
                @pl.when(me < count - 1)
                def _():
                    self.to_right(me - k, k, self.x_ref).wait_send()

                if self.core:
                    self.to_core(me - k, k, self.x_ref).wait_send()
                    self.from_core(me - k, k).wait_recv()

            @pl.when(me + k < count)
            def _():
                @pl.when(me > 0)
                def _():
                    self.to_left(me + k, k, self.x_ref).wait_send()

                if self.core:
                    self.to_core(me + k, count - 1 + k, self.x_ref).wait_send()
                    self.from_core(me + k, count - 1 + k).wait_recv()


class Swap:
    def __init__(self, source, shape, take, place, axis="row"):
        self.source, self.shape, self.take, self.place = source, shape, take, place
        self.axis = axis

    def semaphores(self, count, data):
        size = count if self.axis == "row" else data
        return [pltpu.SemaphoreType.DMA((size,)), pltpu.SemaphoreType.DMA((size,))]

    def bind(self, x_ref, o_ref, sems, spots, sizes):
        self.x_ref, self.o_ref, self.sems = x_ref, o_ref, sems
        self.me = spots[0] if self.axis == "row" else spots[2]
        self.count = sizes[0] if self.axis == "row" else sizes[1]

    def copy(self, k):
        target = lax.rem(self.me + k, self.count)
        return push(
            self.take(self.x_ref, target),
            self.place(self.o_ref, self.me),
            self.sems[0].at[k],
            self.sems[1].at[k],
            {self.axis: target},
        )

    def own(self):
        return pltpu.make_async_copy(
            self.take(self.x_ref, self.me), self.place(self.o_ref, self.me), self.sems[0].at[0]
        )

    def start(self):
        for k in range(1, self.count):
            self.copy(k).start()
        self.own().start()

    def step(self, k):
        pass

    def finish(self):
        self.own().wait()
        for k in range(1, self.count):
            self.copy(k).wait_send()
            origin = lax.rem(self.me + self.count - k, self.count)
            there = self.place(self.o_ref, origin)
            push(there, there, self.sems[0].at[k], self.sems[1].at[k], {self.axis: origin}).wait_recv()


class Pair:
    core = True

    def __init__(self, source):
        self.source, self.shape = source, source.shape

    def semaphores(self, count, data):
        dma = pltpu.SemaphoreType.DMA
        return [dma, dma, dma]

    def bind(self, x_ref, o_ref, sems, spots, sizes):
        self.x_ref, self.o_ref, self.sems = x_ref, o_ref, sems
        self.column = spots[1]

    def copy(self):
        other = 1 - self.column
        return push(self.x_ref.at[other], self.o_ref.at[1], self.sems[0], self.sems[1], {"col": other})

    def own(self):
        return pltpu.make_async_copy(self.x_ref.at[self.column], self.o_ref.at[0], self.sems[2])

    def start(self):
        self.copy().start()
        self.own().start()

    def step(self, k):
        pass

    def finish(self):
        self.own().wait()
        self.copy().wait()


class Reduce:
    def __init__(self, source, shape, cut, core=True):
        self.source, self.shape, self.cut, self.core = source, shape, cut, core
        self.high, self.wide = shape
        self.dtype = FULL

    def semaphores(self, count, data):
        dma = pltpu.SemaphoreType.DMA
        slots = pltpu.VMEM((count,) + self.shape, self.source.dtype)
        whole = pltpu.VMEM(self.source.shape[1:] if self.core else self.source.shape, self.source.dtype)
        stage = pltpu.VMEM(self.shape, FULL)
        fourth = slots if self.core else pltpu.VMEM((1, 16, 128), self.source.dtype)
        return [whole, stage, slots, slots, slots, fourth] + [dma((count,))] * 6 + [dma, dma]

    def bind(self, x_ref, o_ref, sems, spots, sizes):
        self.x_ref, self.o_ref = x_ref, o_ref
        self.mine, self.stage, self.out, self.left_in, self.right_in, self.core_in = sems[:6]
        self.sems = sems[6:]
        self.me, self.column = spots[0], spots[1]
        self.count = sizes[0]

    def beside(self, q):
        return push(
            self.cut(self.x_ref.at[1 - self.column], q),
            self.core_in.at[q],
            self.sems[0].at[q],
            self.sems[3].at[q],
            {"col": 1 - self.column},
        )

    def to_left(self, q):
        return push(self.out.at[q], self.left_in.at[q], self.sems[1].at[q], self.sems[4].at[q], {"row": self.me - 1})

    def to_right(self, q):
        return push(self.out.at[q], self.right_in.at[q], self.sems[2].at[q], self.sems[5].at[q], {"row": self.me + 1})

    def from_right(self, q):
        return push(self.left_in.at[q], self.left_in.at[q], self.sems[1].at[q], self.sems[4].at[q], {"row": self.me + 1})

    def from_left(self, q):
        return push(self.right_in.at[q], self.right_in.at[q], self.sems[2].at[q], self.sems[5].at[q], {"row": self.me - 1})

    def own(self):
        return pltpu.make_async_copy(
            self.x_ref.at[self.column] if self.core else self.x_ref, self.mine, self.sems[6]
        )

    def start(self):
        self.own().start()
        if self.core:
            for q in range(self.count):
                self.beside(q).start()

    def added(self, target, q, others):
        step = min(self.high, max(16, 65536 // self.wide))
        while self.high % step:
            step //= 2
        cut = self.cut(self.mine, q)
        others = ([self.core_in] if self.core else []) + others

        @pl.loop(0, self.high // step)
        def _(at):
            rows = pl.ds(pl.multiple_of(at * step, step), step)
            total = cut[rows].astype(FULL)
            for other in others:
                total = total + other[q, rows].astype(FULL)
            target[rows] = total.astype(target.dtype)

    def step(self, k):
        me, count = self.me, self.count
        t = k - 1
        q_left = t - (count - 1 - me)
        q_right = count - 1 - (t - me)

        @pl.when(t == 0)
        def _():
            self.own().wait()

        @pl.when((q_left >= 0) & (q_left < me))
        def _():
            if self.core:
                self.beside(q_left).wait()

            @pl.when(me < count - 1)
            def _():
                self.from_right(q_left).wait_recv()
                self.added(self.out.at[q_left], q_left, [self.left_in])

            @pl.when(me == count - 1)
            def _():
                self.added(self.out.at[q_left], q_left, [])

            self.to_left(q_left).start()

        @pl.when((t >= me) & (q_right > me))
        def _():
            if self.core:
                self.beside(q_right).wait()

            @pl.when(me > 0)
            def _():
                self.from_left(q_right).wait_recv()
                self.added(self.out.at[q_right], q_right, [self.right_in])

            @pl.when(me == 0)
            def _():
                self.added(self.out.at[q_right], q_right, [])

            self.to_right(q_right).start()

    def finish(self):
        me, count = self.me, self.count
        if self.core:
            self.beside(me).wait()

        @pl.when(me < count - 1)
        def _():
            self.from_right(me).wait_recv()

        @pl.when(me > 0)
        def _():
            self.from_left(me).wait_recv()

        @pl.when(me == 0)
        def _():
            self.added(self.stage, me, [self.left_in])

        @pl.when(me == count - 1)
        def _():
            self.added(self.stage, me, [self.right_in])

        @pl.when((me > 0) & (me < count - 1))
        def _():
            self.added(self.stage, me, [self.left_in, self.right_in])

        out = pltpu.make_async_copy(self.stage, self.o_ref, self.sems[7])
        out.start()

        @pl.loop(0, count)
        def _(q):
            @pl.when(q < me)
            def _():
                self.to_left(q).wait_send()

            @pl.when(q > me)
            def _():
                self.to_right(q).wait_send()

        out.wait()


class ShardSum:
    axis = "dp"

    def __init__(self, source, out_cols):
        self.source, self.out_cols = source, out_cols
        self.parts = source.shape[1] // out_cols // lax.axis_size("dp")
        self.shape = (source.shape[0], self.parts * out_cols)

    def semaphores(self, count, data):
        dma = pltpu.SemaphoreType.DMA
        buf = pltpu.VMEM((data,) + self.shape, self.source.dtype)
        stage = pltpu.VMEM(self.shape, self.source.dtype)
        return [buf, stage, dma((data, self.parts)), dma((data, self.parts)), dma]

    def bind(self, x_ref, o_ref, sems, spots, sizes):
        self.x_ref, self.o_ref = x_ref, o_ref
        self.buf, self.stage, self.send, self.recv, self.local = sems
        self.at, self.data = spots[2], sizes[1]

    def copy(self, k, s):
        target = lax.rem(self.at + k, self.data)
        wide = self.out_cols
        source = self.x_ref.at[:, pl.ds(pl.multiple_of((s * self.data + target) * wide, wide), wide)]
        slot = self.buf.at[k, :, pl.ds(s * wide, wide)]
        if k == 0:
            return pltpu.make_async_copy(source, slot, self.send.at[k, s])
        return push(source, slot, self.send.at[k, s], self.recv.at[k, s], {"dp": target})

    def start(self):
        for k in range(self.data):
            for s in range(self.parts):
                self.copy(k, s).start()

    def step(self, k):
        pass

    def finish(self):
        for k in range(self.data):
            for s in range(self.parts):
                self.copy(k, s).wait()

        @pl.loop(0, self.shape[0] // 64)
        def _(at):
            rows = pl.ds(pl.multiple_of(at * 64, 64), 64)
            total = self.buf[0, rows].astype(FULL)
            for k in range(1, self.data):
                total = total + self.buf[k, rows].astype(FULL)
            self.stage[rows] = total.astype(self.stage.dtype)

        out = pltpu.make_async_copy(self.stage, self.o_ref, self.local)
        out.start()
        out.wait()


class Bundle:
    def __init__(self, items):
        self.items = items
        self.number = len(items)
        self.sizes = lax.axis_size("row"), lax.axis_size("dp")
        self.kinds = [item.semaphores(*self.sizes) for item in items]
        self.across = any(getattr(item, "axis", None) == "dp" for item in items)
        self.cores = any(getattr(item, "core", False) for item in items)
        self.sources = [item.source for item in items]
        self.shapes = [
            jax.ShapeDtypeStruct(item.shape, getattr(item, "dtype", item.source.dtype)) for item in items
        ]
        self.specs = [pl.BlockSpec(memory_space=pl.ANY)] * self.number
        self.scratch = sum(self.kinds, [])

    def bind(self, x_refs, o_refs, sems):
        self.spots = lax.axis_index("row"), lax.axis_index("col"), lax.axis_index("dp")
        for item, x_ref, o_ref, kind in zip(self.items, x_refs, o_refs, self.kinds):
            item.bind(x_ref, o_ref, sems[: len(kind)], self.spots, self.sizes)
            sems = sems[len(kind) :]

    def greet(self, across=False, cores=False):
        me, column, at = self.spots
        count, data = self.sizes
        across, cores = across or self.across, cores or self.cores
        barrier = pltpu.get_barrier_semaphore()
        for k in range(1, count):
            pl.semaphore_signal(
                barrier, inc=1, device_id={"row": lax.rem(me + k, count)}, device_id_type=MESH
            )
        if across:
            for k in range(1, data):
                pl.semaphore_signal(
                    barrier, inc=1, device_id={"dp": lax.rem(at + k, data)}, device_id_type=MESH
                )
        if cores:
            pl.semaphore_signal(barrier, inc=1, device_id={"col": 1 - column}, device_id_type=MESH)
        pl.semaphore_wait(barrier, count - 1 + (data - 1) * int(across) + int(cores))

    def start(self):
        for item in self.items:
            item.start()

    def step(self, k):
        for item in self.items:
            item.step(k)

    def finish(self):
        for item in self.items:
            item.finish()


def transfers(items, ident, micros, mebibytes=16):
    bundle = Bundle(items)
    number = bundle.number

    def kernel(*refs):
        bundle.bind(refs[:number], refs[number : 2 * number], refs[2 * number :])
        bundle.greet()
        bundle.start()
        for k in range(1, bundle.sizes[0]):
            bundle.step(k)
        bundle.finish()

    return pl.pallas_call(
        kernel,
        out_shape=bundle.shapes,
        in_specs=bundle.specs,
        out_specs=bundle.specs,
        scratch_shapes=bundle.scratch,
        compiler_params=params(ident, mebibytes),
        cost_estimate=cost(micros),
    )(*bundle.sources)


def shard_total(query_parts, kv_parts, flat_parts, items, ident):
    data = lax.axis_size("dp")
    bundle = Bundle(items)
    number = bundle.number

    def kernel(q_ref, kv_ref, f_ref, *refs):
        x_refs, refs = refs[:number], refs[number:]
        oq_ref, okv_ref, of_ref = refs[:3]
        o_refs, refs = refs[3 : 3 + number], refs[3 + number :]
        q_buf, kv_buf, f_buf = refs[:3]
        sems = refs[3:11]
        bundle.bind(x_refs, o_refs, refs[11:])
        column, at = lax.axis_index("col"), lax.axis_index("dp")
        bundle.greet(True, True)
        bundle.start()
        mine = lax.rem(at, 2) == column

        def copies(k):
            target = lax.rem(at + k, data)
            device = {"dp": target}
            return (
                push(q_ref.at[target], q_buf.at[k], sems[0].at[k], sems[1].at[k], device),
                push(kv_ref.at[target // 2], kv_buf.at[k], sems[2].at[k], sems[3].at[k], device),
                push(f_ref.at[target], f_buf.at[k], sems[4].at[k], sems[5].at[k], device),
                lax.rem(target, 2) == column,
            )

        for k in range(1, data):
            query_copy, kv_copy, flat_copy, there = copies(k)
            query_copy.start()
            flat_copy.start()

            @pl.when(there)
            def _():
                kv_copy.start()

        for k in range(1, data):
            query_copy, kv_copy, flat_copy, there = copies(k)
            query_copy.wait()
            flat_copy.wait()

            @pl.when(there)
            def _():
                kv_copy.wait_send()

            @pl.when(mine)
            def _():
                kv_copy.wait_recv()

        def added(target, own, buf, chunk):
            @pl.loop(0, target.shape[0] // chunk)
            def _(step):
                rows = pl.ds(pl.multiple_of(step * chunk, chunk), chunk)
                total = own[rows].astype(FULL)
                for k in range(1, data):
                    total = total + buf[k, rows].astype(FULL)
                target[rows] = total

        share = push(okv_ref, okv_ref, sems[6], sems[7], {"col": 1 - column})

        @pl.when(mine)
        def _():
            added(okv_ref, kv_ref.at[at // 2], kv_buf, 128)
            share.start()

        added(oq_ref, q_ref.at[at], q_buf, 128)
        added(of_ref, f_ref.at[at], f_buf, 64)

        @pl.when(mine)
        def _():
            share.wait_send()

        @pl.when(jnp.logical_not(mine))
        def _():
            share.wait_recv()

        for k in range(1, bundle.sizes[0]):
            bundle.step(k)
        bundle.finish()

    vmem = pl.BlockSpec(memory_space=pltpu.VMEM)
    dma = pltpu.SemaphoreType.DMA
    shapes = [query_parts.shape[1:], kv_parts.shape[1:], flat_parts.shape[1:]]
    return pl.pallas_call(
        kernel,
        out_shape=[jax.ShapeDtypeStruct(shape, FULL) for shape in shapes] + bundle.shapes,
        in_specs=[vmem] * 3 + bundle.specs,
        out_specs=[vmem] * 3 + bundle.specs,
        scratch_shapes=[pltpu.VMEM((data,) + shape, LOW) for shape in shapes]
        + [dma((data,))] * 6
        + [dma, dma]
        + bundle.scratch,
        compiler_params=params(ident),
        cost_estimate=cost(40),
    )(query_parts, kv_parts, flat_parts, *bundle.sources)


CHUNKS = 4


class Flow:
    def __init__(self, x_ref, blocks, own, core_out, core_in, left_in, right_in, sems):
        self.x_ref, self.blocks, self.own = x_ref, blocks, own
        self.core_out, self.core_in = core_out, core_in
        self.left_in, self.right_in = left_in, right_in
        self.sems = sems
        self.me, self.column = lax.axis_index("row"), lax.axis_index("col")
        self.count = blocks.shape[0]

    @staticmethod
    def scratch(count, share, width):
        dma = pltpu.SemaphoreType.DMA
        slots = (count, share, width)
        return [
            pltpu.VMEM((count, 2, share, width), LOW),
            pltpu.VMEM(slots, FULL),
            pltpu.VMEM(slots, LOW),
            pltpu.VMEM(slots, LOW),
            pltpu.VMEM(slots, LOW),
            pltpu.VMEM(slots, LOW),
        ], [dma((count,))] * 7 + [dma((count * CHUNKS,))] * 2 + [dma((count,))] + [
            dma((count * CHUNKS,))
        ] * 2 + [dma]

    def left(self):
        return {"row": self.me - 1}

    def right(self):
        return {"row": self.me + 1}

    def beside(self):
        return {"col": 1 - self.column}

    def to_left(self, source, k, origin):
        return push(origin, self.blocks.at[source, 0], self.sems[0].at[k], self.sems[4].at[k], self.left())

    def to_right(self, source, k, origin):
        return push(origin, self.blocks.at[source, 0], self.sems[1].at[k], self.sems[3].at[k], self.right())

    def to_core(self, source, origin):
        return push(origin, self.blocks.at[source, 1], self.sems[2].at[source], self.sems[5].at[source], self.beside())

    def back_core(self, q):
        return push(self.core_out.at[q], self.core_in.at[q], self.sems[6].at[q], self.sems[9].at[q], self.beside())

    def part(self, ref, q, j):
        size = ref.shape[1] // CHUNKS
        return ref.at[q, pl.ds(pl.multiple_of(j * size, size), size)]

    def back_left(self, q, j):
        at = q * CHUNKS + j
        return push(
            self.part(self.core_out, q, j),
            self.part(self.left_in, q, j),
            self.sems[7].at[at],
            self.sems[10].at[at],
            self.left(),
        )

    def back_right(self, q, j):
        at = q * CHUNKS + j
        return push(
            self.part(self.core_out, q, j),
            self.part(self.right_in, q, j),
            self.sems[8].at[at],
            self.sems[11].at[at],
            self.right(),
        )

    def from_right(self, q, j):
        at, there = q * CHUNKS + j, self.part(self.left_in, q, j)
        return push(there, there, self.sems[7].at[at], self.sems[10].at[at], self.right())

    def from_left(self, q, j):
        at, there = q * CHUNKS + j, self.part(self.right_in, q, j)
        return push(there, there, self.sems[8].at[at], self.sems[11].at[at], self.left())

    def mine(self):
        return pltpu.make_async_copy(self.x_ref, self.blocks.at[self.me, 0], self.sems[12])

    def start(self):
        me, count = self.me, self.count

        @pl.when(me > 0)
        def _():
            self.to_left(me, 0, self.x_ref).start()

        @pl.when(me < count - 1)
        def _():
            self.to_right(me, 0, self.x_ref).start()

        self.to_core(me, self.x_ref).start()
        self.mine().start()

    def arrive(self, k):
        me, count = self.me, self.count

        @pl.when(k == 0)
        def _():
            self.mine().wait()
            self.to_core(me, self.x_ref).wait()

        @pl.when((k > 0) & (me - k >= 0))
        def _():
            source = me - k
            block = self.blocks.at[source, 0]
            push(block, block, self.sems[1].at[k], self.sems[3].at[k - 1], self.left()).wait_recv()

            @pl.when(me < count - 1)
            def _():
                self.to_right(source, k, block).start()

            self.to_core(source, block).start()

        @pl.when((k > 0) & (me + k < count))
        def _():
            source = me + k
            block = self.blocks.at[source, 0]
            push(block, block, self.sems[0].at[k], self.sems[4].at[k - 1], self.right()).wait_recv()

            @pl.when(me > 0)
            def _():
                self.to_left(source, k, block).start()

            self.to_core(source, block).start()

        @pl.when((k > 0) & (me - k >= 0))
        def _():
            self.to_core(me - k, self.x_ref).wait()

        @pl.when((k > 0) & (me + k < count))
        def _():
            self.to_core(me + k, self.x_ref).wait()

    def visit(self, body, bundle):
        me, count = self.me, self.count

        @pl.loop(0, count)
        def _(k):
            self.arrive(k)

            @pl.when(k == count - 2)
            def _():
                bundle.start()

            @pl.when(k == count - 1)
            def _():
                bundle.step(1)

            @pl.loop(0, 2)
            def _(side):
                source = jnp.where(side == 0, me - k, me + k)

                @pl.when((source >= 0) & (source < count) & ((side == 0) | (k > 0)))
                def _():
                    body(source)
                    self.back_core(source).start()

            self.give_back(k)

    def added(self, target, terms):
        total = terms[0][...]
        for term in terms[1:]:
            total = total + term[...].astype(FULL)
        target[...] = total.astype(target.dtype)

    def give_back(self, t):
        me, count = self.me, self.count
        q_left = 2 * (count - 1) - me - t
        q_right = t - me

        def leftward():
            q = q_left
            self.back_core(q).wait()

            @pl.loop(0, CHUNKS)
            def _(j):
                base = [self.part(self.own, q, j), self.part(self.core_in, q, j)]
                target = self.part(self.core_out, q, j)

                @pl.when(me < count - 1)
                def _():
                    self.from_right(q, j).wait_recv()
                    self.added(target, base + [self.part(self.left_in, q, j)])

                @pl.when(me == count - 1)
                def _():
                    self.added(target, base)

                self.back_left(q, j).start()

        def rightward():
            q = q_right
            self.back_core(q).wait()

            @pl.loop(0, CHUNKS)
            def _(j):
                base = [self.part(self.own, q, j), self.part(self.core_in, q, j)]
                target = self.part(self.core_out, q, j)

                @pl.when(me > 0)
                def _():
                    self.from_left(q, j).wait_recv()
                    self.added(target, base + [self.part(self.right_in, q, j)])

                @pl.when(me == 0)
                def _():
                    self.added(target, base)

                self.back_right(q, j).start()

        pl.when((q_left >= 0) & (q_left < me))(leftward)
        pl.when((q_right > me) & (q_right < count))(rightward)

    def finish(self, o_ref):
        me, count = self.me, self.count
        self.back_core(me).wait()

        @pl.loop(0, CHUNKS)
        def _(j):
            size = o_ref.shape[0] // CHUNKS
            target = o_ref.at[pl.ds(pl.multiple_of(j * size, size), size)]
            base = [self.part(self.own, me, j), self.part(self.core_in, me, j)]

            @pl.when(me < count - 1)
            def _():
                self.from_right(me, j).wait_recv()

            @pl.when(me > 0)
            def _():
                self.from_left(me, j).wait_recv()

            @pl.when(me == 0)
            def _():
                self.added(target, base + [self.part(self.left_in, me, j)])

            @pl.when(me == count - 1)
            def _():
                self.added(target, base + [self.part(self.right_in, me, j)])

            @pl.when((me > 0) & (me < count - 1))
            def _():
                self.added(
                    target, base + [self.part(self.left_in, me, j), self.part(self.right_in, me, j)]
                )

        @pl.when(me > 0)
        def _():
            self.to_left(me, 0, self.x_ref).wait_send()

        @pl.when(me < count - 1)
        def _():
            self.to_right(me, 0, self.x_ref).wait_send()

        @pl.loop(1, count)
        def _(k):
            @pl.when((me - k >= 0) & (me < count - 1))
            def _():
                self.to_right(me - k, k, self.x_ref).wait_send()

            @pl.when((me + k < count) & (me > 0))
            def _():
                self.to_left(me + k, k, self.x_ref).wait_send()

        @pl.loop(0, count * CHUNKS)
        def _(at):
            q, j = at // CHUNKS, lax.rem(at, CHUNKS)

            @pl.when(q < me)
            def _():
                self.back_left(q, j).wait_send()

            @pl.when(q > me)
            def _():
                self.back_right(q, j).wait_send()


GELU_ONE = 0.7978845608028654
GELU_TWO = 0.044715


def gelu_of(values_in):
    inner = GELU_ONE * (values_in + GELU_TWO * values_in * values_in * values_in)
    bend = jnp.tanh(inner)
    half = 0.5 * (1.0 + bend)
    slope = half + 0.5 * values_in * (1.0 - bend * bend) * GELU_ONE * (
        1.0 + 3.0 * GELU_TWO * values_in * values_in
    )
    return values_in * half, slope


def ffn_forward(block, gateup, down, items, ident):
    count = lax.axis_size("row")
    share, width = block.shape
    groups, _, _, part = gateup.shape
    hidden = groups * part
    out_cols = down.shape[2] // count
    rows = 2 * share
    bundle = Bundle(items)
    number = bundle.number

    def kernel(x_ref, gw_hbm, dw_hbm, *refs):
        x_refs, refs = refs[:number], refs[number:]
        o_ref, xt_hbm, at_hbm, g_hbm, u_hbm = refs[:5]
        o_refs, scratch = refs[5 : 5 + number], refs[5 + number :]
        flow = Flow(x_ref, *scratch[:6], scratch[6:19])
        gw, dw, xt, at, act, gate, up = scratch[19:26]
        gw_sem, dw_sem, xt_sem, at_sem, g_sem, u_sem = scratch[26:32]
        bundle.bind(x_refs, o_refs, scratch[32:])
        gw_load = pltpu.make_async_copy(gw_hbm, gw, gw_sem)
        dw_load = pltpu.make_async_copy(dw_hbm, dw, dw_sem)
        gw_load.start()
        dw_load.start()
        bundle.greet(False, True)
        flow.start()
        gw_load.wait()
        dw_load.wait()

        def stores(source):
            return (
                pltpu.make_async_copy(gate.at[source], g_hbm.at[source], g_sem.at[source]),
                pltpu.make_async_copy(up.at[source], u_hbm.at[source], u_sem.at[source]),
            )

        def body(source):
            x = flow.blocks[source].reshape(rows, width)

            @pl.loop(0, groups)
            def _(d):
                columns = pl.ds(pl.multiple_of(d * part, part), part)
                g = flat_dot(x, gw[d, 0])
                u = flat_dot(x, gw[d, 1])
                gate[source, :, columns] = g
                up[source, :, columns] = u
                act[source, :, columns] = (gelu_of(g)[0] * u).astype(LOW)

            for copy in stores(source):
                copy.start()
            for d in range(groups):
                out = flat_dot(act[source], dw[d])
                for s in range(count):
                    columns = slice((s * groups + d) * out_cols, (s * groups + d + 1) * out_cols)
                    piece = out[:, s * out_cols : (s + 1) * out_cols]
                    flow.own[source, :, columns] = piece[:share]
                    flow.core_out[source, :, columns] = piece[share:].astype(LOW)

        flow.visit(body, bundle)

        @pl.loop(0, count)
        def _(source):
            here = pl.ds(pl.multiple_of(source * rows, rows), rows)
            xt[:, here] = flow.blocks[source].reshape(rows, width).T
            at[:, here] = act[source].T

        xt_store = pltpu.make_async_copy(xt, xt_hbm, xt_sem)
        at_store = pltpu.make_async_copy(at, at_hbm, at_sem)
        xt_store.start()
        at_store.start()

        @pl.loop(count, 2 * count - 2)
        def _(t):
            flow.give_back(t)

        for k in range(2, count):
            bundle.step(k)
        flow.finish(o_ref)
        bundle.finish()
        xt_store.wait()
        at_store.wait()

        @pl.loop(0, count)
        def _(source):
            for copy in stores(source):
                copy.wait()

    dma = pltpu.SemaphoreType.DMA
    buffers, sems = Flow.scratch(count, share, width)
    vmem, anywhere = pl.BlockSpec(memory_space=pltpu.VMEM), pl.BlockSpec(memory_space=pl.ANY)
    tokens = count * rows
    return pl.pallas_call(
        kernel,
        out_shape=[
            jax.ShapeDtypeStruct((share, width), FULL),
            jax.ShapeDtypeStruct((width, tokens), LOW),
            jax.ShapeDtypeStruct((hidden, tokens), LOW),
            jax.ShapeDtypeStruct((count, rows, hidden), FULL),
            jax.ShapeDtypeStruct((count, rows, hidden), FULL),
        ]
        + bundle.shapes,
        in_specs=[vmem, anywhere, anywhere] + bundle.specs,
        out_specs=[vmem] + [anywhere] * 4 + bundle.specs,
        scratch_shapes=buffers
        + sems
        + [
            pltpu.VMEM(gateup.shape, LOW),
            pltpu.VMEM(down.shape, LOW),
            pltpu.VMEM((width, tokens), LOW),
            pltpu.VMEM((hidden, tokens), LOW),
            pltpu.VMEM((count, rows, hidden), LOW),
            pltpu.VMEM((count, rows, hidden), FULL),
            pltpu.VMEM((count, rows, hidden), FULL),
        ]
        + [dma, dma, dma, dma, dma((count,)), dma((count,))]
        + bundle.scratch,
        compiler_params=params(ident, 60),
        cost_estimate=cost(80),
    )(block, gateup, down, *bundle.sources)


def ffn_backward(block, gateup, down, xt, at, gate, up, items, ident):
    count = lax.axis_size("row")
    share, width = block.shape
    groups, _, _, part = gateup.shape
    hidden = groups * part
    out_cols = down.shape[2] // count
    rows = 2 * share
    tokens = count * rows
    bundle = Bundle(items)
    number = bundle.number

    def kernel(x_ref, gw_hbm, dw_hbm, xt_hbm, at_hbm, g_hbm, u_hbm, *refs):
        x_refs, refs = refs[:number], refs[number:]
        o_ref, dgu_hbm, ddn_hbm = refs[:3]
        o_refs, scratch = refs[3 : 3 + number], refs[3 + number :]
        flow = Flow(x_ref, *scratch[:6], scratch[6:19])
        gw, dw, xt_own, at_own, gate_own, up_own, d_gate, d_up, total, stage, stage_down = scratch[19:30]
        load_sems, g_sem, u_sem, out_sem, down_sem = scratch[30:35]
        bundle.bind(x_refs, o_refs, scratch[35:])
        loads = [
            pltpu.make_async_copy(source, target, load_sems.at[k])
            for k, (source, target) in enumerate(
                [(dw_hbm, dw), (gw_hbm, gw), (xt_hbm, xt_own), (at_hbm, at_own)]
            )
        ]

        def fetches(source):
            return (
                pltpu.make_async_copy(g_hbm.at[source], gate_own.at[source], g_sem.at[source]),
                pltpu.make_async_copy(u_hbm.at[source], up_own.at[source], u_sem.at[source]),
            )

        for load in loads[:2]:
            load.start()

        @pl.loop(0, count)
        def _(source):
            for copy in fetches(source):
                copy.start()

        for load in loads[2:]:
            load.start()
        bundle.greet(False, True)
        flow.start()
        loads[0].wait()
        loads[1].wait()

        def columns_of(s, d):
            return pl.ds(pl.multiple_of((s * groups + d) * out_cols, out_cols), out_cols)

        def body(source):
            for copy in fetches(source):
                copy.wait()
            grad = flow.blocks[source].reshape(rows, width)
            d_act = None
            for d in range(groups):
                cut = jnp.concatenate(
                    [
                        grad[:, (s * groups + d) * out_cols : (s * groups + d + 1) * out_cols]
                        for s in range(count)
                    ],
                    axis=1,
                )
                term = against(cut, dw[d])
                d_act = term if d_act is None else d_act + term
            total[:, :hidden] = d_act

            @pl.loop(0, groups)
            def _(d):
                columns = pl.ds(pl.multiple_of(d * part, part), part)
                grad_act = total[:, columns]
                curve, slope = gelu_of(gate_own[source, :, columns])
                d_gate[source, :, columns] = (grad_act * up_own[source, :, columns] * slope).astype(LOW)
                d_up[source, :, columns] = (grad_act * curve).astype(LOW)

            total[...] = jnp.zeros(total.shape, FULL)

            @pl.loop(0, groups)
            def _(d):
                columns = pl.ds(pl.multiple_of(d * part, part), part)
                total[...] += against(d_gate[source, :, columns], gw[d, 0]) + against(
                    d_up[source, :, columns], gw[d, 1]
                )

            flow.own[source] = total[:share]
            flow.core_out[source] = total[share:].astype(LOW)

        flow.visit(body, bundle)
        loads[2].wait()
        loads[3].wait()

        def gateup_store(d, which):
            return pltpu.make_async_copy(stage.at[which], dgu_hbm.at[d, which], out_sem.at[which])

        def down_store(d):
            return pltpu.make_async_copy(stage_down, ddn_hbm.at[d], down_sem)

        def weights(d):
            columns = pl.ds(pl.multiple_of(d * part, part), part)
            for which, grads in ((0, d_gate), (1, d_up)):

                @pl.when(d > 0)
                def _():
                    gateup_store(d - 1, which).wait()

                right = grads[:, :, columns].reshape(tokens, part)

                @pl.loop(0, width // 512)
                def _(k):
                    high = pl.ds(pl.multiple_of(k * 512, 512), 512)
                    stage[which, high] = flat_dot(xt_own[high], right).astype(LOW)

                gateup_store(d, which).start()

            @pl.when(d > 0)
            def _():
                down_store(d - 1).wait()

            right = jnp.concatenate(
                [flow.blocks[:, :, :, columns_of(s, d)].reshape(tokens, out_cols) for s in range(count)],
                axis=1,
            )

            @pl.loop(0, hidden // 256)
            def _(k):
                high = pl.ds(pl.multiple_of(k * 256, 256), 256)
                stage_down[high] = flat_dot(at_own[high], right).astype(LOW)

            down_store(d).start()

        @pl.loop(0, count - 2)
        def _(t):
            weights(t)
            flow.give_back(count + t)

        for k in range(2, count):
            bundle.step(k)

        @pl.loop(count - 2, groups)
        def _(d):
            weights(d)

        for which in range(2):
            gateup_store(groups - 1, which).wait()
        down_store(groups - 1).wait()
        flow.finish(o_ref)
        bundle.finish()

    dma = pltpu.SemaphoreType.DMA
    buffers, sems = Flow.scratch(count, share, width)
    vmem, anywhere = pl.BlockSpec(memory_space=pltpu.VMEM), pl.BlockSpec(memory_space=pl.ANY)
    return pl.pallas_call(
        kernel,
        out_shape=[
            jax.ShapeDtypeStruct((share, width), FULL),
            jax.ShapeDtypeStruct(gateup.shape, LOW),
            jax.ShapeDtypeStruct(down.shape, LOW),
        ]
        + bundle.shapes,
        in_specs=[vmem] + [anywhere] * 6 + bundle.specs,
        out_specs=[vmem, anywhere, anywhere] + bundle.specs,
        scratch_shapes=buffers
        + sems
        + [
            pltpu.VMEM(gateup.shape, LOW),
            pltpu.VMEM(down.shape, LOW),
            pltpu.VMEM((width, tokens), LOW),
            pltpu.VMEM((hidden, tokens), LOW),
            pltpu.VMEM((count, rows, hidden), FULL),
            pltpu.VMEM((count, rows, hidden), FULL),
            pltpu.VMEM((count, rows, hidden), LOW),
            pltpu.VMEM((count, rows, hidden), LOW),
            pltpu.VMEM((rows, width), FULL),
            pltpu.VMEM((2, width, part), LOW),
            pltpu.VMEM((hidden, count * out_cols), LOW),
        ]
        + [dma((4,)), dma((count,)), dma((count,)), dma((2,)), dma]
        + bundle.scratch,
        compiler_params=params(ident, 62),
        cost_estimate=cost(90),
    )(block, gateup, down, xt, at, gate, up, *bundle.sources)


def last_sums(small, ident):
    axes = ("col", "row", "dp")
    sizes = [lax.axis_size(axis) for axis in axes]
    high = small.shape[0]

    def kernel(x_ref, o_ref, *refs):
        slots, sends, recvs = (refs[k::3] for k in range(3))
        spots = [lax.axis_index(axis) for axis in axes]
        barrier = pltpu.get_barrier_semaphore()
        for axis, size, me in zip(axes, sizes, spots):
            for k in range(1, size):
                pl.semaphore_signal(
                    barrier, inc=1, device_id={axis: lax.rem(me + k, size)}, device_id_type=MESH
                )
        pl.semaphore_wait(barrier, sum(sizes) - len(sizes))
        for at, (axis, size, me) in enumerate(zip(axes, sizes, spots)):
            buf, send, recv = slots[at], sends[at], recvs[at]
            buf[me] = x_ref[...] if at == 0 else o_ref[...]
            for k in range(1, size):
                push(buf.at[me], buf.at[me], send.at[k], recv.at[k], {axis: lax.rem(me + k, size)}).start()
            for k in range(1, size):
                origin = lax.rem(me + size - k, size)
                push(buf.at[origin], buf.at[origin], send.at[k], recv.at[k], {axis: origin}).wait()
            total = buf[0]
            top = buf[0, high - 8 :]
            for k in range(1, size):
                total = total + buf[k]
                top = jnp.maximum(top, buf[k, high - 8 :])
            o_ref[...] = total
            o_ref[high - 8 :] = top

    dma = pltpu.SemaphoreType.DMA
    vmem = pl.BlockSpec(memory_space=pltpu.VMEM)
    scratch = []
    for size in sizes:
        scratch += [pltpu.VMEM((size,) + small.shape, FULL), dma((size,)), dma((size,))]
    return pl.pallas_call(
        kernel,
        out_shape=jax.ShapeDtypeStruct(small.shape, FULL),
        in_specs=[vmem],
        out_specs=vmem,
        scratch_shapes=scratch,
        compiler_params=params(ident, 16),
        cost_estimate=cost(14),
    )(small)


def adam_all(small, sum_rows, groups):
    high = small.shape[0]
    number = len(groups)
    arrays = [array for group in groups for array in group[:4]]
    cuts = []
    for group in range(number):
        rows, cols = arrays[4 * group].shape
        pieces = max(1, rows * cols // 262144)
        cuts += [(group, piece, rows // pieces) for piece in range(pieces)]

    def kernel(x_ref, *refs):
        sources, refs = refs[: 4 * number], refs[4 * number :]
        info_ref, outs, refs = refs[0], refs[1 : 1 + 3 * number], refs[1 + 3 * number :]
        held, load_sem, store_sem = refs[: 4 * number], refs[4 * number], refs[4 * number + 1]

        def rows_of(at):
            group, piece, rows = cuts[at]
            return pl.ds(piece * rows, rows) if rows < arrays[4 * group].shape[0] else slice(None)

        def load(at, k):
            here, array = rows_of(at), 4 * cuts[at][0] + k
            return pltpu.make_async_copy(
                sources[array].at[here], held[array].at[here], load_sem.at[at, k]
            )

        def store(at, k):
            here, group = rows_of(at), cuts[at][0]
            return pltpu.make_async_copy(
                held[4 * group + (1, 2, 0)[k]].at[here], outs[3 * group + k].at[here], store_sem.at[at, k]
            )

        for at in range(len(cuts)):
            for k in range(4):
                load(at, k).start()
        column, data_at = lax.axis_index("col"), lax.axis_index("dp")
        sums = x_ref[:sum_rows]
        squares = jnp.sum(jnp.sum(sums * sums, axis=1, keepdims=True), axis=0, keepdims=True)
        squares = squares + x_ref[sum_rows : sum_rows + 1, :1]
        norm = jnp.sqrt(squares)
        clip = CLIP / jnp.maximum(norm, CLIP)
        tops = x_ref[high - 1 :]
        lanes = lax.broadcasted_iota(jnp.int32, (1, 128), 1)
        group_size = QUERY_HEADS // KEY_VALUE_HEADS
        info_ref[0:1] = jnp.broadcast_to(norm, (1, 128))
        info_ref[1:2] = LOGIT_CAP / jnp.maximum(tops, LOGIT_CAP)

        def factor(first, count):
            chosen = (lanes >= first) & (lanes < first + count)
            top = jnp.max(jnp.where(chosen, tops, NEGATIVE), axis=1, keepdims=True)
            return jnp.sqrt(LOGIT_CAP / jnp.maximum(top, LOGIT_CAP))

        factors = {
            "query": factor(column * lax.axis_size("dp") + data_at, 1),
            "keyval": jnp.where(
                data_at < KEY_VALUE_HEADS, factor(data_at * group_size, group_size), 1.0
            ),
        }
        for at, (group, piece, rows) in enumerate(cuts):
            rate, decay, kind = groups[group][4:]
            for k in range(4):
                load(at, k).wait()
            w_ref, m_ref, v_ref, g_ref = held[4 * group : 4 * group + 4]
            cols = w_ref.shape[1]
            step = rows if rows % 8 else min(rows, max(16, 32768 // max(cols, 128)))

            def stepped(here):
                new = adamw_step(
                    w_ref[here], m_ref[here], v_ref[here], g_ref[here].astype(FULL) * clip, rate, decay
                )
                m_ref[here], v_ref[here] = new[0], new[1]
                w_ref[here] = new[2] * factors[kind] if kind else new[2]

            if step == rows:
                stepped(rows_of(at))
            else:

                @pl.loop(0, rows // step)
                def _(k):
                    stepped(pl.ds(pl.multiple_of(piece * rows + k * step, step), step))

            for k in range(3):
                store(at, k).start()
        for at in range(len(cuts)):
            for k in range(3):
                store(at, k).wait()

    dma = pltpu.SemaphoreType.DMA
    vmem, anywhere = pl.BlockSpec(memory_space=pltpu.VMEM), pl.BlockSpec(memory_space=pl.ANY)
    outs = [jax.ShapeDtypeStruct(group[0].shape, FULL) for group in groups for _ in range(3)]
    return pl.pallas_call(
        kernel,
        out_shape=[jax.ShapeDtypeStruct((8, 128), FULL)] + outs,
        in_specs=[vmem] + [anywhere] * (4 * number),
        out_specs=[vmem] + [anywhere] * (3 * number),
        scratch_shapes=[pltpu.VMEM(array.shape, array.dtype) for array in arrays]
        + [dma((len(cuts), 4)), dma((len(cuts), 3))],
        compiler_params=pltpu.CompilerParams(vmem_limit_bytes=56 * 2**20),
        cost_estimate=cost(25),
    )(small, *arrays)


def allowed_block(at, high, width, spans):
    key_places = lax.broadcasted_iota(jnp.int32, (high, width), 1)
    query_places = at * high + lax.broadcasted_iota(jnp.int32, (high, width), 0)
    seen = key_places <= query_places
    for piece in range(spans.shape[0] - 1):
        start = spans[piece + 1]
        both = (
            (key_places >= start)
            & (key_places < start + IMG)
            & (query_places >= start)
            & (query_places < start + IMG)
        )
        seen = seen | both
    return seen & (key_places < spans[0])


def softmax_block(block_rows, keys, allowed):
    scores = against(block_rows, keys)
    masked = jnp.where(allowed, scores, NEGATIVE)
    peak_row = jnp.max(masked, axis=-1, keepdims=True)
    raw_weights = jnp.where(allowed, jnp.exp(masked - peak_row), 0.0)
    return raw_weights / jnp.sum(raw_weights, axis=-1, keepdims=True), peak_row


def attention_forward_head(acts, gain, head_w, key_w, value_w, query_gain, key_gain, cos_tab, sin_tab, spans, items, ident):
    tokens, width = acts.shape
    step = 256
    bundle = Bundle(items)
    number = bundle.number

    def kernel(spans_ref, x_ref, gain_ref, qw_ref, kw_ref, vw_ref, qg_ref, kg_ref, cos_ref, sin_ref, *refs):
        x_refs, refs = refs[:number], refs[number:]
        h_ref, scale_ref, qr_ref, kr_ref, vr_ref, q_ref, k_ref, v_ref, o_ref, top_ref = refs[:10]
        o_refs, sems = refs[10 : 10 + number], refs[10 + number :]
        bundle.bind(x_refs, o_refs, sems)
        bundle.greet()
        bundle.start()

        def project(at):
            here = pl.ds(pl.multiple_of(at * step, step), step)
            rows = x_ref[here].astype(FULL)
            scale = lax.rsqrt(jnp.mean(rows * rows, axis=-1, keepdims=True) + EPS)
            scale_ref[here] = jnp.broadcast_to(scale, (step, 128))
            h_ref[here] = (rows * scale * gain_ref[...]).astype(LOW)
            hidden = h_ref[here]
            cos_rows, sin_rows = cos_ref[here], sin_ref[here]
            query = flat_dot(hidden, qw_ref[...])
            qr_ref[here] = query
            q_ref[here] = turn(whole_norm(query, qg_ref[...])[0], cos_rows, sin_rows).astype(LOW)
            key = flat_dot(hidden, kw_ref[...])
            kr_ref[here] = key
            k_ref[here] = turn(whole_norm(key, kg_ref[...])[0], cos_rows, sin_rows).astype(LOW)
            value = flat_dot(hidden, vw_ref[...])
            vr_ref[here] = value
            v_ref[here] = whole_norm(value, 1.0)[0].astype(LOW)

        def attend(at):
            here = pl.ds(pl.multiple_of(at * step, step), step)
            allowed = allowed_block(at, step, tokens, spans_ref)
            probs, peak_row = softmax_block(q_ref[here], k_ref[...], allowed)
            o_ref[here] = flat_dot(probs.astype(LOW), v_ref[...]).astype(LOW)
            top_ref[...] = jnp.maximum(top_ref[...], jnp.max(peak_row))

        top_ref[...] = jnp.full(top_ref.shape, NEGATIVE, FULL)
        pl.loop(0, tokens // step)(project)
        bundle.step(1)
        pl.loop(0, tokens // step)(attend)
        for k in range(2, bundle.sizes[0]):
            bundle.step(k)
        bundle.finish()

    vmem = pl.BlockSpec(memory_space=pltpu.VMEM)
    low = jax.ShapeDtypeStruct((tokens, HEAD_WIDTH), LOW)
    full = jax.ShapeDtypeStruct((tokens, HEAD_WIDTH), FULL)
    return pl.pallas_call(
        kernel,
        out_shape=[
            jax.ShapeDtypeStruct((tokens, width), LOW),
            jax.ShapeDtypeStruct((tokens, 128), FULL),
            full,
            full,
            full,
            low,
            low,
            low,
            low,
            jax.ShapeDtypeStruct((8, 128), FULL),
        ]
        + bundle.shapes,
        in_specs=[pl.BlockSpec(memory_space=pltpu.SMEM)] + [vmem] * 9 + bundle.specs,
        out_specs=[vmem] * 10 + bundle.specs,
        scratch_shapes=bundle.scratch,
        compiler_params=params(ident),
        cost_estimate=cost(40),
    )(spans, acts, gain, head_w, key_w, value_w, query_gain, key_gain, cos_tab, sin_tab, *bundle.sources)


def head_backward(queries, keys, values, grads, spans, items, ident):
    rows = queries.shape[0]
    step = min(256, rows)

    bundle = Bundle(items)
    number = bundle.number

    def kernel(spans_ref, q_ref, k_ref, v_ref, g_ref, *refs):
        x_refs, refs = refs[:number], refs[number:]
        dq_ref, dk_ref, dv_ref = refs[:3]
        bundle.bind(x_refs, refs[3 : 3 + number], refs[3 + number :])
        bundle.greet()
        bundle.start()
        dk_ref[...] = jnp.zeros(dk_ref.shape, FULL)
        dv_ref[...] = jnp.zeros(dv_ref.shape, FULL)

        blocks = rows // step
        ahead = min(blocks, bundle.sizes[0])

        @pl.loop(0, blocks)
        def _(at):
            @pl.when((at > 0) & (at < ahead))
            def _():
                bundle.step(at)

            here = pl.ds(pl.multiple_of(at * step, step), step)
            allowed = allowed_block(at, step, keys.shape[0], spans_ref)
            block_rows, grad_rows = q_ref[here], g_ref[here]
            probs, _ = softmax_block(block_rows, k_ref[...], allowed)
            grad_probs = against(grad_rows, v_ref[...])
            delta_row = jnp.sum(probs * grad_probs, axis=-1, keepdims=True)
            grad_scores = (probs * (grad_probs - delta_row)).astype(LOW)
            dq_ref[here] = flat_dot(grad_scores, k_ref[...])
            dk_ref[...] += inner_rows(grad_scores, block_rows)
            dv_ref[...] += inner_rows(probs.astype(LOW), grad_rows)

        for k in range(ahead, bundle.sizes[0]):
            bundle.step(k)
        bundle.finish()

    vmem = pl.BlockSpec(memory_space=pltpu.VMEM)
    return pl.pallas_call(
        kernel,
        out_shape=[jax.ShapeDtypeStruct(queries.shape, FULL)]
        + [jax.ShapeDtypeStruct(keys.shape, FULL)] * 2
        + bundle.shapes,
        in_specs=[pl.BlockSpec(memory_space=pltpu.SMEM)] + [vmem] * 4 + bundle.specs,
        out_specs=[vmem] * 3 + bundle.specs,
        scratch_shapes=bundle.scratch,
        compiler_params=params(ident),
        cost_estimate=cost(25),
    )(spans, queries, keys, values, grads, *bundle.sources)


def whole_norm(values_in, gain_vec):
    scale = lax.rsqrt(jnp.mean(values_in * values_in, axis=-1, keepdims=True) + EPS)
    return values_in * scale * gain_vec, scale


def whole_norm_backward(values_in, scale, gain_vec, grad_out):
    weighted = grad_out * gain_vec
    inner = jnp.mean(weighted * values_in, axis=-1, keepdims=True)
    return (
        scale * weighted - values_in * (scale * scale * scale) * inner,
        jnp.sum(grad_out * values_in * scale, axis=0),
    )


def turn(values_in, cos_tab, sin_tab):
    half_width = values_in.shape[-1] // 2
    one, two = values_in[:, :half_width], values_in[:, half_width:]
    return jnp.concatenate(
        [one * cos_tab - two * sin_tab, two * cos_tab + one * sin_tab], axis=1
    )


def turn_back(values_in, cos_tab, sin_tab):
    return turn(values_in, cos_tab, -sin_tab)


def line_device(
    activations,
    per_layer,
    cotangent,
    lengths,
    starts,
    w_query,
    m_query,
    v_query,
    key_value_weight,
    key_value_first_moment,
    key_value_second_moment,
    w_attend,
    m_attend,
    v_attend,
    w_gateup,
    m_gateup,
    v_gateup,
    w_down,
    m_down,
    v_down,
    w_left,
    m_left,
    v_left,
    w_right,
    m_right,
    v_right,
    w_pergate,
    m_pergate,
    v_pergate,
    w_perproj,
    m_perproj,
    v_perproj,
    w_gains,
    m_gains,
    v_gains,
    w_heads,
    m_heads,
    v_heads,
):
    rows_n = lax.axis_size("row")
    cols_n = lax.axis_size("col")
    data_n = lax.axis_size("dp")
    me = lax.axis_index("row")
    column = lax.axis_index("col")
    data_at = lax.axis_index("dp")
    half_tok, width_a = activations.shape
    tokens = half_tok * cols_n
    share = half_tok // rows_n
    quarter = tokens // rows_n
    width = width_a * rows_n

    ff_part = w_gateup.shape[2] // rows_n
    out_cols = w_down.shape[1]
    heads_here = data_n
    left_cols, right_rows = w_left.shape[1], w_right.shape[0]
    gate_cols, proj_rows = w_pergate.shape[1], w_perproj.shape[0]

    def columns_of(at, size):
        return pl.ds(pl.multiple_of(at * size, size), size)

    def across(source, by_rows):
        high, wide = source.shape
        if by_rows:
            return Swap(
                source,
                (data_n * high, wide),
                lambda ref, q: ref,
                lambda ref, at: ref.at[columns_of(at, high)],
                "dp",
            )
        return Swap(
            source,
            (high, data_n * wide),
            lambda ref, q: ref,
            lambda ref, at: ref.at[:, columns_of(at, wide)],
            "dp",
        )

    def along(source):
        high, wide = source.shape
        return Line(
            source,
            (cols_n * high, rows_n * wide),
            lambda ref, c, r: ref.at[columns_of(c, high), columns_of(r, wide)],
            True,
        )

    gateup_own, attend_own, qkv_w, left_t, right_w, pergate_t, perproj_w = transfers(
        [
            Swap(
                w_gateup.astype(LOW),
                (2, width, ff_part),
                lambda ref, q: ref.at[:, :, columns_of(q, ff_part)],
                lambda ref, at: ref.at[:, columns_of(at, width_a), :],
            ),
            Swap(
                w_attend.astype(LOW).reshape(rows_n, HEAD_WIDTH, out_cols),
                (HEAD_WIDTH, rows_n * out_cols),
                lambda ref, q: ref.at[q],
                lambda ref, at: ref.at[:, columns_of(at, out_cols)],
            ),
            Swap(
                jnp.concatenate([w_query, key_value_weight], axis=1).astype(LOW),
                (data_n, width_a, 2 * HEAD_WIDTH),
                lambda ref, q: ref,
                lambda ref, at: ref.at[at],
                "dp",
            ),
            across(w_left.T, True),
            across(w_right.astype(LOW), False),
            across(w_pergate.T.astype(LOW), True),
            across(w_perproj.astype(LOW), False),
        ],
        1,
        60,
    )
    gateup_all = lax.all_gather(gateup_own, "dp")
    query_w = qkv_w[:, :, :HEAD_WIDTH]
    kv_w = qkv_w[:, :, HEAD_WIDTH:]
    key_w = lax.dynamic_index_in_dim(kv_w, column, 0, False)
    value_w = lax.dynamic_index_in_dim(kv_w, KEY_VALUE_HEADS + column, 0, False)
    last = pl.ds(HEAD_WIDTH, HEAD_WIDTH)
    whole_acts, whole_key, whole_value, head_w, gains, extras, attend_all = transfers(
        [
            along(activations),
            Line(
                qkv_w,
                (width, HEAD_WIDTH),
                lambda ref, c, r: ref.at[columns_of(r, width_a)],
                False,
                lambda ref, c: ref.at[c, :, last],
            ),
            Line(
                qkv_w,
                (width, HEAD_WIDTH),
                lambda ref, c, r: ref.at[columns_of(r, width_a)],
                False,
                lambda ref, c: ref.at[KEY_VALUE_HEADS + c, :, last],
            ),
            Swap(
                qkv_w,
                (width, HEAD_WIDTH),
                lambda ref, q: ref.at[q, :, pl.ds(0, HEAD_WIDTH)],
                lambda ref, at: ref.at[columns_of(at, width_a)],
            ),
            Line(w_gains, (6, width), lambda ref, c, r: ref.at[:, columns_of(r, width_a)]),
            Line(
                per_layer,
                (tokens, PLD),
                lambda ref, c, r: ref.at[columns_of(r, quarter), columns_of(c, PLD // cols_n)],
                True,
            ),
            Swap(
                attend_own,
                (data_n, HEAD_WIDTH, rows_n * out_cols),
                lambda ref, q: ref,
                lambda ref, at: ref.at[at],
                "dp",
            ),
        ],
        2,
        95,
    )
    attend_w = (
        attend_all.reshape(data_n, HEAD_WIDTH, rows_n, out_cols)
        .transpose(1, 2, 0, 3)
        .reshape(HEAD_WIDTH, width)
    )
    token_at = column * half_tok + me * share
    extras = lax.dynamic_slice_in_dim(extras, token_at, share, 0).astype(FULL)
    length = lax.dynamic_index_in_dim(lengths, data_at, 0, keepdims=True)
    piece_starts = lax.dynamic_index_in_dim(starts, data_at, 0, keepdims=False)
    spans = jnp.concatenate([length, piece_starts])

    query_gain = lax.dynamic_index_in_dim(w_heads, column * rows_n + me, 0, True)
    key_gain = w_heads[QUERY_HEADS:]
    all_cos, all_sin = rope_tables(jnp.arange(tokens, dtype=jnp.int32), HEAD_WIDTH)
    own_cos = lax.dynamic_slice_in_dim(all_cos, me * quarter, quarter, 0)
    own_sin = lax.dynamic_slice_in_dim(all_sin, me * quarter, quarter, 0)
    (
        whole_hidden,
        whole_scale,
        query_raw,
        all_key_raw,
        all_value_raw,
        queries,
        keys,
        values,
        attended,
        top,
        down_own,
        left_t,
        right_w,
    ) = attention_forward_head(
        whole_acts,
        gains[:1],
        head_w,
        whole_key,
        whole_value,
        query_gain,
        key_gain,
        all_cos,
        all_sin,
        spans,
        [
            Swap(
                w_down.astype(LOW).reshape(data_n, rows_n, ff_part, out_cols),
                (data_n, ff_part, rows_n * out_cols),
                lambda ref, q: ref.at[:, q],
                lambda ref, at: ref.at[:, :, columns_of(at, out_cols)],
            ),
            along(left_t.astype(LOW)),
            along(right_w),
        ],
        3,
    )
    down_own, gateup_all = lax.optimization_barrier((down_own, gateup_all))
    down_all = lax.all_gather(down_own, "dp").reshape(data_n, data_n * ff_part, -1)
    inputs = lax.dynamic_slice_in_dim(whole_acts, token_at, share, 0).astype(FULL)
    key_raw = lax.dynamic_slice_in_dim(all_key_raw, me * quarter, quarter, 0)
    value_raw = lax.dynamic_slice_in_dim(all_value_raw, me * quarter, quarter, 0)
    _, query_scale = whole_norm(query_raw, query_gain)
    _, key_scale = whole_norm(key_raw, key_gain)
    _, value_scale = whole_norm(value_raw, 1.0)

    def shares(parts):
        return parts.astype(LOW).reshape(cols_n, rows_n, share, width)

    hidden, _ = whole_norm(inputs, gains[0])
    hidden_low = hidden.astype(LOW)
    middle = against(hidden_low, left_t).astype(LOW)
    right_raw = flat_dot(middle, right_w)
    right_n, scale_r = whole_norm(right_raw, gains[1])
    projected, pergate_t, perproj_w = transfers(
        [
            Reduce(
                shares(flat_dot(attended, attend_w)), (share, width), lambda ref, q: ref.at[q]
            ),
            along(pergate_t),
            along(perproj_w),
        ],
        5,
        45,
        30,
    )
    proj_n, scale_p = whole_norm(projected, gains[2])
    mixture = ((inputs + proj_n) + (hidden + right_n)) * HALF_ROOT
    ffn_n, scale_f = whole_norm(mixture, gains[3])
    down_raw, spread_ft, act_t, gate_raw, up_raw, upstream = ffn_forward(
        ffn_n.astype(LOW),
        gateup_all,
        down_all,
        [
            Swap(
                cotangent,
                (share, width),
                lambda ref, q: ref.at[columns_of(q, share)],
                lambda ref, at: ref.at[:, columns_of(at, width_a)],
            ),
        ],
        6,
    )
    upstream = upstream.astype(FULL)
    down_n, scale_d = whole_norm(down_raw, gains[4])
    block_out = mixture + down_n
    out_low = block_out.astype(LOW)
    pgate = against(out_low, pergate_t)
    pact = (jax.nn.gelu(pgate, approximate=True) * extras).astype(LOW)
    perproj = flat_dot(pact, perproj_w)
    perproj_n, scale_pp = whole_norm(perproj, gains[5])
    result = (block_out + perproj_n).astype(LOW)

    gain_grads = [None] * 6
    d_perproj, gain_grads[5] = whole_norm_backward(perproj, scale_pp, gains[5], upstream)
    d_perproj = d_perproj.astype(LOW)
    dw_perproj = inner_rows(pact, d_perproj)
    d_pact = against(d_perproj, perproj_w)
    _, pullback = jax.vjp(lambda v: jax.nn.gelu(v, approximate=True), pgate)
    (d_pgate,) = pullback(d_pact * extras)
    d_pgate = d_pgate.astype(LOW)
    dw_pergate = inner_rows(d_pgate, out_low)
    d_out = upstream + flat_dot(d_pgate, pergate_t)
    d_down, gain_grads[4] = whole_norm_backward(down_raw, scale_d, gains[4], d_out)
    d_ffn, dw_gateup, dw_down, result = ffn_backward(
        d_down.astype(LOW),
        gateup_all,
        down_all,
        spread_ft,
        act_t,
        gate_raw,
        up_raw,
        [
            Swap(
                result,
                (half_tok, width_a),
                lambda ref, q: ref.at[:, columns_of(q, width_a)],
                lambda ref, at: ref.at[columns_of(at, share)],
            )
        ],
        8,
    )
    g_gateup = lax.psum_scatter(dw_gateup, "dp", scatter_dimension=0)
    d_mix, gain_grads[3] = whole_norm_backward(mixture, scale_f, gains[3], d_ffn)
    d_half = (d_out + d_mix) * HALF_ROOT
    d_proj, gain_grads[2] = whole_norm_backward(projected, scale_p, gains[2], d_half)
    d_right, gain_grads[1] = whole_norm_backward(right_raw, scale_r, gains[1], d_half)
    d_right = d_right.astype(LOW)
    dw_right = inner_rows(middle, d_right)
    d_middle = against(d_right, right_w).astype(LOW)
    dw_left = inner_rows(d_middle, hidden_low)
    d_hidden_share = d_half + flat_dot(d_middle, left_t)
    inner_share = jnp.sum(d_hidden_share * gains[0] * inputs, axis=1)
    small_parts = jnp.concatenate(
        [
            grad.astype(LOW).reshape(cols_n, -1, width)
            for grad in (dw_left, dw_right, dw_pergate, dw_perproj)
        ],
        axis=1,
    )
    spread_p, small_parts = transfers(
        [
            Line(
                d_proj.astype(LOW),
                (cols_n, rows_n, share, width),
                lambda ref, c, r: ref.at[c, r],
                True,
            ),
            Reduce(
                small_parts,
                (small_parts.shape[1], width_a),
                lambda ref, q: ref.at[:, columns_of(q, width_a)],
            ),
        ],
        10,
        50,
        30,
    )
    spread_p = spread_p.reshape(tokens, width)
    d_attended = against(spread_p, attend_w).astype(LOW)
    dw_attend = inner_rows(attended, spread_p).astype(LOW)
    d_queries, d_keys, d_values, half_here, middle_here = head_backward(
        queries,
        keys,
        values,
        d_attended,
        spans,
        [
            Swap(
                d_half.astype(LOW),
                (half_tok, width_a),
                lambda ref, q: ref.at[:, columns_of(q, width_a)],
                lambda ref, at: ref.at[columns_of(at, share)],
            ),
            Line(
                d_middle, (half_tok, d_middle.shape[1]), lambda ref, c, r: ref.at[columns_of(r, share)]
            ),
        ],
        4,
    )

    small_parts = small_parts.astype(LOW)
    d_queries, dw_down, g_gateup = lax.optimization_barrier((d_queries, dw_down, g_gateup))
    g_down = lax.psum_scatter(
        dw_down.reshape(data_n, data_n, ff_part, -1), "dp", scatter_dimension=0
    )
    kv_parts = jnp.concatenate(
        [
            d_keys.astype(LOW).reshape(rows_n, quarter, HEAD_WIDTH),
            d_values.astype(LOW).reshape(rows_n, quarter, HEAD_WIDTH),
        ],
        axis=1,
    )
    d_q_raw, dg_query = whole_norm_backward(
        query_raw, query_scale, query_gain, turn_back(d_queries, all_cos, all_sin)
    )
    d_q_all, d_kv = transfers(
        [
            Line(
                d_q_raw.astype(LOW), (rows_n,) + d_q_raw.shape, lambda ref, c, r: ref.at[r]
            ),
            Reduce(kv_parts, kv_parts.shape[1:], lambda ref, q: ref.at[q], False),
        ],
        11,
        45,
        30,
    )
    d_k_raw, dg_key = whole_norm_backward(
        key_raw, key_scale, key_gain, turn_back(d_kv[:quarter], own_cos, own_sin)
    )
    d_v_raw, _ = whole_norm_backward(value_raw, value_scale, 1.0, d_kv[quarter:])
    d_raw = jnp.stack([d_k_raw, d_v_raw]).astype(LOW)
    gateup_squares = jnp.sum(jnp.square(g_gateup.astype(FULL)))
    d_kv_all, g_gateup, g_attend = transfers(
        [
            Line(
                d_raw,
                (2, tokens, HEAD_WIDTH),
                lambda ref, c, r: ref.at[:, columns_of(r, quarter)],
            ),
            Swap(
                g_gateup,
                w_gateup.shape,
                lambda ref, q: ref.at[:, columns_of(q, width_a), :],
                lambda ref, at: ref.at[:, :, columns_of(at, ff_part)],
            ),
            ShardSum(dw_attend, out_cols),
        ],
        12,
        100,
    )
    d_k_all, d_v_all = d_kv_all[0], d_kv_all[1]
    d_hidden = against(d_k_all, key_w) + against(d_v_all, value_w)
    for k in range(heads_here):
        d_hidden = d_hidden + against(d_q_all[k], query_w[k])
    acts = activations.astype(FULL)
    gains_here = lax.dynamic_slice_in_dim(w_gains, 0, 1, 0)[0]
    scale_here = lax.dynamic_slice_in_dim(whole_scale[:, :1], column * half_tok, half_tok, 0)
    own_acts = lax.dynamic_slice_in_dim(whole_acts, me * width_a, width_a, 1).astype(FULL)
    inner = jnp.sum(d_hidden * gains_here * own_acts, axis=1)
    inner = lax.dynamic_update_slice_in_dim(
        inner, lax.dynamic_slice_in_dim(inner, token_at, share, 0) + inner_share, token_at, 0
    ).reshape(-1, 128)

    spread_h = lax.dynamic_slice_in_dim(whole_hidden, me * width_a, width_a, 1)
    dw_query = jnp.stack([inner_rows(spread_h, d_q_all[k]).astype(LOW) for k in range(heads_here)])
    dw_kv = jnp.stack(
        [inner_rows(spread_h, d_k_all).astype(LOW), inner_rows(spread_h, d_v_all).astype(LOW)]
    )
    cuts = []
    start = 0
    for rows, by_rows in (
        (data_n * left_cols, True),
        (right_rows, False),
        (data_n * gate_cols, True),
        (proj_rows, False),
    ):
        cut = small_parts[start : start + rows]
        start += rows
        if by_rows:
            cut = cut.reshape(data_n, -1, width_a)
            cut = [cut[:, :, k * out_cols : (k + 1) * out_cols] for k in range(data_n)]
            cuts.append(jnp.concatenate(cut, axis=1))
        else:
            cuts.append(jnp.stack([cut[:, k * out_cols : (k + 1) * out_cols] for k in range(data_n)]))
    squares = gateup_squares
    for gradient in (g_attend, g_down):
        squares = squares + jnp.sum(jnp.square(gradient.astype(FULL)))
    g_query, g_keyval, flat_grads, g_down, g_attend, d_hidden, inner = shard_total(
        dw_query,
        dw_kv,
        jnp.concatenate(cuts, axis=1),
        [
            Swap(
                g_down,
                (data_n, rows_n, ff_part, out_cols),
                lambda ref, q: ref.at[:, :, columns_of(q, out_cols)],
                lambda ref, at: ref.at[:, at],
            ),
            Swap(
                g_attend,
                (rows_n, HEAD_WIDTH, out_cols),
                lambda ref, q: ref.at[:, columns_of(q, out_cols)],
                lambda ref, at: ref.at[at],
            ),
            Pair(d_hidden.astype(LOW).reshape(cols_n, half_tok, width_a)),
            Line(inner, (cols_n, rows_n) + inner.shape, lambda ref, c, r: ref.at[c, r], True),
        ],
        13,
    )
    squares = squares + jnp.where(column == 0, jnp.sum(g_keyval * g_keyval), 0.0)
    squares = squares + jnp.sum(g_query * g_query) + jnp.sum(flat_grads * flat_grads)
    g_down = g_down.reshape(w_down.shape)
    g_attend = g_attend.reshape(w_attend.shape)
    small_grads = []
    start = 0
    for w, by_rows in ((w_left, True), (w_right, False), (w_pergate, True), (w_perproj, False)):
        rows = w.size // out_cols
        cut = flat_grads[start : start + rows]
        start += rows
        if by_rows:
            high = rows // data_n
            cut = [cut[k * high : (k + 1) * high] for k in range(data_n)]
            cut = jnp.concatenate(cut, axis=1).T
        small_grads.append(cut)
    g_left, g_right, g_pergate, g_perproj = small_grads

    inner = jnp.sum(inner, axis=(0, 1)).reshape(cols_n, half_tok) / MODEL_WIDTH
    inner = lax.dynamic_index_in_dim(inner, column, 0, False)[:, None]
    half_here = half_here.astype(FULL)
    own_left = lax.dynamic_slice_in_dim(left_t, me * width_a, width_a, 1)
    d_hidden = d_hidden[0].astype(FULL) + d_hidden[1].astype(FULL) + half_here
    d_hidden = d_hidden + flat_dot(middle_here, own_left)
    grad_input = (
        half_here
        + scale_here * d_hidden * gains_here
        - acts * (scale_here * scale_here * scale_here) * inner
    ).astype(LOW)
    gain_zero = jnp.sum(d_hidden * acts * scale_here, axis=0)

    gain_full = jnp.stack(
        [
            lax.dynamic_update_slice_in_dim(
                jnp.zeros((width,), FULL), gain_zero, me * width_a, 0
            )
        ]
        + gain_grads[1:]
    )
    head_full = lax.dynamic_update_slice_in_dim(
        jnp.zeros((QUERY_HEADS + 1, HEAD_WIDTH), FULL), dg_query[None], column * rows_n + me, 0
    )
    head_full = head_full.at[QUERY_HEADS].add(dg_key)
    logit_row = lax.dynamic_update_slice_in_dim(
        jnp.full((128,), NEGATIVE, FULL), top[0, :1], column * rows_n + me, 0
    )
    gain_rows = gain_full.size // 128
    head_rows = head_full.size // 128
    pad_rows = -(gain_rows + head_rows) % 8
    small = jnp.concatenate(
        [
            gain_full.reshape(-1, 128),
            head_full.reshape(-1, 128),
            jnp.broadcast_to(squares, (pad_rows, 128)),
            jnp.broadcast_to(logit_row[None], (8, 128)),
        ]
    )
    small = last_sums(small, 15)
    gain_sum = small[:gain_rows].reshape(6, width)
    head_sum = small[gain_rows : gain_rows + head_rows].reshape(QUERY_HEADS + 1, HEAD_WIDTH)
    g_gains = lax.dynamic_slice_in_dim(gain_sum, me * width_a, width_a, 1)
    matrix_rate = MODEL_WIDTH ** (-0.5)

    def flat_rows_of(array):
        return array.reshape(-1, array.shape[-1])

    def kept(array):
        return array

    def turned(array):
        return array.T

    groups = [
        tuple(change(array) for array in arrays) + rest
        for arrays, change, rest in (
            ((w_gateup, m_gateup, v_gateup, g_gateup), flat_rows_of, (matrix_rate, DECAY, None)),
            ((w_down, m_down, v_down, g_down), kept, (FF ** (-0.5), DECAY, None)),
            ((w_query, m_query, v_query, g_query), kept, (matrix_rate, DECAY, "query")),
            (
                (key_value_weight, key_value_first_moment, key_value_second_moment, g_keyval),
                kept,
                (matrix_rate, DECAY, "keyval"),
            ),
            (
                (w_attend, m_attend, v_attend, g_attend),
                kept,
                ((QUERY_HEADS * HEAD_WIDTH) ** (-0.5), DECAY, None),
            ),
            ((w_left, m_left, v_left, g_left), turned, (matrix_rate, DECAY, None)),
            ((w_right, m_right, v_right, g_right), kept, (RANK ** (-0.5), DECAY, None)),
            ((w_pergate, m_pergate, v_pergate, g_pergate), turned, (matrix_rate, DECAY, None)),
            ((w_perproj, m_perproj, v_perproj, g_perproj), kept, (PLD ** (-0.5), DECAY, None)),
            ((w_gains, m_gains, v_gains, g_gains), kept, (GAIN_RATE, 0.0, None)),
            ((w_heads, m_heads, v_heads, head_sum), kept, (HEAD_RATE, 0.0, None)),
        )
    ]
    info, *stepped = adam_all(small, gain_rows + head_rows, groups)
    grad_norm = info[0, 0]
    scale_factors = info[1, :QUERY_HEADS]
    gateup, down, query, keyval, attend, left, right, pergate, perproj, gain, head = (
        stepped[3 * k : 3 * k + 3] for k in range(11)
    )
    gateup = [array.reshape(w_gateup.shape) for array in gateup]
    left = [array.T for array in left]
    pergate = [array.T for array in pergate]
    return (
        result,
        grad_input,
        grad_norm,
        scale_factors,
        *query,
        *keyval,
        *attend,
        *gateup,
        *down,
        *left,
        *right,
        *pergate,
        *perproj,
        *gain,
        *head,
    )


def per_device(
    activations,
    per_layer,
    cotangent,
    lengths,
    starts,
    w_query,
    m_query,
    v_query,
    key_value_weight,
    key_value_first_moment,
    key_value_second_moment,
    w_attend,
    m_attend,
    v_attend,
    w_gateup,
    m_gateup,
    v_gateup,
    w_down,
    m_down,
    v_down,
    w_left,
    m_left,
    v_left,
    w_right,
    m_right,
    v_right,
    w_pergate,
    m_pergate,
    v_pergate,
    w_perproj,
    m_perproj,
    v_perproj,
    w_gains,
    m_gains,
    v_gains,
    w_heads,
    m_heads,
    v_heads,
):
    row_devs = lax.axis_size("row")
    col_devs = lax.axis_size("col")
    data_devs = lax.axis_size("dp")
    row_place = lax.axis_index("row")
    column_place = lax.axis_index("col")
    data_at = lax.axis_index("dp")
    bf16 = jnp.bfloat16
    single_float = jnp.float32
    query_b, keyval_b, attend_b, gateup_b, down_b, left_b, right_b, pergate_b, perproj_b = (
        lax.all_gather(w_query.astype(bf16), "dp", axis=1, tiled=True),
        lax.all_gather(key_value_weight.astype(bf16), "dp", axis=1, tiled=True),
        lax.all_gather(w_attend.astype(bf16), "dp", axis=1, tiled=True),
        lax.all_gather(w_gateup.astype(bf16), "dp", axis=2, tiled=True),
        lax.all_gather(w_down.astype(bf16), "dp", axis=1, tiled=True),
        lax.all_gather(w_left.astype(bf16), "dp", axis=1, tiled=True),
        lax.all_gather(w_right.astype(bf16), "dp", axis=1, tiled=True),
        lax.all_gather(w_pergate.astype(bf16), "dp", axis=1, tiled=True),
        lax.all_gather(w_perproj.astype(bf16), "dp", axis=1, tiled=True),
    )
    inputs = activations.astype(single_float)
    tok_a, width_a = inputs.shape
    grouped_rows = tok_a * col_devs
    token_batch = grouped_rows // row_devs
    q_cols = query_b.shape[1]
    l_cols = left_b.shape[1]
    kv_cols = keyval_b.shape[1]
    ff_here = gateup_b.shape[2]
    local_heads = q_cols // HEAD_WIDTH
    length = lax.dynamic_index_in_dim(lengths, data_at, 0, keepdims=False)
    piece_starts = lax.dynamic_index_in_dim(starts, data_at, 0, keepdims=False)
    own_places = row_place * token_batch + jnp.arange(token_batch, dtype=jnp.int32)
    all_places = jnp.arange(grouped_rows, dtype=jnp.int32)
    own_cos, own_sin = rope_tables(own_places, HEAD_WIDTH)
    query_gains = lax.dynamic_slice_in_dim(w_heads, column_place * local_heads, local_heads, 0)
    key_gain = w_heads[QUERY_HEADS]
    hidden, scale_in = norm_forward(inputs, w_gains[0])
    hidden_b = hidden.astype(bf16)
    spread_h = spread_col(hidden_b)
    type_one = reduce_row(flat_dot(spread_h, jnp.concatenate([query_b, left_b], axis=1)))
    key_raw_all = lax.psum(flat_dot(spread_h, keyval_b), "row")
    all_cos, all_sin = rope_tables(all_places, HEAD_WIDTH)
    key_value_whole = key_form(key_raw_all, key_gain, all_cos, all_sin).astype(bf16)
    key_raw = lax.dynamic_slice_in_dim(key_raw_all, row_place * token_batch, token_batch, 0)
    query_raw = type_one[:, :q_cols]
    middle_b = type_one[:, q_cols : q_cols + l_cols].astype(bf16)
    queries = query_form(query_raw, query_gains, own_cos, own_sin).astype(bf16)
    key_value_heads = (column_place * local_heads + jnp.arange(local_heads, dtype=jnp.int32)) // (
        QUERY_HEADS // KEY_VALUE_HEADS
    )
    every_key = key_value_whole[:, : KEY_VALUE_HEADS * HEAD_WIDTH].reshape(
        grouped_rows, KEY_VALUE_HEADS, HEAD_WIDTH
    )
    every_value = key_value_whole[:, KEY_VALUE_HEADS * HEAD_WIDTH :].reshape(
        grouped_rows, KEY_VALUE_HEADS, HEAD_WIDTH
    )
    key_sel = jnp.take(every_key, key_value_heads, axis=1)
    value_sel = jnp.take(every_value, key_value_heads, axis=1)
    attended, block_peaks, block_totals = attention_forward(
        queries, key_sel, value_sel, own_places, all_places, length, piece_starts
    )
    attended_b = attended.reshape(token_batch, q_cols).astype(bf16)
    joined_b = jnp.concatenate([attended_b, middle_b], axis=1)
    spread_j = spread_row(joined_b)
    type_two = reduce_col(
        jnp.concatenate(
            [flat_dot(spread_j[:, :q_cols], attend_b), flat_dot(spread_j[:, q_cols:], right_b)],
            axis=1,
        )
    )
    projected = type_two[:, :width_a]
    right_raw = type_two[:, width_a:]
    right_n, scale_r = norm_forward(right_raw, w_gains[1])
    laurel = hidden + right_n
    proj_n, scale_p = norm_forward(projected, w_gains[2])
    gated_sum = inputs + proj_n
    mixture = (gated_sum + laurel) * HALF_ROOT
    ffn_n, scale_f = norm_forward(mixture, w_gains[3])
    ffn_b = ffn_n.astype(bf16)
    spread_f = spread_col(ffn_b)
    gateup_pair = jnp.concatenate([gateup_b[0], gateup_b[1]], axis=1)
    gate_up = reduce_row(flat_dot(spread_f, gateup_pair))
    gate_raw = gate_up[:, :ff_here]
    up_raw = gate_up[:, ff_here:]
    act_b = (jax.nn.gelu(gate_raw, approximate=True) * up_raw).astype(bf16)
    spread_a = spread_row(act_b)
    down_raw = reduce_col(flat_dot(spread_a, down_b))
    down_n, scale_d = norm_forward(down_raw, w_gains[4])
    block_out = mixture + down_n
    out_b = block_out.astype(bf16)
    spread_o = spread_col(out_b)
    pgate = reduce_row(flat_dot(spread_o, pergate_b))
    extras = per_layer.astype(single_float)
    pact_b = (jax.nn.gelu(pgate, approximate=True) * extras).astype(bf16)
    spread_p = spread_row(pact_b)
    perproj = reduce_col(flat_dot(spread_p, perproj_b))
    perproj_n, scale_pp = norm_forward(perproj, w_gains[5])
    result = (block_out + perproj_n).astype(bf16)
    upstream = cotangent.astype(single_float)
    gain_grads = [None, None, None, None, None, None]
    d_perproj, gain_grads[5] = norm_backward(perproj, scale_pp, w_gains[5], upstream)
    grads_five = grads_col(d_perproj.astype(bf16))
    dw_perproj = inner_rows(spread_p, grads_five)
    d_pact = reduce_row(against(grads_five, perproj_b))
    gelu_out, pullback = jax.vjp(lambda v: jax.nn.gelu(v, approximate=True), pgate)
    (d_pgate,) = pullback(d_pact * extras)
    grads_four = grads_row(d_pgate.astype(bf16))
    dw_pergate = inner_rows(spread_o, grads_four)
    d_out = upstream + reduce_col(against(grads_four, pergate_b))
    d_down, gain_grads[4] = norm_backward(down_raw, scale_d, w_gains[4], d_out)
    grads_three = grads_col(d_down.astype(bf16))
    dw_down = inner_rows(spread_a, grads_three)
    d_act = reduce_row(against(grads_three, down_b))
    act_out, pullback = jax.vjp(lambda a, b: jax.nn.gelu(a, approximate=True) * b, gate_raw, up_raw)
    d_gate, d_up = pullback(d_act)
    local_two = jnp.concatenate([d_gate, d_up], axis=1).astype(bf16)
    grads_two = grads_row(local_two)
    dw_gateup = jnp.stack(
        [inner_rows(spread_f, grads_two[:, :ff_here]), inner_rows(spread_f, grads_two[:, ff_here:])]
    )
    d_ffn = reduce_col(
        against(grads_two[:, :ff_here], gateup_b[0]) + against(grads_two[:, ff_here:], gateup_b[1])
    )
    d_mix_norm, gain_grads[3] = norm_backward(mixture, scale_f, w_gains[3], d_ffn)
    d_half = (d_out + d_mix_norm) * HALF_ROOT
    d_proj, gain_grads[2] = norm_backward(projected, scale_p, w_gains[2], d_half)
    d_right, gain_grads[1] = norm_backward(right_raw, scale_r, w_gains[1], d_half)
    grads_one = grads_col(jnp.concatenate([d_proj, d_right], axis=1).astype(bf16))
    dw_attend = inner_rows(spread_j[:, :q_cols], grads_one[:, :width_a])
    dw_right = inner_rows(spread_j[:, q_cols:], grads_one[:, width_a:])
    d_joined = reduce_row(
        jnp.concatenate(
            [against(grads_one[:, :width_a], attend_b), against(grads_one[:, width_a:], right_b)],
            axis=1,
        )
    )
    d_attended = d_joined[:, :q_cols].astype(bf16).reshape(token_batch, local_heads, HEAD_WIDTH)
    d_middle = d_joined[:, q_cols:]
    d_queries, d_key_sel, d_value_sel = attention_backward(
        queries,
        key_sel,
        value_sel,
        d_attended,
        block_peaks,
        block_totals,
        own_places,
        all_places,
        length,
        piece_starts,
    )
    single_hot_mask = (
        key_value_heads[:, None] == jnp.arange(KEY_VALUE_HEADS, dtype=jnp.int32)[None, :]
    ).astype(single_float)
    key_gradient = jnp.sum(d_key_sel[:, :, None, :] * single_hot_mask[None, :, :, None], axis=1)
    value_gradient = jnp.sum(d_value_sel[:, :, None, :] * single_hot_mask[None, :, :, None], axis=1)
    key_gradient, value_gradient = lax.psum((key_gradient, value_gradient), ("row", "col"))
    local_key_gradient = lax.dynamic_slice_in_dim(
        key_gradient, row_place * token_batch, token_batch, 0
    ).reshape(token_batch, KEY_VALUE_HEADS * HEAD_WIDTH)
    local_value_gradient = lax.dynamic_slice_in_dim(
        value_gradient, row_place * token_batch, token_batch, 0
    ).reshape(token_batch, KEY_VALUE_HEADS * HEAD_WIDTH)
    query_out, pullback = jax.vjp(
        lambda r, g: query_form(r, g, own_cos, own_sin), query_raw, query_gains
    )
    d_query_raw, dg_query = pullback(d_queries)
    key_tile = jnp.broadcast_to(key_gain, (token_batch, 1, HEAD_WIDTH))
    key_out, pullback = jax.vjp(lambda r, g: key_form(r, g, own_cos, own_sin), key_raw, key_tile)
    d_key_raw, dg_key_rows = pullback(
        jnp.concatenate([local_key_gradient, local_value_gradient], axis=1)
    )
    slice_rows = token_batch // col_devs
    dg_key = jnp.sum(
        lax.dynamic_slice_in_dim(dg_key_rows, column_place * slice_rows, slice_rows, 0), axis=(0, 1)
    )
    grads_zero = grads_row(jnp.concatenate([d_query_raw, d_middle, d_key_raw], axis=1).astype(bf16))
    dw_query = inner_rows(spread_h, grads_zero[:, :q_cols])
    dw_left = inner_rows(spread_h, grads_zero[:, q_cols : q_cols + l_cols])
    key_grad_rows = grads_zero[:, q_cols + l_cols :]
    dw_keyval = inner_rows(spread_h, key_grad_rows)
    slab_width = kv_cols // col_devs
    d_hidden = reduce_col(
        against(grads_zero[:, :q_cols], query_b)
        + against(grads_zero[:, q_cols : q_cols + l_cols], left_b)
        + against(
            lax.dynamic_slice_in_dim(key_grad_rows, column_place * slab_width, slab_width, 1),
            lax.dynamic_slice_in_dim(keyval_b, column_place * slab_width, slab_width, 1),
        )
    )
    d_in, gain_grads[0] = norm_backward(inputs, scale_in, w_gains[0], d_hidden + d_half)
    grad_input = (d_half + d_in).astype(bf16)
    g_query, g_keyval, g_attend, g_gateup, g_down, g_left, g_right, g_pergate, g_perproj = (
        lax.psum_scatter(dw_query, "dp", scatter_dimension=1, tiled=True),
        lax.psum_scatter(dw_keyval, "dp", scatter_dimension=1, tiled=True),
        lax.psum_scatter(dw_attend, "dp", scatter_dimension=1, tiled=True),
        lax.psum_scatter(dw_gateup, "dp", scatter_dimension=2, tiled=True),
        lax.psum_scatter(dw_down, "dp", scatter_dimension=1, tiled=True),
        lax.psum_scatter(dw_left, "dp", scatter_dimension=1, tiled=True),
        lax.psum_scatter(dw_right, "dp", scatter_dimension=1, tiled=True),
        lax.psum_scatter(dw_pergate, "dp", scatter_dimension=1, tiled=True),
        lax.psum_scatter(dw_perproj, "dp", scatter_dimension=1, tiled=True),
    )
    gain_full = lax.dynamic_update_slice_in_dim(
        jnp.zeros((6, MODEL_WIDTH), single_float), jnp.stack(gain_grads), row_place * width_a, 1
    )
    head_full = lax.dynamic_update_slice_in_dim(
        jnp.zeros((QUERY_HEADS + 1, HEAD_WIDTH), single_float),
        dg_query,
        column_place * local_heads,
        0,
    )
    head_full = head_full.at[QUERY_HEADS].add(dg_key)
    logit_here = lax.dynamic_update_slice_in_dim(
        jnp.full((QUERY_HEADS,), NEGATIVE, single_float),
        jnp.max(block_peaks, axis=(0, 2)),
        column_place * local_heads,
        0,
    )

    def combine(left_part, right_part):
        return (
            left_part[0] + right_part[0],
            left_part[1] + right_part[1],
            jnp.maximum(left_part[2], right_part[2]),
        )

    gain_sum, head_sum, logit_top = joined(
        (gain_full, head_full, logit_here), ("dp", "row", "col"), combine
    )
    g_gains = lax.dynamic_slice_in_dim(gain_sum, row_place * width_a, width_a, 1)
    lead_device = (column_place == 0) & (data_at == 0)
    solo_device = lead_device & (row_place == 0)
    squares = jnp.float32(0.0)
    for gradient in (g_query, g_attend, g_gateup, g_down, g_left, g_right, g_pergate, g_perproj):
        squares = squares + jnp.sum(gradient * gradient)
    squares = squares + jnp.where(column_place == 0, jnp.sum(g_keyval * g_keyval), 0.0)
    squares = squares + jnp.where(lead_device, jnp.sum(g_gains * g_gains), 0.0)
    squares = squares + jnp.where(solo_device, jnp.sum(head_sum * head_sum), 0.0)
    grad_norm = jnp.sqrt(lax.psum(squares, ("dp", "row", "col")))
    clip_scale = CLIP / jnp.maximum(grad_norm, CLIP)
    scale_factors = LOGIT_CAP / jnp.maximum(logit_top, LOGIT_CAP)
    weights = (
        w_query,
        key_value_weight,
        w_attend,
        w_gateup,
        w_down,
        w_left,
        w_right,
        w_pergate,
        w_perproj,
        w_gains,
        w_heads,
    )
    moments = (
        m_query,
        key_value_first_moment,
        m_attend,
        m_gateup,
        m_down,
        m_left,
        m_right,
        m_pergate,
        m_perproj,
        m_gains,
        m_heads,
    )
    seconds = (
        v_query,
        key_value_second_moment,
        v_attend,
        v_gateup,
        v_down,
        v_left,
        v_right,
        v_pergate,
        v_perproj,
        v_gains,
        v_heads,
    )
    gradients = (
        g_query,
        g_keyval,
        g_attend,
        g_gateup,
        g_down,
        g_left,
        g_right,
        g_pergate,
        g_perproj,
        g_gains,
        head_sum,
    )
    step_rates = (
        MODEL_WIDTH ** (-0.5),
        MODEL_WIDTH ** (-0.5),
        (QUERY_HEADS * HEAD_WIDTH) ** (-0.5),
        MODEL_WIDTH ** (-0.5),
        FF ** (-0.5),
        MODEL_WIDTH ** (-0.5),
        RANK ** (-0.5),
        MODEL_WIDTH ** (-0.5),
        PLD ** (-0.5),
        GAIN_RATE,
        HEAD_RATE,
    )
    decays = (DECAY, DECAY, DECAY, DECAY, DECAY, DECAY, DECAY, DECAY, DECAY, 0.0, 0.0)
    updated = [
        adamw_step(
            weights[k], moments[k], seconds[k], gradients[k] * clip_scale, step_rates[k], decays[k]
        )
        for k in range(11)
    ]
    head_scale = jnp.sqrt(scale_factors)
    q_width = w_query.shape[1]
    q_head = (
        (column_place * data_devs + data_at) * q_width + jnp.arange(q_width, dtype=jnp.int32)
    ) // HEAD_WIDTH
    q_factor = jnp.sum(
        jnp.where(
            q_head[:, None] == jnp.arange(QUERY_HEADS, dtype=jnp.int32)[None, :],
            head_scale[None, :],
            0.0,
        ),
        axis=1,
    )
    new_query = updated[0][2] * q_factor[None, :]
    kv_width = key_value_weight.shape[1]
    key_value_index = data_at * kv_width + jnp.arange(kv_width, dtype=jnp.int32)
    key_value_scale = jnp.sqrt(
        jnp.min(scale_factors.reshape(KEY_VALUE_HEADS, QUERY_HEADS // KEY_VALUE_HEADS), axis=1)
    )
    key_value_choice = jnp.sum(
        jnp.where(
            (key_value_index // HEAD_WIDTH)[:, None]
            == jnp.arange(KEY_VALUE_HEADS, dtype=jnp.int32)[None, :],
            key_value_scale[None, :],
            0.0,
        ),
        axis=1,
    )
    key_value_factor = jnp.where(
        key_value_index < KEY_VALUE_HEADS * HEAD_WIDTH, key_value_choice, 1.0
    )
    new_keyval = updated[1][2] * key_value_factor[None, :]
    return (
        result,
        grad_input,
        grad_norm,
        scale_factors,
        updated[0][0],
        updated[0][1],
        new_query,
        updated[1][0],
        updated[1][1],
        new_keyval,
        updated[2][0],
        updated[2][1],
        updated[2][2],
        updated[3][0],
        updated[3][1],
        updated[3][2],
        updated[4][0],
        updated[4][1],
        updated[4][2],
        updated[5][0],
        updated[5][1],
        updated[5][2],
        updated[6][0],
        updated[6][1],
        updated[6][2],
        updated[7][0],
        updated[7][1],
        updated[7][2],
        updated[8][0],
        updated[8][1],
        updated[8][2],
        updated[9][0],
        updated[9][1],
        updated[9][2],
        updated[10][0],
        updated[10][1],
        updated[10][2],
    )


def solution(mesh):
    placed = (
        P(("dp", "col"), "row"),
        P(("dp", "row"), "col"),
        P(("dp", "col"), "row"),
        P(),
        P(),
        P("row", ("col", "dp")),
        P("row", ("col", "dp")),
        P("row", ("col", "dp")),
        P("row", "dp"),
        P("row", "dp"),
        P("row", "dp"),
        P("col", ("row", "dp")),
        P("col", ("row", "dp")),
        P("col", ("row", "dp")),
        P(None, "row", ("col", "dp")),
        P(None, "row", ("col", "dp")),
        P(None, "row", ("col", "dp")),
        P("col", ("row", "dp")),
        P("col", ("row", "dp")),
        P("col", ("row", "dp")),
        P("row", ("col", "dp")),
        P("row", ("col", "dp")),
        P("row", ("col", "dp")),
        P("col", ("row", "dp")),
        P("col", ("row", "dp")),
        P("col", ("row", "dp")),
        P("row", ("col", "dp")),
        P("row", ("col", "dp")),
        P("row", ("col", "dp")),
        P("col", ("row", "dp")),
        P("col", ("row", "dp")),
        P("col", ("row", "dp")),
        P(None, "row"),
        P(None, "row"),
        P(None, "row"),
        P(),
        P(),
        P(),
    )
    fits = (
        mesh.shape["col"] == KEY_VALUE_HEADS
        and mesh.shape["row"] * KEY_VALUE_HEADS == QUERY_HEADS
        and mesh.shape["dp"] == mesh.shape["row"]
    )
    return jax.shard_map(
        line_device if fits else per_device,
        mesh=mesh,
        in_specs=placed,
        out_specs=(
            P(("dp", "col"), "row"),
            P(("dp", "col"), "row"),
            P(),
            P(),
            P("row", ("col", "dp")),
            P("row", ("col", "dp")),
            P("row", ("col", "dp")),
            P("row", "dp"),
            P("row", "dp"),
            P("row", "dp"),
            P("col", ("row", "dp")),
            P("col", ("row", "dp")),
            P("col", ("row", "dp")),
            P(None, "row", ("col", "dp")),
            P(None, "row", ("col", "dp")),
            P(None, "row", ("col", "dp")),
            P("col", ("row", "dp")),
            P("col", ("row", "dp")),
            P("col", ("row", "dp")),
            P("row", ("col", "dp")),
            P("row", ("col", "dp")),
            P("row", ("col", "dp")),
            P("col", ("row", "dp")),
            P("col", ("row", "dp")),
            P("col", ("row", "dp")),
            P("row", ("col", "dp")),
            P("row", ("col", "dp")),
            P("row", ("col", "dp")),
            P("col", ("row", "dp")),
            P("col", ("row", "dp")),
            P("col", ("row", "dp")),
            P(None, "row"),
            P(None, "row"),
            P(None, "row"),
            P(),
            P(),
            P(),
        ),
        check_vma=False,
    )
```

```python
import functools

import jax
import jax.numpy as jnp
from jax import lax
from jax.experimental import pallas as pl
from jax.experimental.pallas import tpu as pltpu
from jax.sharding import PartitionSpec as P

MODEL_WIDTH = 2048
QUERY_HEADS = 8
KEY_VALUE_HEADS = 2
HEAD_WIDTH = 256
FF = 8192
RANK = 64
PLD = 256
IMG = 256
STEP = 10


EPS = 1e-06
ROPE_BASE = 1000000.0
BETA_ONE = 0.5
BETA_TWO = 0.5
ADAM_EPS = 1e-08
DECAY = 0.01
CLIP = 1.0
LOGIT_CAP = 4.0
GAIN_RATE = 0.6
HEAD_RATE = 0.1
HALF_ROOT = 0.7071067811865476
NEGATIVE = -1e30


def joined(part, axis, combine):
    gathered = jax.tree.map(lambda a: lax.all_gather(a, axis), part)

    def take(source):
        return jax.tree.map(lambda a: lax.dynamic_index_in_dim(a, source, 0, False), gathered)

    return lax.fori_loop(
        1, lax.axis_size(axis), lambda source, state: combine(state, take(source)), take(0)
    )


def row_total(values_in):
    return lax.psum(values_in, "row")


def spread_col(values_in):
    return lax.all_gather(values_in, "col", axis=0, tiled=True)


def reduce_row(values_in):
    return lax.psum_scatter(values_in, "row", scatter_dimension=0, tiled=True)


def spread_row(values_in):
    return lax.all_gather(values_in, "row", axis=0, tiled=True)


def reduce_col(values_in):
    return lax.psum_scatter(values_in, "col", scatter_dimension=0, tiled=True)


def grads_col(values_in):
    return lax.all_gather(values_in, "col", axis=0, tiled=True)


def grads_row(values_in):
    return lax.all_gather(values_in, "row", axis=0, tiled=True)


def inner_rows(left_mat, right_mat):
    return lax.dot_general(
        left_mat, right_mat, (((0,), (0,)), ((), ())), preferred_element_type=jnp.float32
    )


def against(grad_mat, weight_mat):
    return lax.dot_general(
        grad_mat, weight_mat, (((1,), (1,)), ((), ())), preferred_element_type=jnp.float32
    )


def flat_dot(left_mat, right_mat):
    return jnp.dot(left_mat, right_mat, preferred_element_type=jnp.float32)


def norm_forward(values_in, gain_vec):
    total_sq = row_total(jnp.sum(values_in * values_in, axis=-1, keepdims=True))
    norm_scale = lax.rsqrt(total_sq / MODEL_WIDTH + EPS)
    return (values_in * norm_scale * gain_vec, norm_scale)


def norm_backward(values_in, norm_scale, gain_vec, grad_out):
    weighted = grad_out * gain_vec
    inner_sum = row_total(jnp.sum(weighted * values_in, axis=-1, keepdims=True))
    grad_in = norm_scale * weighted - values_in * (norm_scale * norm_scale * norm_scale) * (
        inner_sum / MODEL_WIDTH
    )
    return (grad_in, jnp.sum(grad_out * values_in * norm_scale, axis=0))


def norm_rows(values_in, gain_vec):
    return (
        values_in
        * lax.rsqrt(jnp.mean(values_in * values_in, axis=-1, keepdims=True) + EPS)
        * gain_vec
    )


def rope_tables(places, feat_width):
    half_width = feat_width // 2
    powers = jnp.arange(half_width, dtype=jnp.int32).astype(jnp.float32) * (2.0 / feat_width)
    frequency = jnp.power(jnp.float32(ROPE_BASE), -powers)
    angles = places.astype(jnp.float32)[:, None] * frequency[None, :]
    return (jnp.cos(angles), jnp.sin(angles))


def rotate(values_in, cos_tab, sin_tab):
    half_width = values_in.shape[-1] // 2
    part_one = values_in[..., :half_width]
    part_two = values_in[..., half_width:]
    cos_row = cos_tab[:, None, :]
    sin_row = sin_tab[:, None, :]
    return jnp.concatenate(
        [part_one * cos_row - part_two * sin_row, part_two * cos_row + part_one * sin_row], axis=-1
    )


def query_form(unscaled_rows, gain_rows, cos_tab, sin_tab):
    shaped = unscaled_rows.reshape(unscaled_rows.shape[0], gain_rows.shape[0], HEAD_WIDTH)
    return rotate(norm_rows(shaped, gain_rows[None]), cos_tab, sin_tab)


def key_form(unscaled_rows, gain_vec, cos_tab, sin_tab):
    count_of_rows = unscaled_rows.shape[0]
    key_rows = unscaled_rows[:, : KEY_VALUE_HEADS * HEAD_WIDTH].reshape(
        count_of_rows, KEY_VALUE_HEADS, HEAD_WIDTH
    )
    value_rows = unscaled_rows[:, KEY_VALUE_HEADS * HEAD_WIDTH :].reshape(
        count_of_rows, KEY_VALUE_HEADS, HEAD_WIDTH
    )
    key_rows = rotate(norm_rows(key_rows, gain_vec), cos_tab, sin_tab)
    value_rows = norm_rows(value_rows, 1.0)
    return jnp.concatenate(
        [
            key_rows.reshape(count_of_rows, KEY_VALUE_HEADS * HEAD_WIDTH),
            value_rows.reshape(count_of_rows, KEY_VALUE_HEADS * HEAD_WIDTH),
        ],
        axis=1,
    )


def piece_of(places, starts):
    inside = (places[:, None] >= starts[None, :]) & (places[:, None] < starts[None, :] + IMG)
    labels = jnp.arange(1, starts.shape[0] + 1, dtype=jnp.int32)
    return jnp.sum(jnp.where(inside, labels[None, :], 0), axis=1) - 1


def visible(query_places, key_places, query_pieces, key_pieces, length):
    causal = key_places[None, :] <= query_places[:, None]
    same_piece = (query_pieces[:, None] == key_pieces[None, :]) & (query_pieces[:, None] >= 0)
    return (key_places[None, :] < length) & (causal | same_piece)


def block_mask(own_places, key_places, key_pieces, length, starts):
    return visible(own_places, key_places, piece_of(own_places, starts), key_pieces, length)


def attention_forward(queries, key_sel, value_sel, own_places, key_places, length, starts):
    count_of_rows, head_count = (queries.shape[0], queries.shape[1])
    block_size = min(512, count_of_rows)
    key_pieces = piece_of(key_places, starts)
    stacked = queries.reshape(count_of_rows // block_size, block_size, head_count, HEAD_WIDTH)

    def one_block(element):
        block_rows, block_at = element
        allowed = block_mask(own_places, key_places, key_pieces, length, starts)
        scores = jnp.einsum("qhd,khd->hqk", block_rows, key_sel, preferred_element_type=jnp.float32)
        masked = jnp.where(allowed[None], scores, NEGATIVE)
        peak_row = jnp.max(masked, axis=-1, keepdims=True)
        raw_weights = jnp.where(allowed[None], jnp.exp(masked - peak_row), 0.0)
        total_row = jnp.sum(raw_weights, axis=-1, keepdims=True)
        attn_probs = (raw_weights / total_row).astype(jnp.bfloat16)
        outputs = jnp.einsum(
            "hqk,khd->qhd", attn_probs, value_sel, preferred_element_type=jnp.float32
        )
        return (outputs, peak_row[..., 0], total_row[..., 0])

    return lax.map(one_block, (stacked, jnp.arange(count_of_rows // block_size, dtype=jnp.int32)))


def attention_backward(
    queries,
    key_sel,
    value_sel,
    grad_attended,
    block_peaks,
    block_totals,
    own_places,
    key_places,
    length,
    starts,
):
    count_of_rows, head_count = (queries.shape[0], queries.shape[1])
    block_size = min(512, count_of_rows)
    block_count = count_of_rows // block_size
    key_pieces = piece_of(key_places, starts)
    stacked = queries.reshape(block_count, block_size, head_count, HEAD_WIDTH)
    grad_stacked = grad_attended.reshape(block_count, block_size, head_count, HEAD_WIDTH)

    def one_block(carry, element):
        dk_sum, dv_sum = carry
        block_rows, grad_rows, peak_row, total_row, block_at = element
        allowed = block_mask(own_places, key_places, key_pieces, length, starts)
        scores = jnp.einsum("qhd,khd->hqk", block_rows, key_sel, preferred_element_type=jnp.float32)
        masked = jnp.where(allowed[None], scores, NEGATIVE)
        raw_weights = jnp.where(allowed[None], jnp.exp(masked - peak_row[..., None]), 0.0)
        attn_probs = raw_weights / total_row[..., None]
        probs_low = attn_probs.astype(jnp.bfloat16)
        grad_probs = jnp.einsum(
            "qhd,khd->hqk", grad_rows, value_sel, preferred_element_type=jnp.float32
        )
        delta_row = jnp.sum(attn_probs * grad_probs, axis=-1, keepdims=True)
        grad_scores = (attn_probs * (grad_probs - delta_row)).astype(jnp.bfloat16)
        grad_query = jnp.einsum(
            "hqk,khd->qhd", grad_scores, key_sel, preferred_element_type=jnp.float32
        )
        dk_sum = dk_sum + jnp.einsum(
            "hqk,qhd->khd", grad_scores, block_rows, preferred_element_type=jnp.float32
        )
        dv_sum = dv_sum + jnp.einsum(
            "hqk,qhd->khd", probs_low, grad_rows, preferred_element_type=jnp.float32
        )
        return ((dk_sum, dv_sum), grad_query)

    zero_keys = jnp.zeros(key_sel.shape, jnp.float32)
    (dk_sum, dv_sum), grad_query = lax.scan(
        one_block,
        (zero_keys, zero_keys),
        (
            stacked,
            grad_stacked,
            block_peaks,
            block_totals,
            jnp.arange(block_count, dtype=jnp.int32),
        ),
    )
    return (grad_query.reshape(count_of_rows, head_count, HEAD_WIDTH), dk_sum, dv_sum)


def adamw_step(weight, moment_one, moment_two, gradient, rate, decay):
    moment_one = BETA_ONE * moment_one + (1.0 - BETA_ONE) * gradient
    moment_two = BETA_TWO * moment_two + (1.0 - BETA_TWO) * gradient * gradient
    mean_step = moment_one / (1.0 - BETA_ONE**STEP)
    spread = moment_two / (1.0 - BETA_TWO**STEP)
    return (
        moment_one,
        moment_two,
        weight - rate * (mean_step / (jnp.sqrt(spread) + ADAM_EPS) + decay * weight),
    )


MESH = pl.DeviceIdType.MESH
LOW = jnp.bfloat16
FULL = jnp.float32


def cost(micros, flops=0):
    return pl.CostEstimate(
        flops=flops, bytes_accessed=int(micros * 3.0e6), transcendentals=0
    )


def params(ident, mebibytes=48):
    return pltpu.CompilerParams(
        collective_id=ident, has_side_effects=True, vmem_limit_bytes=mebibytes * 2**20
    )


def push(source, target, send, recv, device):
    return pltpu.make_async_remote_copy(
        source, target, send, recv, device_id=device, device_id_type=MESH
    )


class Line:
    def __init__(self, source, shape, place, core=False, view=None):
        self.source, self.shape, self.place, self.core = source, shape, place, core
        self.view = view

    def semaphores(self, count, data):
        dma = pltpu.SemaphoreType.DMA
        return [dma((count,)), dma((count,)), dma((2 * count,))] * 2 + [dma]

    def bind(self, x_ref, o_ref, sems, spots, sizes):
        self.o_ref, self.sems = o_ref, sems
        self.me, self.column, self.at = spots
        self.count = sizes[0]
        self.x_ref = self.view(x_ref, self.column) if self.view else x_ref

    def slot(self, source):
        return self.place(self.o_ref, self.column, source)

    def other(self, source):
        return self.place(self.o_ref, 1 - self.column, source)

    def to_left(self, source, k, origin):
        return push(origin, self.slot(source), self.sems[0].at[k], self.sems[4].at[k], {"row": self.me - 1})

    def to_right(self, source, k, origin):
        return push(origin, self.slot(source), self.sems[1].at[k], self.sems[3].at[k], {"row": self.me + 1})

    def to_core(self, source, k, origin):
        return push(origin, self.slot(source), self.sems[2].at[k], self.sems[5].at[k], {"col": 1 - self.column})

    def from_core(self, source, k):
        there = self.other(source)
        return push(there, there, self.sems[2].at[k], self.sems[5].at[k], {"col": 1 - self.column})

    def from_left(self, source, k):
        there = self.slot(source)
        return push(there, there, self.sems[1].at[k], self.sems[3].at[k - 1], {"row": self.me - 1})

    def from_right(self, source, k):
        there = self.slot(source)
        return push(there, there, self.sems[0].at[k], self.sems[4].at[k - 1], {"row": self.me + 1})

    def own(self):
        return pltpu.make_async_copy(self.x_ref, self.slot(self.me), self.sems[6])

    def start(self):
        me, count = self.me, self.count

        @pl.when(me > 0)
        def _():
            self.to_left(me, 0, self.x_ref).start()

        @pl.when(me < count - 1)
        def _():
            self.to_right(me, 0, self.x_ref).start()

        if self.core:
            self.to_core(me, 0, self.x_ref).start()
        self.own().start()

    def step(self, k):
        me, count = self.me, self.count

        @pl.when(me - k >= 0)
        def _():
            self.from_left(me - k, k).wait_recv()
            block = self.slot(me - k)

            @pl.when(me < count - 1)
            def _():
                self.to_right(me - k, k, block).start()

            if self.core:
                self.to_core(me - k, k, block).start()

        @pl.when(me + k < count)
        def _():
            self.from_right(me + k, k).wait_recv()
            block = self.slot(me + k)

            @pl.when(me > 0)
            def _():
                self.to_left(me + k, k, block).start()

            if self.core:
                self.to_core(me + k, count - 1 + k, block).start()

    def finish(self):
        me, count = self.me, self.count
        self.own().wait()

        @pl.when(me > 0)
        def _():
            self.to_left(me, 0, self.x_ref).wait_send()

        @pl.when(me < count - 1)
        def _():
            self.to_right(me, 0, self.x_ref).wait_send()

        if self.core:
            self.to_core(me, 0, self.x_ref).wait_send()
            self.from_core(me, 0).wait_recv()

        @pl.loop(1, count)
        def _(k):
            @pl.when(me - k >= 0)
            def _():
                @pl.when(me < count - 1)
                def _():
                    self.to_right(me - k, k, self.x_ref).wait_send()

                if self.core:
                    self.to_core(me - k, k, self.x_ref).wait_send()
                    self.from_core(me - k, k).wait_recv()

            @pl.when(me + k < count)
            def _():
                @pl.when(me > 0)
                def _():
                    self.to_left(me + k, k, self.x_ref).wait_send()

                if self.core:
                    self.to_core(me + k, count - 1 + k, self.x_ref).wait_send()
                    self.from_core(me + k, count - 1 + k).wait_recv()


class Swap:
    def __init__(self, source, shape, take, place, axis="row"):
        self.source, self.shape, self.take, self.place = source, shape, take, place
        self.axis = axis

    def semaphores(self, count, data):
        size = count if self.axis == "row" else data
        return [pltpu.SemaphoreType.DMA((size,)), pltpu.SemaphoreType.DMA((size,))]

    def bind(self, x_ref, o_ref, sems, spots, sizes):
        self.x_ref, self.o_ref, self.sems = x_ref, o_ref, sems
        self.me = spots[0] if self.axis == "row" else spots[2]
        self.count = sizes[0] if self.axis == "row" else sizes[1]

    def copy(self, k):
        target = lax.rem(self.me + k, self.count)
        return push(
            self.take(self.x_ref, target),
            self.place(self.o_ref, self.me),
            self.sems[0].at[k],
            self.sems[1].at[k],
            {self.axis: target},
        )

    def own(self):
        return pltpu.make_async_copy(
            self.take(self.x_ref, self.me), self.place(self.o_ref, self.me), self.sems[0].at[0]
        )

    def start(self):
        for k in range(1, self.count):
            self.copy(k).start()
        self.own().start()

    def step(self, k):
        pass

    def finish(self):
        self.own().wait()
        for k in range(1, self.count):
            self.copy(k).wait_send()
            origin = lax.rem(self.me + self.count - k, self.count)
            there = self.place(self.o_ref, origin)
            push(there, there, self.sems[0].at[k], self.sems[1].at[k], {self.axis: origin}).wait_recv()


class Pair:
    core = True

    def __init__(self, source):
        self.source, self.shape = source, source.shape

    def semaphores(self, count, data):
        dma = pltpu.SemaphoreType.DMA
        return [dma, dma, dma]

    def bind(self, x_ref, o_ref, sems, spots, sizes):
        self.x_ref, self.o_ref, self.sems = x_ref, o_ref, sems
        self.column = spots[1]

    def copy(self):
        other = 1 - self.column
        return push(self.x_ref.at[other], self.o_ref.at[1], self.sems[0], self.sems[1], {"col": other})

    def own(self):
        return pltpu.make_async_copy(self.x_ref.at[self.column], self.o_ref.at[0], self.sems[2])

    def start(self):
        self.copy().start()
        self.own().start()

    def step(self, k):
        pass

    def finish(self):
        self.own().wait()
        self.copy().wait()


class Reduce:
    def __init__(self, source, shape, cut, core=True):
        self.source, self.shape, self.cut, self.core = source, shape, cut, core
        self.high, self.wide = shape
        self.dtype = FULL

    def semaphores(self, count, data):
        dma = pltpu.SemaphoreType.DMA
        slots = pltpu.VMEM((count,) + self.shape, self.source.dtype)
        whole = pltpu.VMEM(self.source.shape[1:] if self.core else self.source.shape, self.source.dtype)
        stage = pltpu.VMEM(self.shape, FULL)
        fourth = slots if self.core else pltpu.VMEM((1, 16, 128), self.source.dtype)
        return [whole, stage, slots, slots, slots, fourth] + [dma((count,))] * 6 + [dma, dma]

    def bind(self, x_ref, o_ref, sems, spots, sizes):
        self.x_ref, self.o_ref = x_ref, o_ref
        self.mine, self.stage, self.out, self.left_in, self.right_in, self.core_in = sems[:6]
        self.sems = sems[6:]
        self.me, self.column = spots[0], spots[1]
        self.count = sizes[0]

    def beside(self, q):
        return push(
            self.cut(self.x_ref.at[1 - self.column], q),
            self.core_in.at[q],
            self.sems[0].at[q],
            self.sems[3].at[q],
            {"col": 1 - self.column},
        )

    def to_left(self, q):
        return push(self.out.at[q], self.left_in.at[q], self.sems[1].at[q], self.sems[4].at[q], {"row": self.me - 1})

    def to_right(self, q):
        return push(self.out.at[q], self.right_in.at[q], self.sems[2].at[q], self.sems[5].at[q], {"row": self.me + 1})

    def from_right(self, q):
        return push(self.left_in.at[q], self.left_in.at[q], self.sems[1].at[q], self.sems[4].at[q], {"row": self.me + 1})

    def from_left(self, q):
        return push(self.right_in.at[q], self.right_in.at[q], self.sems[2].at[q], self.sems[5].at[q], {"row": self.me - 1})

    def own(self):
        return pltpu.make_async_copy(
            self.x_ref.at[self.column] if self.core else self.x_ref, self.mine, self.sems[6]
        )

    def start(self):
        self.own().start()
        if self.core:
            for q in range(self.count):
                self.beside(q).start()

    def added(self, target, q, others):
        step = min(self.high, max(16, 65536 // self.wide))
        while self.high % step:
            step //= 2
        cut = self.cut(self.mine, q)
        others = ([self.core_in] if self.core else []) + others

        @pl.loop(0, self.high // step)
        def _(at):
            rows = pl.ds(pl.multiple_of(at * step, step), step)
            total = cut[rows].astype(FULL)
            for other in others:
                total = total + other[q, rows].astype(FULL)
            target[rows] = total.astype(target.dtype)

    def step(self, k):
        me, count = self.me, self.count
        t = k - 1
        q_left = t - (count - 1 - me)
        q_right = count - 1 - (t - me)

        @pl.when(t == 0)
        def _():
            self.own().wait()

        @pl.when((q_left >= 0) & (q_left < me))
        def _():
            if self.core:
                self.beside(q_left).wait()

            @pl.when(me < count - 1)
            def _():
                self.from_right(q_left).wait_recv()
                self.added(self.out.at[q_left], q_left, [self.left_in])

            @pl.when(me == count - 1)
            def _():
                self.added(self.out.at[q_left], q_left, [])

            self.to_left(q_left).start()

        @pl.when((t >= me) & (q_right > me))
        def _():
            if self.core:
                self.beside(q_right).wait()

            @pl.when(me > 0)
            def _():
                self.from_left(q_right).wait_recv()
                self.added(self.out.at[q_right], q_right, [self.right_in])

            @pl.when(me == 0)
            def _():
                self.added(self.out.at[q_right], q_right, [])

            self.to_right(q_right).start()

    def finish(self):
        me, count = self.me, self.count
        if self.core:
            self.beside(me).wait()

        @pl.when(me < count - 1)
        def _():
            self.from_right(me).wait_recv()

        @pl.when(me > 0)
        def _():
            self.from_left(me).wait_recv()

        @pl.when(me == 0)
        def _():
            self.added(self.stage, me, [self.left_in])

        @pl.when(me == count - 1)
        def _():
            self.added(self.stage, me, [self.right_in])

        @pl.when((me > 0) & (me < count - 1))
        def _():
            self.added(self.stage, me, [self.left_in, self.right_in])

        out = pltpu.make_async_copy(self.stage, self.o_ref, self.sems[7])
        out.start()

        @pl.loop(0, count)
        def _(q):
            @pl.when(q < me)
            def _():
                self.to_left(q).wait_send()

            @pl.when(q > me)
            def _():
                self.to_right(q).wait_send()

        out.wait()


class ShardSum:
    axis = "dp"

    def __init__(self, source, out_cols):
        self.source, self.out_cols = source, out_cols
        self.parts = source.shape[1] // out_cols // lax.axis_size("dp")
        self.shape = (source.shape[0], self.parts * out_cols)

    def semaphores(self, count, data):
        dma = pltpu.SemaphoreType.DMA
        buf = pltpu.VMEM((data,) + self.shape, self.source.dtype)
        stage = pltpu.VMEM(self.shape, self.source.dtype)
        return [buf, stage, dma((data, self.parts)), dma((data, self.parts)), dma]

    def bind(self, x_ref, o_ref, sems, spots, sizes):
        self.x_ref, self.o_ref = x_ref, o_ref
        self.buf, self.stage, self.send, self.recv, self.local = sems
        self.at, self.data = spots[2], sizes[1]

    def copy(self, k, s):
        target = lax.rem(self.at + k, self.data)
        wide = self.out_cols
        source = self.x_ref.at[:, pl.ds(pl.multiple_of((s * self.data + target) * wide, wide), wide)]
        slot = self.buf.at[k, :, pl.ds(s * wide, wide)]
        if k == 0:
            return pltpu.make_async_copy(source, slot, self.send.at[k, s])
        return push(source, slot, self.send.at[k, s], self.recv.at[k, s], {"dp": target})

    def start(self):
        for k in range(self.data):
            for s in range(self.parts):
                self.copy(k, s).start()

    def step(self, k):
        pass

    def finish(self):
        for k in range(self.data):
            for s in range(self.parts):
                self.copy(k, s).wait()

        @pl.loop(0, self.shape[0] // 64)
        def _(at):
            rows = pl.ds(pl.multiple_of(at * 64, 64), 64)
            total = self.buf[0, rows].astype(FULL)
            for k in range(1, self.data):
                total = total + self.buf[k, rows].astype(FULL)
            self.stage[rows] = total.astype(self.stage.dtype)

        out = pltpu.make_async_copy(self.stage, self.o_ref, self.local)
        out.start()
        out.wait()


class Bundle:
    def __init__(self, items):
        self.items = items
        self.number = len(items)
        self.sizes = lax.axis_size("row"), lax.axis_size("dp")
        self.kinds = [item.semaphores(*self.sizes) for item in items]
        self.across = any(getattr(item, "axis", None) == "dp" for item in items)
        self.cores = any(getattr(item, "core", False) for item in items)
        self.sources = [item.source for item in items]
        self.shapes = [
            jax.ShapeDtypeStruct(item.shape, getattr(item, "dtype", item.source.dtype)) for item in items
        ]
        self.specs = [pl.BlockSpec(memory_space=pl.ANY)] * self.number
        self.scratch = sum(self.kinds, [])

    def bind(self, x_refs, o_refs, sems):
        self.spots = lax.axis_index("row"), lax.axis_index("col"), lax.axis_index("dp")
        for item, x_ref, o_ref, kind in zip(self.items, x_refs, o_refs, self.kinds):
            item.bind(x_ref, o_ref, sems[: len(kind)], self.spots, self.sizes)
            sems = sems[len(kind) :]

    def greet(self, across=False, cores=False):
        me, column, at = self.spots
        count, data = self.sizes
        across, cores = across or self.across, cores or self.cores
        barrier = pltpu.get_barrier_semaphore()
        for k in range(1, count):
            pl.semaphore_signal(
                barrier, inc=1, device_id={"row": lax.rem(me + k, count)}, device_id_type=MESH
            )
        if across:
            for k in range(1, data):
                pl.semaphore_signal(
                    barrier, inc=1, device_id={"dp": lax.rem(at + k, data)}, device_id_type=MESH
                )
        if cores:
            pl.semaphore_signal(barrier, inc=1, device_id={"col": 1 - column}, device_id_type=MESH)
        pl.semaphore_wait(barrier, count - 1 + (data - 1) * int(across) + int(cores))

    def start(self):
        for item in self.items:
            item.start()

    def step(self, k):
        for item in self.items:
            item.step(k)

    def finish(self):
        for item in self.items:
            item.finish()


def transfers(items, ident, micros, mebibytes=16, work=None, arrays=(), shapes=()):
    bundle = Bundle(items)
    number, given, made = bundle.number, len(arrays), len(shapes)

    def kernel(*refs):
        inputs, refs = refs[:given], refs[given:]
        x_refs, refs = refs[:number], refs[number:]
        outputs, refs = refs[:made], refs[made:]
        bundle.bind(x_refs, refs[:number], refs[number:])
        bundle.greet()
        bundle.start()
        if work:
            work(inputs, outputs)
        for k in range(1, bundle.sizes[0]):
            bundle.step(k)
        bundle.finish()

    vmem = pl.BlockSpec(memory_space=pltpu.VMEM)
    return pl.pallas_call(
        kernel,
        out_shape=list(shapes) + bundle.shapes,
        in_specs=[vmem] * given + bundle.specs,
        out_specs=[vmem] * made + bundle.specs,
        scratch_shapes=bundle.scratch,
        compiler_params=params(ident, mebibytes),
        cost_estimate=cost(micros),
    )(*arrays, *bundle.sources)


def local(function, shapes, *arrays, mebibytes=60):
    def kernel(*refs):
        results = function(*[ref[...] for ref in refs[: len(arrays)]])
        for ref, value in zip(refs[len(arrays) :], results):
            ref[...] = value.astype(ref.dtype)

    vmem = pl.BlockSpec(memory_space=pltpu.VMEM)
    return pl.pallas_call(
        kernel,
        out_shape=[jax.ShapeDtypeStruct(shape, kind) for shape, kind in shapes],
        in_specs=[vmem] * len(arrays),
        out_specs=[vmem] * len(shapes),
        compiler_params=pltpu.CompilerParams(vmem_limit_bytes=mebibytes * 2**20),
        cost_estimate=cost(5),
    )(*arrays)


def norm_back(values_in, gain, grad_out):
    scale = lax.rsqrt(jnp.mean(values_in * values_in, axis=-1, keepdims=True) + EPS)
    weighted = grad_out * gain
    inner = jnp.mean(weighted * values_in, axis=-1, keepdims=True)
    return (
        scale * weighted - values_in * (scale * scale * scale) * inner,
        jnp.sum(grad_out * values_in * scale, axis=0, keepdims=True),
    )


def mix(acts, projected, gains, left_t, right_w):
    inputs = acts.astype(FULL)
    hidden, _ = whole_norm(inputs, gains[0:1])
    hidden_low = hidden.astype(LOW)
    middle = against(hidden_low, left_t).astype(LOW)
    right_raw = flat_dot(middle, right_w)
    right_n, _ = whole_norm(right_raw, gains[1:2])
    proj_n, _ = whole_norm(projected, gains[2:3])
    mixture = ((inputs + proj_n) + (hidden + right_n)) * HALF_ROOT
    ffn_n, _ = whole_norm(mixture, gains[3:4])
    return hidden_low, middle, right_raw, mixture, ffn_n


def per_layer_both(mixture, down_raw, gains, extras, pergate_t, perproj_w, upstream):
    extras, upstream = extras.astype(FULL), upstream.astype(FULL)
    down_n, _ = whole_norm(down_raw, gains[4:5])
    block_out = mixture + down_n
    out_low = block_out.astype(LOW)
    pgate = against(out_low, pergate_t)
    curve, slope = gelu_of(pgate)
    pact = (curve * extras).astype(LOW)
    perproj = flat_dot(pact, perproj_w)
    perproj_n, _ = whole_norm(perproj, gains[5:6])
    result = block_out + perproj_n
    d_perproj, gain_five = norm_back(perproj, gains[5:6], upstream)
    d_perproj = d_perproj.astype(LOW)
    d_pact = against(d_perproj, perproj_w)
    d_pgate = (d_pact * extras * slope).astype(LOW)
    d_out = upstream + flat_dot(d_pgate, pergate_t)
    d_down, gain_four = norm_back(down_raw, gains[4:5], d_out)
    return (
        result,
        d_out,
        d_down,
        inner_rows(pact, d_perproj),
        inner_rows(d_pgate, out_low),
        gain_four,
        gain_five,
    )


def mix_back(
    d_out, d_ffn, mixture, projected, right_raw, gains, acts, left_t, right_w, hidden_low, middle, dw_pergate, dw_perproj
):
    d_mix, gain_three = norm_back(mixture, gains[3:4], d_ffn)
    d_half = (d_out + d_mix) * HALF_ROOT
    d_proj, gain_two = norm_back(projected, gains[2:3], d_half)
    d_right, gain_one = norm_back(right_raw, gains[1:2], d_half)
    d_right = d_right.astype(LOW)
    dw_right = inner_rows(middle, d_right).astype(LOW)
    d_middle = against(d_right, right_w).astype(LOW)
    dw_left = inner_rows(d_middle, hidden_low).astype(LOW)
    d_hidden = d_half + flat_dot(d_middle, left_t)
    inner = row_sums(d_hidden * gains[0:1] * acts.astype(FULL))
    parts = []
    for core in range(2):
        for grad in (dw_left, dw_right, dw_pergate, dw_perproj):
            high = grad.shape[0] // 2
            parts.append(grad[core * high : (core + 1) * high])
    return d_proj, d_half, d_middle, jnp.concatenate(parts, axis=0), inner, gain_one, gain_two, gain_three


def row_sums(values_in):
    ones = jnp.ones((8, values_in.shape[1]), FULL)
    return lax.dot_general(
        ones,
        values_in,
        (((1,), (1,)), ((), ())),
        precision=lax.Precision.HIGHEST,
        preferred_element_type=FULL,
    )


def shard_parts(sums, extents):
    out_cols, data = 128, sums.shape[1] // 128
    parts = []
    for at in range(data):
        start = 0
        for rows, by_rows in extents:
            if by_rows:
                high = rows // data
                cut = sums[start + at * high : start + (at + 1) * high]
                parts += [cut[:, k * out_cols : (k + 1) * out_cols] for k in range(data)]
            else:
                parts.append(sums[start : start + rows, at * out_cols : (at + 1) * out_cols])
            start += rows
    return jnp.concatenate(parts, axis=0)


def key_value_ends(hidden, d_key, d_value, qkv_w, d_hidden, acts, gain, sums, extents):
    first = lax.axis_index("col") == 0
    key_w = jnp.where(first, qkv_w[0, :, HEAD_WIDTH:], qkv_w[1, :, HEAD_WIDTH:])
    value_w = jnp.where(first, qkv_w[2, :, HEAD_WIDTH:], qkv_w[3, :, HEAD_WIDTH:])
    d_hidden = d_hidden + against(d_key, key_w) + against(d_value, value_w)
    return (
        jnp.concatenate([inner_rows(hidden, d_key), inner_rows(hidden, d_value)], axis=0),
        d_hidden,
        row_sums(d_hidden * gain[0:1] * acts.astype(FULL)),
        shard_parts(sums, extents),
    )


def input_ends(pair, half, middle, left_t, acts, scale, gains, inner, inner_share, grads, gateup_squares, gain_grads, dg_query, dg_key, top):
    half_tok, wide = acts.shape
    rows_n = inner.shape[1]
    width = gain_grads[0].shape[1]
    lanes = width // 128
    head_rows = (QUERY_HEADS + 1) * HEAD_WIDTH // 128
    sum_rows = 6 * lanes + head_rows
    high = -(-(sum_rows + 1) // 8) * 8 + 8
    given = (pair, half, middle, left_t, acts, scale, gains, inner, inner_share, gateup_squares, dg_query, dg_key, top)
    given += tuple(gain_grads) + tuple(grads)

    def kernel(*refs):
        pair, half, middle, left_t, acts, scale, gains, inner, inner_share, gateup_squares, dg_query, dg_key, top = refs[:13]
        gain_grads, grads = refs[13:18], refs[18:23]
        out_ref, small_ref = refs[23:]
        me, column = lax.axis_index("row"), lax.axis_index("col")
        total = None
        for core in range(2):
            for row in range(rows_n):
                part = jnp.where(
                    column == 0, inner[core, row, :, :half_tok], inner[core, row, :, half_tok:]
                )
                total = part if total is None else total + part
        shares = jnp.concatenate(
            [jnp.where(column == 0, inner_share[0, row], inner_share[1, row]) for row in range(rows_n)],
            axis=1,
        )
        mean = ((total + shares) / MODEL_WIDTH).T[:, :1]
        inputs = acts[...].astype(FULL)
        factor = scale[:, :1]
        gain = gains[0:1]
        left = left_t[:, pl.ds(pl.multiple_of(me * wide, wide), wide)]
        d_hidden = (
            pair[0].astype(FULL) + pair[1].astype(FULL) + half[...].astype(FULL) + flat_dot(middle[...], left)
        )
        out_ref[...] = (
            half[...].astype(FULL)
            + factor * (d_hidden * gain)
            - inputs * (factor * factor * factor) * mean
        ).astype(LOW)
        small_ref[...] = jnp.zeros(small_ref.shape, FULL)
        gain_zero = jnp.sum(d_hidden * inputs * factor, axis=0, keepdims=True)
        for k in range(wide // 128):
            small_ref[pl.ds(me * (wide // 128) + k, 1)] = gain_zero[:, k * 128 : (k + 1) * 128]
        for at, grad in enumerate(gain_grads):
            for k in range(lanes):
                small_ref[(at + 1) * lanes + k : (at + 1) * lanes + k + 1] = grad[:, k * 128 : (k + 1) * 128]
        head = column * rows_n + me
        for k in range(HEAD_WIDTH // 128):
            cut = slice(k * 128, (k + 1) * 128)
            small_ref[pl.ds(6 * lanes + head * (HEAD_WIDTH // 128) + k, 1)] = dg_query[:, cut]
            last = 6 * lanes + QUERY_HEADS * (HEAD_WIDTH // 128) + k
            small_ref[last : last + 1] = dg_key[:, cut]
        squares = jnp.zeros((1, 128), FULL)
        first = jnp.where(column == 0, 1.0, 0.0)
        for grad, weight in zip(grads, (1.0, first, 1.0, 1.0, 1.0)):
            values = grad[...].astype(FULL).reshape(-1, grad.shape[-1])
            line = jnp.sum(values * values, axis=0, keepdims=True)
            for cut in range(0, values.shape[1], 128):
                squares = squares + weight * line[:, cut : cut + 128]
        line = jnp.sum(gateup_squares[...], axis=0, keepdims=True)
        for cut in range(0, line.shape[1], 128):
            squares = squares + line[:, cut : cut + 128]
        small_ref[sum_rows : sum_rows + 1] = jnp.broadcast_to(
            jnp.sum(squares, axis=1, keepdims=True), (1, 128)
        )
        places = lax.broadcasted_iota(jnp.int32, (8, 128), 1)
        small_ref[high - 8 :] = jnp.where(places == head, top[...], NEGATIVE)

    vmem = pl.BlockSpec(memory_space=pltpu.VMEM)
    return pl.pallas_call(
        kernel,
        out_shape=[
            jax.ShapeDtypeStruct((half_tok, wide), LOW),
            jax.ShapeDtypeStruct((high, 128), FULL),
        ],
        in_specs=[vmem] * 23,
        out_specs=[vmem] * 2,
        compiler_params=pltpu.CompilerParams(vmem_limit_bytes=24 * 2**20),
        cost_estimate=cost(3),
    )(*given)


def key_value_back(d_kv, key_raw, value_raw, heads, cos_tab, sin_tab):
    key_gain = heads[QUERY_HEADS:]
    quarter = key_raw.shape[0]
    d_key, dg_key = norm_back(key_raw, key_gain, turn_back(d_kv[:quarter], cos_tab, sin_tab))
    d_value, _ = norm_back(value_raw, 1.0, d_kv[quarter:])
    return d_key, d_value, dg_key


def shard_total(query_parts, kv_parts, flat_parts, items, ident):
    data = lax.axis_size("dp")
    bundle = Bundle(items)
    number = bundle.number

    def kernel(q_ref, kv_ref, f_ref, *refs):
        x_refs, refs = refs[:number], refs[number:]
        oq_ref, okv_ref, of_ref = refs[:3]
        o_refs, refs = refs[3 : 3 + number], refs[3 + number :]
        q_buf, kv_buf, f_buf = refs[:3]
        sems = refs[3:11]
        bundle.bind(x_refs, o_refs, refs[11:])
        column, at = lax.axis_index("col"), lax.axis_index("dp")
        bundle.greet(True, True)
        bundle.start()
        mine = lax.rem(at, 2) == column

        def copies(k):
            target = lax.rem(at + k, data)
            device = {"dp": target}
            return (
                push(q_ref.at[target], q_buf.at[k], sems[0].at[k], sems[1].at[k], device),
                push(kv_ref.at[target // 2], kv_buf.at[k], sems[2].at[k], sems[3].at[k], device),
                push(f_ref.at[target], f_buf.at[k], sems[4].at[k], sems[5].at[k], device),
                lax.rem(target, 2) == column,
            )

        for k in range(1, data):
            query_copy, kv_copy, flat_copy, there = copies(k)
            query_copy.start()
            flat_copy.start()

            @pl.when(there)
            def _():
                kv_copy.start()

        for k in range(1, data):
            query_copy, kv_copy, flat_copy, there = copies(k)
            query_copy.wait()
            flat_copy.wait()

            @pl.when(there)
            def _():
                kv_copy.wait_send()

            @pl.when(mine)
            def _():
                kv_copy.wait_recv()

        def added(target, own, buf, chunk):
            @pl.loop(0, target.shape[0] // chunk)
            def _(step):
                rows = pl.ds(pl.multiple_of(step * chunk, chunk), chunk)
                total = own[rows].astype(FULL)
                for k in range(1, data):
                    total = total + buf[k, rows].astype(FULL)
                target[rows] = total

        share = push(okv_ref, okv_ref, sems[6], sems[7], {"col": 1 - column})

        @pl.when(mine)
        def _():
            added(okv_ref, kv_ref.at[at // 2], kv_buf, 128)
            share.start()

        added(oq_ref, q_ref.at[at], q_buf, 128)
        added(of_ref, f_ref.at[at], f_buf, 64)

        @pl.when(mine)
        def _():
            share.wait_send()

        @pl.when(jnp.logical_not(mine))
        def _():
            share.wait_recv()

        for k in range(1, bundle.sizes[0]):
            bundle.step(k)
        bundle.finish()

    vmem = pl.BlockSpec(memory_space=pltpu.VMEM)
    dma = pltpu.SemaphoreType.DMA
    shapes = [query_parts.shape[1:], kv_parts.shape[1:], flat_parts.shape[1:]]
    return pl.pallas_call(
        kernel,
        out_shape=[jax.ShapeDtypeStruct(shape, FULL) for shape in shapes] + bundle.shapes,
        in_specs=[vmem] * 3 + bundle.specs,
        out_specs=[vmem] * 3 + bundle.specs,
        scratch_shapes=[pltpu.VMEM((data,) + shape, LOW) for shape in shapes]
        + [dma((data,))] * 6
        + [dma, dma]
        + bundle.scratch,
        compiler_params=params(ident),
        cost_estimate=cost(40),
    )(query_parts, kv_parts, flat_parts, *bundle.sources)


CHUNKS = 4


class Flow:
    def __init__(self, x_ref, blocks, own, core_out, core_in, left_in, right_in, sems):
        self.x_ref, self.blocks, self.own = x_ref, blocks, own
        self.core_out, self.core_in = core_out, core_in
        self.left_in, self.right_in = left_in, right_in
        self.sems = sems
        self.me, self.column = lax.axis_index("row"), lax.axis_index("col")
        self.count = blocks.shape[0]

    @staticmethod
    def scratch(count, share, width):
        dma = pltpu.SemaphoreType.DMA
        slots = (count, share, width)
        return [
            pltpu.VMEM((count, 2, share, width), LOW),
            pltpu.VMEM(slots, FULL),
            pltpu.VMEM(slots, LOW),
            pltpu.VMEM(slots, LOW),
            pltpu.VMEM(slots, LOW),
            pltpu.VMEM(slots, LOW),
        ], [dma((count,))] * 7 + [dma((count * CHUNKS,))] * 2 + [dma((count,))] + [
            dma((count * CHUNKS,))
        ] * 2 + [dma]

    def left(self):
        return {"row": self.me - 1}

    def right(self):
        return {"row": self.me + 1}

    def beside(self):
        return {"col": 1 - self.column}

    def to_left(self, source, k, origin):
        return push(origin, self.blocks.at[source, 0], self.sems[0].at[k], self.sems[4].at[k], self.left())

    def to_right(self, source, k, origin):
        return push(origin, self.blocks.at[source, 0], self.sems[1].at[k], self.sems[3].at[k], self.right())

    def to_core(self, source, origin):
        return push(origin, self.blocks.at[source, 1], self.sems[2].at[source], self.sems[5].at[source], self.beside())

    def back_core(self, q):
        return push(self.core_out.at[q], self.core_in.at[q], self.sems[6].at[q], self.sems[9].at[q], self.beside())

    def part(self, ref, q, j):
        size = ref.shape[1] // CHUNKS
        return ref.at[q, pl.ds(pl.multiple_of(j * size, size), size)]

    def back_left(self, q, j):
        at = q * CHUNKS + j
        return push(
            self.part(self.core_out, q, j),
            self.part(self.left_in, q, j),
            self.sems[7].at[at],
            self.sems[10].at[at],
            self.left(),
        )

    def back_right(self, q, j):
        at = q * CHUNKS + j
        return push(
            self.part(self.core_out, q, j),
            self.part(self.right_in, q, j),
            self.sems[8].at[at],
            self.sems[11].at[at],
            self.right(),
        )

    def from_right(self, q, j):
        at, there = q * CHUNKS + j, self.part(self.left_in, q, j)
        return push(there, there, self.sems[7].at[at], self.sems[10].at[at], self.right())

    def from_left(self, q, j):
        at, there = q * CHUNKS + j, self.part(self.right_in, q, j)
        return push(there, there, self.sems[8].at[at], self.sems[11].at[at], self.left())

    def mine(self):
        return pltpu.make_async_copy(self.x_ref, self.blocks.at[self.me, 0], self.sems[12])

    def start(self):
        me, count = self.me, self.count

        @pl.when(me > 0)
        def _():
            self.to_left(me, 0, self.x_ref).start()

        @pl.when(me < count - 1)
        def _():
            self.to_right(me, 0, self.x_ref).start()

        self.to_core(me, self.x_ref).start()
        self.mine().start()

    def arrive(self, k):
        me, count = self.me, self.count

        @pl.when(k == 0)
        def _():
            self.mine().wait()
            self.to_core(me, self.x_ref).wait()

        @pl.when((k > 0) & (me - k >= 0))
        def _():
            source = me - k
            block = self.blocks.at[source, 0]
            push(block, block, self.sems[1].at[k], self.sems[3].at[k - 1], self.left()).wait_recv()

            @pl.when(me < count - 1)
            def _():
                self.to_right(source, k, block).start()

            self.to_core(source, block).start()

        @pl.when((k > 0) & (me + k < count))
        def _():
            source = me + k
            block = self.blocks.at[source, 0]
            push(block, block, self.sems[0].at[k], self.sems[4].at[k - 1], self.right()).wait_recv()

            @pl.when(me > 0)
            def _():
                self.to_left(source, k, block).start()

            self.to_core(source, block).start()

        @pl.when((k > 0) & (me - k >= 0))
        def _():
            self.to_core(me - k, self.x_ref).wait()

        @pl.when((k > 0) & (me + k < count))
        def _():
            self.to_core(me + k, self.x_ref).wait()

    def reach(self):
        return jnp.maximum(self.me, self.count - 1 - self.me)

    def visit(self, body, bundle, after=None):
        me, count = self.me, self.count

        @pl.loop(0, count)
        def _(k):
            self.arrive(k)

            @pl.when(k == count - 2)
            def _():
                bundle.start()

            @pl.when(k == count - 1)
            def _():
                bundle.step(1)

            @pl.loop(0, 2)
            def _(side):
                source = jnp.where(side == 0, me - k, me + k)

                @pl.when((source >= 0) & (source < count) & ((side == 0) | (k > 0)))
                def _():
                    body(source)
                    self.back_core(source).start()

            if after:
                after(k, k - self.reach() - 1)
            self.give_back(k)

    def added(self, target, terms):
        total = terms[0][...]
        for term in terms[1:]:
            total = total + term[...].astype(FULL)
        target[...] = total.astype(target.dtype)

    def give_back(self, t):
        me, count = self.me, self.count
        q_left = 2 * (count - 1) - me - t
        q_right = t - me

        def leftward():
            q = q_left
            self.back_core(q).wait()

            @pl.loop(0, CHUNKS)
            def _(j):
                base = [self.part(self.own, q, j), self.part(self.core_in, q, j)]
                target = self.part(self.core_out, q, j)

                @pl.when(me < count - 1)
                def _():
                    self.from_right(q, j).wait_recv()
                    self.added(target, base + [self.part(self.left_in, q, j)])

                @pl.when(me == count - 1)
                def _():
                    self.added(target, base)

                self.back_left(q, j).start()

        def rightward():
            q = q_right
            self.back_core(q).wait()

            @pl.loop(0, CHUNKS)
            def _(j):
                base = [self.part(self.own, q, j), self.part(self.core_in, q, j)]
                target = self.part(self.core_out, q, j)

                @pl.when(me > 0)
                def _():
                    self.from_left(q, j).wait_recv()
                    self.added(target, base + [self.part(self.right_in, q, j)])

                @pl.when(me == 0)
                def _():
                    self.added(target, base)

                self.back_right(q, j).start()

        pl.when((q_left >= 0) & (q_left < me))(leftward)
        pl.when((q_right > me) & (q_right < count))(rightward)

    def finish(self, o_ref):
        me, count = self.me, self.count
        self.back_core(me).wait()

        @pl.loop(0, CHUNKS)
        def _(j):
            size = o_ref.shape[0] // CHUNKS
            target = o_ref.at[pl.ds(pl.multiple_of(j * size, size), size)]
            base = [self.part(self.own, me, j), self.part(self.core_in, me, j)]

            @pl.when(me < count - 1)
            def _():
                self.from_right(me, j).wait_recv()

            @pl.when(me > 0)
            def _():
                self.from_left(me, j).wait_recv()

            @pl.when(me == 0)
            def _():
                self.added(target, base + [self.part(self.left_in, me, j)])

            @pl.when(me == count - 1)
            def _():
                self.added(target, base + [self.part(self.right_in, me, j)])

            @pl.when((me > 0) & (me < count - 1))
            def _():
                self.added(
                    target, base + [self.part(self.left_in, me, j), self.part(self.right_in, me, j)]
                )

        @pl.when(me > 0)
        def _():
            self.to_left(me, 0, self.x_ref).wait_send()

        @pl.when(me < count - 1)
        def _():
            self.to_right(me, 0, self.x_ref).wait_send()

        @pl.loop(1, count)
        def _(k):
            @pl.when((me - k >= 0) & (me < count - 1))
            def _():
                self.to_right(me - k, k, self.x_ref).wait_send()

            @pl.when((me + k < count) & (me > 0))
            def _():
                self.to_left(me + k, k, self.x_ref).wait_send()

        @pl.loop(0, count * CHUNKS)
        def _(at):
            q, j = at // CHUNKS, lax.rem(at, CHUNKS)

            @pl.when(q < me)
            def _():
                self.back_left(q, j).wait_send()

            @pl.when(q > me)
            def _():
                self.back_right(q, j).wait_send()


GELU_ONE = 0.7978845608028654
GELU_TWO = 0.044715


def gelu_of(values_in):
    inner = GELU_ONE * (values_in + GELU_TWO * values_in * values_in * values_in)
    bend = jnp.tanh(inner)
    half = 0.5 * (1.0 + bend)
    slope = half + 0.5 * values_in * (1.0 - bend * bend) * GELU_ONE * (
        1.0 + 3.0 * GELU_TWO * values_in * values_in
    )
    return values_in * half, slope


def ffn_forward(block, gateup, down, items, ident):
    count = lax.axis_size("row")
    share, width = block.shape
    groups, _, _, part = gateup.shape
    hidden = groups * part
    out_cols = down.shape[2] // count
    rows = 2 * share
    bundle = Bundle(items)
    number = bundle.number

    def kernel(x_ref, gw_hbm, dw_hbm, *refs):
        x_refs, refs = refs[:number], refs[number:]
        o_ref, xt_hbm, at_hbm, g_hbm, u_hbm = refs[:5]
        o_refs, scratch = refs[5 : 5 + number], refs[5 + number :]
        flow = Flow(x_ref, *scratch[:6], scratch[6:19])
        gw, dw, xt, at, act, gate, up = scratch[19:26]
        gw_sem, dw_sem, xt_sem, at_sem, g_sem, u_sem = scratch[26:32]
        bundle.bind(x_refs, o_refs, scratch[32:])
        gw_load = pltpu.make_async_copy(gw_hbm, gw, gw_sem)
        dw_load = pltpu.make_async_copy(dw_hbm, dw, dw_sem)
        gw_load.start()
        dw_load.start()
        bundle.greet(False, True)
        flow.start()
        gw_load.wait()
        dw_load.wait()

        def stores(source):
            return (
                pltpu.make_async_copy(gate.at[source], g_hbm.at[source], g_sem.at[source]),
                pltpu.make_async_copy(up.at[source], u_hbm.at[source], u_sem.at[source]),
            )

        def body(source):
            x = flow.blocks[source].reshape(rows, width)

            @pl.loop(0, groups)
            def _(d):
                columns = pl.ds(pl.multiple_of(d * part, part), part)
                g = flat_dot(x, gw[d, 0])
                u = flat_dot(x, gw[d, 1])
                gate[source, :, columns] = g
                up[source, :, columns] = u
                act[source, :, columns] = (gelu_of(g)[0] * u).astype(LOW)

            for copy in stores(source):
                copy.start()
            for d in range(groups):
                out = flat_dot(act[source], dw[d])
                for s in range(count):
                    columns = slice((s * groups + d) * out_cols, (s * groups + d + 1) * out_cols)
                    piece = out[:, s * out_cols : (s + 1) * out_cols]
                    flow.own[source, :, columns] = piece[:share]
                    flow.core_out[source, :, columns] = piece[share:].astype(LOW)

        flow.visit(body, bundle)

        @pl.loop(0, count)
        def _(source):
            here = pl.ds(pl.multiple_of(source * rows, rows), rows)
            xt[:, here] = flow.blocks[source].reshape(rows, width).T
            at[:, here] = act[source].T

        xt_store = pltpu.make_async_copy(xt, xt_hbm, xt_sem)
        at_store = pltpu.make_async_copy(at, at_hbm, at_sem)
        xt_store.start()
        at_store.start()

        @pl.loop(count, 2 * count - 2)
        def _(t):
            flow.give_back(t)

        for k in range(2, count):
            bundle.step(k)
        flow.finish(o_ref)
        bundle.finish()
        xt_store.wait()
        at_store.wait()

        @pl.loop(0, count)
        def _(source):
            for copy in stores(source):
                copy.wait()

    dma = pltpu.SemaphoreType.DMA
    buffers, sems = Flow.scratch(count, share, width)
    vmem, anywhere = pl.BlockSpec(memory_space=pltpu.VMEM), pl.BlockSpec(memory_space=pl.ANY)
    tokens = count * rows
    return pl.pallas_call(
        kernel,
        out_shape=[
            jax.ShapeDtypeStruct((share, width), FULL),
            jax.ShapeDtypeStruct((width, tokens), LOW),
            jax.ShapeDtypeStruct((hidden, tokens), LOW),
            jax.ShapeDtypeStruct((count, rows, hidden), FULL),
            jax.ShapeDtypeStruct((count, rows, hidden), FULL),
        ]
        + bundle.shapes,
        in_specs=[vmem, anywhere, anywhere] + bundle.specs,
        out_specs=[vmem] + [anywhere] * 4 + bundle.specs,
        scratch_shapes=buffers
        + sems
        + [
            pltpu.VMEM(gateup.shape, LOW),
            pltpu.VMEM(down.shape, LOW),
            pltpu.VMEM((width, tokens), LOW),
            pltpu.VMEM((hidden, tokens), LOW),
            pltpu.VMEM((count, rows, hidden), LOW),
            pltpu.VMEM((count, rows, hidden), FULL),
            pltpu.VMEM((count, rows, hidden), FULL),
        ]
        + [dma, dma, dma, dma, dma((count,)), dma((count,))]
        + bundle.scratch,
        compiler_params=params(ident, 60),
        cost_estimate=cost(80),
    )(block, gateup, down, *bundle.sources)


def ffn_backward(block, gateup, down, xt, at, gate, up, items, ident):
    count = lax.axis_size("row")
    share, width = block.shape
    groups, _, _, part = gateup.shape
    hidden = groups * part
    out_cols = down.shape[2] // count
    rows = 2 * share
    tokens = count * rows
    bundle = Bundle(items)
    number = bundle.number

    def kernel(x_ref, gw_hbm, dw_hbm, xt_hbm, at_hbm, g_hbm, u_hbm, *refs):
        x_refs, refs = refs[:number], refs[number:]
        o_ref, dgu_hbm, ddn_hbm = refs[:3]
        o_refs, scratch = refs[3 : 3 + number], refs[3 + number :]
        flow = Flow(x_ref, *scratch[:6], scratch[6:19])
        gw, dw, xt_own, at_own, gate_own, up_own, d_gate, d_up, total, stage, stage_down = scratch[19:30]
        load_sems, g_sem, u_sem, out_sem, down_sem = scratch[30:35]
        bundle.bind(x_refs, o_refs, scratch[35:])
        loads = [
            pltpu.make_async_copy(source, target, load_sems.at[k])
            for k, (source, target) in enumerate(
                [(dw_hbm, dw), (gw_hbm, gw), (xt_hbm, xt_own), (at_hbm, at_own)]
            )
        ]

        def fetches(source):
            return (
                pltpu.make_async_copy(g_hbm.at[source], gate_own.at[source], g_sem.at[source]),
                pltpu.make_async_copy(u_hbm.at[source], up_own.at[source], u_sem.at[source]),
            )

        for load in loads[:2]:
            load.start()

        @pl.loop(0, count)
        def _(source):
            for copy in fetches(source):
                copy.start()

        for load in loads[2:]:
            load.start()
        bundle.greet(False, True)
        flow.start()
        loads[0].wait()
        loads[1].wait()

        def columns_of(s, d):
            return pl.ds(pl.multiple_of((s * groups + d) * out_cols, out_cols), out_cols)

        def body(source):
            for copy in fetches(source):
                copy.wait()
            grad = flow.blocks[source].reshape(rows, width)
            d_act = None
            for d in range(groups):
                cut = jnp.concatenate(
                    [
                        grad[:, (s * groups + d) * out_cols : (s * groups + d + 1) * out_cols]
                        for s in range(count)
                    ],
                    axis=1,
                )
                term = against(cut, dw[d])
                d_act = term if d_act is None else d_act + term
            total[:, :hidden] = d_act

            @pl.loop(0, groups)
            def _(d):
                columns = pl.ds(pl.multiple_of(d * part, part), part)
                grad_act = total[:, columns]
                curve, slope = gelu_of(gate_own[source, :, columns])
                d_gate[source, :, columns] = (grad_act * up_own[source, :, columns] * slope).astype(LOW)
                d_up[source, :, columns] = (grad_act * curve).astype(LOW)

            total[...] = jnp.zeros(total.shape, FULL)

            @pl.loop(0, groups)
            def _(d):
                columns = pl.ds(pl.multiple_of(d * part, part), part)
                total[...] += against(d_gate[source, :, columns], gw[d, 0]) + against(
                    d_up[source, :, columns], gw[d, 1]
                )

            flow.own[source] = total[:share]
            flow.core_out[source] = total[share:].astype(LOW)

        def gateup_store(d, which):
            return pltpu.make_async_copy(stage.at[which], dgu_hbm.at[d, which], out_sem.at[which])

        def down_store(d):
            return pltpu.make_async_copy(stage_down, ddn_hbm.at[d], down_sem)

        def weights(d):
            columns = pl.ds(pl.multiple_of(d * part, part), part)
            for which, grads in ((0, d_gate), (1, d_up)):

                @pl.when(d > 0)
                def _():
                    gateup_store(d - 1, which).wait()

                right = grads[:, :, columns].reshape(tokens, part)

                @pl.loop(0, width // 512)
                def _(k):
                    high = pl.ds(pl.multiple_of(k * 512, 512), 512)
                    stage[which, high] = flat_dot(xt_own[high], right).astype(LOW)

                gateup_store(d, which).start()

            @pl.when(d > 0)
            def _():
                down_store(d - 1).wait()

            right = jnp.concatenate(
                [flow.blocks[:, :, :, columns_of(s, d)].reshape(tokens, out_cols) for s in range(count)],
                axis=1,
            )

            @pl.loop(0, hidden // 256)
            def _(k):
                high = pl.ds(pl.multiple_of(k * 256, 256), 256)
                stage_down[high] = flat_dot(at_own[high], right).astype(LOW)

            down_store(d).start()

        def early(k, d):
            @pl.when(k == count - 1)
            def _():
                loads[2].wait()
                loads[3].wait()

            @pl.when(d >= 0)
            def _():
                weights(d)

        flow.visit(body, bundle, early)
        done = count - 1 - flow.reach()

        @pl.loop(0, count - 2)
        def _(t):
            weights(done + t)
            flow.give_back(count + t)

        for k in range(2, count):
            bundle.step(k)

        @pl.loop(count - 2, groups)
        def _(d):
            @pl.when(d + done < groups)
            def _():
                weights(d + done)

        for which in range(2):
            gateup_store(groups - 1, which).wait()
        down_store(groups - 1).wait()
        flow.finish(o_ref)
        bundle.finish()

    dma = pltpu.SemaphoreType.DMA
    buffers, sems = Flow.scratch(count, share, width)
    vmem, anywhere = pl.BlockSpec(memory_space=pltpu.VMEM), pl.BlockSpec(memory_space=pl.ANY)
    return pl.pallas_call(
        kernel,
        out_shape=[
            jax.ShapeDtypeStruct((share, width), FULL),
            jax.ShapeDtypeStruct(gateup.shape, LOW),
            jax.ShapeDtypeStruct(down.shape, LOW),
        ]
        + bundle.shapes,
        in_specs=[vmem] + [anywhere] * 6 + bundle.specs,
        out_specs=[vmem, anywhere, anywhere] + bundle.specs,
        scratch_shapes=buffers
        + sems
        + [
            pltpu.VMEM(gateup.shape, LOW),
            pltpu.VMEM(down.shape, LOW),
            pltpu.VMEM((width, tokens), LOW),
            pltpu.VMEM((hidden, tokens), LOW),
            pltpu.VMEM((count, rows, hidden), FULL),
            pltpu.VMEM((count, rows, hidden), FULL),
            pltpu.VMEM((count, rows, hidden), LOW),
            pltpu.VMEM((count, rows, hidden), LOW),
            pltpu.VMEM((rows, width), FULL),
            pltpu.VMEM((2, width, part), LOW),
            pltpu.VMEM((hidden, count * out_cols), LOW),
        ]
        + [dma((4,)), dma((count,)), dma((count,)), dma((2,)), dma]
        + bundle.scratch,
        compiler_params=params(ident, 62),
        cost_estimate=cost(90),
    )(block, gateup, down, xt, at, gate, up, *bundle.sources)


def last_sums(small, ident):
    axes = ("col", "row", "dp")
    sizes = [lax.axis_size(axis) for axis in axes]
    high = small.shape[0]

    def kernel(x_ref, o_ref, *refs):
        slots, sends, recvs = (refs[k::3] for k in range(3))
        spots = [lax.axis_index(axis) for axis in axes]
        barrier = pltpu.get_barrier_semaphore()
        for axis, size, me in zip(axes, sizes, spots):
            for k in range(1, size):
                pl.semaphore_signal(
                    barrier, inc=1, device_id={axis: lax.rem(me + k, size)}, device_id_type=MESH
                )
        pl.semaphore_wait(barrier, sum(sizes) - len(sizes))
        for at, (axis, size, me) in enumerate(zip(axes, sizes, spots)):
            buf, send, recv = slots[at], sends[at], recvs[at]
            buf[me] = x_ref[...] if at == 0 else o_ref[...]
            for k in range(1, size):
                push(buf.at[me], buf.at[me], send.at[k], recv.at[k], {axis: lax.rem(me + k, size)}).start()
            for k in range(1, size):
                origin = lax.rem(me + size - k, size)
                push(buf.at[origin], buf.at[origin], send.at[k], recv.at[k], {axis: origin}).wait()
            total = buf[0]
            top = buf[0, high - 8 :]
            for k in range(1, size):
                total = total + buf[k]
                top = jnp.maximum(top, buf[k, high - 8 :])
            o_ref[...] = total
            o_ref[high - 8 :] = top

    dma = pltpu.SemaphoreType.DMA
    vmem = pl.BlockSpec(memory_space=pltpu.VMEM)
    scratch = []
    for size in sizes:
        scratch += [pltpu.VMEM((size,) + small.shape, FULL), dma((size,)), dma((size,))]
    return pl.pallas_call(
        kernel,
        out_shape=jax.ShapeDtypeStruct(small.shape, FULL),
        in_specs=[vmem],
        out_specs=vmem,
        scratch_shapes=scratch,
        compiler_params=params(ident, 16),
        cost_estimate=cost(14),
    )(small)


def adam_all(small, sum_rows, groups):
    high = small.shape[0]
    number = len(groups)
    arrays = [array for group in groups for array in group[:4]]
    cuts = []
    for group in range(number):
        rows, cols = arrays[4 * group].shape
        pieces = max(1, rows * cols // 262144)
        cuts += [(group, piece, rows // pieces) for piece in range(pieces)]

    def kernel(x_ref, *refs):
        sources, refs = refs[: 4 * number], refs[4 * number :]
        norm_ref, factor_ref = refs[:2]
        outs, refs = refs[2 : 2 + 3 * number], refs[2 + 3 * number :]
        held, load_sem, store_sem = refs[: 4 * number], refs[4 * number], refs[4 * number + 1]

        def rows_of(at):
            group, piece, rows = cuts[at]
            return pl.ds(piece * rows, rows) if rows < arrays[4 * group].shape[0] else slice(None)

        def load(at, k):
            here, array = rows_of(at), 4 * cuts[at][0] + k
            return pltpu.make_async_copy(
                sources[array].at[here], held[array].at[here], load_sem.at[at, k]
            )

        def store(at, k):
            here, group = rows_of(at), cuts[at][0]
            return pltpu.make_async_copy(
                held[4 * group + (1, 2, 0)[k]].at[here], outs[3 * group + k].at[here], store_sem.at[at, k]
            )

        for at in range(len(cuts)):
            for k in range(4):
                load(at, k).start()
        column, data_at = lax.axis_index("col"), lax.axis_index("dp")
        sums = x_ref[:sum_rows]
        squares = jnp.sum(jnp.sum(sums * sums, axis=1, keepdims=True), axis=0, keepdims=True)
        squares = squares + x_ref[sum_rows : sum_rows + 1, :1]
        norm = jnp.sqrt(squares)
        clip = CLIP / jnp.maximum(norm, CLIP)
        tops = x_ref[high - 1 :]
        lanes = lax.broadcasted_iota(jnp.int32, (1, 128), 1)
        group_size = QUERY_HEADS // KEY_VALUE_HEADS
        norm_ref[...] = norm
        factor_ref[...] = (LOGIT_CAP / jnp.maximum(tops, LOGIT_CAP))[:, :QUERY_HEADS]

        def factor(first, count):
            chosen = (lanes >= first) & (lanes < first + count)
            top = jnp.max(jnp.where(chosen, tops, NEGATIVE), axis=1, keepdims=True)
            return jnp.sqrt(LOGIT_CAP / jnp.maximum(top, LOGIT_CAP))

        factors = {
            "query": factor(column * lax.axis_size("dp") + data_at, 1),
            "keyval": jnp.where(
                data_at < KEY_VALUE_HEADS, factor(data_at * group_size, group_size), 1.0
            ),
        }
        for at, (group, piece, rows) in enumerate(cuts):
            rate, decay, kind = groups[group][4:]
            for k in range(4):
                load(at, k).wait()
            w_ref, m_ref, v_ref, g_ref = held[4 * group : 4 * group + 4]
            cols = w_ref.shape[1]
            step = rows if rows % 8 else min(rows, max(16, 32768 // max(cols, 128)))

            def stepped(here):
                new = adamw_step(
                    w_ref[here], m_ref[here], v_ref[here], g_ref[here].astype(FULL) * clip, rate, decay
                )
                m_ref[here], v_ref[here] = new[0], new[1]
                w_ref[here] = new[2] * factors[kind] if kind else new[2]

            if step == rows:
                stepped(rows_of(at))
            else:

                @pl.loop(0, rows // step)
                def _(k):
                    stepped(pl.ds(pl.multiple_of(piece * rows + k * step, step), step))

            for k in range(3):
                store(at, k).start()
        for at in range(len(cuts)):
            for k in range(3):
                store(at, k).wait()

    dma = pltpu.SemaphoreType.DMA
    vmem, anywhere = pl.BlockSpec(memory_space=pltpu.VMEM), pl.BlockSpec(memory_space=pl.ANY)
    outs = [jax.ShapeDtypeStruct(group[0].shape, FULL) for group in groups for _ in range(3)]
    return pl.pallas_call(
        kernel,
        out_shape=[
            jax.ShapeDtypeStruct((1, 1), FULL),
            jax.ShapeDtypeStruct((1, QUERY_HEADS), FULL),
        ]
        + outs,
        in_specs=[vmem] + [anywhere] * (4 * number),
        out_specs=[vmem] * 2 + [anywhere] * (3 * number),
        scratch_shapes=[pltpu.VMEM(array.shape, array.dtype) for array in arrays]
        + [dma((len(cuts), 4)), dma((len(cuts), 3))],
        compiler_params=pltpu.CompilerParams(vmem_limit_bytes=56 * 2**20),
        cost_estimate=cost(25),
    )(small, *arrays)


def allowed_block(at, high, width, spans):
    key_places = lax.broadcasted_iota(jnp.int32, (high, width), 1)
    query_places = at * high + lax.broadcasted_iota(jnp.int32, (high, width), 0)
    seen = key_places <= query_places
    for start in spans[1:]:
        both = (
            (key_places >= start)
            & (key_places < start + IMG)
            & (query_places >= start)
            & (query_places < start + IMG)
        )
        seen = seen | both
    return seen & (key_places < spans[0])


def softmax_block(block_rows, keys, allowed):
    scores = against(block_rows, keys)
    masked = jnp.where(allowed, scores, NEGATIVE)
    peak_row = jnp.max(masked, axis=-1, keepdims=True)
    raw_weights = jnp.where(allowed, jnp.exp(masked - peak_row), 0.0)
    return raw_weights / jnp.sum(raw_weights, axis=-1, keepdims=True), peak_row


def spans_of(lengths_ref, starts_ref):
    at = lax.axis_index("dp")
    return [lengths_ref[at]] + [starts_ref[at, piece] for piece in range(starts_ref.shape[1])]


def attention_forward_head(acts, gains, head_w, key_w, value_w, heads, cos_tab, sin_tab, extras, lengths, starts, items, ident):
    tokens, width = acts.shape
    step = 256
    bundle = Bundle(items)
    number = bundle.number
    rows_n, cols_n = lax.axis_size("row"), lax.axis_size("col")
    half_tok, wide = tokens // cols_n, width // rows_n
    share, quarter = half_tok // rows_n, tokens // rows_n

    def kernel(l_ref, s_ref, x_ref, gain_ref, qw_ref, kw_ref, vw_ref, heads_ref, cos_ref, sin_ref, e_ref, *refs):
        x_refs, refs = refs[:number], refs[number:]
        hidden_ref, acts_ref, share_ref, scale_ref, qr_ref, kr_ref, vr_ref = refs[:7]
        q_ref, k_ref, v_ref, o_ref, top_ref, es_ref, oc_ref, os_ref = refs[7:15]
        o_refs, refs = refs[15 : 15 + number], refs[15 + number :]
        h_ref, sc_ref, key_ref, value_ref = refs[:4]
        bundle.bind(x_refs, o_refs, refs[4:])
        bundle.greet()
        bundle.start()
        me, column = lax.axis_index("row"), lax.axis_index("col")
        spans = spans_of(l_ref, s_ref)
        query_gain, key_gain = heads_ref[pl.ds(column * rows_n + me, 1)], heads_ref[QUERY_HEADS:]

        def project(at):
            here = pl.ds(pl.multiple_of(at * step, step), step)
            rows = x_ref[here].astype(FULL)
            scale = lax.rsqrt(jnp.mean(rows * rows, axis=-1, keepdims=True) + EPS)
            sc_ref[here] = jnp.broadcast_to(scale, (step, 128))
            h_ref[here] = (rows * scale * gain_ref[0:1]).astype(LOW)
            hidden = h_ref[here]
            cos_rows, sin_rows = cos_ref[here], sin_ref[here]
            query = flat_dot(hidden, qw_ref[...])
            qr_ref[here] = query
            q_ref[here] = turn(whole_norm(query, query_gain)[0], cos_rows, sin_rows).astype(LOW)
            key = flat_dot(hidden, kw_ref[...])
            key_ref[here] = key
            k_ref[here] = turn(whole_norm(key, key_gain)[0], cos_rows, sin_rows).astype(LOW)
            value = flat_dot(hidden, vw_ref[...])
            value_ref[here] = value
            v_ref[here] = whole_norm(value, 1.0)[0].astype(LOW)

        def attend(at):
            here = pl.ds(pl.multiple_of(at * step, step), step)
            allowed = allowed_block(at, step, tokens, spans)
            probs, peak_row = softmax_block(q_ref[here], k_ref[...], allowed)
            o_ref[here] = flat_dot(probs.astype(LOW), v_ref[...]).astype(LOW)
            top_ref[...] = jnp.maximum(top_ref[...], jnp.max(peak_row))

        top_ref[...] = jnp.full(top_ref.shape, NEGATIVE, FULL)
        blocks = tokens // step
        half = max(blocks // 2, 1)
        pl.loop(0, half)(project)
        bundle.step(1)
        pl.loop(half, blocks)(project)
        bundle.step(2)
        pl.loop(0, half)(attend)
        for k in range(3, bundle.sizes[0]):
            bundle.step(k)
        pl.loop(half, blocks)(attend)
        columns = pl.ds(pl.multiple_of(me * wide, wide), wide)

        @pl.loop(0, blocks)
        def _(at):
            here = pl.ds(pl.multiple_of(at * step, step), step)
            hidden_ref[here] = h_ref[here, columns]
            acts_ref[here] = x_ref[here, columns]

        mine = pl.ds(pl.multiple_of(column * half_tok + me * share, share), share)
        share_ref[...] = x_ref[mine]
        es_ref[...] = e_ref[mine]
        scale_ref[...] = sc_ref[pl.ds(pl.multiple_of(column * half_tok, half_tok), half_tok)]
        fourth = pl.ds(pl.multiple_of(me * quarter, quarter), quarter)
        kr_ref[...] = key_ref[fourth]
        vr_ref[...] = value_ref[fourth]
        oc_ref[...] = cos_ref[fourth]
        os_ref[...] = sin_ref[fourth]
        bundle.finish()

    vmem = pl.BlockSpec(memory_space=pltpu.VMEM)
    smem = pl.BlockSpec(memory_space=pltpu.SMEM)

    def low(*shape):
        return jax.ShapeDtypeStruct(shape, LOW)

    def full(*shape):
        return jax.ShapeDtypeStruct(shape, FULL)

    return pl.pallas_call(
        kernel,
        out_shape=[
            low(tokens, wide),
            low(tokens, wide),
            low(share, width),
            full(half_tok, 128),
            full(tokens, HEAD_WIDTH),
            full(quarter, HEAD_WIDTH),
            full(quarter, HEAD_WIDTH),
            low(tokens, HEAD_WIDTH),
            low(tokens, HEAD_WIDTH),
            low(tokens, HEAD_WIDTH),
            low(tokens, HEAD_WIDTH),
            full(8, 128),
            low(share, PLD),
            full(quarter, HEAD_WIDTH // 2),
            full(quarter, HEAD_WIDTH // 2),
        ]
        + bundle.shapes,
        in_specs=[smem, smem] + [vmem] * 9 + bundle.specs,
        out_specs=[vmem] * 15 + bundle.specs,
        scratch_shapes=[
            pltpu.VMEM((tokens, width), LOW),
            pltpu.VMEM((tokens, 128), FULL),
            pltpu.VMEM((tokens, HEAD_WIDTH), FULL),
            pltpu.VMEM((tokens, HEAD_WIDTH), FULL),
        ]
        + bundle.scratch,
        compiler_params=params(ident, 60),
        cost_estimate=cost(40),
    )(lengths, starts, acts, gains, head_w, key_w, value_w, heads, cos_tab, sin_tab, extras, *bundle.sources)


def head_backward(queries, keys, values, attended, grads, attend_w, query_raw, heads, cos_tab, sin_tab, lengths, starts, items, ident):
    rows = queries.shape[0]
    step = min(256, rows)
    bundle = Bundle(items)
    number = bundle.number
    devices = lax.axis_size("row")
    quarter = rows // devices

    def kernel(l_ref, s_ref, q_ref, k_ref, v_ref, a_ref, g_ref, w_ref, r_ref, heads_ref, cos_ref, sin_ref, *refs):
        x_refs, refs = refs[:number], refs[number:]
        dq_ref, kv_ref, dg_ref, dw_ref = refs[:4]
        o_refs, refs = refs[4 : 4 + number], refs[4 + number :]
        dk_ref, dv_ref = refs[:2]
        bundle.bind(x_refs, o_refs, refs[2:])
        bundle.greet()
        bundle.start()
        spans = spans_of(l_ref, s_ref)
        gain = heads_ref[pl.ds(lax.axis_index("col") * devices + lax.axis_index("row"), 1)]
        dk_ref[...] = jnp.zeros(dk_ref.shape, FULL)
        dv_ref[...] = jnp.zeros(dv_ref.shape, FULL)
        dg_ref[...] = jnp.zeros(dg_ref.shape, FULL)

        @pl.loop(0, rows // step)
        def _(at):
            here = pl.ds(pl.multiple_of(at * step, step), step)
            allowed = allowed_block(at, step, keys.shape[0], spans)
            block_rows, grad_rows = q_ref[here], against(g_ref[here], w_ref[...]).astype(LOW)
            probs, _ = softmax_block(block_rows, k_ref[...], allowed)
            grad_probs = against(grad_rows, v_ref[...])
            delta_row = jnp.sum(probs * grad_probs, axis=-1, keepdims=True)
            grad_scores = (probs * (grad_probs - delta_row)).astype(LOW)
            d_query = turn_back(flat_dot(grad_scores, k_ref[...]), cos_ref[here], sin_ref[here])
            d_query, d_gain = norm_back(r_ref[here], gain, d_query)
            dq_ref[here] = d_query.astype(LOW)
            dg_ref[...] += d_gain
            dk_ref[...] += inner_rows(grad_scores, block_rows)
            dv_ref[...] += inner_rows(probs.astype(LOW), grad_rows)

        for device in range(devices):
            cut = slice(device * quarter, (device + 1) * quarter)
            kv_ref[device, :quarter] = dk_ref[cut].astype(LOW)
            kv_ref[device, quarter:] = dv_ref[cut].astype(LOW)
        for cut in range(0, grads.shape[1], 512):
            dw_ref[:, cut : cut + 512] = inner_rows(a_ref[...], g_ref[:, cut : cut + 512]).astype(LOW)
        for k in range(1, bundle.sizes[0]):
            bundle.step(k)
        bundle.finish()

    vmem = pl.BlockSpec(memory_space=pltpu.VMEM)
    return pl.pallas_call(
        kernel,
        out_shape=[
            jax.ShapeDtypeStruct(queries.shape, LOW),
            jax.ShapeDtypeStruct((devices, 2 * quarter, HEAD_WIDTH), LOW),
            jax.ShapeDtypeStruct((1, HEAD_WIDTH), FULL),
            jax.ShapeDtypeStruct((HEAD_WIDTH, grads.shape[1]), LOW),
        ]
        + bundle.shapes,
        in_specs=[pl.BlockSpec(memory_space=pltpu.SMEM)] * 2 + [vmem] * 10 + bundle.specs,
        out_specs=[vmem] * 4 + bundle.specs,
        scratch_shapes=[pltpu.VMEM(keys.shape, FULL)] * 2 + bundle.scratch,
        compiler_params=params(ident, 60),
        cost_estimate=cost(25),
    )(
        lengths, starts, queries, keys, values, attended, grads, attend_w, query_raw, heads, cos_tab, sin_tab, *bundle.sources
    )


def whole_norm(values_in, gain_vec):
    scale = lax.rsqrt(jnp.mean(values_in * values_in, axis=-1, keepdims=True) + EPS)
    return values_in * scale * gain_vec, scale


def whole_norm_backward(values_in, scale, gain_vec, grad_out):
    weighted = grad_out * gain_vec
    inner = jnp.mean(weighted * values_in, axis=-1, keepdims=True)
    return (
        scale * weighted - values_in * (scale * scale * scale) * inner,
        jnp.sum(grad_out * values_in * scale, axis=0),
    )


def turn(values_in, cos_tab, sin_tab):
    half_width = values_in.shape[-1] // 2
    one, two = values_in[:, :half_width], values_in[:, half_width:]
    return jnp.concatenate(
        [one * cos_tab - two * sin_tab, two * cos_tab + one * sin_tab], axis=1
    )


def turn_back(values_in, cos_tab, sin_tab):
    return turn(values_in, cos_tab, -sin_tab)


def line_device(
    activations,
    per_layer,
    cotangent,
    lengths,
    starts,
    w_query,
    m_query,
    v_query,
    key_value_weight,
    key_value_first_moment,
    key_value_second_moment,
    w_attend,
    m_attend,
    v_attend,
    w_gateup,
    m_gateup,
    v_gateup,
    w_down,
    m_down,
    v_down,
    w_left,
    m_left,
    v_left,
    w_right,
    m_right,
    v_right,
    w_pergate,
    m_pergate,
    v_pergate,
    w_perproj,
    m_perproj,
    v_perproj,
    w_gains,
    m_gains,
    v_gains,
    w_heads,
    m_heads,
    v_heads,
):
    rows_n = lax.axis_size("row")
    cols_n = lax.axis_size("col")
    data_n = lax.axis_size("dp")
    me = lax.axis_index("row")
    column = lax.axis_index("col")
    data_at = lax.axis_index("dp")
    half_tok, width_a = activations.shape
    tokens = half_tok * cols_n
    share = half_tok // rows_n
    quarter = tokens // rows_n
    width = width_a * rows_n

    ff_part = w_gateup.shape[2] // rows_n
    out_cols = w_down.shape[1]
    heads_here = data_n
    left_cols, right_rows = w_left.shape[1], w_right.shape[0]
    gate_cols, proj_rows = w_pergate.shape[1], w_perproj.shape[0]

    def columns_of(at, size):
        return pl.ds(pl.multiple_of(at * size, size), size)

    def across(source, by_rows):
        high, wide = source.shape
        if by_rows:
            return Swap(
                source,
                (data_n * high, wide),
                lambda ref, q: ref,
                lambda ref, at: ref.at[columns_of(at, high)],
                "dp",
            )
        return Swap(
            source,
            (high, data_n * wide),
            lambda ref, q: ref,
            lambda ref, at: ref.at[:, columns_of(at, wide)],
            "dp",
        )

    def along(source):
        high, wide = source.shape
        return Line(
            source,
            (cols_n * high, rows_n * wide),
            lambda ref, c, r: ref.at[columns_of(c, high), columns_of(r, wide)],
            True,
        )

    gateup_own, attend_own, qkv_w, left_t, right_w, pergate_t, perproj_w = transfers(
        [
            Swap(
                w_gateup.astype(LOW),
                (2, width, ff_part),
                lambda ref, q: ref.at[:, :, columns_of(q, ff_part)],
                lambda ref, at: ref.at[:, columns_of(at, width_a), :],
            ),
            Swap(
                w_attend.astype(LOW).reshape(rows_n, HEAD_WIDTH, out_cols),
                (HEAD_WIDTH, rows_n * out_cols),
                lambda ref, q: ref.at[q],
                lambda ref, at: ref.at[:, columns_of(at, out_cols)],
            ),
            Swap(
                jnp.concatenate([w_query, key_value_weight], axis=1).astype(LOW),
                (data_n, width_a, 2 * HEAD_WIDTH),
                lambda ref, q: ref,
                lambda ref, at: ref.at[at],
                "dp",
            ),
            across(w_left.T, True),
            across(w_right.astype(LOW), False),
            across(w_pergate.T.astype(LOW), True),
            across(w_perproj.astype(LOW), False),
        ],
        1,
        60,
    )
    gateup_all = lax.all_gather(gateup_own, "dp")

    def lower(inputs, outputs):
        @pl.loop(0, inputs[0].shape[0] // 256)
        def _(at):
            rows = pl.ds(pl.multiple_of(at * 256, 256), 256)
            outputs[0][rows] = inputs[0][rows].astype(LOW)

    last = pl.ds(HEAD_WIDTH, HEAD_WIDTH)
    down_low, whole_acts, whole_key, whole_value, head_w, gains, extras, attend_all = transfers(
        [
            along(activations),
            Line(
                qkv_w,
                (width, HEAD_WIDTH),
                lambda ref, c, r: ref.at[columns_of(r, width_a)],
                False,
                lambda ref, c: ref.at[c, :, last],
            ),
            Line(
                qkv_w,
                (width, HEAD_WIDTH),
                lambda ref, c, r: ref.at[columns_of(r, width_a)],
                False,
                lambda ref, c: ref.at[KEY_VALUE_HEADS + c, :, last],
            ),
            Swap(
                qkv_w,
                (width, HEAD_WIDTH),
                lambda ref, q: ref.at[q, :, pl.ds(0, HEAD_WIDTH)],
                lambda ref, at: ref.at[columns_of(at, width_a)],
            ),
            Line(w_gains, (6, width), lambda ref, c, r: ref.at[:, columns_of(r, width_a)]),
            Line(
                per_layer,
                (tokens, PLD),
                lambda ref, c, r: ref.at[columns_of(r, quarter), columns_of(c, PLD // cols_n)],
                True,
            ),
            Swap(
                attend_own,
                (data_n, HEAD_WIDTH, rows_n * out_cols),
                lambda ref, q: ref,
                lambda ref, at: ref.at[at],
                "dp",
            ),
        ],
        2,
        95,
        60,
        lower,
        (w_down,),
        [jax.ShapeDtypeStruct(w_down.shape, LOW)],
    )
    attend_w = (
        attend_all.reshape(data_n, HEAD_WIDTH, rows_n, out_cols)
        .transpose(1, 2, 0, 3)
        .reshape(HEAD_WIDTH, width)
    )
    all_cos, all_sin = rope_tables(jnp.arange(tokens, dtype=jnp.int32), HEAD_WIDTH)
    (
        spread_h,
        own_acts,
        acts_share,
        scale_here,
        query_raw,
        key_raw,
        value_raw,
        queries,
        keys,
        values,
        attended,
        top,
        extras,
        own_cos,
        own_sin,
        left_t,
        right_w,
        down_own,
    ) = attention_forward_head(
        whole_acts,
        gains,
        head_w,
        whole_key,
        whole_value,
        w_heads,
        all_cos,
        all_sin,
        extras,
        lengths,
        starts,
        [
            along(left_t.astype(LOW)),
            along(right_w),
            Swap(
                down_low.reshape(data_n, rows_n, ff_part, out_cols),
                (data_n, ff_part, rows_n * out_cols),
                lambda ref, q: ref.at[:, q],
                lambda ref, at: ref.at[:, :, columns_of(at, out_cols)],
            ),
        ],
        3,
    )
    down_own, gateup_all = lax.optimization_barrier((down_own, gateup_all))
    down_all = lax.all_gather(down_own, "dp").reshape(data_n, data_n * ff_part, -1)
    def shares(parts):
        return parts.astype(LOW).reshape(cols_n, rows_n, share, width)

    projected, pergate_t, perproj_w = transfers(
        [
            Reduce(
                shares(flat_dot(attended, attend_w)), (share, width), lambda ref, q: ref.at[q]
            ),
            along(pergate_t),
            along(perproj_w),
        ],
        5,
        45,
        60,
    )
    wide_low, wide_full = ((share, width), LOW), ((share, width), FULL)
    line = ((1, width), FULL)
    hidden_low, middle, right_raw, mixture, ffn_in = local(
        mix,
        [wide_low, ((share, RANK), LOW), wide_full, wide_full, wide_low],
        acts_share,
        projected,
        gains,
        left_t,
        right_w,
    )
    down_raw, spread_ft, act_t, gate_raw, up_raw, upstream = ffn_forward(
        ffn_in,
        gateup_all,
        down_all,
        [
            Swap(
                cotangent,
                (share, width),
                lambda ref, q: ref.at[columns_of(q, share)],
                lambda ref, at: ref.at[:, columns_of(at, width_a)],
            )
        ],
        6,
    )
    result, d_out, d_down, dw_perproj, dw_pergate, gain_four, gain_five = local(
        per_layer_both,
        [wide_low, wide_full, wide_low, ((PLD, width), LOW), ((PLD, width), LOW), line, line],
        mixture,
        down_raw,
        gains,
        extras,
        pergate_t,
        perproj_w,
        upstream,
    )
    d_ffn, dw_gateup, dw_down = ffn_backward(
        d_down, gateup_all, down_all, spread_ft, act_t, gate_raw, up_raw, [], 8
    )
    g_gateup = lax.psum_scatter(dw_gateup, "dp", scatter_dimension=0)
    d_proj, d_half, d_middle, small_parts, inner_share, gain_one, gain_two, gain_three = local(
        mix_back,
        [
            wide_low,
            wide_low,
            ((share, RANK), LOW),
            ((2 * (RANK + PLD), width), LOW),
            ((8, share), FULL),
            line,
            line,
            line,
        ],
        d_out,
        d_ffn,
        mixture,
        projected,
        right_raw,
        gains,
        acts_share,
        left_t,
        right_w,
        hidden_low,
        middle,
        dw_pergate,
        dw_perproj,
    )
    small_parts = small_parts.reshape(cols_n, -1, width)
    spread_p, small_parts = transfers(
        [
            Line(
                d_proj.astype(LOW),
                (cols_n, rows_n, share, width),
                lambda ref, c, r: ref.at[c, r],
                True,
            ),
            Reduce(
                small_parts,
                (small_parts.shape[1], width_a),
                lambda ref, q: ref.at[:, columns_of(q, width_a)],
            ),
        ],
        10,
        50,
        60,
    )
    spread_p = spread_p.reshape(tokens, width)
    d_q_raw, kv_parts, dg_query, dw_attend, middle_here, half_here, result = head_backward(
        queries,
        keys,
        values,
        attended,
        spread_p,
        attend_w,
        query_raw,
        w_heads,
        all_cos,
        all_sin,
        lengths,
        starts,
        [
            Line(
                d_middle, (half_tok, d_middle.shape[1]), lambda ref, c, r: ref.at[columns_of(r, share)]
            )
        ]
        + [
            Swap(
                source,
                (half_tok, width_a),
                lambda ref, q: ref.at[:, columns_of(q, width_a)],
                lambda ref, at: ref.at[columns_of(at, share)],
            )
            for source in (d_half, result)
        ],
        4,
    )

    d_q_raw, dw_down, g_gateup = lax.optimization_barrier((d_q_raw, dw_down, g_gateup))
    g_down = lax.psum_scatter(
        dw_down.reshape(data_n, data_n, ff_part, -1), "dp", scatter_dimension=0
    )

    d_q_all, d_kv = transfers(
        [
            Line(d_q_raw, (rows_n,) + d_q_raw.shape, lambda ref, c, r: ref.at[r]),
            Reduce(kv_parts, kv_parts.shape[1:], lambda ref, q: ref.at[q], False),
        ],
        11,
        45,
        60,
    )
    d_k_raw, d_v_raw, dg_key = local(
        key_value_back,
        [((quarter, HEAD_WIDTH), LOW), ((quarter, HEAD_WIDTH), LOW), ((1, HEAD_WIDTH), FULL)],
        d_kv,
        key_raw,
        value_raw,
        w_heads,
        own_cos,
        own_sin,
        mebibytes=16,
    )

    def query_work(inputs, outputs):
        h_ref, dq_ref, qw_ref, g_ref = inputs
        dw_ref, dh_ref, sq_ref = outputs
        hidden = h_ref[...]
        for k in range(heads_here):
            dw_ref[k] = inner_rows(hidden, dq_ref[k]).astype(LOW)
        total = against(dq_ref[0], qw_ref[0, :, :HEAD_WIDTH])
        for k in range(1, heads_here):
            total = total + against(dq_ref[k], qw_ref[k, :, :HEAD_WIDTH])
        dh_ref[...] = total
        sq_ref[...] = jnp.zeros(sq_ref.shape, FULL)
        for which in range(2):

            @pl.loop(0, width // 128)
            def _(at):
                rows = g_ref[which, pl.ds(pl.multiple_of(at * 128, 128), 128)].astype(FULL)
                sq_ref[...] += jnp.sum((rows * rows).reshape(16, 8, ff_part), axis=0)

    dw_query, d_hidden, gateup_squares, d_k_all, d_v_all, g_gateup, g_attend = transfers(
        [
            Line(
                d_raw, (tokens, HEAD_WIDTH), lambda ref, c, r: ref.at[columns_of(r, quarter)]
            )
            for d_raw in (d_k_raw, d_v_raw)
        ]
        + [
            Swap(
                g_gateup,
                w_gateup.shape,
                lambda ref, q: ref.at[:, columns_of(q, width_a), :],
                lambda ref, at: ref.at[:, :, columns_of(at, ff_part)],
            ),
            ShardSum(dw_attend, out_cols),
        ],
        12,
        65,
        40,
        query_work,
        (spread_h, d_q_all, qkv_w, g_gateup),
        [
            jax.ShapeDtypeStruct((heads_here, width_a, HEAD_WIDTH), LOW),
            jax.ShapeDtypeStruct((tokens, width_a), FULL),
            jax.ShapeDtypeStruct((8, ff_part), FULL),
        ],
    )
    extents = (
        (data_n * left_cols, True),
        (right_rows, False),
        (data_n * gate_cols, True),
        (proj_rows, False),
    )
    flat_rows = sum(rows for rows, _ in extents)
    dw_kv, d_hidden, inner, flat_parts = local(
        functools.partial(key_value_ends, extents=extents),
        [
            ((2 * width_a, HEAD_WIDTH), LOW),
            ((tokens, width_a), LOW),
            ((8, tokens), FULL),
            ((data_n * flat_rows, out_cols), LOW),
        ],
        spread_h,
        d_k_all,
        d_v_all,
        qkv_w,
        d_hidden,
        own_acts,
        w_gains,
        small_parts,
        mebibytes=24,
    )
    dw_kv = dw_kv.reshape(2, width_a, HEAD_WIDTH)
    down_sums = g_down
    g_query, g_keyval, flat_grads, inner, inner_share, d_hidden, g_attend, g_down = shard_total(
        dw_query,
        dw_kv,
        flat_parts.reshape(data_n, flat_rows, out_cols),
        [
            Line(inner, (cols_n, rows_n) + inner.shape, lambda ref, c, r: ref.at[c, r], True),
            Line(
                inner_share,
                (cols_n, rows_n) + inner_share.shape,
                lambda ref, c, r: ref.at[c, r],
                True,
            ),
            Pair(d_hidden.reshape(cols_n, half_tok, width_a)),
            Swap(
                g_attend,
                (rows_n, HEAD_WIDTH, out_cols),
                lambda ref, q: ref.at[:, columns_of(q, out_cols)],
                lambda ref, at: ref.at[at],
            ),
            Swap(
                g_down,
                (data_n, rows_n, ff_part, out_cols),
                lambda ref, q: ref.at[:, :, columns_of(q, out_cols)],
                lambda ref, at: ref.at[:, at],
            ),
        ],
        13,
    )
    g_down = g_down.reshape(w_down.shape)
    g_attend = g_attend.reshape(w_attend.shape)
    small_grads = []
    start = 0
    for w, by_rows in ((w_left, True), (w_right, False), (w_pergate, True), (w_perproj, False)):
        rows = w.size // out_cols
        cut = flat_grads[start : start + rows]
        start += rows
        if by_rows:
            high = rows // data_n
            cut = [cut[k * high : (k + 1) * high] for k in range(data_n)]
            cut = jnp.concatenate(cut, axis=1).T
        small_grads.append(cut)
    g_left, g_right, g_pergate, g_perproj = small_grads

    grad_input, small = input_ends(
        d_hidden,
        half_here,
        middle_here,
        left_t,
        activations,
        scale_here,
        w_gains,
        inner,
        inner_share,
        (g_query, g_keyval, flat_grads, g_attend, down_sums),
        gateup_squares,
        (gain_one, gain_two, gain_three, gain_four, gain_five),
        dg_query,
        dg_key,
        top,
    )
    gain_rows = 6 * width // 128
    head_rows = (QUERY_HEADS + 1) * HEAD_WIDTH // 128
    small = last_sums(small, 15)
    gain_sum = small[:gain_rows].reshape(6, width)
    head_sum = small[gain_rows : gain_rows + head_rows].reshape(QUERY_HEADS + 1, HEAD_WIDTH)
    g_gains = lax.dynamic_slice_in_dim(gain_sum, me * width_a, width_a, 1)
    matrix_rate = MODEL_WIDTH ** (-0.5)

    def flat_rows_of(array):
        return array.reshape(-1, array.shape[-1])

    def kept(array):
        return array

    def turned(array):
        return array.T

    groups = [
        tuple(change(array) for array in arrays) + rest
        for arrays, change, rest in (
            ((w_gateup, m_gateup, v_gateup, g_gateup), flat_rows_of, (matrix_rate, DECAY, None)),
            ((w_down, m_down, v_down, g_down), kept, (FF ** (-0.5), DECAY, None)),
            ((w_query, m_query, v_query, g_query), kept, (matrix_rate, DECAY, "query")),
            (
                (key_value_weight, key_value_first_moment, key_value_second_moment, g_keyval),
                kept,
                (matrix_rate, DECAY, "keyval"),
            ),
            (
                (w_attend, m_attend, v_attend, g_attend),
                kept,
                ((QUERY_HEADS * HEAD_WIDTH) ** (-0.5), DECAY, None),
            ),
            ((w_left, m_left, v_left, g_left), turned, (matrix_rate, DECAY, None)),
            ((w_right, m_right, v_right, g_right), kept, (RANK ** (-0.5), DECAY, None)),
            ((w_pergate, m_pergate, v_pergate, g_pergate), turned, (matrix_rate, DECAY, None)),
            ((w_perproj, m_perproj, v_perproj, g_perproj), kept, (PLD ** (-0.5), DECAY, None)),
            ((w_gains, m_gains, v_gains, g_gains), kept, (GAIN_RATE, 0.0, None)),
            ((w_heads, m_heads, v_heads, head_sum), kept, (HEAD_RATE, 0.0, None)),
        )
    ]
    grad_norm, scale_factors, *stepped = adam_all(small, gain_rows + head_rows, groups)
    grad_norm = grad_norm.reshape(())
    scale_factors = scale_factors.reshape(-1)
    gateup, down, query, keyval, attend, left, right, pergate, perproj, gain, head = (
        stepped[3 * k : 3 * k + 3] for k in range(11)
    )
    gateup = [array.reshape(w_gateup.shape) for array in gateup]
    left = [array.T for array in left]
    pergate = [array.T for array in pergate]
    return (
        result,
        grad_input,
        grad_norm,
        scale_factors,
        *query,
        *keyval,
        *attend,
        *gateup,
        *down,
        *left,
        *right,
        *pergate,
        *perproj,
        *gain,
        *head,
    )


def per_device(
    activations,
    per_layer,
    cotangent,
    lengths,
    starts,
    w_query,
    m_query,
    v_query,
    key_value_weight,
    key_value_first_moment,
    key_value_second_moment,
    w_attend,
    m_attend,
    v_attend,
    w_gateup,
    m_gateup,
    v_gateup,
    w_down,
    m_down,
    v_down,
    w_left,
    m_left,
    v_left,
    w_right,
    m_right,
    v_right,
    w_pergate,
    m_pergate,
    v_pergate,
    w_perproj,
    m_perproj,
    v_perproj,
    w_gains,
    m_gains,
    v_gains,
    w_heads,
    m_heads,
    v_heads,
):
    row_devs = lax.axis_size("row")
    col_devs = lax.axis_size("col")
    data_devs = lax.axis_size("dp")
    row_place = lax.axis_index("row")
    column_place = lax.axis_index("col")
    data_at = lax.axis_index("dp")
    bf16 = jnp.bfloat16
    single_float = jnp.float32
    query_b, keyval_b, attend_b, gateup_b, down_b, left_b, right_b, pergate_b, perproj_b = (
        lax.all_gather(w_query.astype(bf16), "dp", axis=1, tiled=True),
        lax.all_gather(key_value_weight.astype(bf16), "dp", axis=1, tiled=True),
        lax.all_gather(w_attend.astype(bf16), "dp", axis=1, tiled=True),
        lax.all_gather(w_gateup.astype(bf16), "dp", axis=2, tiled=True),
        lax.all_gather(w_down.astype(bf16), "dp", axis=1, tiled=True),
        lax.all_gather(w_left.astype(bf16), "dp", axis=1, tiled=True),
        lax.all_gather(w_right.astype(bf16), "dp", axis=1, tiled=True),
        lax.all_gather(w_pergate.astype(bf16), "dp", axis=1, tiled=True),
        lax.all_gather(w_perproj.astype(bf16), "dp", axis=1, tiled=True),
    )
    inputs = activations.astype(single_float)
    tok_a, width_a = inputs.shape
    grouped_rows = tok_a * col_devs
    token_batch = grouped_rows // row_devs
    q_cols = query_b.shape[1]
    l_cols = left_b.shape[1]
    kv_cols = keyval_b.shape[1]
    ff_here = gateup_b.shape[2]
    local_heads = q_cols // HEAD_WIDTH
    length = lax.dynamic_index_in_dim(lengths, data_at, 0, keepdims=False)
    piece_starts = lax.dynamic_index_in_dim(starts, data_at, 0, keepdims=False)
    own_places = row_place * token_batch + jnp.arange(token_batch, dtype=jnp.int32)
    all_places = jnp.arange(grouped_rows, dtype=jnp.int32)
    own_cos, own_sin = rope_tables(own_places, HEAD_WIDTH)
    query_gains = lax.dynamic_slice_in_dim(w_heads, column_place * local_heads, local_heads, 0)
    key_gain = w_heads[QUERY_HEADS]
    hidden, scale_in = norm_forward(inputs, w_gains[0])
    hidden_b = hidden.astype(bf16)
    spread_h = spread_col(hidden_b)
    type_one = reduce_row(flat_dot(spread_h, jnp.concatenate([query_b, left_b], axis=1)))
    key_raw_all = lax.psum(flat_dot(spread_h, keyval_b), "row")
    all_cos, all_sin = rope_tables(all_places, HEAD_WIDTH)
    key_value_whole = key_form(key_raw_all, key_gain, all_cos, all_sin).astype(bf16)
    key_raw = lax.dynamic_slice_in_dim(key_raw_all, row_place * token_batch, token_batch, 0)
    query_raw = type_one[:, :q_cols]
    middle_b = type_one[:, q_cols : q_cols + l_cols].astype(bf16)
    queries = query_form(query_raw, query_gains, own_cos, own_sin).astype(bf16)
    key_value_heads = (column_place * local_heads + jnp.arange(local_heads, dtype=jnp.int32)) // (
        QUERY_HEADS // KEY_VALUE_HEADS
    )
    every_key = key_value_whole[:, : KEY_VALUE_HEADS * HEAD_WIDTH].reshape(
        grouped_rows, KEY_VALUE_HEADS, HEAD_WIDTH
    )
    every_value = key_value_whole[:, KEY_VALUE_HEADS * HEAD_WIDTH :].reshape(
        grouped_rows, KEY_VALUE_HEADS, HEAD_WIDTH
    )
    key_sel = jnp.take(every_key, key_value_heads, axis=1)
    value_sel = jnp.take(every_value, key_value_heads, axis=1)
    attended, block_peaks, block_totals = attention_forward(
        queries, key_sel, value_sel, own_places, all_places, length, piece_starts
    )
    attended_b = attended.reshape(token_batch, q_cols).astype(bf16)
    joined_b = jnp.concatenate([attended_b, middle_b], axis=1)
    spread_j = spread_row(joined_b)
    type_two = reduce_col(
        jnp.concatenate(
            [flat_dot(spread_j[:, :q_cols], attend_b), flat_dot(spread_j[:, q_cols:], right_b)],
            axis=1,
        )
    )
    projected = type_two[:, :width_a]
    right_raw = type_two[:, width_a:]
    right_n, scale_r = norm_forward(right_raw, w_gains[1])
    laurel = hidden + right_n
    proj_n, scale_p = norm_forward(projected, w_gains[2])
    gated_sum = inputs + proj_n
    mixture = (gated_sum + laurel) * HALF_ROOT
    ffn_n, scale_f = norm_forward(mixture, w_gains[3])
    ffn_b = ffn_n.astype(bf16)
    spread_f = spread_col(ffn_b)
    gateup_pair = jnp.concatenate([gateup_b[0], gateup_b[1]], axis=1)
    gate_up = reduce_row(flat_dot(spread_f, gateup_pair))
    gate_raw = gate_up[:, :ff_here]
    up_raw = gate_up[:, ff_here:]
    act_b = (jax.nn.gelu(gate_raw, approximate=True) * up_raw).astype(bf16)
    spread_a = spread_row(act_b)
    down_raw = reduce_col(flat_dot(spread_a, down_b))
    down_n, scale_d = norm_forward(down_raw, w_gains[4])
    block_out = mixture + down_n
    out_b = block_out.astype(bf16)
    spread_o = spread_col(out_b)
    pgate = reduce_row(flat_dot(spread_o, pergate_b))
    extras = per_layer.astype(single_float)
    pact_b = (jax.nn.gelu(pgate, approximate=True) * extras).astype(bf16)
    spread_p = spread_row(pact_b)
    perproj = reduce_col(flat_dot(spread_p, perproj_b))
    perproj_n, scale_pp = norm_forward(perproj, w_gains[5])
    result = (block_out + perproj_n).astype(bf16)
    upstream = cotangent.astype(single_float)
    gain_grads = [None, None, None, None, None, None]
    d_perproj, gain_grads[5] = norm_backward(perproj, scale_pp, w_gains[5], upstream)
    grads_five = grads_col(d_perproj.astype(bf16))
    dw_perproj = inner_rows(spread_p, grads_five)
    d_pact = reduce_row(against(grads_five, perproj_b))
    gelu_out, pullback = jax.vjp(lambda v: jax.nn.gelu(v, approximate=True), pgate)
    (d_pgate,) = pullback(d_pact * extras)
    grads_four = grads_row(d_pgate.astype(bf16))
    dw_pergate = inner_rows(spread_o, grads_four)
    d_out = upstream + reduce_col(against(grads_four, pergate_b))
    d_down, gain_grads[4] = norm_backward(down_raw, scale_d, w_gains[4], d_out)
    grads_three = grads_col(d_down.astype(bf16))
    dw_down = inner_rows(spread_a, grads_three)
    d_act = reduce_row(against(grads_three, down_b))
    act_out, pullback = jax.vjp(lambda a, b: jax.nn.gelu(a, approximate=True) * b, gate_raw, up_raw)
    d_gate, d_up = pullback(d_act)
    local_two = jnp.concatenate([d_gate, d_up], axis=1).astype(bf16)
    grads_two = grads_row(local_two)
    dw_gateup = jnp.stack(
        [inner_rows(spread_f, grads_two[:, :ff_here]), inner_rows(spread_f, grads_two[:, ff_here:])]
    )
    d_ffn = reduce_col(
        against(grads_two[:, :ff_here], gateup_b[0]) + against(grads_two[:, ff_here:], gateup_b[1])
    )
    d_mix_norm, gain_grads[3] = norm_backward(mixture, scale_f, w_gains[3], d_ffn)
    d_half = (d_out + d_mix_norm) * HALF_ROOT
    d_proj, gain_grads[2] = norm_backward(projected, scale_p, w_gains[2], d_half)
    d_right, gain_grads[1] = norm_backward(right_raw, scale_r, w_gains[1], d_half)
    grads_one = grads_col(jnp.concatenate([d_proj, d_right], axis=1).astype(bf16))
    dw_attend = inner_rows(spread_j[:, :q_cols], grads_one[:, :width_a])
    dw_right = inner_rows(spread_j[:, q_cols:], grads_one[:, width_a:])
    d_joined = reduce_row(
        jnp.concatenate(
            [against(grads_one[:, :width_a], attend_b), against(grads_one[:, width_a:], right_b)],
            axis=1,
        )
    )
    d_attended = d_joined[:, :q_cols].astype(bf16).reshape(token_batch, local_heads, HEAD_WIDTH)
    d_middle = d_joined[:, q_cols:]
    d_queries, d_key_sel, d_value_sel = attention_backward(
        queries,
        key_sel,
        value_sel,
        d_attended,
        block_peaks,
        block_totals,
        own_places,
        all_places,
        length,
        piece_starts,
    )
    single_hot_mask = (
        key_value_heads[:, None] == jnp.arange(KEY_VALUE_HEADS, dtype=jnp.int32)[None, :]
    ).astype(single_float)
    key_gradient = jnp.sum(d_key_sel[:, :, None, :] * single_hot_mask[None, :, :, None], axis=1)
    value_gradient = jnp.sum(d_value_sel[:, :, None, :] * single_hot_mask[None, :, :, None], axis=1)
    key_gradient, value_gradient = lax.psum((key_gradient, value_gradient), ("row", "col"))
    local_key_gradient = lax.dynamic_slice_in_dim(
        key_gradient, row_place * token_batch, token_batch, 0
    ).reshape(token_batch, KEY_VALUE_HEADS * HEAD_WIDTH)
    local_value_gradient = lax.dynamic_slice_in_dim(
        value_gradient, row_place * token_batch, token_batch, 0
    ).reshape(token_batch, KEY_VALUE_HEADS * HEAD_WIDTH)
    query_out, pullback = jax.vjp(
        lambda r, g: query_form(r, g, own_cos, own_sin), query_raw, query_gains
    )
    d_query_raw, dg_query = pullback(d_queries)
    key_tile = jnp.broadcast_to(key_gain, (token_batch, 1, HEAD_WIDTH))
    key_out, pullback = jax.vjp(lambda r, g: key_form(r, g, own_cos, own_sin), key_raw, key_tile)
    d_key_raw, dg_key_rows = pullback(
        jnp.concatenate([local_key_gradient, local_value_gradient], axis=1)
    )
    slice_rows = token_batch // col_devs
    dg_key = jnp.sum(
        lax.dynamic_slice_in_dim(dg_key_rows, column_place * slice_rows, slice_rows, 0), axis=(0, 1)
    )
    grads_zero = grads_row(jnp.concatenate([d_query_raw, d_middle, d_key_raw], axis=1).astype(bf16))
    dw_query = inner_rows(spread_h, grads_zero[:, :q_cols])
    dw_left = inner_rows(spread_h, grads_zero[:, q_cols : q_cols + l_cols])
    key_grad_rows = grads_zero[:, q_cols + l_cols :]
    dw_keyval = inner_rows(spread_h, key_grad_rows)
    slab_width = kv_cols // col_devs
    d_hidden = reduce_col(
        against(grads_zero[:, :q_cols], query_b)
        + against(grads_zero[:, q_cols : q_cols + l_cols], left_b)
        + against(
            lax.dynamic_slice_in_dim(key_grad_rows, column_place * slab_width, slab_width, 1),
            lax.dynamic_slice_in_dim(keyval_b, column_place * slab_width, slab_width, 1),
        )
    )
    d_in, gain_grads[0] = norm_backward(inputs, scale_in, w_gains[0], d_hidden + d_half)
    grad_input = (d_half + d_in).astype(bf16)
    g_query, g_keyval, g_attend, g_gateup, g_down, g_left, g_right, g_pergate, g_perproj = (
        lax.psum_scatter(dw_query, "dp", scatter_dimension=1, tiled=True),
        lax.psum_scatter(dw_keyval, "dp", scatter_dimension=1, tiled=True),
        lax.psum_scatter(dw_attend, "dp", scatter_dimension=1, tiled=True),
        lax.psum_scatter(dw_gateup, "dp", scatter_dimension=2, tiled=True),
        lax.psum_scatter(dw_down, "dp", scatter_dimension=1, tiled=True),
        lax.psum_scatter(dw_left, "dp", scatter_dimension=1, tiled=True),
        lax.psum_scatter(dw_right, "dp", scatter_dimension=1, tiled=True),
        lax.psum_scatter(dw_pergate, "dp", scatter_dimension=1, tiled=True),
        lax.psum_scatter(dw_perproj, "dp", scatter_dimension=1, tiled=True),
    )
    gain_full = lax.dynamic_update_slice_in_dim(
        jnp.zeros((6, MODEL_WIDTH), single_float), jnp.stack(gain_grads), row_place * width_a, 1
    )
    head_full = lax.dynamic_update_slice_in_dim(
        jnp.zeros((QUERY_HEADS + 1, HEAD_WIDTH), single_float),
        dg_query,
        column_place * local_heads,
        0,
    )
    head_full = head_full.at[QUERY_HEADS].add(dg_key)
    logit_here = lax.dynamic_update_slice_in_dim(
        jnp.full((QUERY_HEADS,), NEGATIVE, single_float),
        jnp.max(block_peaks, axis=(0, 2)),
        column_place * local_heads,
        0,
    )

    def combine(left_part, right_part):
        return (
            left_part[0] + right_part[0],
            left_part[1] + right_part[1],
            jnp.maximum(left_part[2], right_part[2]),
        )

    gain_sum, head_sum, logit_top = joined(
        (gain_full, head_full, logit_here), ("dp", "row", "col"), combine
    )
    g_gains = lax.dynamic_slice_in_dim(gain_sum, row_place * width_a, width_a, 1)
    lead_device = (column_place == 0) & (data_at == 0)
    solo_device = lead_device & (row_place == 0)
    squares = jnp.float32(0.0)
    for gradient in (g_query, g_attend, g_gateup, g_down, g_left, g_right, g_pergate, g_perproj):
        squares = squares + jnp.sum(gradient * gradient)
    squares = squares + jnp.where(column_place == 0, jnp.sum(g_keyval * g_keyval), 0.0)
    squares = squares + jnp.where(lead_device, jnp.sum(g_gains * g_gains), 0.0)
    squares = squares + jnp.where(solo_device, jnp.sum(head_sum * head_sum), 0.0)
    grad_norm = jnp.sqrt(lax.psum(squares, ("dp", "row", "col")))
    clip_scale = CLIP / jnp.maximum(grad_norm, CLIP)
    scale_factors = LOGIT_CAP / jnp.maximum(logit_top, LOGIT_CAP)
    weights = (
        w_query,
        key_value_weight,
        w_attend,
        w_gateup,
        w_down,
        w_left,
        w_right,
        w_pergate,
        w_perproj,
        w_gains,
        w_heads,
    )
    moments = (
        m_query,
        key_value_first_moment,
        m_attend,
        m_gateup,
        m_down,
        m_left,
        m_right,
        m_pergate,
        m_perproj,
        m_gains,
        m_heads,
    )
    seconds = (
        v_query,
        key_value_second_moment,
        v_attend,
        v_gateup,
        v_down,
        v_left,
        v_right,
        v_pergate,
        v_perproj,
        v_gains,
        v_heads,
    )
    gradients = (
        g_query,
        g_keyval,
        g_attend,
        g_gateup,
        g_down,
        g_left,
        g_right,
        g_pergate,
        g_perproj,
        g_gains,
        head_sum,
    )
    step_rates = (
        MODEL_WIDTH ** (-0.5),
        MODEL_WIDTH ** (-0.5),
        (QUERY_HEADS * HEAD_WIDTH) ** (-0.5),
        MODEL_WIDTH ** (-0.5),
        FF ** (-0.5),
        MODEL_WIDTH ** (-0.5),
        RANK ** (-0.5),
        MODEL_WIDTH ** (-0.5),
        PLD ** (-0.5),
        GAIN_RATE,
        HEAD_RATE,
    )
    decays = (DECAY, DECAY, DECAY, DECAY, DECAY, DECAY, DECAY, DECAY, DECAY, 0.0, 0.0)
    updated = [
        adamw_step(
            weights[k], moments[k], seconds[k], gradients[k] * clip_scale, step_rates[k], decays[k]
        )
        for k in range(11)
    ]
    head_scale = jnp.sqrt(scale_factors)
    q_width = w_query.shape[1]
    q_head = (
        (column_place * data_devs + data_at) * q_width + jnp.arange(q_width, dtype=jnp.int32)
    ) // HEAD_WIDTH
    q_factor = jnp.sum(
        jnp.where(
            q_head[:, None] == jnp.arange(QUERY_HEADS, dtype=jnp.int32)[None, :],
            head_scale[None, :],
            0.0,
        ),
        axis=1,
    )
    new_query = updated[0][2] * q_factor[None, :]
    kv_width = key_value_weight.shape[1]
    key_value_index = data_at * kv_width + jnp.arange(kv_width, dtype=jnp.int32)
    key_value_scale = jnp.sqrt(
        jnp.min(scale_factors.reshape(KEY_VALUE_HEADS, QUERY_HEADS // KEY_VALUE_HEADS), axis=1)
    )
    key_value_choice = jnp.sum(
        jnp.where(
            (key_value_index // HEAD_WIDTH)[:, None]
            == jnp.arange(KEY_VALUE_HEADS, dtype=jnp.int32)[None, :],
            key_value_scale[None, :],
            0.0,
        ),
        axis=1,
    )
    key_value_factor = jnp.where(
        key_value_index < KEY_VALUE_HEADS * HEAD_WIDTH, key_value_choice, 1.0
    )
    new_keyval = updated[1][2] * key_value_factor[None, :]
    return (
        result,
        grad_input,
        grad_norm,
        scale_factors,
        updated[0][0],
        updated[0][1],
        new_query,
        updated[1][0],
        updated[1][1],
        new_keyval,
        updated[2][0],
        updated[2][1],
        updated[2][2],
        updated[3][0],
        updated[3][1],
        updated[3][2],
        updated[4][0],
        updated[4][1],
        updated[4][2],
        updated[5][0],
        updated[5][1],
        updated[5][2],
        updated[6][0],
        updated[6][1],
        updated[6][2],
        updated[7][0],
        updated[7][1],
        updated[7][2],
        updated[8][0],
        updated[8][1],
        updated[8][2],
        updated[9][0],
        updated[9][1],
        updated[9][2],
        updated[10][0],
        updated[10][1],
        updated[10][2],
    )


def solution(mesh):
    placed = (
        P(("dp", "col"), "row"),
        P(("dp", "row"), "col"),
        P(("dp", "col"), "row"),
        P(),
        P(),
        P("row", ("col", "dp")),
        P("row", ("col", "dp")),
        P("row", ("col", "dp")),
        P("row", "dp"),
        P("row", "dp"),
        P("row", "dp"),
        P("col", ("row", "dp")),
        P("col", ("row", "dp")),
        P("col", ("row", "dp")),
        P(None, "row", ("col", "dp")),
        P(None, "row", ("col", "dp")),
        P(None, "row", ("col", "dp")),
        P("col", ("row", "dp")),
        P("col", ("row", "dp")),
        P("col", ("row", "dp")),
        P("row", ("col", "dp")),
        P("row", ("col", "dp")),
        P("row", ("col", "dp")),
        P("col", ("row", "dp")),
        P("col", ("row", "dp")),
        P("col", ("row", "dp")),
        P("row", ("col", "dp")),
        P("row", ("col", "dp")),
        P("row", ("col", "dp")),
        P("col", ("row", "dp")),
        P("col", ("row", "dp")),
        P("col", ("row", "dp")),
        P(None, "row"),
        P(None, "row"),
        P(None, "row"),
        P(),
        P(),
        P(),
    )
    fits = (
        mesh.shape["col"] == KEY_VALUE_HEADS
        and mesh.shape["row"] * KEY_VALUE_HEADS == QUERY_HEADS
        and mesh.shape["dp"] == mesh.shape["row"]
    )
    return jax.shard_map(
        line_device if fits else per_device,
        mesh=mesh,
        in_specs=placed,
        out_specs=(
            P(("dp", "col"), "row"),
            P(("dp", "col"), "row"),
            P(),
            P(),
            P("row", ("col", "dp")),
            P("row", ("col", "dp")),
            P("row", ("col", "dp")),
            P("row", "dp"),
            P("row", "dp"),
            P("row", "dp"),
            P("col", ("row", "dp")),
            P("col", ("row", "dp")),
            P("col", ("row", "dp")),
            P(None, "row", ("col", "dp")),
            P(None, "row", ("col", "dp")),
            P(None, "row", ("col", "dp")),
            P("col", ("row", "dp")),
            P("col", ("row", "dp")),
            P("col", ("row", "dp")),
            P("row", ("col", "dp")),
            P("row", ("col", "dp")),
            P("row", ("col", "dp")),
            P("col", ("row", "dp")),
            P("col", ("row", "dp")),
            P("col", ("row", "dp")),
            P("row", ("col", "dp")),
            P("row", ("col", "dp")),
            P("row", ("col", "dp")),
            P("col", ("row", "dp")),
            P("col", ("row", "dp")),
            P("col", ("row", "dp")),
            P(None, "row"),
            P(None, "row"),
            P(None, "row"),
            P(),
            P(),
            P(),
        ),
        check_vma=False,
    )
```

```python
import functools

import jax
import jax.numpy as jnp
from jax import lax
from jax.experimental import pallas as pl
from jax.experimental.pallas import tpu as pltpu
from jax.sharding import PartitionSpec as P

MODEL_WIDTH = 2048
QUERY_HEADS = 8
KEY_VALUE_HEADS = 2
HEAD_WIDTH = 256
FF = 8192
RANK = 64
PLD = 256
IMG = 256
STEP = 10


EPS = 1e-06
ROPE_BASE = 1000000.0
BETA_ONE = 0.5
BETA_TWO = 0.5
ADAM_EPS = 1e-08
DECAY = 0.01
CLIP = 1.0
LOGIT_CAP = 4.0
GAIN_RATE = 0.6
HEAD_RATE = 0.1
HALF_ROOT = 0.7071067811865476
NEGATIVE = -1e30


def joined(part, axis, combine):
    gathered = jax.tree.map(lambda a: lax.all_gather(a, axis), part)

    def take(source):
        return jax.tree.map(lambda a: lax.dynamic_index_in_dim(a, source, 0, False), gathered)

    return lax.fori_loop(
        1, lax.axis_size(axis), lambda source, state: combine(state, take(source)), take(0)
    )


def row_total(values_in):
    return lax.psum(values_in, "row")


def spread_col(values_in):
    return lax.all_gather(values_in, "col", axis=0, tiled=True)


def reduce_row(values_in):
    return lax.psum_scatter(values_in, "row", scatter_dimension=0, tiled=True)


def spread_row(values_in):
    return lax.all_gather(values_in, "row", axis=0, tiled=True)


def reduce_col(values_in):
    return lax.psum_scatter(values_in, "col", scatter_dimension=0, tiled=True)


def grads_col(values_in):
    return lax.all_gather(values_in, "col", axis=0, tiled=True)


def grads_row(values_in):
    return lax.all_gather(values_in, "row", axis=0, tiled=True)


def inner_rows(left_mat, right_mat):
    return lax.dot_general(
        left_mat, right_mat, (((0,), (0,)), ((), ())), preferred_element_type=jnp.float32
    )


def against(grad_mat, weight_mat):
    return lax.dot_general(
        grad_mat, weight_mat, (((1,), (1,)), ((), ())), preferred_element_type=jnp.float32
    )


def flat_dot(left_mat, right_mat):
    return jnp.dot(left_mat, right_mat, preferred_element_type=jnp.float32)


def norm_forward(values_in, gain_vec):
    total_sq = row_total(jnp.sum(values_in * values_in, axis=-1, keepdims=True))
    norm_scale = lax.rsqrt(total_sq / MODEL_WIDTH + EPS)
    return (values_in * norm_scale * gain_vec, norm_scale)


def norm_backward(values_in, norm_scale, gain_vec, grad_out):
    weighted = grad_out * gain_vec
    inner_sum = row_total(jnp.sum(weighted * values_in, axis=-1, keepdims=True))
    grad_in = norm_scale * weighted - values_in * (norm_scale * norm_scale * norm_scale) * (
        inner_sum / MODEL_WIDTH
    )
    return (grad_in, jnp.sum(grad_out * values_in * norm_scale, axis=0))


def norm_rows(values_in, gain_vec):
    return (
        values_in
        * lax.rsqrt(jnp.mean(values_in * values_in, axis=-1, keepdims=True) + EPS)
        * gain_vec
    )


def rope_tables(places, feat_width):
    half_width = feat_width // 2
    powers = jnp.arange(half_width, dtype=jnp.int32).astype(jnp.float32) * (2.0 / feat_width)
    frequency = jnp.power(jnp.float32(ROPE_BASE), -powers)
    angles = places.astype(jnp.float32)[:, None] * frequency[None, :]
    return (jnp.cos(angles), jnp.sin(angles))


def rotate(values_in, cos_tab, sin_tab):
    half_width = values_in.shape[-1] // 2
    part_one = values_in[..., :half_width]
    part_two = values_in[..., half_width:]
    cos_row = cos_tab[:, None, :]
    sin_row = sin_tab[:, None, :]
    return jnp.concatenate(
        [part_one * cos_row - part_two * sin_row, part_two * cos_row + part_one * sin_row], axis=-1
    )


def query_form(unscaled_rows, gain_rows, cos_tab, sin_tab):
    shaped = unscaled_rows.reshape(unscaled_rows.shape[0], gain_rows.shape[0], HEAD_WIDTH)
    return rotate(norm_rows(shaped, gain_rows[None]), cos_tab, sin_tab)


def key_form(unscaled_rows, gain_vec, cos_tab, sin_tab):
    count_of_rows = unscaled_rows.shape[0]
    key_rows = unscaled_rows[:, : KEY_VALUE_HEADS * HEAD_WIDTH].reshape(
        count_of_rows, KEY_VALUE_HEADS, HEAD_WIDTH
    )
    value_rows = unscaled_rows[:, KEY_VALUE_HEADS * HEAD_WIDTH :].reshape(
        count_of_rows, KEY_VALUE_HEADS, HEAD_WIDTH
    )
    key_rows = rotate(norm_rows(key_rows, gain_vec), cos_tab, sin_tab)
    value_rows = norm_rows(value_rows, 1.0)
    return jnp.concatenate(
        [
            key_rows.reshape(count_of_rows, KEY_VALUE_HEADS * HEAD_WIDTH),
            value_rows.reshape(count_of_rows, KEY_VALUE_HEADS * HEAD_WIDTH),
        ],
        axis=1,
    )


def piece_of(places, starts):
    inside = (places[:, None] >= starts[None, :]) & (places[:, None] < starts[None, :] + IMG)
    labels = jnp.arange(1, starts.shape[0] + 1, dtype=jnp.int32)
    return jnp.sum(jnp.where(inside, labels[None, :], 0), axis=1) - 1


def visible(query_places, key_places, query_pieces, key_pieces, length):
    causal = key_places[None, :] <= query_places[:, None]
    same_piece = (query_pieces[:, None] == key_pieces[None, :]) & (query_pieces[:, None] >= 0)
    return (key_places[None, :] < length) & (causal | same_piece)


def block_mask(own_places, key_places, key_pieces, length, starts):
    return visible(own_places, key_places, piece_of(own_places, starts), key_pieces, length)


def attention_forward(queries, key_sel, value_sel, own_places, key_places, length, starts):
    count_of_rows, head_count = (queries.shape[0], queries.shape[1])
    block_size = min(512, count_of_rows)
    key_pieces = piece_of(key_places, starts)
    stacked = queries.reshape(count_of_rows // block_size, block_size, head_count, HEAD_WIDTH)

    def one_block(element):
        block_rows, block_at = element
        allowed = block_mask(own_places, key_places, key_pieces, length, starts)
        scores = jnp.einsum("qhd,khd->hqk", block_rows, key_sel, preferred_element_type=jnp.float32)
        masked = jnp.where(allowed[None], scores, NEGATIVE)
        peak_row = jnp.max(masked, axis=-1, keepdims=True)
        raw_weights = jnp.where(allowed[None], jnp.exp(masked - peak_row), 0.0)
        total_row = jnp.sum(raw_weights, axis=-1, keepdims=True)
        attn_probs = (raw_weights / total_row).astype(jnp.bfloat16)
        outputs = jnp.einsum(
            "hqk,khd->qhd", attn_probs, value_sel, preferred_element_type=jnp.float32
        )
        return (outputs, peak_row[..., 0], total_row[..., 0])

    return lax.map(one_block, (stacked, jnp.arange(count_of_rows // block_size, dtype=jnp.int32)))


def attention_backward(
    queries,
    key_sel,
    value_sel,
    grad_attended,
    block_peaks,
    block_totals,
    own_places,
    key_places,
    length,
    starts,
):
    count_of_rows, head_count = (queries.shape[0], queries.shape[1])
    block_size = min(512, count_of_rows)
    block_count = count_of_rows // block_size
    key_pieces = piece_of(key_places, starts)
    stacked = queries.reshape(block_count, block_size, head_count, HEAD_WIDTH)
    grad_stacked = grad_attended.reshape(block_count, block_size, head_count, HEAD_WIDTH)

    def one_block(carry, element):
        dk_sum, dv_sum = carry
        block_rows, grad_rows, peak_row, total_row, block_at = element
        allowed = block_mask(own_places, key_places, key_pieces, length, starts)
        scores = jnp.einsum("qhd,khd->hqk", block_rows, key_sel, preferred_element_type=jnp.float32)
        masked = jnp.where(allowed[None], scores, NEGATIVE)
        raw_weights = jnp.where(allowed[None], jnp.exp(masked - peak_row[..., None]), 0.0)
        attn_probs = raw_weights / total_row[..., None]
        probs_low = attn_probs.astype(jnp.bfloat16)
        grad_probs = jnp.einsum(
            "qhd,khd->hqk", grad_rows, value_sel, preferred_element_type=jnp.float32
        )
        delta_row = jnp.sum(attn_probs * grad_probs, axis=-1, keepdims=True)
        grad_scores = (attn_probs * (grad_probs - delta_row)).astype(jnp.bfloat16)
        grad_query = jnp.einsum(
            "hqk,khd->qhd", grad_scores, key_sel, preferred_element_type=jnp.float32
        )
        dk_sum = dk_sum + jnp.einsum(
            "hqk,qhd->khd", grad_scores, block_rows, preferred_element_type=jnp.float32
        )
        dv_sum = dv_sum + jnp.einsum(
            "hqk,qhd->khd", probs_low, grad_rows, preferred_element_type=jnp.float32
        )
        return ((dk_sum, dv_sum), grad_query)

    zero_keys = jnp.zeros(key_sel.shape, jnp.float32)
    (dk_sum, dv_sum), grad_query = lax.scan(
        one_block,
        (zero_keys, zero_keys),
        (
            stacked,
            grad_stacked,
            block_peaks,
            block_totals,
            jnp.arange(block_count, dtype=jnp.int32),
        ),
    )
    return (grad_query.reshape(count_of_rows, head_count, HEAD_WIDTH), dk_sum, dv_sum)


def adamw_step(weight, moment_one, moment_two, gradient, rate, decay):
    moment_one = BETA_ONE * moment_one + (1.0 - BETA_ONE) * gradient
    moment_two = BETA_TWO * moment_two + (1.0 - BETA_TWO) * gradient * gradient
    mean_step = moment_one / (1.0 - BETA_ONE**STEP)
    spread = moment_two / (1.0 - BETA_TWO**STEP)
    return (
        moment_one,
        moment_two,
        weight - rate * (mean_step / (jnp.sqrt(spread) + ADAM_EPS) + decay * weight),
    )


MESH = pl.DeviceIdType.MESH
LOW = jnp.bfloat16
FULL = jnp.float32


def cost(micros, flops=0):
    return pl.CostEstimate(
        flops=flops, bytes_accessed=int(micros * 3.0e6), transcendentals=0
    )


def params(ident, mebibytes=48):
    return pltpu.CompilerParams(
        collective_id=ident, has_side_effects=True, vmem_limit_bytes=mebibytes * 2**20
    )


def push(source, target, send, recv, device):
    return pltpu.make_async_remote_copy(
        source, target, send, recv, device_id=device, device_id_type=MESH
    )


class Line:
    def __init__(self, source, shape, place, core=False, view=None):
        self.source, self.shape, self.place, self.core = source, shape, place, core
        self.view = view

    def semaphores(self, count, data):
        dma = pltpu.SemaphoreType.DMA
        return [dma((count,)), dma((count,)), dma((2 * count,))] * 2 + [dma]

    def bind(self, x_ref, o_ref, sems, spots, sizes):
        self.o_ref, self.sems = o_ref, sems
        self.me, self.column, self.at = spots
        self.count = sizes[0]
        self.x_ref = self.view(x_ref, self.column) if self.view else x_ref

    def slot(self, source):
        return self.place(self.o_ref, self.column, source)

    def other(self, source):
        return self.place(self.o_ref, 1 - self.column, source)

    def to_left(self, source, k, origin):
        return push(origin, self.slot(source), self.sems[0].at[k], self.sems[4].at[k], {"row": self.me - 1})

    def to_right(self, source, k, origin):
        return push(origin, self.slot(source), self.sems[1].at[k], self.sems[3].at[k], {"row": self.me + 1})

    def to_core(self, source, k, origin):
        return push(origin, self.slot(source), self.sems[2].at[k], self.sems[5].at[k], {"col": 1 - self.column})

    def from_core(self, source, k):
        there = self.other(source)
        return push(there, there, self.sems[2].at[k], self.sems[5].at[k], {"col": 1 - self.column})

    def from_left(self, source, k):
        there = self.slot(source)
        return push(there, there, self.sems[1].at[k], self.sems[3].at[k - 1], {"row": self.me - 1})

    def from_right(self, source, k):
        there = self.slot(source)
        return push(there, there, self.sems[0].at[k], self.sems[4].at[k - 1], {"row": self.me + 1})

    def own(self):
        return pltpu.make_async_copy(self.x_ref, self.slot(self.me), self.sems[6])

    def start(self):
        me, count = self.me, self.count

        @pl.when(me > 0)
        def _():
            self.to_left(me, 0, self.x_ref).start()

        @pl.when(me < count - 1)
        def _():
            self.to_right(me, 0, self.x_ref).start()

        if self.core:
            self.to_core(me, 0, self.x_ref).start()
        self.own().start()

    def step(self, k):
        me, count = self.me, self.count

        @pl.when(me - k >= 0)
        def _():
            self.from_left(me - k, k).wait_recv()
            block = self.slot(me - k)

            @pl.when(me < count - 1)
            def _():
                self.to_right(me - k, k, block).start()

            if self.core:
                self.to_core(me - k, k, block).start()

        @pl.when(me + k < count)
        def _():
            self.from_right(me + k, k).wait_recv()
            block = self.slot(me + k)

            @pl.when(me > 0)
            def _():
                self.to_left(me + k, k, block).start()

            if self.core:
                self.to_core(me + k, count - 1 + k, block).start()

    def finish(self):
        me, count = self.me, self.count
        self.own().wait()

        @pl.when(me > 0)
        def _():
            self.to_left(me, 0, self.x_ref).wait_send()

        @pl.when(me < count - 1)
        def _():
            self.to_right(me, 0, self.x_ref).wait_send()

        if self.core:
            self.to_core(me, 0, self.x_ref).wait_send()
            self.from_core(me, 0).wait_recv()

        @pl.loop(1, count)
        def _(k):
            @pl.when(me - k >= 0)
            def _():
                @pl.when(me < count - 1)
                def _():
                    self.to_right(me - k, k, self.x_ref).wait_send()

                if self.core:
                    self.to_core(me - k, k, self.x_ref).wait_send()
                    self.from_core(me - k, k).wait_recv()

            @pl.when(me + k < count)
            def _():
                @pl.when(me > 0)
                def _():
                    self.to_left(me + k, k, self.x_ref).wait_send()

                if self.core:
                    self.to_core(me + k, count - 1 + k, self.x_ref).wait_send()
                    self.from_core(me + k, count - 1 + k).wait_recv()


class Swap:
    def __init__(self, source, shape, take, place, axis="row"):
        self.source, self.shape, self.take, self.place = source, shape, take, place
        self.axis = axis

    def semaphores(self, count, data):
        size = count if self.axis == "row" else data
        return [pltpu.SemaphoreType.DMA((size,)), pltpu.SemaphoreType.DMA((size,))]

    def bind(self, x_ref, o_ref, sems, spots, sizes):
        self.x_ref, self.o_ref, self.sems = x_ref, o_ref, sems
        self.me = spots[0] if self.axis == "row" else spots[2]
        self.count = sizes[0] if self.axis == "row" else sizes[1]

    def copy(self, k):
        target = lax.rem(self.me + k, self.count)
        return push(
            self.take(self.x_ref, target),
            self.place(self.o_ref, self.me),
            self.sems[0].at[k],
            self.sems[1].at[k],
            {self.axis: target},
        )

    def own(self):
        return pltpu.make_async_copy(
            self.take(self.x_ref, self.me), self.place(self.o_ref, self.me), self.sems[0].at[0]
        )

    def start(self):
        for k in range(1, self.count):
            self.copy(k).start()
        self.own().start()

    def step(self, k):
        pass

    def finish(self):
        self.own().wait()
        for k in range(1, self.count):
            self.copy(k).wait_send()
            origin = lax.rem(self.me + self.count - k, self.count)
            there = self.place(self.o_ref, origin)
            push(there, there, self.sems[0].at[k], self.sems[1].at[k], {self.axis: origin}).wait_recv()


class Pair:
    core = True

    def __init__(self, source):
        self.source, self.shape = source, source.shape

    def semaphores(self, count, data):
        dma = pltpu.SemaphoreType.DMA
        return [dma, dma, dma]

    def bind(self, x_ref, o_ref, sems, spots, sizes):
        self.x_ref, self.o_ref, self.sems = x_ref, o_ref, sems
        self.column = spots[1]

    def copy(self):
        other = 1 - self.column
        return push(self.x_ref.at[other], self.o_ref.at[1], self.sems[0], self.sems[1], {"col": other})

    def own(self):
        return pltpu.make_async_copy(self.x_ref.at[self.column], self.o_ref.at[0], self.sems[2])

    def start(self):
        self.copy().start()
        self.own().start()

    def step(self, k):
        pass

    def finish(self):
        self.own().wait()
        self.copy().wait()


class Reduce:
    def __init__(self, source, shape, cut, core=True):
        self.source, self.shape, self.cut, self.core = source, shape, cut, core
        self.high, self.wide = shape
        self.dtype = FULL

    def semaphores(self, count, data):
        dma = pltpu.SemaphoreType.DMA
        slots = pltpu.VMEM((count,) + self.shape, self.source.dtype)
        whole = pltpu.VMEM(self.source.shape[1:] if self.core else self.source.shape, self.source.dtype)
        stage = pltpu.VMEM(self.shape, FULL)
        fourth = slots if self.core else pltpu.VMEM((1, 16, 128), self.source.dtype)
        return [whole, stage, slots, slots, slots, fourth] + [dma((count,))] * 6 + [dma, dma]

    def bind(self, x_ref, o_ref, sems, spots, sizes):
        self.x_ref, self.o_ref = x_ref, o_ref
        self.mine, self.stage, self.out, self.left_in, self.right_in, self.core_in = sems[:6]
        self.sems = sems[6:]
        self.me, self.column = spots[0], spots[1]
        self.count = sizes[0]

    def beside(self, q):
        return push(
            self.cut(self.x_ref.at[1 - self.column], q),
            self.core_in.at[q],
            self.sems[0].at[q],
            self.sems[3].at[q],
            {"col": 1 - self.column},
        )

    def to_left(self, q):
        return push(self.out.at[q], self.left_in.at[q], self.sems[1].at[q], self.sems[4].at[q], {"row": self.me - 1})

    def to_right(self, q):
        return push(self.out.at[q], self.right_in.at[q], self.sems[2].at[q], self.sems[5].at[q], {"row": self.me + 1})

    def from_right(self, q):
        return push(self.left_in.at[q], self.left_in.at[q], self.sems[1].at[q], self.sems[4].at[q], {"row": self.me + 1})

    def from_left(self, q):
        return push(self.right_in.at[q], self.right_in.at[q], self.sems[2].at[q], self.sems[5].at[q], {"row": self.me - 1})

    def own(self):
        return pltpu.make_async_copy(
            self.x_ref.at[self.column] if self.core else self.x_ref, self.mine, self.sems[6]
        )

    def start(self):
        self.own().start()
        if self.core:
            for q in range(self.count):
                self.beside(q).start()

    def added(self, target, q, others):
        step = min(self.high, max(16, 65536 // self.wide))
        while self.high % step:
            step //= 2
        cut = self.cut(self.mine, q)
        others = ([self.core_in] if self.core else []) + others

        @pl.loop(0, self.high // step)
        def _(at):
            rows = pl.ds(pl.multiple_of(at * step, step), step)
            total = cut[rows].astype(FULL)
            for other in others:
                total = total + other[q, rows].astype(FULL)
            target[rows] = total.astype(target.dtype)

    def step(self, k):
        me, count = self.me, self.count
        t = k - 1
        q_left = t - (count - 1 - me)
        q_right = count - 1 - (t - me)

        @pl.when(t == 0)
        def _():
            self.own().wait()

        @pl.when((q_left >= 0) & (q_left < me))
        def _():
            if self.core:
                self.beside(q_left).wait()

            @pl.when(me < count - 1)
            def _():
                self.from_right(q_left).wait_recv()
                self.added(self.out.at[q_left], q_left, [self.left_in])

            @pl.when(me == count - 1)
            def _():
                self.added(self.out.at[q_left], q_left, [])

            self.to_left(q_left).start()

        @pl.when((t >= me) & (q_right > me))
        def _():
            if self.core:
                self.beside(q_right).wait()

            @pl.when(me > 0)
            def _():
                self.from_left(q_right).wait_recv()
                self.added(self.out.at[q_right], q_right, [self.right_in])

            @pl.when(me == 0)
            def _():
                self.added(self.out.at[q_right], q_right, [])

            self.to_right(q_right).start()

    def finish(self):
        me, count = self.me, self.count
        if self.core:
            self.beside(me).wait()

        @pl.when(me < count - 1)
        def _():
            self.from_right(me).wait_recv()

        @pl.when(me > 0)
        def _():
            self.from_left(me).wait_recv()

        @pl.when(me == 0)
        def _():
            self.added(self.stage, me, [self.left_in])

        @pl.when(me == count - 1)
        def _():
            self.added(self.stage, me, [self.right_in])

        @pl.when((me > 0) & (me < count - 1))
        def _():
            self.added(self.stage, me, [self.left_in, self.right_in])

        out = pltpu.make_async_copy(self.stage, self.o_ref, self.sems[7])
        out.start()

        @pl.loop(0, count)
        def _(q):
            @pl.when(q < me)
            def _():
                self.to_left(q).wait_send()

            @pl.when(q > me)
            def _():
                self.to_right(q).wait_send()

        out.wait()


class ShardSum:
    axis = "dp"

    def __init__(self, source, out_cols):
        self.source, self.out_cols = source, out_cols
        self.parts = source.shape[1] // out_cols // lax.axis_size("dp")
        self.shape = (source.shape[0], self.parts * out_cols)

    def semaphores(self, count, data):
        dma = pltpu.SemaphoreType.DMA
        buf = pltpu.VMEM((data,) + self.shape, self.source.dtype)
        stage = pltpu.VMEM(self.shape, self.source.dtype)
        return [buf, stage, dma((data, self.parts)), dma((data, self.parts)), dma]

    def bind(self, x_ref, o_ref, sems, spots, sizes):
        self.x_ref, self.o_ref = x_ref, o_ref
        self.buf, self.stage, self.send, self.recv, self.local = sems
        self.at, self.data = spots[2], sizes[1]

    def copy(self, k, s):
        target = lax.rem(self.at + k, self.data)
        wide = self.out_cols
        source = self.x_ref.at[:, pl.ds(pl.multiple_of((s * self.data + target) * wide, wide), wide)]
        slot = self.buf.at[k, :, pl.ds(s * wide, wide)]
        if k == 0:
            return pltpu.make_async_copy(source, slot, self.send.at[k, s])
        return push(source, slot, self.send.at[k, s], self.recv.at[k, s], {"dp": target})

    def start(self):
        for k in range(self.data):
            for s in range(self.parts):
                self.copy(k, s).start()

    def step(self, k):
        pass

    def finish(self):
        for k in range(self.data):
            for s in range(self.parts):
                self.copy(k, s).wait()

        @pl.loop(0, self.shape[0] // 64)
        def _(at):
            rows = pl.ds(pl.multiple_of(at * 64, 64), 64)
            total = self.buf[0, rows].astype(FULL)
            for k in range(1, self.data):
                total = total + self.buf[k, rows].astype(FULL)
            self.stage[rows] = total.astype(self.stage.dtype)

        out = pltpu.make_async_copy(self.stage, self.o_ref, self.local)
        out.start()
        out.wait()


class Bundle:
    def __init__(self, items):
        self.items = items
        self.number = len(items)
        self.sizes = lax.axis_size("row"), lax.axis_size("dp")
        self.kinds = [item.semaphores(*self.sizes) for item in items]
        self.across = any(getattr(item, "axis", None) == "dp" for item in items)
        self.cores = any(getattr(item, "core", False) for item in items)
        self.sources = [item.source for item in items]
        self.shapes = [
            jax.ShapeDtypeStruct(item.shape, getattr(item, "dtype", item.source.dtype)) for item in items
        ]
        self.specs = [pl.BlockSpec(memory_space=pl.ANY)] * self.number
        self.scratch = sum(self.kinds, [])

    def bind(self, x_refs, o_refs, sems):
        self.spots = lax.axis_index("row"), lax.axis_index("col"), lax.axis_index("dp")
        for item, x_ref, o_ref, kind in zip(self.items, x_refs, o_refs, self.kinds):
            item.bind(x_ref, o_ref, sems[: len(kind)], self.spots, self.sizes)
            sems = sems[len(kind) :]

    def greet(self, across=False, cores=False):
        me, column, at = self.spots
        count, data = self.sizes
        across, cores = across or self.across, cores or self.cores
        barrier = pltpu.get_barrier_semaphore()
        for k in range(1, count):
            pl.semaphore_signal(
                barrier, inc=1, device_id={"row": lax.rem(me + k, count)}, device_id_type=MESH
            )
        if across:
            for k in range(1, data):
                pl.semaphore_signal(
                    barrier, inc=1, device_id={"dp": lax.rem(at + k, data)}, device_id_type=MESH
                )
        if cores:
            pl.semaphore_signal(barrier, inc=1, device_id={"col": 1 - column}, device_id_type=MESH)
        pl.semaphore_wait(barrier, count - 1 + (data - 1) * int(across) + int(cores))

    def start(self):
        for item in self.items:
            item.start()

    def step(self, k):
        for item in self.items:
            item.step(k)

    def finish(self):
        for item in self.items:
            item.finish()


def transfers(items, ident, micros, mebibytes=16, work=None, arrays=(), shapes=()):
    bundle = Bundle(items)
    number, given, made = bundle.number, len(arrays), len(shapes)

    def kernel(*refs):
        inputs, refs = refs[:given], refs[given:]
        x_refs, refs = refs[:number], refs[number:]
        outputs, refs = refs[:made], refs[made:]
        bundle.bind(x_refs, refs[:number], refs[number:])
        bundle.greet()
        bundle.start()
        if work:
            work(inputs, outputs)
        for k in range(1, bundle.sizes[0]):
            bundle.step(k)
        bundle.finish()

    vmem = pl.BlockSpec(memory_space=pltpu.VMEM)
    return pl.pallas_call(
        kernel,
        out_shape=list(shapes) + bundle.shapes,
        in_specs=[vmem] * given + bundle.specs,
        out_specs=[vmem] * made + bundle.specs,
        scratch_shapes=bundle.scratch,
        compiler_params=params(ident, mebibytes),
        cost_estimate=cost(micros),
    )(*arrays, *bundle.sources)


def local(function, shapes, *arrays, mebibytes=60):
    def kernel(*refs):
        results = function(*[ref[...] for ref in refs[: len(arrays)]])
        for ref, value in zip(refs[len(arrays) :], results):
            ref[...] = value.astype(ref.dtype)

    vmem = pl.BlockSpec(memory_space=pltpu.VMEM)
    return pl.pallas_call(
        kernel,
        out_shape=[jax.ShapeDtypeStruct(shape, kind) for shape, kind in shapes],
        in_specs=[vmem] * len(arrays),
        out_specs=[vmem] * len(shapes),
        compiler_params=pltpu.CompilerParams(vmem_limit_bytes=mebibytes * 2**20),
        cost_estimate=cost(5),
    )(*arrays)


def norm_back(values_in, gain, grad_out):
    scale = lax.rsqrt(jnp.mean(values_in * values_in, axis=-1, keepdims=True) + EPS)
    weighted = grad_out * gain
    inner = jnp.mean(weighted * values_in, axis=-1, keepdims=True)
    return (
        scale * weighted - values_in * (scale * scale * scale) * inner,
        jnp.sum(grad_out * values_in * scale, axis=0, keepdims=True),
    )


def mix(acts, projected, gains, left_t, right_w):
    inputs = acts.astype(FULL)
    hidden, _ = whole_norm(inputs, gains[0:1])
    hidden_low = hidden.astype(LOW)
    middle = against(hidden_low, left_t).astype(LOW)
    right_raw = flat_dot(middle, right_w)
    right_n, _ = whole_norm(right_raw, gains[1:2])
    proj_n, _ = whole_norm(projected, gains[2:3])
    mixture = ((inputs + proj_n) + (hidden + right_n)) * HALF_ROOT
    ffn_n, _ = whole_norm(mixture, gains[3:4])
    return hidden_low, middle, right_raw, mixture, ffn_n


def per_layer_both(mixture, down_raw, gains, extras, pergate_t, perproj_w, upstream):
    extras, upstream = extras.astype(FULL), upstream.astype(FULL)
    down_n, _ = whole_norm(down_raw, gains[4:5])
    block_out = mixture + down_n
    out_low = block_out.astype(LOW)
    pgate = against(out_low, pergate_t)
    curve, slope = gelu_of(pgate)
    pact = (curve * extras).astype(LOW)
    perproj = flat_dot(pact, perproj_w)
    perproj_n, _ = whole_norm(perproj, gains[5:6])
    result = block_out + perproj_n
    d_perproj, gain_five = norm_back(perproj, gains[5:6], upstream)
    d_perproj = d_perproj.astype(LOW)
    d_pact = against(d_perproj, perproj_w)
    d_pgate = (d_pact * extras * slope).astype(LOW)
    d_out = upstream + flat_dot(d_pgate, pergate_t)
    d_down, gain_four = norm_back(down_raw, gains[4:5], d_out)
    return (
        result,
        d_out,
        d_down,
        inner_rows(pact, d_perproj),
        inner_rows(d_pgate, out_low),
        gain_four,
        gain_five,
    )


def mix_back(
    d_out, d_ffn, mixture, projected, right_raw, gains, acts, left_t, right_w, hidden_low, middle, dw_pergate, dw_perproj
):
    d_mix, gain_three = norm_back(mixture, gains[3:4], d_ffn)
    d_half = (d_out + d_mix) * HALF_ROOT
    d_proj, gain_two = norm_back(projected, gains[2:3], d_half)
    d_right, gain_one = norm_back(right_raw, gains[1:2], d_half)
    d_right = d_right.astype(LOW)
    dw_right = inner_rows(middle, d_right).astype(LOW)
    d_middle = against(d_right, right_w).astype(LOW)
    dw_left = inner_rows(d_middle, hidden_low).astype(LOW)
    d_hidden = d_half + flat_dot(d_middle, left_t)
    inner = row_sums(d_hidden * gains[0:1] * acts.astype(FULL))
    parts = []
    for core in range(2):
        for grad in (dw_left, dw_right, dw_pergate, dw_perproj):
            high = grad.shape[0] // 2
            parts.append(grad[core * high : (core + 1) * high])
    return d_proj, d_half, d_middle, jnp.concatenate(parts, axis=0), inner, gain_one, gain_two, gain_three


def row_sums(values_in):
    ones = jnp.ones((8, values_in.shape[1]), FULL)
    return lax.dot_general(
        ones,
        values_in,
        (((1,), (1,)), ((), ())),
        precision=lax.Precision.HIGHEST,
        preferred_element_type=FULL,
    )


def shard_parts(sums, extents):
    out_cols, data = 128, sums.shape[1] // 128
    parts = []
    for at in range(data):
        start = 0
        for rows, by_rows in extents:
            if by_rows:
                high = rows // data
                cut = sums[start + at * high : start + (at + 1) * high]
                parts += [cut[:, k * out_cols : (k + 1) * out_cols] for k in range(data)]
            else:
                parts.append(sums[start : start + rows, at * out_cols : (at + 1) * out_cols])
            start += rows
    return jnp.concatenate(parts, axis=0)


def key_value_ends(hidden, d_key, d_value, qkv_w, d_hidden, acts, gain, sums, extents):
    first = lax.axis_index("col") == 0
    key_w = jnp.where(first, qkv_w[0, :, HEAD_WIDTH:], qkv_w[1, :, HEAD_WIDTH:])
    value_w = jnp.where(first, qkv_w[2, :, HEAD_WIDTH:], qkv_w[3, :, HEAD_WIDTH:])
    d_hidden = d_hidden + against(d_key, key_w) + against(d_value, value_w)
    return (
        jnp.concatenate([inner_rows(hidden, d_key), inner_rows(hidden, d_value)], axis=0),
        d_hidden,
        row_sums(d_hidden * gain[0:1] * acts.astype(FULL)),
        shard_parts(sums, extents),
    )


def input_ends(pair, half, middle, left_t, acts, scale, gains, inner, inner_share, grads, gateup_squares, gain_grads, dg_query, dg_key, top):
    half_tok, wide = acts.shape
    rows_n = inner.shape[1]
    width = gain_grads[0].shape[1]
    lanes = width // 128
    head_rows = (QUERY_HEADS + 1) * HEAD_WIDTH // 128
    sum_rows = 6 * lanes + head_rows
    high = -(-(sum_rows + 1) // 8) * 8 + 8
    given = (pair, half, middle, left_t, acts, scale, gains, inner, inner_share, gateup_squares, dg_query, dg_key, top)
    given += tuple(gain_grads) + tuple(grads)

    def kernel(*refs):
        pair, half, middle, left_t, acts, scale, gains, inner, inner_share, gateup_squares, dg_query, dg_key, top = refs[:13]
        gain_grads, grads = refs[13:18], refs[18:23]
        out_ref, small_ref = refs[23:]
        me, column = lax.axis_index("row"), lax.axis_index("col")
        total = None
        for core in range(2):
            for row in range(rows_n):
                part = jnp.where(
                    column == 0, inner[core, row, :, :half_tok], inner[core, row, :, half_tok:]
                )
                total = part if total is None else total + part
        shares = jnp.concatenate(
            [jnp.where(column == 0, inner_share[0, row], inner_share[1, row]) for row in range(rows_n)],
            axis=1,
        )
        mean = ((total + shares) / MODEL_WIDTH).T[:, :1]
        inputs = acts[...].astype(FULL)
        factor = scale[:, :1]
        gain = gains[0:1]
        left = left_t[:, pl.ds(pl.multiple_of(me * wide, wide), wide)]
        d_hidden = (
            pair[0].astype(FULL) + pair[1].astype(FULL) + half[...].astype(FULL) + flat_dot(middle[...], left)
        )
        out_ref[...] = (
            half[...].astype(FULL)
            + factor * (d_hidden * gain)
            - inputs * (factor * factor * factor) * mean
        ).astype(LOW)
        small_ref[...] = jnp.zeros(small_ref.shape, FULL)
        gain_zero = jnp.sum(d_hidden * inputs * factor, axis=0, keepdims=True)
        for k in range(wide // 128):
            small_ref[pl.ds(me * (wide // 128) + k, 1)] = gain_zero[:, k * 128 : (k + 1) * 128]
        for at, grad in enumerate(gain_grads):
            for k in range(lanes):
                small_ref[(at + 1) * lanes + k : (at + 1) * lanes + k + 1] = grad[:, k * 128 : (k + 1) * 128]
        head = column * rows_n + me
        for k in range(HEAD_WIDTH // 128):
            cut = slice(k * 128, (k + 1) * 128)
            small_ref[pl.ds(6 * lanes + head * (HEAD_WIDTH // 128) + k, 1)] = dg_query[:, cut]
            last = 6 * lanes + QUERY_HEADS * (HEAD_WIDTH // 128) + k
            small_ref[last : last + 1] = dg_key[:, cut]
        squares = jnp.zeros((1, 128), FULL)
        first = jnp.where(column == 0, 1.0, 0.0)
        for grad, weight in zip(grads, (1.0, first, 1.0, 1.0, 1.0)):
            values = grad[...].astype(FULL).reshape(-1, grad.shape[-1])
            line = jnp.sum(values * values, axis=0, keepdims=True)
            for cut in range(0, values.shape[1], 128):
                squares = squares + weight * line[:, cut : cut + 128]
        line = jnp.sum(gateup_squares[...], axis=0, keepdims=True)
        for cut in range(0, line.shape[1], 128):
            squares = squares + line[:, cut : cut + 128]
        small_ref[sum_rows : sum_rows + 1] = jnp.broadcast_to(
            jnp.sum(squares, axis=1, keepdims=True), (1, 128)
        )
        places = lax.broadcasted_iota(jnp.int32, (8, 128), 1)
        small_ref[high - 8 :] = jnp.where(places == head, top[...], NEGATIVE)

    vmem = pl.BlockSpec(memory_space=pltpu.VMEM)
    return pl.pallas_call(
        kernel,
        out_shape=[
            jax.ShapeDtypeStruct((half_tok, wide), LOW),
            jax.ShapeDtypeStruct((high, 128), FULL),
        ],
        in_specs=[vmem] * 23,
        out_specs=[vmem] * 2,
        compiler_params=pltpu.CompilerParams(vmem_limit_bytes=24 * 2**20),
        cost_estimate=cost(3),
    )(*given)


def key_value_back(d_kv, key_raw, value_raw, heads, cos_tab, sin_tab):
    key_gain = heads[QUERY_HEADS:]
    quarter = key_raw.shape[0]
    d_key, dg_key = norm_back(key_raw, key_gain, turn_back(d_kv[:quarter], cos_tab, sin_tab))
    d_value, _ = norm_back(value_raw, 1.0, d_kv[quarter:])
    return d_key, d_value, dg_key


def shard_total(query_parts, kv_parts, flat_parts, items, ident):
    data = lax.axis_size("dp")
    bundle = Bundle(items)
    number = bundle.number

    def kernel(q_ref, kv_ref, f_ref, *refs):
        x_refs, refs = refs[:number], refs[number:]
        oq_ref, okv_ref, of_ref = refs[:3]
        o_refs, refs = refs[3 : 3 + number], refs[3 + number :]
        q_buf, kv_buf, f_buf = refs[:3]
        sems = refs[3:11]
        bundle.bind(x_refs, o_refs, refs[11:])
        column, at = lax.axis_index("col"), lax.axis_index("dp")
        bundle.greet(True, True)
        bundle.start()
        mine = lax.rem(at, 2) == column

        def copies(k):
            target = lax.rem(at + k, data)
            device = {"dp": target}
            return (
                push(q_ref.at[target], q_buf.at[k], sems[0].at[k], sems[1].at[k], device),
                push(kv_ref.at[target // 2], kv_buf.at[k], sems[2].at[k], sems[3].at[k], device),
                push(f_ref.at[target], f_buf.at[k], sems[4].at[k], sems[5].at[k], device),
                lax.rem(target, 2) == column,
            )

        for k in range(1, data):
            query_copy, kv_copy, flat_copy, there = copies(k)
            query_copy.start()
            flat_copy.start()

            @pl.when(there)
            def _():
                kv_copy.start()

        for k in range(1, data):
            query_copy, kv_copy, flat_copy, there = copies(k)
            query_copy.wait()
            flat_copy.wait()

            @pl.when(there)
            def _():
                kv_copy.wait_send()

            @pl.when(mine)
            def _():
                kv_copy.wait_recv()

        def added(target, own, buf, chunk):
            @pl.loop(0, target.shape[0] // chunk)
            def _(step):
                rows = pl.ds(pl.multiple_of(step * chunk, chunk), chunk)
                total = own[rows].astype(FULL)
                for k in range(1, data):
                    total = total + buf[k, rows].astype(FULL)
                target[rows] = total

        share = push(okv_ref, okv_ref, sems[6], sems[7], {"col": 1 - column})

        @pl.when(mine)
        def _():
            added(okv_ref, kv_ref.at[at // 2], kv_buf, 128)
            share.start()

        added(oq_ref, q_ref.at[at], q_buf, 128)
        added(of_ref, f_ref.at[at], f_buf, 64)

        @pl.when(mine)
        def _():
            share.wait_send()

        @pl.when(jnp.logical_not(mine))
        def _():
            share.wait_recv()

        for k in range(1, bundle.sizes[0]):
            bundle.step(k)
        bundle.finish()

    vmem = pl.BlockSpec(memory_space=pltpu.VMEM)
    dma = pltpu.SemaphoreType.DMA
    shapes = [query_parts.shape[1:], kv_parts.shape[1:], flat_parts.shape[1:]]
    return pl.pallas_call(
        kernel,
        out_shape=[jax.ShapeDtypeStruct(shape, FULL) for shape in shapes] + bundle.shapes,
        in_specs=[vmem] * 3 + bundle.specs,
        out_specs=[vmem] * 3 + bundle.specs,
        scratch_shapes=[pltpu.VMEM((data,) + shape, LOW) for shape in shapes]
        + [dma((data,))] * 6
        + [dma, dma]
        + bundle.scratch,
        compiler_params=params(ident),
        cost_estimate=cost(40),
    )(query_parts, kv_parts, flat_parts, *bundle.sources)


CHUNKS = 4


class Flow:
    def __init__(self, x_ref, blocks, own, core_out, core_in, left_in, right_in, sems):
        self.x_ref, self.blocks, self.own = x_ref, blocks, own
        self.core_out, self.core_in = core_out, core_in
        self.left_in, self.right_in = left_in, right_in
        self.sems = sems
        self.me, self.column = lax.axis_index("row"), lax.axis_index("col")
        self.count = blocks.shape[0]

    @staticmethod
    def scratch(count, share, width):
        dma = pltpu.SemaphoreType.DMA
        slots = (count, share, width)
        return [
            pltpu.VMEM((count, 2, share, width), LOW),
            pltpu.VMEM(slots, FULL),
            pltpu.VMEM(slots, LOW),
            pltpu.VMEM(slots, LOW),
            pltpu.VMEM(slots, LOW),
            pltpu.VMEM(slots, LOW),
        ], [dma((count,))] * 7 + [dma((count * CHUNKS,))] * 2 + [dma((count,))] + [
            dma((count * CHUNKS,))
        ] * 2 + [dma]

    def left(self):
        return {"row": self.me - 1}

    def right(self):
        return {"row": self.me + 1}

    def beside(self):
        return {"col": 1 - self.column}

    def to_left(self, source, k, origin):
        return push(origin, self.blocks.at[source, 0], self.sems[0].at[k], self.sems[4].at[k], self.left())

    def to_right(self, source, k, origin):
        return push(origin, self.blocks.at[source, 0], self.sems[1].at[k], self.sems[3].at[k], self.right())

    def to_core(self, source, origin):
        return push(origin, self.blocks.at[source, 1], self.sems[2].at[source], self.sems[5].at[source], self.beside())

    def back_core(self, q):
        return push(self.core_out.at[q], self.core_in.at[q], self.sems[6].at[q], self.sems[9].at[q], self.beside())

    def part(self, ref, q, j):
        size = ref.shape[1] // CHUNKS
        return ref.at[q, pl.ds(pl.multiple_of(j * size, size), size)]

    def back_left(self, q, j):
        at = q * CHUNKS + j
        return push(
            self.part(self.core_out, q, j),
            self.part(self.left_in, q, j),
            self.sems[7].at[at],
            self.sems[10].at[at],
            self.left(),
        )

    def back_right(self, q, j):
        at = q * CHUNKS + j
        return push(
            self.part(self.core_out, q, j),
            self.part(self.right_in, q, j),
            self.sems[8].at[at],
            self.sems[11].at[at],
            self.right(),
        )

    def from_right(self, q, j):
        at, there = q * CHUNKS + j, self.part(self.left_in, q, j)
        return push(there, there, self.sems[7].at[at], self.sems[10].at[at], self.right())

    def from_left(self, q, j):
        at, there = q * CHUNKS + j, self.part(self.right_in, q, j)
        return push(there, there, self.sems[8].at[at], self.sems[11].at[at], self.left())

    def mine(self):
        return pltpu.make_async_copy(self.x_ref, self.blocks.at[self.me, 0], self.sems[12])

    def start(self):
        me, count = self.me, self.count

        @pl.when(me > 0)
        def _():
            self.to_left(me, 0, self.x_ref).start()

        @pl.when(me < count - 1)
        def _():
            self.to_right(me, 0, self.x_ref).start()

        self.to_core(me, self.x_ref).start()
        self.mine().start()

    def arrive(self, k):
        me, count = self.me, self.count

        @pl.when(k == 0)
        def _():
            self.mine().wait()
            self.to_core(me, self.x_ref).wait()

        @pl.when((k > 0) & (me - k >= 0))
        def _():
            source = me - k
            block = self.blocks.at[source, 0]
            push(block, block, self.sems[1].at[k], self.sems[3].at[k - 1], self.left()).wait_recv()

            @pl.when(me < count - 1)
            def _():
                self.to_right(source, k, block).start()

            self.to_core(source, block).start()

        @pl.when((k > 0) & (me + k < count))
        def _():
            source = me + k
            block = self.blocks.at[source, 0]
            push(block, block, self.sems[0].at[k], self.sems[4].at[k - 1], self.right()).wait_recv()

            @pl.when(me > 0)
            def _():
                self.to_left(source, k, block).start()

            self.to_core(source, block).start()

        @pl.when((k > 0) & (me - k >= 0))
        def _():
            self.to_core(me - k, self.x_ref).wait()

        @pl.when((k > 0) & (me + k < count))
        def _():
            self.to_core(me + k, self.x_ref).wait()

    def reach(self):
        return jnp.maximum(self.me, self.count - 1 - self.me)

    def visit(self, body, bundle, after=None):
        me, count = self.me, self.count

        @pl.loop(0, count)
        def _(k):
            self.arrive(k)

            @pl.when(k == count - 2)
            def _():
                bundle.start()

            @pl.when(k == count - 1)
            def _():
                bundle.step(1)

            @pl.loop(0, 2)
            def _(side):
                source = jnp.where(side == 0, me - k, me + k)

                @pl.when((source >= 0) & (source < count) & ((side == 0) | (k > 0)))
                def _():
                    body(source)
                    self.back_core(source).start()

            if after:
                after(k, k - self.reach() - 1)
            self.give_back(k)

    def added(self, target, terms):
        total = terms[0][...]
        for term in terms[1:]:
            total = total + term[...].astype(FULL)
        target[...] = total.astype(target.dtype)

    def give_back(self, t):
        me, count = self.me, self.count
        q_left = 2 * (count - 1) - me - t
        q_right = t - me

        def leftward():
            q = q_left
            self.back_core(q).wait()

            @pl.loop(0, CHUNKS)
            def _(j):
                base = [self.part(self.own, q, j), self.part(self.core_in, q, j)]
                target = self.part(self.core_out, q, j)

                @pl.when(me < count - 1)
                def _():
                    self.from_right(q, j).wait_recv()
                    self.added(target, base + [self.part(self.left_in, q, j)])

                @pl.when(me == count - 1)
                def _():
                    self.added(target, base)

                self.back_left(q, j).start()

        def rightward():
            q = q_right
            self.back_core(q).wait()

            @pl.loop(0, CHUNKS)
            def _(j):
                base = [self.part(self.own, q, j), self.part(self.core_in, q, j)]
                target = self.part(self.core_out, q, j)

                @pl.when(me > 0)
                def _():
                    self.from_left(q, j).wait_recv()
                    self.added(target, base + [self.part(self.right_in, q, j)])

                @pl.when(me == 0)
                def _():
                    self.added(target, base)

                self.back_right(q, j).start()

        pl.when((q_left >= 0) & (q_left < me))(leftward)
        pl.when((q_right > me) & (q_right < count))(rightward)

    def finish(self, o_ref):
        me, count = self.me, self.count
        self.back_core(me).wait()

        @pl.loop(0, CHUNKS)
        def _(j):
            size = o_ref.shape[0] // CHUNKS
            target = o_ref.at[pl.ds(pl.multiple_of(j * size, size), size)]
            base = [self.part(self.own, me, j), self.part(self.core_in, me, j)]

            @pl.when(me < count - 1)
            def _():
                self.from_right(me, j).wait_recv()

            @pl.when(me > 0)
            def _():
                self.from_left(me, j).wait_recv()

            @pl.when(me == 0)
            def _():
                self.added(target, base + [self.part(self.left_in, me, j)])

            @pl.when(me == count - 1)
            def _():
                self.added(target, base + [self.part(self.right_in, me, j)])

            @pl.when((me > 0) & (me < count - 1))
            def _():
                self.added(
                    target, base + [self.part(self.left_in, me, j), self.part(self.right_in, me, j)]
                )

        @pl.when(me > 0)
        def _():
            self.to_left(me, 0, self.x_ref).wait_send()

        @pl.when(me < count - 1)
        def _():
            self.to_right(me, 0, self.x_ref).wait_send()

        @pl.loop(1, count)
        def _(k):
            @pl.when((me - k >= 0) & (me < count - 1))
            def _():
                self.to_right(me - k, k, self.x_ref).wait_send()

            @pl.when((me + k < count) & (me > 0))
            def _():
                self.to_left(me + k, k, self.x_ref).wait_send()

        @pl.loop(0, count * CHUNKS)
        def _(at):
            q, j = at // CHUNKS, lax.rem(at, CHUNKS)

            @pl.when(q < me)
            def _():
                self.back_left(q, j).wait_send()

            @pl.when(q > me)
            def _():
                self.back_right(q, j).wait_send()


GELU_ONE = 0.7978845608028654
GELU_TWO = 0.044715


def gelu_of(values_in):
    inner = GELU_ONE * (values_in + GELU_TWO * values_in * values_in * values_in)
    bend = jnp.tanh(inner)
    half = 0.5 * (1.0 + bend)
    slope = half + 0.5 * values_in * (1.0 - bend * bend) * GELU_ONE * (
        1.0 + 3.0 * GELU_TWO * values_in * values_in
    )
    return values_in * half, slope


def ffn_forward(block, gateup, downs, items, ident):
    count = lax.axis_size("row")
    share, width = block.shape
    groups, _, _, part = gateup.shape
    hidden = groups * part
    down_shape = (groups, hidden, downs[0].shape[2])
    out_cols = down_shape[2] // count
    rows = 2 * share
    bundle = Bundle(items)
    number = bundle.number

    def kernel(x_ref, gw_hbm, dw_one, dw_two, *refs):
        x_refs, refs = refs[:number], refs[number:]
        o_ref, xt_hbm, at_hbm, g_hbm, u_hbm = refs[:5]
        o_refs, scratch = refs[5 : 5 + number], refs[5 + number :]
        flow = Flow(x_ref, *scratch[:6], scratch[6:19])
        gw, dw, xt, at, act, gate, up = scratch[19:26]
        gw_sem, dw_sem, xt_sem, at_sem, g_sem, u_sem = scratch[26:32]
        bundle.bind(x_refs, o_refs, scratch[32:])
        gw_load = pltpu.make_async_copy(gw_hbm, gw, gw_sem)
        dw_loads = [
            pltpu.make_async_copy(source, dw.at[:, pl.ds(k * hidden // 2, hidden // 2)], dw_sem.at[k])
            for k, source in enumerate((dw_one, dw_two))
        ]
        gw_load.start()
        for dw_load in dw_loads:
            dw_load.start()
        bundle.greet(False, True)
        flow.start()
        gw_load.wait()
        for dw_load in dw_loads:
            dw_load.wait()

        def stores(source):
            return (
                pltpu.make_async_copy(gate.at[source], g_hbm.at[source], g_sem.at[source]),
                pltpu.make_async_copy(up.at[source], u_hbm.at[source], u_sem.at[source]),
            )

        def body(source):
            x = flow.blocks[source].reshape(rows, width)

            @pl.loop(0, groups)
            def _(d):
                columns = pl.ds(pl.multiple_of(d * part, part), part)
                g = flat_dot(x, gw[d, 0])
                u = flat_dot(x, gw[d, 1])
                gate[source, :, columns] = g
                up[source, :, columns] = u
                act[source, :, columns] = (gelu_of(g)[0] * u).astype(LOW)

            for copy in stores(source):
                copy.start()
            for d in range(groups):
                out = flat_dot(act[source], dw[d])
                for s in range(count):
                    columns = slice((s * groups + d) * out_cols, (s * groups + d + 1) * out_cols)
                    piece = out[:, s * out_cols : (s + 1) * out_cols]
                    flow.own[source, :, columns] = piece[:share]
                    flow.core_out[source, :, columns] = piece[share:].astype(LOW)

        flow.visit(body, bundle)

        @pl.loop(0, count)
        def _(source):
            here = pl.ds(pl.multiple_of(source * rows, rows), rows)
            xt[:, here] = flow.blocks[source].reshape(rows, width).T
            at[:, here] = act[source].T

        xt_store = pltpu.make_async_copy(xt, xt_hbm, xt_sem)
        at_store = pltpu.make_async_copy(at, at_hbm, at_sem)
        xt_store.start()
        at_store.start()

        @pl.loop(count, 2 * count - 2)
        def _(t):
            flow.give_back(t)

        for k in range(2, count):
            bundle.step(k)
        flow.finish(o_ref)
        bundle.finish()
        xt_store.wait()
        at_store.wait()

        @pl.loop(0, count)
        def _(source):
            for copy in stores(source):
                copy.wait()

    dma = pltpu.SemaphoreType.DMA
    buffers, sems = Flow.scratch(count, share, width)
    vmem, anywhere = pl.BlockSpec(memory_space=pltpu.VMEM), pl.BlockSpec(memory_space=pl.ANY)
    tokens = count * rows
    return pl.pallas_call(
        kernel,
        out_shape=[
            jax.ShapeDtypeStruct((share, width), FULL),
            jax.ShapeDtypeStruct((width, tokens), LOW),
            jax.ShapeDtypeStruct((hidden, tokens), LOW),
            jax.ShapeDtypeStruct((count, rows, hidden), FULL),
            jax.ShapeDtypeStruct((count, rows, hidden), FULL),
        ]
        + bundle.shapes,
        in_specs=[vmem] + [anywhere] * 3 + bundle.specs,
        out_specs=[vmem] + [anywhere] * 4 + bundle.specs,
        scratch_shapes=buffers
        + sems
        + [
            pltpu.VMEM(gateup.shape, LOW),
            pltpu.VMEM(down_shape, LOW),
            pltpu.VMEM((width, tokens), LOW),
            pltpu.VMEM((hidden, tokens), LOW),
            pltpu.VMEM((count, rows, hidden), LOW),
            pltpu.VMEM((count, rows, hidden), FULL),
            pltpu.VMEM((count, rows, hidden), FULL),
        ]
        + [dma, dma((2,)), dma, dma, dma((count,)), dma((count,))]
        + bundle.scratch,
        compiler_params=params(ident, 60),
        cost_estimate=cost(80),
    )(block, gateup, *downs, *bundle.sources)


def ffn_backward(block, gateup, downs, xt, at, gate, up, items, ident):
    count = lax.axis_size("row")
    share, width = block.shape
    groups, _, _, part = gateup.shape
    hidden = groups * part
    down_shape = (groups, hidden, downs[0].shape[2])
    out_cols = down_shape[2] // count
    rows = 2 * share
    tokens = count * rows
    bundle = Bundle(items)
    number = bundle.number

    def kernel(x_ref, gw_hbm, dw_one, dw_two, xt_hbm, at_hbm, g_hbm, u_hbm, *refs):
        x_refs, refs = refs[:number], refs[number:]
        o_ref, dgu_hbm, ddn_hbm = refs[:3]
        o_refs, scratch = refs[3 : 3 + number], refs[3 + number :]
        flow = Flow(x_ref, *scratch[:6], scratch[6:19])
        gw, dw, xt_own, at_own, gate_own, up_own, d_gate, d_up, total, stage, stage_down = scratch[19:30]
        load_sems, g_sem, u_sem, out_sem, down_sem = scratch[30:35]
        bundle.bind(x_refs, o_refs, scratch[35:])
        loads = [
            pltpu.make_async_copy(source, target, load_sems.at[k])
            for k, (source, target) in enumerate(
                [
                    (dw_one, dw.at[:, pl.ds(0, hidden // 2)]),
                    (dw_two, dw.at[:, pl.ds(hidden // 2, hidden // 2)]),
                    (gw_hbm, gw),
                    (xt_hbm, xt_own),
                    (at_hbm, at_own),
                ]
            )
        ]

        def fetches(source):
            return (
                pltpu.make_async_copy(g_hbm.at[source], gate_own.at[source], g_sem.at[source]),
                pltpu.make_async_copy(u_hbm.at[source], up_own.at[source], u_sem.at[source]),
            )

        for load in loads[:3]:
            load.start()

        @pl.loop(0, count)
        def _(source):
            for copy in fetches(source):
                copy.start()

        for load in loads[3:]:
            load.start()
        bundle.greet(False, True)
        flow.start()
        for load in loads[:3]:
            load.wait()

        def columns_of(s, d):
            return pl.ds(pl.multiple_of((s * groups + d) * out_cols, out_cols), out_cols)

        def body(source):
            for copy in fetches(source):
                copy.wait()
            grad = flow.blocks[source].reshape(rows, width)
            d_act = None
            for d in range(groups):
                cut = jnp.concatenate(
                    [
                        grad[:, (s * groups + d) * out_cols : (s * groups + d + 1) * out_cols]
                        for s in range(count)
                    ],
                    axis=1,
                )
                term = against(cut, dw[d])
                d_act = term if d_act is None else d_act + term
            total[:, :hidden] = d_act

            @pl.loop(0, groups)
            def _(d):
                columns = pl.ds(pl.multiple_of(d * part, part), part)
                grad_act = total[:, columns]
                curve, slope = gelu_of(gate_own[source, :, columns])
                d_gate[source, :, columns] = (grad_act * up_own[source, :, columns] * slope).astype(LOW)
                d_up[source, :, columns] = (grad_act * curve).astype(LOW)

            total[...] = jnp.zeros(total.shape, FULL)

            @pl.loop(0, groups)
            def _(d):
                columns = pl.ds(pl.multiple_of(d * part, part), part)
                total[...] += against(d_gate[source, :, columns], gw[d, 0]) + against(
                    d_up[source, :, columns], gw[d, 1]
                )

            flow.own[source] = total[:share]
            flow.core_out[source] = total[share:].astype(LOW)

        def gateup_store(d, which):
            return pltpu.make_async_copy(stage.at[which], dgu_hbm.at[d, which], out_sem.at[which])

        def down_store(d):
            return pltpu.make_async_copy(stage_down, ddn_hbm.at[d], down_sem)

        def weights(d):
            columns = pl.ds(pl.multiple_of(d * part, part), part)
            for which, grads in ((0, d_gate), (1, d_up)):

                @pl.when(d > 0)
                def _():
                    gateup_store(d - 1, which).wait()

                right = grads[:, :, columns].reshape(tokens, part)

                @pl.loop(0, width // 512)
                def _(k):
                    high = pl.ds(pl.multiple_of(k * 512, 512), 512)
                    stage[which, high] = flat_dot(xt_own[high], right).astype(LOW)

                gateup_store(d, which).start()

            @pl.when(d > 0)
            def _():
                down_store(d - 1).wait()

            right = jnp.concatenate(
                [flow.blocks[:, :, :, columns_of(s, d)].reshape(tokens, out_cols) for s in range(count)],
                axis=1,
            )

            @pl.loop(0, hidden // 256)
            def _(k):
                high = pl.ds(pl.multiple_of(k * 256, 256), 256)
                stage_down[high] = flat_dot(at_own[high], right).astype(LOW)

            down_store(d).start()

        def early(k, d):
            @pl.when(k == count - 1)
            def _():
                loads[3].wait()
                loads[4].wait()

            @pl.when(d >= 0)
            def _():
                weights(d)

        flow.visit(body, bundle, early)
        done = count - 1 - flow.reach()

        @pl.loop(0, count - 2)
        def _(t):
            weights(done + t)
            flow.give_back(count + t)

        for k in range(2, count):
            bundle.step(k)

        @pl.loop(count - 2, groups)
        def _(d):
            @pl.when(d + done < groups)
            def _():
                weights(d + done)

        for which in range(2):
            gateup_store(groups - 1, which).wait()
        down_store(groups - 1).wait()
        flow.finish(o_ref)
        bundle.finish()

    dma = pltpu.SemaphoreType.DMA
    buffers, sems = Flow.scratch(count, share, width)
    vmem, anywhere = pl.BlockSpec(memory_space=pltpu.VMEM), pl.BlockSpec(memory_space=pl.ANY)
    return pl.pallas_call(
        kernel,
        out_shape=[
            jax.ShapeDtypeStruct((share, width), FULL),
            jax.ShapeDtypeStruct(gateup.shape, LOW),
            jax.ShapeDtypeStruct(down_shape, LOW),
        ]
        + bundle.shapes,
        in_specs=[vmem] + [anywhere] * 7 + bundle.specs,
        out_specs=[vmem, anywhere, anywhere] + bundle.specs,
        scratch_shapes=buffers
        + sems
        + [
            pltpu.VMEM(gateup.shape, LOW),
            pltpu.VMEM(down_shape, LOW),
            pltpu.VMEM((width, tokens), LOW),
            pltpu.VMEM((hidden, tokens), LOW),
            pltpu.VMEM((count, rows, hidden), FULL),
            pltpu.VMEM((count, rows, hidden), FULL),
            pltpu.VMEM((count, rows, hidden), LOW),
            pltpu.VMEM((count, rows, hidden), LOW),
            pltpu.VMEM((rows, width), FULL),
            pltpu.VMEM((2, width, part), LOW),
            pltpu.VMEM((hidden, count * out_cols), LOW),
        ]
        + [dma((5,)), dma((count,)), dma((count,)), dma((2,)), dma]
        + bundle.scratch,
        compiler_params=params(ident, 62),
        cost_estimate=cost(90),
    )(block, gateup, *downs, xt, at, gate, up, *bundle.sources)


def last_sums(small, ident):
    axes = ("col", "row", "dp")
    sizes = [lax.axis_size(axis) for axis in axes]
    high = small.shape[0]

    def kernel(x_ref, o_ref, *refs):
        slots, sends, recvs = (refs[k::3] for k in range(3))
        spots = [lax.axis_index(axis) for axis in axes]
        barrier = pltpu.get_barrier_semaphore()
        for axis, size, me in zip(axes, sizes, spots):
            for k in range(1, size):
                pl.semaphore_signal(
                    barrier, inc=1, device_id={axis: lax.rem(me + k, size)}, device_id_type=MESH
                )
        pl.semaphore_wait(barrier, sum(sizes) - len(sizes))
        for at, (axis, size, me) in enumerate(zip(axes, sizes, spots)):
            buf, send, recv = slots[at], sends[at], recvs[at]
            buf[me] = x_ref[...] if at == 0 else o_ref[...]
            for k in range(1, size):
                push(buf.at[me], buf.at[me], send.at[k], recv.at[k], {axis: lax.rem(me + k, size)}).start()
            for k in range(1, size):
                origin = lax.rem(me + size - k, size)
                push(buf.at[origin], buf.at[origin], send.at[k], recv.at[k], {axis: origin}).wait()
            total = buf[0]
            top = buf[0, high - 8 :]
            for k in range(1, size):
                total = total + buf[k]
                top = jnp.maximum(top, buf[k, high - 8 :])
            o_ref[...] = total
            o_ref[high - 8 :] = top

    dma = pltpu.SemaphoreType.DMA
    vmem = pl.BlockSpec(memory_space=pltpu.VMEM)
    scratch = []
    for size in sizes:
        scratch += [pltpu.VMEM((size,) + small.shape, FULL), dma((size,)), dma((size,))]
    return pl.pallas_call(
        kernel,
        out_shape=jax.ShapeDtypeStruct(small.shape, FULL),
        in_specs=[vmem],
        out_specs=vmem,
        scratch_shapes=scratch,
        compiler_params=params(ident, 16),
        cost_estimate=cost(14),
    )(small)


def adam_all(small, sum_rows, groups):
    high = small.shape[0]
    number = len(groups)
    arrays = [array for group in groups for array in group[:4]]
    cuts = []
    for group in range(number):
        rows, cols = arrays[4 * group].shape
        pieces = max(1, rows * cols // 262144)
        cuts += [(group, piece, rows // pieces) for piece in range(pieces)]

    def kernel(x_ref, *refs):
        sources, refs = refs[: 4 * number], refs[4 * number :]
        norm_ref, factor_ref = refs[:2]
        outs, refs = refs[2 : 2 + 3 * number], refs[2 + 3 * number :]
        held, load_sem, store_sem = refs[: 4 * number], refs[4 * number], refs[4 * number + 1]

        def rows_of(at):
            group, piece, rows = cuts[at]
            return pl.ds(piece * rows, rows) if rows < arrays[4 * group].shape[0] else slice(None)

        def load(at, k):
            here, array = rows_of(at), 4 * cuts[at][0] + k
            return pltpu.make_async_copy(
                sources[array].at[here], held[array].at[here], load_sem.at[at, k]
            )

        def store(at, k):
            here, group = rows_of(at), cuts[at][0]
            return pltpu.make_async_copy(
                held[4 * group + (1, 2, 0)[k]].at[here], outs[3 * group + k].at[here], store_sem.at[at, k]
            )

        for at in range(len(cuts)):
            for k in range(4):
                load(at, k).start()
        column, data_at = lax.axis_index("col"), lax.axis_index("dp")
        sums = x_ref[:sum_rows]
        squares = jnp.sum(jnp.sum(sums * sums, axis=1, keepdims=True), axis=0, keepdims=True)
        squares = squares + x_ref[sum_rows : sum_rows + 1, :1]
        norm = jnp.sqrt(squares)
        clip = CLIP / jnp.maximum(norm, CLIP)
        tops = x_ref[high - 1 :]
        lanes = lax.broadcasted_iota(jnp.int32, (1, 128), 1)
        group_size = QUERY_HEADS // KEY_VALUE_HEADS
        norm_ref[...] = norm
        factor_ref[...] = (LOGIT_CAP / jnp.maximum(tops, LOGIT_CAP))[:, :QUERY_HEADS]

        def factor(first, count):
            chosen = (lanes >= first) & (lanes < first + count)
            top = jnp.max(jnp.where(chosen, tops, NEGATIVE), axis=1, keepdims=True)
            return jnp.sqrt(LOGIT_CAP / jnp.maximum(top, LOGIT_CAP))

        factors = {
            "query": factor(column * lax.axis_size("dp") + data_at, 1),
            "keyval": jnp.where(
                data_at < KEY_VALUE_HEADS, factor(data_at * group_size, group_size), 1.0
            ),
        }
        for at, (group, piece, rows) in enumerate(cuts):
            rate, decay, kind = groups[group][4:]
            for k in range(4):
                load(at, k).wait()
            w_ref, m_ref, v_ref, g_ref = held[4 * group : 4 * group + 4]
            cols = w_ref.shape[1]
            step = rows if rows % 8 else min(rows, max(16, 32768 // max(cols, 128)))

            def stepped(here):
                new = adamw_step(
                    w_ref[here], m_ref[here], v_ref[here], g_ref[here].astype(FULL) * clip, rate, decay
                )
                m_ref[here], v_ref[here] = new[0], new[1]
                w_ref[here] = new[2] * factors[kind] if kind else new[2]

            if step == rows:
                stepped(rows_of(at))
            else:

                @pl.loop(0, rows // step)
                def _(k):
                    stepped(pl.ds(pl.multiple_of(piece * rows + k * step, step), step))

            for k in range(3):
                store(at, k).start()
        for at in range(len(cuts)):
            for k in range(3):
                store(at, k).wait()

    dma = pltpu.SemaphoreType.DMA
    vmem, anywhere = pl.BlockSpec(memory_space=pltpu.VMEM), pl.BlockSpec(memory_space=pl.ANY)
    outs = [jax.ShapeDtypeStruct(group[0].shape, FULL) for group in groups for _ in range(3)]
    return pl.pallas_call(
        kernel,
        out_shape=[
            jax.ShapeDtypeStruct((1, 1), FULL),
            jax.ShapeDtypeStruct((1, QUERY_HEADS), FULL),
        ]
        + outs,
        in_specs=[vmem] + [anywhere] * (4 * number),
        out_specs=[vmem] * 2 + [anywhere] * (3 * number),
        scratch_shapes=[pltpu.VMEM(array.shape, array.dtype) for array in arrays]
        + [dma((len(cuts), 4)), dma((len(cuts), 3))],
        compiler_params=pltpu.CompilerParams(vmem_limit_bytes=56 * 2**20),
        cost_estimate=cost(25),
    )(small, *arrays)


def allowed_block(at, high, width, spans):
    key_places = lax.broadcasted_iota(jnp.int32, (high, width), 1)
    query_places = at * high + lax.broadcasted_iota(jnp.int32, (high, width), 0)
    seen = key_places <= query_places
    for start in spans[1:]:
        both = (
            (key_places >= start)
            & (key_places < start + IMG)
            & (query_places >= start)
            & (query_places < start + IMG)
        )
        seen = seen | both
    return seen & (key_places < spans[0])


def softmax_block(block_rows, keys, allowed):
    scores = against(block_rows, keys)
    masked = jnp.where(allowed, scores, NEGATIVE)
    peak_row = jnp.max(masked, axis=-1, keepdims=True)
    raw_weights = jnp.where(allowed, jnp.exp(masked - peak_row), 0.0)
    return raw_weights / jnp.sum(raw_weights, axis=-1, keepdims=True), peak_row


def spans_of(lengths_ref, starts_ref):
    at = lax.axis_index("dp")
    return [lengths_ref[at]] + [starts_ref[at, piece] for piece in range(starts_ref.shape[1])]


def attention_forward_head(acts, gains, head_w, key_w, value_w, attend_w, heads, cos_tab, sin_tab, extras, lengths, starts, items, ident):
    tokens, width = acts.shape
    step = 256
    bundle = Bundle(items)
    number = bundle.number
    rows_n, cols_n = lax.axis_size("row"), lax.axis_size("col")
    half_tok, wide = tokens // cols_n, width // rows_n
    share, quarter = half_tok // rows_n, tokens // rows_n
    groups, out_cols = attend_w.shape[0], attend_w.shape[2] // rows_n

    def kernel(l_ref, s_ref, x_ref, gain_ref, qw_ref, kw_ref, vw_ref, aw_ref, heads_ref, cos_ref, sin_ref, e_ref, *refs):
        x_refs, refs = refs[:number], refs[number:]
        hidden_ref, acts_ref, share_ref, scale_ref, qr_ref, kr_ref, vr_ref = refs[:7]
        q_ref, k_ref, v_ref, o_ref, top_ref, es_ref, oc_ref, os_ref, p_ref = refs[7:16]
        o_refs, refs = refs[16 : 16 + number], refs[16 + number :]
        h_ref, sc_ref, key_ref, value_ref = refs[:4]
        bundle.bind(x_refs, o_refs, refs[4:])
        bundle.greet()
        bundle.start()
        me, column = lax.axis_index("row"), lax.axis_index("col")
        spans = spans_of(l_ref, s_ref)
        query_gain, key_gain = heads_ref[pl.ds(column * rows_n + me, 1)], heads_ref[QUERY_HEADS:]

        def project(at):
            here = pl.ds(pl.multiple_of(at * step, step), step)
            rows = x_ref[here].astype(FULL)
            scale = lax.rsqrt(jnp.mean(rows * rows, axis=-1, keepdims=True) + EPS)
            sc_ref[here] = jnp.broadcast_to(scale, (step, 128))
            h_ref[here] = (rows * scale * gain_ref[0:1]).astype(LOW)
            hidden = h_ref[here]
            cos_rows, sin_rows = cos_ref[here], sin_ref[here]
            query = flat_dot(hidden, qw_ref[...])
            qr_ref[here] = query
            q_ref[here] = turn(whole_norm(query, query_gain)[0], cos_rows, sin_rows).astype(LOW)
            key = flat_dot(hidden, kw_ref[...])
            key_ref[here] = key
            k_ref[here] = turn(whole_norm(key, key_gain)[0], cos_rows, sin_rows).astype(LOW)
            value = flat_dot(hidden, vw_ref[...])
            value_ref[here] = value
            v_ref[here] = whole_norm(value, 1.0)[0].astype(LOW)

        def attend(at):
            here = pl.ds(pl.multiple_of(at * step, step), step)
            allowed = allowed_block(at, step, tokens, spans)
            probs, peak_row = softmax_block(q_ref[here], k_ref[...], allowed)
            outputs = flat_dot(probs.astype(LOW), v_ref[...]).astype(LOW)
            o_ref[here] = outputs
            for d in range(groups):
                part = flat_dot(outputs, aw_ref[d])
                for s in range(rows_n):
                    cut = slice((s * groups + d) * out_cols, (s * groups + d + 1) * out_cols)
                    p_ref[here, cut] = part[:, s * out_cols : (s + 1) * out_cols].astype(LOW)
            top_ref[...] = jnp.maximum(top_ref[...], jnp.max(peak_row))

        top_ref[...] = jnp.full(top_ref.shape, NEGATIVE, FULL)
        blocks = tokens // step
        half = max(blocks // 2, 1)
        pl.loop(0, half)(project)
        bundle.step(1)
        pl.loop(half, blocks)(project)
        bundle.step(2)
        pl.loop(0, half)(attend)
        for k in range(3, bundle.sizes[0]):
            bundle.step(k)
        pl.loop(half, blocks)(attend)
        columns = pl.ds(pl.multiple_of(me * wide, wide), wide)

        @pl.loop(0, blocks)
        def _(at):
            here = pl.ds(pl.multiple_of(at * step, step), step)
            hidden_ref[here] = h_ref[here, columns]
            acts_ref[here] = x_ref[here, columns]

        mine = pl.ds(pl.multiple_of(column * half_tok + me * share, share), share)
        share_ref[...] = x_ref[mine]
        es_ref[...] = e_ref[mine]
        scale_ref[...] = sc_ref[pl.ds(pl.multiple_of(column * half_tok, half_tok), half_tok)]
        fourth = pl.ds(pl.multiple_of(me * quarter, quarter), quarter)
        kr_ref[...] = key_ref[fourth]
        vr_ref[...] = value_ref[fourth]
        oc_ref[...] = cos_ref[fourth]
        os_ref[...] = sin_ref[fourth]
        bundle.finish()

    vmem = pl.BlockSpec(memory_space=pltpu.VMEM)
    smem = pl.BlockSpec(memory_space=pltpu.SMEM)

    def low(*shape):
        return jax.ShapeDtypeStruct(shape, LOW)

    def full(*shape):
        return jax.ShapeDtypeStruct(shape, FULL)

    return pl.pallas_call(
        kernel,
        out_shape=[
            low(tokens, wide),
            low(tokens, wide),
            low(share, width),
            full(half_tok, 128),
            full(tokens, HEAD_WIDTH),
            full(quarter, HEAD_WIDTH),
            full(quarter, HEAD_WIDTH),
            low(tokens, HEAD_WIDTH),
            low(tokens, HEAD_WIDTH),
            low(tokens, HEAD_WIDTH),
            low(tokens, HEAD_WIDTH),
            full(8, 128),
            low(share, PLD),
            full(quarter, HEAD_WIDTH // 2),
            full(quarter, HEAD_WIDTH // 2),
            low(tokens, width),
        ]
        + bundle.shapes,
        in_specs=[smem, smem] + [vmem] * 10 + bundle.specs,
        out_specs=[vmem] * 16 + bundle.specs,
        scratch_shapes=[
            pltpu.VMEM((tokens, width), LOW),
            pltpu.VMEM((tokens, 128), FULL),
            pltpu.VMEM((tokens, HEAD_WIDTH), FULL),
            pltpu.VMEM((tokens, HEAD_WIDTH), FULL),
        ]
        + bundle.scratch,
        compiler_params=params(ident, 60),
        cost_estimate=cost(40),
    )(
        lengths, starts, acts, gains, head_w, key_w, value_w, attend_w, heads, cos_tab, sin_tab, extras, *bundle.sources
    )


def head_backward(queries, keys, values, attended, grads, attend_w, query_raw, heads, cos_tab, sin_tab, lengths, starts, items, ident):
    rows = queries.shape[0]
    step = min(256, rows)
    bundle = Bundle(items)
    number = bundle.number
    devices = lax.axis_size("row")
    quarter = rows // devices
    groups, out_cols = attend_w.shape[0], attend_w.shape[2] // devices

    def kernel(l_ref, s_ref, q_ref, k_ref, v_ref, a_ref, g_ref, w_ref, r_ref, heads_ref, cos_ref, sin_ref, *refs):
        x_refs, refs = refs[:number], refs[number:]
        dq_ref, kv_ref, dg_ref, dw_ref = refs[:4]
        o_refs, refs = refs[4 : 4 + number], refs[4 + number :]
        dk_ref, dv_ref = refs[:2]
        bundle.bind(x_refs, o_refs, refs[2:])
        bundle.greet()
        bundle.start()
        spans = spans_of(l_ref, s_ref)
        gain = heads_ref[pl.ds(lax.axis_index("col") * devices + lax.axis_index("row"), 1)]
        dk_ref[...] = jnp.zeros(dk_ref.shape, FULL)
        dv_ref[...] = jnp.zeros(dv_ref.shape, FULL)
        dg_ref[...] = jnp.zeros(dg_ref.shape, FULL)

        @pl.loop(0, rows // step)
        def _(at):
            here = pl.ds(pl.multiple_of(at * step, step), step)
            allowed = allowed_block(at, step, keys.shape[0], spans)
            block_rows, grad_rows = q_ref[here], None
            for d in range(groups):
                cut = jnp.concatenate(
                    [
                        g_ref[here, (s * groups + d) * out_cols : (s * groups + d + 1) * out_cols]
                        for s in range(devices)
                    ],
                    axis=1,
                )
                term = against(cut, w_ref[d])
                grad_rows = term if grad_rows is None else grad_rows + term
            grad_rows = grad_rows.astype(LOW)
            probs, _ = softmax_block(block_rows, k_ref[...], allowed)
            grad_probs = against(grad_rows, v_ref[...])
            delta_row = jnp.sum(probs * grad_probs, axis=-1, keepdims=True)
            grad_scores = (probs * (grad_probs - delta_row)).astype(LOW)
            d_query = turn_back(flat_dot(grad_scores, k_ref[...]), cos_ref[here], sin_ref[here])
            d_query, d_gain = norm_back(r_ref[here], gain, d_query)
            dq_ref[here] = d_query.astype(LOW)
            dg_ref[...] += d_gain
            dk_ref[...] += inner_rows(grad_scores, block_rows)
            dv_ref[...] += inner_rows(probs.astype(LOW), grad_rows)

        for device in range(devices):
            cut = slice(device * quarter, (device + 1) * quarter)
            kv_ref[device, :quarter] = dk_ref[cut].astype(LOW)
            kv_ref[device, quarter:] = dv_ref[cut].astype(LOW)
        for cut in range(0, grads.shape[1], 512):
            dw_ref[:, cut : cut + 512] = inner_rows(a_ref[...], g_ref[:, cut : cut + 512]).astype(LOW)
        for k in range(1, bundle.sizes[0]):
            bundle.step(k)
        bundle.finish()

    vmem = pl.BlockSpec(memory_space=pltpu.VMEM)
    return pl.pallas_call(
        kernel,
        out_shape=[
            jax.ShapeDtypeStruct(queries.shape, LOW),
            jax.ShapeDtypeStruct((devices, 2 * quarter, HEAD_WIDTH), LOW),
            jax.ShapeDtypeStruct((1, HEAD_WIDTH), FULL),
            jax.ShapeDtypeStruct((HEAD_WIDTH, grads.shape[1]), LOW),
        ]
        + bundle.shapes,
        in_specs=[pl.BlockSpec(memory_space=pltpu.SMEM)] * 2 + [vmem] * 10 + bundle.specs,
        out_specs=[vmem] * 4 + bundle.specs,
        scratch_shapes=[pltpu.VMEM(keys.shape, FULL)] * 2 + bundle.scratch,
        compiler_params=params(ident, 60),
        cost_estimate=cost(25),
    )(
        lengths, starts, queries, keys, values, attended, grads, attend_w, query_raw, heads, cos_tab, sin_tab, *bundle.sources
    )


def whole_norm(values_in, gain_vec):
    scale = lax.rsqrt(jnp.mean(values_in * values_in, axis=-1, keepdims=True) + EPS)
    return values_in * scale * gain_vec, scale


def whole_norm_backward(values_in, scale, gain_vec, grad_out):
    weighted = grad_out * gain_vec
    inner = jnp.mean(weighted * values_in, axis=-1, keepdims=True)
    return (
        scale * weighted - values_in * (scale * scale * scale) * inner,
        jnp.sum(grad_out * values_in * scale, axis=0),
    )


def turn(values_in, cos_tab, sin_tab):
    half_width = values_in.shape[-1] // 2
    one, two = values_in[:, :half_width], values_in[:, half_width:]
    return jnp.concatenate(
        [one * cos_tab - two * sin_tab, two * cos_tab + one * sin_tab], axis=1
    )


def turn_back(values_in, cos_tab, sin_tab):
    return turn(values_in, cos_tab, -sin_tab)


def line_device(
    activations,
    per_layer,
    cotangent,
    lengths,
    starts,
    w_query,
    m_query,
    v_query,
    key_value_weight,
    key_value_first_moment,
    key_value_second_moment,
    w_attend,
    m_attend,
    v_attend,
    w_gateup,
    m_gateup,
    v_gateup,
    w_down,
    m_down,
    v_down,
    w_left,
    m_left,
    v_left,
    w_right,
    m_right,
    v_right,
    w_pergate,
    m_pergate,
    v_pergate,
    w_perproj,
    m_perproj,
    v_perproj,
    w_gains,
    m_gains,
    v_gains,
    w_heads,
    m_heads,
    v_heads,
):
    rows_n = lax.axis_size("row")
    cols_n = lax.axis_size("col")
    data_n = lax.axis_size("dp")
    me = lax.axis_index("row")
    column = lax.axis_index("col")
    data_at = lax.axis_index("dp")
    half_tok, width_a = activations.shape
    tokens = half_tok * cols_n
    share = half_tok // rows_n
    quarter = tokens // rows_n
    width = width_a * rows_n

    ff_part = w_gateup.shape[2] // rows_n
    out_cols = w_down.shape[1]
    heads_here = data_n
    left_cols, right_rows = w_left.shape[1], w_right.shape[0]
    gate_cols, proj_rows = w_pergate.shape[1], w_perproj.shape[0]

    def columns_of(at, size):
        return pl.ds(pl.multiple_of(at * size, size), size)

    def across(source, by_rows):
        high, wide = source.shape
        if by_rows:
            return Swap(
                source,
                (data_n * high, wide),
                lambda ref, q: ref,
                lambda ref, at: ref.at[columns_of(at, high)],
                "dp",
            )
        return Swap(
            source,
            (high, data_n * wide),
            lambda ref, q: ref,
            lambda ref, at: ref.at[:, columns_of(at, wide)],
            "dp",
        )

    def along(source):
        high, wide = source.shape
        return Line(
            source,
            (cols_n * high, rows_n * wide),
            lambda ref, c, r: ref.at[columns_of(c, high), columns_of(r, wide)],
            True,
        )

    def lower(inputs, outputs):
        @pl.loop(0, inputs[0].shape[0] // 256)
        def _(at):
            rows = pl.ds(pl.multiple_of(at * 256, 256), 256)
            outputs[0][rows] = inputs[0][rows].astype(LOW)

    down_low, gateup_own, attend_own, qkv_w, left_t, right_w, pergate_t, perproj_w = transfers(
        [
            Swap(
                w_gateup.astype(LOW),
                (2, width, ff_part),
                lambda ref, q: ref.at[:, :, columns_of(q, ff_part)],
                lambda ref, at: ref.at[:, columns_of(at, width_a), :],
            ),
            Swap(
                w_attend.astype(LOW).reshape(rows_n, HEAD_WIDTH, out_cols),
                (HEAD_WIDTH, rows_n * out_cols),
                lambda ref, q: ref.at[q],
                lambda ref, at: ref.at[:, columns_of(at, out_cols)],
            ),
            Swap(
                jnp.concatenate([w_query, key_value_weight], axis=1).astype(LOW),
                (data_n, width_a, 2 * HEAD_WIDTH),
                lambda ref, q: ref,
                lambda ref, at: ref.at[at],
                "dp",
            ),
            across(w_left.T, True),
            across(w_right.astype(LOW), False),
            across(w_pergate.T.astype(LOW), True),
            across(w_perproj.astype(LOW), False),
        ],
        1,
        60,
        16,
        lower,
        (w_down,),
        [jax.ShapeDtypeStruct(w_down.shape, LOW)],
    )
    down_low = down_low.reshape(data_n, rows_n, ff_part, out_cols)

    def down_half(k):
        return Swap(
            down_low[k * data_n // 2 : (k + 1) * data_n // 2],
            (data_n // 2, ff_part, rows_n * out_cols),
            lambda ref, q: ref.at[:, q],
            lambda ref, at: ref.at[:, :, columns_of(at, out_cols)],
        )

    gateup_all = lax.all_gather(gateup_own, "dp")
    last = pl.ds(HEAD_WIDTH, HEAD_WIDTH)
    whole_acts, whole_key, whole_value, head_w, gains, extras, attend_all, down_one = transfers(
        [
            along(activations),
            Line(
                qkv_w,
                (width, HEAD_WIDTH),
                lambda ref, c, r: ref.at[columns_of(r, width_a)],
                False,
                lambda ref, c: ref.at[c, :, last],
            ),
            Line(
                qkv_w,
                (width, HEAD_WIDTH),
                lambda ref, c, r: ref.at[columns_of(r, width_a)],
                False,
                lambda ref, c: ref.at[KEY_VALUE_HEADS + c, :, last],
            ),
            Swap(
                qkv_w,
                (width, HEAD_WIDTH),
                lambda ref, q: ref.at[q, :, pl.ds(0, HEAD_WIDTH)],
                lambda ref, at: ref.at[columns_of(at, width_a)],
            ),
            Line(w_gains, (6, width), lambda ref, c, r: ref.at[:, columns_of(r, width_a)]),
            Line(
                per_layer,
                (tokens, PLD),
                lambda ref, c, r: ref.at[columns_of(r, quarter), columns_of(c, PLD // cols_n)],
                True,
            ),
            Swap(
                attend_own,
                (data_n, HEAD_WIDTH, rows_n * out_cols),
                lambda ref, q: ref,
                lambda ref, at: ref.at[at],
                "dp",
            ),
            down_half(0),
        ],
        2,
        105,
        60,
    )
    down_one, gateup_all = lax.optimization_barrier((down_one, gateup_all))
    down_one = lax.all_gather(down_one, "dp").reshape(data_n, data_n * ff_part // 2, -1)
    all_cos, all_sin = rope_tables(jnp.arange(tokens, dtype=jnp.int32), HEAD_WIDTH)
    (
        spread_h,
        own_acts,
        acts_share,
        scale_here,
        query_raw,
        key_raw,
        value_raw,
        queries,
        keys,
        values,
        attended,
        top,
        extras,
        own_cos,
        own_sin,
        projected,
        left_t,
        right_w,
        down_two,
    ) = attention_forward_head(
        whole_acts,
        gains,
        head_w,
        whole_key,
        whole_value,
        attend_all,
        w_heads,
        all_cos,
        all_sin,
        extras,
        lengths,
        starts,
        [
            along(left_t.astype(LOW)),
            along(right_w),
            down_half(1),
        ],
        3,
    )
    down_two, down_one = lax.optimization_barrier((down_two, down_one))
    down_two = lax.all_gather(down_two, "dp").reshape(data_n, data_n * ff_part // 2, -1)
    down_all = (down_one, down_two)
    projected, pergate_t, perproj_w = transfers(
        [
            Reduce(
                projected.reshape(cols_n, rows_n, share, width),
                (share, width),
                lambda ref, q: ref.at[q],
            ),
            along(pergate_t),
            along(perproj_w),
        ],
        5,
        45,
        60,
    )
    wide_low, wide_full = ((share, width), LOW), ((share, width), FULL)
    line = ((1, width), FULL)
    hidden_low, middle, right_raw, mixture, ffn_in = local(
        mix,
        [wide_low, ((share, RANK), LOW), wide_full, wide_full, wide_low],
        acts_share,
        projected,
        gains,
        left_t,
        right_w,
    )
    down_raw, spread_ft, act_t, gate_raw, up_raw, upstream = ffn_forward(
        ffn_in,
        gateup_all,
        down_all,
        [
            Swap(
                cotangent,
                (share, width),
                lambda ref, q: ref.at[columns_of(q, share)],
                lambda ref, at: ref.at[:, columns_of(at, width_a)],
            )
        ],
        6,
    )
    result, d_out, d_down, dw_perproj, dw_pergate, gain_four, gain_five = local(
        per_layer_both,
        [wide_low, wide_full, wide_low, ((PLD, width), LOW), ((PLD, width), LOW), line, line],
        mixture,
        down_raw,
        gains,
        extras,
        pergate_t,
        perproj_w,
        upstream,
    )
    d_ffn, dw_gateup, dw_down = ffn_backward(
        d_down, gateup_all, down_all, spread_ft, act_t, gate_raw, up_raw, [], 8
    )
    g_gateup = lax.psum_scatter(dw_gateup, "dp", scatter_dimension=0)
    d_proj, d_half, d_middle, small_parts, inner_share, gain_one, gain_two, gain_three = local(
        mix_back,
        [
            wide_low,
            wide_low,
            ((share, RANK), LOW),
            ((2 * (RANK + PLD), width), LOW),
            ((8, share), FULL),
            line,
            line,
            line,
        ],
        d_out,
        d_ffn,
        mixture,
        projected,
        right_raw,
        gains,
        acts_share,
        left_t,
        right_w,
        hidden_low,
        middle,
        dw_pergate,
        dw_perproj,
    )
    small_parts = small_parts.reshape(cols_n, -1, width)
    spread_p, small_parts = transfers(
        [
            Line(
                d_proj.astype(LOW),
                (cols_n, rows_n, share, width),
                lambda ref, c, r: ref.at[c, r],
                True,
            ),
            Reduce(
                small_parts,
                (small_parts.shape[1], width_a),
                lambda ref, q: ref.at[:, columns_of(q, width_a)],
            ),
        ],
        10,
        50,
        60,
    )
    spread_p = spread_p.reshape(tokens, width)
    d_q_raw, kv_parts, dg_query, dw_attend, middle_here, half_here, result = head_backward(
        queries,
        keys,
        values,
        attended,
        spread_p,
        attend_all,
        query_raw,
        w_heads,
        all_cos,
        all_sin,
        lengths,
        starts,
        [
            Line(
                d_middle, (half_tok, d_middle.shape[1]), lambda ref, c, r: ref.at[columns_of(r, share)]
            )
        ]
        + [
            Swap(
                source,
                (half_tok, width_a),
                lambda ref, q: ref.at[:, columns_of(q, width_a)],
                lambda ref, at: ref.at[columns_of(at, share)],
            )
            for source in (d_half, result)
        ],
        4,
    )

    d_q_raw, dw_down, g_gateup = lax.optimization_barrier((d_q_raw, dw_down, g_gateup))
    g_down = lax.psum_scatter(
        dw_down.reshape(data_n, data_n, ff_part, -1), "dp", scatter_dimension=0
    )

    d_q_all, d_kv = transfers(
        [
            Line(d_q_raw, (rows_n,) + d_q_raw.shape, lambda ref, c, r: ref.at[r]),
            Reduce(kv_parts, kv_parts.shape[1:], lambda ref, q: ref.at[q], False),
        ],
        11,
        45,
        60,
    )
    d_k_raw, d_v_raw, dg_key = local(
        key_value_back,
        [((quarter, HEAD_WIDTH), LOW), ((quarter, HEAD_WIDTH), LOW), ((1, HEAD_WIDTH), FULL)],
        d_kv,
        key_raw,
        value_raw,
        w_heads,
        own_cos,
        own_sin,
        mebibytes=16,
    )

    def query_work(inputs, outputs):
        h_ref, dq_ref, qw_ref, g_ref = inputs
        dw_ref, dh_ref, sq_ref = outputs
        hidden = h_ref[...]
        for k in range(heads_here):
            dw_ref[k] = inner_rows(hidden, dq_ref[k]).astype(LOW)
        total = against(dq_ref[0], qw_ref[0, :, :HEAD_WIDTH])
        for k in range(1, heads_here):
            total = total + against(dq_ref[k], qw_ref[k, :, :HEAD_WIDTH])
        dh_ref[...] = total
        sq_ref[...] = jnp.zeros(sq_ref.shape, FULL)
        for which in range(2):

            @pl.loop(0, width // 128)
            def _(at):
                rows = g_ref[which, pl.ds(pl.multiple_of(at * 128, 128), 128)].astype(FULL)
                sq_ref[...] += jnp.sum((rows * rows).reshape(16, 8, ff_part), axis=0)

    dw_query, d_hidden, gateup_squares, d_k_all, d_v_all, g_gateup, g_attend = transfers(
        [
            Line(
                d_raw, (tokens, HEAD_WIDTH), lambda ref, c, r: ref.at[columns_of(r, quarter)]
            )
            for d_raw in (d_k_raw, d_v_raw)
        ]
        + [
            Swap(
                g_gateup,
                w_gateup.shape,
                lambda ref, q: ref.at[:, columns_of(q, width_a), :],
                lambda ref, at: ref.at[:, :, columns_of(at, ff_part)],
            ),
            ShardSum(dw_attend, out_cols),
        ],
        12,
        65,
        40,
        query_work,
        (spread_h, d_q_all, qkv_w, g_gateup),
        [
            jax.ShapeDtypeStruct((heads_here, width_a, HEAD_WIDTH), LOW),
            jax.ShapeDtypeStruct((tokens, width_a), FULL),
            jax.ShapeDtypeStruct((8, ff_part), FULL),
        ],
    )
    extents = (
        (data_n * left_cols, True),
        (right_rows, False),
        (data_n * gate_cols, True),
        (proj_rows, False),
    )
    flat_rows = sum(rows for rows, _ in extents)
    dw_kv, d_hidden, inner, flat_parts = local(
        functools.partial(key_value_ends, extents=extents),
        [
            ((2 * width_a, HEAD_WIDTH), LOW),
            ((tokens, width_a), LOW),
            ((8, tokens), FULL),
            ((data_n * flat_rows, out_cols), LOW),
        ],
        spread_h,
        d_k_all,
        d_v_all,
        qkv_w,
        d_hidden,
        own_acts,
        w_gains,
        small_parts,
        mebibytes=24,
    )
    dw_kv = dw_kv.reshape(2, width_a, HEAD_WIDTH)
    down_sums = g_down
    g_query, g_keyval, flat_grads, inner, inner_share, d_hidden, g_attend, g_down = shard_total(
        dw_query,
        dw_kv,
        flat_parts.reshape(data_n, flat_rows, out_cols),
        [
            Line(inner, (cols_n, rows_n) + inner.shape, lambda ref, c, r: ref.at[c, r], True),
            Line(
                inner_share,
                (cols_n, rows_n) + inner_share.shape,
                lambda ref, c, r: ref.at[c, r],
                True,
            ),
            Pair(d_hidden.reshape(cols_n, half_tok, width_a)),
            Swap(
                g_attend,
                (rows_n, HEAD_WIDTH, out_cols),
                lambda ref, q: ref.at[:, columns_of(q, out_cols)],
                lambda ref, at: ref.at[at],
            ),
            Swap(
                g_down,
                (data_n, rows_n, ff_part, out_cols),
                lambda ref, q: ref.at[:, :, columns_of(q, out_cols)],
                lambda ref, at: ref.at[:, at],
            ),
        ],
        13,
    )
    g_down = g_down.reshape(w_down.shape)
    g_attend = g_attend.reshape(w_attend.shape)
    small_grads = []
    start = 0
    for w, by_rows in ((w_left, True), (w_right, False), (w_pergate, True), (w_perproj, False)):
        rows = w.size // out_cols
        cut = flat_grads[start : start + rows]
        start += rows
        if by_rows:
            high = rows // data_n
            cut = [cut[k * high : (k + 1) * high] for k in range(data_n)]
            cut = jnp.concatenate(cut, axis=1).T
        small_grads.append(cut)
    g_left, g_right, g_pergate, g_perproj = small_grads

    grad_input, small = input_ends(
        d_hidden,
        half_here,
        middle_here,
        left_t,
        activations,
        scale_here,
        w_gains,
        inner,
        inner_share,
        (g_query, g_keyval, flat_grads, g_attend, down_sums),
        gateup_squares,
        (gain_one, gain_two, gain_three, gain_four, gain_five),
        dg_query,
        dg_key,
        top,
    )
    gain_rows = 6 * width // 128
    head_rows = (QUERY_HEADS + 1) * HEAD_WIDTH // 128
    small = last_sums(small, 15)
    gain_sum = small[:gain_rows].reshape(6, width)
    head_sum = small[gain_rows : gain_rows + head_rows].reshape(QUERY_HEADS + 1, HEAD_WIDTH)
    g_gains = lax.dynamic_slice_in_dim(gain_sum, me * width_a, width_a, 1)
    matrix_rate = MODEL_WIDTH ** (-0.5)

    def flat_rows_of(array):
        return array.reshape(-1, array.shape[-1])

    def kept(array):
        return array

    def turned(array):
        return array.T

    groups = [
        tuple(change(array) for array in arrays) + rest
        for arrays, change, rest in (
            ((w_gateup, m_gateup, v_gateup, g_gateup), flat_rows_of, (matrix_rate, DECAY, None)),
            ((w_down, m_down, v_down, g_down), kept, (FF ** (-0.5), DECAY, None)),
            ((w_query, m_query, v_query, g_query), kept, (matrix_rate, DECAY, "query")),
            (
                (key_value_weight, key_value_first_moment, key_value_second_moment, g_keyval),
                kept,
                (matrix_rate, DECAY, "keyval"),
            ),
            (
                (w_attend, m_attend, v_attend, g_attend),
                kept,
                ((QUERY_HEADS * HEAD_WIDTH) ** (-0.5), DECAY, None),
            ),
            ((w_left, m_left, v_left, g_left), turned, (matrix_rate, DECAY, None)),
            ((w_right, m_right, v_right, g_right), kept, (RANK ** (-0.5), DECAY, None)),
            ((w_pergate, m_pergate, v_pergate, g_pergate), turned, (matrix_rate, DECAY, None)),
            ((w_perproj, m_perproj, v_perproj, g_perproj), kept, (PLD ** (-0.5), DECAY, None)),
            ((w_gains, m_gains, v_gains, g_gains), kept, (GAIN_RATE, 0.0, None)),
            ((w_heads, m_heads, v_heads, head_sum), kept, (HEAD_RATE, 0.0, None)),
        )
    ]
    grad_norm, scale_factors, *stepped = adam_all(small, gain_rows + head_rows, groups)
    grad_norm = grad_norm.reshape(())
    scale_factors = scale_factors.reshape(-1)
    gateup, down, query, keyval, attend, left, right, pergate, perproj, gain, head = (
        stepped[3 * k : 3 * k + 3] for k in range(11)
    )
    gateup = [array.reshape(w_gateup.shape) for array in gateup]
    left = [array.T for array in left]
    pergate = [array.T for array in pergate]
    return (
        result,
        grad_input,
        grad_norm,
        scale_factors,
        *query,
        *keyval,
        *attend,
        *gateup,
        *down,
        *left,
        *right,
        *pergate,
        *perproj,
        *gain,
        *head,
    )


def per_device(
    activations,
    per_layer,
    cotangent,
    lengths,
    starts,
    w_query,
    m_query,
    v_query,
    key_value_weight,
    key_value_first_moment,
    key_value_second_moment,
    w_attend,
    m_attend,
    v_attend,
    w_gateup,
    m_gateup,
    v_gateup,
    w_down,
    m_down,
    v_down,
    w_left,
    m_left,
    v_left,
    w_right,
    m_right,
    v_right,
    w_pergate,
    m_pergate,
    v_pergate,
    w_perproj,
    m_perproj,
    v_perproj,
    w_gains,
    m_gains,
    v_gains,
    w_heads,
    m_heads,
    v_heads,
):
    row_devs = lax.axis_size("row")
    col_devs = lax.axis_size("col")
    data_devs = lax.axis_size("dp")
    row_place = lax.axis_index("row")
    column_place = lax.axis_index("col")
    data_at = lax.axis_index("dp")
    bf16 = jnp.bfloat16
    single_float = jnp.float32
    query_b, keyval_b, attend_b, gateup_b, down_b, left_b, right_b, pergate_b, perproj_b = (
        lax.all_gather(w_query.astype(bf16), "dp", axis=1, tiled=True),
        lax.all_gather(key_value_weight.astype(bf16), "dp", axis=1, tiled=True),
        lax.all_gather(w_attend.astype(bf16), "dp", axis=1, tiled=True),
        lax.all_gather(w_gateup.astype(bf16), "dp", axis=2, tiled=True),
        lax.all_gather(w_down.astype(bf16), "dp", axis=1, tiled=True),
        lax.all_gather(w_left.astype(bf16), "dp", axis=1, tiled=True),
        lax.all_gather(w_right.astype(bf16), "dp", axis=1, tiled=True),
        lax.all_gather(w_pergate.astype(bf16), "dp", axis=1, tiled=True),
        lax.all_gather(w_perproj.astype(bf16), "dp", axis=1, tiled=True),
    )
    inputs = activations.astype(single_float)
    tok_a, width_a = inputs.shape
    grouped_rows = tok_a * col_devs
    token_batch = grouped_rows // row_devs
    q_cols = query_b.shape[1]
    l_cols = left_b.shape[1]
    kv_cols = keyval_b.shape[1]
    ff_here = gateup_b.shape[2]
    local_heads = q_cols // HEAD_WIDTH
    length = lax.dynamic_index_in_dim(lengths, data_at, 0, keepdims=False)
    piece_starts = lax.dynamic_index_in_dim(starts, data_at, 0, keepdims=False)
    own_places = row_place * token_batch + jnp.arange(token_batch, dtype=jnp.int32)
    all_places = jnp.arange(grouped_rows, dtype=jnp.int32)
    own_cos, own_sin = rope_tables(own_places, HEAD_WIDTH)
    query_gains = lax.dynamic_slice_in_dim(w_heads, column_place * local_heads, local_heads, 0)
    key_gain = w_heads[QUERY_HEADS]
    hidden, scale_in = norm_forward(inputs, w_gains[0])
    hidden_b = hidden.astype(bf16)
    spread_h = spread_col(hidden_b)
    type_one = reduce_row(flat_dot(spread_h, jnp.concatenate([query_b, left_b], axis=1)))
    key_raw_all = lax.psum(flat_dot(spread_h, keyval_b), "row")
    all_cos, all_sin = rope_tables(all_places, HEAD_WIDTH)
    key_value_whole = key_form(key_raw_all, key_gain, all_cos, all_sin).astype(bf16)
    key_raw = lax.dynamic_slice_in_dim(key_raw_all, row_place * token_batch, token_batch, 0)
    query_raw = type_one[:, :q_cols]
    middle_b = type_one[:, q_cols : q_cols + l_cols].astype(bf16)
    queries = query_form(query_raw, query_gains, own_cos, own_sin).astype(bf16)
    key_value_heads = (column_place * local_heads + jnp.arange(local_heads, dtype=jnp.int32)) // (
        QUERY_HEADS // KEY_VALUE_HEADS
    )
    every_key = key_value_whole[:, : KEY_VALUE_HEADS * HEAD_WIDTH].reshape(
        grouped_rows, KEY_VALUE_HEADS, HEAD_WIDTH
    )
    every_value = key_value_whole[:, KEY_VALUE_HEADS * HEAD_WIDTH :].reshape(
        grouped_rows, KEY_VALUE_HEADS, HEAD_WIDTH
    )
    key_sel = jnp.take(every_key, key_value_heads, axis=1)
    value_sel = jnp.take(every_value, key_value_heads, axis=1)
    attended, block_peaks, block_totals = attention_forward(
        queries, key_sel, value_sel, own_places, all_places, length, piece_starts
    )
    attended_b = attended.reshape(token_batch, q_cols).astype(bf16)
    joined_b = jnp.concatenate([attended_b, middle_b], axis=1)
    spread_j = spread_row(joined_b)
    type_two = reduce_col(
        jnp.concatenate(
            [flat_dot(spread_j[:, :q_cols], attend_b), flat_dot(spread_j[:, q_cols:], right_b)],
            axis=1,
        )
    )
    projected = type_two[:, :width_a]
    right_raw = type_two[:, width_a:]
    right_n, scale_r = norm_forward(right_raw, w_gains[1])
    laurel = hidden + right_n
    proj_n, scale_p = norm_forward(projected, w_gains[2])
    gated_sum = inputs + proj_n
    mixture = (gated_sum + laurel) * HALF_ROOT
    ffn_n, scale_f = norm_forward(mixture, w_gains[3])
    ffn_b = ffn_n.astype(bf16)
    spread_f = spread_col(ffn_b)
    gateup_pair = jnp.concatenate([gateup_b[0], gateup_b[1]], axis=1)
    gate_up = reduce_row(flat_dot(spread_f, gateup_pair))
    gate_raw = gate_up[:, :ff_here]
    up_raw = gate_up[:, ff_here:]
    act_b = (jax.nn.gelu(gate_raw, approximate=True) * up_raw).astype(bf16)
    spread_a = spread_row(act_b)
    down_raw = reduce_col(flat_dot(spread_a, down_b))
    down_n, scale_d = norm_forward(down_raw, w_gains[4])
    block_out = mixture + down_n
    out_b = block_out.astype(bf16)
    spread_o = spread_col(out_b)
    pgate = reduce_row(flat_dot(spread_o, pergate_b))
    extras = per_layer.astype(single_float)
    pact_b = (jax.nn.gelu(pgate, approximate=True) * extras).astype(bf16)
    spread_p = spread_row(pact_b)
    perproj = reduce_col(flat_dot(spread_p, perproj_b))
    perproj_n, scale_pp = norm_forward(perproj, w_gains[5])
    result = (block_out + perproj_n).astype(bf16)
    upstream = cotangent.astype(single_float)
    gain_grads = [None, None, None, None, None, None]
    d_perproj, gain_grads[5] = norm_backward(perproj, scale_pp, w_gains[5], upstream)
    grads_five = grads_col(d_perproj.astype(bf16))
    dw_perproj = inner_rows(spread_p, grads_five)
    d_pact = reduce_row(against(grads_five, perproj_b))
    gelu_out, pullback = jax.vjp(lambda v: jax.nn.gelu(v, approximate=True), pgate)
    (d_pgate,) = pullback(d_pact * extras)
    grads_four = grads_row(d_pgate.astype(bf16))
    dw_pergate = inner_rows(spread_o, grads_four)
    d_out = upstream + reduce_col(against(grads_four, pergate_b))
    d_down, gain_grads[4] = norm_backward(down_raw, scale_d, w_gains[4], d_out)
    grads_three = grads_col(d_down.astype(bf16))
    dw_down = inner_rows(spread_a, grads_three)
    d_act = reduce_row(against(grads_three, down_b))
    act_out, pullback = jax.vjp(lambda a, b: jax.nn.gelu(a, approximate=True) * b, gate_raw, up_raw)
    d_gate, d_up = pullback(d_act)
    local_two = jnp.concatenate([d_gate, d_up], axis=1).astype(bf16)
    grads_two = grads_row(local_two)
    dw_gateup = jnp.stack(
        [inner_rows(spread_f, grads_two[:, :ff_here]), inner_rows(spread_f, grads_two[:, ff_here:])]
    )
    d_ffn = reduce_col(
        against(grads_two[:, :ff_here], gateup_b[0]) + against(grads_two[:, ff_here:], gateup_b[1])
    )
    d_mix_norm, gain_grads[3] = norm_backward(mixture, scale_f, w_gains[3], d_ffn)
    d_half = (d_out + d_mix_norm) * HALF_ROOT
    d_proj, gain_grads[2] = norm_backward(projected, scale_p, w_gains[2], d_half)
    d_right, gain_grads[1] = norm_backward(right_raw, scale_r, w_gains[1], d_half)
    grads_one = grads_col(jnp.concatenate([d_proj, d_right], axis=1).astype(bf16))
    dw_attend = inner_rows(spread_j[:, :q_cols], grads_one[:, :width_a])
    dw_right = inner_rows(spread_j[:, q_cols:], grads_one[:, width_a:])
    d_joined = reduce_row(
        jnp.concatenate(
            [against(grads_one[:, :width_a], attend_b), against(grads_one[:, width_a:], right_b)],
            axis=1,
        )
    )
    d_attended = d_joined[:, :q_cols].astype(bf16).reshape(token_batch, local_heads, HEAD_WIDTH)
    d_middle = d_joined[:, q_cols:]
    d_queries, d_key_sel, d_value_sel = attention_backward(
        queries,
        key_sel,
        value_sel,
        d_attended,
        block_peaks,
        block_totals,
        own_places,
        all_places,
        length,
        piece_starts,
    )
    single_hot_mask = (
        key_value_heads[:, None] == jnp.arange(KEY_VALUE_HEADS, dtype=jnp.int32)[None, :]
    ).astype(single_float)
    key_gradient = jnp.sum(d_key_sel[:, :, None, :] * single_hot_mask[None, :, :, None], axis=1)
    value_gradient = jnp.sum(d_value_sel[:, :, None, :] * single_hot_mask[None, :, :, None], axis=1)
    key_gradient, value_gradient = lax.psum((key_gradient, value_gradient), ("row", "col"))
    local_key_gradient = lax.dynamic_slice_in_dim(
        key_gradient, row_place * token_batch, token_batch, 0
    ).reshape(token_batch, KEY_VALUE_HEADS * HEAD_WIDTH)
    local_value_gradient = lax.dynamic_slice_in_dim(
        value_gradient, row_place * token_batch, token_batch, 0
    ).reshape(token_batch, KEY_VALUE_HEADS * HEAD_WIDTH)
    query_out, pullback = jax.vjp(
        lambda r, g: query_form(r, g, own_cos, own_sin), query_raw, query_gains
    )
    d_query_raw, dg_query = pullback(d_queries)
    key_tile = jnp.broadcast_to(key_gain, (token_batch, 1, HEAD_WIDTH))
    key_out, pullback = jax.vjp(lambda r, g: key_form(r, g, own_cos, own_sin), key_raw, key_tile)
    d_key_raw, dg_key_rows = pullback(
        jnp.concatenate([local_key_gradient, local_value_gradient], axis=1)
    )
    slice_rows = token_batch // col_devs
    dg_key = jnp.sum(
        lax.dynamic_slice_in_dim(dg_key_rows, column_place * slice_rows, slice_rows, 0), axis=(0, 1)
    )
    grads_zero = grads_row(jnp.concatenate([d_query_raw, d_middle, d_key_raw], axis=1).astype(bf16))
    dw_query = inner_rows(spread_h, grads_zero[:, :q_cols])
    dw_left = inner_rows(spread_h, grads_zero[:, q_cols : q_cols + l_cols])
    key_grad_rows = grads_zero[:, q_cols + l_cols :]
    dw_keyval = inner_rows(spread_h, key_grad_rows)
    slab_width = kv_cols // col_devs
    d_hidden = reduce_col(
        against(grads_zero[:, :q_cols], query_b)
        + against(grads_zero[:, q_cols : q_cols + l_cols], left_b)
        + against(
            lax.dynamic_slice_in_dim(key_grad_rows, column_place * slab_width, slab_width, 1),
            lax.dynamic_slice_in_dim(keyval_b, column_place * slab_width, slab_width, 1),
        )
    )
    d_in, gain_grads[0] = norm_backward(inputs, scale_in, w_gains[0], d_hidden + d_half)
    grad_input = (d_half + d_in).astype(bf16)
    g_query, g_keyval, g_attend, g_gateup, g_down, g_left, g_right, g_pergate, g_perproj = (
        lax.psum_scatter(dw_query, "dp", scatter_dimension=1, tiled=True),
        lax.psum_scatter(dw_keyval, "dp", scatter_dimension=1, tiled=True),
        lax.psum_scatter(dw_attend, "dp", scatter_dimension=1, tiled=True),
        lax.psum_scatter(dw_gateup, "dp", scatter_dimension=2, tiled=True),
        lax.psum_scatter(dw_down, "dp", scatter_dimension=1, tiled=True),
        lax.psum_scatter(dw_left, "dp", scatter_dimension=1, tiled=True),
        lax.psum_scatter(dw_right, "dp", scatter_dimension=1, tiled=True),
        lax.psum_scatter(dw_pergate, "dp", scatter_dimension=1, tiled=True),
        lax.psum_scatter(dw_perproj, "dp", scatter_dimension=1, tiled=True),
    )
    gain_full = lax.dynamic_update_slice_in_dim(
        jnp.zeros((6, MODEL_WIDTH), single_float), jnp.stack(gain_grads), row_place * width_a, 1
    )
    head_full = lax.dynamic_update_slice_in_dim(
        jnp.zeros((QUERY_HEADS + 1, HEAD_WIDTH), single_float),
        dg_query,
        column_place * local_heads,
        0,
    )
    head_full = head_full.at[QUERY_HEADS].add(dg_key)
    logit_here = lax.dynamic_update_slice_in_dim(
        jnp.full((QUERY_HEADS,), NEGATIVE, single_float),
        jnp.max(block_peaks, axis=(0, 2)),
        column_place * local_heads,
        0,
    )

    def combine(left_part, right_part):
        return (
            left_part[0] + right_part[0],
            left_part[1] + right_part[1],
            jnp.maximum(left_part[2], right_part[2]),
        )

    gain_sum, head_sum, logit_top = joined(
        (gain_full, head_full, logit_here), ("dp", "row", "col"), combine
    )
    g_gains = lax.dynamic_slice_in_dim(gain_sum, row_place * width_a, width_a, 1)
    lead_device = (column_place == 0) & (data_at == 0)
    solo_device = lead_device & (row_place == 0)
    squares = jnp.float32(0.0)
    for gradient in (g_query, g_attend, g_gateup, g_down, g_left, g_right, g_pergate, g_perproj):
        squares = squares + jnp.sum(gradient * gradient)
    squares = squares + jnp.where(column_place == 0, jnp.sum(g_keyval * g_keyval), 0.0)
    squares = squares + jnp.where(lead_device, jnp.sum(g_gains * g_gains), 0.0)
    squares = squares + jnp.where(solo_device, jnp.sum(head_sum * head_sum), 0.0)
    grad_norm = jnp.sqrt(lax.psum(squares, ("dp", "row", "col")))
    clip_scale = CLIP / jnp.maximum(grad_norm, CLIP)
    scale_factors = LOGIT_CAP / jnp.maximum(logit_top, LOGIT_CAP)
    weights = (
        w_query,
        key_value_weight,
        w_attend,
        w_gateup,
        w_down,
        w_left,
        w_right,
        w_pergate,
        w_perproj,
        w_gains,
        w_heads,
    )
    moments = (
        m_query,
        key_value_first_moment,
        m_attend,
        m_gateup,
        m_down,
        m_left,
        m_right,
        m_pergate,
        m_perproj,
        m_gains,
        m_heads,
    )
    seconds = (
        v_query,
        key_value_second_moment,
        v_attend,
        v_gateup,
        v_down,
        v_left,
        v_right,
        v_pergate,
        v_perproj,
        v_gains,
        v_heads,
    )
    gradients = (
        g_query,
        g_keyval,
        g_attend,
        g_gateup,
        g_down,
        g_left,
        g_right,
        g_pergate,
        g_perproj,
        g_gains,
        head_sum,
    )
    step_rates = (
        MODEL_WIDTH ** (-0.5),
        MODEL_WIDTH ** (-0.5),
        (QUERY_HEADS * HEAD_WIDTH) ** (-0.5),
        MODEL_WIDTH ** (-0.5),
        FF ** (-0.5),
        MODEL_WIDTH ** (-0.5),
        RANK ** (-0.5),
        MODEL_WIDTH ** (-0.5),
        PLD ** (-0.5),
        GAIN_RATE,
        HEAD_RATE,
    )
    decays = (DECAY, DECAY, DECAY, DECAY, DECAY, DECAY, DECAY, DECAY, DECAY, 0.0, 0.0)
    updated = [
        adamw_step(
            weights[k], moments[k], seconds[k], gradients[k] * clip_scale, step_rates[k], decays[k]
        )
        for k in range(11)
    ]
    head_scale = jnp.sqrt(scale_factors)
    q_width = w_query.shape[1]
    q_head = (
        (column_place * data_devs + data_at) * q_width + jnp.arange(q_width, dtype=jnp.int32)
    ) // HEAD_WIDTH
    q_factor = jnp.sum(
        jnp.where(
            q_head[:, None] == jnp.arange(QUERY_HEADS, dtype=jnp.int32)[None, :],
            head_scale[None, :],
            0.0,
        ),
        axis=1,
    )
    new_query = updated[0][2] * q_factor[None, :]
    kv_width = key_value_weight.shape[1]
    key_value_index = data_at * kv_width + jnp.arange(kv_width, dtype=jnp.int32)
    key_value_scale = jnp.sqrt(
        jnp.min(scale_factors.reshape(KEY_VALUE_HEADS, QUERY_HEADS // KEY_VALUE_HEADS), axis=1)
    )
    key_value_choice = jnp.sum(
        jnp.where(
            (key_value_index // HEAD_WIDTH)[:, None]
            == jnp.arange(KEY_VALUE_HEADS, dtype=jnp.int32)[None, :],
            key_value_scale[None, :],
            0.0,
        ),
        axis=1,
    )
    key_value_factor = jnp.where(
        key_value_index < KEY_VALUE_HEADS * HEAD_WIDTH, key_value_choice, 1.0
    )
    new_keyval = updated[1][2] * key_value_factor[None, :]
    return (
        result,
        grad_input,
        grad_norm,
        scale_factors,
        updated[0][0],
        updated[0][1],
        new_query,
        updated[1][0],
        updated[1][1],
        new_keyval,
        updated[2][0],
        updated[2][1],
        updated[2][2],
        updated[3][0],
        updated[3][1],
        updated[3][2],
        updated[4][0],
        updated[4][1],
        updated[4][2],
        updated[5][0],
        updated[5][1],
        updated[5][2],
        updated[6][0],
        updated[6][1],
        updated[6][2],
        updated[7][0],
        updated[7][1],
        updated[7][2],
        updated[8][0],
        updated[8][1],
        updated[8][2],
        updated[9][0],
        updated[9][1],
        updated[9][2],
        updated[10][0],
        updated[10][1],
        updated[10][2],
    )


def solution(mesh):
    placed = (
        P(("dp", "col"), "row"),
        P(("dp", "row"), "col"),
        P(("dp", "col"), "row"),
        P(),
        P(),
        P("row", ("col", "dp")),
        P("row", ("col", "dp")),
        P("row", ("col", "dp")),
        P("row", "dp"),
        P("row", "dp"),
        P("row", "dp"),
        P("col", ("row", "dp")),
        P("col", ("row", "dp")),
        P("col", ("row", "dp")),
        P(None, "row", ("col", "dp")),
        P(None, "row", ("col", "dp")),
        P(None, "row", ("col", "dp")),
        P("col", ("row", "dp")),
        P("col", ("row", "dp")),
        P("col", ("row", "dp")),
        P("row", ("col", "dp")),
        P("row", ("col", "dp")),
        P("row", ("col", "dp")),
        P("col", ("row", "dp")),
        P("col", ("row", "dp")),
        P("col", ("row", "dp")),
        P("row", ("col", "dp")),
        P("row", ("col", "dp")),
        P("row", ("col", "dp")),
        P("col", ("row", "dp")),
        P("col", ("row", "dp")),
        P("col", ("row", "dp")),
        P(None, "row"),
        P(None, "row"),
        P(None, "row"),
        P(),
        P(),
        P(),
    )
    fits = (
        mesh.shape["col"] == KEY_VALUE_HEADS
        and mesh.shape["row"] * KEY_VALUE_HEADS == QUERY_HEADS
        and mesh.shape["dp"] == mesh.shape["row"]
    )
    return jax.shard_map(
        line_device if fits else per_device,
        mesh=mesh,
        in_specs=placed,
        out_specs=(
            P(("dp", "col"), "row"),
            P(("dp", "col"), "row"),
            P(),
            P(),
            P("row", ("col", "dp")),
            P("row", ("col", "dp")),
            P("row", ("col", "dp")),
            P("row", "dp"),
            P("row", "dp"),
            P("row", "dp"),
            P("col", ("row", "dp")),
            P("col", ("row", "dp")),
            P("col", ("row", "dp")),
            P(None, "row", ("col", "dp")),
            P(None, "row", ("col", "dp")),
            P(None, "row", ("col", "dp")),
            P("col", ("row", "dp")),
            P("col", ("row", "dp")),
            P("col", ("row", "dp")),
            P("row", ("col", "dp")),
            P("row", ("col", "dp")),
            P("row", ("col", "dp")),
            P("col", ("row", "dp")),
            P("col", ("row", "dp")),
            P("col", ("row", "dp")),
            P("row", ("col", "dp")),
            P("row", ("col", "dp")),
            P("row", ("col", "dp")),
            P("col", ("row", "dp")),
            P("col", ("row", "dp")),
            P("col", ("row", "dp")),
            P(None, "row"),
            P(None, "row"),
            P(None, "row"),
            P(),
            P(),
            P(),
        ),
        check_vma=False,
    )
```

```python
import functools

import jax
import jax.numpy as jnp
from jax import lax
from jax.experimental import pallas as pl
from jax.experimental.pallas import tpu as pltpu
from jax.sharding import PartitionSpec as P

MODEL_WIDTH = 2048
QUERY_HEADS = 8
KEY_VALUE_HEADS = 2
HEAD_WIDTH = 256
FF = 8192
RANK = 64
PLD = 256
IMG = 256
STEP = 10


EPS = 1e-06
ROPE_BASE = 1000000.0
BETA_ONE = 0.5
BETA_TWO = 0.5
ADAM_EPS = 1e-08
DECAY = 0.01
CLIP = 1.0
LOGIT_CAP = 4.0
GAIN_RATE = 0.6
HEAD_RATE = 0.1
HALF_ROOT = 0.7071067811865476
NEGATIVE = -1e30


def joined(part, axis, combine):
    gathered = jax.tree.map(lambda a: lax.all_gather(a, axis), part)

    def take(source):
        return jax.tree.map(lambda a: lax.dynamic_index_in_dim(a, source, 0, False), gathered)

    return lax.fori_loop(
        1, lax.axis_size(axis), lambda source, state: combine(state, take(source)), take(0)
    )


def row_total(values_in):
    return lax.psum(values_in, "row")


def spread_col(values_in):
    return lax.all_gather(values_in, "col", axis=0, tiled=True)


def reduce_row(values_in):
    return lax.psum_scatter(values_in, "row", scatter_dimension=0, tiled=True)


def spread_row(values_in):
    return lax.all_gather(values_in, "row", axis=0, tiled=True)


def reduce_col(values_in):
    return lax.psum_scatter(values_in, "col", scatter_dimension=0, tiled=True)


def grads_col(values_in):
    return lax.all_gather(values_in, "col", axis=0, tiled=True)


def grads_row(values_in):
    return lax.all_gather(values_in, "row", axis=0, tiled=True)


def inner_rows(left_mat, right_mat):
    return lax.dot_general(
        left_mat, right_mat, (((0,), (0,)), ((), ())), preferred_element_type=jnp.float32
    )


def against(grad_mat, weight_mat):
    return lax.dot_general(
        grad_mat, weight_mat, (((1,), (1,)), ((), ())), preferred_element_type=jnp.float32
    )


def flat_dot(left_mat, right_mat):
    return jnp.dot(left_mat, right_mat, preferred_element_type=jnp.float32)


def norm_forward(values_in, gain_vec):
    total_sq = row_total(jnp.sum(values_in * values_in, axis=-1, keepdims=True))
    norm_scale = lax.rsqrt(total_sq / MODEL_WIDTH + EPS)
    return (values_in * norm_scale * gain_vec, norm_scale)


def norm_backward(values_in, norm_scale, gain_vec, grad_out):
    weighted = grad_out * gain_vec
    inner_sum = row_total(jnp.sum(weighted * values_in, axis=-1, keepdims=True))
    grad_in = norm_scale * weighted - values_in * (norm_scale * norm_scale * norm_scale) * (
        inner_sum / MODEL_WIDTH
    )
    return (grad_in, jnp.sum(grad_out * values_in * norm_scale, axis=0))


def norm_rows(values_in, gain_vec):
    return (
        values_in
        * lax.rsqrt(jnp.mean(values_in * values_in, axis=-1, keepdims=True) + EPS)
        * gain_vec
    )


def rope_tables(places, feat_width):
    half_width = feat_width // 2
    powers = jnp.arange(half_width, dtype=jnp.int32).astype(jnp.float32) * (2.0 / feat_width)
    frequency = jnp.power(jnp.float32(ROPE_BASE), -powers)
    angles = places.astype(jnp.float32)[:, None] * frequency[None, :]
    return (jnp.cos(angles), jnp.sin(angles))


def rotate(values_in, cos_tab, sin_tab):
    half_width = values_in.shape[-1] // 2
    part_one = values_in[..., :half_width]
    part_two = values_in[..., half_width:]
    cos_row = cos_tab[:, None, :]
    sin_row = sin_tab[:, None, :]
    return jnp.concatenate(
        [part_one * cos_row - part_two * sin_row, part_two * cos_row + part_one * sin_row], axis=-1
    )


def query_form(unscaled_rows, gain_rows, cos_tab, sin_tab):
    shaped = unscaled_rows.reshape(unscaled_rows.shape[0], gain_rows.shape[0], HEAD_WIDTH)
    return rotate(norm_rows(shaped, gain_rows[None]), cos_tab, sin_tab)


def key_form(unscaled_rows, gain_vec, cos_tab, sin_tab):
    count_of_rows = unscaled_rows.shape[0]
    key_rows = unscaled_rows[:, : KEY_VALUE_HEADS * HEAD_WIDTH].reshape(
        count_of_rows, KEY_VALUE_HEADS, HEAD_WIDTH
    )
    value_rows = unscaled_rows[:, KEY_VALUE_HEADS * HEAD_WIDTH :].reshape(
        count_of_rows, KEY_VALUE_HEADS, HEAD_WIDTH
    )
    key_rows = rotate(norm_rows(key_rows, gain_vec), cos_tab, sin_tab)
    value_rows = norm_rows(value_rows, 1.0)
    return jnp.concatenate(
        [
            key_rows.reshape(count_of_rows, KEY_VALUE_HEADS * HEAD_WIDTH),
            value_rows.reshape(count_of_rows, KEY_VALUE_HEADS * HEAD_WIDTH),
        ],
        axis=1,
    )


def piece_of(places, starts):
    inside = (places[:, None] >= starts[None, :]) & (places[:, None] < starts[None, :] + IMG)
    labels = jnp.arange(1, starts.shape[0] + 1, dtype=jnp.int32)
    return jnp.sum(jnp.where(inside, labels[None, :], 0), axis=1) - 1


def visible(query_places, key_places, query_pieces, key_pieces, length):
    causal = key_places[None, :] <= query_places[:, None]
    same_piece = (query_pieces[:, None] == key_pieces[None, :]) & (query_pieces[:, None] >= 0)
    return (key_places[None, :] < length) & (causal | same_piece)


def block_mask(own_places, key_places, key_pieces, length, starts):
    return visible(own_places, key_places, piece_of(own_places, starts), key_pieces, length)


def attention_forward(queries, key_sel, value_sel, own_places, key_places, length, starts):
    count_of_rows, head_count = (queries.shape[0], queries.shape[1])
    block_size = min(512, count_of_rows)
    key_pieces = piece_of(key_places, starts)
    stacked = queries.reshape(count_of_rows // block_size, block_size, head_count, HEAD_WIDTH)

    def one_block(element):
        block_rows, block_at = element
        allowed = block_mask(own_places, key_places, key_pieces, length, starts)
        scores = jnp.einsum("qhd,khd->hqk", block_rows, key_sel, preferred_element_type=jnp.float32)
        masked = jnp.where(allowed[None], scores, NEGATIVE)
        peak_row = jnp.max(masked, axis=-1, keepdims=True)
        raw_weights = jnp.where(allowed[None], jnp.exp(masked - peak_row), 0.0)
        total_row = jnp.sum(raw_weights, axis=-1, keepdims=True)
        attn_probs = (raw_weights / total_row).astype(jnp.bfloat16)
        outputs = jnp.einsum(
            "hqk,khd->qhd", attn_probs, value_sel, preferred_element_type=jnp.float32
        )
        return (outputs, peak_row[..., 0], total_row[..., 0])

    return lax.map(one_block, (stacked, jnp.arange(count_of_rows // block_size, dtype=jnp.int32)))


def attention_backward(
    queries,
    key_sel,
    value_sel,
    grad_attended,
    block_peaks,
    block_totals,
    own_places,
    key_places,
    length,
    starts,
):
    count_of_rows, head_count = (queries.shape[0], queries.shape[1])
    block_size = min(512, count_of_rows)
    block_count = count_of_rows // block_size
    key_pieces = piece_of(key_places, starts)
    stacked = queries.reshape(block_count, block_size, head_count, HEAD_WIDTH)
    grad_stacked = grad_attended.reshape(block_count, block_size, head_count, HEAD_WIDTH)

    def one_block(carry, element):
        dk_sum, dv_sum = carry
        block_rows, grad_rows, peak_row, total_row, block_at = element
        allowed = block_mask(own_places, key_places, key_pieces, length, starts)
        scores = jnp.einsum("qhd,khd->hqk", block_rows, key_sel, preferred_element_type=jnp.float32)
        masked = jnp.where(allowed[None], scores, NEGATIVE)
        raw_weights = jnp.where(allowed[None], jnp.exp(masked - peak_row[..., None]), 0.0)
        attn_probs = raw_weights / total_row[..., None]
        probs_low = attn_probs.astype(jnp.bfloat16)
        grad_probs = jnp.einsum(
            "qhd,khd->hqk", grad_rows, value_sel, preferred_element_type=jnp.float32
        )
        delta_row = jnp.sum(attn_probs * grad_probs, axis=-1, keepdims=True)
        grad_scores = (attn_probs * (grad_probs - delta_row)).astype(jnp.bfloat16)
        grad_query = jnp.einsum(
            "hqk,khd->qhd", grad_scores, key_sel, preferred_element_type=jnp.float32
        )
        dk_sum = dk_sum + jnp.einsum(
            "hqk,qhd->khd", grad_scores, block_rows, preferred_element_type=jnp.float32
        )
        dv_sum = dv_sum + jnp.einsum(
            "hqk,qhd->khd", probs_low, grad_rows, preferred_element_type=jnp.float32
        )
        return ((dk_sum, dv_sum), grad_query)

    zero_keys = jnp.zeros(key_sel.shape, jnp.float32)
    (dk_sum, dv_sum), grad_query = lax.scan(
        one_block,
        (zero_keys, zero_keys),
        (
            stacked,
            grad_stacked,
            block_peaks,
            block_totals,
            jnp.arange(block_count, dtype=jnp.int32),
        ),
    )
    return (grad_query.reshape(count_of_rows, head_count, HEAD_WIDTH), dk_sum, dv_sum)


def adamw_step(weight, moment_one, moment_two, gradient, rate, decay):
    moment_one = BETA_ONE * moment_one + (1.0 - BETA_ONE) * gradient
    moment_two = BETA_TWO * moment_two + (1.0 - BETA_TWO) * gradient * gradient
    mean_step = moment_one / (1.0 - BETA_ONE**STEP)
    spread = moment_two / (1.0 - BETA_TWO**STEP)
    return (
        moment_one,
        moment_two,
        weight - rate * (mean_step / (jnp.sqrt(spread) + ADAM_EPS) + decay * weight),
    )


MESH = pl.DeviceIdType.MESH
LOW = jnp.bfloat16
FULL = jnp.float32


def cost(micros, flops=0):
    return pl.CostEstimate(
        flops=flops, bytes_accessed=int(micros * 3.0e6), transcendentals=0
    )


def params(ident, mebibytes=48):
    return pltpu.CompilerParams(
        collective_id=ident, has_side_effects=True, vmem_limit_bytes=mebibytes * 2**20
    )


def push(source, target, send, recv, device):
    return pltpu.make_async_remote_copy(
        source, target, send, recv, device_id=device, device_id_type=MESH
    )


class Line:
    def __init__(self, source, shape, place, core=False, view=None):
        self.source, self.shape, self.place, self.core = source, shape, place, core
        self.view = view

    def semaphores(self, count, data):
        dma = pltpu.SemaphoreType.DMA
        return [dma((count,)), dma((count,)), dma((2 * count,))] * 2 + [dma]

    def bind(self, x_ref, o_ref, sems, spots, sizes):
        self.o_ref, self.sems = o_ref, sems
        self.me, self.column, self.at = spots
        self.count = sizes[0]
        self.x_ref = self.view(x_ref, self.column) if self.view else x_ref

    def slot(self, source):
        return self.place(self.o_ref, self.column, source)

    def other(self, source):
        return self.place(self.o_ref, 1 - self.column, source)

    def to_left(self, source, k, origin):
        return push(origin, self.slot(source), self.sems[0].at[k], self.sems[4].at[k], {"row": self.me - 1})

    def to_right(self, source, k, origin):
        return push(origin, self.slot(source), self.sems[1].at[k], self.sems[3].at[k], {"row": self.me + 1})

    def to_core(self, source, k, origin):
        return push(origin, self.slot(source), self.sems[2].at[k], self.sems[5].at[k], {"col": 1 - self.column})

    def from_core(self, source, k):
        there = self.other(source)
        return push(there, there, self.sems[2].at[k], self.sems[5].at[k], {"col": 1 - self.column})

    def from_left(self, source, k):
        there = self.slot(source)
        return push(there, there, self.sems[1].at[k], self.sems[3].at[k - 1], {"row": self.me - 1})

    def from_right(self, source, k):
        there = self.slot(source)
        return push(there, there, self.sems[0].at[k], self.sems[4].at[k - 1], {"row": self.me + 1})

    def own(self):
        return pltpu.make_async_copy(self.x_ref, self.slot(self.me), self.sems[6])

    def start(self):
        me, count = self.me, self.count

        @pl.when(me > 0)
        def _():
            self.to_left(me, 0, self.x_ref).start()

        @pl.when(me < count - 1)
        def _():
            self.to_right(me, 0, self.x_ref).start()

        if self.core:
            self.to_core(me, 0, self.x_ref).start()
        self.own().start()

    def step(self, k):
        me, count = self.me, self.count

        @pl.when(me - k >= 0)
        def _():
            self.from_left(me - k, k).wait_recv()
            block = self.slot(me - k)

            @pl.when(me < count - 1)
            def _():
                self.to_right(me - k, k, block).start()

            if self.core:
                self.to_core(me - k, k, block).start()

        @pl.when(me + k < count)
        def _():
            self.from_right(me + k, k).wait_recv()
            block = self.slot(me + k)

            @pl.when(me > 0)
            def _():
                self.to_left(me + k, k, block).start()

            if self.core:
                self.to_core(me + k, count - 1 + k, block).start()

    def finish(self):
        me, count = self.me, self.count
        self.own().wait()

        @pl.when(me > 0)
        def _():
            self.to_left(me, 0, self.x_ref).wait_send()

        @pl.when(me < count - 1)
        def _():
            self.to_right(me, 0, self.x_ref).wait_send()

        if self.core:
            self.to_core(me, 0, self.x_ref).wait_send()
            self.from_core(me, 0).wait_recv()

        @pl.loop(1, count)
        def _(k):
            @pl.when(me - k >= 0)
            def _():
                @pl.when(me < count - 1)
                def _():
                    self.to_right(me - k, k, self.x_ref).wait_send()

                if self.core:
                    self.to_core(me - k, k, self.x_ref).wait_send()
                    self.from_core(me - k, k).wait_recv()

            @pl.when(me + k < count)
            def _():
                @pl.when(me > 0)
                def _():
                    self.to_left(me + k, k, self.x_ref).wait_send()

                if self.core:
                    self.to_core(me + k, count - 1 + k, self.x_ref).wait_send()
                    self.from_core(me + k, count - 1 + k).wait_recv()


class Swap:
    def __init__(self, source, shape, take, place, axis="row"):
        self.source, self.shape, self.take, self.place = source, shape, take, place
        self.axis = axis

    def semaphores(self, count, data):
        size = count if self.axis == "row" else data
        return [pltpu.SemaphoreType.DMA((size,)), pltpu.SemaphoreType.DMA((size,))]

    def bind(self, x_ref, o_ref, sems, spots, sizes):
        self.x_ref, self.o_ref, self.sems = x_ref, o_ref, sems
        self.me = spots[0] if self.axis == "row" else spots[2]
        self.count = sizes[0] if self.axis == "row" else sizes[1]

    def copy(self, k):
        target = lax.rem(self.me + k, self.count)
        return push(
            self.take(self.x_ref, target),
            self.place(self.o_ref, self.me),
            self.sems[0].at[k],
            self.sems[1].at[k],
            {self.axis: target},
        )

    def own(self):
        return pltpu.make_async_copy(
            self.take(self.x_ref, self.me), self.place(self.o_ref, self.me), self.sems[0].at[0]
        )

    def start(self):
        for k in range(1, self.count):
            self.copy(k).start()
        self.own().start()

    def step(self, k):
        pass

    def finish(self):
        self.own().wait()
        for k in range(1, self.count):
            self.copy(k).wait_send()
            origin = lax.rem(self.me + self.count - k, self.count)
            there = self.place(self.o_ref, origin)
            push(there, there, self.sems[0].at[k], self.sems[1].at[k], {self.axis: origin}).wait_recv()


class Pair:
    core = True

    def __init__(self, source):
        self.source, self.shape = source, source.shape

    def semaphores(self, count, data):
        dma = pltpu.SemaphoreType.DMA
        return [dma, dma, dma]

    def bind(self, x_ref, o_ref, sems, spots, sizes):
        self.x_ref, self.o_ref, self.sems = x_ref, o_ref, sems
        self.column = spots[1]

    def copy(self):
        other = 1 - self.column
        return push(self.x_ref.at[other], self.o_ref.at[1], self.sems[0], self.sems[1], {"col": other})

    def own(self):
        return pltpu.make_async_copy(self.x_ref.at[self.column], self.o_ref.at[0], self.sems[2])

    def start(self):
        self.copy().start()
        self.own().start()

    def step(self, k):
        pass

    def finish(self):
        self.own().wait()
        self.copy().wait()


class Reduce:
    def __init__(self, source, shape, cut, core=True):
        self.source, self.shape, self.cut, self.core = source, shape, cut, core
        self.high, self.wide = shape
        self.dtype = FULL

    def semaphores(self, count, data):
        dma = pltpu.SemaphoreType.DMA
        slots = pltpu.VMEM((count,) + self.shape, self.source.dtype)
        whole = pltpu.VMEM(self.source.shape[1:] if self.core else self.source.shape, self.source.dtype)
        stage = pltpu.VMEM(self.shape, FULL)
        fourth = slots if self.core else pltpu.VMEM((1, 16, 128), self.source.dtype)
        return [whole, stage, slots, slots, slots, fourth] + [dma((count,))] * 6 + [dma, dma]

    def bind(self, x_ref, o_ref, sems, spots, sizes):
        self.x_ref, self.o_ref = x_ref, o_ref
        self.mine, self.stage, self.out, self.left_in, self.right_in, self.core_in = sems[:6]
        self.sems = sems[6:]
        self.me, self.column = spots[0], spots[1]
        self.count = sizes[0]

    def beside(self, q):
        return push(
            self.cut(self.x_ref.at[1 - self.column], q),
            self.core_in.at[q],
            self.sems[0].at[q],
            self.sems[3].at[q],
            {"col": 1 - self.column},
        )

    def to_left(self, q):
        return push(self.out.at[q], self.left_in.at[q], self.sems[1].at[q], self.sems[4].at[q], {"row": self.me - 1})

    def to_right(self, q):
        return push(self.out.at[q], self.right_in.at[q], self.sems[2].at[q], self.sems[5].at[q], {"row": self.me + 1})

    def from_right(self, q):
        return push(self.left_in.at[q], self.left_in.at[q], self.sems[1].at[q], self.sems[4].at[q], {"row": self.me + 1})

    def from_left(self, q):
        return push(self.right_in.at[q], self.right_in.at[q], self.sems[2].at[q], self.sems[5].at[q], {"row": self.me - 1})

    def own(self):
        return pltpu.make_async_copy(
            self.x_ref.at[self.column] if self.core else self.x_ref, self.mine, self.sems[6]
        )

    def start(self):
        self.own().start()
        if self.core:
            for q in range(self.count):
                self.beside(q).start()

    def added(self, target, q, others):
        step = min(self.high, max(16, 65536 // self.wide))
        while self.high % step:
            step //= 2
        cut = self.cut(self.mine, q)
        others = ([self.core_in] if self.core else []) + others

        @pl.loop(0, self.high // step)
        def _(at):
            rows = pl.ds(pl.multiple_of(at * step, step), step)
            total = cut[rows].astype(FULL)
            for other in others:
                total = total + other[q, rows].astype(FULL)
            target[rows] = total.astype(target.dtype)

    def step(self, k):
        me, count = self.me, self.count
        t = k - 1
        q_left = t - (count - 1 - me)
        q_right = count - 1 - (t - me)

        @pl.when(t == 0)
        def _():
            self.own().wait()

        @pl.when((q_left >= 0) & (q_left < me))
        def _():
            if self.core:
                self.beside(q_left).wait()

            @pl.when(me < count - 1)
            def _():
                self.from_right(q_left).wait_recv()
                self.added(self.out.at[q_left], q_left, [self.left_in])

            @pl.when(me == count - 1)
            def _():
                self.added(self.out.at[q_left], q_left, [])

            self.to_left(q_left).start()

        @pl.when((t >= me) & (q_right > me))
        def _():
            if self.core:
                self.beside(q_right).wait()

            @pl.when(me > 0)
            def _():
                self.from_left(q_right).wait_recv()
                self.added(self.out.at[q_right], q_right, [self.right_in])

            @pl.when(me == 0)
            def _():
                self.added(self.out.at[q_right], q_right, [])

            self.to_right(q_right).start()

    def finish(self):
        me, count = self.me, self.count
        if self.core:
            self.beside(me).wait()

        @pl.when(me < count - 1)
        def _():
            self.from_right(me).wait_recv()

        @pl.when(me > 0)
        def _():
            self.from_left(me).wait_recv()

        @pl.when(me == 0)
        def _():
            self.added(self.stage, me, [self.left_in])

        @pl.when(me == count - 1)
        def _():
            self.added(self.stage, me, [self.right_in])

        @pl.when((me > 0) & (me < count - 1))
        def _():
            self.added(self.stage, me, [self.left_in, self.right_in])

        out = pltpu.make_async_copy(self.stage, self.o_ref, self.sems[7])
        out.start()

        @pl.loop(0, count)
        def _(q):
            @pl.when(q < me)
            def _():
                self.to_left(q).wait_send()

            @pl.when(q > me)
            def _():
                self.to_right(q).wait_send()

        out.wait()


class ShardSum:
    axis = "dp"

    def __init__(self, source, out_cols):
        self.source, self.out_cols = source, out_cols
        self.parts = source.shape[1] // out_cols // lax.axis_size("dp")
        self.shape = (source.shape[0], self.parts * out_cols)

    def semaphores(self, count, data):
        dma = pltpu.SemaphoreType.DMA
        buf = pltpu.VMEM((data,) + self.shape, self.source.dtype)
        stage = pltpu.VMEM(self.shape, self.source.dtype)
        return [buf, stage, dma((data, self.parts)), dma((data, self.parts)), dma]

    def bind(self, x_ref, o_ref, sems, spots, sizes):
        self.x_ref, self.o_ref = x_ref, o_ref
        self.buf, self.stage, self.send, self.recv, self.local = sems
        self.at, self.data = spots[2], sizes[1]

    def copy(self, k, s):
        target = lax.rem(self.at + k, self.data)
        wide = self.out_cols
        source = self.x_ref.at[:, pl.ds(pl.multiple_of((s * self.data + target) * wide, wide), wide)]
        slot = self.buf.at[k, :, pl.ds(s * wide, wide)]
        if k == 0:
            return pltpu.make_async_copy(source, slot, self.send.at[k, s])
        return push(source, slot, self.send.at[k, s], self.recv.at[k, s], {"dp": target})

    def start(self):
        for k in range(self.data):
            for s in range(self.parts):
                self.copy(k, s).start()

    def step(self, k):
        pass

    def finish(self):
        for k in range(self.data):
            for s in range(self.parts):
                self.copy(k, s).wait()

        @pl.loop(0, self.shape[0] // 64)
        def _(at):
            rows = pl.ds(pl.multiple_of(at * 64, 64), 64)
            total = self.buf[0, rows].astype(FULL)
            for k in range(1, self.data):
                total = total + self.buf[k, rows].astype(FULL)
            self.stage[rows] = total.astype(self.stage.dtype)

        out = pltpu.make_async_copy(self.stage, self.o_ref, self.local)
        out.start()
        out.wait()


class Bundle:
    def __init__(self, items):
        self.items = items
        self.number = len(items)
        self.sizes = lax.axis_size("row"), lax.axis_size("dp")
        self.kinds = [item.semaphores(*self.sizes) for item in items]
        self.across = any(getattr(item, "axis", None) == "dp" for item in items)
        self.cores = any(getattr(item, "core", False) for item in items)
        self.sources = [item.source for item in items]
        self.shapes = [
            jax.ShapeDtypeStruct(item.shape, getattr(item, "dtype", item.source.dtype)) for item in items
        ]
        self.specs = [pl.BlockSpec(memory_space=pl.ANY)] * self.number
        self.scratch = sum(self.kinds, [])

    def bind(self, x_refs, o_refs, sems):
        self.spots = lax.axis_index("row"), lax.axis_index("col"), lax.axis_index("dp")
        for item, x_ref, o_ref, kind in zip(self.items, x_refs, o_refs, self.kinds):
            item.bind(x_ref, o_ref, sems[: len(kind)], self.spots, self.sizes)
            sems = sems[len(kind) :]

    def greet(self, across=False, cores=False):
        me, column, at = self.spots
        count, data = self.sizes
        across, cores = across or self.across, cores or self.cores
        barrier = pltpu.get_barrier_semaphore()
        for k in range(1, count):
            pl.semaphore_signal(
                barrier, inc=1, device_id={"row": lax.rem(me + k, count)}, device_id_type=MESH
            )
        if across:
            for k in range(1, data):
                pl.semaphore_signal(
                    barrier, inc=1, device_id={"dp": lax.rem(at + k, data)}, device_id_type=MESH
                )
        if cores:
            pl.semaphore_signal(barrier, inc=1, device_id={"col": 1 - column}, device_id_type=MESH)
        pl.semaphore_wait(barrier, count - 1 + (data - 1) * int(across) + int(cores))

    def start(self):
        for item in self.items:
            item.start()

    def step(self, k):
        for item in self.items:
            item.step(k)

    def finish(self):
        for item in self.items:
            item.finish()


def transfers(items, ident, micros, mebibytes=16, work=None, arrays=(), shapes=()):
    bundle = Bundle(items)
    number, given, made = bundle.number, len(arrays), len(shapes)

    def kernel(*refs):
        inputs, refs = refs[:given], refs[given:]
        x_refs, refs = refs[:number], refs[number:]
        outputs, refs = refs[:made], refs[made:]
        bundle.bind(x_refs, refs[:number], refs[number:])
        bundle.greet()
        bundle.start()
        if work:
            work(inputs, outputs)
        for k in range(1, bundle.sizes[0]):
            bundle.step(k)
        bundle.finish()

    vmem = pl.BlockSpec(memory_space=pltpu.VMEM)
    return pl.pallas_call(
        kernel,
        out_shape=list(shapes) + bundle.shapes,
        in_specs=[vmem] * given + bundle.specs,
        out_specs=[vmem] * made + bundle.specs,
        scratch_shapes=bundle.scratch,
        compiler_params=params(ident, mebibytes),
        cost_estimate=cost(micros),
    )(*arrays, *bundle.sources)


def local(function, shapes, *arrays, mebibytes=60):
    def kernel(*refs):
        results = function(*[ref[...] for ref in refs[: len(arrays)]])
        for ref, value in zip(refs[len(arrays) :], results):
            ref[...] = value.astype(ref.dtype)

    vmem = pl.BlockSpec(memory_space=pltpu.VMEM)
    return pl.pallas_call(
        kernel,
        out_shape=[jax.ShapeDtypeStruct(shape, kind) for shape, kind in shapes],
        in_specs=[vmem] * len(arrays),
        out_specs=[vmem] * len(shapes),
        compiler_params=pltpu.CompilerParams(vmem_limit_bytes=mebibytes * 2**20),
        cost_estimate=cost(5),
    )(*arrays)


def norm_back(values_in, gain, grad_out):
    scale = lax.rsqrt(jnp.mean(values_in * values_in, axis=-1, keepdims=True) + EPS)
    weighted = grad_out * gain
    inner = jnp.mean(weighted * values_in, axis=-1, keepdims=True)
    return (
        scale * weighted - values_in * (scale * scale * scale) * inner,
        jnp.sum(grad_out * values_in * scale, axis=0, keepdims=True),
    )


def mix(acts, projected, gains, left_t, right_w):
    inputs = acts.astype(FULL)
    hidden, _ = whole_norm(inputs, gains[0:1])
    hidden_low = hidden.astype(LOW)
    middle = against(hidden_low, left_t).astype(LOW)
    right_raw = flat_dot(middle, right_w)
    right_n, _ = whole_norm(right_raw, gains[1:2])
    proj_n, _ = whole_norm(projected, gains[2:3])
    mixture = ((inputs + proj_n) + (hidden + right_n)) * HALF_ROOT
    ffn_n, _ = whole_norm(mixture, gains[3:4])
    return hidden_low, middle, right_raw, mixture, ffn_n


def per_layer_both(mixture, down_raw, gains, extras, pergate_t, perproj_w, upstream):
    extras, upstream = extras.astype(FULL), upstream.astype(FULL)
    down_n, _ = whole_norm(down_raw, gains[4:5])
    block_out = mixture + down_n
    out_low = block_out.astype(LOW)
    pgate = against(out_low, pergate_t)
    curve, slope = gelu_of(pgate)
    pact = (curve * extras).astype(LOW)
    perproj = flat_dot(pact, perproj_w)
    perproj_n, _ = whole_norm(perproj, gains[5:6])
    result = block_out + perproj_n
    d_perproj, gain_five = norm_back(perproj, gains[5:6], upstream)
    d_perproj = d_perproj.astype(LOW)
    d_pact = against(d_perproj, perproj_w)
    d_pgate = (d_pact * extras * slope).astype(LOW)
    d_out = upstream + flat_dot(d_pgate, pergate_t)
    d_down, gain_four = norm_back(down_raw, gains[4:5], d_out)
    return (
        result,
        d_out,
        d_down,
        inner_rows(pact, d_perproj),
        inner_rows(d_pgate, out_low),
        gain_four,
        gain_five,
    )


def mix_back(
    d_out, d_ffn, mixture, projected, right_raw, gains, acts, left_t, right_w, hidden_low, middle, dw_pergate, dw_perproj
):
    d_mix, gain_three = norm_back(mixture, gains[3:4], d_ffn)
    d_half = (d_out + d_mix) * HALF_ROOT
    d_proj, gain_two = norm_back(projected, gains[2:3], d_half)
    d_right, gain_one = norm_back(right_raw, gains[1:2], d_half)
    d_right = d_right.astype(LOW)
    dw_right = inner_rows(middle, d_right).astype(LOW)
    d_middle = against(d_right, right_w).astype(LOW)
    dw_left = inner_rows(d_middle, hidden_low).astype(LOW)
    d_hidden = d_half + flat_dot(d_middle, left_t)
    inner = row_sums(d_hidden * gains[0:1] * acts.astype(FULL))
    parts = []
    for core in range(2):
        for grad in (dw_left, dw_right, dw_pergate, dw_perproj):
            high = grad.shape[0] // 2
            parts.append(grad[core * high : (core + 1) * high])
    return d_proj, d_half, d_middle, jnp.concatenate(parts, axis=0), inner, gain_one, gain_two, gain_three


def row_sums(values_in):
    ones = jnp.ones((8, values_in.shape[1]), FULL)
    return lax.dot_general(
        ones,
        values_in,
        (((1,), (1,)), ((), ())),
        precision=lax.Precision.HIGHEST,
        preferred_element_type=FULL,
    )


def shard_parts(sums, extents):
    out_cols, data = 128, sums.shape[1] // 128
    parts = []
    for at in range(data):
        start = 0
        for rows, by_rows in extents:
            if by_rows:
                high = rows // data
                cut = sums[start + at * high : start + (at + 1) * high]
                parts += [cut[:, k * out_cols : (k + 1) * out_cols] for k in range(data)]
            else:
                parts.append(sums[start : start + rows, at * out_cols : (at + 1) * out_cols])
            start += rows
    return jnp.concatenate(parts, axis=0)


def key_value_ends(hidden, d_key, d_value, qkv_w, d_hidden, acts, gain, sums, extents):
    first = lax.axis_index("col") == 0
    key_w = jnp.where(first, qkv_w[0, :, HEAD_WIDTH:], qkv_w[1, :, HEAD_WIDTH:])
    value_w = jnp.where(first, qkv_w[2, :, HEAD_WIDTH:], qkv_w[3, :, HEAD_WIDTH:])
    d_hidden = d_hidden + against(d_key, key_w) + against(d_value, value_w)
    return (
        jnp.concatenate([inner_rows(hidden, d_key), inner_rows(hidden, d_value)], axis=0),
        d_hidden,
        row_sums(d_hidden * gain[0:1] * acts.astype(FULL)),
        shard_parts(sums, extents),
    )


def input_ends(pair, half, middle, left_t, acts, scale, gains, inner, inner_share, grads, gateup_squares, gain_grads, dg_query, dg_key, top):
    half_tok, wide = acts.shape
    rows_n = inner.shape[1]
    width = gain_grads[0].shape[1]
    lanes = width // 128
    head_rows = (QUERY_HEADS + 1) * HEAD_WIDTH // 128
    sum_rows = 6 * lanes + head_rows
    high = -(-(sum_rows + 1) // 8) * 8 + 8
    given = (pair, half, middle, left_t, acts, scale, gains, inner, inner_share, gateup_squares, dg_query, dg_key, top)
    given += tuple(gain_grads) + tuple(grads)

    def kernel(*refs):
        pair, half, middle, left_t, acts, scale, gains, inner, inner_share, gateup_squares, dg_query, dg_key, top = refs[:13]
        gain_grads, grads = refs[13:18], refs[18:23]
        out_ref, small_ref = refs[23:]
        me, column = lax.axis_index("row"), lax.axis_index("col")
        total = None
        for core in range(2):
            for row in range(rows_n):
                part = jnp.where(
                    column == 0, inner[core, row, :, :half_tok], inner[core, row, :, half_tok:]
                )
                total = part if total is None else total + part
        shares = jnp.concatenate(
            [jnp.where(column == 0, inner_share[0, row], inner_share[1, row]) for row in range(rows_n)],
            axis=1,
        )
        mean = ((total + shares) / MODEL_WIDTH).T[:, :1]
        inputs = acts[...].astype(FULL)
        factor = scale[:, :1]
        gain = gains[0:1]
        left = left_t[:, pl.ds(pl.multiple_of(me * wide, wide), wide)]
        d_hidden = (
            pair[0].astype(FULL) + pair[1].astype(FULL) + half[...].astype(FULL) + flat_dot(middle[...], left)
        )
        out_ref[...] = (
            half[...].astype(FULL)
            + factor * (d_hidden * gain)
            - inputs * (factor * factor * factor) * mean
        ).astype(LOW)
        small_ref[...] = jnp.zeros(small_ref.shape, FULL)
        gain_zero = jnp.sum(d_hidden * inputs * factor, axis=0, keepdims=True)
        for k in range(wide // 128):
            small_ref[pl.ds(me * (wide // 128) + k, 1)] = gain_zero[:, k * 128 : (k + 1) * 128]
        for at, grad in enumerate(gain_grads):
            for k in range(lanes):
                small_ref[(at + 1) * lanes + k : (at + 1) * lanes + k + 1] = grad[:, k * 128 : (k + 1) * 128]
        head = column * rows_n + me
        for k in range(HEAD_WIDTH // 128):
            cut = slice(k * 128, (k + 1) * 128)
            small_ref[pl.ds(6 * lanes + head * (HEAD_WIDTH // 128) + k, 1)] = dg_query[:, cut]
            last = 6 * lanes + QUERY_HEADS * (HEAD_WIDTH // 128) + k
            small_ref[last : last + 1] = dg_key[:, cut]
        squares = jnp.zeros((1, 128), FULL)
        first = jnp.where(column == 0, 1.0, 0.0)
        for grad, weight in zip(grads, (1.0, first, 1.0, 1.0, 1.0)):
            values = grad[...].astype(FULL).reshape(-1, grad.shape[-1])
            line = jnp.sum(values * values, axis=0, keepdims=True)
            for cut in range(0, values.shape[1], 128):
                squares = squares + weight * line[:, cut : cut + 128]
        line = jnp.sum(gateup_squares[...], axis=0, keepdims=True)
        for cut in range(0, line.shape[1], 128):
            squares = squares + line[:, cut : cut + 128]
        small_ref[sum_rows : sum_rows + 1] = jnp.broadcast_to(
            jnp.sum(squares, axis=1, keepdims=True), (1, 128)
        )
        places = lax.broadcasted_iota(jnp.int32, (8, 128), 1)
        small_ref[high - 8 :] = jnp.where(places == head, top[...], NEGATIVE)

    vmem = pl.BlockSpec(memory_space=pltpu.VMEM)
    return pl.pallas_call(
        kernel,
        out_shape=[
            jax.ShapeDtypeStruct((half_tok, wide), LOW),
            jax.ShapeDtypeStruct((high, 128), FULL),
        ],
        in_specs=[vmem] * 23,
        out_specs=[vmem] * 2,
        compiler_params=pltpu.CompilerParams(vmem_limit_bytes=24 * 2**20),
        cost_estimate=cost(3),
    )(*given)


def key_value_back(d_kv, key_raw, value_raw, heads, cos_tab, sin_tab):
    key_gain = heads[QUERY_HEADS:]
    quarter = key_raw.shape[0]
    d_key, dg_key = norm_back(key_raw, key_gain, turn_back(d_kv[:quarter], cos_tab, sin_tab))
    d_value, _ = norm_back(value_raw, 1.0, d_kv[quarter:])
    return d_key, d_value, dg_key


def shard_total(query_parts, kv_parts, flat_parts, items, ident):
    data = lax.axis_size("dp")
    bundle = Bundle(items)
    number = bundle.number

    def kernel(q_ref, kv_ref, f_ref, *refs):
        x_refs, refs = refs[:number], refs[number:]
        oq_ref, okv_ref, of_ref = refs[:3]
        o_refs, refs = refs[3 : 3 + number], refs[3 + number :]
        q_buf, kv_buf, f_buf = refs[:3]
        sems = refs[3:11]
        bundle.bind(x_refs, o_refs, refs[11:])
        column, at = lax.axis_index("col"), lax.axis_index("dp")
        bundle.greet(True, True)
        bundle.start()
        mine = lax.rem(at, 2) == column

        def copies(k):
            target = lax.rem(at + k, data)
            device = {"dp": target}
            return (
                push(q_ref.at[target], q_buf.at[k], sems[0].at[k], sems[1].at[k], device),
                push(kv_ref.at[target // 2], kv_buf.at[k], sems[2].at[k], sems[3].at[k], device),
                push(f_ref.at[target], f_buf.at[k], sems[4].at[k], sems[5].at[k], device),
                lax.rem(target, 2) == column,
            )

        for k in range(1, data):
            query_copy, kv_copy, flat_copy, there = copies(k)
            query_copy.start()
            flat_copy.start()

            @pl.when(there)
            def _():
                kv_copy.start()

        for k in range(1, data):
            query_copy, kv_copy, flat_copy, there = copies(k)
            query_copy.wait()
            flat_copy.wait()

            @pl.when(there)
            def _():
                kv_copy.wait_send()

            @pl.when(mine)
            def _():
                kv_copy.wait_recv()

        def added(target, own, buf, chunk):
            @pl.loop(0, target.shape[0] // chunk)
            def _(step):
                rows = pl.ds(pl.multiple_of(step * chunk, chunk), chunk)
                total = own[rows].astype(FULL)
                for k in range(1, data):
                    total = total + buf[k, rows].astype(FULL)
                target[rows] = total

        share = push(okv_ref, okv_ref, sems[6], sems[7], {"col": 1 - column})

        @pl.when(mine)
        def _():
            added(okv_ref, kv_ref.at[at // 2], kv_buf, 128)
            share.start()

        added(oq_ref, q_ref.at[at], q_buf, 128)
        added(of_ref, f_ref.at[at], f_buf, 64)

        @pl.when(mine)
        def _():
            share.wait_send()

        @pl.when(jnp.logical_not(mine))
        def _():
            share.wait_recv()

        for k in range(1, bundle.sizes[0]):
            bundle.step(k)
        bundle.finish()

    vmem = pl.BlockSpec(memory_space=pltpu.VMEM)
    dma = pltpu.SemaphoreType.DMA
    shapes = [query_parts.shape[1:], kv_parts.shape[1:], flat_parts.shape[1:]]
    return pl.pallas_call(
        kernel,
        out_shape=[jax.ShapeDtypeStruct(shape, FULL) for shape in shapes] + bundle.shapes,
        in_specs=[vmem] * 3 + bundle.specs,
        out_specs=[vmem] * 3 + bundle.specs,
        scratch_shapes=[pltpu.VMEM((data,) + shape, LOW) for shape in shapes]
        + [dma((data,))] * 6
        + [dma, dma]
        + bundle.scratch,
        compiler_params=params(ident),
        cost_estimate=cost(40),
    )(query_parts, kv_parts, flat_parts, *bundle.sources)


CHUNKS = 4


class Flow:
    def __init__(self, x_ref, blocks, own, core_out, core_in, left_in, right_in, sems):
        self.x_ref, self.blocks, self.own = x_ref, blocks, own
        self.core_out, self.core_in = core_out, core_in
        self.left_in, self.right_in = left_in, right_in
        self.sems = sems
        self.me, self.column = lax.axis_index("row"), lax.axis_index("col")
        self.count = blocks.shape[0]

    @staticmethod
    def scratch(count, share, width):
        dma = pltpu.SemaphoreType.DMA
        slots = (count, share, width)
        return [
            pltpu.VMEM((count, 2, share, width), LOW),
            pltpu.VMEM(slots, FULL),
            pltpu.VMEM(slots, LOW),
            pltpu.VMEM(slots, LOW),
            pltpu.VMEM(slots, LOW),
            pltpu.VMEM(slots, LOW),
        ], [dma((count,))] * 7 + [dma((count * CHUNKS,))] * 2 + [dma((count,))] + [
            dma((count * CHUNKS,))
        ] * 2 + [dma]

    def left(self):
        return {"row": self.me - 1}

    def right(self):
        return {"row": self.me + 1}

    def beside(self):
        return {"col": 1 - self.column}

    def to_left(self, source, k, origin):
        return push(origin, self.blocks.at[source, 0], self.sems[0].at[k], self.sems[4].at[k], self.left())

    def to_right(self, source, k, origin):
        return push(origin, self.blocks.at[source, 0], self.sems[1].at[k], self.sems[3].at[k], self.right())

    def to_core(self, source, origin):
        return push(origin, self.blocks.at[source, 1], self.sems[2].at[source], self.sems[5].at[source], self.beside())

    def back_core(self, q):
        return push(self.core_out.at[q], self.core_in.at[q], self.sems[6].at[q], self.sems[9].at[q], self.beside())

    def part(self, ref, q, j):
        size = ref.shape[1] // CHUNKS
        return ref.at[q, pl.ds(pl.multiple_of(j * size, size), size)]

    def back_left(self, q, j):
        at = q * CHUNKS + j
        return push(
            self.part(self.core_out, q, j),
            self.part(self.left_in, q, j),
            self.sems[7].at[at],
            self.sems[10].at[at],
            self.left(),
        )

    def back_right(self, q, j):
        at = q * CHUNKS + j
        return push(
            self.part(self.core_out, q, j),
            self.part(self.right_in, q, j),
            self.sems[8].at[at],
            self.sems[11].at[at],
            self.right(),
        )

    def from_right(self, q, j):
        at, there = q * CHUNKS + j, self.part(self.left_in, q, j)
        return push(there, there, self.sems[7].at[at], self.sems[10].at[at], self.right())

    def from_left(self, q, j):
        at, there = q * CHUNKS + j, self.part(self.right_in, q, j)
        return push(there, there, self.sems[8].at[at], self.sems[11].at[at], self.left())

    def mine(self):
        return pltpu.make_async_copy(self.x_ref, self.blocks.at[self.me, 0], self.sems[12])

    def start(self):
        me, count = self.me, self.count

        @pl.when(me > 0)
        def _():
            self.to_left(me, 0, self.x_ref).start()

        @pl.when(me < count - 1)
        def _():
            self.to_right(me, 0, self.x_ref).start()

        self.to_core(me, self.x_ref).start()
        self.mine().start()

    def arrive(self, k):
        me, count = self.me, self.count

        @pl.when(k == 0)
        def _():
            self.mine().wait()
            self.to_core(me, self.x_ref).wait()

        @pl.when((k > 0) & (me - k >= 0))
        def _():
            source = me - k
            block = self.blocks.at[source, 0]
            push(block, block, self.sems[1].at[k], self.sems[3].at[k - 1], self.left()).wait_recv()

            @pl.when(me < count - 1)
            def _():
                self.to_right(source, k, block).start()

            self.to_core(source, block).start()

        @pl.when((k > 0) & (me + k < count))
        def _():
            source = me + k
            block = self.blocks.at[source, 0]
            push(block, block, self.sems[0].at[k], self.sems[4].at[k - 1], self.right()).wait_recv()

            @pl.when(me > 0)
            def _():
                self.to_left(source, k, block).start()

            self.to_core(source, block).start()

        @pl.when((k > 0) & (me - k >= 0))
        def _():
            self.to_core(me - k, self.x_ref).wait()

        @pl.when((k > 0) & (me + k < count))
        def _():
            self.to_core(me + k, self.x_ref).wait()

    def reach(self):
        return jnp.maximum(self.me, self.count - 1 - self.me)

    def visit(self, body, bundle, after=None):
        me, count = self.me, self.count

        @pl.loop(0, count)
        def _(k):
            self.arrive(k)

            @pl.when(k == count - 2)
            def _():
                bundle.start()

            @pl.when(k == count - 1)
            def _():
                bundle.step(1)

            @pl.loop(0, 2)
            def _(side):
                source = jnp.where(side == 0, me - k, me + k)

                @pl.when((source >= 0) & (source < count) & ((side == 0) | (k > 0)))
                def _():
                    body(source)
                    self.back_core(source).start()

            if after:
                after(k, k - self.reach() - 1)
            self.give_back(k)

    def added(self, target, terms):
        total = terms[0][...]
        for term in terms[1:]:
            total = total + term[...].astype(FULL)
        target[...] = total.astype(target.dtype)

    def give_back(self, t):
        me, count = self.me, self.count
        q_left = 2 * (count - 1) - me - t
        q_right = t - me

        def leftward():
            q = q_left
            self.back_core(q).wait()

            @pl.loop(0, CHUNKS)
            def _(j):
                base = [self.part(self.own, q, j), self.part(self.core_in, q, j)]
                target = self.part(self.core_out, q, j)

                @pl.when(me < count - 1)
                def _():
                    self.from_right(q, j).wait_recv()
                    self.added(target, base + [self.part(self.left_in, q, j)])

                @pl.when(me == count - 1)
                def _():
                    self.added(target, base)

                self.back_left(q, j).start()

        def rightward():
            q = q_right
            self.back_core(q).wait()

            @pl.loop(0, CHUNKS)
            def _(j):
                base = [self.part(self.own, q, j), self.part(self.core_in, q, j)]
                target = self.part(self.core_out, q, j)

                @pl.when(me > 0)
                def _():
                    self.from_left(q, j).wait_recv()
                    self.added(target, base + [self.part(self.right_in, q, j)])

                @pl.when(me == 0)
                def _():
                    self.added(target, base)

                self.back_right(q, j).start()

        pl.when((q_left >= 0) & (q_left < me))(leftward)
        pl.when((q_right > me) & (q_right < count))(rightward)

    def finish(self, o_ref):
        me, count = self.me, self.count
        self.back_core(me).wait()

        @pl.loop(0, CHUNKS)
        def _(j):
            size = o_ref.shape[0] // CHUNKS
            target = o_ref.at[pl.ds(pl.multiple_of(j * size, size), size)]
            base = [self.part(self.own, me, j), self.part(self.core_in, me, j)]

            @pl.when(me < count - 1)
            def _():
                self.from_right(me, j).wait_recv()

            @pl.when(me > 0)
            def _():
                self.from_left(me, j).wait_recv()

            @pl.when(me == 0)
            def _():
                self.added(target, base + [self.part(self.left_in, me, j)])

            @pl.when(me == count - 1)
            def _():
                self.added(target, base + [self.part(self.right_in, me, j)])

            @pl.when((me > 0) & (me < count - 1))
            def _():
                self.added(
                    target, base + [self.part(self.left_in, me, j), self.part(self.right_in, me, j)]
                )

        @pl.when(me > 0)
        def _():
            self.to_left(me, 0, self.x_ref).wait_send()

        @pl.when(me < count - 1)
        def _():
            self.to_right(me, 0, self.x_ref).wait_send()

        @pl.loop(1, count)
        def _(k):
            @pl.when((me - k >= 0) & (me < count - 1))
            def _():
                self.to_right(me - k, k, self.x_ref).wait_send()

            @pl.when((me + k < count) & (me > 0))
            def _():
                self.to_left(me + k, k, self.x_ref).wait_send()

        @pl.loop(0, count * CHUNKS)
        def _(at):
            q, j = at // CHUNKS, lax.rem(at, CHUNKS)

            @pl.when(q < me)
            def _():
                self.back_left(q, j).wait_send()

            @pl.when(q > me)
            def _():
                self.back_right(q, j).wait_send()


GELU_ONE = 0.7978845608028654
GELU_TWO = 0.044715


def gelu_of(values_in):
    inner = GELU_ONE * (values_in + GELU_TWO * values_in * values_in * values_in)
    bend = jnp.tanh(inner)
    half = 0.5 * (1.0 + bend)
    slope = half + 0.5 * values_in * (1.0 - bend * bend) * GELU_ONE * (
        1.0 + 3.0 * GELU_TWO * values_in * values_in
    )
    return values_in * half, slope


def ffn_forward(block, gateup, downs, items, ident):
    count = lax.axis_size("row")
    share, width = block.shape
    groups, _, _, part = gateup.shape
    hidden = groups * part
    down_shape = (groups, hidden, downs[0].shape[2])
    out_cols = down_shape[2] // count
    rows = 2 * share
    bundle = Bundle(items)
    number = bundle.number

    def kernel(x_ref, gw_hbm, dw_one, dw_two, *refs):
        x_refs, refs = refs[:number], refs[number:]
        o_ref, xt_hbm, at_hbm, g_hbm, u_hbm = refs[:5]
        o_refs, scratch = refs[5 : 5 + number], refs[5 + number :]
        flow = Flow(x_ref, *scratch[:6], scratch[6:19])
        gw, dw, xt, at, act, gate, up = scratch[19:26]
        gw_sem, dw_sem, xt_sem, at_sem, g_sem, u_sem = scratch[26:32]
        bundle.bind(x_refs, o_refs, scratch[32:])
        gw_load = pltpu.make_async_copy(gw_hbm, gw, gw_sem)
        dw_loads = [
            pltpu.make_async_copy(source, dw.at[:, pl.ds(k * hidden // 2, hidden // 2)], dw_sem.at[k])
            for k, source in enumerate((dw_one, dw_two))
        ]
        gw_load.start()
        for dw_load in dw_loads:
            dw_load.start()
        bundle.greet(False, True)
        flow.start()
        gw_load.wait()
        for dw_load in dw_loads:
            dw_load.wait()

        def stores(source):
            return (
                pltpu.make_async_copy(gate.at[source], g_hbm.at[source], g_sem.at[source]),
                pltpu.make_async_copy(up.at[source], u_hbm.at[source], u_sem.at[source]),
            )

        def body(source):
            x = flow.blocks[source].reshape(rows, width)

            @pl.loop(0, groups)
            def _(d):
                columns = pl.ds(pl.multiple_of(d * part, part), part)
                g = flat_dot(x, gw[d, 0])
                u = flat_dot(x, gw[d, 1])
                gate[source, :, columns] = g
                up[source, :, columns] = u
                act[source, :, columns] = (gelu_of(g)[0] * u).astype(LOW)

            for copy in stores(source):
                copy.start()
            for d in range(groups):
                out = flat_dot(act[source], dw[d])
                for s in range(count):
                    columns = slice((s * groups + d) * out_cols, (s * groups + d + 1) * out_cols)
                    piece = out[:, s * out_cols : (s + 1) * out_cols]
                    flow.own[source, :, columns] = piece[:share]
                    flow.core_out[source, :, columns] = piece[share:].astype(LOW)

        flow.visit(body, bundle)

        @pl.loop(0, count)
        def _(source):
            here = pl.ds(pl.multiple_of(source * rows, rows), rows)
            xt[:, here] = flow.blocks[source].reshape(rows, width).T
            at[:, here] = act[source].T

        xt_store = pltpu.make_async_copy(xt, xt_hbm, xt_sem)
        at_store = pltpu.make_async_copy(at, at_hbm, at_sem)
        xt_store.start()
        at_store.start()

        @pl.loop(count, 2 * count - 2)
        def _(t):
            flow.give_back(t)

        for k in range(2, count):
            bundle.step(k)
        flow.finish(o_ref)
        bundle.finish()
        xt_store.wait()
        at_store.wait()

        @pl.loop(0, count)
        def _(source):
            for copy in stores(source):
                copy.wait()

    dma = pltpu.SemaphoreType.DMA
    buffers, sems = Flow.scratch(count, share, width)
    vmem, anywhere = pl.BlockSpec(memory_space=pltpu.VMEM), pl.BlockSpec(memory_space=pl.ANY)
    tokens = count * rows
    return pl.pallas_call(
        kernel,
        out_shape=[
            jax.ShapeDtypeStruct((share, width), FULL),
            jax.ShapeDtypeStruct((width, tokens), LOW),
            jax.ShapeDtypeStruct((hidden, tokens), LOW),
            jax.ShapeDtypeStruct((count, rows, hidden), FULL),
            jax.ShapeDtypeStruct((count, rows, hidden), FULL),
        ]
        + bundle.shapes,
        in_specs=[vmem] + [anywhere] * 3 + bundle.specs,
        out_specs=[vmem] + [anywhere] * 4 + bundle.specs,
        scratch_shapes=buffers
        + sems
        + [
            pltpu.VMEM(gateup.shape, LOW),
            pltpu.VMEM(down_shape, LOW),
            pltpu.VMEM((width, tokens), LOW),
            pltpu.VMEM((hidden, tokens), LOW),
            pltpu.VMEM((count, rows, hidden), LOW),
            pltpu.VMEM((count, rows, hidden), FULL),
            pltpu.VMEM((count, rows, hidden), FULL),
        ]
        + [dma, dma((2,)), dma, dma, dma((count,)), dma((count,))]
        + bundle.scratch,
        compiler_params=params(ident, 60),
        cost_estimate=cost(80),
    )(block, gateup, *downs, *bundle.sources)


def ffn_backward(block, gateup, downs, xt, at, gate, up, items, ident):
    count = lax.axis_size("row")
    share, width = block.shape
    groups, _, _, part = gateup.shape
    hidden = groups * part
    down_shape = (groups, hidden, downs[0].shape[2])
    out_cols = down_shape[2] // count
    rows = 2 * share
    tokens = count * rows
    bundle = Bundle(items)
    number = bundle.number

    def kernel(x_ref, gw_hbm, dw_one, dw_two, xt_hbm, at_hbm, g_hbm, u_hbm, *refs):
        x_refs, refs = refs[:number], refs[number:]
        o_ref, dgu_hbm, ddn_hbm = refs[:3]
        o_refs, scratch = refs[3 : 3 + number], refs[3 + number :]
        flow = Flow(x_ref, *scratch[:6], scratch[6:19])
        gw, dw, xt_own, at_own, gate_own, up_own, d_gate, d_up, total, stage, stage_down = scratch[19:30]
        load_sems, g_sem, u_sem, out_sem, down_sem = scratch[30:35]
        bundle.bind(x_refs, o_refs, scratch[35:])
        loads = [
            pltpu.make_async_copy(source, target, load_sems.at[k])
            for k, (source, target) in enumerate(
                [
                    (dw_one, dw.at[:, pl.ds(0, hidden // 2)]),
                    (dw_two, dw.at[:, pl.ds(hidden // 2, hidden // 2)]),
                    (gw_hbm, gw),
                    (xt_hbm, xt_own),
                    (at_hbm, at_own),
                ]
            )
        ]

        def fetches(source):
            return (
                pltpu.make_async_copy(g_hbm.at[source], gate_own.at[source], g_sem.at[source]),
                pltpu.make_async_copy(u_hbm.at[source], up_own.at[source], u_sem.at[source]),
            )

        for load in loads[:3]:
            load.start()

        @pl.loop(0, count)
        def _(source):
            for copy in fetches(source):
                copy.start()

        for load in loads[3:]:
            load.start()
        bundle.greet(False, True)
        flow.start()
        for load in loads[:3]:
            load.wait()

        def columns_of(s, d):
            return pl.ds(pl.multiple_of((s * groups + d) * out_cols, out_cols), out_cols)

        def body(source):
            for copy in fetches(source):
                copy.wait()
            grad = flow.blocks[source].reshape(rows, width)
            d_act = None
            for d in range(groups):
                cut = jnp.concatenate(
                    [
                        grad[:, (s * groups + d) * out_cols : (s * groups + d + 1) * out_cols]
                        for s in range(count)
                    ],
                    axis=1,
                )
                term = against(cut, dw[d])
                d_act = term if d_act is None else d_act + term
            total[:, :hidden] = d_act

            @pl.loop(0, groups)
            def _(d):
                columns = pl.ds(pl.multiple_of(d * part, part), part)
                grad_act = total[:, columns]
                curve, slope = gelu_of(gate_own[source, :, columns])
                d_gate[source, :, columns] = (grad_act * up_own[source, :, columns] * slope).astype(LOW)
                d_up[source, :, columns] = (grad_act * curve).astype(LOW)

            total[...] = jnp.zeros(total.shape, FULL)

            @pl.loop(0, groups)
            def _(d):
                columns = pl.ds(pl.multiple_of(d * part, part), part)
                total[...] += against(d_gate[source, :, columns], gw[d, 0]) + against(
                    d_up[source, :, columns], gw[d, 1]
                )

            flow.own[source] = total[:share]
            flow.core_out[source] = total[share:].astype(LOW)

        def gateup_store(d, which):
            return pltpu.make_async_copy(stage.at[which], dgu_hbm.at[d, which], out_sem.at[which])

        def down_store(d):
            return pltpu.make_async_copy(stage_down, ddn_hbm.at[d], down_sem)

        def weights(d):
            columns = pl.ds(pl.multiple_of(d * part, part), part)
            for which, grads in ((0, d_gate), (1, d_up)):

                @pl.when(d > 0)
                def _():
                    gateup_store(d - 1, which).wait()

                right = grads[:, :, columns].reshape(tokens, part)

                @pl.loop(0, width // 512)
                def _(k):
                    high = pl.ds(pl.multiple_of(k * 512, 512), 512)
                    stage[which, high] = flat_dot(xt_own[high], right).astype(LOW)

                gateup_store(d, which).start()

            @pl.when(d > 0)
            def _():
                down_store(d - 1).wait()

            right = jnp.concatenate(
                [flow.blocks[:, :, :, columns_of(s, d)].reshape(tokens, out_cols) for s in range(count)],
                axis=1,
            )

            @pl.loop(0, hidden // 256)
            def _(k):
                high = pl.ds(pl.multiple_of(k * 256, 256), 256)
                stage_down[high] = flat_dot(at_own[high], right).astype(LOW)

            down_store(d).start()

        def early(k, d):
            @pl.when(k == count - 1)
            def _():
                loads[3].wait()
                loads[4].wait()

            @pl.when(d >= 0)
            def _():
                weights(d)

        flow.visit(body, bundle, early)
        done = count - 1 - flow.reach()

        @pl.loop(0, count - 2)
        def _(t):
            weights(done + t)
            flow.give_back(count + t)

        for k in range(2, count):
            bundle.step(k)

        @pl.loop(count - 2, groups)
        def _(d):
            @pl.when(d + done < groups)
            def _():
                weights(d + done)

        for which in range(2):
            gateup_store(groups - 1, which).wait()
        down_store(groups - 1).wait()
        flow.finish(o_ref)
        bundle.finish()

    dma = pltpu.SemaphoreType.DMA
    buffers, sems = Flow.scratch(count, share, width)
    vmem, anywhere = pl.BlockSpec(memory_space=pltpu.VMEM), pl.BlockSpec(memory_space=pl.ANY)
    return pl.pallas_call(
        kernel,
        out_shape=[
            jax.ShapeDtypeStruct((share, width), FULL),
            jax.ShapeDtypeStruct(gateup.shape, LOW),
            jax.ShapeDtypeStruct(down_shape, LOW),
        ]
        + bundle.shapes,
        in_specs=[vmem] + [anywhere] * 7 + bundle.specs,
        out_specs=[vmem, anywhere, anywhere] + bundle.specs,
        scratch_shapes=buffers
        + sems
        + [
            pltpu.VMEM(gateup.shape, LOW),
            pltpu.VMEM(down_shape, LOW),
            pltpu.VMEM((width, tokens), LOW),
            pltpu.VMEM((hidden, tokens), LOW),
            pltpu.VMEM((count, rows, hidden), FULL),
            pltpu.VMEM((count, rows, hidden), FULL),
            pltpu.VMEM((count, rows, hidden), LOW),
            pltpu.VMEM((count, rows, hidden), LOW),
            pltpu.VMEM((rows, width), FULL),
            pltpu.VMEM((2, width, part), LOW),
            pltpu.VMEM((hidden, count * out_cols), LOW),
        ]
        + [dma((5,)), dma((count,)), dma((count,)), dma((2,)), dma]
        + bundle.scratch,
        compiler_params=params(ident, 62),
        cost_estimate=cost(90),
    )(block, gateup, *downs, xt, at, gate, up, *bundle.sources)


def last_sums(small, ident):
    axes = ("col", "row", "dp")
    sizes = [lax.axis_size(axis) for axis in axes]
    high = small.shape[0]

    def kernel(x_ref, o_ref, *refs):
        slots, sends, recvs = (refs[k::3] for k in range(3))
        spots = [lax.axis_index(axis) for axis in axes]
        barrier = pltpu.get_barrier_semaphore()
        for axis, size, me in zip(axes, sizes, spots):
            for k in range(1, size):
                pl.semaphore_signal(
                    barrier, inc=1, device_id={axis: lax.rem(me + k, size)}, device_id_type=MESH
                )
        pl.semaphore_wait(barrier, sum(sizes) - len(sizes))
        for at, (axis, size, me) in enumerate(zip(axes, sizes, spots)):
            buf, send, recv = slots[at], sends[at], recvs[at]
            buf[me] = x_ref[...] if at == 0 else o_ref[...]
            for k in range(1, size):
                push(buf.at[me], buf.at[me], send.at[k], recv.at[k], {axis: lax.rem(me + k, size)}).start()
            for k in range(1, size):
                origin = lax.rem(me + size - k, size)
                push(buf.at[origin], buf.at[origin], send.at[k], recv.at[k], {axis: origin}).wait()
            total = buf[0]
            top = buf[0, high - 8 :]
            for k in range(1, size):
                total = total + buf[k]
                top = jnp.maximum(top, buf[k, high - 8 :])
            o_ref[...] = total
            o_ref[high - 8 :] = top

    dma = pltpu.SemaphoreType.DMA
    vmem = pl.BlockSpec(memory_space=pltpu.VMEM)
    scratch = []
    for size in sizes:
        scratch += [pltpu.VMEM((size,) + small.shape, FULL), dma((size,)), dma((size,))]
    return pl.pallas_call(
        kernel,
        out_shape=jax.ShapeDtypeStruct(small.shape, FULL),
        in_specs=[vmem],
        out_specs=vmem,
        scratch_shapes=scratch,
        compiler_params=params(ident, 16),
        cost_estimate=cost(14),
    )(small)


def adam_all(small, sum_rows, groups):
    high = small.shape[0]
    number = len(groups)
    arrays = [array for group in groups for array in group[:4]]
    cuts = []
    for group in range(number):
        rows, cols = arrays[4 * group].shape
        pieces = max(1, rows * cols // 262144)
        cuts += [(group, piece, rows // pieces) for piece in range(pieces)]

    def kernel(x_ref, *refs):
        sources, refs = refs[: 4 * number], refs[4 * number :]
        norm_ref, factor_ref = refs[:2]
        outs, refs = refs[2 : 2 + 3 * number], refs[2 + 3 * number :]
        held, load_sem, store_sem = refs[: 4 * number], refs[4 * number], refs[4 * number + 1]

        def rows_of(at):
            group, piece, rows = cuts[at]
            return pl.ds(piece * rows, rows) if rows < arrays[4 * group].shape[0] else slice(None)

        def load(at, k):
            here, array = rows_of(at), 4 * cuts[at][0] + k
            return pltpu.make_async_copy(
                sources[array].at[here], held[array].at[here], load_sem.at[at, k]
            )

        def store(at, k):
            here, group = rows_of(at), cuts[at][0]
            return pltpu.make_async_copy(
                held[4 * group + (1, 2, 0)[k]].at[here], outs[3 * group + k].at[here], store_sem.at[at, k]
            )

        for at in range(len(cuts)):
            for k in range(4):
                load(at, k).start()
        column, data_at = lax.axis_index("col"), lax.axis_index("dp")
        sums = x_ref[:sum_rows]
        squares = jnp.sum(jnp.sum(sums * sums, axis=1, keepdims=True), axis=0, keepdims=True)
        squares = squares + x_ref[sum_rows : sum_rows + 1, :1]
        norm = jnp.sqrt(squares)
        clip = CLIP / jnp.maximum(norm, CLIP)
        tops = x_ref[high - 1 :]
        lanes = lax.broadcasted_iota(jnp.int32, (1, 128), 1)
        group_size = QUERY_HEADS // KEY_VALUE_HEADS
        norm_ref[...] = norm
        factor_ref[...] = (LOGIT_CAP / jnp.maximum(tops, LOGIT_CAP))[:, :QUERY_HEADS]

        def factor(first, count):
            chosen = (lanes >= first) & (lanes < first + count)
            top = jnp.max(jnp.where(chosen, tops, NEGATIVE), axis=1, keepdims=True)
            return jnp.sqrt(LOGIT_CAP / jnp.maximum(top, LOGIT_CAP))

        factors = {
            "query": factor(column * lax.axis_size("dp") + data_at, 1),
            "keyval": jnp.where(
                data_at < KEY_VALUE_HEADS, factor(data_at * group_size, group_size), 1.0
            ),
        }
        for at, (group, piece, rows) in enumerate(cuts):
            rate, decay, kind = groups[group][4:]
            for k in range(4):
                load(at, k).wait()
            w_ref, m_ref, v_ref, g_ref = held[4 * group : 4 * group + 4]
            cols = w_ref.shape[1]
            step = rows if rows % 8 else min(rows, max(16, 32768 // max(cols, 128)))

            def stepped(here):
                new = adamw_step(
                    w_ref[here], m_ref[here], v_ref[here], g_ref[here].astype(FULL) * clip, rate, decay
                )
                m_ref[here], v_ref[here] = new[0], new[1]
                w_ref[here] = new[2] * factors[kind] if kind else new[2]

            if step == rows:
                stepped(rows_of(at))
            else:

                @pl.loop(0, rows // step)
                def _(k):
                    stepped(pl.ds(pl.multiple_of(piece * rows + k * step, step), step))

            for k in range(3):
                store(at, k).start()
        for at in range(len(cuts)):
            for k in range(3):
                store(at, k).wait()

    dma = pltpu.SemaphoreType.DMA
    vmem, anywhere = pl.BlockSpec(memory_space=pltpu.VMEM), pl.BlockSpec(memory_space=pl.ANY)
    outs = [jax.ShapeDtypeStruct(group[0].shape, FULL) for group in groups for _ in range(3)]
    return pl.pallas_call(
        kernel,
        out_shape=[
            jax.ShapeDtypeStruct((1, 1), FULL),
            jax.ShapeDtypeStruct((1, QUERY_HEADS), FULL),
        ]
        + outs,
        in_specs=[vmem] + [anywhere] * (4 * number),
        out_specs=[vmem] * 2 + [anywhere] * (3 * number),
        scratch_shapes=[pltpu.VMEM(array.shape, array.dtype) for array in arrays]
        + [dma((len(cuts), 4)), dma((len(cuts), 3))],
        compiler_params=pltpu.CompilerParams(vmem_limit_bytes=56 * 2**20),
        cost_estimate=cost(25),
    )(small, *arrays)


def allowed_block(at, high, width, spans):
    key_places = lax.broadcasted_iota(jnp.int32, (high, width), 1)
    query_places = at * high + lax.broadcasted_iota(jnp.int32, (high, width), 0)
    seen = key_places <= query_places
    for start in spans[1:]:
        both = (
            (key_places >= start)
            & (key_places < start + IMG)
            & (query_places >= start)
            & (query_places < start + IMG)
        )
        seen = seen | both
    return seen & (key_places < spans[0])


def softmax_block(block_rows, keys, allowed):
    scores = against(block_rows, keys)
    masked = jnp.where(allowed, scores, NEGATIVE)
    peak_row = jnp.max(masked, axis=-1, keepdims=True)
    raw_weights = jnp.where(allowed, jnp.exp(masked - peak_row), 0.0)
    return raw_weights / jnp.sum(raw_weights, axis=-1, keepdims=True), peak_row


def spans_of(lengths_ref, starts_ref):
    at = lax.axis_index("dp")
    return [lengths_ref[at]] + [starts_ref[at, piece] for piece in range(starts_ref.shape[1])]


def attention_forward_head(acts, gains, head_w, key_w, value_w, attend_w, heads, cos_tab, sin_tab, extras, lengths, starts, items, ident):
    tokens, width = acts.shape
    step = 256
    bundle = Bundle(items)
    number = bundle.number
    rows_n, cols_n = lax.axis_size("row"), lax.axis_size("col")
    half_tok, wide = tokens // cols_n, width // rows_n
    share, quarter = half_tok // rows_n, tokens // rows_n
    groups, out_cols = attend_w.shape[0], attend_w.shape[2] // rows_n

    def kernel(l_ref, s_ref, x_ref, gain_ref, qw_ref, kw_ref, vw_ref, aw_ref, heads_ref, cos_ref, sin_ref, e_ref, *refs):
        x_refs, refs = refs[:number], refs[number:]
        hidden_ref, acts_ref, share_ref, scale_ref, qr_ref, kr_ref, vr_ref = refs[:7]
        q_ref, k_ref, v_ref, o_ref, top_ref, es_ref, oc_ref, os_ref, p_ref = refs[7:16]
        o_refs, refs = refs[16 : 16 + number], refs[16 + number :]
        h_ref, sc_ref, key_ref, value_ref = refs[:4]
        bundle.bind(x_refs, o_refs, refs[4:])
        bundle.greet()
        bundle.start()
        me, column = lax.axis_index("row"), lax.axis_index("col")
        spans = spans_of(l_ref, s_ref)
        query_gain, key_gain = heads_ref[pl.ds(column * rows_n + me, 1)], heads_ref[QUERY_HEADS:]

        def project(at):
            here = pl.ds(pl.multiple_of(at * step, step), step)
            rows = x_ref[here].astype(FULL)
            scale = lax.rsqrt(jnp.mean(rows * rows, axis=-1, keepdims=True) + EPS)
            sc_ref[here] = jnp.broadcast_to(scale, (step, 128))
            h_ref[here] = (rows * scale * gain_ref[0:1]).astype(LOW)
            hidden = h_ref[here]
            cos_rows, sin_rows = cos_ref[here], sin_ref[here]
            query = flat_dot(hidden, qw_ref[...])
            qr_ref[here] = query
            q_ref[here] = turn(whole_norm(query, query_gain)[0], cos_rows, sin_rows).astype(LOW)
            key = flat_dot(hidden, kw_ref[...])
            key_ref[here] = key
            k_ref[here] = turn(whole_norm(key, key_gain)[0], cos_rows, sin_rows).astype(LOW)
            value = flat_dot(hidden, vw_ref[...])
            value_ref[here] = value
            v_ref[here] = whole_norm(value, 1.0)[0].astype(LOW)

        def attend(at):
            here = pl.ds(pl.multiple_of(at * step, step), step)
            allowed = allowed_block(at, step, tokens, spans)
            probs, peak_row = softmax_block(q_ref[here], k_ref[...], allowed)
            outputs = flat_dot(probs.astype(LOW), v_ref[...]).astype(LOW)
            o_ref[here] = outputs
            for d in range(groups):
                part = flat_dot(outputs, aw_ref[d])
                for s in range(rows_n):
                    cut = slice((s * groups + d) * out_cols, (s * groups + d + 1) * out_cols)
                    p_ref[here, cut] = part[:, s * out_cols : (s + 1) * out_cols].astype(LOW)
            top_ref[...] = jnp.maximum(top_ref[...], jnp.max(peak_row))

        top_ref[...] = jnp.full(top_ref.shape, NEGATIVE, FULL)
        blocks = tokens // step
        half = max(blocks // 2, 1)
        pl.loop(0, half)(project)
        bundle.step(1)
        pl.loop(half, blocks)(project)
        bundle.step(2)
        pl.loop(0, half)(attend)
        for k in range(3, bundle.sizes[0]):
            bundle.step(k)
        pl.loop(half, blocks)(attend)
        columns = pl.ds(pl.multiple_of(me * wide, wide), wide)

        @pl.loop(0, blocks)
        def _(at):
            here = pl.ds(pl.multiple_of(at * step, step), step)
            hidden_ref[here] = h_ref[here, columns]
            acts_ref[here] = x_ref[here, columns]

        mine = pl.ds(pl.multiple_of(column * half_tok + me * share, share), share)
        share_ref[...] = x_ref[mine]
        es_ref[...] = e_ref[mine]
        scale_ref[...] = sc_ref[pl.ds(pl.multiple_of(column * half_tok, half_tok), half_tok)]
        fourth = pl.ds(pl.multiple_of(me * quarter, quarter), quarter)
        kr_ref[...] = key_ref[fourth]
        vr_ref[...] = value_ref[fourth]
        oc_ref[...] = cos_ref[fourth]
        os_ref[...] = sin_ref[fourth]
        bundle.finish()

    vmem = pl.BlockSpec(memory_space=pltpu.VMEM)
    smem = pl.BlockSpec(memory_space=pltpu.SMEM)

    def low(*shape):
        return jax.ShapeDtypeStruct(shape, LOW)

    def full(*shape):
        return jax.ShapeDtypeStruct(shape, FULL)

    return pl.pallas_call(
        kernel,
        out_shape=[
            low(tokens, wide),
            low(tokens, wide),
            low(share, width),
            full(half_tok, 128),
            full(tokens, HEAD_WIDTH),
            full(quarter, HEAD_WIDTH),
            full(quarter, HEAD_WIDTH),
            low(tokens, HEAD_WIDTH),
            low(tokens, HEAD_WIDTH),
            low(tokens, HEAD_WIDTH),
            low(tokens, HEAD_WIDTH),
            full(8, 128),
            low(share, PLD),
            full(quarter, HEAD_WIDTH // 2),
            full(quarter, HEAD_WIDTH // 2),
            low(tokens, width),
        ]
        + bundle.shapes,
        in_specs=[smem, smem] + [vmem] * 10 + bundle.specs,
        out_specs=[vmem] * 16 + bundle.specs,
        scratch_shapes=[
            pltpu.VMEM((tokens, width), LOW),
            pltpu.VMEM((tokens, 128), FULL),
            pltpu.VMEM((tokens, HEAD_WIDTH), FULL),
            pltpu.VMEM((tokens, HEAD_WIDTH), FULL),
        ]
        + bundle.scratch,
        compiler_params=params(ident, 60),
        cost_estimate=cost(40),
    )(
        lengths, starts, acts, gains, head_w, key_w, value_w, attend_w, heads, cos_tab, sin_tab, extras, *bundle.sources
    )


def head_backward(queries, keys, values, attended, grads, attend_w, query_raw, heads, cos_tab, sin_tab, lengths, starts, items, ident):
    rows = queries.shape[0]
    step = min(256, rows)
    bundle = Bundle(items)
    number = bundle.number
    devices = lax.axis_size("row")
    quarter = rows // devices
    groups, out_cols = attend_w.shape[0], attend_w.shape[2] // devices

    def kernel(l_ref, s_ref, q_ref, k_ref, v_ref, a_ref, g_ref, w_ref, r_ref, heads_ref, cos_ref, sin_ref, *refs):
        x_refs, refs = refs[:number], refs[number:]
        dq_ref, kv_ref, dg_ref, dw_ref = refs[:4]
        o_refs, refs = refs[4 : 4 + number], refs[4 + number :]
        dk_ref, dv_ref = refs[:2]
        bundle.bind(x_refs, o_refs, refs[2:])
        bundle.greet()
        bundle.start()
        spans = spans_of(l_ref, s_ref)
        gain = heads_ref[pl.ds(lax.axis_index("col") * devices + lax.axis_index("row"), 1)]
        dk_ref[...] = jnp.zeros(dk_ref.shape, FULL)
        dv_ref[...] = jnp.zeros(dv_ref.shape, FULL)
        dg_ref[...] = jnp.zeros(dg_ref.shape, FULL)

        @pl.loop(0, rows // step)
        def _(at):
            here = pl.ds(pl.multiple_of(at * step, step), step)
            allowed = allowed_block(at, step, keys.shape[0], spans)
            block_rows, grad_rows = q_ref[here], None
            for d in range(groups):
                cut = jnp.concatenate(
                    [
                        g_ref[here, (s * groups + d) * out_cols : (s * groups + d + 1) * out_cols]
                        for s in range(devices)
                    ],
                    axis=1,
                )
                term = against(cut, w_ref[d])
                grad_rows = term if grad_rows is None else grad_rows + term
            grad_rows = grad_rows.astype(LOW)
            probs, _ = softmax_block(block_rows, k_ref[...], allowed)
            grad_probs = against(grad_rows, v_ref[...])
            delta_row = jnp.sum(probs * grad_probs, axis=-1, keepdims=True)
            grad_scores = (probs * (grad_probs - delta_row)).astype(LOW)
            d_query = turn_back(flat_dot(grad_scores, k_ref[...]), cos_ref[here], sin_ref[here])
            d_query, d_gain = norm_back(r_ref[here], gain, d_query)
            dq_ref[here] = d_query.astype(LOW)
            dg_ref[...] += d_gain
            dk_ref[...] += inner_rows(grad_scores, block_rows)
            dv_ref[...] += inner_rows(probs.astype(LOW), grad_rows)

        for device in range(devices):
            cut = slice(device * quarter, (device + 1) * quarter)
            kv_ref[device, :quarter] = dk_ref[cut].astype(LOW)
            kv_ref[device, quarter:] = dv_ref[cut].astype(LOW)
        for cut in range(0, grads.shape[1], 512):
            dw_ref[:, cut : cut + 512] = inner_rows(a_ref[...], g_ref[:, cut : cut + 512]).astype(LOW)
        for k in range(1, bundle.sizes[0]):
            bundle.step(k)
        bundle.finish()

    vmem = pl.BlockSpec(memory_space=pltpu.VMEM)
    return pl.pallas_call(
        kernel,
        out_shape=[
            jax.ShapeDtypeStruct(queries.shape, LOW),
            jax.ShapeDtypeStruct((devices, 2 * quarter, HEAD_WIDTH), LOW),
            jax.ShapeDtypeStruct((1, HEAD_WIDTH), FULL),
            jax.ShapeDtypeStruct((HEAD_WIDTH, grads.shape[1]), LOW),
        ]
        + bundle.shapes,
        in_specs=[pl.BlockSpec(memory_space=pltpu.SMEM)] * 2 + [vmem] * 10 + bundle.specs,
        out_specs=[vmem] * 4 + bundle.specs,
        scratch_shapes=[pltpu.VMEM(keys.shape, FULL)] * 2 + bundle.scratch,
        compiler_params=params(ident, 60),
        cost_estimate=cost(25),
    )(
        lengths, starts, queries, keys, values, attended, grads, attend_w, query_raw, heads, cos_tab, sin_tab, *bundle.sources
    )


def whole_norm(values_in, gain_vec):
    scale = lax.rsqrt(jnp.mean(values_in * values_in, axis=-1, keepdims=True) + EPS)
    return values_in * scale * gain_vec, scale


def whole_norm_backward(values_in, scale, gain_vec, grad_out):
    weighted = grad_out * gain_vec
    inner = jnp.mean(weighted * values_in, axis=-1, keepdims=True)
    return (
        scale * weighted - values_in * (scale * scale * scale) * inner,
        jnp.sum(grad_out * values_in * scale, axis=0),
    )


def turn(values_in, cos_tab, sin_tab):
    half_width = values_in.shape[-1] // 2
    one, two = values_in[:, :half_width], values_in[:, half_width:]
    return jnp.concatenate(
        [one * cos_tab - two * sin_tab, two * cos_tab + one * sin_tab], axis=1
    )


def turn_back(values_in, cos_tab, sin_tab):
    return turn(values_in, cos_tab, -sin_tab)


def line_device(
    activations,
    per_layer,
    cotangent,
    lengths,
    starts,
    w_query,
    m_query,
    v_query,
    key_value_weight,
    key_value_first_moment,
    key_value_second_moment,
    w_attend,
    m_attend,
    v_attend,
    w_gateup,
    m_gateup,
    v_gateup,
    w_down,
    m_down,
    v_down,
    w_left,
    m_left,
    v_left,
    w_right,
    m_right,
    v_right,
    w_pergate,
    m_pergate,
    v_pergate,
    w_perproj,
    m_perproj,
    v_perproj,
    w_gains,
    m_gains,
    v_gains,
    w_heads,
    m_heads,
    v_heads,
):
    rows_n = lax.axis_size("row")
    cols_n = lax.axis_size("col")
    data_n = lax.axis_size("dp")
    me = lax.axis_index("row")
    column = lax.axis_index("col")
    data_at = lax.axis_index("dp")
    half_tok, width_a = activations.shape
    tokens = half_tok * cols_n
    share = half_tok // rows_n
    quarter = tokens // rows_n
    width = width_a * rows_n

    ff_part = w_gateup.shape[2] // rows_n
    out_cols = w_down.shape[1]
    heads_here = data_n
    left_cols, right_rows = w_left.shape[1], w_right.shape[0]
    gate_cols, proj_rows = w_pergate.shape[1], w_perproj.shape[0]

    def columns_of(at, size):
        return pl.ds(pl.multiple_of(at * size, size), size)

    def across(source, by_rows):
        high, wide = source.shape
        if by_rows:
            return Swap(
                source,
                (data_n * high, wide),
                lambda ref, q: ref,
                lambda ref, at: ref.at[columns_of(at, high)],
                "dp",
            )
        return Swap(
            source,
            (high, data_n * wide),
            lambda ref, q: ref,
            lambda ref, at: ref.at[:, columns_of(at, wide)],
            "dp",
        )

    def along(source):
        high, wide = source.shape
        return Line(
            source,
            (cols_n * high, rows_n * wide),
            lambda ref, c, r: ref.at[columns_of(c, high), columns_of(r, wide)],
            True,
        )

    def lower(inputs, outputs):
        @pl.loop(0, inputs[0].shape[0] // 256)
        def _(at):
            rows = pl.ds(pl.multiple_of(at * 256, 256), 256)
            outputs[0][rows] = inputs[0][rows].astype(LOW)

    down_low, gateup_own, attend_own, qkv_w, left_t, right_w, pergate_t, perproj_w = transfers(
        [
            Swap(
                w_gateup.astype(LOW),
                (2, width, ff_part),
                lambda ref, q: ref.at[:, :, columns_of(q, ff_part)],
                lambda ref, at: ref.at[:, columns_of(at, width_a), :],
            ),
            Swap(
                w_attend.astype(LOW).reshape(rows_n, HEAD_WIDTH, out_cols),
                (HEAD_WIDTH, rows_n * out_cols),
                lambda ref, q: ref.at[q],
                lambda ref, at: ref.at[:, columns_of(at, out_cols)],
            ),
            Swap(
                jnp.concatenate([w_query, key_value_weight], axis=1).astype(LOW),
                (data_n, width_a, 2 * HEAD_WIDTH),
                lambda ref, q: ref,
                lambda ref, at: ref.at[at],
                "dp",
            ),
            across(w_left.T, True),
            across(w_right.astype(LOW), False),
            across(w_pergate.T.astype(LOW), True),
            across(w_perproj.astype(LOW), False),
        ],
        1,
        60,
        16,
        lower,
        (w_down,),
        [jax.ShapeDtypeStruct(w_down.shape, LOW)],
    )
    down_low = down_low.reshape(data_n, rows_n, ff_part, out_cols)

    def down_half(k):
        return Swap(
            down_low[k * data_n // 2 : (k + 1) * data_n // 2],
            (data_n // 2, ff_part, rows_n * out_cols),
            lambda ref, q: ref.at[:, q],
            lambda ref, at: ref.at[:, :, columns_of(at, out_cols)],
        )

    gateup_all = lax.all_gather(gateup_own, "dp")
    last = pl.ds(HEAD_WIDTH, HEAD_WIDTH)
    whole_acts, whole_key, whole_value, head_w, gains, extras, attend_all, down_one = transfers(
        [
            along(activations),
            Line(
                qkv_w,
                (width, HEAD_WIDTH),
                lambda ref, c, r: ref.at[columns_of(r, width_a)],
                False,
                lambda ref, c: ref.at[c, :, last],
            ),
            Line(
                qkv_w,
                (width, HEAD_WIDTH),
                lambda ref, c, r: ref.at[columns_of(r, width_a)],
                False,
                lambda ref, c: ref.at[KEY_VALUE_HEADS + c, :, last],
            ),
            Swap(
                qkv_w,
                (width, HEAD_WIDTH),
                lambda ref, q: ref.at[q, :, pl.ds(0, HEAD_WIDTH)],
                lambda ref, at: ref.at[columns_of(at, width_a)],
            ),
            Line(w_gains, (6, width), lambda ref, c, r: ref.at[:, columns_of(r, width_a)]),
            Line(
                per_layer,
                (tokens, PLD),
                lambda ref, c, r: ref.at[columns_of(r, quarter), columns_of(c, PLD // cols_n)],
                True,
            ),
            Swap(
                attend_own,
                (data_n, HEAD_WIDTH, rows_n * out_cols),
                lambda ref, q: ref,
                lambda ref, at: ref.at[at],
                "dp",
            ),
            down_half(0),
        ],
        2,
        105,
        60,
    )
    down_one, gateup_all = lax.optimization_barrier((down_one, gateup_all))
    down_one = lax.all_gather(down_one, "dp").reshape(data_n, data_n * ff_part // 2, -1)
    all_cos, all_sin = rope_tables(jnp.arange(tokens, dtype=jnp.int32), HEAD_WIDTH)
    (
        spread_h,
        own_acts,
        acts_share,
        scale_here,
        query_raw,
        key_raw,
        value_raw,
        queries,
        keys,
        values,
        attended,
        top,
        extras,
        own_cos,
        own_sin,
        projected,
        left_t,
        right_w,
        down_two,
        upstream,
    ) = attention_forward_head(
        whole_acts,
        gains,
        head_w,
        whole_key,
        whole_value,
        attend_all,
        w_heads,
        all_cos,
        all_sin,
        extras,
        lengths,
        starts,
        [
            along(left_t.astype(LOW)),
            along(right_w),
            down_half(1),
            Swap(
                cotangent,
                (share, width),
                lambda ref, q: ref.at[columns_of(q, share)],
                lambda ref, at: ref.at[:, columns_of(at, width_a)],
            ),
        ],
        3,
    )
    down_two, down_one = lax.optimization_barrier((down_two, down_one))
    down_two = lax.all_gather(down_two, "dp").reshape(data_n, data_n * ff_part // 2, -1)
    down_all = (down_one, down_two)
    projected, pergate_t, perproj_w = transfers(
        [
            Reduce(
                projected.reshape(cols_n, rows_n, share, width),
                (share, width),
                lambda ref, q: ref.at[q],
            ),
            along(pergate_t),
            along(perproj_w),
        ],
        5,
        45,
        60,
    )
    wide_low, wide_full = ((share, width), LOW), ((share, width), FULL)
    line = ((1, width), FULL)
    hidden_low, middle, right_raw, mixture, ffn_in = local(
        mix,
        [wide_low, ((share, RANK), LOW), wide_full, wide_full, wide_low],
        acts_share,
        projected,
        gains,
        left_t,
        right_w,
    )
    down_raw, spread_ft, act_t, gate_raw, up_raw = ffn_forward(
        ffn_in,
        gateup_all,
        down_all,
        [],
        6,
    )
    result, d_out, d_down, dw_perproj, dw_pergate, gain_four, gain_five = local(
        per_layer_both,
        [wide_low, wide_full, wide_low, ((PLD, width), LOW), ((PLD, width), LOW), line, line],
        mixture,
        down_raw,
        gains,
        extras,
        pergate_t,
        perproj_w,
        upstream,
    )
    d_ffn, dw_gateup, dw_down = ffn_backward(
        d_down, gateup_all, down_all, spread_ft, act_t, gate_raw, up_raw, [], 8
    )
    g_gateup = lax.psum_scatter(dw_gateup, "dp", scatter_dimension=0)
    d_proj, d_half, d_middle, small_parts, inner_share, gain_one, gain_two, gain_three = local(
        mix_back,
        [
            wide_low,
            wide_low,
            ((share, RANK), LOW),
            ((2 * (RANK + PLD), width), LOW),
            ((8, share), FULL),
            line,
            line,
            line,
        ],
        d_out,
        d_ffn,
        mixture,
        projected,
        right_raw,
        gains,
        acts_share,
        left_t,
        right_w,
        hidden_low,
        middle,
        dw_pergate,
        dw_perproj,
    )
    small_parts = small_parts.reshape(cols_n, -1, width)
    spread_p, small_parts = transfers(
        [
            Line(
                d_proj.astype(LOW),
                (cols_n, rows_n, share, width),
                lambda ref, c, r: ref.at[c, r],
                True,
            ),
            Reduce(
                small_parts,
                (small_parts.shape[1], width_a),
                lambda ref, q: ref.at[:, columns_of(q, width_a)],
            ),
        ],
        10,
        50,
        60,
    )
    spread_p = spread_p.reshape(tokens, width)
    d_q_raw, kv_parts, dg_query, dw_attend, middle_here, half_here, result = head_backward(
        queries,
        keys,
        values,
        attended,
        spread_p,
        attend_all,
        query_raw,
        w_heads,
        all_cos,
        all_sin,
        lengths,
        starts,
        [
            Line(
                d_middle, (half_tok, d_middle.shape[1]), lambda ref, c, r: ref.at[columns_of(r, share)]
            )
        ]
        + [
            Swap(
                source,
                (half_tok, width_a),
                lambda ref, q: ref.at[:, columns_of(q, width_a)],
                lambda ref, at: ref.at[columns_of(at, share)],
            )
            for source in (d_half, result)
        ],
        4,
    )

    d_q_raw, dw_down, g_gateup = lax.optimization_barrier((d_q_raw, dw_down, g_gateup))
    g_down = lax.psum_scatter(
        dw_down.reshape(data_n, data_n, ff_part, -1), "dp", scatter_dimension=0
    )

    d_q_all, d_kv = transfers(
        [
            Line(d_q_raw, (rows_n,) + d_q_raw.shape, lambda ref, c, r: ref.at[r]),
            Reduce(kv_parts, kv_parts.shape[1:], lambda ref, q: ref.at[q], False),
        ],
        11,
        45,
        60,
    )
    d_k_raw, d_v_raw, dg_key = local(
        key_value_back,
        [((quarter, HEAD_WIDTH), LOW), ((quarter, HEAD_WIDTH), LOW), ((1, HEAD_WIDTH), FULL)],
        d_kv,
        key_raw,
        value_raw,
        w_heads,
        own_cos,
        own_sin,
        mebibytes=16,
    )

    def query_work(inputs, outputs):
        h_ref, dq_ref, qw_ref, g_ref = inputs
        dw_ref, dh_ref, sq_ref = outputs
        hidden = h_ref[...]
        for k in range(heads_here):
            dw_ref[k] = inner_rows(hidden, dq_ref[k]).astype(LOW)
        total = against(dq_ref[0], qw_ref[0, :, :HEAD_WIDTH])
        for k in range(1, heads_here):
            total = total + against(dq_ref[k], qw_ref[k, :, :HEAD_WIDTH])
        dh_ref[...] = total
        sq_ref[...] = jnp.zeros(sq_ref.shape, FULL)
        for which in range(2):

            @pl.loop(0, width // 128)
            def _(at):
                rows = g_ref[which, pl.ds(pl.multiple_of(at * 128, 128), 128)].astype(FULL)
                sq_ref[...] += jnp.sum((rows * rows).reshape(16, 8, ff_part), axis=0)

    dw_query, d_hidden, gateup_squares, d_k_all, d_v_all, g_gateup, g_attend = transfers(
        [
            Line(
                d_raw, (tokens, HEAD_WIDTH), lambda ref, c, r: ref.at[columns_of(r, quarter)]
            )
            for d_raw in (d_k_raw, d_v_raw)
        ]
        + [
            Swap(
                g_gateup,
                w_gateup.shape,
                lambda ref, q: ref.at[:, columns_of(q, width_a), :],
                lambda ref, at: ref.at[:, :, columns_of(at, ff_part)],
            ),
            ShardSum(dw_attend, out_cols),
        ],
        12,
        65,
        40,
        query_work,
        (spread_h, d_q_all, qkv_w, g_gateup),
        [
            jax.ShapeDtypeStruct((heads_here, width_a, HEAD_WIDTH), LOW),
            jax.ShapeDtypeStruct((tokens, width_a), FULL),
            jax.ShapeDtypeStruct((8, ff_part), FULL),
        ],
    )
    extents = (
        (data_n * left_cols, True),
        (right_rows, False),
        (data_n * gate_cols, True),
        (proj_rows, False),
    )
    flat_rows = sum(rows for rows, _ in extents)
    dw_kv, d_hidden, inner, flat_parts = local(
        functools.partial(key_value_ends, extents=extents),
        [
            ((2 * width_a, HEAD_WIDTH), LOW),
            ((tokens, width_a), LOW),
            ((8, tokens), FULL),
            ((data_n * flat_rows, out_cols), LOW),
        ],
        spread_h,
        d_k_all,
        d_v_all,
        qkv_w,
        d_hidden,
        own_acts,
        w_gains,
        small_parts,
        mebibytes=24,
    )
    dw_kv = dw_kv.reshape(2, width_a, HEAD_WIDTH)
    down_sums = g_down
    g_query, g_keyval, flat_grads, inner, inner_share, d_hidden, g_attend, g_down = shard_total(
        dw_query,
        dw_kv,
        flat_parts.reshape(data_n, flat_rows, out_cols),
        [
            Line(inner, (cols_n, rows_n) + inner.shape, lambda ref, c, r: ref.at[c, r], True),
            Line(
                inner_share,
                (cols_n, rows_n) + inner_share.shape,
                lambda ref, c, r: ref.at[c, r],
                True,
            ),
            Pair(d_hidden.reshape(cols_n, half_tok, width_a)),
            Swap(
                g_attend,
                (rows_n, HEAD_WIDTH, out_cols),
                lambda ref, q: ref.at[:, columns_of(q, out_cols)],
                lambda ref, at: ref.at[at],
            ),
            Swap(
                g_down,
                (data_n, rows_n, ff_part, out_cols),
                lambda ref, q: ref.at[:, :, columns_of(q, out_cols)],
                lambda ref, at: ref.at[:, at],
            ),
        ],
        13,
    )
    g_down = g_down.reshape(w_down.shape)
    g_attend = g_attend.reshape(w_attend.shape)
    small_grads = []
    start = 0
    for w, by_rows in ((w_left, True), (w_right, False), (w_pergate, True), (w_perproj, False)):
        rows = w.size // out_cols
        cut = flat_grads[start : start + rows]
        start += rows
        if by_rows:
            high = rows // data_n
            cut = [cut[k * high : (k + 1) * high] for k in range(data_n)]
            cut = jnp.concatenate(cut, axis=1).T
        small_grads.append(cut)
    g_left, g_right, g_pergate, g_perproj = small_grads

    grad_input, small = input_ends(
        d_hidden,
        half_here,
        middle_here,
        left_t,
        activations,
        scale_here,
        w_gains,
        inner,
        inner_share,
        (g_query, g_keyval, flat_grads, g_attend, down_sums),
        gateup_squares,
        (gain_one, gain_two, gain_three, gain_four, gain_five),
        dg_query,
        dg_key,
        top,
    )
    gain_rows = 6 * width // 128
    head_rows = (QUERY_HEADS + 1) * HEAD_WIDTH // 128
    small = last_sums(small, 15)
    gain_sum = small[:gain_rows].reshape(6, width)
    head_sum = small[gain_rows : gain_rows + head_rows].reshape(QUERY_HEADS + 1, HEAD_WIDTH)
    g_gains = lax.dynamic_slice_in_dim(gain_sum, me * width_a, width_a, 1)
    matrix_rate = MODEL_WIDTH ** (-0.5)

    def flat_rows_of(array):
        return array.reshape(-1, array.shape[-1])

    def kept(array):
        return array

    def turned(array):
        return array.T

    groups = [
        tuple(change(array) for array in arrays) + rest
        for arrays, change, rest in (
            ((w_gateup, m_gateup, v_gateup, g_gateup), flat_rows_of, (matrix_rate, DECAY, None)),
            ((w_down, m_down, v_down, g_down), kept, (FF ** (-0.5), DECAY, None)),
            ((w_query, m_query, v_query, g_query), kept, (matrix_rate, DECAY, "query")),
            (
                (key_value_weight, key_value_first_moment, key_value_second_moment, g_keyval),
                kept,
                (matrix_rate, DECAY, "keyval"),
            ),
            (
                (w_attend, m_attend, v_attend, g_attend),
                kept,
                ((QUERY_HEADS * HEAD_WIDTH) ** (-0.5), DECAY, None),
            ),
            ((w_left, m_left, v_left, g_left), turned, (matrix_rate, DECAY, None)),
            ((w_right, m_right, v_right, g_right), kept, (RANK ** (-0.5), DECAY, None)),
            ((w_pergate, m_pergate, v_pergate, g_pergate), turned, (matrix_rate, DECAY, None)),
            ((w_perproj, m_perproj, v_perproj, g_perproj), kept, (PLD ** (-0.5), DECAY, None)),
            ((w_gains, m_gains, v_gains, g_gains), kept, (GAIN_RATE, 0.0, None)),
            ((w_heads, m_heads, v_heads, head_sum), kept, (HEAD_RATE, 0.0, None)),
        )
    ]
    grad_norm, scale_factors, *stepped = adam_all(small, gain_rows + head_rows, groups)
    grad_norm = grad_norm.reshape(())
    scale_factors = scale_factors.reshape(-1)
    gateup, down, query, keyval, attend, left, right, pergate, perproj, gain, head = (
        stepped[3 * k : 3 * k + 3] for k in range(11)
    )
    gateup = [array.reshape(w_gateup.shape) for array in gateup]
    left = [array.T for array in left]
    pergate = [array.T for array in pergate]
    return (
        result,
        grad_input,
        grad_norm,
        scale_factors,
        *query,
        *keyval,
        *attend,
        *gateup,
        *down,
        *left,
        *right,
        *pergate,
        *perproj,
        *gain,
        *head,
    )


def per_device(
    activations,
    per_layer,
    cotangent,
    lengths,
    starts,
    w_query,
    m_query,
    v_query,
    key_value_weight,
    key_value_first_moment,
    key_value_second_moment,
    w_attend,
    m_attend,
    v_attend,
    w_gateup,
    m_gateup,
    v_gateup,
    w_down,
    m_down,
    v_down,
    w_left,
    m_left,
    v_left,
    w_right,
    m_right,
    v_right,
    w_pergate,
    m_pergate,
    v_pergate,
    w_perproj,
    m_perproj,
    v_perproj,
    w_gains,
    m_gains,
    v_gains,
    w_heads,
    m_heads,
    v_heads,
):
    row_devs = lax.axis_size("row")
    col_devs = lax.axis_size("col")
    data_devs = lax.axis_size("dp")
    row_place = lax.axis_index("row")
    column_place = lax.axis_index("col")
    data_at = lax.axis_index("dp")
    bf16 = jnp.bfloat16
    single_float = jnp.float32
    query_b, keyval_b, attend_b, gateup_b, down_b, left_b, right_b, pergate_b, perproj_b = (
        lax.all_gather(w_query.astype(bf16), "dp", axis=1, tiled=True),
        lax.all_gather(key_value_weight.astype(bf16), "dp", axis=1, tiled=True),
        lax.all_gather(w_attend.astype(bf16), "dp", axis=1, tiled=True),
        lax.all_gather(w_gateup.astype(bf16), "dp", axis=2, tiled=True),
        lax.all_gather(w_down.astype(bf16), "dp", axis=1, tiled=True),
        lax.all_gather(w_left.astype(bf16), "dp", axis=1, tiled=True),
        lax.all_gather(w_right.astype(bf16), "dp", axis=1, tiled=True),
        lax.all_gather(w_pergate.astype(bf16), "dp", axis=1, tiled=True),
        lax.all_gather(w_perproj.astype(bf16), "dp", axis=1, tiled=True),
    )
    inputs = activations.astype(single_float)
    tok_a, width_a = inputs.shape
    grouped_rows = tok_a * col_devs
    token_batch = grouped_rows // row_devs
    q_cols = query_b.shape[1]
    l_cols = left_b.shape[1]
    kv_cols = keyval_b.shape[1]
    ff_here = gateup_b.shape[2]
    local_heads = q_cols // HEAD_WIDTH
    length = lax.dynamic_index_in_dim(lengths, data_at, 0, keepdims=False)
    piece_starts = lax.dynamic_index_in_dim(starts, data_at, 0, keepdims=False)
    own_places = row_place * token_batch + jnp.arange(token_batch, dtype=jnp.int32)
    all_places = jnp.arange(grouped_rows, dtype=jnp.int32)
    own_cos, own_sin = rope_tables(own_places, HEAD_WIDTH)
    query_gains = lax.dynamic_slice_in_dim(w_heads, column_place * local_heads, local_heads, 0)
    key_gain = w_heads[QUERY_HEADS]
    hidden, scale_in = norm_forward(inputs, w_gains[0])
    hidden_b = hidden.astype(bf16)
    spread_h = spread_col(hidden_b)
    type_one = reduce_row(flat_dot(spread_h, jnp.concatenate([query_b, left_b], axis=1)))
    key_raw_all = lax.psum(flat_dot(spread_h, keyval_b), "row")
    all_cos, all_sin = rope_tables(all_places, HEAD_WIDTH)
    key_value_whole = key_form(key_raw_all, key_gain, all_cos, all_sin).astype(bf16)
    key_raw = lax.dynamic_slice_in_dim(key_raw_all, row_place * token_batch, token_batch, 0)
    query_raw = type_one[:, :q_cols]
    middle_b = type_one[:, q_cols : q_cols + l_cols].astype(bf16)
    queries = query_form(query_raw, query_gains, own_cos, own_sin).astype(bf16)
    key_value_heads = (column_place * local_heads + jnp.arange(local_heads, dtype=jnp.int32)) // (
        QUERY_HEADS // KEY_VALUE_HEADS
    )
    every_key = key_value_whole[:, : KEY_VALUE_HEADS * HEAD_WIDTH].reshape(
        grouped_rows, KEY_VALUE_HEADS, HEAD_WIDTH
    )
    every_value = key_value_whole[:, KEY_VALUE_HEADS * HEAD_WIDTH :].reshape(
        grouped_rows, KEY_VALUE_HEADS, HEAD_WIDTH
    )
    key_sel = jnp.take(every_key, key_value_heads, axis=1)
    value_sel = jnp.take(every_value, key_value_heads, axis=1)
    attended, block_peaks, block_totals = attention_forward(
        queries, key_sel, value_sel, own_places, all_places, length, piece_starts
    )
    attended_b = attended.reshape(token_batch, q_cols).astype(bf16)
    joined_b = jnp.concatenate([attended_b, middle_b], axis=1)
    spread_j = spread_row(joined_b)
    type_two = reduce_col(
        jnp.concatenate(
            [flat_dot(spread_j[:, :q_cols], attend_b), flat_dot(spread_j[:, q_cols:], right_b)],
            axis=1,
        )
    )
    projected = type_two[:, :width_a]
    right_raw = type_two[:, width_a:]
    right_n, scale_r = norm_forward(right_raw, w_gains[1])
    laurel = hidden + right_n
    proj_n, scale_p = norm_forward(projected, w_gains[2])
    gated_sum = inputs + proj_n
    mixture = (gated_sum + laurel) * HALF_ROOT
    ffn_n, scale_f = norm_forward(mixture, w_gains[3])
    ffn_b = ffn_n.astype(bf16)
    spread_f = spread_col(ffn_b)
    gateup_pair = jnp.concatenate([gateup_b[0], gateup_b[1]], axis=1)
    gate_up = reduce_row(flat_dot(spread_f, gateup_pair))
    gate_raw = gate_up[:, :ff_here]
    up_raw = gate_up[:, ff_here:]
    act_b = (jax.nn.gelu(gate_raw, approximate=True) * up_raw).astype(bf16)
    spread_a = spread_row(act_b)
    down_raw = reduce_col(flat_dot(spread_a, down_b))
    down_n, scale_d = norm_forward(down_raw, w_gains[4])
    block_out = mixture + down_n
    out_b = block_out.astype(bf16)
    spread_o = spread_col(out_b)
    pgate = reduce_row(flat_dot(spread_o, pergate_b))
    extras = per_layer.astype(single_float)
    pact_b = (jax.nn.gelu(pgate, approximate=True) * extras).astype(bf16)
    spread_p = spread_row(pact_b)
    perproj = reduce_col(flat_dot(spread_p, perproj_b))
    perproj_n, scale_pp = norm_forward(perproj, w_gains[5])
    result = (block_out + perproj_n).astype(bf16)
    upstream = cotangent.astype(single_float)
    gain_grads = [None, None, None, None, None, None]
    d_perproj, gain_grads[5] = norm_backward(perproj, scale_pp, w_gains[5], upstream)
    grads_five = grads_col(d_perproj.astype(bf16))
    dw_perproj = inner_rows(spread_p, grads_five)
    d_pact = reduce_row(against(grads_five, perproj_b))
    gelu_out, pullback = jax.vjp(lambda v: jax.nn.gelu(v, approximate=True), pgate)
    (d_pgate,) = pullback(d_pact * extras)
    grads_four = grads_row(d_pgate.astype(bf16))
    dw_pergate = inner_rows(spread_o, grads_four)
    d_out = upstream + reduce_col(against(grads_four, pergate_b))
    d_down, gain_grads[4] = norm_backward(down_raw, scale_d, w_gains[4], d_out)
    grads_three = grads_col(d_down.astype(bf16))
    dw_down = inner_rows(spread_a, grads_three)
    d_act = reduce_row(against(grads_three, down_b))
    act_out, pullback = jax.vjp(lambda a, b: jax.nn.gelu(a, approximate=True) * b, gate_raw, up_raw)
    d_gate, d_up = pullback(d_act)
    local_two = jnp.concatenate([d_gate, d_up], axis=1).astype(bf16)
    grads_two = grads_row(local_two)
    dw_gateup = jnp.stack(
        [inner_rows(spread_f, grads_two[:, :ff_here]), inner_rows(spread_f, grads_two[:, ff_here:])]
    )
    d_ffn = reduce_col(
        against(grads_two[:, :ff_here], gateup_b[0]) + against(grads_two[:, ff_here:], gateup_b[1])
    )
    d_mix_norm, gain_grads[3] = norm_backward(mixture, scale_f, w_gains[3], d_ffn)
    d_half = (d_out + d_mix_norm) * HALF_ROOT
    d_proj, gain_grads[2] = norm_backward(projected, scale_p, w_gains[2], d_half)
    d_right, gain_grads[1] = norm_backward(right_raw, scale_r, w_gains[1], d_half)
    grads_one = grads_col(jnp.concatenate([d_proj, d_right], axis=1).astype(bf16))
    dw_attend = inner_rows(spread_j[:, :q_cols], grads_one[:, :width_a])
    dw_right = inner_rows(spread_j[:, q_cols:], grads_one[:, width_a:])
    d_joined = reduce_row(
        jnp.concatenate(
            [against(grads_one[:, :width_a], attend_b), against(grads_one[:, width_a:], right_b)],
            axis=1,
        )
    )
    d_attended = d_joined[:, :q_cols].astype(bf16).reshape(token_batch, local_heads, HEAD_WIDTH)
    d_middle = d_joined[:, q_cols:]
    d_queries, d_key_sel, d_value_sel = attention_backward(
        queries,
        key_sel,
        value_sel,
        d_attended,
        block_peaks,
        block_totals,
        own_places,
        all_places,
        length,
        piece_starts,
    )
    single_hot_mask = (
        key_value_heads[:, None] == jnp.arange(KEY_VALUE_HEADS, dtype=jnp.int32)[None, :]
    ).astype(single_float)
    key_gradient = jnp.sum(d_key_sel[:, :, None, :] * single_hot_mask[None, :, :, None], axis=1)
    value_gradient = jnp.sum(d_value_sel[:, :, None, :] * single_hot_mask[None, :, :, None], axis=1)
    key_gradient, value_gradient = lax.psum((key_gradient, value_gradient), ("row", "col"))
    local_key_gradient = lax.dynamic_slice_in_dim(
        key_gradient, row_place * token_batch, token_batch, 0
    ).reshape(token_batch, KEY_VALUE_HEADS * HEAD_WIDTH)
    local_value_gradient = lax.dynamic_slice_in_dim(
        value_gradient, row_place * token_batch, token_batch, 0
    ).reshape(token_batch, KEY_VALUE_HEADS * HEAD_WIDTH)
    query_out, pullback = jax.vjp(
        lambda r, g: query_form(r, g, own_cos, own_sin), query_raw, query_gains
    )
    d_query_raw, dg_query = pullback(d_queries)
    key_tile = jnp.broadcast_to(key_gain, (token_batch, 1, HEAD_WIDTH))
    key_out, pullback = jax.vjp(lambda r, g: key_form(r, g, own_cos, own_sin), key_raw, key_tile)
    d_key_raw, dg_key_rows = pullback(
        jnp.concatenate([local_key_gradient, local_value_gradient], axis=1)
    )
    slice_rows = token_batch // col_devs
    dg_key = jnp.sum(
        lax.dynamic_slice_in_dim(dg_key_rows, column_place * slice_rows, slice_rows, 0), axis=(0, 1)
    )
    grads_zero = grads_row(jnp.concatenate([d_query_raw, d_middle, d_key_raw], axis=1).astype(bf16))
    dw_query = inner_rows(spread_h, grads_zero[:, :q_cols])
    dw_left = inner_rows(spread_h, grads_zero[:, q_cols : q_cols + l_cols])
    key_grad_rows = grads_zero[:, q_cols + l_cols :]
    dw_keyval = inner_rows(spread_h, key_grad_rows)
    slab_width = kv_cols // col_devs
    d_hidden = reduce_col(
        against(grads_zero[:, :q_cols], query_b)
        + against(grads_zero[:, q_cols : q_cols + l_cols], left_b)
        + against(
            lax.dynamic_slice_in_dim(key_grad_rows, column_place * slab_width, slab_width, 1),
            lax.dynamic_slice_in_dim(keyval_b, column_place * slab_width, slab_width, 1),
        )
    )
    d_in, gain_grads[0] = norm_backward(inputs, scale_in, w_gains[0], d_hidden + d_half)
    grad_input = (d_half + d_in).astype(bf16)
    g_query, g_keyval, g_attend, g_gateup, g_down, g_left, g_right, g_pergate, g_perproj = (
        lax.psum_scatter(dw_query, "dp", scatter_dimension=1, tiled=True),
        lax.psum_scatter(dw_keyval, "dp", scatter_dimension=1, tiled=True),
        lax.psum_scatter(dw_attend, "dp", scatter_dimension=1, tiled=True),
        lax.psum_scatter(dw_gateup, "dp", scatter_dimension=2, tiled=True),
        lax.psum_scatter(dw_down, "dp", scatter_dimension=1, tiled=True),
        lax.psum_scatter(dw_left, "dp", scatter_dimension=1, tiled=True),
        lax.psum_scatter(dw_right, "dp", scatter_dimension=1, tiled=True),
        lax.psum_scatter(dw_pergate, "dp", scatter_dimension=1, tiled=True),
        lax.psum_scatter(dw_perproj, "dp", scatter_dimension=1, tiled=True),
    )
    gain_full = lax.dynamic_update_slice_in_dim(
        jnp.zeros((6, MODEL_WIDTH), single_float), jnp.stack(gain_grads), row_place * width_a, 1
    )
    head_full = lax.dynamic_update_slice_in_dim(
        jnp.zeros((QUERY_HEADS + 1, HEAD_WIDTH), single_float),
        dg_query,
        column_place * local_heads,
        0,
    )
    head_full = head_full.at[QUERY_HEADS].add(dg_key)
    logit_here = lax.dynamic_update_slice_in_dim(
        jnp.full((QUERY_HEADS,), NEGATIVE, single_float),
        jnp.max(block_peaks, axis=(0, 2)),
        column_place * local_heads,
        0,
    )

    def combine(left_part, right_part):
        return (
            left_part[0] + right_part[0],
            left_part[1] + right_part[1],
            jnp.maximum(left_part[2], right_part[2]),
        )

    gain_sum, head_sum, logit_top = joined(
        (gain_full, head_full, logit_here), ("dp", "row", "col"), combine
    )
    g_gains = lax.dynamic_slice_in_dim(gain_sum, row_place * width_a, width_a, 1)
    lead_device = (column_place == 0) & (data_at == 0)
    solo_device = lead_device & (row_place == 0)
    squares = jnp.float32(0.0)
    for gradient in (g_query, g_attend, g_gateup, g_down, g_left, g_right, g_pergate, g_perproj):
        squares = squares + jnp.sum(gradient * gradient)
    squares = squares + jnp.where(column_place == 0, jnp.sum(g_keyval * g_keyval), 0.0)
    squares = squares + jnp.where(lead_device, jnp.sum(g_gains * g_gains), 0.0)
    squares = squares + jnp.where(solo_device, jnp.sum(head_sum * head_sum), 0.0)
    grad_norm = jnp.sqrt(lax.psum(squares, ("dp", "row", "col")))
    clip_scale = CLIP / jnp.maximum(grad_norm, CLIP)
    scale_factors = LOGIT_CAP / jnp.maximum(logit_top, LOGIT_CAP)
    weights = (
        w_query,
        key_value_weight,
        w_attend,
        w_gateup,
        w_down,
        w_left,
        w_right,
        w_pergate,
        w_perproj,
        w_gains,
        w_heads,
    )
    moments = (
        m_query,
        key_value_first_moment,
        m_attend,
        m_gateup,
        m_down,
        m_left,
        m_right,
        m_pergate,
        m_perproj,
        m_gains,
        m_heads,
    )
    seconds = (
        v_query,
        key_value_second_moment,
        v_attend,
        v_gateup,
        v_down,
        v_left,
        v_right,
        v_pergate,
        v_perproj,
        v_gains,
        v_heads,
    )
    gradients = (
        g_query,
        g_keyval,
        g_attend,
        g_gateup,
        g_down,
        g_left,
        g_right,
        g_pergate,
        g_perproj,
        g_gains,
        head_sum,
    )
    step_rates = (
        MODEL_WIDTH ** (-0.5),
        MODEL_WIDTH ** (-0.5),
        (QUERY_HEADS * HEAD_WIDTH) ** (-0.5),
        MODEL_WIDTH ** (-0.5),
        FF ** (-0.5),
        MODEL_WIDTH ** (-0.5),
        RANK ** (-0.5),
        MODEL_WIDTH ** (-0.5),
        PLD ** (-0.5),
        GAIN_RATE,
        HEAD_RATE,
    )
    decays = (DECAY, DECAY, DECAY, DECAY, DECAY, DECAY, DECAY, DECAY, DECAY, 0.0, 0.0)
    updated = [
        adamw_step(
            weights[k], moments[k], seconds[k], gradients[k] * clip_scale, step_rates[k], decays[k]
        )
        for k in range(11)
    ]
    head_scale = jnp.sqrt(scale_factors)
    q_width = w_query.shape[1]
    q_head = (
        (column_place * data_devs + data_at) * q_width + jnp.arange(q_width, dtype=jnp.int32)
    ) // HEAD_WIDTH
    q_factor = jnp.sum(
        jnp.where(
            q_head[:, None] == jnp.arange(QUERY_HEADS, dtype=jnp.int32)[None, :],
            head_scale[None, :],
            0.0,
        ),
        axis=1,
    )
    new_query = updated[0][2] * q_factor[None, :]
    kv_width = key_value_weight.shape[1]
    key_value_index = data_at * kv_width + jnp.arange(kv_width, dtype=jnp.int32)
    key_value_scale = jnp.sqrt(
        jnp.min(scale_factors.reshape(KEY_VALUE_HEADS, QUERY_HEADS // KEY_VALUE_HEADS), axis=1)
    )
    key_value_choice = jnp.sum(
        jnp.where(
            (key_value_index // HEAD_WIDTH)[:, None]
            == jnp.arange(KEY_VALUE_HEADS, dtype=jnp.int32)[None, :],
            key_value_scale[None, :],
            0.0,
        ),
        axis=1,
    )
    key_value_factor = jnp.where(
        key_value_index < KEY_VALUE_HEADS * HEAD_WIDTH, key_value_choice, 1.0
    )
    new_keyval = updated[1][2] * key_value_factor[None, :]
    return (
        result,
        grad_input,
        grad_norm,
        scale_factors,
        updated[0][0],
        updated[0][1],
        new_query,
        updated[1][0],
        updated[1][1],
        new_keyval,
        updated[2][0],
        updated[2][1],
        updated[2][2],
        updated[3][0],
        updated[3][1],
        updated[3][2],
        updated[4][0],
        updated[4][1],
        updated[4][2],
        updated[5][0],
        updated[5][1],
        updated[5][2],
        updated[6][0],
        updated[6][1],
        updated[6][2],
        updated[7][0],
        updated[7][1],
        updated[7][2],
        updated[8][0],
        updated[8][1],
        updated[8][2],
        updated[9][0],
        updated[9][1],
        updated[9][2],
        updated[10][0],
        updated[10][1],
        updated[10][2],
    )


def solution(mesh):
    placed = (
        P(("dp", "col"), "row"),
        P(("dp", "row"), "col"),
        P(("dp", "col"), "row"),
        P(),
        P(),
        P("row", ("col", "dp")),
        P("row", ("col", "dp")),
        P("row", ("col", "dp")),
        P("row", "dp"),
        P("row", "dp"),
        P("row", "dp"),
        P("col", ("row", "dp")),
        P("col", ("row", "dp")),
        P("col", ("row", "dp")),
        P(None, "row", ("col", "dp")),
        P(None, "row", ("col", "dp")),
        P(None, "row", ("col", "dp")),
        P("col", ("row", "dp")),
        P("col", ("row", "dp")),
        P("col", ("row", "dp")),
        P("row", ("col", "dp")),
        P("row", ("col", "dp")),
        P("row", ("col", "dp")),
        P("col", ("row", "dp")),
        P("col", ("row", "dp")),
        P("col", ("row", "dp")),
        P("row", ("col", "dp")),
        P("row", ("col", "dp")),
        P("row", ("col", "dp")),
        P("col", ("row", "dp")),
        P("col", ("row", "dp")),
        P("col", ("row", "dp")),
        P(None, "row"),
        P(None, "row"),
        P(None, "row"),
        P(),
        P(),
        P(),
    )
    fits = (
        mesh.shape["col"] == KEY_VALUE_HEADS
        and mesh.shape["row"] * KEY_VALUE_HEADS == QUERY_HEADS
        and mesh.shape["dp"] == mesh.shape["row"]
    )
    return jax.shard_map(
        line_device if fits else per_device,
        mesh=mesh,
        in_specs=placed,
        out_specs=(
            P(("dp", "col"), "row"),
            P(("dp", "col"), "row"),
            P(),
            P(),
            P("row", ("col", "dp")),
            P("row", ("col", "dp")),
            P("row", ("col", "dp")),
            P("row", "dp"),
            P("row", "dp"),
            P("row", "dp"),
            P("col", ("row", "dp")),
            P("col", ("row", "dp")),
            P("col", ("row", "dp")),
            P(None, "row", ("col", "dp")),
            P(None, "row", ("col", "dp")),
            P(None, "row", ("col", "dp")),
            P("col", ("row", "dp")),
            P("col", ("row", "dp")),
            P("col", ("row", "dp")),
            P("row", ("col", "dp")),
            P("row", ("col", "dp")),
            P("row", ("col", "dp")),
            P("col", ("row", "dp")),
            P("col", ("row", "dp")),
            P("col", ("row", "dp")),
            P("row", ("col", "dp")),
            P("row", ("col", "dp")),
            P("row", ("col", "dp")),
            P("col", ("row", "dp")),
            P("col", ("row", "dp")),
            P("col", ("row", "dp")),
            P(None, "row"),
            P(None, "row"),
            P(None, "row"),
            P(),
            P(),
            P(),
        ),
        check_vma=False,
    )
```
